32 devices in a mesh: groups: 2 (over y), space: 4 (over z), rep: 4 (over x, core).
Axes of the slice: x: 2, y: 2, z: 4, core: 2. Of those that a mesh axis runs over, the one named last changes fastest.
Arguments:
- grid_latent: bfloat16 [8, 512, 512], P(('groups', 'rep'), 'space'), parts along dimension 0, may hold values from -6 to 6
- mesh_latent: bfloat16 [8, 256, 512], P(('groups', 'rep'), 'space'), parts along dimension 0, may hold values from -6 to 6
- mesh_cotangent: bfloat16 [8, 256, 512], P(('groups', 'rep'), 'space'), parts along dimension 0, may hold values from -6 to 6
- weights: bfloat16 [512, 2048], replicated, may hold values from -0.25 to 0.25
- g2m_pick: int32 [4, 3, 16], P('space'), may hold values from 0 to 127
- g2m_sender: int32 [1024], P('space'), may hold values from 0 to 47, as said below
- g2m_receiver: int32 [1024], P('space'), may hold values from 0 to 63
- m2m_pick: int32 [4, 4, 8], P('space'), may hold values from 0 to 63
- m2m_sender: int32 [1024], P('space'), may hold values from 0 to 31, as said below
- m2m_receiver: int32 [1024], P('space'), may hold values from 0 to 63
Outputs:
- mesh_out: bfloat16 [8, 256, 512], P(('groups', 'rep'), 'space'), parts along dimension 0
- grid_grad: bfloat16 [8, 512, 512], P(('groups', 'rep'), 'space'), parts along dimension 0
- weight_grad: float32 [1024, 2048], P(('groups', 'space')), parts along dimension 0
The draws below stay inside these ranges and needn't reach their ends.
There are 2 independent parts, one for each index of `groups`. The reference program is written for one: setup_inputs(seed, part) draws one part's arguments, and reference() takes and returns one part's arrays. A program takes and returns all parts, laid end to end along the dimension named above; an argument that names none is the same for every part. Nothing has to cross between parts.
Inputs may be any that keep to these rules, and one draw needn't show every extreme that they name: `g2m_sender`: for a g2m edge of block d with sender value j*16+k, the source block d+j-1 lies within 0 to 3. `m2m_sender`: for an edge of block d with sender value s*8+k: s is d, d-1 or d+1, or else k < 2; both bounds are reached in every block.
All inputs are finite; a program needn't handle non-finite values.
Results may differ from the reference program's by a relative error of at most 0.014.
Values may be sent and summed in bfloat16 or wider, within the bound.
No kernel may reach another device: no remote copies, remote signals or barrier semaphores. Data moves between devices by JAX's collectives and lax.ppermute only.
A program may use at most 64 MiB of HBM per device.

```python
import jax
import jax.numpy as jnp
from jax import lax

D = 512
G_DEV = 128
M_DEV = 64
E_G = 256
E_M = 256
CAP = 16
CAPM = 8
CAPM_FAR = 2
SAMPLES = 4
NG = 512
NM = 256
NEG = 1024
NEM = 1024
N_SPACE = 4


def draw_slots(key, peers, per_device, capacity, far_capacity):
    total = peers * per_device
    device = (jnp.arange(total, dtype=jnp.int32) // per_device).astype(jnp.int32)
    position = jnp.arange(total, dtype=jnp.int32) % per_device
    key_kind, key_far, key_near, key_slot = jax.random.split(key, 4)
    kind = jax.random.randint(key_kind, (total,), 0, 20)
    far_source = jax.random.randint(key_far, (total,), 0, peers)
    near_slot = jax.random.randint(key_near, (total,), 0, capacity)
    far_slot = jax.random.randint(key_slot, (total,), 0, far_capacity)
    source = jnp.where(kind < 8, device, jnp.where(kind < 11, device - 1, jnp.where(kind < 14, device + 1, far_source)))
    source = jnp.where((source < 0) | (source >= peers), device, source)
    opposite = (device + peers // 2) % peers
    source = jnp.where(position == 0, device, jnp.where(position == 1, opposite, source))
    beside = jnp.abs(source - device) <= 1
    slot = jnp.where(beside, near_slot, far_slot)
    slot = jnp.where(position == 0, capacity - 1, jnp.where(position == 1, far_capacity - 1, slot))
    return (source * capacity + slot).astype(jnp.int32)


def draw_g2m_sender(key, part):
    key = jax.random.fold_in(key, 11)
    peers = NG // G_DEV
    total = NG // G_DEV * E_G
    device = (jnp.arange(total, dtype=jnp.int32) // E_G).astype(jnp.int32)
    position = jnp.arange(total, dtype=jnp.int32) % E_G
    key_kind, key_slot = jax.random.split(key, 2)
    kind = jax.random.randint(key_kind, (total,), 0, 20)
    slot = jax.random.randint(key_slot, (total,), 0, CAP)
    offset = jnp.where(kind < 12, 1, jnp.where(kind < 16, 0, 2))
    source = device + offset - 1
    offset = jnp.where((source < 0) | (source >= peers), 1, offset)
    top_offset = jnp.where(device < peers - 1, 2, 0)
    offset = jnp.where(position == 0, top_offset, offset)
    slot = jnp.where(position == 0, CAP - 1, slot)
    low_offset = jnp.where(device > 0, 0, 1)
    offset = jnp.where(position == 1, low_offset, offset)
    slot = jnp.where(position == 1, 0, slot)
    return (offset * CAP + slot).astype(jnp.int32)


def draw_m2m_sender(key, part):
    key = jax.random.fold_in(key, 23)
    return draw_slots(key, NM // M_DEV, E_M, CAPM, CAPM_FAR)


def place_ends(entries, rng, least, largest):
    dims = entries.shape
    index_at = [jax.random.randint(jax.random.fold_in(rng, axis), (), 0, dims[axis]) for axis in range(len(dims))]
    entries = entries.at[tuple(index_at)].set(least)
    longest = dims.index(max(dims))
    index_at[longest] = (index_at[longest] + 1) % dims[longest]
    return entries.at[tuple(index_at)].set(largest)


def levels(rng, shape, cuts, low, largest):
    def one(dim, blocks):
        heights = jax.random.uniform(jax.random.fold_in(jax.random.fold_in(rng, 6), dim), (blocks,), jnp.float32, low / len(cuts), largest / len(cuts))
        return jnp.repeat(jnp.exp(heights), shape[dim] // blocks).reshape((-1,) + (1,) * (len(shape) - dim - 1))

    gain = one(*cuts[0])
    for cut in cuts[1:]:
        gain = gain * one(*cut)
    return gain


def normal_values(rng, shape, scale, reach, cuts=(), kind=jnp.bfloat16):
    drawn = jax.random.normal(rng, shape, jnp.float32) * scale
    if len(cuts) > 0:
        drawn = levels(rng, shape, cuts, -0.22, 0.18) * drawn
    return jnp.clip(drawn, min=-reach, max=reach).astype(kind)


def setup_inputs(seed: int = 0, part: int = 0) -> dict:
    arg_keys = jax.random.split(jax.random.key(seed), 11)
    own_keys = jax.random.split(jax.random.fold_in(arg_keys[10], part), 11)
    return {
        "grid_latent": normal_values(own_keys[0], (SAMPLES, NG, D), 1.0, 6.0, ((0, 4), (1, 4))),
        "mesh_latent": normal_values(own_keys[1], (SAMPLES, NM, D), 1.0, 6.0, ((0, 4), (1, 4))),
        "mesh_cotangent": normal_values(own_keys[2], (SAMPLES, NM, D), 1.0, 6.0, ((0, 4), (1, 4))),
        "weights": normal_values(arg_keys[3], (D, 4 * D), D ** -0.5, 0.25),
        "g2m_pick": place_ends(jax.random.randint(arg_keys[4], (N_SPACE, 3, CAP), 0, G_DEV), jax.random.fold_in(arg_keys[4], 1), 0, G_DEV - 1).astype(jnp.int32),
        "g2m_sender": draw_g2m_sender(jax.random.fold_in(arg_keys[10], 71), part),
        "g2m_receiver": place_ends(jax.random.randint(arg_keys[6], (NEG,), 0, M_DEV), jax.random.fold_in(arg_keys[6], 1), 0, M_DEV - 1).astype(jnp.int32),
        "m2m_pick": place_ends(jax.random.randint(arg_keys[7], (N_SPACE, N_SPACE, CAPM), 0, M_DEV), jax.random.fold_in(arg_keys[7], 1), 0, M_DEV - 1).astype(jnp.int32),
        "m2m_sender": draw_m2m_sender(jax.random.fold_in(arg_keys[10], 71), part),
        "m2m_receiver": place_ends(jax.random.randint(arg_keys[9], (NEM,), 0, M_DEV), jax.random.fold_in(arg_keys[9], 1), 0, M_DEV - 1).astype(jnp.int32),
    }


EPSILON = 1e-05

def swish(values):
    return values * jax.nn.sigmoid(values)

def swish_slope(values):
    squash = jax.nn.sigmoid(values)
    return squash * (1.0 + values * (1.0 - squash))

def norm_rows(values):
    centred = values - lax.optimization_barrier(jnp.mean(values, -1, keepdims=True))
    return centred * lax.rsqrt(lax.optimization_barrier(jnp.mean(centred * centred, -1, keepdims=True)) + EPSILON)

def norm_rows_back(values, upstream):
    centred = values - lax.optimization_barrier(jnp.mean(values, -1, keepdims=True))
    scaled = lax.rsqrt(lax.optimization_barrier(jnp.mean(centred * centred, -1, keepdims=True)) + EPSILON)
    normed = centred * scaled
    return scaled * (upstream - lax.optimization_barrier(jnp.mean(upstream, -1, keepdims=True)) - normed * lax.optimization_barrier(jnp.mean(upstream * normed, -1, keepdims=True)))

def grid_rows_of(pick, device, slots):
    peers = pick.shape[0]
    offset = (slots // CAP).astype(jnp.int32)
    source = jnp.clip(device + offset - 1, 0, peers - 1).astype(jnp.int32)
    return (source * G_DEV + pick[source, 2 - offset, slots % CAP]).astype(jnp.int32)

def mesh_rows_of(pick, device, slots):
    source = (slots // CAPM).astype(jnp.int32)
    return (source * M_DEV + pick[source, device, slots % CAPM]).astype(jnp.int32)

def edge_ends(rows_of, pick, sender, receiver, recv_rows):
    peers = pick.shape[0]
    count = sender.shape[0] // peers
    device = (jnp.arange(sender.shape[0], dtype=jnp.int32) // count).astype(jnp.int32)
    source_row = rows_of(pick, device, sender)
    target_row = device * recv_rows + receiver
    return (source_row.astype(jnp.int32), target_row.astype(jnp.int32))

def message_pass(table, recv_table, source_row, target_row, w_send, w_recv):
    send_proj = jnp.dot(table, w_send, preferred_element_type=jnp.float32)
    recv_proj = jnp.dot(recv_table, w_recv, preferred_element_type=jnp.float32)
    activation = send_proj[source_row] + recv_proj[target_row]
    message = swish(activation).astype(jnp.bfloat16)
    summed = jax.ops.segment_sum(message.astype(jnp.float32), target_row, num_segments=recv_table.shape[0])
    return (activation, summed)

def sender_back(table, rows_of, pick, sender, edge_grad, slot_count, w_send, accum):
    peers = pick.shape[0]
    count = sender.shape[0] // peers
    slots = jnp.arange(slot_count, dtype=jnp.int32)
    latent = table.shape[1]

    def one_block(carry, device):
        grad_weight, grad_rows = carry
        start = (device * count).astype(jnp.int32)
        block_sender = lax.dynamic_slice_in_dim(sender, start, count, 0)
        block_grad = lax.dynamic_slice_in_dim(edge_grad, start, count, 0)
        slot_sum = jax.ops.segment_sum(block_grad.astype(jnp.float32), block_sender, num_segments=slot_count).astype(jnp.bfloat16)
        rows = rows_of(pick, device, slots)
        grad_weight = grad_weight + jnp.dot(table[rows].T, slot_sum, preferred_element_type=jnp.float32)
        returned = jnp.dot(slot_sum, w_send.T, preferred_element_type=jnp.float32).astype(jnp.bfloat16)
        grad_rows = grad_rows.at[rows].add(returned.astype(jnp.float32))
        return ((grad_weight, grad_rows), None)
    start_carry = (jnp.zeros((latent, latent), jnp.float32), accum)
    (grad_weight, grad_rows), _ = lax.scan(one_block, start_carry, jnp.arange(peers, dtype=jnp.int32))
    return (grad_weight, grad_rows)

def reference(grid_latent, mesh_latent, mesh_cotangent, weights, g2m_pick, g2m_sender, g2m_receiver, m2m_pick, m2m_sender, m2m_receiver):
    latent = weights.shape[0]
    encode_sender = weights[:, :latent]
    encode_receiver = weights[:, latent:2 * latent]
    process_sender = weights[:, 2 * latent:3 * latent]
    process_receiver = weights[:, 3 * latent:]
    peers = m2m_pick.shape[0]
    grid_source, grid_target = edge_ends(grid_rows_of, g2m_pick, g2m_sender, g2m_receiver, M_DEV)
    mesh_source, mesh_target = edge_ends(mesh_rows_of, m2m_pick, m2m_sender, m2m_receiver, M_DEV)
    grid_count = grid_latent.shape[1]
    mesh_count = mesh_latent.shape[1]

    def one_sample(inputs):
        grid_rows, mesh_rows, upstream_in = inputs
        upstream = upstream_in.astype(jnp.float32)
        act_first, summed_first = message_pass(grid_rows, mesh_rows, grid_source, grid_target, encode_sender, encode_receiver)
        mesh_first = (mesh_rows.astype(jnp.float32) + norm_rows(summed_first)).astype(jnp.bfloat16)
        act_second, summed_second = message_pass(mesh_first, mesh_first, mesh_source, mesh_target, process_sender, process_receiver)
        mesh_final = (mesh_first.astype(jnp.float32) + norm_rows(summed_second)).astype(jnp.bfloat16)
        agg_second = norm_rows_back(summed_second, upstream)
        edge_second = (agg_second[mesh_target] * swish_slope(act_second)).astype(jnp.bfloat16)
        recv_second = jax.ops.segment_sum(edge_second.astype(jnp.float32), mesh_target, num_segments=mesh_count).astype(jnp.bfloat16)
        mesh_grad = upstream + jnp.dot(recv_second, process_receiver.T, preferred_element_type=jnp.float32)
        grad_ps, mesh_grad = sender_back(mesh_first, mesh_rows_of, m2m_pick, m2m_sender, edge_second, peers * CAPM, process_sender, mesh_grad)
        agg_first = norm_rows_back(summed_first, mesh_grad)
        edge_first = (agg_first[grid_target] * swish_slope(act_first)).astype(jnp.bfloat16)
        recv_first = jax.ops.segment_sum(edge_first.astype(jnp.float32), grid_target, num_segments=mesh_count).astype(jnp.bfloat16)
        grid_zero = jnp.zeros((grid_count, latent), jnp.float32)
        grad_es, grid_grad = sender_back(grid_rows, grid_rows_of, g2m_pick, g2m_sender, edge_first, 3 * CAP, encode_sender, grid_zero)
        grad_er = jnp.dot(mesh_rows.T, recv_first, preferred_element_type=jnp.float32)
        grad_pr = jnp.dot(mesh_first.T, recv_second, preferred_element_type=jnp.float32)
        weight_part = jnp.concatenate([grad_es, grad_er, grad_ps, grad_pr], axis=1)
        return (mesh_final, grid_grad.astype(jnp.bfloat16), weight_part)
    mesh_all, grid_all, weight_all = lax.map(one_sample, (grid_latent, mesh_latent, mesh_cotangent))
    return (mesh_all, grid_all, lax.optimization_barrier(jnp.sum(weight_all, axis=0)))
```

```python
import functools

import jax
import jax.numpy as jnp
from jax import lax
from jax.experimental import pallas as pl
from jax.experimental.pallas import tpu as pltpu
from jax.sharding import PartitionSpec as P

EPSILON = 1e-05


def with_halo(cells, sides, width):
    for axis, dim in sides:
        count = lax.axis_size(axis)
        ends = count - 1
        head = lax.slice_in_dim(cells, 0, width, axis=dim)
        tail = lax.slice_in_dim(cells, cells.shape[dim] - width, cells.shape[dim], axis=dim)
        cells = jnp.concatenate(
            [
                lax.ppermute(tail, axis, [(i, (i + 1) % count) for i in range(ends)]),
                cells,
                lax.ppermute(head, axis, [((i + 1) % count, i) for i in range(ends)]),
            ],
            axis=dim,
        )
    return cells


def swish(values):
    return values * jax.nn.sigmoid(values)


def swish_slope(values):
    squash = jax.nn.sigmoid(values)
    return squash * (1.0 + values * (1.0 - squash))


def norm_rows(values):
    centred = values - jnp.mean(values, -1, keepdims=True)
    return centred * lax.rsqrt(jnp.mean(centred * centred, -1, keepdims=True) + EPSILON)


def norm_rows_back(values, upstream):
    centred = values - jnp.mean(values, -1, keepdims=True)
    scaled = lax.rsqrt(jnp.mean(centred * centred, -1, keepdims=True) + EPSILON)
    normed = centred * scaled
    return scaled * (
        upstream
        - jnp.mean(upstream, -1, keepdims=True)
        - normed * jnp.mean(upstream * normed, -1, keepdims=True)
    )


def slot_rows(pick_row):
    listed = pick_row.reshape(-1)
    return listed


def mesh_route(outgoing, capacity, peer_count):
    columns = outgoing.shape[1]
    pieces = lax.all_to_all(
        outgoing.reshape(peer_count, capacity, columns),
        "space",
        split_axis=0,
        concat_axis=0,
        tiled=True,
    )
    arrived = pieces.reshape(peer_count * capacity, columns)
    return arrived


def grid_route(outgoing, capacity):
    columns = outgoing.shape[1]
    lists = outgoing.reshape(3, capacity, columns)
    rims = with_halo(jnp.stack([lists[0], lists[2]]), (("space", 0),), 1)
    return jnp.concatenate([rims[0], lists[1], rims[3]], axis=0)


def edge_pass(arrived, recv_table, located, receiver, w_send, w_recv):
    recv_proj = jnp.dot(recv_table, w_recv, preferred_element_type=jnp.float32)
    slot_proj = jnp.dot(arrived, w_send, preferred_element_type=jnp.float32)
    activation = slot_proj[located] + recv_proj[receiver]
    message = swish(activation).astype(jnp.bfloat16)
    member = (
        receiver[None, :] == jnp.arange(recv_table.shape[0], dtype=jnp.int32)[:, None]
    ).astype(jnp.bfloat16)
    summed = jnp.dot(member, message, preferred_element_type=jnp.float32)
    return (activation, member, summed)


def backward_pass(slot_count, located, activation, member, receiver, agg_grad, w_send):
    edge_grad = (agg_grad[receiver] * swish_slope(activation)).astype(jnp.bfloat16)
    recv_sum = jnp.dot(member, edge_grad, preferred_element_type=jnp.float32).astype(jnp.bfloat16)
    slot_member = (located[None, :] == jnp.arange(slot_count, dtype=jnp.int32)[:, None]).astype(
        jnp.bfloat16
    )
    slot_sum = jnp.dot(slot_member, edge_grad, preferred_element_type=jnp.float32).astype(
        jnp.bfloat16
    )
    returned = jnp.dot(slot_sum, w_send.T, preferred_element_type=jnp.float32).astype(jnp.bfloat16)
    return (recv_sum, slot_sum, returned)


def gather_back(listed, back_rows, row_count):
    owner = (listed[None, :] == jnp.arange(row_count, dtype=jnp.int32)[:, None]).astype(
        jnp.bfloat16
    )
    return jnp.dot(owner, back_rows, preferred_element_type=jnp.float32)


def partitioned_body(
    grid_latent,
    mesh_latent,
    mesh_cotangent,
    weights,
    g2m_pick,
    g2m_sender,
    g2m_receiver,
    m2m_pick,
    m2m_sender,
    m2m_receiver,
):
    grid_rows = grid_latent[0]
    mesh_rows = mesh_latent[0]
    upstream = mesh_cotangent[0].astype(jnp.float32)
    latent = weights.shape[0]
    encode_sender = weights[:, :latent]
    encode_receiver = weights[:, latent : 2 * latent]
    process_sender = weights[:, 2 * latent : 3 * latent]
    process_receiver = weights[:, 3 * latent :]
    peer_count = lax.axis_size("space")
    grid_cap = g2m_pick.shape[2]
    mesh_cap = m2m_pick.shape[2]
    grid_listed = g2m_pick[0].reshape(-1)
    grid_arrived = grid_route(grid_rows[grid_listed], grid_cap)
    act_first, member_first, summed_first = edge_pass(
        grid_arrived, mesh_rows, g2m_sender, g2m_receiver, encode_sender, encode_receiver
    )
    mesh_first = (mesh_rows.astype(jnp.float32) + norm_rows(summed_first)).astype(jnp.bfloat16)
    mesh_listed = slot_rows(m2m_pick[0])
    mesh_arrived = mesh_route(mesh_first[mesh_listed], mesh_cap, peer_count)
    act_second, member_second, summed_second = edge_pass(
        mesh_arrived, mesh_first, m2m_sender, m2m_receiver, process_sender, process_receiver
    )
    mesh_final = (mesh_first.astype(jnp.float32) + norm_rows(summed_second)).astype(jnp.bfloat16)
    agg_second = norm_rows_back(summed_second, upstream)
    recv_second, slot_second, returned_second = backward_pass(
        mesh_arrived.shape[0],
        m2m_sender,
        act_second,
        member_second,
        m2m_receiver,
        agg_second,
        process_sender,
    )
    back_second = mesh_route(returned_second, mesh_cap, peer_count)
    mesh_grad = upstream + jnp.dot(
        recv_second, process_receiver.T, preferred_element_type=jnp.float32
    )
    mesh_grad = mesh_grad + gather_back(mesh_listed, back_second, mesh_rows.shape[0])
    agg_first = norm_rows_back(summed_first, mesh_grad)
    recv_first, slot_first, returned_first = backward_pass(
        grid_arrived.shape[0],
        g2m_sender,
        act_first,
        member_first,
        g2m_receiver,
        agg_first,
        encode_sender,
    )
    back_first = grid_route(returned_first, grid_cap)
    grid_grad = gather_back(grid_listed, back_first, grid_rows.shape[0]).astype(jnp.bfloat16)
    factor_pairs = (
        (grid_arrived, slot_first),
        (mesh_rows, recv_first),
        (mesh_arrived, slot_second),
        (mesh_first, recv_second),
    )
    blocks = []
    for first_factor, second_factor in factor_pairs:
        blocks.append(
            lax.dot_general(
                first_factor,
                second_factor,
                (((0,), (0,)), ((), ())),
                preferred_element_type=jnp.float32,
            )
        )
    shares = lax.psum_scatter(
        jnp.concatenate(blocks, axis=1).astype(jnp.bfloat16),
        "space",
        scatter_dimension=0,
        tiled=True,
    )
    weight_grad = lax.psum(shares, "rep").astype(jnp.float32)
    return (mesh_final[None], grid_grad[None], weight_grad)


F32 = jnp.float32
BF16 = jnp.bfloat16
INDEX_ROWS = 16
SAMPLE_EDGE_BYTES = 8 << 20


def dot(left, right):
    return jnp.dot(left, right, preferred_element_type=F32)


def dot_first(left, right):
    return lax.dot_general(left, right, (((0,), (0,)), ((), ())), preferred_element_type=F32)


def dot_last(left, right):
    return lax.dot_general(left, right, (((1,), (1,)), ((), ())), preferred_element_type=F32)


def one_hot(labels, count):
    rows = lax.broadcasted_iota(jnp.int32, (count, labels.shape[-1]), 0)
    return (rows == labels).astype(F32).astype(BF16)


def row_moments(values):
    centred = values - jnp.mean(values, -1, keepdims=True)
    return centred, lax.rsqrt(jnp.mean(centred * centred, -1, keepdims=True) + EPSILON)


def moments_back(normed, scaled, upstream):
    return scaled * (
        upstream
        - jnp.mean(upstream, -1, keepdims=True)
        - normed * jnp.mean(upstream * normed, -1, keepdims=True)
    )


def pack_kernel(
    grid_ref,
    mesh_ref,
    g2m_pick_ref,
    g2m_sender_ref,
    g2m_receiver_ref,
    m2m_pick_ref,
    m2m_sender_ref,
    m2m_receiver_ref,
    packed_ref,
    index_ref,
):
    lists, capacity = g2m_pick_ref.shape[1:]
    mesh_count = mesh_ref.shape[1]
    regions, mesh_cap = m2m_pick_ref.shape[1:]
    edges = g2m_sender_ref.shape[1]
    grid_rows = grid_ref[0]
    for i in range(lists):
        picked = one_hot(g2m_pick_ref[0, i : i + 1, :], grid_rows.shape[0])
        packed_ref[i * capacity : (i + 1) * capacity, :] = dot_first(picked, grid_rows).astype(BF16)
    first = lists * capacity
    packed_ref[first : first + mesh_count, :] = mesh_ref[0]
    index_ref[...] = jnp.zeros_like(index_ref)
    index_ref[0:1, 0:edges] = g2m_sender_ref[...].astype(F32)
    index_ref[0:1, edges : 2 * edges] = g2m_receiver_ref[...].astype(F32)
    index_ref[1:2, 0:edges] = m2m_sender_ref[...].astype(F32)
    index_ref[1:2, edges : 2 * edges] = m2m_receiver_ref[...].astype(F32)
    slots = regions * mesh_cap
    lane = lax.broadcasted_iota(jnp.int32, (mesh_cap, slots), 1)
    spread = (lane % mesh_cap == lax.broadcasted_iota(jnp.int32, (mesh_cap, slots), 0)).astype(F32)
    spread = dot(m2m_pick_ref[0].astype(F32).astype(BF16), spread.astype(BF16))
    lane = lax.broadcasted_iota(jnp.int32, (regions, slots), 1)
    owned = lane // mesh_cap == lax.broadcasted_iota(jnp.int32, (regions, slots), 0)
    index_ref[2:3, 0:slots] = jnp.sum(jnp.where(owned, spread, 0.0), 0, keepdims=True)
    packed_ref[first + mesh_count :, :] = index_ref[...].astype(BF16)


def edge_forward(table, hot, hot_receiver, slope_ref, first):
    activation = dot_first(hot, table)
    squash = 0.5 + 0.5 * jnp.tanh(0.5 * activation)
    message = activation * squash
    slope_ref[first : first + activation.shape[0], :] = (
        squash + message * (1.0 - squash)
    ).astype(BF16)
    return dot(hot_receiver, message.astype(BF16))


def forward_kernel(
    regions,
    listed,
    mesh_count,
    mesh_cap,
    *refs,
):
    packed_refs = refs[:regions]
    (
        weights_ref,
        mesh_out_ref,
        grid_ref,
        mesh_ref,
        first_ref,
        sent_ref,
        index_ref,
        slope_one_ref,
        slope_two_ref,
        normed_one_ref,
        scaled_one_ref,
        normed_two_ref,
        scaled_two_ref,
        packed_index,
    ) = refs[regions:]
    latent = weights_ref.shape[0]
    edges = slope_one_ref.shape[0] // regions
    capacity = listed // 3
    slots = regions * mesh_cap
    me = lax.axis_index("space")
    for back, packed_ref in enumerate(packed_refs):
        region = lax.rem(me + (regions - back), regions)
        at = lambda rows: pl.ds(pl.multiple_of(region * rows, rows), rows)
        grid_ref[at(listed), :] = packed_ref[:listed, :]
        mesh_ref[at(mesh_count), :] = packed_ref[listed : listed + mesh_count, :]
        packed_index[at(INDEX_ROWS), :] = packed_ref[listed + mesh_count :, :]
    index_ref[...] = packed_index[...].astype(F32).astype(jnp.int32)

    grid_proj = dot(grid_ref[...], weights_ref[:, :latent])
    mesh_proj = dot(mesh_ref[...], weights_ref[:, latent : 2 * latent])
    blank = jnp.zeros((capacity, latent), F32)
    for d in range(regions):
        hot_sender = one_hot(index_ref[d * INDEX_ROWS : d * INDEX_ROWS + 1, :edges], listed)
        hot_receiver = one_hot(
            index_ref[d * INDEX_ROWS : d * INDEX_ROWS + 1, edges:], mesh_count
        )
        before = (d - 1) * listed + 2 * capacity
        within = d * listed + capacity
        after = (d + 1) * listed
        table = jnp.concatenate(
            [
                grid_proj[before : before + capacity] if d > 0 else blank,
                grid_proj[within : within + capacity],
                grid_proj[after : after + capacity] if d < regions - 1 else blank,
                mesh_proj[d * mesh_count : (d + 1) * mesh_count],
            ],
            axis=0,
        ).astype(BF16)
        summed = edge_forward(
            table,
            jnp.concatenate([hot_sender, hot_receiver], axis=0),
            hot_receiver,
            slope_one_ref,
            d * edges,
        )
        centred, scaled = row_moments(summed)
        normed = centred * scaled
        rows = slice(d * mesh_count, (d + 1) * mesh_count)
        normed_one_ref[rows, :] = normed
        scaled_one_ref[rows, :] = jnp.broadcast_to(scaled, (mesh_count, scaled_one_ref.shape[1]))
        first_ref[rows, :] = (mesh_ref[rows, :].astype(F32) + normed).astype(BF16)

    for s in range(regions):
        hot = one_hot(index_ref[s * INDEX_ROWS + 2 : s * INDEX_ROWS + 3, :slots], mesh_count)
        sent_ref[s * slots : (s + 1) * slots, :] = dot_first(
            hot, first_ref[s * mesh_count : (s + 1) * mesh_count, :]
        ).astype(BF16)
    sent_proj = dot(sent_ref[...], weights_ref[:, 2 * latent : 3 * latent])
    first_proj = dot(first_ref[...], weights_ref[:, 3 * latent :])
    for d in range(regions):
        hot_sender = one_hot(index_ref[d * INDEX_ROWS + 1 : d * INDEX_ROWS + 2, :edges], slots)
        hot_receiver = one_hot(
            index_ref[d * INDEX_ROWS + 1 : d * INDEX_ROWS + 2, edges:], mesh_count
        )
        pieces = [
            sent_proj[s * slots + d * mesh_cap : s * slots + (d + 1) * mesh_cap]
            for s in range(regions)
        ]
        table = jnp.concatenate(
            pieces + [first_proj[d * mesh_count : (d + 1) * mesh_count]], axis=0
        ).astype(BF16)
        summed = edge_forward(
            table,
            jnp.concatenate([hot_sender, hot_receiver], axis=0),
            hot_receiver,
            slope_two_ref,
            d * edges,
        )
        centred, scaled = row_moments(summed)
        rows = slice(d * mesh_count, (d + 1) * mesh_count)
        normed_two_ref[rows, :] = centred * scaled
        scaled_two_ref[rows, :] = jnp.broadcast_to(scaled, (mesh_count, scaled_two_ref.shape[1]))
    own = pl.ds(pl.multiple_of(me * mesh_count, mesh_count), mesh_count)
    mesh_out_ref[0] = (first_ref[own, :].astype(F32) + normed_two_ref[own, :]).astype(BF16)


def edge_backward(agg_grad, hot, hot_receiver, slope):
    edge_grad = (dot_first(hot_receiver, agg_grad) * slope.astype(F32)).astype(BF16)
    return dot(hot, edge_grad)


def process_back_kernel(regions, mesh_cap, *refs):
    cotangent_refs = refs[:regions]
    (
        weights_ref,
        first_ref,
        sent_ref,
        index_ref,
        slope_ref,
        normed_ref,
        scaled_ref,
        mesh_grad_ref,
        share_ref,
        upstream_ref,
        slot_ref,
        recv_ref,
    ) = refs[regions:]
    latent = first_ref.shape[1]
    mesh_count = first_ref.shape[0] // regions
    edges = slope_ref.shape[0] // regions
    slots = regions * mesh_cap
    me = lax.axis_index("space")
    for back, cotangent_ref in enumerate(cotangent_refs):
        region = lax.rem(me + (regions - back), regions)
        at = pl.ds(pl.multiple_of(region * mesh_count, mesh_count), mesh_count)
        upstream_ref[at, :] = cotangent_ref[0].astype(F32)
    agg_grad = moments_back(normed_ref[...], scaled_ref[:, 0:1], upstream_ref[...]).astype(BF16)
    for d in range(regions):
        labels = slice(d * INDEX_ROWS + 1, d * INDEX_ROWS + 2)
        hot_sender = one_hot(index_ref[labels, :edges], slots)
        hot_receiver = one_hot(index_ref[labels, edges:], mesh_count)
        rows = slice(d * mesh_count, (d + 1) * mesh_count)
        sums = edge_backward(
            agg_grad[rows],
            jnp.concatenate([hot_sender, hot_receiver], axis=0),
            hot_receiver,
            slope_ref[d * edges : (d + 1) * edges, :],
        )
        for s in range(regions):
            first = s * slots + d * mesh_cap
            slot_ref[first : first + mesh_cap, :] = sums[s * mesh_cap : (s + 1) * mesh_cap]
        recv_ref[rows, :] = sums[slots:].astype(BF16)
    slot_sum = slot_ref[...].astype(BF16)
    columns = share_ref.shape[0]
    mine = pl.ds(pl.multiple_of(me * columns, columns), columns)
    share_ref[:, :latent] = dot_first(sent_ref[:, mine], slot_sum).astype(BF16)
    share_ref[:, latent:] = dot_first(first_ref[:, mine], recv_ref[...]).astype(BF16)
    returned = dot_last(slot_sum, weights_ref[:, 2 * latent : 3 * latent]).astype(BF16)
    grad = upstream_ref[...] + dot_last(recv_ref[...], weights_ref[:, 3 * latent :])
    for s in range(regions):
        hot = one_hot(index_ref[s * INDEX_ROWS + 2 : s * INDEX_ROWS + 3, :slots], mesh_count)
        rows = slice(s * mesh_count, (s + 1) * mesh_count)
        mesh_grad_ref[rows, :] = grad[rows] + dot(hot, returned[s * slots : (s + 1) * slots])


def encode_back_kernel(
    regions,
    weights_ref,
    pick_ref,
    grid_ref,
    mesh_ref,
    index_ref,
    slope_ref,
    normed_ref,
    scaled_ref,
    mesh_grad_ref,
    grid_grad_ref,
    share_ref,
    slot_ref,
    recv_ref,
):
    latent = mesh_ref.shape[1]
    mesh_count = mesh_ref.shape[0] // regions
    listed = grid_ref.shape[0] // regions
    capacity = listed // 3
    edges = slope_ref.shape[0] // regions
    me = lax.axis_index("space")
    agg_grad = moments_back(normed_ref[...], scaled_ref[:, 0:1], mesh_grad_ref[...]).astype(BF16)
    blank = jnp.zeros((capacity, latent), BF16)
    slot_ref[0:capacity, :] = blank
    slot_ref[regions * listed - capacity :, :] = blank
    for d in range(regions):
        labels = slice(d * INDEX_ROWS, d * INDEX_ROWS + 1)
        hot_sender = one_hot(index_ref[labels, :edges], listed)
        hot_receiver = one_hot(index_ref[labels, edges:], mesh_count)
        rows = slice(d * mesh_count, (d + 1) * mesh_count)
        sums = edge_backward(
            agg_grad[rows],
            jnp.concatenate([hot_sender, hot_receiver], axis=0),
            hot_receiver,
            slope_ref[d * edges : (d + 1) * edges, :],
        ).astype(BF16)
        for j in range(3):
            source = d + j - 1
            if 0 <= source < regions:
                first = source * listed + (2 - j) * capacity
                slot_ref[first : first + capacity, :] = sums[j * capacity : (j + 1) * capacity]
        recv_ref[rows, :] = sums[listed:]
    columns = share_ref.shape[0]
    mine = pl.ds(pl.multiple_of(me * columns, columns), columns)
    share_ref[:, :latent] = dot_first(grid_ref[:, mine], slot_ref[...]).astype(BF16)
    share_ref[:, latent:] = dot_first(mesh_ref[:, mine], recv_ref[...]).astype(BF16)
    own = pl.ds(pl.multiple_of(me * listed, listed), listed)
    returned = dot_last(slot_ref[own, :], weights_ref[:, :latent]).astype(BF16)
    total = None
    for i in range(3):
        owner = one_hot(pick_ref[0, i : i + 1, :], grid_grad_ref.shape[1])
        part = dot(owner, returned[i * capacity : (i + 1) * capacity])
        total = part if total is None else total + part
    grid_grad_ref[0] = total.astype(BF16)


VMEM = pl.BlockSpec(memory_space=pltpu.VMEM)


def call(kernel, operands, outputs, scratch, flops):
    return pl.pallas_call(
        kernel,
        out_shape=[jax.ShapeDtypeStruct(shape, kind) for shape, kind in outputs],
        in_specs=[VMEM] * len(operands),
        out_specs=[VMEM] * len(outputs),
        scratch_shapes=[pltpu.VMEM(shape, kind) for shape, kind in scratch],
        compiler_params=pltpu.CompilerParams(vmem_limit_bytes=40 << 20),
        cost_estimate=pl.CostEstimate(flops=flops, bytes_accessed=4 << 20, transcendentals=0),
    )(*operands)


def from_others(block):
    count = lax.axis_size("space")
    return [block] + [
        lax.ppermute(block, "space", [(i, (i + step) % count) for i in range(count)])
        for step in range(1, count)
    ]


def pair_sums(share):
    count = lax.axis_size("rep")
    bit = 1
    total = share
    while bit < count:
        other = lax.ppermute(
            total.astype(BF16), "rep", [(i, i ^ bit) for i in range(count)]
        )
        total = total.astype(F32) + other.astype(F32)
        bit *= 2
        if bit < count:
            total = total.astype(BF16)
    return total


def whole_sample_body(
    grid_latent,
    mesh_latent,
    mesh_cotangent,
    weights,
    g2m_pick,
    g2m_sender,
    g2m_receiver,
    m2m_pick,
    m2m_sender,
    m2m_receiver,
):
    regions = lax.axis_size("space")
    latent = weights.shape[0]
    listed = g2m_pick.shape[1] * g2m_pick.shape[2]
    mesh_count = mesh_latent.shape[1]
    mesh_cap = m2m_pick.shape[2]
    edges = g2m_sender.shape[0]
    columns = latent // regions
    packed = call(
        pack_kernel,
        (
            grid_latent,
            mesh_latent,
            g2m_pick,
            g2m_sender.reshape(1, -1),
            g2m_receiver.reshape(1, -1),
            m2m_pick,
            m2m_sender.reshape(1, -1),
            m2m_receiver.reshape(1, -1),
        ),
        [((listed + mesh_count + INDEX_ROWS, latent), BF16)],
        [((INDEX_ROWS, latent), F32)],
        10**7,
    )[0]
    packed, cotangent = lax.optimization_barrier((packed, mesh_cotangent))
    packs = from_others(packed)
    cotangents = from_others(cotangent)
    rows = regions * mesh_count
    (
        mesh_out,
        grid_all,
        mesh_all,
        mesh_first,
        mesh_sent,
        index,
        slope_one,
        slope_two,
        normed_one,
        scaled_one,
        normed_two,
        scaled_two,
    ) = call(
        functools.partial(forward_kernel, regions, listed, mesh_count, mesh_cap),
        (*packs, weights),
        [
            (mesh_latent.shape, BF16),
            ((regions * listed, latent), BF16),
            ((rows, latent), BF16),
            ((rows, latent), BF16),
            ((regions * regions * mesh_cap, latent), BF16),
            ((regions * INDEX_ROWS, latent), jnp.int32),
            ((regions * edges, latent), BF16),
            ((regions * edges, latent), BF16),
            ((rows, latent), F32),
            ((rows, 128), F32),
            ((rows, latent), F32),
            ((rows, 128), F32),
        ],
        [((regions * INDEX_ROWS, latent), BF16)],
        2 * 10**9,
    )
    mesh_grad, share_two = call(
        functools.partial(process_back_kernel, regions, mesh_cap),
        (
            *cotangents,
            weights,
            mesh_first,
            mesh_sent,
            index,
            slope_two,
            normed_two,
            scaled_two,
        ),
        [((rows, latent), F32), ((columns, 2 * latent), BF16)],
        [
            ((rows, latent), F32),
            ((regions * regions * mesh_cap, latent), F32),
            ((rows, latent), BF16),
        ],
        10**9,
    )
    grid_grad, share_one = call(
        functools.partial(encode_back_kernel, regions),
        (
            weights,
            g2m_pick,
            grid_all,
            mesh_all,
            index,
            slope_one,
            normed_one,
            scaled_one,
            mesh_grad,
        ),
        [(grid_latent.shape, BF16), ((columns, 2 * latent), BF16)],
        [((regions * listed, latent), BF16), ((rows, latent), BF16)],
        10**9,
    )
    weight_grad = jnp.concatenate([pair_sums(share_one), pair_sums(share_two)], axis=1)
    return (mesh_out, grid_grad, weight_grad)


def solution(mesh):
    regions = mesh.shape["space"]
    samples = mesh.shape["rep"]

    def whole(*arguments):
        edges = arguments[5].shape[0] + arguments[8].shape[0]
        latent = arguments[3].shape[0]
        fits = edges * latent * 4 <= SAMPLE_EDGE_BYTES and latent % (128 * regions) == 0
        paired = samples & (samples - 1) == 0
        return sharded(whole_sample_body if fits and paired else partitioned_body)(*arguments)

    def sharded(body):
        return jax.shard_map(
            body,
            mesh=mesh,
            in_specs=(
                P(("groups", "rep"), "space", None),
                P(("groups", "rep"), "space", None),
                P(("groups", "rep"), "space", None),
                P(),
                P("space", None, None),
                P("space"),
                P("space"),
                P("space", None, None),
                P("space"),
                P("space"),
            ),
            out_specs=(
                P(("groups", "rep"), "space", None),
                P(("groups", "rep"), "space", None),
                P(("groups", "space"), None),
            ),
            check_vma=False,
        )

    return whole
```

```python
import functools

import jax
import jax.numpy as jnp
from jax import lax
from jax.experimental import pallas as pl
from jax.experimental.pallas import tpu as pltpu
from jax.sharding import PartitionSpec as P

EPSILON = 1e-05


def with_halo(cells, sides, width):
    for axis, dim in sides:
        count = lax.axis_size(axis)
        ends = count - 1
        head = lax.slice_in_dim(cells, 0, width, axis=dim)
        tail = lax.slice_in_dim(cells, cells.shape[dim] - width, cells.shape[dim], axis=dim)
        cells = jnp.concatenate(
            [
                lax.ppermute(tail, axis, [(i, (i + 1) % count) for i in range(ends)]),
                cells,
                lax.ppermute(head, axis, [((i + 1) % count, i) for i in range(ends)]),
            ],
            axis=dim,
        )
    return cells


def swish(values):
    return values * jax.nn.sigmoid(values)


def swish_slope(values):
    squash = jax.nn.sigmoid(values)
    return squash * (1.0 + values * (1.0 - squash))


def norm_rows(values):
    centred = values - jnp.mean(values, -1, keepdims=True)
    return centred * lax.rsqrt(jnp.mean(centred * centred, -1, keepdims=True) + EPSILON)


def norm_rows_back(values, upstream):
    centred = values - jnp.mean(values, -1, keepdims=True)
    scaled = lax.rsqrt(jnp.mean(centred * centred, -1, keepdims=True) + EPSILON)
    normed = centred * scaled
    return scaled * (
        upstream
        - jnp.mean(upstream, -1, keepdims=True)
        - normed * jnp.mean(upstream * normed, -1, keepdims=True)
    )


def slot_rows(pick_row):
    listed = pick_row.reshape(-1)
    return listed


def mesh_route(outgoing, capacity, peer_count):
    columns = outgoing.shape[1]
    pieces = lax.all_to_all(
        outgoing.reshape(peer_count, capacity, columns),
        "space",
        split_axis=0,
        concat_axis=0,
        tiled=True,
    )
    arrived = pieces.reshape(peer_count * capacity, columns)
    return arrived


def grid_route(outgoing, capacity):
    columns = outgoing.shape[1]
    lists = outgoing.reshape(3, capacity, columns)
    rims = with_halo(jnp.stack([lists[0], lists[2]]), (("space", 0),), 1)
    return jnp.concatenate([rims[0], lists[1], rims[3]], axis=0)


def edge_pass(arrived, recv_table, located, receiver, w_send, w_recv):
    recv_proj = jnp.dot(recv_table, w_recv, preferred_element_type=jnp.float32)
    slot_proj = jnp.dot(arrived, w_send, preferred_element_type=jnp.float32)
    activation = slot_proj[located] + recv_proj[receiver]
    message = swish(activation).astype(jnp.bfloat16)
    member = (
        receiver[None, :] == jnp.arange(recv_table.shape[0], dtype=jnp.int32)[:, None]
    ).astype(jnp.bfloat16)
    summed = jnp.dot(member, message, preferred_element_type=jnp.float32)
    return (activation, member, summed)


def backward_pass(slot_count, located, activation, member, receiver, agg_grad, w_send):
    edge_grad = (agg_grad[receiver] * swish_slope(activation)).astype(jnp.bfloat16)
    recv_sum = jnp.dot(member, edge_grad, preferred_element_type=jnp.float32).astype(jnp.bfloat16)
    slot_member = (located[None, :] == jnp.arange(slot_count, dtype=jnp.int32)[:, None]).astype(
        jnp.bfloat16
    )
    slot_sum = jnp.dot(slot_member, edge_grad, preferred_element_type=jnp.float32).astype(
        jnp.bfloat16
    )
    returned = jnp.dot(slot_sum, w_send.T, preferred_element_type=jnp.float32).astype(jnp.bfloat16)
    return (recv_sum, slot_sum, returned)


def gather_back(listed, back_rows, row_count):
    owner = (listed[None, :] == jnp.arange(row_count, dtype=jnp.int32)[:, None]).astype(
        jnp.bfloat16
    )
    return jnp.dot(owner, back_rows, preferred_element_type=jnp.float32)


def partitioned_body(
    grid_latent,
    mesh_latent,
    mesh_cotangent,
    weights,
    g2m_pick,
    g2m_sender,
    g2m_receiver,
    m2m_pick,
    m2m_sender,
    m2m_receiver,
):
    grid_rows = grid_latent[0]
    mesh_rows = mesh_latent[0]
    upstream = mesh_cotangent[0].astype(jnp.float32)
    latent = weights.shape[0]
    encode_sender = weights[:, :latent]
    encode_receiver = weights[:, latent : 2 * latent]
    process_sender = weights[:, 2 * latent : 3 * latent]
    process_receiver = weights[:, 3 * latent :]
    peer_count = lax.axis_size("space")
    grid_cap = g2m_pick.shape[2]
    mesh_cap = m2m_pick.shape[2]
    grid_listed = g2m_pick[0].reshape(-1)
    grid_arrived = grid_route(grid_rows[grid_listed], grid_cap)
    act_first, member_first, summed_first = edge_pass(
        grid_arrived, mesh_rows, g2m_sender, g2m_receiver, encode_sender, encode_receiver
    )
    mesh_first = (mesh_rows.astype(jnp.float32) + norm_rows(summed_first)).astype(jnp.bfloat16)
    mesh_listed = slot_rows(m2m_pick[0])
    mesh_arrived = mesh_route(mesh_first[mesh_listed], mesh_cap, peer_count)
    act_second, member_second, summed_second = edge_pass(
        mesh_arrived, mesh_first, m2m_sender, m2m_receiver, process_sender, process_receiver
    )
    mesh_final = (mesh_first.astype(jnp.float32) + norm_rows(summed_second)).astype(jnp.bfloat16)
    agg_second = norm_rows_back(summed_second, upstream)
    recv_second, slot_second, returned_second = backward_pass(
        mesh_arrived.shape[0],
        m2m_sender,
        act_second,
        member_second,
        m2m_receiver,
        agg_second,
        process_sender,
    )
    back_second = mesh_route(returned_second, mesh_cap, peer_count)
    mesh_grad = upstream + jnp.dot(
        recv_second, process_receiver.T, preferred_element_type=jnp.float32
    )
    mesh_grad = mesh_grad + gather_back(mesh_listed, back_second, mesh_rows.shape[0])
    agg_first = norm_rows_back(summed_first, mesh_grad)
    recv_first, slot_first, returned_first = backward_pass(
        grid_arrived.shape[0],
        g2m_sender,
        act_first,
        member_first,
        g2m_receiver,
        agg_first,
        encode_sender,
    )
    back_first = grid_route(returned_first, grid_cap)
    grid_grad = gather_back(grid_listed, back_first, grid_rows.shape[0]).astype(jnp.bfloat16)
    factor_pairs = (
        (grid_arrived, slot_first),
        (mesh_rows, recv_first),
        (mesh_arrived, slot_second),
        (mesh_first, recv_second),
    )
    blocks = []
    for first_factor, second_factor in factor_pairs:
        blocks.append(
            lax.dot_general(
                first_factor,
                second_factor,
                (((0,), (0,)), ((), ())),
                preferred_element_type=jnp.float32,
            )
        )
    shares = lax.psum_scatter(
        jnp.concatenate(blocks, axis=1).astype(jnp.bfloat16),
        "space",
        scatter_dimension=0,
        tiled=True,
    )
    weight_grad = lax.psum(shares, "rep").astype(jnp.float32)
    return (mesh_final[None], grid_grad[None], weight_grad)


F32 = jnp.float32
BF16 = jnp.bfloat16
INDEX_ROWS = 16
SAMPLE_EDGE_BYTES = 8 << 20


def dot(left, right):
    return jnp.dot(left, right, preferred_element_type=F32)


def dot_first(left, right):
    return lax.dot_general(left, right, (((0,), (0,)), ((), ())), preferred_element_type=F32)


def one_hot(labels, count):
    rows = lax.broadcasted_iota(jnp.int32, (count, labels.shape[-1]), 0)
    return (rows == labels).astype(F32).astype(BF16)


def row_moments(values):
    centred = values - jnp.mean(values, -1, keepdims=True)
    return centred, lax.rsqrt(jnp.mean(centred * centred, -1, keepdims=True) + EPSILON)


def moments_back(normed, scaled, upstream):
    return scaled * (
        upstream
        - jnp.mean(upstream, -1, keepdims=True)
        - normed * jnp.mean(upstream * normed, -1, keepdims=True)
    )


def fetch(pairs, semaphores):
    copies = [
        pltpu.make_async_copy(source, target, semaphores.at[n])
        for n, (source, target) in enumerate(pairs)
    ]
    for copy in copies:
        copy.start()
    for copy in copies:
        copy.wait()


def pack_kernel(*refs):
    sources, packed_ref, index_ref = refs[:8], refs[8], refs[9]
    local, semaphores = refs[10:18], refs[18]
    fetch(list(zip(sources, local)), semaphores)
    (
        grid_ref,
        mesh_ref,
        g2m_pick_ref,
        g2m_sender_ref,
        g2m_receiver_ref,
        m2m_pick_ref,
        m2m_sender_ref,
        m2m_receiver_ref,
    ) = local
    lists, _, capacity = g2m_pick_ref.shape
    mesh_count = mesh_ref.shape[1]
    regions, mesh_cap = m2m_pick_ref.shape[1:]
    edges = g2m_sender_ref.shape[1]
    grid_rows = grid_ref[0]
    for i in range(lists):
        picked = one_hot(g2m_pick_ref[i], grid_rows.shape[0])
        packed_ref[i * capacity : (i + 1) * capacity, :] = dot_first(picked, grid_rows).astype(BF16)
    first = lists * capacity
    packed_ref[first : first + mesh_count, :] = mesh_ref[0]
    index_ref[...] = jnp.zeros_like(index_ref)
    index_ref[0:1, 0:edges] = g2m_sender_ref[...].astype(F32)
    index_ref[0:1, edges : 2 * edges] = g2m_receiver_ref[...].astype(F32)
    index_ref[1:2, 0:edges] = m2m_sender_ref[...].astype(F32)
    index_ref[1:2, edges : 2 * edges] = m2m_receiver_ref[...].astype(F32)
    slots = regions * mesh_cap
    lane = lax.broadcasted_iota(jnp.int32, (mesh_cap, slots), 1)
    spread = (lane % mesh_cap == lax.broadcasted_iota(jnp.int32, (mesh_cap, slots), 0)).astype(F32)
    spread = dot(m2m_pick_ref[0].astype(F32).astype(BF16), spread.astype(BF16))
    lane = lax.broadcasted_iota(jnp.int32, (regions, slots), 1)
    owned = lane // mesh_cap == lax.broadcasted_iota(jnp.int32, (regions, slots), 0)
    index_ref[2:3, 0:slots] = jnp.sum(jnp.where(owned, spread, 0.0), 0, keepdims=True)
    packed_ref[first + mesh_count :, :] = index_ref[...].astype(BF16)


def weights_kernel(source_ref, weights_ref, turned_ref, semaphores):
    fetch([(source_ref, weights_ref)], semaphores)
    latent = weights_ref.shape[0]
    for n, block in enumerate((0, 2, 3)):
        turned_ref[:, n * latent : (n + 1) * latent] = weights_ref[
            :, block * latent : (block + 1) * latent
        ].T


def edge_forward(table, hot, hot_receiver, slope_ref, first):
    activation = dot_first(hot, table)
    squash = 0.5 + 0.5 * jnp.tanh(0.5 * activation)
    message = activation * squash
    slope_ref[first : first + activation.shape[0], :] = (
        squash + message * (1.0 - squash)
    ).astype(BF16)
    return dot(hot_receiver, message.astype(BF16))


def forward_kernel(
    regions,
    listed,
    mesh_count,
    mesh_cap,
    *refs,
):
    packed_refs = refs[:regions]
    (
        weights_ref,
        mesh_out_ref,
        grid_ref,
        mesh_ref,
        first_ref,
        sent_ref,
        index_ref,
        slope_one_ref,
        slope_two_ref,
        normed_one_ref,
        scaled_one_ref,
        normed_two_ref,
        scaled_two_ref,
        packed_index,
    ) = refs[regions:]
    latent = weights_ref.shape[0]
    edges = slope_one_ref.shape[0] // regions
    capacity = listed // 3
    slots = regions * mesh_cap
    me = lax.axis_index("space")
    for back, packed_ref in enumerate(packed_refs):
        region = lax.bitwise_xor(me, back)
        at = lambda rows: pl.ds(pl.multiple_of(region * rows, rows), rows)
        grid_ref[at(listed), :] = packed_ref[:listed, :]
        mesh_ref[at(mesh_count), :] = packed_ref[listed : listed + mesh_count, :]
        packed_index[at(INDEX_ROWS), :] = packed_ref[listed + mesh_count :, :]
    index_ref[...] = packed_index[...].astype(F32).astype(jnp.int32)

    grid_proj = dot(grid_ref[...], weights_ref[:, :latent])
    mesh_proj = dot(mesh_ref[...], weights_ref[:, latent : 2 * latent])
    blank = jnp.zeros((capacity, latent), F32)
    for d in range(regions):
        hot_sender = one_hot(index_ref[d * INDEX_ROWS : d * INDEX_ROWS + 1, :edges], listed)
        hot_receiver = one_hot(
            index_ref[d * INDEX_ROWS : d * INDEX_ROWS + 1, edges:], mesh_count
        )
        before = (d - 1) * listed + 2 * capacity
        within = d * listed + capacity
        after = (d + 1) * listed
        table = jnp.concatenate(
            [
                grid_proj[before : before + capacity] if d > 0 else blank,
                grid_proj[within : within + capacity],
                grid_proj[after : after + capacity] if d < regions - 1 else blank,
                mesh_proj[d * mesh_count : (d + 1) * mesh_count],
            ],
            axis=0,
        ).astype(BF16)
        summed = edge_forward(
            table,
            jnp.concatenate([hot_sender, hot_receiver], axis=0),
            hot_receiver,
            slope_one_ref,
            d * edges,
        )
        centred, scaled = row_moments(summed)
        normed = centred * scaled
        rows = slice(d * mesh_count, (d + 1) * mesh_count)
        normed_one_ref[rows, :] = normed
        scaled_one_ref[rows, :] = jnp.broadcast_to(scaled, (mesh_count, scaled_one_ref.shape[1]))
        first_ref[rows, :] = (mesh_ref[rows, :].astype(F32) + normed).astype(BF16)

    for s in range(regions):
        hot = one_hot(index_ref[s * INDEX_ROWS + 2 : s * INDEX_ROWS + 3, :slots], mesh_count)
        sent_ref[s * slots : (s + 1) * slots, :] = dot_first(
            hot, first_ref[s * mesh_count : (s + 1) * mesh_count, :]
        ).astype(BF16)
    sent_proj = dot(sent_ref[...], weights_ref[:, 2 * latent : 3 * latent])
    first_proj = dot(first_ref[...], weights_ref[:, 3 * latent :])
    for d in range(regions):
        hot_sender = one_hot(index_ref[d * INDEX_ROWS + 1 : d * INDEX_ROWS + 2, :edges], slots)
        hot_receiver = one_hot(
            index_ref[d * INDEX_ROWS + 1 : d * INDEX_ROWS + 2, edges:], mesh_count
        )
        pieces = [
            sent_proj[s * slots + d * mesh_cap : s * slots + (d + 1) * mesh_cap]
            for s in range(regions)
        ]
        table = jnp.concatenate(
            pieces + [first_proj[d * mesh_count : (d + 1) * mesh_count]], axis=0
        ).astype(BF16)
        summed = edge_forward(
            table,
            jnp.concatenate([hot_sender, hot_receiver], axis=0),
            hot_receiver,
            slope_two_ref,
            d * edges,
        )
        centred, scaled = row_moments(summed)
        rows = slice(d * mesh_count, (d + 1) * mesh_count)
        normed_two_ref[rows, :] = centred * scaled
        scaled_two_ref[rows, :] = jnp.broadcast_to(scaled, (mesh_count, scaled_two_ref.shape[1]))
    own = pl.ds(pl.multiple_of(me * mesh_count, mesh_count), mesh_count)
    mesh_out_ref[0] = (first_ref[own, :].astype(F32) + normed_two_ref[own, :]).astype(BF16)


def edge_backward(agg_grad, hot, hot_receiver, slope):
    edge_grad = (dot_first(hot_receiver, agg_grad) * slope.astype(F32)).astype(BF16)
    return dot(hot, edge_grad)


def halve(share_ref, keep_ref, give_ref):
    half = keep_ref.shape[0]
    core = lax.bitwise_and(lax.axis_index("rep"), 1)
    keep_ref[...] = share_ref[pl.ds(pl.multiple_of(core * half, half), half), :]
    give_ref[...] = share_ref[pl.ds(pl.multiple_of((1 - core) * half, half), half), :]


def process_back_kernel(regions, mesh_cap, *refs):
    cotangent_refs = refs[:regions]
    (
        turned_ref,
        first_ref,
        sent_ref,
        index_ref,
        slope_ref,
        normed_ref,
        scaled_ref,
        mesh_grad_ref,
        keep_ref,
        give_ref,
        upstream_ref,
        slot_ref,
        recv_ref,
        share_ref,
    ) = refs[regions:]
    latent = first_ref.shape[1]
    mesh_count = first_ref.shape[0] // regions
    edges = slope_ref.shape[0] // regions
    slots = regions * mesh_cap
    me = lax.axis_index("space")
    for back, cotangent_ref in enumerate(cotangent_refs):
        region = lax.bitwise_xor(me, back)
        at = pl.ds(pl.multiple_of(region * mesh_count, mesh_count), mesh_count)
        upstream_ref[at, :] = cotangent_ref[0].astype(F32)
    agg_grad = moments_back(normed_ref[...], scaled_ref[:, 0:1], upstream_ref[...]).astype(BF16)
    for d in range(regions):
        labels = slice(d * INDEX_ROWS + 1, d * INDEX_ROWS + 2)
        hot_sender = one_hot(index_ref[labels, :edges], slots)
        hot_receiver = one_hot(index_ref[labels, edges:], mesh_count)
        rows = slice(d * mesh_count, (d + 1) * mesh_count)
        sums = edge_backward(
            agg_grad[rows],
            jnp.concatenate([hot_sender, hot_receiver], axis=0),
            hot_receiver,
            slope_ref[d * edges : (d + 1) * edges, :],
        )
        for s in range(regions):
            first = s * slots + d * mesh_cap
            slot_ref[first : first + mesh_cap, :] = sums[s * mesh_cap : (s + 1) * mesh_cap]
        recv_ref[rows, :] = sums[slots:].astype(BF16)
    slot_sum = slot_ref[...].astype(BF16)
    columns = share_ref.shape[0]
    mine = pl.ds(pl.multiple_of(me * columns, columns), columns)
    share_ref[:, :latent] = dot_first(sent_ref[:, mine], slot_sum).astype(BF16)
    share_ref[:, latent:] = dot_first(first_ref[:, mine], recv_ref[...]).astype(BF16)
    halve(share_ref, keep_ref, give_ref)
    returned = dot(slot_sum, turned_ref[:, latent : 2 * latent]).astype(BF16)
    grad = upstream_ref[...] + dot(recv_ref[...], turned_ref[:, 2 * latent :])
    for s in range(regions):
        hot = one_hot(index_ref[s * INDEX_ROWS + 2 : s * INDEX_ROWS + 3, :slots], mesh_count)
        rows = slice(s * mesh_count, (s + 1) * mesh_count)
        mesh_grad_ref[rows, :] = grad[rows] + dot(hot, returned[s * slots : (s + 1) * slots])


def encode_back_kernel(
    regions,
    grid_ref,
    mesh_ref,
    index_ref,
    slope_ref,
    normed_ref,
    scaled_ref,
    mesh_grad_ref,
    own_slot_ref,
    keep_ref,
    give_ref,
    slot_ref,
    recv_ref,
    share_ref,
):
    latent = mesh_ref.shape[1]
    mesh_count = mesh_ref.shape[0] // regions
    listed = grid_ref.shape[0] // regions
    capacity = listed // 3
    edges = slope_ref.shape[0] // regions
    me = lax.axis_index("space")
    agg_grad = moments_back(normed_ref[...], scaled_ref[:, 0:1], mesh_grad_ref[...]).astype(BF16)
    blank = jnp.zeros((capacity, latent), BF16)
    slot_ref[0:capacity, :] = blank
    slot_ref[regions * listed - capacity :, :] = blank
    for d in range(regions):
        labels = slice(d * INDEX_ROWS, d * INDEX_ROWS + 1)
        hot_sender = one_hot(index_ref[labels, :edges], listed)
        hot_receiver = one_hot(index_ref[labels, edges:], mesh_count)
        rows = slice(d * mesh_count, (d + 1) * mesh_count)
        sums = edge_backward(
            agg_grad[rows],
            jnp.concatenate([hot_sender, hot_receiver], axis=0),
            hot_receiver,
            slope_ref[d * edges : (d + 1) * edges, :],
        ).astype(BF16)
        for j in range(3):
            source = d + j - 1
            if 0 <= source < regions:
                first = source * listed + (2 - j) * capacity
                slot_ref[first : first + capacity, :] = sums[j * capacity : (j + 1) * capacity]
        recv_ref[rows, :] = sums[listed:]
    columns = share_ref.shape[0]
    mine = pl.ds(pl.multiple_of(me * columns, columns), columns)
    share_ref[:, :latent] = dot_first(grid_ref[:, mine], slot_ref[...]).astype(BF16)
    share_ref[:, latent:] = dot_first(mesh_ref[:, mine], recv_ref[...]).astype(BF16)
    halve(share_ref, keep_ref, give_ref)
    own = pl.ds(pl.multiple_of(me * listed, listed), listed)
    own_slot_ref[...] = slot_ref[own, :]


def grid_back_kernel(turned_ref, pick_ref, own_slot_ref, grid_grad_ref):
    lists, _, capacity = pick_ref.shape
    latent = own_slot_ref.shape[1]
    returned = dot(own_slot_ref[...], turned_ref[:, :latent]).astype(BF16)
    total = None
    for i in range(lists):
        owner = one_hot(pick_ref[i], grid_grad_ref.shape[1])
        part = dot(owner, returned[i * capacity : (i + 1) * capacity])
        total = part if total is None else total + part
    grid_grad_ref[0] = total.astype(BF16)


def finish_kernel(one_ref, other_one_ref, two_ref, other_two_ref, weight_grad_ref):
    half, width = one_ref.shape
    core = lax.bitwise_and(lax.axis_index("rep"), 1)
    mine = pl.ds(pl.multiple_of(core * half, half), half)
    other = pl.ds(pl.multiple_of((1 - core) * half, half), half)
    weight_grad_ref[mine, :width] = one_ref[...].astype(F32)
    weight_grad_ref[other, :width] = other_one_ref[...].astype(F32)
    weight_grad_ref[mine, width:] = two_ref[...].astype(F32)
    weight_grad_ref[other, width:] = other_two_ref[...].astype(F32)


VMEM = pl.BlockSpec(memory_space=pltpu.VMEM)


def call(kernel, operands, outputs, scratch, flops, fetched=0, megabytes=40):
    hbm = pl.BlockSpec(memory_space=pltpu.HBM)
    return pl.pallas_call(
        kernel,
        out_shape=[jax.ShapeDtypeStruct(shape, kind) for shape, kind in outputs],
        in_specs=[hbm] * fetched + [VMEM] * (len(operands) - fetched),
        out_specs=[VMEM] * len(outputs),
        scratch_shapes=[pltpu.VMEM(shape, kind) for shape, kind in scratch]
        + ([pltpu.SemaphoreType.DMA((fetched,))] if fetched else []),
        compiler_params=pltpu.CompilerParams(vmem_limit_bytes=megabytes << 20),
        cost_estimate=pl.CostEstimate(flops=flops, bytes_accessed=4 << 20, transcendentals=0),
    )(*operands)


def swap(block, axis, bits):
    return lax.ppermute(block, axis, [(i, i ^ bits) for i in range(lax.axis_size(axis))])


def added(left, right):
    return (left.astype(F32) + right.astype(F32)).astype(BF16)


def summed_half(keep, give):
    half = added(keep, swap(give, "rep", 1))
    bit = 2
    while bit < lax.axis_size("rep"):
        half = added(half, swap(half, "rep", bit))
        bit *= 2
    return half, swap(half, "rep", 1)


def whole_sample_body(
    grid_latent,
    mesh_latent,
    mesh_cotangent,
    weights,
    g2m_pick,
    g2m_sender,
    g2m_receiver,
    m2m_pick,
    m2m_sender,
    m2m_receiver,
):
    regions = lax.axis_size("space")
    latent = weights.shape[0]
    listed = g2m_pick.shape[1] * g2m_pick.shape[2]
    mesh_count = mesh_latent.shape[1]
    mesh_cap = m2m_pick.shape[2]
    edges = g2m_sender.shape[0]
    columns = latent // regions
    half = columns // 2
    g2m_pick = g2m_pick.transpose(1, 0, 2)
    sources = (
        grid_latent,
        mesh_latent,
        g2m_pick,
        g2m_sender.reshape(1, -1),
        g2m_receiver.reshape(1, -1),
        m2m_pick,
        m2m_sender.reshape(1, -1),
        m2m_receiver.reshape(1, -1),
    )
    packed = call(
        pack_kernel,
        sources,
        [((listed + mesh_count + INDEX_ROWS, latent), BF16)],
        [((INDEX_ROWS, latent), F32)] + [(source.shape, source.dtype) for source in sources],
        10**7,
        fetched=len(sources),
        megabytes=56,
    )[0]
    packed, cotangent, weights = lax.optimization_barrier((packed, mesh_cotangent, weights))
    steps = sorted(range(1, regions), key=lambda step: -step)
    packs = {step: swap(packed, "space", step) for step in steps}
    cotangents = {1: swap(cotangent, "space", 1)}
    weights, turned = call(
        weights_kernel,
        (weights,),
        [(weights.shape, BF16), ((latent, 3 * latent), BF16)],
        [],
        10**8,
        fetched=1,
    )
    *packs, cotangent = lax.optimization_barrier(
        [packed] + [packs[step] for step in range(1, regions)] + [cotangent]
    )
    for step in steps:
        if step > 1:
            cotangents[step] = swap(cotangent, "space", step)
    cotangents = [cotangent] + [cotangents[step] for step in range(1, regions)]
    rows = regions * mesh_count
    (
        mesh_out,
        grid_all,
        mesh_all,
        mesh_first,
        mesh_sent,
        index,
        slope_one,
        slope_two,
        normed_one,
        scaled_one,
        normed_two,
        scaled_two,
    ) = call(
        functools.partial(forward_kernel, regions, listed, mesh_count, mesh_cap),
        (*packs, weights),
        [
            (mesh_latent.shape, BF16),
            ((regions * listed, latent), BF16),
            ((rows, latent), BF16),
            ((rows, latent), BF16),
            ((regions * regions * mesh_cap, latent), BF16),
            ((regions * INDEX_ROWS, latent), jnp.int32),
            ((regions * edges, latent), BF16),
            ((regions * edges, latent), BF16),
            ((rows, latent), F32),
            ((rows, 128), F32),
            ((rows, latent), F32),
            ((rows, 128), F32),
        ],
        [((regions * INDEX_ROWS, latent), BF16)],
        2 * 10**9,
    )
    mesh_grad, keep_two, give_two = call(
        functools.partial(process_back_kernel, regions, mesh_cap),
        (
            *cotangents,
            turned,
            mesh_first,
            mesh_sent,
            index,
            slope_two,
            normed_two,
            scaled_two,
        ),
        [((rows, latent), F32)] + [((half, 2 * latent), BF16)] * 2,
        [
            ((rows, latent), F32),
            ((regions * regions * mesh_cap, latent), F32),
            ((rows, latent), BF16),
            ((columns, 2 * latent), BF16),
        ],
        10**9,
    )
    own_slots, keep_one, give_one = call(
        functools.partial(encode_back_kernel, regions),
        (
            grid_all,
            mesh_all,
            index,
            slope_one,
            normed_one,
            scaled_one,
            mesh_grad,
        ),
        [((listed, latent), BF16)] + [((half, 2 * latent), BF16)] * 2,
        [
            ((regions * listed, latent), BF16),
            ((rows, latent), BF16),
            ((columns, 2 * latent), BF16),
        ],
        10**9,
    )
    grid_grad = call(
        grid_back_kernel,
        (turned, g2m_pick, own_slots),
        [(grid_latent.shape, BF16)],
        [],
        10**8,
    )[0]
    weight_grad = call(
        finish_kernel,
        (*summed_half(keep_one, give_one), *summed_half(keep_two, give_two)),
        [((columns, 4 * latent), F32)],
        [],
        10**6,
    )[0]
    return (mesh_out, grid_grad, weight_grad)


def solution(mesh):
    regions = mesh.shape["space"]
    samples = mesh.shape["rep"]

    def whole(*arguments):
        edges = arguments[5].shape[0] + arguments[8].shape[0]
        latent = arguments[3].shape[0]
        fits = edges * latent * 4 <= SAMPLE_EDGE_BYTES and latent % (128 * regions) == 0
        paired = all(n > 1 and n & (n - 1) == 0 for n in (regions, samples))
        return sharded(whole_sample_body if fits and paired else partitioned_body)(*arguments)

    def sharded(body):
        return jax.shard_map(
            body,
            mesh=mesh,
            in_specs=(
                P(("groups", "rep"), "space", None),
                P(("groups", "rep"), "space", None),
                P(("groups", "rep"), "space", None),
                P(),
                P("space", None, None),
                P("space"),
                P("space"),
                P("space", None, None),
                P("space"),
                P("space"),
            ),
            out_specs=(
                P(("groups", "rep"), "space", None),
                P(("groups", "rep"), "space", None),
                P(("groups", "space"), None),
            ),
            check_vma=False,
        )

    return whole
```

```python
import functools

import jax
import jax.numpy as jnp
from jax import lax
from jax.experimental import pallas as pl
from jax.experimental.pallas import tpu as pltpu
from jax.sharding import PartitionSpec as P

EPSILON = 1e-05


def with_halo(cells, sides, width):
    for axis, dim in sides:
        count = lax.axis_size(axis)
        ends = count - 1
        head = lax.slice_in_dim(cells, 0, width, axis=dim)
        tail = lax.slice_in_dim(cells, cells.shape[dim] - width, cells.shape[dim], axis=dim)
        cells = jnp.concatenate(
            [
                lax.ppermute(tail, axis, [(i, (i + 1) % count) for i in range(ends)]),
                cells,
                lax.ppermute(head, axis, [((i + 1) % count, i) for i in range(ends)]),
            ],
            axis=dim,
        )
    return cells


def swish(values):
    return values * jax.nn.sigmoid(values)


def swish_slope(values):
    squash = jax.nn.sigmoid(values)
    return squash * (1.0 + values * (1.0 - squash))


def norm_rows(values):
    centred = values - jnp.mean(values, -1, keepdims=True)
    return centred * lax.rsqrt(jnp.mean(centred * centred, -1, keepdims=True) + EPSILON)


def norm_rows_back(values, upstream):
    centred = values - jnp.mean(values, -1, keepdims=True)
    scaled = lax.rsqrt(jnp.mean(centred * centred, -1, keepdims=True) + EPSILON)
    normed = centred * scaled
    return scaled * (
        upstream
        - jnp.mean(upstream, -1, keepdims=True)
        - normed * jnp.mean(upstream * normed, -1, keepdims=True)
    )


def slot_rows(pick_row):
    listed = pick_row.reshape(-1)
    return listed


def mesh_route(outgoing, capacity, peer_count):
    columns = outgoing.shape[1]
    pieces = lax.all_to_all(
        outgoing.reshape(peer_count, capacity, columns),
        "space",
        split_axis=0,
        concat_axis=0,
        tiled=True,
    )
    arrived = pieces.reshape(peer_count * capacity, columns)
    return arrived


def grid_route(outgoing, capacity):
    columns = outgoing.shape[1]
    lists = outgoing.reshape(3, capacity, columns)
    rims = with_halo(jnp.stack([lists[0], lists[2]]), (("space", 0),), 1)
    return jnp.concatenate([rims[0], lists[1], rims[3]], axis=0)


def edge_pass(arrived, recv_table, located, receiver, w_send, w_recv):
    recv_proj = jnp.dot(recv_table, w_recv, preferred_element_type=jnp.float32)
    slot_proj = jnp.dot(arrived, w_send, preferred_element_type=jnp.float32)
    activation = slot_proj[located] + recv_proj[receiver]
    message = swish(activation).astype(jnp.bfloat16)
    member = (
        receiver[None, :] == jnp.arange(recv_table.shape[0], dtype=jnp.int32)[:, None]
    ).astype(jnp.bfloat16)
    summed = jnp.dot(member, message, preferred_element_type=jnp.float32)
    return (activation, member, summed)


def backward_pass(slot_count, located, activation, member, receiver, agg_grad, w_send):
    edge_grad = (agg_grad[receiver] * swish_slope(activation)).astype(jnp.bfloat16)
    recv_sum = jnp.dot(member, edge_grad, preferred_element_type=jnp.float32).astype(jnp.bfloat16)
    slot_member = (located[None, :] == jnp.arange(slot_count, dtype=jnp.int32)[:, None]).astype(
        jnp.bfloat16
    )
    slot_sum = jnp.dot(slot_member, edge_grad, preferred_element_type=jnp.float32).astype(
        jnp.bfloat16
    )
    returned = jnp.dot(slot_sum, w_send.T, preferred_element_type=jnp.float32).astype(jnp.bfloat16)
    return (recv_sum, slot_sum, returned)


def gather_back(listed, back_rows, row_count):
    owner = (listed[None, :] == jnp.arange(row_count, dtype=jnp.int32)[:, None]).astype(
        jnp.bfloat16
    )
    return jnp.dot(owner, back_rows, preferred_element_type=jnp.float32)


def partitioned_body(
    grid_latent,
    mesh_latent,
    mesh_cotangent,
    weights,
    g2m_pick,
    g2m_sender,
    g2m_receiver,
    m2m_pick,
    m2m_sender,
    m2m_receiver,
):
    grid_rows = grid_latent[0]
    mesh_rows = mesh_latent[0]
    upstream = mesh_cotangent[0].astype(jnp.float32)
    latent = weights.shape[0]
    encode_sender = weights[:, :latent]
    encode_receiver = weights[:, latent : 2 * latent]
    process_sender = weights[:, 2 * latent : 3 * latent]
    process_receiver = weights[:, 3 * latent :]
    peer_count = lax.axis_size("space")
    grid_cap = g2m_pick.shape[2]
    mesh_cap = m2m_pick.shape[2]
    grid_listed = g2m_pick[0].reshape(-1)
    grid_arrived = grid_route(grid_rows[grid_listed], grid_cap)
    act_first, member_first, summed_first = edge_pass(
        grid_arrived, mesh_rows, g2m_sender, g2m_receiver, encode_sender, encode_receiver
    )
    mesh_first = (mesh_rows.astype(jnp.float32) + norm_rows(summed_first)).astype(jnp.bfloat16)
    mesh_listed = slot_rows(m2m_pick[0])
    mesh_arrived = mesh_route(mesh_first[mesh_listed], mesh_cap, peer_count)
    act_second, member_second, summed_second = edge_pass(
        mesh_arrived, mesh_first, m2m_sender, m2m_receiver, process_sender, process_receiver
    )
    mesh_final = (mesh_first.astype(jnp.float32) + norm_rows(summed_second)).astype(jnp.bfloat16)
    agg_second = norm_rows_back(summed_second, upstream)
    recv_second, slot_second, returned_second = backward_pass(
        mesh_arrived.shape[0],
        m2m_sender,
        act_second,
        member_second,
        m2m_receiver,
        agg_second,
        process_sender,
    )
    back_second = mesh_route(returned_second, mesh_cap, peer_count)
    mesh_grad = upstream + jnp.dot(
        recv_second, process_receiver.T, preferred_element_type=jnp.float32
    )
    mesh_grad = mesh_grad + gather_back(mesh_listed, back_second, mesh_rows.shape[0])
    agg_first = norm_rows_back(summed_first, mesh_grad)
    recv_first, slot_first, returned_first = backward_pass(
        grid_arrived.shape[0],
        g2m_sender,
        act_first,
        member_first,
        g2m_receiver,
        agg_first,
        encode_sender,
    )
    back_first = grid_route(returned_first, grid_cap)
    grid_grad = gather_back(grid_listed, back_first, grid_rows.shape[0]).astype(jnp.bfloat16)
    factor_pairs = (
        (grid_arrived, slot_first),
        (mesh_rows, recv_first),
        (mesh_arrived, slot_second),
        (mesh_first, recv_second),
    )
    blocks = []
    for first_factor, second_factor in factor_pairs:
        blocks.append(
            lax.dot_general(
                first_factor,
                second_factor,
                (((0,), (0,)), ((), ())),
                preferred_element_type=jnp.float32,
            )
        )
    shares = lax.psum_scatter(
        jnp.concatenate(blocks, axis=1).astype(jnp.bfloat16),
        "space",
        scatter_dimension=0,
        tiled=True,
    )
    weight_grad = lax.psum(shares, "rep").astype(jnp.float32)
    return (mesh_final[None], grid_grad[None], weight_grad)


F32 = jnp.float32
BF16 = jnp.bfloat16
INDEX_ROWS = 16
SAMPLE_EDGE_BYTES = 8 << 20


def dot(left, right):
    return jnp.dot(left, right, preferred_element_type=F32)


def dot_first(left, right):
    return lax.dot_general(left, right, (((0,), (0,)), ((), ())), preferred_element_type=F32)


def one_hot(labels, count):
    rows = lax.broadcasted_iota(jnp.int32, (count, labels.shape[-1]), 0)
    return (rows == labels).astype(F32).astype(BF16)


def row_moments(values):
    centred = values - jnp.mean(values, -1, keepdims=True)
    return centred, lax.rsqrt(jnp.mean(centred * centred, -1, keepdims=True) + EPSILON)


def moments_back(normed, scaled, upstream):
    return scaled * (
        upstream
        - jnp.mean(upstream, -1, keepdims=True)
        - normed * jnp.mean(upstream * normed, -1, keepdims=True)
    )


def fetch(pairs, semaphores):
    copies = [
        pltpu.make_async_copy(source, target, semaphores.at[n])
        for n, (source, target) in enumerate(pairs)
    ]
    for copy in copies:
        copy.start()
    for copy in copies:
        copy.wait()


def pack_kernel(*refs):
    sources, packed_ref, index_ref = refs[:7], refs[7], refs[8]
    local, semaphores = refs[9:16], refs[16]
    fetch(list(zip(sources, local)), semaphores)
    (
        grid_ref,
        g2m_pick_ref,
        g2m_sender_ref,
        g2m_receiver_ref,
        m2m_pick_ref,
        m2m_sender_ref,
        m2m_receiver_ref,
    ) = local
    lists, _, capacity = g2m_pick_ref.shape
    regions, mesh_cap = m2m_pick_ref.shape[1:]
    edges = g2m_sender_ref.shape[1]
    grid_rows = grid_ref[0]
    for i in range(lists):
        picked = one_hot(g2m_pick_ref[i], grid_rows.shape[0])
        packed_ref[i * capacity : (i + 1) * capacity, :] = dot_first(picked, grid_rows).astype(BF16)
    first = lists * capacity
    index_ref[...] = jnp.zeros_like(index_ref)
    index_ref[0:1, 0:edges] = g2m_sender_ref[...].astype(F32)
    index_ref[0:1, edges : 2 * edges] = g2m_receiver_ref[...].astype(F32)
    index_ref[1:2, 0:edges] = m2m_sender_ref[...].astype(F32)
    index_ref[1:2, edges : 2 * edges] = m2m_receiver_ref[...].astype(F32)
    slots = regions * mesh_cap
    lane = lax.broadcasted_iota(jnp.int32, (mesh_cap, slots), 1)
    spread = (lane % mesh_cap == lax.broadcasted_iota(jnp.int32, (mesh_cap, slots), 0)).astype(F32)
    spread = dot(m2m_pick_ref[0].astype(F32).astype(BF16), spread.astype(BF16))
    lane = lax.broadcasted_iota(jnp.int32, (regions, slots), 1)
    owned = lane // mesh_cap == lax.broadcasted_iota(jnp.int32, (regions, slots), 0)
    index_ref[2:3, 0:slots] = jnp.sum(jnp.where(owned, spread, 0.0), 0, keepdims=True)
    packed_ref[first:, :] = index_ref[...].astype(BF16)


def weights_kernel(source_ref, weights_ref, turned_ref, semaphores):
    fetch([(source_ref, weights_ref)], semaphores)
    latent = weights_ref.shape[0]
    for n, block in enumerate((0, 2, 3)):
        turned_ref[:, n * latent : (n + 1) * latent] = weights_ref[
            :, block * latent : (block + 1) * latent
        ].T


def edge_forward(table, hot, hot_receiver, slope_ref, first):
    activation = dot_first(hot, table)
    squash = 0.5 + 0.5 * jnp.tanh(0.5 * activation)
    message = activation * squash
    slope_ref[first : first + activation.shape[0], :] = (
        squash + message * (1.0 - squash)
    ).astype(BF16)
    return dot(hot_receiver, message.astype(BF16))


def forward_kernel(
    regions,
    listed,
    mesh_count,
    mesh_cap,
    *refs,
):
    packed_refs, latent_refs = refs[:regions], refs[regions : 2 * regions]
    (
        weights_ref,
        mesh_out_ref,
        grid_ref,
        mesh_ref,
        first_ref,
        sent_ref,
        index_ref,
        slope_one_ref,
        slope_two_ref,
        normed_one_ref,
        scaled_one_ref,
        normed_two_ref,
        scaled_two_ref,
        packed_index,
    ) = refs[2 * regions :]
    latent = weights_ref.shape[0]
    edges = slope_one_ref.shape[0] // regions
    capacity = listed // 3
    slots = regions * mesh_cap
    me = lax.axis_index("space")
    for back, (packed_ref, latent_ref) in enumerate(zip(packed_refs, latent_refs)):
        region = lax.bitwise_xor(me, back)
        at = lambda rows: pl.ds(pl.multiple_of(region * rows, rows), rows)
        grid_ref[at(listed), :] = packed_ref[:listed, :]
        mesh_ref[at(mesh_count), :] = latent_ref[0]
        packed_index[at(INDEX_ROWS), :] = packed_ref[listed:, :]
    index_ref[...] = packed_index[...].astype(F32).astype(jnp.int32)

    grid_proj = dot(grid_ref[...], weights_ref[:, :latent])
    mesh_proj = dot(mesh_ref[...], weights_ref[:, latent : 2 * latent])
    blank = jnp.zeros((capacity, latent), F32)
    for d in range(regions):
        hot_sender = one_hot(index_ref[d * INDEX_ROWS : d * INDEX_ROWS + 1, :edges], listed)
        hot_receiver = one_hot(
            index_ref[d * INDEX_ROWS : d * INDEX_ROWS + 1, edges:], mesh_count
        )
        before = (d - 1) * listed + 2 * capacity
        within = d * listed + capacity
        after = (d + 1) * listed
        table = jnp.concatenate(
            [
                grid_proj[before : before + capacity] if d > 0 else blank,
                grid_proj[within : within + capacity],
                grid_proj[after : after + capacity] if d < regions - 1 else blank,
                mesh_proj[d * mesh_count : (d + 1) * mesh_count],
            ],
            axis=0,
        ).astype(BF16)
        summed = edge_forward(
            table,
            jnp.concatenate([hot_sender, hot_receiver], axis=0),
            hot_receiver,
            slope_one_ref,
            d * edges,
        )
        centred, scaled = row_moments(summed)
        normed = centred * scaled
        rows = slice(d * mesh_count, (d + 1) * mesh_count)
        normed_one_ref[rows, :] = normed
        scaled_one_ref[rows, :] = jnp.broadcast_to(scaled, (mesh_count, scaled_one_ref.shape[1]))
        first_ref[rows, :] = (mesh_ref[rows, :].astype(F32) + normed).astype(BF16)

    for s in range(regions):
        hot = one_hot(index_ref[s * INDEX_ROWS + 2 : s * INDEX_ROWS + 3, :slots], mesh_count)
        sent_ref[s * slots : (s + 1) * slots, :] = dot_first(
            hot, first_ref[s * mesh_count : (s + 1) * mesh_count, :]
        ).astype(BF16)
    sent_proj = dot(sent_ref[...], weights_ref[:, 2 * latent : 3 * latent])
    first_proj = dot(first_ref[...], weights_ref[:, 3 * latent :])
    for d in range(regions):
        hot_sender = one_hot(index_ref[d * INDEX_ROWS + 1 : d * INDEX_ROWS + 2, :edges], slots)
        hot_receiver = one_hot(
            index_ref[d * INDEX_ROWS + 1 : d * INDEX_ROWS + 2, edges:], mesh_count
        )
        pieces = [
            sent_proj[s * slots + d * mesh_cap : s * slots + (d + 1) * mesh_cap]
            for s in range(regions)
        ]
        table = jnp.concatenate(
            pieces + [first_proj[d * mesh_count : (d + 1) * mesh_count]], axis=0
        ).astype(BF16)
        summed = edge_forward(
            table,
            jnp.concatenate([hot_sender, hot_receiver], axis=0),
            hot_receiver,
            slope_two_ref,
            d * edges,
        )
        centred, scaled = row_moments(summed)
        rows = slice(d * mesh_count, (d + 1) * mesh_count)
        normed_two_ref[rows, :] = centred * scaled
        scaled_two_ref[rows, :] = jnp.broadcast_to(scaled, (mesh_count, scaled_two_ref.shape[1]))
    own = pl.ds(pl.multiple_of(me * mesh_count, mesh_count), mesh_count)
    mesh_out_ref[0] = (first_ref[own, :].astype(F32) + normed_two_ref[own, :]).astype(BF16)


def edge_backward(agg_grad, hot, hot_receiver, slope):
    edge_grad = (dot_first(hot_receiver, agg_grad) * slope.astype(F32)).astype(BF16)
    return dot(hot, edge_grad)


def halve(share_ref, keep_ref, give_ref):
    half = keep_ref.shape[0]
    core = lax.bitwise_and(lax.axis_index("rep"), 1)
    keep_ref[...] = share_ref[pl.ds(pl.multiple_of(core * half, half), half), :]
    give_ref[...] = share_ref[pl.ds(pl.multiple_of((1 - core) * half, half), half), :]


def process_back_kernel(regions, mesh_cap, *refs):
    cotangent_refs = refs[:regions]
    (
        turned_ref,
        first_ref,
        sent_ref,
        index_ref,
        slope_ref,
        normed_ref,
        scaled_ref,
        mesh_grad_ref,
        keep_ref,
        give_ref,
        upstream_ref,
        slot_ref,
        recv_ref,
        share_ref,
    ) = refs[regions:]
    latent = first_ref.shape[1]
    mesh_count = first_ref.shape[0] // regions
    edges = slope_ref.shape[0] // regions
    slots = regions * mesh_cap
    me = lax.axis_index("space")
    for back, cotangent_ref in enumerate(cotangent_refs):
        region = lax.bitwise_xor(me, back)
        at = pl.ds(pl.multiple_of(region * mesh_count, mesh_count), mesh_count)
        upstream_ref[at, :] = cotangent_ref[0].astype(F32)
    agg_grad = moments_back(normed_ref[...], scaled_ref[:, 0:1], upstream_ref[...]).astype(BF16)
    for d in range(regions):
        labels = slice(d * INDEX_ROWS + 1, d * INDEX_ROWS + 2)
        hot_sender = one_hot(index_ref[labels, :edges], slots)
        hot_receiver = one_hot(index_ref[labels, edges:], mesh_count)
        rows = slice(d * mesh_count, (d + 1) * mesh_count)
        sums = edge_backward(
            agg_grad[rows],
            jnp.concatenate([hot_sender, hot_receiver], axis=0),
            hot_receiver,
            slope_ref[d * edges : (d + 1) * edges, :],
        )
        for s in range(regions):
            first = s * slots + d * mesh_cap
            slot_ref[first : first + mesh_cap, :] = sums[s * mesh_cap : (s + 1) * mesh_cap]
        recv_ref[rows, :] = sums[slots:].astype(BF16)
    slot_sum = slot_ref[...].astype(BF16)
    columns = share_ref.shape[0]
    mine = pl.ds(pl.multiple_of(me * columns, columns), columns)
    share_ref[:, :latent] = dot_first(sent_ref[:, mine], slot_sum).astype(BF16)
    share_ref[:, latent:] = dot_first(first_ref[:, mine], recv_ref[...]).astype(BF16)
    halve(share_ref, keep_ref, give_ref)
    returned = dot(slot_sum, turned_ref[:, latent : 2 * latent]).astype(BF16)
    grad = upstream_ref[...] + dot(recv_ref[...], turned_ref[:, 2 * latent :])
    for s in range(regions):
        hot = one_hot(index_ref[s * INDEX_ROWS + 2 : s * INDEX_ROWS + 3, :slots], mesh_count)
        rows = slice(s * mesh_count, (s + 1) * mesh_count)
        mesh_grad_ref[rows, :] = grad[rows] + dot(hot, returned[s * slots : (s + 1) * slots])


def encode_back_kernel(
    regions,
    grid_ref,
    mesh_ref,
    index_ref,
    slope_ref,
    normed_ref,
    scaled_ref,
    mesh_grad_ref,
    own_slot_ref,
    keep_ref,
    give_ref,
    slot_ref,
    recv_ref,
    share_ref,
):
    latent = mesh_ref.shape[1]
    mesh_count = mesh_ref.shape[0] // regions
    listed = grid_ref.shape[0] // regions
    capacity = listed // 3
    edges = slope_ref.shape[0] // regions
    me = lax.axis_index("space")
    agg_grad = moments_back(normed_ref[...], scaled_ref[:, 0:1], mesh_grad_ref[...]).astype(BF16)
    blank = jnp.zeros((capacity, latent), BF16)
    slot_ref[0:capacity, :] = blank
    slot_ref[regions * listed - capacity :, :] = blank
    for d in range(regions):
        labels = slice(d * INDEX_ROWS, d * INDEX_ROWS + 1)
        hot_sender = one_hot(index_ref[labels, :edges], listed)
        hot_receiver = one_hot(index_ref[labels, edges:], mesh_count)
        rows = slice(d * mesh_count, (d + 1) * mesh_count)
        sums = edge_backward(
            agg_grad[rows],
            jnp.concatenate([hot_sender, hot_receiver], axis=0),
            hot_receiver,
            slope_ref[d * edges : (d + 1) * edges, :],
        ).astype(BF16)
        for j in range(3):
            source = d + j - 1
            if 0 <= source < regions:
                first = source * listed + (2 - j) * capacity
                slot_ref[first : first + capacity, :] = sums[j * capacity : (j + 1) * capacity]
        recv_ref[rows, :] = sums[listed:]
    columns = share_ref.shape[0]
    mine = pl.ds(pl.multiple_of(me * columns, columns), columns)
    share_ref[:, :latent] = dot_first(grid_ref[:, mine], slot_ref[...]).astype(BF16)
    share_ref[:, latent:] = dot_first(mesh_ref[:, mine], recv_ref[...]).astype(BF16)
    halve(share_ref, keep_ref, give_ref)
    own = pl.ds(pl.multiple_of(me * listed, listed), listed)
    own_slot_ref[...] = slot_ref[own, :]


def grid_back_kernel(turned_ref, pick_ref, own_slot_ref, grid_grad_ref):
    lists, _, capacity = pick_ref.shape
    latent = own_slot_ref.shape[1]
    returned = dot(own_slot_ref[...], turned_ref[:, :latent]).astype(BF16)
    total = None
    for i in range(lists):
        owner = one_hot(pick_ref[i], grid_grad_ref.shape[1])
        part = dot(owner, returned[i * capacity : (i + 1) * capacity])
        total = part if total is None else total + part
    grid_grad_ref[0] = total.astype(BF16)


def place(pairs, stages, semaphores):
    copies = []
    for n, (block_ref, target) in enumerate(pairs):
        stages[n][...] = block_ref[...].astype(F32)
        copies.append(pltpu.make_async_copy(stages[n], target, semaphores.at[n]))
        copies[n].start()
    for copy in copies:
        copy.wait()


def half_rows(half):
    core = lax.bitwise_and(lax.axis_index("rep"), 1)
    mine = pl.ds(pl.multiple_of(core * half, half), half)
    return mine, pl.ds(pl.multiple_of((1 - core) * half, half), half)


def settle_kernel(one_ref, two_ref, other_two_ref, weight_grad_ref, *scratch):
    half, width = one_ref.shape
    mine, other = half_rows(half)
    place(
        [
            (two_ref, weight_grad_ref.at[mine, width:]),
            (other_two_ref, weight_grad_ref.at[other, width:]),
            (one_ref, weight_grad_ref.at[mine, :width]),
        ],
        scratch[:3],
        scratch[3],
    )


def finish_kernel(other_one_ref, settled_ref, weight_grad_ref, stage, semaphores):
    half, width = other_one_ref.shape
    _, other = half_rows(half)
    place([(other_one_ref, weight_grad_ref.at[other, :width])], [stage], semaphores)


VMEM = pl.BlockSpec(memory_space=pltpu.VMEM)


def call(kernel, operands, outputs, scratch, flops, fetched=0, megabytes=40):
    hbm = pl.BlockSpec(memory_space=pltpu.HBM)
    return pl.pallas_call(
        kernel,
        out_shape=[jax.ShapeDtypeStruct(shape, kind) for shape, kind in outputs],
        in_specs=[hbm] * fetched + [VMEM] * (len(operands) - fetched),
        out_specs=[VMEM] * len(outputs),
        scratch_shapes=[pltpu.VMEM(shape, kind) for shape, kind in scratch]
        + ([pltpu.SemaphoreType.DMA((fetched,))] if fetched else []),
        compiler_params=pltpu.CompilerParams(vmem_limit_bytes=megabytes << 20),
        cost_estimate=pl.CostEstimate(flops=flops, bytes_accessed=4 << 20, transcendentals=0),
    )(*operands)


def swap(block, axis, bits):
    return lax.ppermute(block, axis, [(i, i ^ bits) for i in range(lax.axis_size(axis))])


def added(left, right):
    return (left.astype(F32) + right.astype(F32)).astype(BF16)


def summed_half(keep, give):
    half = added(keep, swap(give, "rep", 1))
    bit = 2
    while bit < lax.axis_size("rep"):
        half = added(half, swap(half, "rep", bit))
        bit *= 2
    return half, swap(half, "rep", 1)


def whole_sample_body(
    grid_latent,
    mesh_latent,
    mesh_cotangent,
    weights,
    g2m_pick,
    g2m_sender,
    g2m_receiver,
    m2m_pick,
    m2m_sender,
    m2m_receiver,
):
    regions = lax.axis_size("space")
    latent = weights.shape[0]
    listed = g2m_pick.shape[1] * g2m_pick.shape[2]
    mesh_count = mesh_latent.shape[1]
    mesh_cap = m2m_pick.shape[2]
    edges = g2m_sender.shape[0]
    columns = latent // regions
    half = columns // 2
    g2m_pick = g2m_pick.transpose(1, 0, 2)
    sources = (
        grid_latent,
        g2m_pick,
        g2m_sender.reshape(1, -1),
        g2m_receiver.reshape(1, -1),
        m2m_pick,
        m2m_sender.reshape(1, -1),
        m2m_receiver.reshape(1, -1),
    )
    packed = call(
        pack_kernel,
        sources,
        [((listed + INDEX_ROWS, latent), BF16)],
        [((INDEX_ROWS, latent), F32)] + [(source.shape, source.dtype) for source in sources],
        10**7,
        fetched=len(sources),
        megabytes=56,
    )[0]
    steps = range(1, regions)
    latents = [mesh_latent] + [swap(mesh_latent, "space", step) for step in steps]
    packed, cotangent, weights = lax.optimization_barrier((packed, mesh_cotangent, weights))
    packs = [packed] + [swap(packed, "space", step) for step in steps]
    cotangents = [cotangent, swap(cotangent, "space", 1)]
    weights, turned = call(
        weights_kernel,
        (weights,),
        [(weights.shape, BF16), ((latent, 3 * latent), BF16)],
        [],
        10**8,
        fetched=1,
    )
    near = regions - 1
    *nearer, cotangent = lax.optimization_barrier(packs[:near] + latents[:near] + [cotangent])
    packs = nearer[:near] + packs[near:]
    latents = nearer[near:] + latents[near:]
    cotangents = cotangents + [swap(cotangent, "space", step) for step in steps if step > 1]
    rows = regions * mesh_count
    (
        mesh_out,
        grid_all,
        mesh_all,
        mesh_first,
        mesh_sent,
        index,
        slope_one,
        slope_two,
        normed_one,
        scaled_one,
        normed_two,
        scaled_two,
    ) = call(
        functools.partial(forward_kernel, regions, listed, mesh_count, mesh_cap),
        (*packs, *latents, weights),
        [
            (mesh_latent.shape, BF16),
            ((regions * listed, latent), BF16),
            ((rows, latent), BF16),
            ((rows, latent), BF16),
            ((regions * regions * mesh_cap, latent), BF16),
            ((regions * INDEX_ROWS, latent), jnp.int32),
            ((regions * edges, latent), BF16),
            ((regions * edges, latent), BF16),
            ((rows, latent), F32),
            ((rows, 128), F32),
            ((rows, latent), F32),
            ((rows, 128), F32),
        ],
        [((regions * INDEX_ROWS, latent), BF16)],
        2 * 10**9,
    )
    mesh_grad, keep_two, give_two = call(
        functools.partial(process_back_kernel, regions, mesh_cap),
        (
            *cotangents,
            turned,
            mesh_first,
            mesh_sent,
            index,
            slope_two,
            normed_two,
            scaled_two,
        ),
        [((rows, latent), F32)] + [((half, 2 * latent), BF16)] * 2,
        [
            ((rows, latent), F32),
            ((regions * regions * mesh_cap, latent), F32),
            ((rows, latent), BF16),
            ((columns, 2 * latent), BF16),
        ],
        10**9,
    )
    own_slots, keep_one, give_one = call(
        functools.partial(encode_back_kernel, regions),
        (
            grid_all,
            mesh_all,
            index,
            slope_one,
            normed_one,
            scaled_one,
            mesh_grad,
        ),
        [((listed, latent), BF16)] + [((half, 2 * latent), BF16)] * 2,
        [
            ((regions * listed, latent), BF16),
            ((rows, latent), BF16),
            ((columns, 2 * latent), BF16),
        ],
        10**9,
    )
    grid_grad = call(
        grid_back_kernel,
        (turned, g2m_pick, own_slots),
        [(grid_latent.shape, BF16)],
        [],
        10**8,
    )[0]
    one, other_one = summed_half(keep_one, give_one)
    two, other_two = summed_half(keep_two, give_two)
    hbm = pl.BlockSpec(memory_space=pltpu.HBM)
    stage = pltpu.VMEM((half, 2 * latent), F32)
    weight_shape = jax.ShapeDtypeStruct((columns, 4 * latent), F32)
    settled = pl.pallas_call(
        settle_kernel,
        out_shape=weight_shape,
        in_specs=[VMEM] * 3,
        out_specs=hbm,
        scratch_shapes=[stage] * 3 + [pltpu.SemaphoreType.DMA((3,))],
    )(one, two, other_two)
    weight_grad = pl.pallas_call(
        finish_kernel,
        out_shape=weight_shape,
        in_specs=[VMEM, hbm],
        out_specs=hbm,
        scratch_shapes=[stage, pltpu.SemaphoreType.DMA((1,))],
        input_output_aliases={1: 0},
    )(other_one, settled)
    return (mesh_out, grid_grad, weight_grad)


def solution(mesh):
    regions = mesh.shape["space"]
    samples = mesh.shape["rep"]

    def whole(*arguments):
        edges = arguments[5].shape[0] + arguments[8].shape[0]
        latent = arguments[3].shape[0]
        fits = edges * latent * 4 <= SAMPLE_EDGE_BYTES and latent % (128 * regions) == 0
        paired = all(n > 1 and n & (n - 1) == 0 for n in (regions, samples))
        return sharded(whole_sample_body if fits and paired else partitioned_body)(*arguments)

    def sharded(body):
        return jax.shard_map(
            body,
            mesh=mesh,
            in_specs=(
                P(("groups", "rep"), "space", None),
                P(("groups", "rep"), "space", None),
                P(("groups", "rep"), "space", None),
                P(),
                P("space", None, None),
                P("space"),
                P("space"),
                P("space", None, None),
                P("space"),
                P("space"),
            ),
            out_specs=(
                P(("groups", "rep"), "space", None),
                P(("groups", "rep"), "space", None),
                P(("groups", "space"), None),
            ),
            check_vma=False,
        )

    return whole
```

```python
import functools

import jax
import jax.numpy as jnp
from jax import lax
from jax.experimental import pallas as pl
from jax.experimental.pallas import tpu as pltpu
from jax.sharding import PartitionSpec as P

EPSILON = 1e-05


def with_halo(cells, sides, width):
    for axis, dim in sides:
        count = lax.axis_size(axis)
        ends = count - 1
        head = lax.slice_in_dim(cells, 0, width, axis=dim)
        tail = lax.slice_in_dim(cells, cells.shape[dim] - width, cells.shape[dim], axis=dim)
        cells = jnp.concatenate(
            [
                lax.ppermute(tail, axis, [(i, (i + 1) % count) for i in range(ends)]),
                cells,
                lax.ppermute(head, axis, [((i + 1) % count, i) for i in range(ends)]),
            ],
            axis=dim,
        )
    return cells


def swish(values):
    return values * jax.nn.sigmoid(values)


def swish_slope(values):
    squash = jax.nn.sigmoid(values)
    return squash * (1.0 + values * (1.0 - squash))


def norm_rows(values):
    centred = values - jnp.mean(values, -1, keepdims=True)
    return centred * lax.rsqrt(jnp.mean(centred * centred, -1, keepdims=True) + EPSILON)


def norm_rows_back(values, upstream):
    centred = values - jnp.mean(values, -1, keepdims=True)
    scaled = lax.rsqrt(jnp.mean(centred * centred, -1, keepdims=True) + EPSILON)
    normed = centred * scaled
    return scaled * (
        upstream
        - jnp.mean(upstream, -1, keepdims=True)
        - normed * jnp.mean(upstream * normed, -1, keepdims=True)
    )


def slot_rows(pick_row):
    listed = pick_row.reshape(-1)
    return listed


def mesh_route(outgoing, capacity, peer_count):
    columns = outgoing.shape[1]
    pieces = lax.all_to_all(
        outgoing.reshape(peer_count, capacity, columns),
        "space",
        split_axis=0,
        concat_axis=0,
        tiled=True,
    )
    arrived = pieces.reshape(peer_count * capacity, columns)
    return arrived


def grid_route(outgoing, capacity):
    columns = outgoing.shape[1]
    lists = outgoing.reshape(3, capacity, columns)
    rims = with_halo(jnp.stack([lists[0], lists[2]]), (("space", 0),), 1)
    return jnp.concatenate([rims[0], lists[1], rims[3]], axis=0)


def edge_pass(arrived, recv_table, located, receiver, w_send, w_recv):
    recv_proj = jnp.dot(recv_table, w_recv, preferred_element_type=jnp.float32)
    slot_proj = jnp.dot(arrived, w_send, preferred_element_type=jnp.float32)
    activation = slot_proj[located] + recv_proj[receiver]
    message = swish(activation).astype(jnp.bfloat16)
    member = (
        receiver[None, :] == jnp.arange(recv_table.shape[0], dtype=jnp.int32)[:, None]
    ).astype(jnp.bfloat16)
    summed = jnp.dot(member, message, preferred_element_type=jnp.float32)
    return (activation, member, summed)


def backward_pass(slot_count, located, activation, member, receiver, agg_grad, w_send):
    edge_grad = (agg_grad[receiver] * swish_slope(activation)).astype(jnp.bfloat16)
    recv_sum = jnp.dot(member, edge_grad, preferred_element_type=jnp.float32).astype(jnp.bfloat16)
    slot_member = (located[None, :] == jnp.arange(slot_count, dtype=jnp.int32)[:, None]).astype(
        jnp.bfloat16
    )
    slot_sum = jnp.dot(slot_member, edge_grad, preferred_element_type=jnp.float32).astype(
        jnp.bfloat16
    )
    returned = jnp.dot(slot_sum, w_send.T, preferred_element_type=jnp.float32).astype(jnp.bfloat16)
    return (recv_sum, slot_sum, returned)


def gather_back(listed, back_rows, row_count):
    owner = (listed[None, :] == jnp.arange(row_count, dtype=jnp.int32)[:, None]).astype(
        jnp.bfloat16
    )
    return jnp.dot(owner, back_rows, preferred_element_type=jnp.float32)


def partitioned_body(
    grid_latent,
    mesh_latent,
    mesh_cotangent,
    weights,
    g2m_pick,
    g2m_sender,
    g2m_receiver,
    m2m_pick,
    m2m_sender,
    m2m_receiver,
):
    grid_rows = grid_latent[0]
    mesh_rows = mesh_latent[0]
    upstream = mesh_cotangent[0].astype(jnp.float32)
    latent = weights.shape[0]
    encode_sender = weights[:, :latent]
    encode_receiver = weights[:, latent : 2 * latent]
    process_sender = weights[:, 2 * latent : 3 * latent]
    process_receiver = weights[:, 3 * latent :]
    peer_count = lax.axis_size("space")
    grid_cap = g2m_pick.shape[2]
    mesh_cap = m2m_pick.shape[2]
    grid_listed = g2m_pick[0].reshape(-1)
    grid_arrived = grid_route(grid_rows[grid_listed], grid_cap)
    act_first, member_first, summed_first = edge_pass(
        grid_arrived, mesh_rows, g2m_sender, g2m_receiver, encode_sender, encode_receiver
    )
    mesh_first = (mesh_rows.astype(jnp.float32) + norm_rows(summed_first)).astype(jnp.bfloat16)
    mesh_listed = slot_rows(m2m_pick[0])
    mesh_arrived = mesh_route(mesh_first[mesh_listed], mesh_cap, peer_count)
    act_second, member_second, summed_second = edge_pass(
        mesh_arrived, mesh_first, m2m_sender, m2m_receiver, process_sender, process_receiver
    )
    mesh_final = (mesh_first.astype(jnp.float32) + norm_rows(summed_second)).astype(jnp.bfloat16)
    agg_second = norm_rows_back(summed_second, upstream)
    recv_second, slot_second, returned_second = backward_pass(
        mesh_arrived.shape[0],
        m2m_sender,
        act_second,
        member_second,
        m2m_receiver,
        agg_second,
        process_sender,
    )
    back_second = mesh_route(returned_second, mesh_cap, peer_count)
    mesh_grad = upstream + jnp.dot(
        recv_second, process_receiver.T, preferred_element_type=jnp.float32
    )
    mesh_grad = mesh_grad + gather_back(mesh_listed, back_second, mesh_rows.shape[0])
    agg_first = norm_rows_back(summed_first, mesh_grad)
    recv_first, slot_first, returned_first = backward_pass(
        grid_arrived.shape[0],
        g2m_sender,
        act_first,
        member_first,
        g2m_receiver,
        agg_first,
        encode_sender,
    )
    back_first = grid_route(returned_first, grid_cap)
    grid_grad = gather_back(grid_listed, back_first, grid_rows.shape[0]).astype(jnp.bfloat16)
    factor_pairs = (
        (grid_arrived, slot_first),
        (mesh_rows, recv_first),
        (mesh_arrived, slot_second),
        (mesh_first, recv_second),
    )
    blocks = []
    for first_factor, second_factor in factor_pairs:
        blocks.append(
            lax.dot_general(
                first_factor,
                second_factor,
                (((0,), (0,)), ((), ())),
                preferred_element_type=jnp.float32,
            )
        )
    shares = lax.psum_scatter(
        jnp.concatenate(blocks, axis=1).astype(jnp.bfloat16),
        "space",
        scatter_dimension=0,
        tiled=True,
    )
    weight_grad = lax.psum(shares, "rep").astype(jnp.float32)
    return (mesh_final[None], grid_grad[None], weight_grad)


F32 = jnp.float32
BF16 = jnp.bfloat16
INDEX_ROWS = 16
FAR_STEP = 3
SAMPLE_EDGE_BYTES = 8 << 20


def dot(left, right):
    return jnp.dot(left, right, preferred_element_type=F32)


def dot_first(left, right):
    return lax.dot_general(left, right, (((0,), (0,)), ((), ())), preferred_element_type=F32)


def one_hot(labels, count):
    rows = lax.broadcasted_iota(jnp.int32, (count, labels.shape[-1]), 0)
    return (rows == labels).astype(F32).astype(BF16)


def row_moments(values):
    centred = values - jnp.mean(values, -1, keepdims=True)
    return centred, lax.rsqrt(jnp.mean(centred * centred, -1, keepdims=True) + EPSILON)


def moments_back(normed, scaled, upstream):
    return scaled * (
        upstream
        - jnp.mean(upstream, -1, keepdims=True)
        - normed * jnp.mean(upstream * normed, -1, keepdims=True)
    )


def fetch(pairs, semaphores):
    copies = [
        pltpu.make_async_copy(source, target, semaphores.at[n])
        for n, (source, target) in enumerate(pairs)
    ]
    for copy in copies:
        copy.start()
    for copy in copies:
        copy.wait()


def pack_kernel(*refs):
    sources, packed_ref, index_ref = refs[:8], refs[8], refs[9]
    local, semaphores = refs[10:18], refs[18]
    fetch(list(zip(sources, local)), semaphores)
    (
        grid_ref,
        mesh_ref,
        g2m_pick_ref,
        g2m_sender_ref,
        g2m_receiver_ref,
        m2m_pick_ref,
        m2m_sender_ref,
        m2m_receiver_ref,
    ) = local
    lists, _, capacity = g2m_pick_ref.shape
    mesh_count = mesh_ref.shape[1]
    regions, mesh_cap = m2m_pick_ref.shape[1:]
    edges = g2m_sender_ref.shape[1]
    grid_rows = grid_ref[0]
    for i in range(lists):
        picked = one_hot(g2m_pick_ref[i], grid_rows.shape[0])
        packed_ref[i * capacity : (i + 1) * capacity, :] = dot_first(picked, grid_rows).astype(BF16)
    first = lists * capacity
    packed_ref[first : first + mesh_count, :] = mesh_ref[0]
    index_ref[...] = jnp.zeros_like(index_ref)
    index_ref[0:1, 0:edges] = g2m_sender_ref[...].astype(F32)
    index_ref[0:1, edges : 2 * edges] = g2m_receiver_ref[...].astype(F32)
    index_ref[1:2, 0:edges] = m2m_sender_ref[...].astype(F32)
    index_ref[1:2, edges : 2 * edges] = m2m_receiver_ref[...].astype(F32)
    slots = regions * mesh_cap
    lane = lax.broadcasted_iota(jnp.int32, (mesh_cap, slots), 1)
    spread = (lane % mesh_cap == lax.broadcasted_iota(jnp.int32, (mesh_cap, slots), 0)).astype(F32)
    spread = dot(m2m_pick_ref[0].astype(F32).astype(BF16), spread.astype(BF16))
    lane = lax.broadcasted_iota(jnp.int32, (regions, slots), 1)
    owned = lane // mesh_cap == lax.broadcasted_iota(jnp.int32, (regions, slots), 0)
    index_ref[2:3, 0:slots] = jnp.sum(jnp.where(owned, spread, 0.0), 0, keepdims=True)
    packed_ref[first + mesh_count :, :] = index_ref[...].astype(BF16)


def weights_kernel(source_ref, weights_ref, turned_ref, semaphores):
    fetch([(source_ref, weights_ref)], semaphores)
    latent = weights_ref.shape[0]
    for n, block in enumerate((0, 2, 3)):
        turned_ref[:, n * latent : (n + 1) * latent] = weights_ref[
            :, block * latent : (block + 1) * latent
        ].T


def edge_forward(table, hot, hot_receiver, slope_ref, first):
    activation = dot_first(hot, table)
    squash = 0.5 + 0.5 * jnp.tanh(0.5 * activation)
    message = activation * squash
    slope_ref[first : first + activation.shape[0], :] = (
        squash + message * (1.0 - squash)
    ).astype(BF16)
    return dot(hot_receiver, message.astype(BF16))


def forward_kernel(
    regions,
    listed,
    mesh_count,
    mesh_cap,
    *refs,
):
    packed_refs, forwarded_ref = refs[:regions], refs[regions]
    (
        weights_ref,
        mesh_out_ref,
        grid_ref,
        mesh_ref,
        first_ref,
        sent_ref,
        index_ref,
        slope_one_ref,
        slope_two_ref,
        normed_one_ref,
        scaled_one_ref,
        normed_two_ref,
        scaled_two_ref,
        packed_index,
    ) = refs[regions + 1 :]
    latent = weights_ref.shape[0]
    edges = slope_one_ref.shape[0] // regions
    capacity = listed // 3
    slots = regions * mesh_cap
    me = lax.axis_index("space")

    def unpack(packed_ref, region):
        at = lambda rows: pl.ds(pl.multiple_of(region * rows, rows), rows)
        grid_ref[at(listed), :] = packed_ref[:listed, :]
        mesh_ref[at(mesh_count), :] = packed_ref[listed : listed + mesh_count, :]
        packed_index[at(INDEX_ROWS), :] = packed_ref[listed + mesh_count :, :]

    for step, packed_ref in enumerate(packed_refs):
        region = lax.bitwise_xor(me, step)
        if step < FAR_STEP:
            unpack(packed_ref, region)
        else:
            inner = jnp.logical_and(me > 0, me < regions - 1)
            pl.when(inner)(functools.partial(unpack, packed_ref, region))
            pl.when(jnp.logical_not(inner))(functools.partial(unpack, forwarded_ref, region))
    index_ref[...] = packed_index[...].astype(F32).astype(jnp.int32)

    grid_proj = dot(grid_ref[...], weights_ref[:, :latent])
    mesh_proj = dot(mesh_ref[...], weights_ref[:, latent : 2 * latent])
    blank = jnp.zeros((capacity, latent), F32)
    for d in range(regions):
        hot_sender = one_hot(index_ref[d * INDEX_ROWS : d * INDEX_ROWS + 1, :edges], listed)
        hot_receiver = one_hot(
            index_ref[d * INDEX_ROWS : d * INDEX_ROWS + 1, edges:], mesh_count
        )
        before = (d - 1) * listed + 2 * capacity
        within = d * listed + capacity
        after = (d + 1) * listed
        table = jnp.concatenate(
            [
                grid_proj[before : before + capacity] if d > 0 else blank,
                grid_proj[within : within + capacity],
                grid_proj[after : after + capacity] if d < regions - 1 else blank,
                mesh_proj[d * mesh_count : (d + 1) * mesh_count],
            ],
            axis=0,
        ).astype(BF16)
        summed = edge_forward(
            table,
            jnp.concatenate([hot_sender, hot_receiver], axis=0),
            hot_receiver,
            slope_one_ref,
            d * edges,
        )
        centred, scaled = row_moments(summed)
        normed = centred * scaled
        rows = slice(d * mesh_count, (d + 1) * mesh_count)
        normed_one_ref[rows, :] = normed
        scaled_one_ref[rows, :] = jnp.broadcast_to(scaled, (mesh_count, scaled_one_ref.shape[1]))
        first_ref[rows, :] = (mesh_ref[rows, :].astype(F32) + normed).astype(BF16)

    for s in range(regions):
        hot = one_hot(index_ref[s * INDEX_ROWS + 2 : s * INDEX_ROWS + 3, :slots], mesh_count)
        sent_ref[s * slots : (s + 1) * slots, :] = dot_first(
            hot, first_ref[s * mesh_count : (s + 1) * mesh_count, :]
        ).astype(BF16)
    sent_proj = dot(sent_ref[...], weights_ref[:, 2 * latent : 3 * latent])
    first_proj = dot(first_ref[...], weights_ref[:, 3 * latent :])
    for d in range(regions):
        hot_sender = one_hot(index_ref[d * INDEX_ROWS + 1 : d * INDEX_ROWS + 2, :edges], slots)
        hot_receiver = one_hot(
            index_ref[d * INDEX_ROWS + 1 : d * INDEX_ROWS + 2, edges:], mesh_count
        )
        pieces = [
            sent_proj[s * slots + d * mesh_cap : s * slots + (d + 1) * mesh_cap]
            for s in range(regions)
        ]
        table = jnp.concatenate(
            pieces + [first_proj[d * mesh_count : (d + 1) * mesh_count]], axis=0
        ).astype(BF16)
        summed = edge_forward(
            table,
            jnp.concatenate([hot_sender, hot_receiver], axis=0),
            hot_receiver,
            slope_two_ref,
            d * edges,
        )
        centred, scaled = row_moments(summed)
        rows = slice(d * mesh_count, (d + 1) * mesh_count)
        normed_two_ref[rows, :] = centred * scaled
        scaled_two_ref[rows, :] = jnp.broadcast_to(scaled, (mesh_count, scaled_two_ref.shape[1]))
    own = pl.ds(pl.multiple_of(me * mesh_count, mesh_count), mesh_count)
    mesh_out_ref[0] = (first_ref[own, :].astype(F32) + normed_two_ref[own, :]).astype(BF16)


def edge_backward(agg_grad, hot, hot_receiver, slope):
    edge_grad = (dot_first(hot_receiver, agg_grad) * slope.astype(F32)).astype(BF16)
    return dot(hot, edge_grad)


def halve(share_ref, keep_ref, give_ref):
    half = keep_ref.shape[0]
    core = lax.bitwise_and(lax.axis_index("rep"), 1)
    keep_ref[...] = share_ref[pl.ds(pl.multiple_of(core * half, half), half), :]
    give_ref[...] = share_ref[pl.ds(pl.multiple_of((1 - core) * half, half), half), :]


def process_back_kernel(regions, mesh_cap, *refs):
    cotangent_refs = refs[:regions]
    (
        turned_ref,
        first_ref,
        sent_ref,
        index_ref,
        slope_ref,
        normed_ref,
        scaled_ref,
        mesh_grad_ref,
        keep_ref,
        give_ref,
        upstream_ref,
        slot_ref,
        recv_ref,
        share_ref,
    ) = refs[regions:]
    latent = first_ref.shape[1]
    mesh_count = first_ref.shape[0] // regions
    edges = slope_ref.shape[0] // regions
    slots = regions * mesh_cap
    me = lax.axis_index("space")
    for step, cotangent_ref in enumerate(cotangent_refs):
        region = lax.bitwise_xor(me, step)
        at = pl.ds(pl.multiple_of(region * mesh_count, mesh_count), mesh_count)
        upstream_ref[at, :] = cotangent_ref[0].astype(F32)
    agg_grad = moments_back(normed_ref[...], scaled_ref[:, 0:1], upstream_ref[...]).astype(BF16)
    for d in range(regions):
        labels = slice(d * INDEX_ROWS + 1, d * INDEX_ROWS + 2)
        hot_sender = one_hot(index_ref[labels, :edges], slots)
        hot_receiver = one_hot(index_ref[labels, edges:], mesh_count)
        rows = slice(d * mesh_count, (d + 1) * mesh_count)
        sums = edge_backward(
            agg_grad[rows],
            jnp.concatenate([hot_sender, hot_receiver], axis=0),
            hot_receiver,
            slope_ref[d * edges : (d + 1) * edges, :],
        )
        for s in range(regions):
            first = s * slots + d * mesh_cap
            slot_ref[first : first + mesh_cap, :] = sums[s * mesh_cap : (s + 1) * mesh_cap]
        recv_ref[rows, :] = sums[slots:].astype(BF16)
    slot_sum = slot_ref[...].astype(BF16)
    columns = share_ref.shape[0]
    mine = pl.ds(pl.multiple_of(me * columns, columns), columns)
    share_ref[:, :latent] = dot_first(sent_ref[:, mine], slot_sum).astype(BF16)
    share_ref[:, latent:] = dot_first(first_ref[:, mine], recv_ref[...]).astype(BF16)
    halve(share_ref, keep_ref, give_ref)
    returned = dot(slot_sum, turned_ref[:, latent : 2 * latent]).astype(BF16)
    grad = upstream_ref[...] + dot(recv_ref[...], turned_ref[:, 2 * latent :])
    for s in range(regions):
        hot = one_hot(index_ref[s * INDEX_ROWS + 2 : s * INDEX_ROWS + 3, :slots], mesh_count)
        rows = slice(s * mesh_count, (s + 1) * mesh_count)
        mesh_grad_ref[rows, :] = grad[rows] + dot(hot, returned[s * slots : (s + 1) * slots])


def encode_sums(d, index_ref, slope_ref, agg_grad, listed):
    mesh_count = agg_grad.shape[0]
    edges = slope_ref.shape[0] // (index_ref.shape[0] // INDEX_ROWS)
    labels = slice(d * INDEX_ROWS, d * INDEX_ROWS + 1)
    hot_sender = one_hot(index_ref[labels, :edges], listed)
    hot_receiver = one_hot(index_ref[labels, edges:], mesh_count)
    return edge_backward(
        agg_grad,
        jnp.concatenate([hot_sender, hot_receiver], axis=0),
        hot_receiver,
        slope_ref[d * edges : (d + 1) * edges, :],
    ).astype(BF16)


def encode_back_first_kernel(
    regions,
    listed,
    index_ref,
    slope_ref,
    normed_ref,
    scaled_ref,
    mesh_grad_ref,
    agg_grad_ref,
    sums_ref,
):
    mesh_count = normed_ref.shape[0] // regions
    count = listed + mesh_count
    agg_grad_ref[...] = moments_back(
        normed_ref[...], scaled_ref[:, 0:1], mesh_grad_ref[...]
    ).astype(BF16)
    for d in range(regions // 2):
        rows = slice(d * mesh_count, (d + 1) * mesh_count)
        sums_ref[d * count : (d + 1) * count, :] = encode_sums(
            d, index_ref, slope_ref, agg_grad_ref[rows, :], listed
        )


def encode_back_kernel(
    regions,
    listed,
    grid_ref,
    mesh_ref,
    index_ref,
    slope_ref,
    agg_grad_ref,
    sums_ref,
    own_slot_ref,
    keep_ref,
    give_ref,
    slot_ref,
    recv_ref,
    share_ref,
):
    latent = mesh_ref.shape[1]
    mesh_count = mesh_ref.shape[0] // regions
    count = listed + mesh_count
    capacity = listed // 3
    me = lax.axis_index("space")
    blank = jnp.zeros((capacity, latent), BF16)
    slot_ref[0:capacity, :] = blank
    slot_ref[regions * listed - capacity :, :] = blank
    for d in range(regions):
        rows = slice(d * mesh_count, (d + 1) * mesh_count)
        if d < regions // 2:
            sums = sums_ref[d * count : (d + 1) * count, :]
        else:
            sums = encode_sums(d, index_ref, slope_ref, agg_grad_ref[rows, :], listed)
        for j in range(3):
            source = d + j - 1
            if 0 <= source < regions:
                first = source * listed + (2 - j) * capacity
                slot_ref[first : first + capacity, :] = sums[j * capacity : (j + 1) * capacity]
        recv_ref[rows, :] = sums[listed:]
    columns = share_ref.shape[0]
    mine = pl.ds(pl.multiple_of(me * columns, columns), columns)
    share_ref[:, :latent] = dot_first(grid_ref[:, mine], slot_ref[...]).astype(BF16)
    share_ref[:, latent:] = dot_first(mesh_ref[:, mine], recv_ref[...]).astype(BF16)
    halve(share_ref, keep_ref, give_ref)
    own = pl.ds(pl.multiple_of(me * listed, listed), listed)
    own_slot_ref[...] = slot_ref[own, :]


def grid_back_kernel(turned_ref, pick_ref, own_slot_ref, grid_grad_ref):
    lists, _, capacity = pick_ref.shape
    latent = own_slot_ref.shape[1]
    returned = dot(own_slot_ref[...], turned_ref[:, :latent]).astype(BF16)
    total = None
    for i in range(lists):
        owner = one_hot(pick_ref[i], grid_grad_ref.shape[1])
        part = dot(owner, returned[i * capacity : (i + 1) * capacity])
        total = part if total is None else total + part
    grid_grad_ref[0] = total.astype(BF16)


def finish_kernel(one_ref, other_one_ref, two_ref, other_two_ref, weight_grad_ref):
    half, width = one_ref.shape
    core = lax.bitwise_and(lax.axis_index("rep"), 1)
    mine = pl.ds(pl.multiple_of(core * half, half), half)
    other = pl.ds(pl.multiple_of((1 - core) * half, half), half)
    weight_grad_ref[mine, :width] = one_ref[...].astype(F32)
    weight_grad_ref[other, :width] = other_one_ref[...].astype(F32)
    weight_grad_ref[mine, width:] = two_ref[...].astype(F32)
    weight_grad_ref[other, width:] = other_two_ref[...].astype(F32)


VMEM = pl.BlockSpec(memory_space=pltpu.VMEM)


def call(kernel, operands, outputs, scratch, flops, fetched=0, megabytes=40):
    hbm = pl.BlockSpec(memory_space=pltpu.HBM)
    return pl.pallas_call(
        kernel,
        out_shape=[jax.ShapeDtypeStruct(shape, kind) for shape, kind in outputs],
        in_specs=[hbm] * fetched + [VMEM] * (len(operands) - fetched),
        out_specs=[VMEM] * len(outputs),
        scratch_shapes=[pltpu.VMEM(shape, kind) for shape, kind in scratch]
        + ([pltpu.SemaphoreType.DMA((fetched,))] if fetched else []),
        compiler_params=pltpu.CompilerParams(vmem_limit_bytes=megabytes << 20),
        cost_estimate=pl.CostEstimate(flops=flops, bytes_accessed=4 << 20, transcendentals=0),
    )(*operands)


def swap(block, axis, bits):
    return lax.ppermute(block, axis, [(i, i ^ bits) for i in range(lax.axis_size(axis))])


def added(left, right):
    return (left.astype(F32) + right.astype(F32)).astype(BF16)


def summed_over_chips(half):
    bit = 2
    while bit < lax.axis_size("rep"):
        half = added(half, swap(half, "rep", bit))
        bit *= 2
    return half, swap(half, "rep", 1)


def whole_sample_body(
    grid_latent,
    mesh_latent,
    mesh_cotangent,
    weights,
    g2m_pick,
    g2m_sender,
    g2m_receiver,
    m2m_pick,
    m2m_sender,
    m2m_receiver,
):
    regions = lax.axis_size("space")
    latent = weights.shape[0]
    listed = g2m_pick.shape[1] * g2m_pick.shape[2]
    mesh_count = mesh_latent.shape[1]
    mesh_cap = m2m_pick.shape[2]
    edges = g2m_sender.shape[0]
    columns = latent // regions
    half = columns // 2
    g2m_pick = g2m_pick.transpose(1, 0, 2)
    sources = (
        grid_latent,
        mesh_latent,
        g2m_pick,
        g2m_sender.reshape(1, -1),
        g2m_receiver.reshape(1, -1),
        m2m_pick,
        m2m_sender.reshape(1, -1),
        m2m_receiver.reshape(1, -1),
    )
    packed = call(
        pack_kernel,
        sources,
        [((listed + mesh_count + INDEX_ROWS, latent), BF16)],
        [((INDEX_ROWS, latent), F32)] + [(source.shape, source.dtype) for source in sources],
        10**7,
        fetched=len(sources),
        megabytes=56,
    )[0]
    packed, cotangent, weights = lax.optimization_barrier((packed, mesh_cotangent, weights))
    packs = [packed] + [swap(packed, "space", step) for step in range(1, min(regions, FAR_STEP))]
    cotangents = [cotangent, swap(cotangent, "space", 1)]
    weights, turned = call(
        weights_kernel,
        (weights,),
        [(weights.shape, BF16), ((latent, 3 * latent), BF16)],
        [],
        10**8,
        fetched=1,
    )
    forwarded = packed
    if regions > FAR_STEP:
        packs[2], packed, cotangent = lax.optimization_barrier((packs[2], packed, cotangent))
        packs.append(lax.ppermute(packed, "space", [(1, 2), (2, 1)]))
        forwarded = lax.ppermute(packs[2], "space", [(1, 0), (2, 3)])
        cotangents += [swap(cotangent, "space", step) for step in (2, 3)]
    rows = regions * mesh_count
    (
        mesh_out,
        grid_all,
        mesh_all,
        mesh_first,
        mesh_sent,
        index,
        slope_one,
        slope_two,
        normed_one,
        scaled_one,
        normed_two,
        scaled_two,
    ) = call(
        functools.partial(forward_kernel, regions, listed, mesh_count, mesh_cap),
        (*packs, forwarded, weights),
        [
            (mesh_latent.shape, BF16),
            ((regions * listed, latent), BF16),
            ((rows, latent), BF16),
            ((rows, latent), BF16),
            ((regions * regions * mesh_cap, latent), BF16),
            ((regions * INDEX_ROWS, latent), jnp.int32),
            ((regions * edges, latent), BF16),
            ((regions * edges, latent), BF16),
            ((rows, latent), F32),
            ((rows, 128), F32),
            ((rows, latent), F32),
            ((rows, 128), F32),
        ],
        [((regions * INDEX_ROWS, latent), BF16)],
        2 * 10**9,
    )
    mesh_grad, keep_two, give_two = call(
        functools.partial(process_back_kernel, regions, mesh_cap),
        (
            *cotangents,
            turned,
            mesh_first,
            mesh_sent,
            index,
            slope_two,
            normed_two,
            scaled_two,
        ),
        [((rows, latent), F32)] + [((half, 2 * latent), BF16)] * 2,
        [
            ((rows, latent), F32),
            ((regions * regions * mesh_cap, latent), F32),
            ((rows, latent), BF16),
            ((columns, 2 * latent), BF16),
        ],
        10**9,
    )
    agg_grad, sums = call(
        functools.partial(encode_back_first_kernel, regions, listed),
        (index, slope_one, normed_one, scaled_one, mesh_grad),
        [((rows, latent), BF16), ((regions // 2 * (listed + mesh_count), latent), BF16)],
        [],
        10**9,
    )
    half_two, sums = lax.optimization_barrier((added(keep_two, swap(give_two, "rep", 1)), sums))
    two, other_two = summed_over_chips(half_two)
    own_slots, keep_one, give_one = call(
        functools.partial(encode_back_kernel, regions, listed),
        (grid_all, mesh_all, index, slope_one, agg_grad, sums),
        [((listed, latent), BF16)] + [((half, 2 * latent), BF16)] * 2,
        [
            ((regions * listed, latent), BF16),
            ((rows, latent), BF16),
            ((columns, 2 * latent), BF16),
        ],
        10**9,
    )
    one, other_one = summed_over_chips(added(keep_one, swap(give_one, "rep", 1)))
    grid_grad = call(
        grid_back_kernel,
        (turned, g2m_pick, own_slots),
        [(grid_latent.shape, BF16)],
        [],
        10**8,
    )[0]
    weight_grad = call(
        finish_kernel,
        (one, other_one, two, other_two),
        [((columns, 4 * latent), F32)],
        [],
        10**6,
    )[0]
    return (mesh_out, grid_grad, weight_grad)


def solution(mesh):
    regions = mesh.shape["space"]
    samples = mesh.shape["rep"]

    def whole(*arguments):
        edges = arguments[5].shape[0] + arguments[8].shape[0]
        latent = arguments[3].shape[0]
        fits = edges * latent * 4 <= SAMPLE_EDGE_BYTES and latent % (128 * regions) == 0
        paired = regions in (2, 4) and samples > 1 and samples & (samples - 1) == 0
        return sharded(whole_sample_body if fits and paired else partitioned_body)(*arguments)

    def sharded(body):
        return jax.shard_map(
            body,
            mesh=mesh,
            in_specs=(
                P(("groups", "rep"), "space", None),
                P(("groups", "rep"), "space", None),
                P(("groups", "rep"), "space", None),
                P(),
                P("space", None, None),
                P("space"),
                P("space"),
                P("space", None, None),
                P("space"),
                P("space"),
            ),
            out_specs=(
                P(("groups", "rep"), "space", None),
                P(("groups", "rep"), "space", None),
                P(("groups", "space"), None),
            ),
            check_vma=False,
        )

    return whole
```

```python
import functools

import jax
import jax.numpy as jnp
from jax import lax
from jax.experimental import pallas as pl
from jax.experimental.pallas import tpu as pltpu
from jax.sharding import PartitionSpec as P

EPSILON = 1e-05


def with_halo(cells, sides, width):
    for axis, dim in sides:
        count = lax.axis_size(axis)
        ends = count - 1
        head = lax.slice_in_dim(cells, 0, width, axis=dim)
        tail = lax.slice_in_dim(cells, cells.shape[dim] - width, cells.shape[dim], axis=dim)
        cells = jnp.concatenate(
            [
                lax.ppermute(tail, axis, [(i, (i + 1) % count) for i in range(ends)]),
                cells,
                lax.ppermute(head, axis, [((i + 1) % count, i) for i in range(ends)]),
            ],
            axis=dim,
        )
    return cells


def swish(values):
    return values * jax.nn.sigmoid(values)


def swish_slope(values):
    squash = jax.nn.sigmoid(values)
    return squash * (1.0 + values * (1.0 - squash))


def norm_rows(values):
    centred = values - jnp.mean(values, -1, keepdims=True)
    return centred * lax.rsqrt(jnp.mean(centred * centred, -1, keepdims=True) + EPSILON)


def norm_rows_back(values, upstream):
    centred = values - jnp.mean(values, -1, keepdims=True)
    scaled = lax.rsqrt(jnp.mean(centred * centred, -1, keepdims=True) + EPSILON)
    normed = centred * scaled
    return scaled * (
        upstream
        - jnp.mean(upstream, -1, keepdims=True)
        - normed * jnp.mean(upstream * normed, -1, keepdims=True)
    )


def slot_rows(pick_row):
    listed = pick_row.reshape(-1)
    return listed


def mesh_route(outgoing, capacity, peer_count):
    columns = outgoing.shape[1]
    pieces = lax.all_to_all(
        outgoing.reshape(peer_count, capacity, columns),
        "space",
        split_axis=0,
        concat_axis=0,
        tiled=True,
    )
    arrived = pieces.reshape(peer_count * capacity, columns)
    return arrived


def grid_route(outgoing, capacity):
    columns = outgoing.shape[1]
    lists = outgoing.reshape(3, capacity, columns)
    rims = with_halo(jnp.stack([lists[0], lists[2]]), (("space", 0),), 1)
    return jnp.concatenate([rims[0], lists[1], rims[3]], axis=0)


def edge_pass(arrived, recv_table, located, receiver, w_send, w_recv):
    recv_proj = jnp.dot(recv_table, w_recv, preferred_element_type=jnp.float32)
    slot_proj = jnp.dot(arrived, w_send, preferred_element_type=jnp.float32)
    activation = slot_proj[located] + recv_proj[receiver]
    message = swish(activation).astype(jnp.bfloat16)
    member = (
        receiver[None, :] == jnp.arange(recv_table.shape[0], dtype=jnp.int32)[:, None]
    ).astype(jnp.bfloat16)
    summed = jnp.dot(member, message, preferred_element_type=jnp.float32)
    return (activation, member, summed)


def backward_pass(slot_count, located, activation, member, receiver, agg_grad, w_send):
    edge_grad = (agg_grad[receiver] * swish_slope(activation)).astype(jnp.bfloat16)
    recv_sum = jnp.dot(member, edge_grad, preferred_element_type=jnp.float32).astype(jnp.bfloat16)
    slot_member = (located[None, :] == jnp.arange(slot_count, dtype=jnp.int32)[:, None]).astype(
        jnp.bfloat16
    )
    slot_sum = jnp.dot(slot_member, edge_grad, preferred_element_type=jnp.float32).astype(
        jnp.bfloat16
    )
    returned = jnp.dot(slot_sum, w_send.T, preferred_element_type=jnp.float32).astype(jnp.bfloat16)
    return (recv_sum, slot_sum, returned)


def gather_back(listed, back_rows, row_count):
    owner = (listed[None, :] == jnp.arange(row_count, dtype=jnp.int32)[:, None]).astype(
        jnp.bfloat16
    )
    return jnp.dot(owner, back_rows, preferred_element_type=jnp.float32)


def partitioned_body(
    grid_latent,
    mesh_latent,
    mesh_cotangent,
    weights,
    g2m_pick,
    g2m_sender,
    g2m_receiver,
    m2m_pick,
    m2m_sender,
    m2m_receiver,
):
    grid_rows = grid_latent[0]
    mesh_rows = mesh_latent[0]
    upstream = mesh_cotangent[0].astype(jnp.float32)
    latent = weights.shape[0]
    encode_sender = weights[:, :latent]
    encode_receiver = weights[:, latent : 2 * latent]
    process_sender = weights[:, 2 * latent : 3 * latent]
    process_receiver = weights[:, 3 * latent :]
    peer_count = lax.axis_size("space")
    grid_cap = g2m_pick.shape[2]
    mesh_cap = m2m_pick.shape[2]
    grid_listed = g2m_pick[0].reshape(-1)
    grid_arrived = grid_route(grid_rows[grid_listed], grid_cap)
    act_first, member_first, summed_first = edge_pass(
        grid_arrived, mesh_rows, g2m_sender, g2m_receiver, encode_sender, encode_receiver
    )
    mesh_first = (mesh_rows.astype(jnp.float32) + norm_rows(summed_first)).astype(jnp.bfloat16)
    mesh_listed = slot_rows(m2m_pick[0])
    mesh_arrived = mesh_route(mesh_first[mesh_listed], mesh_cap, peer_count)
    act_second, member_second, summed_second = edge_pass(
        mesh_arrived, mesh_first, m2m_sender, m2m_receiver, process_sender, process_receiver
    )
    mesh_final = (mesh_first.astype(jnp.float32) + norm_rows(summed_second)).astype(jnp.bfloat16)
    agg_second = norm_rows_back(summed_second, upstream)
    recv_second, slot_second, returned_second = backward_pass(
        mesh_arrived.shape[0],
        m2m_sender,
        act_second,
        member_second,
        m2m_receiver,
        agg_second,
        process_sender,
    )
    back_second = mesh_route(returned_second, mesh_cap, peer_count)
    mesh_grad = upstream + jnp.dot(
        recv_second, process_receiver.T, preferred_element_type=jnp.float32
    )
    mesh_grad = mesh_grad + gather_back(mesh_listed, back_second, mesh_rows.shape[0])
    agg_first = norm_rows_back(summed_first, mesh_grad)
    recv_first, slot_first, returned_first = backward_pass(
        grid_arrived.shape[0],
        g2m_sender,
        act_first,
        member_first,
        g2m_receiver,
        agg_first,
        encode_sender,
    )
    back_first = grid_route(returned_first, grid_cap)
    grid_grad = gather_back(grid_listed, back_first, grid_rows.shape[0]).astype(jnp.bfloat16)
    factor_pairs = (
        (grid_arrived, slot_first),
        (mesh_rows, recv_first),
        (mesh_arrived, slot_second),
        (mesh_first, recv_second),
    )
    blocks = []
    for first_factor, second_factor in factor_pairs:
        blocks.append(
            lax.dot_general(
                first_factor,
                second_factor,
                (((0,), (0,)), ((), ())),
                preferred_element_type=jnp.float32,
            )
        )
    shares = lax.psum_scatter(
        jnp.concatenate(blocks, axis=1).astype(jnp.bfloat16),
        "space",
        scatter_dimension=0,
        tiled=True,
    )
    weight_grad = lax.psum(shares, "rep").astype(jnp.float32)
    return (mesh_final[None], grid_grad[None], weight_grad)


F32 = jnp.float32
BF16 = jnp.bfloat16
INDEX_ROWS = 16
SAMPLE_EDGE_BYTES = 8 << 20


def dot(left, right):
    return jnp.dot(left, right, preferred_element_type=F32)


def dot_first(left, right):
    return lax.dot_general(left, right, (((0,), (0,)), ((), ())), preferred_element_type=F32)


def one_hot(labels, count):
    rows = lax.broadcasted_iota(jnp.int32, (count, labels.shape[-1]), 0)
    return (rows == labels).astype(F32).astype(BF16)


def row_moments(values):
    centred = values - jnp.mean(values, -1, keepdims=True)
    return centred, lax.rsqrt(jnp.mean(centred * centred, -1, keepdims=True) + EPSILON)


def moments_back(normed, scaled, upstream):
    return scaled * (
        upstream
        - jnp.mean(upstream, -1, keepdims=True)
        - normed * jnp.mean(upstream * normed, -1, keepdims=True)
    )


def fetch(pairs, semaphores):
    copies = [
        pltpu.make_async_copy(source, target, semaphores.at[n])
        for n, (source, target) in enumerate(pairs)
    ]
    for copy in copies:
        copy.start()
    for copy in copies:
        copy.wait()


def pack_kernel(*refs):
    sources, packed_ref, index_ref = refs[:8], refs[8], refs[9]
    local, semaphores = refs[10:18], refs[18]
    fetch(list(zip(sources, local)), semaphores)
    (
        grid_ref,
        mesh_ref,
        g2m_pick_ref,
        g2m_sender_ref,
        g2m_receiver_ref,
        m2m_pick_ref,
        m2m_sender_ref,
        m2m_receiver_ref,
    ) = local
    lists, _, capacity = g2m_pick_ref.shape
    mesh_count = mesh_ref.shape[1]
    regions, mesh_cap = m2m_pick_ref.shape[1:]
    edges = g2m_sender_ref.shape[1]
    grid_rows = grid_ref[0]
    for i in range(lists):
        picked = one_hot(g2m_pick_ref[i], grid_rows.shape[0])
        packed_ref[i * capacity : (i + 1) * capacity, :] = dot_first(picked, grid_rows).astype(BF16)
    first = lists * capacity
    packed_ref[first : first + mesh_count, :] = mesh_ref[0]
    index_ref[...] = jnp.zeros_like(index_ref)
    index_ref[0:1, 0:edges] = g2m_sender_ref[...].astype(F32)
    index_ref[0:1, edges : 2 * edges] = g2m_receiver_ref[...].astype(F32)
    index_ref[1:2, 0:edges] = m2m_sender_ref[...].astype(F32)
    index_ref[1:2, edges : 2 * edges] = m2m_receiver_ref[...].astype(F32)
    slots = regions * mesh_cap
    lane = lax.broadcasted_iota(jnp.int32, (mesh_cap, slots), 1)
    spread = (lane % mesh_cap == lax.broadcasted_iota(jnp.int32, (mesh_cap, slots), 0)).astype(F32)
    spread = dot(m2m_pick_ref[0].astype(F32).astype(BF16), spread.astype(BF16))
    lane = lax.broadcasted_iota(jnp.int32, (regions, slots), 1)
    owned = lane // mesh_cap == lax.broadcasted_iota(jnp.int32, (regions, slots), 0)
    index_ref[2:3, 0:slots] = jnp.sum(jnp.where(owned, spread, 0.0), 0, keepdims=True)
    packed_ref[first + mesh_count :, :] = index_ref[...].astype(BF16)


def weights_kernel(source_ref, weights_ref, turned_ref, semaphores):
    fetch([(source_ref, weights_ref)], semaphores)
    latent = weights_ref.shape[0]
    for n, block in enumerate((0, 2, 3)):
        turned_ref[:, n * latent : (n + 1) * latent] = weights_ref[
            :, block * latent : (block + 1) * latent
        ].T


def edge_forward(table, hot, hot_receiver, slope_ref, first):
    activation = dot_first(hot, table)
    squash = 0.5 + 0.5 * jnp.tanh(0.5 * activation)
    message = activation * squash
    slope_ref[first : first + activation.shape[0], :] = (
        squash + message * (1.0 - squash)
    ).astype(BF16)
    return dot(hot_receiver, message.astype(BF16))


def forward_kernel(
    steps,
    listed,
    mesh_count,
    mesh_cap,
    *refs,
):
    regions = len(steps)
    packed_refs = refs[:regions]
    (
        weights_ref,
        mesh_out_ref,
        grid_ref,
        mesh_ref,
        first_ref,
        sent_ref,
        index_ref,
        slope_one_ref,
        slope_two_ref,
        normed_one_ref,
        scaled_one_ref,
        normed_two_ref,
        scaled_two_ref,
        packed_index,
    ) = refs[regions:]
    latent = weights_ref.shape[0]
    edges = slope_one_ref.shape[0] // regions
    capacity = listed // 3
    slots = regions * mesh_cap
    me = lax.axis_index("space")
    for step, packed_ref in zip(steps, packed_refs):
        region = lax.bitwise_xor(me, step)
        at = lambda rows: pl.ds(pl.multiple_of(region * rows, rows), rows)
        grid_ref[at(listed), :] = packed_ref[:listed, :]
        mesh_ref[at(mesh_count), :] = packed_ref[listed : listed + mesh_count, :]
        packed_index[at(INDEX_ROWS), :] = packed_ref[listed + mesh_count :, :]
    index_ref[...] = packed_index[...].astype(F32).astype(jnp.int32)

    grid_proj = dot(grid_ref[...], weights_ref[:, :latent])
    mesh_proj = dot(mesh_ref[...], weights_ref[:, latent : 2 * latent])
    blank = jnp.zeros((capacity, latent), F32)
    for d in range(regions):
        hot_sender = one_hot(index_ref[d * INDEX_ROWS : d * INDEX_ROWS + 1, :edges], listed)
        hot_receiver = one_hot(
            index_ref[d * INDEX_ROWS : d * INDEX_ROWS + 1, edges:], mesh_count
        )
        before = (d - 1) * listed + 2 * capacity
        within = d * listed + capacity
        after = (d + 1) * listed
        table = jnp.concatenate(
            [
                grid_proj[before : before + capacity] if d > 0 else blank,
                grid_proj[within : within + capacity],
                grid_proj[after : after + capacity] if d < regions - 1 else blank,
                mesh_proj[d * mesh_count : (d + 1) * mesh_count],
            ],
            axis=0,
        ).astype(BF16)
        summed = edge_forward(
            table,
            jnp.concatenate([hot_sender, hot_receiver], axis=0),
            hot_receiver,
            slope_one_ref,
            d * edges,
        )
        centred, scaled = row_moments(summed)
        normed = centred * scaled
        rows = slice(d * mesh_count, (d + 1) * mesh_count)
        normed_one_ref[rows, :] = normed
        scaled_one_ref[rows, :] = jnp.broadcast_to(scaled, (mesh_count, scaled_one_ref.shape[1]))
        first_ref[rows, :] = (mesh_ref[rows, :].astype(F32) + normed).astype(BF16)

    for s in range(regions):
        hot = one_hot(index_ref[s * INDEX_ROWS + 2 : s * INDEX_ROWS + 3, :slots], mesh_count)
        sent_ref[s * slots : (s + 1) * slots, :] = dot_first(
            hot, first_ref[s * mesh_count : (s + 1) * mesh_count, :]
        ).astype(BF16)
    sent_proj = dot(sent_ref[...], weights_ref[:, 2 * latent : 3 * latent])
    first_proj = dot(first_ref[...], weights_ref[:, 3 * latent :])
    for d in range(regions):
        hot_sender = one_hot(index_ref[d * INDEX_ROWS + 1 : d * INDEX_ROWS + 2, :edges], slots)
        hot_receiver = one_hot(
            index_ref[d * INDEX_ROWS + 1 : d * INDEX_ROWS + 2, edges:], mesh_count
        )
        pieces = [
            sent_proj[s * slots + d * mesh_cap : s * slots + (d + 1) * mesh_cap]
            for s in range(regions)
        ]
        table = jnp.concatenate(
            pieces + [first_proj[d * mesh_count : (d + 1) * mesh_count]], axis=0
        ).astype(BF16)
        summed = edge_forward(
            table,
            jnp.concatenate([hot_sender, hot_receiver], axis=0),
            hot_receiver,
            slope_two_ref,
            d * edges,
        )
        centred, scaled = row_moments(summed)
        rows = slice(d * mesh_count, (d + 1) * mesh_count)
        normed_two_ref[rows, :] = centred * scaled
        scaled_two_ref[rows, :] = jnp.broadcast_to(scaled, (mesh_count, scaled_two_ref.shape[1]))
    own = pl.ds(pl.multiple_of(me * mesh_count, mesh_count), mesh_count)
    mesh_out_ref[0] = (first_ref[own, :].astype(F32) + normed_two_ref[own, :]).astype(BF16)


def edge_backward(agg_grad, hot, hot_receiver, slope):
    edge_grad = (dot_first(hot_receiver, agg_grad) * slope.astype(F32)).astype(BF16)
    return dot(hot, edge_grad)


def halve(share_ref, keep_ref, give_ref):
    half = keep_ref.shape[0]
    core = lax.bitwise_and(lax.axis_index("rep"), 1)
    keep_ref[...] = share_ref[pl.ds(pl.multiple_of(core * half, half), half), :]
    give_ref[...] = share_ref[pl.ds(pl.multiple_of((1 - core) * half, half), half), :]


def process_back_kernel(steps, mesh_cap, *refs):
    regions = len(steps)
    cotangent_refs = refs[:regions]
    (
        turned_ref,
        first_ref,
        sent_ref,
        index_ref,
        slope_ref,
        normed_ref,
        scaled_ref,
        mesh_grad_ref,
        keep_ref,
        give_ref,
        upstream_ref,
        slot_ref,
        recv_ref,
        share_ref,
    ) = refs[regions:]
    latent = first_ref.shape[1]
    mesh_count = first_ref.shape[0] // regions
    edges = slope_ref.shape[0] // regions
    slots = regions * mesh_cap
    me = lax.axis_index("space")
    for step, cotangent_ref in zip(steps, cotangent_refs):
        region = lax.bitwise_xor(me, step)
        at = pl.ds(pl.multiple_of(region * mesh_count, mesh_count), mesh_count)
        upstream_ref[at, :] = cotangent_ref[0].astype(F32)
    agg_grad = moments_back(normed_ref[...], scaled_ref[:, 0:1], upstream_ref[...]).astype(BF16)
    for d in range(regions):
        labels = slice(d * INDEX_ROWS + 1, d * INDEX_ROWS + 2)
        hot_sender = one_hot(index_ref[labels, :edges], slots)
        hot_receiver = one_hot(index_ref[labels, edges:], mesh_count)
        rows = slice(d * mesh_count, (d + 1) * mesh_count)
        sums = edge_backward(
            agg_grad[rows],
            jnp.concatenate([hot_sender, hot_receiver], axis=0),
            hot_receiver,
            slope_ref[d * edges : (d + 1) * edges, :],
        )
        for s in range(regions):
            first = s * slots + d * mesh_cap
            slot_ref[first : first + mesh_cap, :] = sums[s * mesh_cap : (s + 1) * mesh_cap]
        recv_ref[rows, :] = sums[slots:].astype(BF16)
    slot_sum = slot_ref[...].astype(BF16)
    columns = share_ref.shape[0]
    mine = pl.ds(pl.multiple_of(me * columns, columns), columns)
    share_ref[:, :latent] = dot_first(sent_ref[:, mine], slot_sum).astype(BF16)
    share_ref[:, latent:] = dot_first(first_ref[:, mine], recv_ref[...]).astype(BF16)
    halve(share_ref, keep_ref, give_ref)
    returned = dot(slot_sum, turned_ref[:, latent : 2 * latent]).astype(BF16)
    grad = upstream_ref[...] + dot(recv_ref[...], turned_ref[:, 2 * latent :])
    for s in range(regions):
        hot = one_hot(index_ref[s * INDEX_ROWS + 2 : s * INDEX_ROWS + 3, :slots], mesh_count)
        rows = slice(s * mesh_count, (s + 1) * mesh_count)
        mesh_grad_ref[rows, :] = grad[rows] + dot(hot, returned[s * slots : (s + 1) * slots])


def encode_back_kernel(
    regions,
    grid_ref,
    mesh_ref,
    index_ref,
    slope_ref,
    normed_ref,
    scaled_ref,
    mesh_grad_ref,
    own_slot_ref,
    keep_ref,
    give_ref,
    slot_ref,
    recv_ref,
    share_ref,
):
    latent = mesh_ref.shape[1]
    mesh_count = mesh_ref.shape[0] // regions
    listed = grid_ref.shape[0] // regions
    capacity = listed // 3
    edges = slope_ref.shape[0] // regions
    me = lax.axis_index("space")
    agg_grad = moments_back(normed_ref[...], scaled_ref[:, 0:1], mesh_grad_ref[...]).astype(BF16)
    blank = jnp.zeros((capacity, latent), BF16)
    slot_ref[0:capacity, :] = blank
    slot_ref[regions * listed - capacity :, :] = blank
    for d in range(regions):
        labels = slice(d * INDEX_ROWS, d * INDEX_ROWS + 1)
        hot_sender = one_hot(index_ref[labels, :edges], listed)
        hot_receiver = one_hot(index_ref[labels, edges:], mesh_count)
        rows = slice(d * mesh_count, (d + 1) * mesh_count)
        sums = edge_backward(
            agg_grad[rows],
            jnp.concatenate([hot_sender, hot_receiver], axis=0),
            hot_receiver,
            slope_ref[d * edges : (d + 1) * edges, :],
        ).astype(BF16)
        for j in range(3):
            source = d + j - 1
            if 0 <= source < regions:
                first = source * listed + (2 - j) * capacity
                slot_ref[first : first + capacity, :] = sums[j * capacity : (j + 1) * capacity]
        recv_ref[rows, :] = sums[listed:]
    columns = share_ref.shape[0]
    mine = pl.ds(pl.multiple_of(me * columns, columns), columns)
    share_ref[:, :latent] = dot_first(grid_ref[:, mine], slot_ref[...]).astype(BF16)
    share_ref[:, latent:] = dot_first(mesh_ref[:, mine], recv_ref[...]).astype(BF16)
    halve(share_ref, keep_ref, give_ref)
    own = pl.ds(pl.multiple_of(me * listed, listed), listed)
    own_slot_ref[...] = slot_ref[own, :]


def grid_back_kernel(turned_ref, pick_ref, own_slot_ref, grid_grad_ref):
    lists, _, capacity = pick_ref.shape
    latent = own_slot_ref.shape[1]
    returned = dot(own_slot_ref[...], turned_ref[:, :latent]).astype(BF16)
    total = None
    for i in range(lists):
        owner = one_hot(pick_ref[i], grid_grad_ref.shape[1])
        part = dot(owner, returned[i * capacity : (i + 1) * capacity])
        total = part if total is None else total + part
    grid_grad_ref[0] = total.astype(BF16)


def finish_kernel(one_ref, other_one_ref, two_ref, other_two_ref, weight_grad_ref):
    half, width = one_ref.shape
    core = lax.bitwise_and(lax.axis_index("rep"), 1)
    mine = pl.ds(pl.multiple_of(core * half, half), half)
    other = pl.ds(pl.multiple_of((1 - core) * half, half), half)
    weight_grad_ref[mine, :width] = one_ref[...].astype(F32)
    weight_grad_ref[other, :width] = other_one_ref[...].astype(F32)
    weight_grad_ref[mine, width:] = two_ref[...].astype(F32)
    weight_grad_ref[other, width:] = other_two_ref[...].astype(F32)


VMEM = pl.BlockSpec(memory_space=pltpu.VMEM)


def call(kernel, operands, outputs, scratch, flops, fetched=0, megabytes=40):
    hbm = pl.BlockSpec(memory_space=pltpu.HBM)
    return pl.pallas_call(
        kernel,
        out_shape=[jax.ShapeDtypeStruct(shape, kind) for shape, kind in outputs],
        in_specs=[hbm] * fetched + [VMEM] * (len(operands) - fetched),
        out_specs=[VMEM] * len(outputs),
        scratch_shapes=[pltpu.VMEM(shape, kind) for shape, kind in scratch]
        + ([pltpu.SemaphoreType.DMA((fetched,))] if fetched else []),
        compiler_params=pltpu.CompilerParams(vmem_limit_bytes=megabytes << 20),
        cost_estimate=pl.CostEstimate(flops=flops, bytes_accessed=4 << 20, transcendentals=0),
    )(*operands)


def swap(block, axis, bits):
    return lax.ppermute(block, axis, [(i, i ^ bits) for i in range(lax.axis_size(axis))])


def added(left, right):
    return (left.astype(F32) + right.astype(F32)).astype(BF16)


def summed_half(keep, give):
    half = added(keep, swap(give, "rep", 1))
    bit = 2
    while bit < lax.axis_size("rep"):
        half = added(half, swap(half, "rep", bit))
        bit *= 2
    return half, swap(half, "rep", 1)


def whole_sample_body(
    grid_latent,
    mesh_latent,
    mesh_cotangent,
    weights,
    g2m_pick,
    g2m_sender,
    g2m_receiver,
    m2m_pick,
    m2m_sender,
    m2m_receiver,
):
    regions = lax.axis_size("space")
    latent = weights.shape[0]
    listed = g2m_pick.shape[1] * g2m_pick.shape[2]
    mesh_count = mesh_latent.shape[1]
    mesh_cap = m2m_pick.shape[2]
    edges = g2m_sender.shape[0]
    columns = latent // regions
    half = columns // 2
    g2m_pick = g2m_pick.transpose(1, 0, 2)
    sources = (
        grid_latent,
        mesh_latent,
        g2m_pick,
        g2m_sender.reshape(1, -1),
        g2m_receiver.reshape(1, -1),
        m2m_pick,
        m2m_sender.reshape(1, -1),
        m2m_receiver.reshape(1, -1),
    )
    packed = call(
        pack_kernel,
        sources,
        [((listed + mesh_count + INDEX_ROWS, latent), BF16)],
        [((INDEX_ROWS, latent), F32)] + [(source.shape, source.dtype) for source in sources],
        10**7,
        fetched=len(sources),
        megabytes=56,
    )[0]
    packed, cotangent, weights = lax.optimization_barrier((packed, mesh_cotangent, weights))
    steps = (0, *range(2, regions), 1)
    packs = [packed] + [swap(packed, "space", step) for step in steps[1:]]
    near = swap(cotangent, "space", 1)
    weights, turned = call(
        weights_kernel,
        (weights,),
        [(weights.shape, BF16), ((latent, 3 * latent), BF16)],
        [],
        10**8,
        fetched=1,
    )
    turned, cotangent = lax.optimization_barrier((turned, cotangent))
    cotangents = [cotangent] + [swap(cotangent, "space", step) for step in steps[1:-1]] + [near]
    rows = regions * mesh_count
    (
        mesh_out,
        grid_all,
        mesh_all,
        mesh_first,
        mesh_sent,
        index,
        slope_one,
        slope_two,
        normed_one,
        scaled_one,
        normed_two,
        scaled_two,
    ) = call(
        functools.partial(forward_kernel, steps, listed, mesh_count, mesh_cap),
        (*packs, weights),
        [
            (mesh_latent.shape, BF16),
            ((regions * listed, latent), BF16),
            ((rows, latent), BF16),
            ((rows, latent), BF16),
            ((regions * regions * mesh_cap, latent), BF16),
            ((regions * INDEX_ROWS, latent), jnp.int32),
            ((regions * edges, latent), BF16),
            ((regions * edges, latent), BF16),
            ((rows, latent), F32),
            ((rows, 128), F32),
            ((rows, latent), F32),
            ((rows, 128), F32),
        ],
        [((regions * INDEX_ROWS, latent), BF16)],
        2 * 10**9,
    )
    mesh_grad, keep_two, give_two = call(
        functools.partial(process_back_kernel, steps, mesh_cap),
        (
            *cotangents,
            turned,
            mesh_first,
            mesh_sent,
            index,
            slope_two,
            normed_two,
            scaled_two,
        ),
        [((rows, latent), F32)] + [((half, 2 * latent), BF16)] * 2,
        [
            ((rows, latent), F32),
            ((regions * regions * mesh_cap, latent), F32),
            ((rows, latent), BF16),
            ((columns, 2 * latent), BF16),
        ],
        10**9,
    )
    own_slots, keep_one, give_one = call(
        functools.partial(encode_back_kernel, regions),
        (
            grid_all,
            mesh_all,
            index,
            slope_one,
            normed_one,
            scaled_one,
            mesh_grad,
        ),
        [((listed, latent), BF16)] + [((half, 2 * latent), BF16)] * 2,
        [
            ((regions * listed, latent), BF16),
            ((rows, latent), BF16),
            ((columns, 2 * latent), BF16),
        ],
        10**9,
    )
    grid_grad = call(
        grid_back_kernel,
        (turned, g2m_pick, own_slots),
        [(grid_latent.shape, BF16)],
        [],
        10**8,
    )[0]
    weight_grad = call(
        finish_kernel,
        (*summed_half(keep_one, give_one), *summed_half(keep_two, give_two)),
        [((columns, 4 * latent), F32)],
        [],
        10**6,
    )[0]
    return (mesh_out, grid_grad, weight_grad)


def solution(mesh):
    regions = mesh.shape["space"]
    samples = mesh.shape["rep"]

    def whole(*arguments):
        edges = arguments[5].shape[0] + arguments[8].shape[0]
        latent = arguments[3].shape[0]
        fits = edges * latent * 4 <= SAMPLE_EDGE_BYTES and latent % (128 * regions) == 0
        paired = all(n > 1 and n & (n - 1) == 0 for n in (regions, samples))
        return sharded(whole_sample_body if fits and paired else partitioned_body)(*arguments)

    def sharded(body):
        return jax.shard_map(
            body,
            mesh=mesh,
            in_specs=(
                P(("groups", "rep"), "space", None),
                P(("groups", "rep"), "space", None),
                P(("groups", "rep"), "space", None),
                P(),
                P("space", None, None),
                P("space"),
                P("space"),
                P("space", None, None),
                P("space"),
                P("space"),
            ),
            out_specs=(
                P(("groups", "rep"), "space", None),
                P(("groups", "rep"), "space", None),
                P(("groups", "space"), None),
            ),
            check_vma=False,
        )

    return whole
```

```python
import functools

import jax
import jax.numpy as jnp
from jax import lax
from jax.experimental import pallas as pl
from jax.experimental.pallas import tpu as pltpu
from jax.sharding import PartitionSpec as P

EPSILON = 1e-05


def with_halo(cells, sides, width):
    for axis, dim in sides:
        count = lax.axis_size(axis)
        ends = count - 1
        head = lax.slice_in_dim(cells, 0, width, axis=dim)
        tail = lax.slice_in_dim(cells, cells.shape[dim] - width, cells.shape[dim], axis=dim)
        cells = jnp.concatenate(
            [
                lax.ppermute(tail, axis, [(i, (i + 1) % count) for i in range(ends)]),
                cells,
                lax.ppermute(head, axis, [((i + 1) % count, i) for i in range(ends)]),
            ],
            axis=dim,
        )
    return cells


def swish(values):
    return values * jax.nn.sigmoid(values)


def swish_slope(values):
    squash = jax.nn.sigmoid(values)
    return squash * (1.0 + values * (1.0 - squash))


def norm_rows(values):
    centred = values - jnp.mean(values, -1, keepdims=True)
    return centred * lax.rsqrt(jnp.mean(centred * centred, -1, keepdims=True) + EPSILON)


def norm_rows_back(values, upstream):
    centred = values - jnp.mean(values, -1, keepdims=True)
    scaled = lax.rsqrt(jnp.mean(centred * centred, -1, keepdims=True) + EPSILON)
    normed = centred * scaled
    return scaled * (
        upstream
        - jnp.mean(upstream, -1, keepdims=True)
        - normed * jnp.mean(upstream * normed, -1, keepdims=True)
    )


def slot_rows(pick_row):
    listed = pick_row.reshape(-1)
    return listed


def mesh_route(outgoing, capacity, peer_count):
    columns = outgoing.shape[1]
    pieces = lax.all_to_all(
        outgoing.reshape(peer_count, capacity, columns),
        "space",
        split_axis=0,
        concat_axis=0,
        tiled=True,
    )
    arrived = pieces.reshape(peer_count * capacity, columns)
    return arrived


def grid_route(outgoing, capacity):
    columns = outgoing.shape[1]
    lists = outgoing.reshape(3, capacity, columns)
    rims = with_halo(jnp.stack([lists[0], lists[2]]), (("space", 0),), 1)
    return jnp.concatenate([rims[0], lists[1], rims[3]], axis=0)


def edge_pass(arrived, recv_table, located, receiver, w_send, w_recv):
    recv_proj = jnp.dot(recv_table, w_recv, preferred_element_type=jnp.float32)
    slot_proj = jnp.dot(arrived, w_send, preferred_element_type=jnp.float32)
    activation = slot_proj[located] + recv_proj[receiver]
    message = swish(activation).astype(jnp.bfloat16)
    member = (
        receiver[None, :] == jnp.arange(recv_table.shape[0], dtype=jnp.int32)[:, None]
    ).astype(jnp.bfloat16)
    summed = jnp.dot(member, message, preferred_element_type=jnp.float32)
    return (activation, member, summed)


def backward_pass(slot_count, located, activation, member, receiver, agg_grad, w_send):
    edge_grad = (agg_grad[receiver] * swish_slope(activation)).astype(jnp.bfloat16)
    recv_sum = jnp.dot(member, edge_grad, preferred_element_type=jnp.float32).astype(jnp.bfloat16)
    slot_member = (located[None, :] == jnp.arange(slot_count, dtype=jnp.int32)[:, None]).astype(
        jnp.bfloat16
    )
    slot_sum = jnp.dot(slot_member, edge_grad, preferred_element_type=jnp.float32).astype(
        jnp.bfloat16
    )
    returned = jnp.dot(slot_sum, w_send.T, preferred_element_type=jnp.float32).astype(jnp.bfloat16)
    return (recv_sum, slot_sum, returned)


def gather_back(listed, back_rows, row_count):
    owner = (listed[None, :] == jnp.arange(row_count, dtype=jnp.int32)[:, None]).astype(
        jnp.bfloat16
    )
    return jnp.dot(owner, back_rows, preferred_element_type=jnp.float32)


def partitioned_body(
    grid_latent,
    mesh_latent,
    mesh_cotangent,
    weights,
    g2m_pick,
    g2m_sender,
    g2m_receiver,
    m2m_pick,
    m2m_sender,
    m2m_receiver,
):
    grid_rows = grid_latent[0]
    mesh_rows = mesh_latent[0]
    upstream = mesh_cotangent[0].astype(jnp.float32)
    latent = weights.shape[0]
    encode_sender = weights[:, :latent]
    encode_receiver = weights[:, latent : 2 * latent]
    process_sender = weights[:, 2 * latent : 3 * latent]
    process_receiver = weights[:, 3 * latent :]
    peer_count = lax.axis_size("space")
    grid_cap = g2m_pick.shape[2]
    mesh_cap = m2m_pick.shape[2]
    grid_listed = g2m_pick[0].reshape(-1)
    grid_arrived = grid_route(grid_rows[grid_listed], grid_cap)
    act_first, member_first, summed_first = edge_pass(
        grid_arrived, mesh_rows, g2m_sender, g2m_receiver, encode_sender, encode_receiver
    )
    mesh_first = (mesh_rows.astype(jnp.float32) + norm_rows(summed_first)).astype(jnp.bfloat16)
    mesh_listed = slot_rows(m2m_pick[0])
    mesh_arrived = mesh_route(mesh_first[mesh_listed], mesh_cap, peer_count)
    act_second, member_second, summed_second = edge_pass(
        mesh_arrived, mesh_first, m2m_sender, m2m_receiver, process_sender, process_receiver
    )
    mesh_final = (mesh_first.astype(jnp.float32) + norm_rows(summed_second)).astype(jnp.bfloat16)
    agg_second = norm_rows_back(summed_second, upstream)
    recv_second, slot_second, returned_second = backward_pass(
        mesh_arrived.shape[0],
        m2m_sender,
        act_second,
        member_second,
        m2m_receiver,
        agg_second,
        process_sender,
    )
    back_second = mesh_route(returned_second, mesh_cap, peer_count)
    mesh_grad = upstream + jnp.dot(
        recv_second, process_receiver.T, preferred_element_type=jnp.float32
    )
    mesh_grad = mesh_grad + gather_back(mesh_listed, back_second, mesh_rows.shape[0])
    agg_first = norm_rows_back(summed_first, mesh_grad)
    recv_first, slot_first, returned_first = backward_pass(
        grid_arrived.shape[0],
        g2m_sender,
        act_first,
        member_first,
        g2m_receiver,
        agg_first,
        encode_sender,
    )
    back_first = grid_route(returned_first, grid_cap)
    grid_grad = gather_back(grid_listed, back_first, grid_rows.shape[0]).astype(jnp.bfloat16)
    factor_pairs = (
        (grid_arrived, slot_first),
        (mesh_rows, recv_first),
        (mesh_arrived, slot_second),
        (mesh_first, recv_second),
    )
    blocks = []
    for first_factor, second_factor in factor_pairs:
        blocks.append(
            lax.dot_general(
                first_factor,
                second_factor,
                (((0,), (0,)), ((), ())),
                preferred_element_type=jnp.float32,
            )
        )
    shares = lax.psum_scatter(
        jnp.concatenate(blocks, axis=1).astype(jnp.bfloat16),
        "space",
        scatter_dimension=0,
        tiled=True,
    )
    weight_grad = lax.psum(shares, "rep").astype(jnp.float32)
    return (mesh_final[None], grid_grad[None], weight_grad)


F32 = jnp.float32
BF16 = jnp.bfloat16
INDEX_ROWS = 16
SAMPLE_EDGE_BYTES = 8 << 20


def dot(left, right):
    return jnp.dot(left, right, preferred_element_type=F32)


def dot_first(left, right):
    return lax.dot_general(left, right, (((0,), (0,)), ((), ())), preferred_element_type=F32)


def one_hot(labels, count):
    rows = lax.broadcasted_iota(jnp.int32, (count, labels.shape[-1]), 0)
    return (rows == labels).astype(F32).astype(BF16)


def row_moments(values):
    centred = values - jnp.mean(values, -1, keepdims=True)
    return centred, lax.rsqrt(jnp.mean(centred * centred, -1, keepdims=True) + EPSILON)


def moments_back(normed, scaled, upstream):
    return scaled * (
        upstream
        - jnp.mean(upstream, -1, keepdims=True)
        - normed * jnp.mean(upstream * normed, -1, keepdims=True)
    )


def fetch(pairs, semaphores):
    copies = [
        pltpu.make_async_copy(source, target, semaphores.at[n])
        for n, (source, target) in enumerate(pairs)
    ]
    for copy in copies:
        copy.start()
    for copy in copies:
        copy.wait()


def pack_kernel(*refs):
    sources, packed_ref, index_ref = refs[:8], refs[8], refs[9]
    local, semaphores = refs[10:18], refs[18]
    fetch(list(zip(sources, local)), semaphores)
    (
        grid_ref,
        mesh_ref,
        g2m_pick_ref,
        g2m_sender_ref,
        g2m_receiver_ref,
        m2m_pick_ref,
        m2m_sender_ref,
        m2m_receiver_ref,
    ) = local
    lists, _, capacity = g2m_pick_ref.shape
    mesh_count = mesh_ref.shape[1]
    regions, mesh_cap = m2m_pick_ref.shape[1:]
    edges = g2m_sender_ref.shape[1]
    grid_rows = grid_ref[0]
    for i in range(lists):
        picked = one_hot(g2m_pick_ref[i], grid_rows.shape[0])
        packed_ref[i * capacity : (i + 1) * capacity, :] = dot_first(picked, grid_rows).astype(BF16)
    first = lists * capacity
    packed_ref[first : first + mesh_count, :] = mesh_ref[0]
    index_ref[...] = jnp.zeros_like(index_ref)
    index_ref[0:1, 0:edges] = g2m_sender_ref[...].astype(F32)
    index_ref[0:1, edges : 2 * edges] = g2m_receiver_ref[...].astype(F32)
    index_ref[1:2, 0:edges] = m2m_sender_ref[...].astype(F32)
    index_ref[1:2, edges : 2 * edges] = m2m_receiver_ref[...].astype(F32)
    slots = regions * mesh_cap
    lane = lax.broadcasted_iota(jnp.int32, (mesh_cap, slots), 1)
    spread = (lane % mesh_cap == lax.broadcasted_iota(jnp.int32, (mesh_cap, slots), 0)).astype(F32)
    spread = dot(m2m_pick_ref[0].astype(F32).astype(BF16), spread.astype(BF16))
    lane = lax.broadcasted_iota(jnp.int32, (regions, slots), 1)
    owned = lane // mesh_cap == lax.broadcasted_iota(jnp.int32, (regions, slots), 0)
    index_ref[2:3, 0:slots] = jnp.sum(jnp.where(owned, spread, 0.0), 0, keepdims=True)
    packed_ref[first + mesh_count :, :] = index_ref[...].astype(BF16)


def weights_kernel(source_ref, weights_ref, turned_ref, semaphores):
    fetch([(source_ref, weights_ref)], semaphores)
    latent = weights_ref.shape[0]
    for n, block in enumerate((0, 2, 3)):
        turned_ref[:, n * latent : (n + 1) * latent] = weights_ref[
            :, block * latent : (block + 1) * latent
        ].T


def edge_forward(table, hot, hot_receiver, slope_ref, first):
    activation = dot_first(hot, table)
    squash = 0.5 + 0.5 * jnp.tanh(0.5 * activation)
    message = activation * squash
    slope_ref[first : first + activation.shape[0], :] = (
        squash + message * (1.0 - squash)
    ).astype(BF16)
    return dot(hot_receiver, message.astype(BF16))


def forward_kernel(
    steps,
    listed,
    mesh_count,
    mesh_cap,
    *refs,
):
    regions = len(steps)
    packed_refs = refs[:regions]
    (
        weights_ref,
        mesh_out_ref,
        grid_ref,
        mesh_ref,
        first_ref,
        sent_ref,
        index_ref,
        slope_one_ref,
        slope_two_ref,
        normed_one_ref,
        scaled_one_ref,
        normed_two_ref,
        scaled_two_ref,
        packed_index,
    ) = refs[regions:]
    latent = weights_ref.shape[0]
    edges = slope_one_ref.shape[0] // regions
    capacity = listed // 3
    slots = regions * mesh_cap
    me = lax.axis_index("space")
    for step, packed_ref in zip(steps, packed_refs):
        region = lax.bitwise_xor(me, step)
        at = lambda rows: pl.ds(pl.multiple_of(region * rows, rows), rows)
        grid_ref[at(listed), :] = packed_ref[:listed, :]
        mesh_ref[at(mesh_count), :] = packed_ref[listed : listed + mesh_count, :]
        packed_index[at(INDEX_ROWS), :] = packed_ref[listed + mesh_count :, :]
    index_ref[...] = packed_index[...].astype(F32).astype(jnp.int32)

    grid_proj = dot(grid_ref[...], weights_ref[:, :latent])
    mesh_proj = dot(mesh_ref[...], weights_ref[:, latent : 2 * latent])
    blank = jnp.zeros((capacity, latent), F32)
    for d in range(regions):
        hot_sender = one_hot(index_ref[d * INDEX_ROWS : d * INDEX_ROWS + 1, :edges], listed)
        hot_receiver = one_hot(
            index_ref[d * INDEX_ROWS : d * INDEX_ROWS + 1, edges:], mesh_count
        )
        before = (d - 1) * listed + 2 * capacity
        within = d * listed + capacity
        after = (d + 1) * listed
        table = jnp.concatenate(
            [
                grid_proj[before : before + capacity] if d > 0 else blank,
                grid_proj[within : within + capacity],
                grid_proj[after : after + capacity] if d < regions - 1 else blank,
                mesh_proj[d * mesh_count : (d + 1) * mesh_count],
            ],
            axis=0,
        ).astype(BF16)
        summed = edge_forward(
            table,
            jnp.concatenate([hot_sender, hot_receiver], axis=0),
            hot_receiver,
            slope_one_ref,
            d * edges,
        )
        centred, scaled = row_moments(summed)
        normed = centred * scaled
        rows = slice(d * mesh_count, (d + 1) * mesh_count)
        normed_one_ref[rows, :] = normed
        scaled_one_ref[rows, :] = jnp.broadcast_to(scaled, (mesh_count, scaled_one_ref.shape[1]))
        first_ref[rows, :] = (mesh_ref[rows, :].astype(F32) + normed).astype(BF16)

    for s in range(regions):
        hot = one_hot(index_ref[s * INDEX_ROWS + 2 : s * INDEX_ROWS + 3, :slots], mesh_count)
        sent_ref[s * slots : (s + 1) * slots, :] = dot_first(
            hot, first_ref[s * mesh_count : (s + 1) * mesh_count, :]
        ).astype(BF16)
    sent_proj = dot(sent_ref[...], weights_ref[:, 2 * latent : 3 * latent])
    first_proj = dot(first_ref[...], weights_ref[:, 3 * latent :])
    for d in range(regions):
        hot_sender = one_hot(index_ref[d * INDEX_ROWS + 1 : d * INDEX_ROWS + 2, :edges], slots)
        hot_receiver = one_hot(
            index_ref[d * INDEX_ROWS + 1 : d * INDEX_ROWS + 2, edges:], mesh_count
        )
        pieces = [
            sent_proj[s * slots + d * mesh_cap : s * slots + (d + 1) * mesh_cap]
            for s in range(regions)
        ]
        table = jnp.concatenate(
            pieces + [first_proj[d * mesh_count : (d + 1) * mesh_count]], axis=0
        ).astype(BF16)
        summed = edge_forward(
            table,
            jnp.concatenate([hot_sender, hot_receiver], axis=0),
            hot_receiver,
            slope_two_ref,
            d * edges,
        )
        centred, scaled = row_moments(summed)
        rows = slice(d * mesh_count, (d + 1) * mesh_count)
        normed_two_ref[rows, :] = centred * scaled
        scaled_two_ref[rows, :] = jnp.broadcast_to(scaled, (mesh_count, scaled_two_ref.shape[1]))
    own = pl.ds(pl.multiple_of(me * mesh_count, mesh_count), mesh_count)
    mesh_out_ref[0] = (first_ref[own, :].astype(F32) + normed_two_ref[own, :]).astype(BF16)


def edge_backward(agg_grad, hot, hot_receiver, slope):
    edge_grad = (dot_first(hot_receiver, agg_grad) * slope.astype(F32)).astype(BF16)
    return dot(hot, edge_grad)


def halve(share_ref, keep_ref, give_ref):
    half = keep_ref.shape[0]
    core = lax.bitwise_and(lax.axis_index("rep"), 1)
    keep_ref[...] = share_ref[pl.ds(pl.multiple_of(core * half, half), half), :]
    give_ref[...] = share_ref[pl.ds(pl.multiple_of((1 - core) * half, half), half), :]


def process_back_kernel(steps, mesh_cap, *refs):
    regions = len(steps)
    cotangent_refs = refs[:regions]
    (
        turned_ref,
        first_ref,
        sent_ref,
        index_ref,
        slope_ref,
        normed_ref,
        scaled_ref,
        mesh_grad_ref,
        keep_ref,
        give_ref,
        upstream_ref,
        slot_ref,
        recv_ref,
        share_ref,
    ) = refs[regions:]
    latent = first_ref.shape[1]
    mesh_count = first_ref.shape[0] // regions
    edges = slope_ref.shape[0] // regions
    slots = regions * mesh_cap
    me = lax.axis_index("space")
    for step, cotangent_ref in zip(steps, cotangent_refs):
        region = lax.bitwise_xor(me, step)
        at = pl.ds(pl.multiple_of(region * mesh_count, mesh_count), mesh_count)
        upstream_ref[at, :] = cotangent_ref[0].astype(F32)
    agg_grad = moments_back(normed_ref[...], scaled_ref[:, 0:1], upstream_ref[...]).astype(BF16)
    for d in range(regions):
        labels = slice(d * INDEX_ROWS + 1, d * INDEX_ROWS + 2)
        hot_sender = one_hot(index_ref[labels, :edges], slots)
        hot_receiver = one_hot(index_ref[labels, edges:], mesh_count)
        rows = slice(d * mesh_count, (d + 1) * mesh_count)
        sums = edge_backward(
            agg_grad[rows],
            jnp.concatenate([hot_sender, hot_receiver], axis=0),
            hot_receiver,
            slope_ref[d * edges : (d + 1) * edges, :],
        )
        for s in range(regions):
            first = s * slots + d * mesh_cap
            slot_ref[first : first + mesh_cap, :] = sums[s * mesh_cap : (s + 1) * mesh_cap]
        recv_ref[rows, :] = sums[slots:].astype(BF16)
    slot_sum = slot_ref[...].astype(BF16)
    columns = share_ref.shape[0]
    mine = pl.ds(pl.multiple_of(me * columns, columns), columns)
    share_ref[:, :latent] = dot_first(sent_ref[:, mine], slot_sum).astype(BF16)
    share_ref[:, latent:] = dot_first(first_ref[:, mine], recv_ref[...]).astype(BF16)
    halve(share_ref, keep_ref, give_ref)
    returned = dot(slot_sum, turned_ref[:, latent : 2 * latent]).astype(BF16)
    grad = upstream_ref[...] + dot(recv_ref[...], turned_ref[:, 2 * latent :])
    for s in range(regions):
        hot = one_hot(index_ref[s * INDEX_ROWS + 2 : s * INDEX_ROWS + 3, :slots], mesh_count)
        rows = slice(s * mesh_count, (s + 1) * mesh_count)
        mesh_grad_ref[rows, :] = grad[rows] + dot(hot, returned[s * slots : (s + 1) * slots])


def encode_back_kernel(
    regions,
    grid_ref,
    mesh_ref,
    index_ref,
    slope_ref,
    normed_ref,
    scaled_ref,
    mesh_grad_ref,
    own_slot_ref,
    keep_ref,
    give_ref,
    slot_ref,
    recv_ref,
    share_ref,
):
    latent = mesh_ref.shape[1]
    mesh_count = mesh_ref.shape[0] // regions
    listed = grid_ref.shape[0] // regions
    capacity = listed // 3
    edges = slope_ref.shape[0] // regions
    me = lax.axis_index("space")
    agg_grad = moments_back(normed_ref[...], scaled_ref[:, 0:1], mesh_grad_ref[...]).astype(BF16)
    blank = jnp.zeros((capacity, latent), BF16)
    slot_ref[0:capacity, :] = blank
    slot_ref[regions * listed - capacity :, :] = blank
    for d in range(regions):
        labels = slice(d * INDEX_ROWS, d * INDEX_ROWS + 1)
        hot_sender = one_hot(index_ref[labels, :edges], listed)
        hot_receiver = one_hot(index_ref[labels, edges:], mesh_count)
        rows = slice(d * mesh_count, (d + 1) * mesh_count)
        sums = edge_backward(
            agg_grad[rows],
            jnp.concatenate([hot_sender, hot_receiver], axis=0),
            hot_receiver,
            slope_ref[d * edges : (d + 1) * edges, :],
        ).astype(BF16)
        for j in range(3):
            source = d + j - 1
            if 0 <= source < regions:
                first = source * listed + (2 - j) * capacity
                slot_ref[first : first + capacity, :] = sums[j * capacity : (j + 1) * capacity]
        recv_ref[rows, :] = sums[listed:]
    columns = share_ref.shape[0]
    mine = pl.ds(pl.multiple_of(me * columns, columns), columns)
    share_ref[:, :latent] = dot_first(grid_ref[:, mine], slot_ref[...]).astype(BF16)
    share_ref[:, latent:] = dot_first(mesh_ref[:, mine], recv_ref[...]).astype(BF16)
    halve(share_ref, keep_ref, give_ref)
    own = pl.ds(pl.multiple_of(me * listed, listed), listed)
    own_slot_ref[...] = slot_ref[own, :]


def grid_back_kernel(turned_ref, pick_ref, own_slot_ref, grid_grad_ref):
    lists, _, capacity = pick_ref.shape
    latent = own_slot_ref.shape[1]
    returned = dot(own_slot_ref[...], turned_ref[:, :latent]).astype(BF16)
    total = None
    for i in range(lists):
        owner = one_hot(pick_ref[i], grid_grad_ref.shape[1])
        part = dot(owner, returned[i * capacity : (i + 1) * capacity])
        total = part if total is None else total + part
    grid_grad_ref[0] = total.astype(BF16)


def finish_kernel(one_ref, other_one_ref, two_ref, other_two_ref, weight_grad_ref):
    half, width = one_ref.shape
    core = lax.bitwise_and(lax.axis_index("rep"), 1)
    mine = pl.ds(pl.multiple_of(core * half, half), half)
    other = pl.ds(pl.multiple_of((1 - core) * half, half), half)
    weight_grad_ref[mine, :width] = one_ref[...].astype(F32)
    weight_grad_ref[other, :width] = other_one_ref[...].astype(F32)
    weight_grad_ref[mine, width:] = two_ref[...].astype(F32)
    weight_grad_ref[other, width:] = other_two_ref[...].astype(F32)


VMEM = pl.BlockSpec(memory_space=pltpu.VMEM)


def call(kernel, operands, outputs, scratch, flops, fetched=0, megabytes=40):
    hbm = pl.BlockSpec(memory_space=pltpu.HBM)
    return pl.pallas_call(
        kernel,
        out_shape=[jax.ShapeDtypeStruct(shape, kind) for shape, kind in outputs],
        in_specs=[hbm] * fetched + [VMEM] * (len(operands) - fetched),
        out_specs=[VMEM] * len(outputs),
        scratch_shapes=[pltpu.VMEM(shape, kind) for shape, kind in scratch]
        + ([pltpu.SemaphoreType.DMA((fetched,))] if fetched else []),
        compiler_params=pltpu.CompilerParams(vmem_limit_bytes=megabytes << 20),
        cost_estimate=pl.CostEstimate(flops=flops, bytes_accessed=4 << 20, transcendentals=0),
    )(*operands)


def swap(block, axis, bits):
    return lax.ppermute(block, axis, [(i, i ^ bits) for i in range(lax.axis_size(axis))])


def added(left, right):
    return (left.astype(F32) + right.astype(F32)).astype(BF16)


def summed_half(keep, give):
    half = added(keep, swap(give, "rep", 1))
    bit = 2
    while bit < lax.axis_size("rep"):
        half = added(half, swap(half, "rep", bit))
        bit *= 2
    return half, swap(half, "rep", 1)


def whole_sample_body(
    grid_latent,
    mesh_latent,
    mesh_cotangent,
    weights,
    g2m_pick,
    g2m_sender,
    g2m_receiver,
    m2m_pick,
    m2m_sender,
    m2m_receiver,
):
    regions = lax.axis_size("space")
    latent = weights.shape[0]
    listed = g2m_pick.shape[1] * g2m_pick.shape[2]
    mesh_count = mesh_latent.shape[1]
    mesh_cap = m2m_pick.shape[2]
    edges = g2m_sender.shape[0]
    columns = latent // regions
    half = columns // 2
    g2m_pick = g2m_pick.transpose(1, 0, 2)
    sources = (
        grid_latent,
        mesh_latent,
        g2m_pick,
        g2m_sender.reshape(1, -1),
        g2m_receiver.reshape(1, -1),
        m2m_pick,
        m2m_sender.reshape(1, -1),
        m2m_receiver.reshape(1, -1),
    )
    packed = call(
        pack_kernel,
        sources,
        [((listed + mesh_count + INDEX_ROWS, latent), BF16)],
        [((INDEX_ROWS, latent), F32)] + [(source.shape, source.dtype) for source in sources],
        10**7,
        fetched=len(sources),
        megabytes=56,
    )[0]
    packed, cotangent, weights = lax.optimization_barrier((packed, mesh_cotangent, weights))
    steps = (0, *range(2, regions), 1)
    packs = [packed] + [swap(packed, "space", step) for step in steps[1:]]
    near = swap(cotangent, "space", 1)
    weights, turned = call(
        weights_kernel,
        (weights,),
        [(weights.shape, BF16), ((latent, 3 * latent), BF16)],
        [],
        10**8,
        fetched=1,
    )
    packs[1], cotangent = lax.optimization_barrier((packs[1], cotangent))
    cotangents = [cotangent] + [swap(cotangent, "space", step) for step in steps[1:-1]] + [near]
    rows = regions * mesh_count
    (
        mesh_out,
        grid_all,
        mesh_all,
        mesh_first,
        mesh_sent,
        index,
        slope_one,
        slope_two,
        normed_one,
        scaled_one,
        normed_two,
        scaled_two,
    ) = call(
        functools.partial(forward_kernel, steps, listed, mesh_count, mesh_cap),
        (*packs, weights),
        [
            (mesh_latent.shape, BF16),
            ((regions * listed, latent), BF16),
            ((rows, latent), BF16),
            ((rows, latent), BF16),
            ((regions * regions * mesh_cap, latent), BF16),
            ((regions * INDEX_ROWS, latent), jnp.int32),
            ((regions * edges, latent), BF16),
            ((regions * edges, latent), BF16),
            ((rows, latent), F32),
            ((rows, 128), F32),
            ((rows, latent), F32),
            ((rows, 128), F32),
        ],
        [((regions * INDEX_ROWS, latent), BF16)],
        2 * 10**9,
    )
    mesh_grad, keep_two, give_two = call(
        functools.partial(process_back_kernel, steps, mesh_cap),
        (
            *cotangents,
            turned,
            mesh_first,
            mesh_sent,
            index,
            slope_two,
            normed_two,
            scaled_two,
        ),
        [((rows, latent), F32)] + [((half, 2 * latent), BF16)] * 2,
        [
            ((rows, latent), F32),
            ((regions * regions * mesh_cap, latent), F32),
            ((rows, latent), BF16),
            ((columns, 2 * latent), BF16),
        ],
        10**9,
    )
    own_slots, keep_one, give_one = call(
        functools.partial(encode_back_kernel, regions),
        (
            grid_all,
            mesh_all,
            index,
            slope_one,
            normed_one,
            scaled_one,
            mesh_grad,
        ),
        [((listed, latent), BF16)] + [((half, 2 * latent), BF16)] * 2,
        [
            ((regions * listed, latent), BF16),
            ((rows, latent), BF16),
            ((columns, 2 * latent), BF16),
        ],
        10**9,
    )
    grid_grad = call(
        grid_back_kernel,
        (turned, g2m_pick, own_slots),
        [(grid_latent.shape, BF16)],
        [],
        10**8,
    )[0]
    weight_grad = call(
        finish_kernel,
        (*summed_half(keep_one, give_one), *summed_half(keep_two, give_two)),
        [((columns, 4 * latent), F32)],
        [],
        10**6,
    )[0]
    return (mesh_out, grid_grad, weight_grad)


def solution(mesh):
    regions = mesh.shape["space"]
    samples = mesh.shape["rep"]

    def whole(*arguments):
        edges = arguments[5].shape[0] + arguments[8].shape[0]
        latent = arguments[3].shape[0]
        fits = edges * latent * 4 <= SAMPLE_EDGE_BYTES and latent % (128 * regions) == 0
        paired = all(n > 1 and n & (n - 1) == 0 for n in (regions, samples))
        return sharded(whole_sample_body if fits and paired else partitioned_body)(*arguments)

    def sharded(body):
        return jax.shard_map(
            body,
            mesh=mesh,
            in_specs=(
                P(("groups", "rep"), "space", None),
                P(("groups", "rep"), "space", None),
                P(("groups", "rep"), "space", None),
                P(),
                P("space", None, None),
                P("space"),
                P("space"),
                P("space", None, None),
                P("space"),
                P("space"),
            ),
            out_specs=(
                P(("groups", "rep"), "space", None),
                P(("groups", "rep"), "space", None),
                P(("groups", "space"), None),
            ),
            check_vma=False,
        )

    return whole
```

```python
import functools

import jax
import jax.numpy as jnp
from jax import lax
from jax.experimental import pallas as pl
from jax.experimental.pallas import tpu as pltpu
from jax.sharding import PartitionSpec as P

EPSILON = 1e-05


def with_halo(cells, sides, width):
    for axis, dim in sides:
        count = lax.axis_size(axis)
        ends = count - 1
        head = lax.slice_in_dim(cells, 0, width, axis=dim)
        tail = lax.slice_in_dim(cells, cells.shape[dim] - width, cells.shape[dim], axis=dim)
        cells = jnp.concatenate(
            [
                lax.ppermute(tail, axis, [(i, (i + 1) % count) for i in range(ends)]),
                cells,
                lax.ppermute(head, axis, [((i + 1) % count, i) for i in range(ends)]),
            ],
            axis=dim,
        )
    return cells


def swish(values):
    return values * jax.nn.sigmoid(values)


def swish_slope(values):
    squash = jax.nn.sigmoid(values)
    return squash * (1.0 + values * (1.0 - squash))


def norm_rows(values):
    centred = values - jnp.mean(values, -1, keepdims=True)
    return centred * lax.rsqrt(jnp.mean(centred * centred, -1, keepdims=True) + EPSILON)


def norm_rows_back(values, upstream):
    centred = values - jnp.mean(values, -1, keepdims=True)
    scaled = lax.rsqrt(jnp.mean(centred * centred, -1, keepdims=True) + EPSILON)
    normed = centred * scaled
    return scaled * (
        upstream
        - jnp.mean(upstream, -1, keepdims=True)
        - normed * jnp.mean(upstream * normed, -1, keepdims=True)
    )


def slot_rows(pick_row):
    listed = pick_row.reshape(-1)
    return listed


def mesh_route(outgoing, capacity, peer_count):
    columns = outgoing.shape[1]
    pieces = lax.all_to_all(
        outgoing.reshape(peer_count, capacity, columns),
        "space",
        split_axis=0,
        concat_axis=0,
        tiled=True,
    )
    arrived = pieces.reshape(peer_count * capacity, columns)
    return arrived


def grid_route(outgoing, capacity):
    columns = outgoing.shape[1]
    lists = outgoing.reshape(3, capacity, columns)
    rims = with_halo(jnp.stack([lists[0], lists[2]]), (("space", 0),), 1)
    return jnp.concatenate([rims[0], lists[1], rims[3]], axis=0)


def edge_pass(arrived, recv_table, located, receiver, w_send, w_recv):
    recv_proj = jnp.dot(recv_table, w_recv, preferred_element_type=jnp.float32)
    slot_proj = jnp.dot(arrived, w_send, preferred_element_type=jnp.float32)
    activation = slot_proj[located] + recv_proj[receiver]
    message = swish(activation).astype(jnp.bfloat16)
    member = (
        receiver[None, :] == jnp.arange(recv_table.shape[0], dtype=jnp.int32)[:, None]
    ).astype(jnp.bfloat16)
    summed = jnp.dot(member, message, preferred_element_type=jnp.float32)
    return (activation, member, summed)


def backward_pass(slot_count, located, activation, member, receiver, agg_grad, w_send):
    edge_grad = (agg_grad[receiver] * swish_slope(activation)).astype(jnp.bfloat16)
    recv_sum = jnp.dot(member, edge_grad, preferred_element_type=jnp.float32).astype(jnp.bfloat16)
    slot_member = (located[None, :] == jnp.arange(slot_count, dtype=jnp.int32)[:, None]).astype(
        jnp.bfloat16
    )
    slot_sum = jnp.dot(slot_member, edge_grad, preferred_element_type=jnp.float32).astype(
        jnp.bfloat16
    )
    returned = jnp.dot(slot_sum, w_send.T, preferred_element_type=jnp.float32).astype(jnp.bfloat16)
    return (recv_sum, slot_sum, returned)


def gather_back(listed, back_rows, row_count):
    owner = (listed[None, :] == jnp.arange(row_count, dtype=jnp.int32)[:, None]).astype(
        jnp.bfloat16
    )
    return jnp.dot(owner, back_rows, preferred_element_type=jnp.float32)


def partitioned_body(
    grid_latent,
    mesh_latent,
    mesh_cotangent,
    weights,
    g2m_pick,
    g2m_sender,
    g2m_receiver,
    m2m_pick,
    m2m_sender,
    m2m_receiver,
):
    grid_rows = grid_latent[0]
    mesh_rows = mesh_latent[0]
    upstream = mesh_cotangent[0].astype(jnp.float32)
    latent = weights.shape[0]
    encode_sender = weights[:, :latent]
    encode_receiver = weights[:, latent : 2 * latent]
    process_sender = weights[:, 2 * latent : 3 * latent]
    process_receiver = weights[:, 3 * latent :]
    peer_count = lax.axis_size("space")
    grid_cap = g2m_pick.shape[2]
    mesh_cap = m2m_pick.shape[2]
    grid_listed = g2m_pick[0].reshape(-1)
    grid_arrived = grid_route(grid_rows[grid_listed], grid_cap)
    act_first, member_first, summed_first = edge_pass(
        grid_arrived, mesh_rows, g2m_sender, g2m_receiver, encode_sender, encode_receiver
    )
    mesh_first = (mesh_rows.astype(jnp.float32) + norm_rows(summed_first)).astype(jnp.bfloat16)
    mesh_listed = slot_rows(m2m_pick[0])
    mesh_arrived = mesh_route(mesh_first[mesh_listed], mesh_cap, peer_count)
    act_second, member_second, summed_second = edge_pass(
        mesh_arrived, mesh_first, m2m_sender, m2m_receiver, process_sender, process_receiver
    )
    mesh_final = (mesh_first.astype(jnp.float32) + norm_rows(summed_second)).astype(jnp.bfloat16)
    agg_second = norm_rows_back(summed_second, upstream)
    recv_second, slot_second, returned_second = backward_pass(
        mesh_arrived.shape[0],
        m2m_sender,
        act_second,
        member_second,
        m2m_receiver,
        agg_second,
        process_sender,
    )
    back_second = mesh_route(returned_second, mesh_cap, peer_count)
    mesh_grad = upstream + jnp.dot(
        recv_second, process_receiver.T, preferred_element_type=jnp.float32
    )
    mesh_grad = mesh_grad + gather_back(mesh_listed, back_second, mesh_rows.shape[0])
    agg_first = norm_rows_back(summed_first, mesh_grad)
    recv_first, slot_first, returned_first = backward_pass(
        grid_arrived.shape[0],
        g2m_sender,
        act_first,
        member_first,
        g2m_receiver,
        agg_first,
        encode_sender,
    )
    back_first = grid_route(returned_first, grid_cap)
    grid_grad = gather_back(grid_listed, back_first, grid_rows.shape[0]).astype(jnp.bfloat16)
    factor_pairs = (
        (grid_arrived, slot_first),
        (mesh_rows, recv_first),
        (mesh_arrived, slot_second),
        (mesh_first, recv_second),
    )
    blocks = []
    for first_factor, second_factor in factor_pairs:
        blocks.append(
            lax.dot_general(
                first_factor,
                second_factor,
                (((0,), (0,)), ((), ())),
                preferred_element_type=jnp.float32,
            )
        )
    shares = lax.psum_scatter(
        jnp.concatenate(blocks, axis=1).astype(jnp.bfloat16),
        "space",
        scatter_dimension=0,
        tiled=True,
    )
    weight_grad = lax.psum(shares, "rep").astype(jnp.float32)
    return (mesh_final[None], grid_grad[None], weight_grad)


F32 = jnp.float32
BF16 = jnp.bfloat16
INDEX_ROWS = 8
SAMPLE_EDGE_BYTES = 8 << 20


def dot(left, right):
    return jnp.dot(left, right, preferred_element_type=F32)


def dot_first(left, right):
    return lax.dot_general(left, right, (((0,), (0,)), ((), ())), preferred_element_type=F32)


def one_hot(labels, count):
    rows = lax.broadcasted_iota(jnp.int32, (count, labels.shape[-1]), 0)
    return (rows == labels).astype(F32).astype(BF16)


def row_moments(values):
    centred = values - jnp.mean(values, -1, keepdims=True)
    return centred, lax.rsqrt(jnp.mean(centred * centred, -1, keepdims=True) + EPSILON)


def moments_back(normed, scaled, upstream):
    return scaled * (
        upstream
        - jnp.mean(upstream, -1, keepdims=True)
        - normed * jnp.mean(upstream * normed, -1, keepdims=True)
    )


def fetch(pairs, semaphores):
    copies = [
        pltpu.make_async_copy(source, target, semaphores.at[n])
        for n, (source, target) in enumerate(pairs)
    ]
    for copy in copies:
        copy.start()
    for copy in copies:
        copy.wait()


def pack_kernel(*refs):
    sources, packed_ref, index_ref = refs[:8], refs[8], refs[9]
    local, semaphores = refs[10:18], refs[18]
    fetch(list(zip(sources, local)), semaphores)
    (
        grid_ref,
        mesh_ref,
        g2m_pick_ref,
        g2m_sender_ref,
        g2m_receiver_ref,
        m2m_pick_ref,
        m2m_sender_ref,
        m2m_receiver_ref,
    ) = local
    lists, _, capacity = g2m_pick_ref.shape
    mesh_count = mesh_ref.shape[1]
    regions, mesh_cap = m2m_pick_ref.shape[1:]
    edges = g2m_sender_ref.shape[1]
    grid_rows = grid_ref[0]
    for i in range(lists):
        picked = one_hot(g2m_pick_ref[i], grid_rows.shape[0])
        packed_ref[i * capacity : (i + 1) * capacity, :] = dot_first(picked, grid_rows).astype(BF16)
    first = lists * capacity
    packed_ref[first : first + mesh_count, :] = mesh_ref[0]
    index_ref[...] = jnp.zeros_like(index_ref)
    index_ref[0:1, 0:edges] = g2m_sender_ref[...].astype(F32)
    index_ref[0:1, edges : 2 * edges] = g2m_receiver_ref[...].astype(F32)
    index_ref[1:2, 0:edges] = m2m_sender_ref[...].astype(F32)
    index_ref[1:2, edges : 2 * edges] = m2m_receiver_ref[...].astype(F32)
    slots = regions * mesh_cap
    lane = lax.broadcasted_iota(jnp.int32, (mesh_cap, slots), 1)
    spread = (lane % mesh_cap == lax.broadcasted_iota(jnp.int32, (mesh_cap, slots), 0)).astype(F32)
    spread = dot(m2m_pick_ref[0].astype(F32).astype(BF16), spread.astype(BF16))
    lane = lax.broadcasted_iota(jnp.int32, (regions, slots), 1)
    owned = lane // mesh_cap == lax.broadcasted_iota(jnp.int32, (regions, slots), 0)
    index_ref[2:3, 0:slots] = jnp.sum(jnp.where(owned, spread, 0.0), 0, keepdims=True)
    packed_ref[first + mesh_count :, :] = index_ref[...].astype(BF16)


def weights_kernel(source_ref, weights_ref, turned_ref, semaphores):
    fetch([(source_ref, weights_ref)], semaphores)
    latent = weights_ref.shape[0]
    for n, block in enumerate((0, 2, 3)):
        turned_ref[:, n * latent : (n + 1) * latent] = weights_ref[
            :, block * latent : (block + 1) * latent
        ].T


def edge_blocks(edges):
    size = min(edges, 128)
    return [(first, min(size, edges - first)) for first in range(0, edges, size)]


def edge_forward(tables, hot_ref, turned_hot_ref, slope_ref, message_ref, mesh_count):
    regions = len(tables)
    edges = slope_ref.shape[0] // regions
    count = hot_ref.shape[0] // regions
    work = [(d, first, size) for d in range(regions) for first, size in edge_blocks(edges)]

    def gathered(d, first, size):
        rows = slice(d * edges + first, d * edges + first + size)
        return dot(turned_hot_ref[rows, :], tables[d])

    sums = []
    activation = gathered(*work[0])
    for n, (d, first, size) in enumerate(work):
        coming = gathered(*work[n + 1]) if n + 1 < len(work) else None
        squash = 0.5 + 0.5 * jnp.tanh(0.5 * activation)
        message = activation * squash
        rows = slice(d * edges + first, d * edges + first + size)
        slope_ref[rows, :] = (squash + message * (1.0 - squash)).astype(BF16)
        message_ref[rows, :] = message.astype(BF16)
        activation = coming
        if first + size == edges:
            hot = hot_ref[(d + 1) * count - mesh_count : (d + 1) * count, :]
            sums.append(dot(hot, message_ref[d * edges : (d + 1) * edges, :]))
    return sums


def forward_kernel(
    steps,
    listed,
    mesh_count,
    mesh_cap,
    *refs,
):
    regions = len(steps)
    packed_refs = refs[:regions]
    (
        weights_ref,
        mesh_out_ref,
        grid_ref,
        mesh_ref,
        first_ref,
        sent_ref,
        hot_one_ref,
        hot_two_ref,
        turned_one_ref,
        turned_two_ref,
        hot_sent_ref,
        slope_one_ref,
        slope_two_ref,
        normed_one_ref,
        scaled_one_ref,
        normed_two_ref,
        scaled_two_ref,
        index_ref,
        message_ref,
        sum_ref,
    ) = refs[regions:]
    latent = weights_ref.shape[0]
    edges = slope_one_ref.shape[0] // regions
    capacity = listed // 3
    slots = regions * mesh_cap
    me = lax.axis_index("space")
    for step, packed_ref in zip(steps, packed_refs):
        region = lax.bitwise_xor(me, step)
        at = lambda rows: pl.ds(pl.multiple_of(region * rows, rows), rows)
        grid_ref[at(listed), :] = packed_ref[:listed, :]
        mesh_ref[at(mesh_count), :] = packed_ref[listed : listed + mesh_count, :]
        index_ref[at(INDEX_ROWS), :] = packed_ref[listed + mesh_count :, :].astype(F32)

    grid_proj = dot(grid_ref[...], weights_ref[:, :latent])
    mesh_proj = dot(mesh_ref[...], weights_ref[:, latent : 2 * latent])
    for d in range(regions):
        index = index_ref[d * INDEX_ROWS : (d + 1) * INDEX_ROWS, :].astype(jnp.int32)
        for row, senders, hot_ref, turned_ref in (
            (0, listed, hot_one_ref, turned_one_ref),
            (1, slots, hot_two_ref, turned_two_ref),
        ):
            count = senders + mesh_count
            hot = jnp.concatenate(
                [
                    one_hot(index[row : row + 1, :edges], senders),
                    one_hot(index[row : row + 1, edges:], mesh_count),
                ],
                axis=0,
            )
            hot_ref[d * count : (d + 1) * count, :] = hot
            turned_ref[d * edges : (d + 1) * edges, :] = hot.T
        hot_sent_ref[d * mesh_count : (d + 1) * mesh_count, :] = one_hot(
            index[2:3, :slots], mesh_count
        )

    blank = jnp.zeros((capacity, latent), F32)
    tables = []
    for d in range(regions):
        before = (d - 1) * listed + 2 * capacity
        within = d * listed + capacity
        after = (d + 1) * listed
        tables.append(
            jnp.concatenate(
                [
                    grid_proj[before : before + capacity] if d > 0 else blank,
                    grid_proj[within : within + capacity],
                    grid_proj[after : after + capacity] if d < regions - 1 else blank,
                    mesh_proj[d * mesh_count : (d + 1) * mesh_count],
                ],
                axis=0,
            ).astype(BF16)
        )
    sums = edge_forward(
        tables, hot_one_ref, turned_one_ref, slope_one_ref, message_ref, mesh_count
    )
    for d in range(regions):
        sum_ref[d * mesh_count : (d + 1) * mesh_count, :] = sums[d]
    centred, scaled = row_moments(sum_ref[...])
    normed = centred * scaled
    normed_one_ref[...] = normed
    scaled_one_ref[...] = jnp.broadcast_to(scaled, scaled_one_ref.shape)
    first_ref[...] = (mesh_ref[...].astype(F32) + normed).astype(BF16)

    for s in range(regions):
        rows = slice(s * mesh_count, (s + 1) * mesh_count)
        sent_ref[s * slots : (s + 1) * slots, :] = dot_first(
            hot_sent_ref[rows, :], first_ref[rows, :]
        ).astype(BF16)
    sent_proj = dot(sent_ref[...], weights_ref[:, 2 * latent : 3 * latent])
    first_proj = dot(first_ref[...], weights_ref[:, 3 * latent :])
    tables = []
    for d in range(regions):
        pieces = [
            sent_proj[s * slots + d * mesh_cap : s * slots + (d + 1) * mesh_cap]
            for s in range(regions)
        ]
        tables.append(
            jnp.concatenate(
                pieces + [first_proj[d * mesh_count : (d + 1) * mesh_count]], axis=0
            ).astype(BF16)
        )
    sums = edge_forward(
        tables, hot_two_ref, turned_two_ref, slope_two_ref, message_ref, mesh_count
    )
    for d in range(regions):
        sum_ref[d * mesh_count : (d + 1) * mesh_count, :] = sums[d]
    centred, scaled = row_moments(sum_ref[...])
    normed_two_ref[...] = centred * scaled
    scaled_two_ref[...] = jnp.broadcast_to(scaled, scaled_two_ref.shape)
    own = pl.ds(pl.multiple_of(me * mesh_count, mesh_count), mesh_count)
    mesh_out_ref[0] = (first_ref[own, :].astype(F32) + normed_two_ref[own, :]).astype(BF16)


def edge_backward(regions, agg_grad, hot_ref, turned_hot_ref, slope_ref, edge_grad_ref):
    edges = slope_ref.shape[0] // regions
    count = hot_ref.shape[0] // regions
    mesh_count = agg_grad.shape[0] // regions
    blank = jnp.zeros((count - mesh_count, agg_grad.shape[1]), BF16)
    work = [(d, first, size) for d in range(regions) for first, size in edge_blocks(edges)]

    def gathered(d, first, size):
        rows = slice(d * edges + first, d * edges + first + size)
        table = jnp.concatenate([blank, agg_grad[d * mesh_count : (d + 1) * mesh_count]], axis=0)
        return dot(turned_hot_ref[rows, :], table)

    sums = []
    upstream = gathered(*work[0])
    for n, (d, first, size) in enumerate(work):
        coming = gathered(*work[n + 1]) if n + 1 < len(work) else None
        rows = slice(d * edges + first, d * edges + first + size)
        edge_grad_ref[rows, :] = (upstream * slope_ref[rows, :].astype(F32)).astype(BF16)
        upstream = coming
        if first + size == edges:
            hot = hot_ref[d * count : (d + 1) * count, :]
            sums.append(dot(hot, edge_grad_ref[d * edges : (d + 1) * edges, :]))
    return sums


def halve(share_ref, keep_ref, give_ref):
    half = keep_ref.shape[0]
    core = lax.bitwise_and(lax.axis_index("rep"), 1)
    keep_ref[...] = share_ref[pl.ds(pl.multiple_of(core * half, half), half), :]
    give_ref[...] = share_ref[pl.ds(pl.multiple_of((1 - core) * half, half), half), :]


def process_back_kernel(steps, mesh_cap, *refs):
    regions = len(steps)
    cotangent_refs = refs[:regions]
    (
        turned_ref,
        first_ref,
        sent_ref,
        hot_ref,
        turned_hot_ref,
        hot_sent_ref,
        slope_ref,
        normed_ref,
        scaled_ref,
        mesh_grad_ref,
        keep_ref,
        give_ref,
        upstream_ref,
        slot_ref,
        recv_ref,
        share_ref,
        edge_grad_ref,
    ) = refs[regions:]
    latent = first_ref.shape[1]
    mesh_count = first_ref.shape[0] // regions
    slots = regions * mesh_cap
    me = lax.axis_index("space")
    for step, cotangent_ref in zip(steps, cotangent_refs):
        region = lax.bitwise_xor(me, step)
        at = pl.ds(pl.multiple_of(region * mesh_count, mesh_count), mesh_count)
        upstream_ref[at, :] = cotangent_ref[0].astype(F32)
    agg_grad = moments_back(normed_ref[...], scaled_ref[:, 0:1], upstream_ref[...]).astype(BF16)
    all_sums = edge_backward(
        regions, agg_grad, hot_ref, turned_hot_ref, slope_ref, edge_grad_ref
    )
    for d, sums in enumerate(all_sums):
        for s in range(regions):
            first = s * slots + d * mesh_cap
            slot_ref[first : first + mesh_cap, :] = sums[s * mesh_cap : (s + 1) * mesh_cap]
        recv_ref[d * mesh_count : (d + 1) * mesh_count, :] = sums[slots:].astype(BF16)
    slot_sum = slot_ref[...].astype(BF16)
    columns = share_ref.shape[0]
    mine = pl.ds(pl.multiple_of(me * columns, columns), columns)
    share_ref[:, :latent] = dot_first(sent_ref[:, mine], slot_sum).astype(BF16)
    share_ref[:, latent:] = dot_first(first_ref[:, mine], recv_ref[...]).astype(BF16)
    halve(share_ref, keep_ref, give_ref)
    returned = dot(slot_sum, turned_ref[:, latent : 2 * latent]).astype(BF16)
    grad = upstream_ref[...] + dot(recv_ref[...], turned_ref[:, 2 * latent :])
    for s in range(regions):
        rows = slice(s * mesh_count, (s + 1) * mesh_count)
        mesh_grad_ref[rows, :] = grad[rows] + dot(
            hot_sent_ref[rows, :], returned[s * slots : (s + 1) * slots]
        )


def encode_back_kernel(
    regions,
    grid_ref,
    mesh_ref,
    hot_ref,
    turned_hot_ref,
    slope_ref,
    normed_ref,
    scaled_ref,
    mesh_grad_ref,
    own_slot_ref,
    keep_ref,
    give_ref,
    slot_ref,
    recv_ref,
    share_ref,
    edge_grad_ref,
):
    latent = mesh_ref.shape[1]
    mesh_count = mesh_ref.shape[0] // regions
    listed = grid_ref.shape[0] // regions
    capacity = listed // 3
    me = lax.axis_index("space")
    agg_grad = moments_back(normed_ref[...], scaled_ref[:, 0:1], mesh_grad_ref[...]).astype(BF16)
    blank = jnp.zeros((capacity, latent), BF16)
    slot_ref[0:capacity, :] = blank
    slot_ref[regions * listed - capacity :, :] = blank
    all_sums = edge_backward(
        regions, agg_grad, hot_ref, turned_hot_ref, slope_ref, edge_grad_ref
    )
    for d, sums in enumerate(all_sums):
        sums = sums.astype(BF16)
        for j in range(3):
            source = d + j - 1
            if 0 <= source < regions:
                first = source * listed + (2 - j) * capacity
                slot_ref[first : first + capacity, :] = sums[j * capacity : (j + 1) * capacity]
        recv_ref[d * mesh_count : (d + 1) * mesh_count, :] = sums[listed:]
    columns = share_ref.shape[0]
    mine = pl.ds(pl.multiple_of(me * columns, columns), columns)
    share_ref[:, :latent] = dot_first(grid_ref[:, mine], slot_ref[...]).astype(BF16)
    share_ref[:, latent:] = dot_first(mesh_ref[:, mine], recv_ref[...]).astype(BF16)
    halve(share_ref, keep_ref, give_ref)
    own = pl.ds(pl.multiple_of(me * listed, listed), listed)
    own_slot_ref[...] = slot_ref[own, :]


def grid_back_kernel(turned_ref, pick_ref, own_slot_ref, grid_grad_ref):
    lists, _, capacity = pick_ref.shape
    latent = own_slot_ref.shape[1]
    returned = dot(own_slot_ref[...], turned_ref[:, :latent]).astype(BF16)
    total = None
    for i in range(lists):
        owner = one_hot(pick_ref[i], grid_grad_ref.shape[1])
        part = dot(owner, returned[i * capacity : (i + 1) * capacity])
        total = part if total is None else total + part
    grid_grad_ref[0] = total.astype(BF16)


def finish_kernel(one_ref, other_one_ref, two_ref, other_two_ref, weight_grad_ref):
    half, width = one_ref.shape
    core = lax.bitwise_and(lax.axis_index("rep"), 1)
    mine = pl.ds(pl.multiple_of(core * half, half), half)
    other = pl.ds(pl.multiple_of((1 - core) * half, half), half)
    weight_grad_ref[mine, :width] = one_ref[...].astype(F32)
    weight_grad_ref[other, :width] = other_one_ref[...].astype(F32)
    weight_grad_ref[mine, width:] = two_ref[...].astype(F32)
    weight_grad_ref[other, width:] = other_two_ref[...].astype(F32)


VMEM = pl.BlockSpec(memory_space=pltpu.VMEM)


def call(kernel, operands, outputs, scratch, flops, fetched=0, megabytes=40):
    hbm = pl.BlockSpec(memory_space=pltpu.HBM)
    return pl.pallas_call(
        kernel,
        out_shape=[jax.ShapeDtypeStruct(shape, kind) for shape, kind in outputs],
        in_specs=[hbm] * fetched + [VMEM] * (len(operands) - fetched),
        out_specs=[VMEM] * len(outputs),
        scratch_shapes=[pltpu.VMEM(shape, kind) for shape, kind in scratch]
        + ([pltpu.SemaphoreType.DMA((fetched,))] if fetched else []),
        compiler_params=pltpu.CompilerParams(vmem_limit_bytes=megabytes << 20),
        cost_estimate=pl.CostEstimate(flops=flops, bytes_accessed=4 << 20, transcendentals=0),
    )(*operands)


def swap(block, axis, bits):
    return lax.ppermute(block, axis, [(i, i ^ bits) for i in range(lax.axis_size(axis))])


def added(left, right):
    return (left.astype(F32) + right.astype(F32)).astype(BF16)


def summed_half(keep, give):
    half = added(keep, swap(give, "rep", 1))
    bit = 2
    while bit < lax.axis_size("rep"):
        half = added(half, swap(half, "rep", bit))
        bit *= 2
    return half, swap(half, "rep", 1)


def whole_sample_body(
    grid_latent,
    mesh_latent,
    mesh_cotangent,
    weights,
    g2m_pick,
    g2m_sender,
    g2m_receiver,
    m2m_pick,
    m2m_sender,
    m2m_receiver,
):
    regions = lax.axis_size("space")
    latent = weights.shape[0]
    listed = g2m_pick.shape[1] * g2m_pick.shape[2]
    mesh_count = mesh_latent.shape[1]
    mesh_cap = m2m_pick.shape[2]
    edges = g2m_sender.shape[0]
    columns = latent // regions
    half = columns // 2
    g2m_pick = g2m_pick.transpose(1, 0, 2)
    sources = (
        grid_latent,
        mesh_latent,
        g2m_pick,
        g2m_sender.reshape(1, -1),
        g2m_receiver.reshape(1, -1),
        m2m_pick,
        m2m_sender.reshape(1, -1),
        m2m_receiver.reshape(1, -1),
    )
    packed = call(
        pack_kernel,
        sources,
        [((listed + mesh_count + INDEX_ROWS, latent), BF16)],
        [((INDEX_ROWS, latent), F32)] + [(source.shape, source.dtype) for source in sources],
        10**7,
        fetched=len(sources),
        megabytes=56,
    )[0]
    packed, cotangent, weights = lax.optimization_barrier((packed, mesh_cotangent, weights))
    steps = (0, *range(2, regions), 1)
    packs = [packed] + [swap(packed, "space", step) for step in steps[1:]]
    near = swap(cotangent, "space", 1)
    weights, turned = call(
        weights_kernel,
        (weights,),
        [(weights.shape, BF16), ((latent, 3 * latent), BF16)],
        [],
        10**8,
        fetched=1,
    )
    packs[1], cotangent = lax.optimization_barrier((packs[1], cotangent))
    cotangents = [cotangent] + [swap(cotangent, "space", step) for step in steps[1:-1]] + [near]
    rows = regions * mesh_count
    slots = regions * mesh_cap
    (
        mesh_out,
        grid_all,
        mesh_all,
        mesh_first,
        mesh_sent,
        hot_one,
        hot_two,
        turned_one,
        turned_two,
        hot_sent,
        slope_one,
        slope_two,
        normed_one,
        scaled_one,
        normed_two,
        scaled_two,
    ) = call(
        functools.partial(forward_kernel, steps, listed, mesh_count, mesh_cap),
        (*packs, weights),
        [
            (mesh_latent.shape, BF16),
            ((regions * listed, latent), BF16),
            ((rows, latent), BF16),
            ((rows, latent), BF16),
            ((regions * slots, latent), BF16),
            ((regions * (listed + mesh_count), edges), BF16),
            ((regions * (slots + mesh_count), edges), BF16),
            ((regions * edges, listed + mesh_count), BF16),
            ((regions * edges, slots + mesh_count), BF16),
            ((rows, slots), BF16),
            ((regions * edges, latent), BF16),
            ((regions * edges, latent), BF16),
            ((rows, latent), F32),
            ((rows, 128), F32),
            ((rows, latent), F32),
            ((rows, 128), F32),
        ],
        [
            ((regions * INDEX_ROWS, latent), F32),
            ((regions * edges, latent), BF16),
            ((rows, latent), F32),
        ],
        2 * 10**9,
    )
    mesh_grad, keep_two, give_two = call(
        functools.partial(process_back_kernel, steps, mesh_cap),
        (
            *cotangents,
            turned,
            mesh_first,
            mesh_sent,
            hot_two,
            turned_two,
            hot_sent,
            slope_two,
            normed_two,
            scaled_two,
        ),
        [((rows, latent), F32)] + [((half, 2 * latent), BF16)] * 2,
        [
            ((rows, latent), F32),
            ((regions * slots, latent), F32),
            ((rows, latent), BF16),
            ((columns, 2 * latent), BF16),
            ((regions * edges, latent), BF16),
        ],
        10**9,
    )
    own_slots, keep_one, give_one = call(
        functools.partial(encode_back_kernel, regions),
        (
            grid_all,
            mesh_all,
            hot_one,
            turned_one,
            slope_one,
            normed_one,
            scaled_one,
            mesh_grad,
        ),
        [((listed, latent), BF16)] + [((half, 2 * latent), BF16)] * 2,
        [
            ((regions * listed, latent), BF16),
            ((rows, latent), BF16),
            ((columns, 2 * latent), BF16),
            ((regions * edges, latent), BF16),
        ],
        10**9,
    )
    grid_grad = call(
        grid_back_kernel,
        (turned, g2m_pick, own_slots),
        [(grid_latent.shape, BF16)],
        [],
        10**8,
    )[0]
    weight_grad = call(
        finish_kernel,
        (*summed_half(keep_one, give_one), *summed_half(keep_two, give_two)),
        [((columns, 4 * latent), F32)],
        [],
        10**6,
    )[0]
    return (mesh_out, grid_grad, weight_grad)


def solution(mesh):
    regions = mesh.shape["space"]
    samples = mesh.shape["rep"]

    def whole(*arguments):
        edges = arguments[5].shape[0] + arguments[8].shape[0]
        latent = arguments[3].shape[0]
        fits = edges * latent * 4 <= SAMPLE_EDGE_BYTES and latent % (128 * regions) == 0
        paired = all(n > 1 and n & (n - 1) == 0 for n in (regions, samples))
        return sharded(whole_sample_body if fits and paired else partitioned_body)(*arguments)

    def sharded(body):
        return jax.shard_map(
            body,
            mesh=mesh,
            in_specs=(
                P(("groups", "rep"), "space", None),
                P(("groups", "rep"), "space", None),
                P(("groups", "rep"), "space", None),
                P(),
                P("space", None, None),
                P("space"),
                P("space"),
                P("space", None, None),
                P("space"),
                P("space"),
            ),
            out_specs=(
                P(("groups", "rep"), "space", None),
                P(("groups", "rep"), "space", None),
                P(("groups", "space"), None),
            ),
            check_vma=False,
        )

    return whole
```

```python
import functools

import jax
import jax.numpy as jnp
from jax import lax
from jax.experimental import pallas as pl
from jax.experimental.pallas import tpu as pltpu
from jax.sharding import PartitionSpec as P

EPSILON = 1e-05


def with_halo(cells, sides, width):
    for axis, dim in sides:
        count = lax.axis_size(axis)
        ends = count - 1
        head = lax.slice_in_dim(cells, 0, width, axis=dim)
        tail = lax.slice_in_dim(cells, cells.shape[dim] - width, cells.shape[dim], axis=dim)
        cells = jnp.concatenate(
            [
                lax.ppermute(tail, axis, [(i, (i + 1) % count) for i in range(ends)]),
                cells,
                lax.ppermute(head, axis, [((i + 1) % count, i) for i in range(ends)]),
            ],
            axis=dim,
        )
    return cells


def swish(values):
    return values * jax.nn.sigmoid(values)


def swish_slope(values):
    squash = jax.nn.sigmoid(values)
    return squash * (1.0 + values * (1.0 - squash))


def norm_rows(values):
    centred = values - jnp.mean(values, -1, keepdims=True)
    return centred * lax.rsqrt(jnp.mean(centred * centred, -1, keepdims=True) + EPSILON)


def norm_rows_back(values, upstream):
    centred = values - jnp.mean(values, -1, keepdims=True)
    scaled = lax.rsqrt(jnp.mean(centred * centred, -1, keepdims=True) + EPSILON)
    normed = centred * scaled
    return scaled * (
        upstream
        - jnp.mean(upstream, -1, keepdims=True)
        - normed * jnp.mean(upstream * normed, -1, keepdims=True)
    )


def slot_rows(pick_row):
    listed = pick_row.reshape(-1)
    return listed


def mesh_route(outgoing, capacity, peer_count):
    columns = outgoing.shape[1]
    pieces = lax.all_to_all(
        outgoing.reshape(peer_count, capacity, columns),
        "space",
        split_axis=0,
        concat_axis=0,
        tiled=True,
    )
    arrived = pieces.reshape(peer_count * capacity, columns)
    return arrived


def grid_route(outgoing, capacity):
    columns = outgoing.shape[1]
    lists = outgoing.reshape(3, capacity, columns)
    rims = with_halo(jnp.stack([lists[0], lists[2]]), (("space", 0),), 1)
    return jnp.concatenate([rims[0], lists[1], rims[3]], axis=0)


def edge_pass(arrived, recv_table, located, receiver, w_send, w_recv):
    recv_proj = jnp.dot(recv_table, w_recv, preferred_element_type=jnp.float32)
    slot_proj = jnp.dot(arrived, w_send, preferred_element_type=jnp.float32)
    activation = slot_proj[located] + recv_proj[receiver]
    message = swish(activation).astype(jnp.bfloat16)
    member = (
        receiver[None, :] == jnp.arange(recv_table.shape[0], dtype=jnp.int32)[:, None]
    ).astype(jnp.bfloat16)
    summed = jnp.dot(member, message, preferred_element_type=jnp.float32)
    return (activation, member, summed)


def backward_pass(slot_count, located, activation, member, receiver, agg_grad, w_send):
    edge_grad = (agg_grad[receiver] * swish_slope(activation)).astype(jnp.bfloat16)
    recv_sum = jnp.dot(member, edge_grad, preferred_element_type=jnp.float32).astype(jnp.bfloat16)
    slot_member = (located[None, :] == jnp.arange(slot_count, dtype=jnp.int32)[:, None]).astype(
        jnp.bfloat16
    )
    slot_sum = jnp.dot(slot_member, edge_grad, preferred_element_type=jnp.float32).astype(
        jnp.bfloat16
    )
    returned = jnp.dot(slot_sum, w_send.T, preferred_element_type=jnp.float32).astype(jnp.bfloat16)
    return (recv_sum, slot_sum, returned)


def gather_back(listed, back_rows, row_count):
    owner = (listed[None, :] == jnp.arange(row_count, dtype=jnp.int32)[:, None]).astype(
        jnp.bfloat16
    )
    return jnp.dot(owner, back_rows, preferred_element_type=jnp.float32)


def partitioned_body(
    grid_latent,
    mesh_latent,
    mesh_cotangent,
    weights,
    g2m_pick,
    g2m_sender,
    g2m_receiver,
    m2m_pick,
    m2m_sender,
    m2m_receiver,
):
    grid_rows = grid_latent[0]
    mesh_rows = mesh_latent[0]
    upstream = mesh_cotangent[0].astype(jnp.float32)
    latent = weights.shape[0]
    encode_sender = weights[:, :latent]
    encode_receiver = weights[:, latent : 2 * latent]
    process_sender = weights[:, 2 * latent : 3 * latent]
    process_receiver = weights[:, 3 * latent :]
    peer_count = lax.axis_size("space")
    grid_cap = g2m_pick.shape[2]
    mesh_cap = m2m_pick.shape[2]
    grid_listed = g2m_pick[0].reshape(-1)
    grid_arrived = grid_route(grid_rows[grid_listed], grid_cap)
    act_first, member_first, summed_first = edge_pass(
        grid_arrived, mesh_rows, g2m_sender, g2m_receiver, encode_sender, encode_receiver
    )
    mesh_first = (mesh_rows.astype(jnp.float32) + norm_rows(summed_first)).astype(jnp.bfloat16)
    mesh_listed = slot_rows(m2m_pick[0])
    mesh_arrived = mesh_route(mesh_first[mesh_listed], mesh_cap, peer_count)
    act_second, member_second, summed_second = edge_pass(
        mesh_arrived, mesh_first, m2m_sender, m2m_receiver, process_sender, process_receiver
    )
    mesh_final = (mesh_first.astype(jnp.float32) + norm_rows(summed_second)).astype(jnp.bfloat16)
    agg_second = norm_rows_back(summed_second, upstream)
    recv_second, slot_second, returned_second = backward_pass(
        mesh_arrived.shape[0],
        m2m_sender,
        act_second,
        member_second,
        m2m_receiver,
        agg_second,
        process_sender,
    )
    back_second = mesh_route(returned_second, mesh_cap, peer_count)
    mesh_grad = upstream + jnp.dot(
        recv_second, process_receiver.T, preferred_element_type=jnp.float32
    )
    mesh_grad = mesh_grad + gather_back(mesh_listed, back_second, mesh_rows.shape[0])
    agg_first = norm_rows_back(summed_first, mesh_grad)
    recv_first, slot_first, returned_first = backward_pass(
        grid_arrived.shape[0],
        g2m_sender,
        act_first,
        member_first,
        g2m_receiver,
        agg_first,
        encode_sender,
    )
    back_first = grid_route(returned_first, grid_cap)
    grid_grad = gather_back(grid_listed, back_first, grid_rows.shape[0]).astype(jnp.bfloat16)
    factor_pairs = (
        (grid_arrived, slot_first),
        (mesh_rows, recv_first),
        (mesh_arrived, slot_second),
        (mesh_first, recv_second),
    )
    blocks = []
    for first_factor, second_factor in factor_pairs:
        blocks.append(
            lax.dot_general(
                first_factor,
                second_factor,
                (((0,), (0,)), ((), ())),
                preferred_element_type=jnp.float32,
            )
        )
    shares = lax.psum_scatter(
        jnp.concatenate(blocks, axis=1).astype(jnp.bfloat16),
        "space",
        scatter_dimension=0,
        tiled=True,
    )
    weight_grad = lax.psum(shares, "rep").astype(jnp.float32)
    return (mesh_final[None], grid_grad[None], weight_grad)


F32 = jnp.float32
BF16 = jnp.bfloat16
INDEX_ROWS = 8
SAMPLE_EDGE_BYTES = 8 << 20


def dot(left, right):
    return jnp.dot(left, right, preferred_element_type=F32)


def dot_first(left, right):
    return lax.dot_general(left, right, (((0,), (0,)), ((), ())), preferred_element_type=F32)


def one_hot(labels, count):
    rows = lax.broadcasted_iota(jnp.int32, (count, labels.shape[-1]), 0)
    return (rows == labels).astype(F32).astype(BF16)


def row_moments(values):
    centred = values - jnp.mean(values, -1, keepdims=True)
    return centred, lax.rsqrt(jnp.mean(centred * centred, -1, keepdims=True) + EPSILON)


def moments_back(normed, scaled, upstream):
    return scaled * (
        upstream
        - jnp.mean(upstream, -1, keepdims=True)
        - normed * jnp.mean(upstream * normed, -1, keepdims=True)
    )


def fetch(pairs, semaphores):
    copies = [
        pltpu.make_async_copy(source, target, semaphores.at[n])
        for n, (source, target) in enumerate(pairs)
    ]
    for copy in copies:
        copy.start()
    for copy in copies:
        copy.wait()


def pack_kernel(*refs):
    sources, packed_ref, index_ref = refs[:8], refs[8], refs[9]
    local, semaphores = refs[10:18], refs[18]
    fetch(list(zip(sources, local)), semaphores)
    (
        grid_ref,
        mesh_ref,
        g2m_pick_ref,
        g2m_sender_ref,
        g2m_receiver_ref,
        m2m_pick_ref,
        m2m_sender_ref,
        m2m_receiver_ref,
    ) = local
    lists, _, capacity = g2m_pick_ref.shape
    mesh_count = mesh_ref.shape[1]
    regions, mesh_cap = m2m_pick_ref.shape[1:]
    edges = g2m_sender_ref.shape[1]
    grid_rows = grid_ref[0]
    for i in range(lists):
        picked = one_hot(g2m_pick_ref[i], grid_rows.shape[0])
        packed_ref[i * capacity : (i + 1) * capacity, :] = dot_first(picked, grid_rows).astype(BF16)
    first = lists * capacity
    packed_ref[first : first + mesh_count, :] = mesh_ref[0]
    index_ref[...] = jnp.zeros_like(index_ref)
    index_ref[0:1, 0:edges] = g2m_sender_ref[...].astype(F32)
    index_ref[0:1, edges : 2 * edges] = g2m_receiver_ref[...].astype(F32)
    index_ref[1:2, 0:edges] = m2m_sender_ref[...].astype(F32)
    index_ref[1:2, edges : 2 * edges] = m2m_receiver_ref[...].astype(F32)
    slots = regions * mesh_cap
    lane = lax.broadcasted_iota(jnp.int32, (mesh_cap, slots), 1)
    spread = (lane % mesh_cap == lax.broadcasted_iota(jnp.int32, (mesh_cap, slots), 0)).astype(F32)
    spread = dot(m2m_pick_ref[0].astype(F32).astype(BF16), spread.astype(BF16))
    lane = lax.broadcasted_iota(jnp.int32, (regions, slots), 1)
    owned = lane // mesh_cap == lax.broadcasted_iota(jnp.int32, (regions, slots), 0)
    index_ref[2:3, 0:slots] = jnp.sum(jnp.where(owned, spread, 0.0), 0, keepdims=True)
    packed_ref[first + mesh_count :, :] = index_ref[...].astype(BF16)


def weights_kernel(source_ref, weights_ref, turned_ref, semaphores):
    fetch([(source_ref, weights_ref)], semaphores)
    latent = weights_ref.shape[0]
    for n, block in enumerate((0, 2, 3)):
        turned_ref[:, n * latent : (n + 1) * latent] = weights_ref[
            :, block * latent : (block + 1) * latent
        ].T


def edge_blocks(edges):
    size = min(edges, 128)
    return [(first, min(size, edges - first)) for first in range(0, edges, size)]


def edge_forward(tables, hot_ref, turned_hot_ref, slope_ref, message_ref, mesh_count):
    regions = len(tables)
    edges = slope_ref.shape[0] // regions
    count = hot_ref.shape[0] // regions
    work = [(d, first, size) for d in range(regions) for first, size in edge_blocks(edges)]

    def gathered(d, first, size):
        rows = slice(d * edges + first, d * edges + first + size)
        return dot(turned_hot_ref[rows, :], tables[d])

    sums = []
    activation = gathered(*work[0])
    for n, (d, first, size) in enumerate(work):
        coming = gathered(*work[n + 1]) if n + 1 < len(work) else None
        squash = 0.5 + 0.5 * jnp.tanh(0.5 * activation)
        message = activation * squash
        rows = slice(d * edges + first, d * edges + first + size)
        slope_ref[rows, :] = (squash + message * (1.0 - squash)).astype(BF16)
        message_ref[rows, :] = message.astype(BF16)
        activation = coming
        if first + size == edges:
            hot = hot_ref[(d + 1) * count - mesh_count : (d + 1) * count, :]
            sums.append(dot(hot, message_ref[d * edges : (d + 1) * edges, :]))
    return sums


def forward_kernel(
    steps,
    listed,
    mesh_count,
    mesh_cap,
    *refs,
):
    regions = len(steps)
    packed_refs = refs[:regions]
    (
        weights_ref,
        mesh_out_ref,
        grid_ref,
        mesh_ref,
        first_ref,
        sent_ref,
        hot_one_ref,
        hot_two_ref,
        turned_one_ref,
        turned_two_ref,
        hot_sent_ref,
        slope_one_ref,
        slope_two_ref,
        normed_one_ref,
        scaled_one_ref,
        normed_two_ref,
        scaled_two_ref,
        index_ref,
        message_ref,
        sum_ref,
    ) = refs[regions:]
    latent = weights_ref.shape[0]
    edges = slope_one_ref.shape[0] // regions
    capacity = listed // 3
    slots = regions * mesh_cap
    me = lax.axis_index("space")
    for step, packed_ref in zip(steps, packed_refs):
        region = lax.bitwise_xor(me, step)
        at = lambda rows: pl.ds(pl.multiple_of(region * rows, rows), rows)
        grid_ref[at(listed), :] = packed_ref[:listed, :]
        mesh_ref[at(mesh_count), :] = packed_ref[listed : listed + mesh_count, :]
        index_ref[at(INDEX_ROWS), :] = packed_ref[listed + mesh_count :, :].astype(F32)

    grid_proj = dot(grid_ref[...], weights_ref[:, :latent])
    mesh_proj = dot(mesh_ref[...], weights_ref[:, latent : 2 * latent])
    for d in range(regions):
        index = index_ref[d * INDEX_ROWS : (d + 1) * INDEX_ROWS, :].astype(jnp.int32)
        for row, senders, hot_ref, turned_ref in (
            (0, listed, hot_one_ref, turned_one_ref),
            (1, slots, hot_two_ref, turned_two_ref),
        ):
            count = senders + mesh_count
            hot = jnp.concatenate(
                [
                    one_hot(index[row : row + 1, :edges], senders),
                    one_hot(index[row : row + 1, edges:], mesh_count),
                ],
                axis=0,
            )
            hot_ref[d * count : (d + 1) * count, :] = hot
            turned_ref[d * edges : (d + 1) * edges, :] = hot.T
        hot_sent_ref[d * mesh_count : (d + 1) * mesh_count, :] = one_hot(
            index[2:3, :slots], mesh_count
        )

    blank = jnp.zeros((capacity, latent), F32)
    tables = []
    for d in range(regions):
        before = (d - 1) * listed + 2 * capacity
        within = d * listed + capacity
        after = (d + 1) * listed
        tables.append(
            jnp.concatenate(
                [
                    grid_proj[before : before + capacity] if d > 0 else blank,
                    grid_proj[within : within + capacity],
                    grid_proj[after : after + capacity] if d < regions - 1 else blank,
                    mesh_proj[d * mesh_count : (d + 1) * mesh_count],
                ],
                axis=0,
            ).astype(BF16)
        )
    sums = edge_forward(
        tables, hot_one_ref, turned_one_ref, slope_one_ref, message_ref, mesh_count
    )
    for d in range(regions):
        sum_ref[d * mesh_count : (d + 1) * mesh_count, :] = sums[d]
    centred, scaled = row_moments(sum_ref[...])
    normed = centred * scaled
    normed_one_ref[...] = normed
    scaled_one_ref[...] = jnp.broadcast_to(scaled, scaled_one_ref.shape)
    first_ref[...] = (mesh_ref[...].astype(F32) + normed).astype(BF16)

    for s in range(regions):
        rows = slice(s * mesh_count, (s + 1) * mesh_count)
        sent_ref[s * slots : (s + 1) * slots, :] = dot_first(
            hot_sent_ref[rows, :], first_ref[rows, :]
        ).astype(BF16)
    sent_proj = dot(sent_ref[...], weights_ref[:, 2 * latent : 3 * latent])
    first_proj = dot(first_ref[...], weights_ref[:, 3 * latent :])
    tables = []
    for d in range(regions):
        pieces = [
            sent_proj[s * slots + d * mesh_cap : s * slots + (d + 1) * mesh_cap]
            for s in range(regions)
        ]
        tables.append(
            jnp.concatenate(
                pieces + [first_proj[d * mesh_count : (d + 1) * mesh_count]], axis=0
            ).astype(BF16)
        )
    sums = edge_forward(
        tables, hot_two_ref, turned_two_ref, slope_two_ref, message_ref, mesh_count
    )
    for d in range(regions):
        sum_ref[d * mesh_count : (d + 1) * mesh_count, :] = sums[d]
    centred, scaled = row_moments(sum_ref[...])
    normed_two_ref[...] = centred * scaled
    scaled_two_ref[...] = jnp.broadcast_to(scaled, scaled_two_ref.shape)
    own = pl.ds(pl.multiple_of(me * mesh_count, mesh_count), mesh_count)
    mesh_out_ref[0] = (first_ref[own, :].astype(F32) + normed_two_ref[own, :]).astype(BF16)


def edge_backward(regions, agg_grad, hot_ref, turned_hot_ref, slope_ref, edge_grad_ref):
    edges = slope_ref.shape[0] // regions
    count = hot_ref.shape[0] // regions
    mesh_count = agg_grad.shape[0] // regions
    blank = jnp.zeros((count - mesh_count, agg_grad.shape[1]), BF16)
    work = [(d, first, size) for d in range(regions) for first, size in edge_blocks(edges)]

    def gathered(d, first, size):
        rows = slice(d * edges + first, d * edges + first + size)
        table = jnp.concatenate([blank, agg_grad[d * mesh_count : (d + 1) * mesh_count]], axis=0)
        return dot(turned_hot_ref[rows, :], table)

    sums = []
    upstream = gathered(*work[0])
    for n, (d, first, size) in enumerate(work):
        coming = gathered(*work[n + 1]) if n + 1 < len(work) else None
        rows = slice(d * edges + first, d * edges + first + size)
        edge_grad_ref[rows, :] = (upstream * slope_ref[rows, :].astype(F32)).astype(BF16)
        upstream = coming
        if first + size == edges:
            hot = hot_ref[d * count : (d + 1) * count, :]
            sums.append(dot(hot, edge_grad_ref[d * edges : (d + 1) * edges, :]))
    return sums


def halve(share_ref, keep_ref, give_ref):
    half = keep_ref.shape[0]
    core = lax.bitwise_and(lax.axis_index("rep"), 1)
    keep_ref[...] = share_ref[pl.ds(pl.multiple_of(core * half, half), half), :]
    give_ref[...] = share_ref[pl.ds(pl.multiple_of((1 - core) * half, half), half), :]


def process_back_kernel(steps, mesh_cap, *refs):
    regions = len(steps)
    cotangent_refs = refs[:regions]
    (
        turned_ref,
        first_ref,
        sent_ref,
        hot_ref,
        turned_hot_ref,
        hot_sent_ref,
        slope_ref,
        normed_ref,
        scaled_ref,
        mesh_grad_ref,
        keep_ref,
        give_ref,
        upstream_ref,
        slot_ref,
        recv_ref,
        share_ref,
        edge_grad_ref,
    ) = refs[regions:]
    latent = first_ref.shape[1]
    mesh_count = first_ref.shape[0] // regions
    slots = regions * mesh_cap
    me = lax.axis_index("space")
    for step, cotangent_ref in zip(steps, cotangent_refs):
        region = lax.bitwise_xor(me, step)
        at = pl.ds(pl.multiple_of(region * mesh_count, mesh_count), mesh_count)
        upstream_ref[at, :] = cotangent_ref[0].astype(F32)
    agg_grad = moments_back(normed_ref[...], scaled_ref[:, 0:1], upstream_ref[...]).astype(BF16)
    all_sums = edge_backward(
        regions, agg_grad, hot_ref, turned_hot_ref, slope_ref, edge_grad_ref
    )
    for d, sums in enumerate(all_sums):
        for s in range(regions):
            first = s * slots + d * mesh_cap
            slot_ref[first : first + mesh_cap, :] = sums[s * mesh_cap : (s + 1) * mesh_cap]
        recv_ref[d * mesh_count : (d + 1) * mesh_count, :] = sums[slots:].astype(BF16)
    slot_sum = slot_ref[...].astype(BF16)
    columns = share_ref.shape[0]
    mine = pl.ds(pl.multiple_of(me * columns, columns), columns)
    share_ref[:, :latent] = dot_first(sent_ref[:, mine], slot_sum).astype(BF16)
    share_ref[:, latent:] = dot_first(first_ref[:, mine], recv_ref[...]).astype(BF16)
    halve(share_ref, keep_ref, give_ref)
    returned = dot(slot_sum, turned_ref[:, latent : 2 * latent]).astype(BF16)
    grad = upstream_ref[...] + dot(recv_ref[...], turned_ref[:, 2 * latent :])
    for s in range(regions):
        rows = slice(s * mesh_count, (s + 1) * mesh_count)
        mesh_grad_ref[rows, :] = grad[rows] + dot(
            hot_sent_ref[rows, :], returned[s * slots : (s + 1) * slots]
        )


def encode_back_kernel(
    regions,
    grid_ref,
    mesh_ref,
    hot_ref,
    turned_hot_ref,
    slope_ref,
    normed_ref,
    scaled_ref,
    mesh_grad_ref,
    own_slot_ref,
    keep_ref,
    give_ref,
    slot_ref,
    recv_ref,
    share_ref,
    edge_grad_ref,
):
    latent = mesh_ref.shape[1]
    mesh_count = mesh_ref.shape[0] // regions
    listed = grid_ref.shape[0] // regions
    capacity = listed // 3
    me = lax.axis_index("space")
    agg_grad = moments_back(normed_ref[...], scaled_ref[:, 0:1], mesh_grad_ref[...]).astype(BF16)
    blank = jnp.zeros((capacity, latent), BF16)
    slot_ref[0:capacity, :] = blank
    slot_ref[regions * listed - capacity :, :] = blank
    all_sums = edge_backward(
        regions, agg_grad, hot_ref, turned_hot_ref, slope_ref, edge_grad_ref
    )
    for d, sums in enumerate(all_sums):
        sums = sums.astype(BF16)
        for j in range(3):
            source = d + j - 1
            if 0 <= source < regions:
                first = source * listed + (2 - j) * capacity
                slot_ref[first : first + capacity, :] = sums[j * capacity : (j + 1) * capacity]
        recv_ref[d * mesh_count : (d + 1) * mesh_count, :] = sums[listed:]
    columns = share_ref.shape[0]
    mine = pl.ds(pl.multiple_of(me * columns, columns), columns)
    share_ref[:, :latent] = dot_first(grid_ref[:, mine], slot_ref[...]).astype(BF16)
    share_ref[:, latent:] = dot_first(mesh_ref[:, mine], recv_ref[...]).astype(BF16)
    halve(share_ref, keep_ref, give_ref)
    own = pl.ds(pl.multiple_of(me * listed, listed), listed)
    own_slot_ref[...] = slot_ref[own, :]


def grid_back_kernel(turned_ref, pick_ref, own_slot_ref, grid_grad_ref):
    lists, _, capacity = pick_ref.shape
    latent = own_slot_ref.shape[1]
    returned = dot(own_slot_ref[...], turned_ref[:, :latent]).astype(BF16)
    total = None
    for i in range(lists):
        owner = one_hot(pick_ref[i], grid_grad_ref.shape[1])
        part = dot(owner, returned[i * capacity : (i + 1) * capacity])
        total = part if total is None else total + part
    grid_grad_ref[0] = total.astype(BF16)


def finish_kernel(one_ref, other_one_ref, two_ref, other_two_ref, weight_grad_ref):
    half, width = one_ref.shape
    core = lax.bitwise_and(lax.axis_index("rep"), 1)
    mine = pl.ds(pl.multiple_of(core * half, half), half)
    other = pl.ds(pl.multiple_of((1 - core) * half, half), half)
    weight_grad_ref[mine, :width] = one_ref[...].astype(F32)
    weight_grad_ref[other, :width] = other_one_ref[...].astype(F32)
    weight_grad_ref[mine, width:] = two_ref[...].astype(F32)
    weight_grad_ref[other, width:] = other_two_ref[...].astype(F32)


VMEM = pl.BlockSpec(memory_space=pltpu.VMEM)


def call(kernel, operands, outputs, scratch, flops, fetched=0, megabytes=40):
    hbm = pl.BlockSpec(memory_space=pltpu.HBM)
    return pl.pallas_call(
        kernel,
        out_shape=[jax.ShapeDtypeStruct(shape, kind) for shape, kind in outputs],
        in_specs=[hbm] * fetched + [VMEM] * (len(operands) - fetched),
        out_specs=[VMEM] * len(outputs),
        scratch_shapes=[pltpu.VMEM(shape, kind) for shape, kind in scratch]
        + ([pltpu.SemaphoreType.DMA((fetched,))] if fetched else []),
        compiler_params=pltpu.CompilerParams(vmem_limit_bytes=megabytes << 20),
        cost_estimate=pl.CostEstimate(flops=flops, bytes_accessed=4 << 20, transcendentals=0),
    )(*operands)


def swap(block, axis, bits):
    return lax.ppermute(block, axis, [(i, i ^ bits) for i in range(lax.axis_size(axis))])


def added(left, right):
    return (left.astype(F32) + right.astype(F32)).astype(BF16)


def summed_half(keep, give):
    half = added(keep, swap(give, "rep", 1))
    bit = 2
    while bit < lax.axis_size("rep"):
        half = added(half, swap(half, "rep", bit))
        bit *= 2
    return half, swap(half, "rep", 1)


def whole_sample_body(
    grid_latent,
    mesh_latent,
    mesh_cotangent,
    weights,
    g2m_pick,
    g2m_sender,
    g2m_receiver,
    m2m_pick,
    m2m_sender,
    m2m_receiver,
):
    regions = lax.axis_size("space")
    latent = weights.shape[0]
    listed = g2m_pick.shape[1] * g2m_pick.shape[2]
    mesh_count = mesh_latent.shape[1]
    mesh_cap = m2m_pick.shape[2]
    edges = g2m_sender.shape[0]
    columns = latent // regions
    half = columns // 2
    g2m_pick = g2m_pick.transpose(1, 0, 2)
    sources = (
        grid_latent,
        mesh_latent,
        g2m_pick,
        g2m_sender.reshape(1, -1),
        g2m_receiver.reshape(1, -1),
        m2m_pick,
        m2m_sender.reshape(1, -1),
        m2m_receiver.reshape(1, -1),
    )
    packed = call(
        pack_kernel,
        sources,
        [((listed + mesh_count + INDEX_ROWS, latent), BF16)],
        [((INDEX_ROWS, latent), F32)] + [(source.shape, source.dtype) for source in sources],
        10**7,
        fetched=len(sources),
        megabytes=56,
    )[0]
    packed, cotangent, weights = lax.optimization_barrier((packed, mesh_cotangent, weights))
    steps = (0, *range(2, regions), 1)
    packs = [packed] + [swap(packed, "space", step) for step in steps[1:]]
    near = swap(cotangent, "space", 1)
    weights, turned = call(
        weights_kernel,
        (weights,),
        [(weights.shape, BF16), ((latent, 3 * latent), BF16)],
        [],
        10**8,
        fetched=1,
    )
    near, cotangent = lax.optimization_barrier((near, cotangent))
    cotangents = [cotangent] + [swap(cotangent, "space", step) for step in steps[1:-1]] + [near]
    rows = regions * mesh_count
    slots = regions * mesh_cap
    (
        mesh_out,
        grid_all,
        mesh_all,
        mesh_first,
        mesh_sent,
        hot_one,
        hot_two,
        turned_one,
        turned_two,
        hot_sent,
        slope_one,
        slope_two,
        normed_one,
        scaled_one,
        normed_two,
        scaled_two,
    ) = call(
        functools.partial(forward_kernel, steps, listed, mesh_count, mesh_cap),
        (*packs, weights),
        [
            (mesh_latent.shape, BF16),
            ((regions * listed, latent), BF16),
            ((rows, latent), BF16),
            ((rows, latent), BF16),
            ((regions * slots, latent), BF16),
            ((regions * (listed + mesh_count), edges), BF16),
            ((regions * (slots + mesh_count), edges), BF16),
            ((regions * edges, listed + mesh_count), BF16),
            ((regions * edges, slots + mesh_count), BF16),
            ((rows, slots), BF16),
            ((regions * edges, latent), BF16),
            ((regions * edges, latent), BF16),
            ((rows, latent), F32),
            ((rows, 128), F32),
            ((rows, latent), F32),
            ((rows, 128), F32),
        ],
        [
            ((regions * INDEX_ROWS, latent), F32),
            ((regions * edges, latent), BF16),
            ((rows, latent), F32),
        ],
        2 * 10**9,
    )
    mesh_grad, keep_two, give_two = call(
        functools.partial(process_back_kernel, steps, mesh_cap),
        (
            *cotangents,
            turned,
            mesh_first,
            mesh_sent,
            hot_two,
            turned_two,
            hot_sent,
            slope_two,
            normed_two,
            scaled_two,
        ),
        [((rows, latent), F32)] + [((half, 2 * latent), BF16)] * 2,
        [
            ((rows, latent), F32),
            ((regions * slots, latent), F32),
            ((rows, latent), BF16),
            ((columns, 2 * latent), BF16),
            ((regions * edges, latent), BF16),
        ],
        10**9,
    )
    own_slots, keep_one, give_one = call(
        functools.partial(encode_back_kernel, regions),
        (
            grid_all,
            mesh_all,
            hot_one,
            turned_one,
            slope_one,
            normed_one,
            scaled_one,
            mesh_grad,
        ),
        [((listed, latent), BF16)] + [((half, 2 * latent), BF16)] * 2,
        [
            ((regions * listed, latent), BF16),
            ((rows, latent), BF16),
            ((columns, 2 * latent), BF16),
            ((regions * edges, latent), BF16),
        ],
        10**9,
    )
    grid_grad = call(
        grid_back_kernel,
        (turned, g2m_pick, own_slots),
        [(grid_latent.shape, BF16)],
        [],
        10**8,
    )[0]
    weight_grad = call(
        finish_kernel,
        (*summed_half(keep_one, give_one), *summed_half(keep_two, give_two)),
        [((columns, 4 * latent), F32)],
        [],
        10**6,
    )[0]
    return (mesh_out, grid_grad, weight_grad)


def solution(mesh):
    regions = mesh.shape["space"]
    samples = mesh.shape["rep"]

    def whole(*arguments):
        edges = arguments[5].shape[0] + arguments[8].shape[0]
        latent = arguments[3].shape[0]
        fits = edges * latent * 4 <= SAMPLE_EDGE_BYTES and latent % (128 * regions) == 0
        paired = all(n > 1 and n & (n - 1) == 0 for n in (regions, samples))
        return sharded(whole_sample_body if fits and paired else partitioned_body)(*arguments)

    def sharded(body):
        return jax.shard_map(
            body,
            mesh=mesh,
            in_specs=(
                P(("groups", "rep"), "space", None),
                P(("groups", "rep"), "space", None),
                P(("groups", "rep"), "space", None),
                P(),
                P("space", None, None),
                P("space"),
                P("space"),
                P("space", None, None),
                P("space"),
                P("space"),
            ),
            out_specs=(
                P(("groups", "rep"), "space", None),
                P(("groups", "rep"), "space", None),
                P(("groups", "space"), None),
            ),
            check_vma=False,
        )

    return whole
```

```python
import functools

import jax
import jax.numpy as jnp
from jax import lax
from jax.experimental import pallas as pl
from jax.experimental.pallas import tpu as pltpu
from jax.sharding import PartitionSpec as P

EPSILON = 1e-05


def with_halo(cells, sides, width):
    for axis, dim in sides:
        count = lax.axis_size(axis)
        ends = count - 1
        head = lax.slice_in_dim(cells, 0, width, axis=dim)
        tail = lax.slice_in_dim(cells, cells.shape[dim] - width, cells.shape[dim], axis=dim)
        cells = jnp.concatenate(
            [
                lax.ppermute(tail, axis, [(i, (i + 1) % count) for i in range(ends)]),
                cells,
                lax.ppermute(head, axis, [((i + 1) % count, i) for i in range(ends)]),
            ],
            axis=dim,
        )
    return cells


def swish(values):
    return values * jax.nn.sigmoid(values)


def swish_slope(values):
    squash = jax.nn.sigmoid(values)
    return squash * (1.0 + values * (1.0 - squash))


def norm_rows(values):
    centred = values - jnp.mean(values, -1, keepdims=True)
    return centred * lax.rsqrt(jnp.mean(centred * centred, -1, keepdims=True) + EPSILON)


def norm_rows_back(values, upstream):
    centred = values - jnp.mean(values, -1, keepdims=True)
    scaled = lax.rsqrt(jnp.mean(centred * centred, -1, keepdims=True) + EPSILON)
    normed = centred * scaled
    return scaled * (
        upstream
        - jnp.mean(upstream, -1, keepdims=True)
        - normed * jnp.mean(upstream * normed, -1, keepdims=True)
    )


def slot_rows(pick_row):
    listed = pick_row.reshape(-1)
    return listed


def mesh_route(outgoing, capacity, peer_count):
    columns = outgoing.shape[1]
    pieces = lax.all_to_all(
        outgoing.reshape(peer_count, capacity, columns),
        "space",
        split_axis=0,
        concat_axis=0,
        tiled=True,
    )
    arrived = pieces.reshape(peer_count * capacity, columns)
    return arrived


def grid_route(outgoing, capacity):
    columns = outgoing.shape[1]
    lists = outgoing.reshape(3, capacity, columns)
    rims = with_halo(jnp.stack([lists[0], lists[2]]), (("space", 0),), 1)
    return jnp.concatenate([rims[0], lists[1], rims[3]], axis=0)


def edge_pass(arrived, recv_table, located, receiver, w_send, w_recv):
    recv_proj = jnp.dot(recv_table, w_recv, preferred_element_type=jnp.float32)
    slot_proj = jnp.dot(arrived, w_send, preferred_element_type=jnp.float32)
    activation = slot_proj[located] + recv_proj[receiver]
    message = swish(activation).astype(jnp.bfloat16)
    member = (
        receiver[None, :] == jnp.arange(recv_table.shape[0], dtype=jnp.int32)[:, None]
    ).astype(jnp.bfloat16)
    summed = jnp.dot(member, message, preferred_element_type=jnp.float32)
    return (activation, member, summed)


def backward_pass(slot_count, located, activation, member, receiver, agg_grad, w_send):
    edge_grad = (agg_grad[receiver] * swish_slope(activation)).astype(jnp.bfloat16)
    recv_sum = jnp.dot(member, edge_grad, preferred_element_type=jnp.float32).astype(jnp.bfloat16)
    slot_member = (located[None, :] == jnp.arange(slot_count, dtype=jnp.int32)[:, None]).astype(
        jnp.bfloat16
    )
    slot_sum = jnp.dot(slot_member, edge_grad, preferred_element_type=jnp.float32).astype(
        jnp.bfloat16
    )
    returned = jnp.dot(slot_sum, w_send.T, preferred_element_type=jnp.float32).astype(jnp.bfloat16)
    return (recv_sum, slot_sum, returned)


def gather_back(listed, back_rows, row_count):
    owner = (listed[None, :] == jnp.arange(row_count, dtype=jnp.int32)[:, None]).astype(
        jnp.bfloat16
    )
    return jnp.dot(owner, back_rows, preferred_element_type=jnp.float32)


def partitioned_body(
    grid_latent,
    mesh_latent,
    mesh_cotangent,
    weights,
    g2m_pick,
    g2m_sender,
    g2m_receiver,
    m2m_pick,
    m2m_sender,
    m2m_receiver,
):
    grid_rows = grid_latent[0]
    mesh_rows = mesh_latent[0]
    upstream = mesh_cotangent[0].astype(jnp.float32)
    latent = weights.shape[0]
    encode_sender = weights[:, :latent]
    encode_receiver = weights[:, latent : 2 * latent]
    process_sender = weights[:, 2 * latent : 3 * latent]
    process_receiver = weights[:, 3 * latent :]
    peer_count = lax.axis_size("space")
    grid_cap = g2m_pick.shape[2]
    mesh_cap = m2m_pick.shape[2]
    grid_listed = g2m_pick[0].reshape(-1)
    grid_arrived = grid_route(grid_rows[grid_listed], grid_cap)
    act_first, member_first, summed_first = edge_pass(
        grid_arrived, mesh_rows, g2m_sender, g2m_receiver, encode_sender, encode_receiver
    )
    mesh_first = (mesh_rows.astype(jnp.float32) + norm_rows(summed_first)).astype(jnp.bfloat16)
    mesh_listed = slot_rows(m2m_pick[0])
    mesh_arrived = mesh_route(mesh_first[mesh_listed], mesh_cap, peer_count)
    act_second, member_second, summed_second = edge_pass(
        mesh_arrived, mesh_first, m2m_sender, m2m_receiver, process_sender, process_receiver
    )
    mesh_final = (mesh_first.astype(jnp.float32) + norm_rows(summed_second)).astype(jnp.bfloat16)
    agg_second = norm_rows_back(summed_second, upstream)
    recv_second, slot_second, returned_second = backward_pass(
        mesh_arrived.shape[0],
        m2m_sender,
        act_second,
        member_second,
        m2m_receiver,
        agg_second,
        process_sender,
    )
    back_second = mesh_route(returned_second, mesh_cap, peer_count)
    mesh_grad = upstream + jnp.dot(
        recv_second, process_receiver.T, preferred_element_type=jnp.float32
    )
    mesh_grad = mesh_grad + gather_back(mesh_listed, back_second, mesh_rows.shape[0])
    agg_first = norm_rows_back(summed_first, mesh_grad)
    recv_first, slot_first, returned_first = backward_pass(
        grid_arrived.shape[0],
        g2m_sender,
        act_first,
        member_first,
        g2m_receiver,
        agg_first,
        encode_sender,
    )
    back_first = grid_route(returned_first, grid_cap)
    grid_grad = gather_back(grid_listed, back_first, grid_rows.shape[0]).astype(jnp.bfloat16)
    factor_pairs = (
        (grid_arrived, slot_first),
        (mesh_rows, recv_first),
        (mesh_arrived, slot_second),
        (mesh_first, recv_second),
    )
    blocks = []
    for first_factor, second_factor in factor_pairs:
        blocks.append(
            lax.dot_general(
                first_factor,
                second_factor,
                (((0,), (0,)), ((), ())),
                preferred_element_type=jnp.float32,
            )
        )
    shares = lax.psum_scatter(
        jnp.concatenate(blocks, axis=1).astype(jnp.bfloat16),
        "space",
        scatter_dimension=0,
        tiled=True,
    )
    weight_grad = lax.psum(shares, "rep").astype(jnp.float32)
    return (mesh_final[None], grid_grad[None], weight_grad)


F32 = jnp.float32
BF16 = jnp.bfloat16
INDEX_ROWS = 8
SAMPLE_EDGE_BYTES = 8 << 20


def dot(left, right):
    return jnp.dot(left, right, preferred_element_type=F32)


def dot_first(left, right):
    return lax.dot_general(left, right, (((0,), (0,)), ((), ())), preferred_element_type=F32)


def one_hot(labels, count):
    rows = lax.broadcasted_iota(jnp.int32, (count, labels.shape[-1]), 0)
    return (rows == labels).astype(F32).astype(BF16)


def row_moments(values):
    centred = values - jnp.mean(values, -1, keepdims=True)
    return centred, lax.rsqrt(jnp.mean(centred * centred, -1, keepdims=True) + EPSILON)


def moments_back(normed, scaled, upstream):
    return scaled * (
        upstream
        - jnp.mean(upstream, -1, keepdims=True)
        - normed * jnp.mean(upstream * normed, -1, keepdims=True)
    )


def fetch(pairs, semaphores):
    copies = [
        pltpu.make_async_copy(source, target, semaphores.at[n])
        for n, (source, target) in enumerate(pairs)
    ]
    for copy in copies:
        copy.start()
    for copy in copies:
        copy.wait()


def pack_kernel(*refs):
    sources, packed_ref, index_ref = refs[:8], refs[8], refs[9]
    local, semaphores = refs[10:18], refs[18]
    fetch(list(zip(sources, local)), semaphores)
    (
        grid_ref,
        mesh_ref,
        g2m_pick_ref,
        g2m_sender_ref,
        g2m_receiver_ref,
        m2m_pick_ref,
        m2m_sender_ref,
        m2m_receiver_ref,
    ) = local
    lists, _, capacity = g2m_pick_ref.shape
    mesh_count = mesh_ref.shape[1]
    regions, mesh_cap = m2m_pick_ref.shape[1:]
    edges = g2m_sender_ref.shape[1]
    grid_rows = grid_ref[0]
    for i in range(lists):
        picked = one_hot(g2m_pick_ref[i], grid_rows.shape[0])
        packed_ref[i * capacity : (i + 1) * capacity, :] = dot_first(picked, grid_rows).astype(BF16)
    first = lists * capacity
    packed_ref[first : first + mesh_count, :] = mesh_ref[0]
    index_ref[...] = jnp.zeros_like(index_ref)
    index_ref[0:1, 0:edges] = g2m_sender_ref[...].astype(F32)
    index_ref[0:1, edges : 2 * edges] = g2m_receiver_ref[...].astype(F32)
    index_ref[1:2, 0:edges] = m2m_sender_ref[...].astype(F32)
    index_ref[1:2, edges : 2 * edges] = m2m_receiver_ref[...].astype(F32)
    slots = regions * mesh_cap
    lane = lax.broadcasted_iota(jnp.int32, (mesh_cap, slots), 1)
    spread = (lane % mesh_cap == lax.broadcasted_iota(jnp.int32, (mesh_cap, slots), 0)).astype(F32)
    spread = dot(m2m_pick_ref[0].astype(F32).astype(BF16), spread.astype(BF16))
    lane = lax.broadcasted_iota(jnp.int32, (regions, slots), 1)
    owned = lane // mesh_cap == lax.broadcasted_iota(jnp.int32, (regions, slots), 0)
    index_ref[2:3, 0:slots] = jnp.sum(jnp.where(owned, spread, 0.0), 0, keepdims=True)
    packed_ref[first + mesh_count :, :] = index_ref[...].astype(BF16)


def weights_kernel(source_ref, weights_ref, turned_ref, semaphores):
    fetch([(source_ref, weights_ref)], semaphores)
    latent = weights_ref.shape[0]
    for n, block in enumerate((0, 2, 3)):
        turned_ref[:, n * latent : (n + 1) * latent] = weights_ref[
            :, block * latent : (block + 1) * latent
        ].T


def edge_blocks(edges):
    size = min(edges, 128)
    return [(first, min(size, edges - first)) for first in range(0, edges, size)]


def edge_forward(tables, hot_ref, turned_hot_ref, slope_ref, message_ref, mesh_count):
    regions = len(tables)
    edges = slope_ref.shape[0] // regions
    count = hot_ref.shape[0] // regions
    work = [(d, first, size) for d in range(regions) for first, size in edge_blocks(edges)]

    def gathered(d, first, size):
        rows = slice(d * edges + first, d * edges + first + size)
        return dot(turned_hot_ref[rows, :], tables[d])

    sums = []
    activation = gathered(*work[0])
    for n, (d, first, size) in enumerate(work):
        coming = gathered(*work[n + 1]) if n + 1 < len(work) else None
        squash = 0.5 + 0.5 * jnp.tanh(0.5 * activation)
        message = activation * squash
        rows = slice(d * edges + first, d * edges + first + size)
        slope_ref[rows, :] = (squash + message * (1.0 - squash)).astype(BF16)
        message_ref[rows, :] = message.astype(BF16)
        activation = coming
        if first + size == edges:
            hot = hot_ref[(d + 1) * count - mesh_count : (d + 1) * count, :]
            sums.append(dot(hot, message_ref[d * edges : (d + 1) * edges, :]))
    return sums


def forward_kernel(
    steps,
    listed,
    mesh_count,
    mesh_cap,
    *refs,
):
    regions = len(steps)
    packed_refs = refs[:regions]
    (
        weights_ref,
        mesh_out_ref,
        grid_ref,
        mesh_ref,
        first_ref,
        sent_ref,
        hot_one_ref,
        hot_two_ref,
        turned_one_ref,
        turned_two_ref,
        hot_sent_ref,
        slope_one_ref,
        slope_two_ref,
        normed_one_ref,
        scaled_one_ref,
        normed_two_ref,
        scaled_two_ref,
        index_ref,
        message_ref,
        sum_ref,
    ) = refs[regions:]
    latent = weights_ref.shape[0]
    edges = slope_one_ref.shape[0] // regions
    capacity = listed // 3
    slots = regions * mesh_cap
    me = lax.axis_index("space")
    for step, packed_ref in zip(steps, packed_refs):
        region = lax.rem(me + (regions - step), regions)
        at = lambda rows: pl.ds(pl.multiple_of(region * rows, rows), rows)
        grid_ref[at(listed), :] = packed_ref[:listed, :]
        mesh_ref[at(mesh_count), :] = packed_ref[listed : listed + mesh_count, :]
        index_ref[at(INDEX_ROWS), :] = packed_ref[listed + mesh_count :, :].astype(F32)

    grid_proj = dot(grid_ref[...], weights_ref[:, :latent])
    mesh_proj = dot(mesh_ref[...], weights_ref[:, latent : 2 * latent])
    for d in range(regions):
        index = index_ref[d * INDEX_ROWS : (d + 1) * INDEX_ROWS, :].astype(jnp.int32)
        for row, senders, hot_ref, turned_ref in (
            (0, listed, hot_one_ref, turned_one_ref),
            (1, slots, hot_two_ref, turned_two_ref),
        ):
            count = senders + mesh_count
            hot = jnp.concatenate(
                [
                    one_hot(index[row : row + 1, :edges], senders),
                    one_hot(index[row : row + 1, edges:], mesh_count),
                ],
                axis=0,
            )
            hot_ref[d * count : (d + 1) * count, :] = hot
            turned_ref[d * edges : (d + 1) * edges, :] = hot.T
        hot_sent_ref[d * mesh_count : (d + 1) * mesh_count, :] = one_hot(
            index[2:3, :slots], mesh_count
        )

    blank = jnp.zeros((capacity, latent), F32)
    tables = []
    for d in range(regions):
        before = (d - 1) * listed + 2 * capacity
        within = d * listed + capacity
        after = (d + 1) * listed
        tables.append(
            jnp.concatenate(
                [
                    grid_proj[before : before + capacity] if d > 0 else blank,
                    grid_proj[within : within + capacity],
                    grid_proj[after : after + capacity] if d < regions - 1 else blank,
                    mesh_proj[d * mesh_count : (d + 1) * mesh_count],
                ],
                axis=0,
            ).astype(BF16)
        )
    sums = edge_forward(
        tables, hot_one_ref, turned_one_ref, slope_one_ref, message_ref, mesh_count
    )
    for d in range(regions):
        sum_ref[d * mesh_count : (d + 1) * mesh_count, :] = sums[d]
    centred, scaled = row_moments(sum_ref[...])
    normed = centred * scaled
    normed_one_ref[...] = normed
    scaled_one_ref[...] = jnp.broadcast_to(scaled, scaled_one_ref.shape)
    first_ref[...] = (mesh_ref[...].astype(F32) + normed).astype(BF16)

    for s in range(regions):
        rows = slice(s * mesh_count, (s + 1) * mesh_count)
        sent_ref[s * slots : (s + 1) * slots, :] = dot_first(
            hot_sent_ref[rows, :], first_ref[rows, :]
        ).astype(BF16)
    sent_proj = dot(sent_ref[...], weights_ref[:, 2 * latent : 3 * latent])
    first_proj = dot(first_ref[...], weights_ref[:, 3 * latent :])
    tables = []
    for d in range(regions):
        pieces = [
            sent_proj[s * slots + d * mesh_cap : s * slots + (d + 1) * mesh_cap]
            for s in range(regions)
        ]
        tables.append(
            jnp.concatenate(
                pieces + [first_proj[d * mesh_count : (d + 1) * mesh_count]], axis=0
            ).astype(BF16)
        )
    sums = edge_forward(
        tables, hot_two_ref, turned_two_ref, slope_two_ref, message_ref, mesh_count
    )
    for d in range(regions):
        sum_ref[d * mesh_count : (d + 1) * mesh_count, :] = sums[d]
    centred, scaled = row_moments(sum_ref[...])
    normed_two_ref[...] = centred * scaled
    scaled_two_ref[...] = jnp.broadcast_to(scaled, scaled_two_ref.shape)
    own = pl.ds(pl.multiple_of(me * mesh_count, mesh_count), mesh_count)
    mesh_out_ref[0] = (first_ref[own, :].astype(F32) + normed_two_ref[own, :]).astype(BF16)


def edge_backward(regions, agg_grad, hot_ref, turned_hot_ref, slope_ref, edge_grad_ref):
    edges = slope_ref.shape[0] // regions
    count = hot_ref.shape[0] // regions
    mesh_count = agg_grad.shape[0] // regions
    blank = jnp.zeros((count - mesh_count, agg_grad.shape[1]), BF16)
    work = [(d, first, size) for d in range(regions) for first, size in edge_blocks(edges)]

    def gathered(d, first, size):
        rows = slice(d * edges + first, d * edges + first + size)
        table = jnp.concatenate([blank, agg_grad[d * mesh_count : (d + 1) * mesh_count]], axis=0)
        return dot(turned_hot_ref[rows, :], table)

    sums = []
    upstream = gathered(*work[0])
    for n, (d, first, size) in enumerate(work):
        coming = gathered(*work[n + 1]) if n + 1 < len(work) else None
        rows = slice(d * edges + first, d * edges + first + size)
        edge_grad_ref[rows, :] = (upstream * slope_ref[rows, :].astype(F32)).astype(BF16)
        upstream = coming
        if first + size == edges:
            hot = hot_ref[d * count : (d + 1) * count, :]
            sums.append(dot(hot, edge_grad_ref[d * edges : (d + 1) * edges, :]))
    return sums


def halve(share_ref, keep_ref, give_ref):
    half = keep_ref.shape[0]
    core = lax.bitwise_and(lax.axis_index("rep"), 1)
    keep_ref[...] = share_ref[pl.ds(pl.multiple_of(core * half, half), half), :]
    give_ref[...] = share_ref[pl.ds(pl.multiple_of((1 - core) * half, half), half), :]


def process_back_kernel(steps, mesh_cap, *refs):
    regions = len(steps)
    cotangent_refs = refs[:regions]
    (
        turned_ref,
        first_ref,
        sent_ref,
        hot_ref,
        turned_hot_ref,
        hot_sent_ref,
        slope_ref,
        normed_ref,
        scaled_ref,
        mesh_grad_ref,
        keep_ref,
        give_ref,
        upstream_ref,
        slot_ref,
        recv_ref,
        share_ref,
        edge_grad_ref,
    ) = refs[regions:]
    latent = first_ref.shape[1]
    mesh_count = first_ref.shape[0] // regions
    slots = regions * mesh_cap
    me = lax.axis_index("space")
    for step, cotangent_ref in zip(steps, cotangent_refs):
        region = lax.rem(me + (regions - step), regions)
        at = pl.ds(pl.multiple_of(region * mesh_count, mesh_count), mesh_count)
        upstream_ref[at, :] = cotangent_ref[0].astype(F32)
    agg_grad = moments_back(normed_ref[...], scaled_ref[:, 0:1], upstream_ref[...]).astype(BF16)
    all_sums = edge_backward(
        regions, agg_grad, hot_ref, turned_hot_ref, slope_ref, edge_grad_ref
    )
    for d, sums in enumerate(all_sums):
        for s in range(regions):
            first = s * slots + d * mesh_cap
            slot_ref[first : first + mesh_cap, :] = sums[s * mesh_cap : (s + 1) * mesh_cap]
        recv_ref[d * mesh_count : (d + 1) * mesh_count, :] = sums[slots:].astype(BF16)
    slot_sum = slot_ref[...].astype(BF16)
    columns = share_ref.shape[0]
    mine = pl.ds(pl.multiple_of(me * columns, columns), columns)
    share_ref[:, :latent] = dot_first(sent_ref[:, mine], slot_sum).astype(BF16)
    share_ref[:, latent:] = dot_first(first_ref[:, mine], recv_ref[...]).astype(BF16)
    halve(share_ref, keep_ref, give_ref)
    returned = dot(slot_sum, turned_ref[:, latent : 2 * latent]).astype(BF16)
    grad = upstream_ref[...] + dot(recv_ref[...], turned_ref[:, 2 * latent :])
    for s in range(regions):
        rows = slice(s * mesh_count, (s + 1) * mesh_count)
        mesh_grad_ref[rows, :] = grad[rows] + dot(
            hot_sent_ref[rows, :], returned[s * slots : (s + 1) * slots]
        )


def encode_back_kernel(
    regions,
    grid_ref,
    mesh_ref,
    hot_ref,
    turned_hot_ref,
    slope_ref,
    normed_ref,
    scaled_ref,
    mesh_grad_ref,
    own_slot_ref,
    keep_ref,
    give_ref,
    slot_ref,
    recv_ref,
    share_ref,
    edge_grad_ref,
):
    latent = mesh_ref.shape[1]
    mesh_count = mesh_ref.shape[0] // regions
    listed = grid_ref.shape[0] // regions
    capacity = listed // 3
    me = lax.axis_index("space")
    agg_grad = moments_back(normed_ref[...], scaled_ref[:, 0:1], mesh_grad_ref[...]).astype(BF16)
    blank = jnp.zeros((capacity, latent), BF16)
    slot_ref[0:capacity, :] = blank
    slot_ref[regions * listed - capacity :, :] = blank
    all_sums = edge_backward(
        regions, agg_grad, hot_ref, turned_hot_ref, slope_ref, edge_grad_ref
    )
    for d, sums in enumerate(all_sums):
        sums = sums.astype(BF16)
        for j in range(3):
            source = d + j - 1
            if 0 <= source < regions:
                first = source * listed + (2 - j) * capacity
                slot_ref[first : first + capacity, :] = sums[j * capacity : (j + 1) * capacity]
        recv_ref[d * mesh_count : (d + 1) * mesh_count, :] = sums[listed:]
    columns = share_ref.shape[0]
    mine = pl.ds(pl.multiple_of(me * columns, columns), columns)
    share_ref[:, :latent] = dot_first(grid_ref[:, mine], slot_ref[...]).astype(BF16)
    share_ref[:, latent:] = dot_first(mesh_ref[:, mine], recv_ref[...]).astype(BF16)
    halve(share_ref, keep_ref, give_ref)
    own = pl.ds(pl.multiple_of(me * listed, listed), listed)
    own_slot_ref[...] = slot_ref[own, :]


def grid_back_kernel(turned_ref, pick_ref, own_slot_ref, grid_grad_ref):
    lists, _, capacity = pick_ref.shape
    latent = own_slot_ref.shape[1]
    returned = dot(own_slot_ref[...], turned_ref[:, :latent]).astype(BF16)
    total = None
    for i in range(lists):
        owner = one_hot(pick_ref[i], grid_grad_ref.shape[1])
        part = dot(owner, returned[i * capacity : (i + 1) * capacity])
        total = part if total is None else total + part
    grid_grad_ref[0] = total.astype(BF16)


def finish_kernel(one_ref, other_one_ref, two_ref, other_two_ref, weight_grad_ref):
    half, width = one_ref.shape
    core = lax.bitwise_and(lax.axis_index("rep"), 1)
    mine = pl.ds(pl.multiple_of(core * half, half), half)
    other = pl.ds(pl.multiple_of((1 - core) * half, half), half)
    weight_grad_ref[mine, :width] = one_ref[...].astype(F32)
    weight_grad_ref[other, :width] = other_one_ref[...].astype(F32)
    weight_grad_ref[mine, width:] = two_ref[...].astype(F32)
    weight_grad_ref[other, width:] = other_two_ref[...].astype(F32)


VMEM = pl.BlockSpec(memory_space=pltpu.VMEM)


def call(kernel, operands, outputs, scratch, flops, fetched=0, megabytes=40):
    hbm = pl.BlockSpec(memory_space=pltpu.HBM)
    return pl.pallas_call(
        kernel,
        out_shape=[jax.ShapeDtypeStruct(shape, kind) for shape, kind in outputs],
        in_specs=[hbm] * fetched + [VMEM] * (len(operands) - fetched),
        out_specs=[VMEM] * len(outputs),
        scratch_shapes=[pltpu.VMEM(shape, kind) for shape, kind in scratch]
        + ([pltpu.SemaphoreType.DMA((fetched,))] if fetched else []),
        compiler_params=pltpu.CompilerParams(vmem_limit_bytes=megabytes << 20),
        cost_estimate=pl.CostEstimate(flops=flops, bytes_accessed=4 << 20, transcendentals=0),
    )(*operands)


def swap(block, axis, bits):
    return lax.ppermute(block, axis, [(i, i ^ bits) for i in range(lax.axis_size(axis))])


def shifted(block, step):
    count = lax.axis_size("space")
    return lax.ppermute(block, "space", [(i, (i + step) % count) for i in range(count)])


def added(left, right):
    return (left.astype(F32) + right.astype(F32)).astype(BF16)


def summed_half(keep, give):
    half = added(keep, swap(give, "rep", 1))
    bit = 2
    while bit < lax.axis_size("rep"):
        half = added(half, swap(half, "rep", bit))
        bit *= 2
    return half, swap(half, "rep", 1)


def whole_sample_body(
    grid_latent,
    mesh_latent,
    mesh_cotangent,
    weights,
    g2m_pick,
    g2m_sender,
    g2m_receiver,
    m2m_pick,
    m2m_sender,
    m2m_receiver,
):
    regions = lax.axis_size("space")
    latent = weights.shape[0]
    listed = g2m_pick.shape[1] * g2m_pick.shape[2]
    mesh_count = mesh_latent.shape[1]
    mesh_cap = m2m_pick.shape[2]
    edges = g2m_sender.shape[0]
    columns = latent // regions
    half = columns // 2
    g2m_pick = g2m_pick.transpose(1, 0, 2)
    sources = (
        grid_latent,
        mesh_latent,
        g2m_pick,
        g2m_sender.reshape(1, -1),
        g2m_receiver.reshape(1, -1),
        m2m_pick,
        m2m_sender.reshape(1, -1),
        m2m_receiver.reshape(1, -1),
    )
    packed = call(
        pack_kernel,
        sources,
        [((listed + mesh_count + INDEX_ROWS, latent), BF16)],
        [((INDEX_ROWS, latent), F32)] + [(source.shape, source.dtype) for source in sources],
        10**7,
        fetched=len(sources),
        megabytes=56,
    )[0]
    packed, cotangent, weights = lax.optimization_barrier((packed, mesh_cotangent, weights))
    steps = (0, *sorted(range(1, regions), key=lambda step: -min(step, regions - step)))
    packs = [packed] + [shifted(packed, step) for step in steps[1:]]
    weights, turned = call(
        weights_kernel,
        (weights,),
        [(weights.shape, BF16), ((latent, 3 * latent), BF16)],
        [],
        10**8,
        fetched=1,
    )
    packs[1], cotangent = lax.optimization_barrier((packs[1], cotangent))
    cotangents = [cotangent] + [shifted(cotangent, step) for step in steps[1:]]
    rows = regions * mesh_count
    slots = regions * mesh_cap
    (
        mesh_out,
        grid_all,
        mesh_all,
        mesh_first,
        mesh_sent,
        hot_one,
        hot_two,
        turned_one,
        turned_two,
        hot_sent,
        slope_one,
        slope_two,
        normed_one,
        scaled_one,
        normed_two,
        scaled_two,
    ) = call(
        functools.partial(forward_kernel, steps, listed, mesh_count, mesh_cap),
        (*packs, weights),
        [
            (mesh_latent.shape, BF16),
            ((regions * listed, latent), BF16),
            ((rows, latent), BF16),
            ((rows, latent), BF16),
            ((regions * slots, latent), BF16),
            ((regions * (listed + mesh_count), edges), BF16),
            ((regions * (slots + mesh_count), edges), BF16),
            ((regions * edges, listed + mesh_count), BF16),
            ((regions * edges, slots + mesh_count), BF16),
            ((rows, slots), BF16),
            ((regions * edges, latent), BF16),
            ((regions * edges, latent), BF16),
            ((rows, latent), F32),
            ((rows, 128), F32),
            ((rows, latent), F32),
            ((rows, 128), F32),
        ],
        [
            ((regions * INDEX_ROWS, latent), F32),
            ((regions * edges, latent), BF16),
            ((rows, latent), F32),
        ],
        2 * 10**9,
    )
    mesh_grad, keep_two, give_two = call(
        functools.partial(process_back_kernel, steps, mesh_cap),
        (
            *cotangents,
            turned,
            mesh_first,
            mesh_sent,
            hot_two,
            turned_two,
            hot_sent,
            slope_two,
            normed_two,
            scaled_two,
        ),
        [((rows, latent), F32)] + [((half, 2 * latent), BF16)] * 2,
        [
            ((rows, latent), F32),
            ((regions * slots, latent), F32),
            ((rows, latent), BF16),
            ((columns, 2 * latent), BF16),
            ((regions * edges, latent), BF16),
        ],
        10**9,
    )
    own_slots, keep_one, give_one = call(
        functools.partial(encode_back_kernel, regions),
        (
            grid_all,
            mesh_all,
            hot_one,
            turned_one,
            slope_one,
            normed_one,
            scaled_one,
            mesh_grad,
        ),
        [((listed, latent), BF16)] + [((half, 2 * latent), BF16)] * 2,
        [
            ((regions * listed, latent), BF16),
            ((rows, latent), BF16),
            ((columns, 2 * latent), BF16),
            ((regions * edges, latent), BF16),
        ],
        10**9,
    )
    grid_grad = call(
        grid_back_kernel,
        (turned, g2m_pick, own_slots),
        [(grid_latent.shape, BF16)],
        [],
        10**8,
    )[0]
    weight_grad = call(
        finish_kernel,
        (*summed_half(keep_one, give_one), *summed_half(keep_two, give_two)),
        [((columns, 4 * latent), F32)],
        [],
        10**6,
    )[0]
    return (mesh_out, grid_grad, weight_grad)


def solution(mesh):
    regions = mesh.shape["space"]
    samples = mesh.shape["rep"]

    def whole(*arguments):
        edges = arguments[5].shape[0] + arguments[8].shape[0]
        latent = arguments[3].shape[0]
        fits = edges * latent * 4 <= SAMPLE_EDGE_BYTES and latent % (128 * regions) == 0
        paired = regions > 1 and samples > 1 and samples & (samples - 1) == 0
        return sharded(whole_sample_body if fits and paired else partitioned_body)(*arguments)

    def sharded(body):
        return jax.shard_map(
            body,
            mesh=mesh,
            in_specs=(
                P(("groups", "rep"), "space", None),
                P(("groups", "rep"), "space", None),
                P(("groups", "rep"), "space", None),
                P(),
                P("space", None, None),
                P("space"),
                P("space"),
                P("space", None, None),
                P("space"),
                P("space"),
            ),
            out_specs=(
                P(("groups", "rep"), "space", None),
                P(("groups", "rep"), "space", None),
                P(("groups", "space"), None),
            ),
            check_vma=False,
        )

    return whole
```

```python
import functools

import jax
import jax.numpy as jnp
from jax import lax
from jax.experimental import pallas as pl
from jax.experimental.pallas import tpu as pltpu
from jax.sharding import PartitionSpec as P

EPSILON = 1e-05


def with_halo(cells, sides, width):
    for axis, dim in sides:
        count = lax.axis_size(axis)
        ends = count - 1
        head = lax.slice_in_dim(cells, 0, width, axis=dim)
        tail = lax.slice_in_dim(cells, cells.shape[dim] - width, cells.shape[dim], axis=dim)
        cells = jnp.concatenate(
            [
                lax.ppermute(tail, axis, [(i, (i + 1) % count) for i in range(ends)]),
                cells,
                lax.ppermute(head, axis, [((i + 1) % count, i) for i in range(ends)]),
            ],
            axis=dim,
        )
    return cells


def swish(values):
    return values * jax.nn.sigmoid(values)


def swish_slope(values):
    squash = jax.nn.sigmoid(values)
    return squash * (1.0 + values * (1.0 - squash))


def norm_rows(values):
    centred = values - jnp.mean(values, -1, keepdims=True)
    return centred * lax.rsqrt(jnp.mean(centred * centred, -1, keepdims=True) + EPSILON)


def norm_rows_back(values, upstream):
    centred = values - jnp.mean(values, -1, keepdims=True)
    scaled = lax.rsqrt(jnp.mean(centred * centred, -1, keepdims=True) + EPSILON)
    normed = centred * scaled
    return scaled * (
        upstream
        - jnp.mean(upstream, -1, keepdims=True)
        - normed * jnp.mean(upstream * normed, -1, keepdims=True)
    )


def slot_rows(pick_row):
    listed = pick_row.reshape(-1)
    return listed


def mesh_route(outgoing, capacity, peer_count):
    columns = outgoing.shape[1]
    pieces = lax.all_to_all(
        outgoing.reshape(peer_count, capacity, columns),
        "space",
        split_axis=0,
        concat_axis=0,
        tiled=True,
    )
    arrived = pieces.reshape(peer_count * capacity, columns)
    return arrived


def grid_route(outgoing, capacity):
    columns = outgoing.shape[1]
    lists = outgoing.reshape(3, capacity, columns)
    rims = with_halo(jnp.stack([lists[0], lists[2]]), (("space", 0),), 1)
    return jnp.concatenate([rims[0], lists[1], rims[3]], axis=0)


def edge_pass(arrived, recv_table, located, receiver, w_send, w_recv):
    recv_proj = jnp.dot(recv_table, w_recv, preferred_element_type=jnp.float32)
    slot_proj = jnp.dot(arrived, w_send, preferred_element_type=jnp.float32)
    activation = slot_proj[located] + recv_proj[receiver]
    message = swish(activation).astype(jnp.bfloat16)
    member = (
        receiver[None, :] == jnp.arange(recv_table.shape[0], dtype=jnp.int32)[:, None]
    ).astype(jnp.bfloat16)
    summed = jnp.dot(member, message, preferred_element_type=jnp.float32)
    return (activation, member, summed)


def backward_pass(slot_count, located, activation, member, receiver, agg_grad, w_send):
    edge_grad = (agg_grad[receiver] * swish_slope(activation)).astype(jnp.bfloat16)
    recv_sum = jnp.dot(member, edge_grad, preferred_element_type=jnp.float32).astype(jnp.bfloat16)
    slot_member = (located[None, :] == jnp.arange(slot_count, dtype=jnp.int32)[:, None]).astype(
        jnp.bfloat16
    )
    slot_sum = jnp.dot(slot_member, edge_grad, preferred_element_type=jnp.float32).astype(
        jnp.bfloat16
    )
    returned = jnp.dot(slot_sum, w_send.T, preferred_element_type=jnp.float32).astype(jnp.bfloat16)
    return (recv_sum, slot_sum, returned)


def gather_back(listed, back_rows, row_count):
    owner = (listed[None, :] == jnp.arange(row_count, dtype=jnp.int32)[:, None]).astype(
        jnp.bfloat16
    )
    return jnp.dot(owner, back_rows, preferred_element_type=jnp.float32)


def partitioned_body(
    grid_latent,
    mesh_latent,
    mesh_cotangent,
    weights,
    g2m_pick,
    g2m_sender,
    g2m_receiver,
    m2m_pick,
    m2m_sender,
    m2m_receiver,
):
    grid_rows = grid_latent[0]
    mesh_rows = mesh_latent[0]
    upstream = mesh_cotangent[0].astype(jnp.float32)
    latent = weights.shape[0]
    encode_sender = weights[:, :latent]
    encode_receiver = weights[:, latent : 2 * latent]
    process_sender = weights[:, 2 * latent : 3 * latent]
    process_receiver = weights[:, 3 * latent :]
    peer_count = lax.axis_size("space")
    grid_cap = g2m_pick.shape[2]
    mesh_cap = m2m_pick.shape[2]
    grid_listed = g2m_pick[0].reshape(-1)
    grid_arrived = grid_route(grid_rows[grid_listed], grid_cap)
    act_first, member_first, summed_first = edge_pass(
        grid_arrived, mesh_rows, g2m_sender, g2m_receiver, encode_sender, encode_receiver
    )
    mesh_first = (mesh_rows.astype(jnp.float32) + norm_rows(summed_first)).astype(jnp.bfloat16)
    mesh_listed = slot_rows(m2m_pick[0])
    mesh_arrived = mesh_route(mesh_first[mesh_listed], mesh_cap, peer_count)
    act_second, member_second, summed_second = edge_pass(
        mesh_arrived, mesh_first, m2m_sender, m2m_receiver, process_sender, process_receiver
    )
    mesh_final = (mesh_first.astype(jnp.float32) + norm_rows(summed_second)).astype(jnp.bfloat16)
    agg_second = norm_rows_back(summed_second, upstream)
    recv_second, slot_second, returned_second = backward_pass(
        mesh_arrived.shape[0],
        m2m_sender,
        act_second,
        member_second,
        m2m_receiver,
        agg_second,
        process_sender,
    )
    back_second = mesh_route(returned_second, mesh_cap, peer_count)
    mesh_grad = upstream + jnp.dot(
        recv_second, process_receiver.T, preferred_element_type=jnp.float32
    )
    mesh_grad = mesh_grad + gather_back(mesh_listed, back_second, mesh_rows.shape[0])
    agg_first = norm_rows_back(summed_first, mesh_grad)
    recv_first, slot_first, returned_first = backward_pass(
        grid_arrived.shape[0],
        g2m_sender,
        act_first,
        member_first,
        g2m_receiver,
        agg_first,
        encode_sender,
    )
    back_first = grid_route(returned_first, grid_cap)
    grid_grad = gather_back(grid_listed, back_first, grid_rows.shape[0]).astype(jnp.bfloat16)
    factor_pairs = (
        (grid_arrived, slot_first),
        (mesh_rows, recv_first),
        (mesh_arrived, slot_second),
        (mesh_first, recv_second),
    )
    blocks = []
    for first_factor, second_factor in factor_pairs:
        blocks.append(
            lax.dot_general(
                first_factor,
                second_factor,
                (((0,), (0,)), ((), ())),
                preferred_element_type=jnp.float32,
            )
        )
    shares = lax.psum_scatter(
        jnp.concatenate(blocks, axis=1).astype(jnp.bfloat16),
        "space",
        scatter_dimension=0,
        tiled=True,
    )
    weight_grad = lax.psum(shares, "rep").astype(jnp.float32)
    return (mesh_final[None], grid_grad[None], weight_grad)


F32 = jnp.float32
BF16 = jnp.bfloat16
INDEX_ROWS = 8
SAMPLE_EDGE_BYTES = 8 << 20


def dot(left, right):
    return jnp.dot(left, right, preferred_element_type=F32)


def dot_first(left, right):
    return lax.dot_general(left, right, (((0,), (0,)), ((), ())), preferred_element_type=F32)


def one_hot(labels, count):
    rows = lax.broadcasted_iota(jnp.int32, (count, labels.shape[-1]), 0)
    return (rows == labels).astype(F32).astype(BF16)


def row_moments(values):
    centred = values - jnp.mean(values, -1, keepdims=True)
    return centred, lax.rsqrt(jnp.mean(centred * centred, -1, keepdims=True) + EPSILON)


def moments_back(normed, scaled, upstream):
    return scaled * (
        upstream
        - jnp.mean(upstream, -1, keepdims=True)
        - normed * jnp.mean(upstream * normed, -1, keepdims=True)
    )


def fetch(pairs, semaphores):
    copies = [
        pltpu.make_async_copy(source, target, semaphores.at[n])
        for n, (source, target) in enumerate(pairs)
    ]
    for copy in copies:
        copy.start()
    for copy in copies:
        copy.wait()


def pack_kernel(*refs):
    sources, packed_ref, index_ref = refs[:8], refs[8], refs[9]
    local, semaphores = refs[10:18], refs[18]
    fetch(list(zip(sources, local)), semaphores)
    (
        grid_ref,
        mesh_ref,
        g2m_pick_ref,
        g2m_sender_ref,
        g2m_receiver_ref,
        m2m_pick_ref,
        m2m_sender_ref,
        m2m_receiver_ref,
    ) = local
    lists, _, capacity = g2m_pick_ref.shape
    mesh_count = mesh_ref.shape[1]
    regions, mesh_cap = m2m_pick_ref.shape[1:]
    edges = g2m_sender_ref.shape[1]
    grid_rows = grid_ref[0]
    for i in range(lists):
        picked = one_hot(g2m_pick_ref[i], grid_rows.shape[0])
        packed_ref[i * capacity : (i + 1) * capacity, :] = dot_first(picked, grid_rows).astype(BF16)
    first = lists * capacity
    packed_ref[first : first + mesh_count, :] = mesh_ref[0]
    index_ref[...] = jnp.zeros_like(index_ref)
    index_ref[0:1, 0:edges] = g2m_sender_ref[...].astype(F32)
    index_ref[0:1, edges : 2 * edges] = g2m_receiver_ref[...].astype(F32)
    index_ref[1:2, 0:edges] = m2m_sender_ref[...].astype(F32)
    index_ref[1:2, edges : 2 * edges] = m2m_receiver_ref[...].astype(F32)
    slots = regions * mesh_cap
    lane = lax.broadcasted_iota(jnp.int32, (mesh_cap, slots), 1)
    spread = (lane % mesh_cap == lax.broadcasted_iota(jnp.int32, (mesh_cap, slots), 0)).astype(F32)
    spread = dot(m2m_pick_ref[0].astype(F32).astype(BF16), spread.astype(BF16))
    lane = lax.broadcasted_iota(jnp.int32, (regions, slots), 1)
    owned = lane // mesh_cap == lax.broadcasted_iota(jnp.int32, (regions, slots), 0)
    index_ref[2:3, 0:slots] = jnp.sum(jnp.where(owned, spread, 0.0), 0, keepdims=True)
    packed_ref[first + mesh_count :, :] = index_ref[...].astype(BF16)


def weights_kernel(source_ref, weights_ref, turned_ref, semaphores):
    fetch([(source_ref, weights_ref)], semaphores)
    latent = weights_ref.shape[0]
    for n, block in enumerate((0, 2, 3)):
        turned_ref[:, n * latent : (n + 1) * latent] = weights_ref[
            :, block * latent : (block + 1) * latent
        ].T


def edge_blocks(edges):
    size = min(edges, 128)
    return [(first, min(size, edges - first)) for first in range(0, edges, size)]


def edge_forward(tables, hot_ref, turned_hot_ref, slope_ref, message_ref, mesh_count):
    regions = len(tables)
    edges = slope_ref.shape[0] // regions
    count = hot_ref.shape[0] // regions
    work = [(d, first, size) for d in range(regions) for first, size in edge_blocks(edges)]

    def gathered(d, first, size):
        rows = slice(d * edges + first, d * edges + first + size)
        return dot(turned_hot_ref[rows, :], tables[d])

    sums = []
    activation = gathered(*work[0])
    for n, (d, first, size) in enumerate(work):
        coming = gathered(*work[n + 1]) if n + 1 < len(work) else None
        squash = 0.5 + 0.5 * jnp.tanh(0.5 * activation)
        message = activation * squash
        rows = slice(d * edges + first, d * edges + first + size)
        slope_ref[rows, :] = (squash + message * (1.0 - squash)).astype(BF16)
        message_ref[rows, :] = message.astype(BF16)
        activation = coming
        if first + size == edges:
            hot = hot_ref[(d + 1) * count - mesh_count : (d + 1) * count, :]
            sums.append(dot(hot, message_ref[d * edges : (d + 1) * edges, :]))
    return sums


def forward_kernel(
    steps,
    listed,
    mesh_count,
    mesh_cap,
    *refs,
):
    regions = len(steps)
    packed_refs = refs[:regions]
    (
        weights_ref,
        mesh_out_ref,
        grid_ref,
        mesh_ref,
        first_ref,
        sent_ref,
        hot_one_ref,
        hot_two_ref,
        turned_one_ref,
        turned_two_ref,
        hot_sent_ref,
        slope_one_ref,
        slope_two_ref,
        normed_one_ref,
        scaled_one_ref,
        normed_two_ref,
        scaled_two_ref,
        index_ref,
        message_ref,
        sum_ref,
    ) = refs[regions:]
    latent = weights_ref.shape[0]
    edges = slope_one_ref.shape[0] // regions
    capacity = listed // 3
    slots = regions * mesh_cap
    me = lax.axis_index("space")
    for step, packed_ref in zip(steps, packed_refs):
        region = lax.bitwise_xor(me, step)
        at = lambda rows: pl.ds(pl.multiple_of(region * rows, rows), rows)
        grid_ref[at(listed), :] = packed_ref[:listed, :]
        mesh_ref[at(mesh_count), :] = packed_ref[listed : listed + mesh_count, :]
        index_ref[at(INDEX_ROWS), :] = packed_ref[listed + mesh_count :, :].astype(F32)

    grid_proj = dot(grid_ref[...], weights_ref[:, :latent])
    mesh_proj = dot(mesh_ref[...], weights_ref[:, latent : 2 * latent])
    for d in range(regions):
        index = index_ref[d * INDEX_ROWS : (d + 1) * INDEX_ROWS, :].astype(jnp.int32)
        for row, senders, hot_ref, turned_ref in (
            (0, listed, hot_one_ref, turned_one_ref),
            (1, slots, hot_two_ref, turned_two_ref),
        ):
            count = senders + mesh_count
            hot = jnp.concatenate(
                [
                    one_hot(index[row : row + 1, :edges], senders),
                    one_hot(index[row : row + 1, edges:], mesh_count),
                ],
                axis=0,
            )
            hot_ref[d * count : (d + 1) * count, :] = hot
            turned_ref[d * edges : (d + 1) * edges, :] = hot.T
        hot_sent_ref[d * mesh_count : (d + 1) * mesh_count, :] = one_hot(
            index[2:3, :slots], mesh_count
        )

    blank = jnp.zeros((capacity, latent), F32)
    tables = []
    for d in range(regions):
        before = (d - 1) * listed + 2 * capacity
        within = d * listed + capacity
        after = (d + 1) * listed
        tables.append(
            jnp.concatenate(
                [
                    grid_proj[before : before + capacity] if d > 0 else blank,
                    grid_proj[within : within + capacity],
                    grid_proj[after : after + capacity] if d < regions - 1 else blank,
                    mesh_proj[d * mesh_count : (d + 1) * mesh_count],
                ],
                axis=0,
            ).astype(BF16)
        )
    sums = edge_forward(
        tables, hot_one_ref, turned_one_ref, slope_one_ref, message_ref, mesh_count
    )
    for d in range(regions):
        sum_ref[d * mesh_count : (d + 1) * mesh_count, :] = sums[d]
    centred, scaled = row_moments(sum_ref[...])
    normed = centred * scaled
    normed_one_ref[...] = normed
    scaled_one_ref[...] = jnp.broadcast_to(scaled, scaled_one_ref.shape)
    first_ref[...] = (mesh_ref[...].astype(F32) + normed).astype(BF16)

    for s in range(regions):
        rows = slice(s * mesh_count, (s + 1) * mesh_count)
        sent_ref[s * slots : (s + 1) * slots, :] = dot_first(
            hot_sent_ref[rows, :], first_ref[rows, :]
        ).astype(BF16)
    sent_proj = dot(sent_ref[...], weights_ref[:, 2 * latent : 3 * latent])
    first_proj = dot(first_ref[...], weights_ref[:, 3 * latent :])
    tables = []
    for d in range(regions):
        pieces = [
            sent_proj[s * slots + d * mesh_cap : s * slots + (d + 1) * mesh_cap]
            for s in range(regions)
        ]
        tables.append(
            jnp.concatenate(
                pieces + [first_proj[d * mesh_count : (d + 1) * mesh_count]], axis=0
            ).astype(BF16)
        )
    sums = edge_forward(
        tables, hot_two_ref, turned_two_ref, slope_two_ref, message_ref, mesh_count
    )
    for d in range(regions):
        sum_ref[d * mesh_count : (d + 1) * mesh_count, :] = sums[d]
    centred, scaled = row_moments(sum_ref[...])
    normed_two_ref[...] = centred * scaled
    scaled_two_ref[...] = jnp.broadcast_to(scaled, scaled_two_ref.shape)
    own = pl.ds(pl.multiple_of(me * mesh_count, mesh_count), mesh_count)
    mesh_out_ref[0] = (first_ref[own, :].astype(F32) + normed_two_ref[own, :]).astype(BF16)


def edge_backward(regions, agg_grad, hot_ref, turned_hot_ref, slope_ref, edge_grad_ref):
    edges = slope_ref.shape[0] // regions
    count = hot_ref.shape[0] // regions
    mesh_count = agg_grad.shape[0] // regions
    blank = jnp.zeros((count - mesh_count, agg_grad.shape[1]), BF16)
    work = [(d, first, size) for d in range(regions) for first, size in edge_blocks(edges)]

    def gathered(d, first, size):
        rows = slice(d * edges + first, d * edges + first + size)
        table = jnp.concatenate([blank, agg_grad[d * mesh_count : (d + 1) * mesh_count]], axis=0)
        return dot(turned_hot_ref[rows, :], table)

    sums = []
    upstream = gathered(*work[0])
    for n, (d, first, size) in enumerate(work):
        coming = gathered(*work[n + 1]) if n + 1 < len(work) else None
        rows = slice(d * edges + first, d * edges + first + size)
        edge_grad_ref[rows, :] = (upstream * slope_ref[rows, :].astype(F32)).astype(BF16)
        upstream = coming
        if first + size == edges:
            hot = hot_ref[d * count : (d + 1) * count, :]
            sums.append(dot(hot, edge_grad_ref[d * edges : (d + 1) * edges, :]))
    return sums


def halve(share_ref, keep_ref, give_ref):
    half = keep_ref.shape[0]
    core = lax.bitwise_and(lax.axis_index("rep"), 1)
    keep_ref[...] = share_ref[pl.ds(pl.multiple_of(core * half, half), half), :]
    give_ref[...] = share_ref[pl.ds(pl.multiple_of((1 - core) * half, half), half), :]


def process_back_kernel(steps, mesh_cap, *refs):
    regions = len(steps)
    cotangent_refs = refs[:regions]
    (
        turned_ref,
        first_ref,
        sent_ref,
        hot_ref,
        turned_hot_ref,
        hot_sent_ref,
        slope_ref,
        normed_ref,
        scaled_ref,
        mesh_grad_ref,
        keep_ref,
        give_ref,
        upstream_ref,
        slot_ref,
        recv_ref,
        share_ref,
        edge_grad_ref,
    ) = refs[regions:]
    latent = first_ref.shape[1]
    mesh_count = first_ref.shape[0] // regions
    slots = regions * mesh_cap
    me = lax.axis_index("space")
    for step, cotangent_ref in zip(steps, cotangent_refs):
        region = lax.bitwise_xor(me, step)
        at = pl.ds(pl.multiple_of(region * mesh_count, mesh_count), mesh_count)
        upstream_ref[at, :] = cotangent_ref[0].astype(F32)
    agg_grad = moments_back(normed_ref[...], scaled_ref[:, 0:1], upstream_ref[...]).astype(BF16)
    all_sums = edge_backward(
        regions, agg_grad, hot_ref, turned_hot_ref, slope_ref, edge_grad_ref
    )
    for d, sums in enumerate(all_sums):
        for s in range(regions):
            first = s * slots + d * mesh_cap
            slot_ref[first : first + mesh_cap, :] = sums[s * mesh_cap : (s + 1) * mesh_cap]
        recv_ref[d * mesh_count : (d + 1) * mesh_count, :] = sums[slots:].astype(BF16)
    slot_sum = slot_ref[...].astype(BF16)
    columns = share_ref.shape[0]
    mine = pl.ds(pl.multiple_of(me * columns, columns), columns)
    share_ref[:, :latent] = dot_first(sent_ref[:, mine], slot_sum).astype(BF16)
    share_ref[:, latent:] = dot_first(first_ref[:, mine], recv_ref[...]).astype(BF16)
    halve(share_ref, keep_ref, give_ref)
    returned = dot(slot_sum, turned_ref[:, latent : 2 * latent]).astype(BF16)
    grad = upstream_ref[...] + dot(recv_ref[...], turned_ref[:, 2 * latent :])
    for s in range(regions):
        rows = slice(s * mesh_count, (s + 1) * mesh_count)
        mesh_grad_ref[rows, :] = grad[rows] + dot(
            hot_sent_ref[rows, :], returned[s * slots : (s + 1) * slots]
        )


def encode_back_kernel(
    regions,
    grid_ref,
    mesh_ref,
    hot_ref,
    turned_hot_ref,
    slope_ref,
    normed_ref,
    scaled_ref,
    mesh_grad_ref,
    own_slot_ref,
    keep_ref,
    give_ref,
    slot_ref,
    recv_ref,
    share_ref,
    edge_grad_ref,
):
    latent = mesh_ref.shape[1]
    mesh_count = mesh_ref.shape[0] // regions
    listed = grid_ref.shape[0] // regions
    capacity = listed // 3
    me = lax.axis_index("space")
    agg_grad = moments_back(normed_ref[...], scaled_ref[:, 0:1], mesh_grad_ref[...]).astype(BF16)
    blank = jnp.zeros((capacity, latent), BF16)
    slot_ref[0:capacity, :] = blank
    slot_ref[regions * listed - capacity :, :] = blank
    all_sums = edge_backward(
        regions, agg_grad, hot_ref, turned_hot_ref, slope_ref, edge_grad_ref
    )
    for d, sums in enumerate(all_sums):
        sums = sums.astype(BF16)
        for j in range(3):
            source = d + j - 1
            if 0 <= source < regions:
                first = source * listed + (2 - j) * capacity
                slot_ref[first : first + capacity, :] = sums[j * capacity : (j + 1) * capacity]
        recv_ref[d * mesh_count : (d + 1) * mesh_count, :] = sums[listed:]
    columns = share_ref.shape[0]
    mine = pl.ds(pl.multiple_of(me * columns, columns), columns)
    share_ref[:, :latent] = dot_first(grid_ref[:, mine], slot_ref[...]).astype(BF16)
    share_ref[:, latent:] = dot_first(mesh_ref[:, mine], recv_ref[...]).astype(BF16)
    halve(share_ref, keep_ref, give_ref)
    own = pl.ds(pl.multiple_of(me * listed, listed), listed)
    own_slot_ref[...] = slot_ref[own, :]


def grid_back_kernel(turned_ref, pick_ref, own_slot_ref, grid_grad_ref):
    lists, _, capacity = pick_ref.shape
    latent = own_slot_ref.shape[1]
    returned = dot(own_slot_ref[...], turned_ref[:, :latent]).astype(BF16)
    total = None
    for i in range(lists):
        owner = one_hot(pick_ref[i], grid_grad_ref.shape[1])
        part = dot(owner, returned[i * capacity : (i + 1) * capacity])
        total = part if total is None else total + part
    grid_grad_ref[0] = total.astype(BF16)


def place(pairs, stages, semaphores):
    copies = []
    for n, (block_ref, target) in enumerate(pairs):
        stages[n][...] = block_ref[...].astype(F32)
        copies.append(pltpu.make_async_copy(stages[n], target, semaphores.at[n]))
        copies[n].start()
    for copy in copies:
        copy.wait()


def half_rows(half):
    core = lax.bitwise_and(lax.axis_index("rep"), 1)
    mine = pl.ds(pl.multiple_of(core * half, half), half)
    return mine, pl.ds(pl.multiple_of((1 - core) * half, half), half)


def finish_kernel(
    one_ref, other_one_ref, two_ref, other_two_ref, weight_grad_ref, *scratch
):
    half, width = one_ref.shape
    mine, other = half_rows(half)
    place(
        [
            (two_ref, weight_grad_ref.at[mine, width:]),
            (other_two_ref, weight_grad_ref.at[other, width:]),
            (one_ref, weight_grad_ref.at[mine, :width]),
            (other_one_ref, weight_grad_ref.at[other, :width]),
        ],
        scratch[:4],
        scratch[4],
    )


VMEM = pl.BlockSpec(memory_space=pltpu.VMEM)


def call(kernel, operands, outputs, scratch, flops, fetched=0, megabytes=40):
    hbm = pl.BlockSpec(memory_space=pltpu.HBM)
    return pl.pallas_call(
        kernel,
        out_shape=[jax.ShapeDtypeStruct(shape, kind) for shape, kind in outputs],
        in_specs=[hbm] * fetched + [VMEM] * (len(operands) - fetched),
        out_specs=[VMEM] * len(outputs),
        scratch_shapes=[pltpu.VMEM(shape, kind) for shape, kind in scratch]
        + ([pltpu.SemaphoreType.DMA((fetched,))] if fetched else []),
        compiler_params=pltpu.CompilerParams(vmem_limit_bytes=megabytes << 20),
        cost_estimate=pl.CostEstimate(flops=flops, bytes_accessed=4 << 20, transcendentals=0),
    )(*operands)


def swap(block, axis, bits):
    return lax.ppermute(block, axis, [(i, i ^ bits) for i in range(lax.axis_size(axis))])


def added(left, right):
    return (left.astype(F32) + right.astype(F32)).astype(BF16)


def summed_over_chips(half):
    bit = 2
    while bit < lax.axis_size("rep"):
        half = added(half, swap(half, "rep", bit))
        bit *= 2
    return half


def whole_sample_body(
    grid_latent,
    mesh_latent,
    mesh_cotangent,
    weights,
    g2m_pick,
    g2m_sender,
    g2m_receiver,
    m2m_pick,
    m2m_sender,
    m2m_receiver,
):
    regions = lax.axis_size("space")
    latent = weights.shape[0]
    listed = g2m_pick.shape[1] * g2m_pick.shape[2]
    mesh_count = mesh_latent.shape[1]
    mesh_cap = m2m_pick.shape[2]
    edges = g2m_sender.shape[0]
    columns = latent // regions
    half = columns // 2
    g2m_pick = g2m_pick.transpose(1, 0, 2)
    sources = (
        grid_latent,
        mesh_latent,
        g2m_pick,
        g2m_sender.reshape(1, -1),
        g2m_receiver.reshape(1, -1),
        m2m_pick,
        m2m_sender.reshape(1, -1),
        m2m_receiver.reshape(1, -1),
    )
    packed = call(
        pack_kernel,
        sources,
        [((listed + mesh_count + INDEX_ROWS, latent), BF16)],
        [((INDEX_ROWS, latent), F32)] + [(source.shape, source.dtype) for source in sources],
        10**7,
        fetched=len(sources),
        megabytes=56,
    )[0]
    packed, cotangent, weights = lax.optimization_barrier((packed, mesh_cotangent, weights))
    steps = (0, *range(2, regions), 1)
    packs = [packed] + [swap(packed, "space", step) for step in steps[1:]]
    weights, turned = call(
        weights_kernel,
        (weights,),
        [(weights.shape, BF16), ((latent, 3 * latent), BF16)],
        [],
        10**8,
        fetched=1,
    )
    packs[1], cotangent = lax.optimization_barrier((packs[1], cotangent))
    cotangents = [cotangent] + [swap(cotangent, "space", step) for step in steps[1:]]
    rows = regions * mesh_count
    slots = regions * mesh_cap
    (
        mesh_out,
        grid_all,
        mesh_all,
        mesh_first,
        mesh_sent,
        hot_one,
        hot_two,
        turned_one,
        turned_two,
        hot_sent,
        slope_one,
        slope_two,
        normed_one,
        scaled_one,
        normed_two,
        scaled_two,
    ) = call(
        functools.partial(forward_kernel, steps, listed, mesh_count, mesh_cap),
        (*packs, weights),
        [
            (mesh_latent.shape, BF16),
            ((regions * listed, latent), BF16),
            ((rows, latent), BF16),
            ((rows, latent), BF16),
            ((regions * slots, latent), BF16),
            ((regions * (listed + mesh_count), edges), BF16),
            ((regions * (slots + mesh_count), edges), BF16),
            ((regions * edges, listed + mesh_count), BF16),
            ((regions * edges, slots + mesh_count), BF16),
            ((rows, slots), BF16),
            ((regions * edges, latent), BF16),
            ((regions * edges, latent), BF16),
            ((rows, latent), F32),
            ((rows, 128), F32),
            ((rows, latent), F32),
            ((rows, 128), F32),
        ],
        [
            ((regions * INDEX_ROWS, latent), F32),
            ((regions * edges, latent), BF16),
            ((rows, latent), F32),
        ],
        2 * 10**9,
    )
    mesh_grad, keep_two, give_two = call(
        functools.partial(process_back_kernel, steps, mesh_cap),
        (
            *cotangents,
            turned,
            mesh_first,
            mesh_sent,
            hot_two,
            turned_two,
            hot_sent,
            slope_two,
            normed_two,
            scaled_two,
        ),
        [((rows, latent), F32)] + [((half, 2 * latent), BF16)] * 2,
        [
            ((rows, latent), F32),
            ((regions * slots, latent), F32),
            ((rows, latent), BF16),
            ((columns, 2 * latent), BF16),
            ((regions * edges, latent), BF16),
        ],
        10**9,
    )
    own_slots, keep_one, give_one = call(
        functools.partial(encode_back_kernel, regions),
        (
            grid_all,
            mesh_all,
            hot_one,
            turned_one,
            slope_one,
            normed_one,
            scaled_one,
            mesh_grad,
        ),
        [((listed, latent), BF16)] + [((half, 2 * latent), BF16)] * 2,
        [
            ((regions * listed, latent), BF16),
            ((rows, latent), BF16),
            ((columns, 2 * latent), BF16),
            ((regions * edges, latent), BF16),
        ],
        10**9,
    )
    half_one = added(keep_one, swap(give_one, "rep", 1))
    half_two = added(keep_two, swap(give_two, "rep", 1))
    half_one, own_slots = lax.optimization_barrier((half_one, own_slots))
    grid_grad = call(
        grid_back_kernel,
        (turned, g2m_pick, own_slots),
        [(grid_latent.shape, BF16)],
        [],
        10**8,
    )[0]
    two = summed_over_chips(half_two)
    one, grid_grad = lax.optimization_barrier((summed_over_chips(half_one), grid_grad))
    weight_grad = pl.pallas_call(
        finish_kernel,
        out_shape=jax.ShapeDtypeStruct((columns, 4 * latent), F32),
        in_specs=[VMEM] * 4,
        out_specs=pl.BlockSpec(memory_space=pltpu.HBM),
        scratch_shapes=[pltpu.VMEM((half, 2 * latent), F32)] * 4
        + [pltpu.SemaphoreType.DMA((4,))],
        compiler_params=pltpu.CompilerParams(vmem_limit_bytes=40 << 20),
    )(one, swap(one, "rep", 1), two, swap(two, "rep", 1))
    return (mesh_out, grid_grad, weight_grad)


def solution(mesh):
    regions = mesh.shape["space"]
    samples = mesh.shape["rep"]

    def whole(*arguments):
        edges = arguments[5].shape[0] + arguments[8].shape[0]
        latent = arguments[3].shape[0]
        fits = edges * latent * 4 <= SAMPLE_EDGE_BYTES and latent % (128 * regions) == 0
        paired = all(n > 1 and n & (n - 1) == 0 for n in (regions, samples))
        return sharded(whole_sample_body if fits and paired else partitioned_body)(*arguments)

    def sharded(body):
        return jax.shard_map(
            body,
            mesh=mesh,
            in_specs=(
                P(("groups", "rep"), "space", None),
                P(("groups", "rep"), "space", None),
                P(("groups", "rep"), "space", None),
                P(),
                P("space", None, None),
                P("space"),
                P("space"),
                P("space", None, None),
                P("space"),
                P("space"),
            ),
            out_specs=(
                P(("groups", "rep"), "space", None),
                P(("groups", "rep"), "space", None),
                P(("groups", "space"), None),
            ),
            check_vma=False,
        )

    return whole
```

```python
import functools

import jax
import jax.numpy as jnp
from jax import lax
from jax.experimental import pallas as pl
from jax.experimental.pallas import tpu as pltpu
from jax.sharding import PartitionSpec as P

EPSILON = 1e-05


def with_halo(cells, sides, width):
    for axis, dim in sides:
        count = lax.axis_size(axis)
        ends = count - 1
        head = lax.slice_in_dim(cells, 0, width, axis=dim)
        tail = lax.slice_in_dim(cells, cells.shape[dim] - width, cells.shape[dim], axis=dim)
        cells = jnp.concatenate(
            [
                lax.ppermute(tail, axis, [(i, (i + 1) % count) for i in range(ends)]),
                cells,
                lax.ppermute(head, axis, [((i + 1) % count, i) for i in range(ends)]),
            ],
            axis=dim,
        )
    return cells


def swish(values):
    return values * jax.nn.sigmoid(values)


def swish_slope(values):
    squash = jax.nn.sigmoid(values)
    return squash * (1.0 + values * (1.0 - squash))


def norm_rows(values):
    centred = values - jnp.mean(values, -1, keepdims=True)
    return centred * lax.rsqrt(jnp.mean(centred * centred, -1, keepdims=True) + EPSILON)


def norm_rows_back(values, upstream):
    centred = values - jnp.mean(values, -1, keepdims=True)
    scaled = lax.rsqrt(jnp.mean(centred * centred, -1, keepdims=True) + EPSILON)
    normed = centred * scaled
    return scaled * (
        upstream
        - jnp.mean(upstream, -1, keepdims=True)
        - normed * jnp.mean(upstream * normed, -1, keepdims=True)
    )


def slot_rows(pick_row):
    listed = pick_row.reshape(-1)
    return listed


def mesh_route(outgoing, capacity, peer_count):
    columns = outgoing.shape[1]
    pieces = lax.all_to_all(
        outgoing.reshape(peer_count, capacity, columns),
        "space",
        split_axis=0,
        concat_axis=0,
        tiled=True,
    )
    arrived = pieces.reshape(peer_count * capacity, columns)
    return arrived


def grid_route(outgoing, capacity):
    columns = outgoing.shape[1]
    lists = outgoing.reshape(3, capacity, columns)
    rims = with_halo(jnp.stack([lists[0], lists[2]]), (("space", 0),), 1)
    return jnp.concatenate([rims[0], lists[1], rims[3]], axis=0)


def edge_pass(arrived, recv_table, located, receiver, w_send, w_recv):
    recv_proj = jnp.dot(recv_table, w_recv, preferred_element_type=jnp.float32)
    slot_proj = jnp.dot(arrived, w_send, preferred_element_type=jnp.float32)
    activation = slot_proj[located] + recv_proj[receiver]
    message = swish(activation).astype(jnp.bfloat16)
    member = (
        receiver[None, :] == jnp.arange(recv_table.shape[0], dtype=jnp.int32)[:, None]
    ).astype(jnp.bfloat16)
    summed = jnp.dot(member, message, preferred_element_type=jnp.float32)
    return (activation, member, summed)


def backward_pass(slot_count, located, activation, member, receiver, agg_grad, w_send):
    edge_grad = (agg_grad[receiver] * swish_slope(activation)).astype(jnp.bfloat16)
    recv_sum = jnp.dot(member, edge_grad, preferred_element_type=jnp.float32).astype(jnp.bfloat16)
    slot_member = (located[None, :] == jnp.arange(slot_count, dtype=jnp.int32)[:, None]).astype(
        jnp.bfloat16
    )
    slot_sum = jnp.dot(slot_member, edge_grad, preferred_element_type=jnp.float32).astype(
        jnp.bfloat16
    )
    returned = jnp.dot(slot_sum, w_send.T, preferred_element_type=jnp.float32).astype(jnp.bfloat16)
    return (recv_sum, slot_sum, returned)


def gather_back(listed, back_rows, row_count):
    owner = (listed[None, :] == jnp.arange(row_count, dtype=jnp.int32)[:, None]).astype(
        jnp.bfloat16
    )
    return jnp.dot(owner, back_rows, preferred_element_type=jnp.float32)


def partitioned_body(
    grid_latent,
    mesh_latent,
    mesh_cotangent,
    weights,
    g2m_pick,
    g2m_sender,
    g2m_receiver,
    m2m_pick,
    m2m_sender,
    m2m_receiver,
):
    grid_rows = grid_latent[0]
    mesh_rows = mesh_latent[0]
    upstream = mesh_cotangent[0].astype(jnp.float32)
    latent = weights.shape[0]
    encode_sender = weights[:, :latent]
    encode_receiver = weights[:, latent : 2 * latent]
    process_sender = weights[:, 2 * latent : 3 * latent]
    process_receiver = weights[:, 3 * latent :]
    peer_count = lax.axis_size("space")
    grid_cap = g2m_pick.shape[2]
    mesh_cap = m2m_pick.shape[2]
    grid_listed = g2m_pick[0].reshape(-1)
    grid_arrived = grid_route(grid_rows[grid_listed], grid_cap)
    act_first, member_first, summed_first = edge_pass(
        grid_arrived, mesh_rows, g2m_sender, g2m_receiver, encode_sender, encode_receiver
    )
    mesh_first = (mesh_rows.astype(jnp.float32) + norm_rows(summed_first)).astype(jnp.bfloat16)
    mesh_listed = slot_rows(m2m_pick[0])
    mesh_arrived = mesh_route(mesh_first[mesh_listed], mesh_cap, peer_count)
    act_second, member_second, summed_second = edge_pass(
        mesh_arrived, mesh_first, m2m_sender, m2m_receiver, process_sender, process_receiver
    )
    mesh_final = (mesh_first.astype(jnp.float32) + norm_rows(summed_second)).astype(jnp.bfloat16)
    agg_second = norm_rows_back(summed_second, upstream)
    recv_second, slot_second, returned_second = backward_pass(
        mesh_arrived.shape[0],
        m2m_sender,
        act_second,
        member_second,
        m2m_receiver,
        agg_second,
        process_sender,
    )
    back_second = mesh_route(returned_second, mesh_cap, peer_count)
    mesh_grad = upstream + jnp.dot(
        recv_second, process_receiver.T, preferred_element_type=jnp.float32
    )
    mesh_grad = mesh_grad + gather_back(mesh_listed, back_second, mesh_rows.shape[0])
    agg_first = norm_rows_back(summed_first, mesh_grad)
    recv_first, slot_first, returned_first = backward_pass(
        grid_arrived.shape[0],
        g2m_sender,
        act_first,
        member_first,
        g2m_receiver,
        agg_first,
        encode_sender,
    )
    back_first = grid_route(returned_first, grid_cap)
    grid_grad = gather_back(grid_listed, back_first, grid_rows.shape[0]).astype(jnp.bfloat16)
    factor_pairs = (
        (grid_arrived, slot_first),
        (mesh_rows, recv_first),
        (mesh_arrived, slot_second),
        (mesh_first, recv_second),
    )
    blocks = []
    for first_factor, second_factor in factor_pairs:
        blocks.append(
            lax.dot_general(
                first_factor,
                second_factor,
                (((0,), (0,)), ((), ())),
                preferred_element_type=jnp.float32,
            )
        )
    shares = lax.psum_scatter(
        jnp.concatenate(blocks, axis=1).astype(jnp.bfloat16),
        "space",
        scatter_dimension=0,
        tiled=True,
    )
    weight_grad = lax.psum(shares, "rep").astype(jnp.float32)
    return (mesh_final[None], grid_grad[None], weight_grad)


F32 = jnp.float32
BF16 = jnp.bfloat16
INDEX_ROWS = 8
SAMPLE_EDGE_BYTES = 8 << 20


def dot(left, right):
    return jnp.dot(left, right, preferred_element_type=F32)


def dot_first(left, right):
    return lax.dot_general(left, right, (((0,), (0,)), ((), ())), preferred_element_type=F32)


def one_hot(labels, count):
    rows = lax.broadcasted_iota(jnp.int32, (count, labels.shape[-1]), 0)
    return (rows == labels).astype(F32).astype(BF16)


def row_moments(values):
    centred = values - jnp.mean(values, -1, keepdims=True)
    return centred, lax.rsqrt(jnp.mean(centred * centred, -1, keepdims=True) + EPSILON)


def moments_back(normed, scaled, upstream):
    return scaled * (
        upstream
        - jnp.mean(upstream, -1, keepdims=True)
        - normed * jnp.mean(upstream * normed, -1, keepdims=True)
    )


def fetch(pairs, semaphores):
    copies = [
        pltpu.make_async_copy(source, target, semaphores.at[n])
        for n, (source, target) in enumerate(pairs)
    ]
    for copy in copies:
        copy.start()
    for copy in copies:
        copy.wait()


def pack_kernel(*refs):
    sources, packed_ref, index_ref = refs[:8], refs[8], refs[9]
    local, semaphores = refs[10:18], refs[18]
    fetch(list(zip(sources, local)), semaphores)
    (
        grid_ref,
        mesh_ref,
        g2m_pick_ref,
        g2m_sender_ref,
        g2m_receiver_ref,
        m2m_pick_ref,
        m2m_sender_ref,
        m2m_receiver_ref,
    ) = local
    lists, _, capacity = g2m_pick_ref.shape
    mesh_count = mesh_ref.shape[1]
    regions, mesh_cap = m2m_pick_ref.shape[1:]
    edges = g2m_sender_ref.shape[1]
    grid_rows = grid_ref[0]
    for i in range(lists):
        picked = one_hot(g2m_pick_ref[i], grid_rows.shape[0])
        packed_ref[i * capacity : (i + 1) * capacity, :] = dot_first(picked, grid_rows).astype(BF16)
    first = lists * capacity
    packed_ref[first : first + mesh_count, :] = mesh_ref[0]
    index_ref[...] = jnp.zeros_like(index_ref)
    index_ref[0:1, 0:edges] = g2m_sender_ref[...].astype(F32)
    index_ref[0:1, edges : 2 * edges] = g2m_receiver_ref[...].astype(F32)
    index_ref[1:2, 0:edges] = m2m_sender_ref[...].astype(F32)
    index_ref[1:2, edges : 2 * edges] = m2m_receiver_ref[...].astype(F32)
    slots = regions * mesh_cap
    lane = lax.broadcasted_iota(jnp.int32, (mesh_cap, slots), 1)
    spread = (lane % mesh_cap == lax.broadcasted_iota(jnp.int32, (mesh_cap, slots), 0)).astype(F32)
    spread = dot(m2m_pick_ref[0].astype(F32).astype(BF16), spread.astype(BF16))
    lane = lax.broadcasted_iota(jnp.int32, (regions, slots), 1)
    owned = lane // mesh_cap == lax.broadcasted_iota(jnp.int32, (regions, slots), 0)
    index_ref[2:3, 0:slots] = jnp.sum(jnp.where(owned, spread, 0.0), 0, keepdims=True)
    packed_ref[first + mesh_count :, :] = index_ref[...].astype(BF16)


def weights_kernel(source_ref, weights_ref, turned_ref, semaphores):
    fetch([(source_ref, weights_ref)], semaphores)
    latent = weights_ref.shape[0]
    for n, block in enumerate((0, 2, 3)):
        turned_ref[:, n * latent : (n + 1) * latent] = weights_ref[
            :, block * latent : (block + 1) * latent
        ].T


def edge_blocks(edges):
    size = min(edges, 128)
    return [(first, min(size, edges - first)) for first in range(0, edges, size)]


def edge_forward(tables, hot_ref, turned_hot_ref, slope_ref, message_ref, mesh_count):
    regions = len(tables)
    edges = slope_ref.shape[0] // regions
    count = hot_ref.shape[0] // regions
    work = [(d, first, size) for d in range(regions) for first, size in edge_blocks(edges)]

    def gathered(d, first, size):
        rows = slice(d * edges + first, d * edges + first + size)
        return dot(turned_hot_ref[rows, :], tables[d])

    sums = []
    activation = gathered(*work[0])
    for n, (d, first, size) in enumerate(work):
        coming = gathered(*work[n + 1]) if n + 1 < len(work) else None
        squash = 0.5 + 0.5 * jnp.tanh(0.5 * activation)
        message = activation * squash
        rows = slice(d * edges + first, d * edges + first + size)
        slope_ref[rows, :] = (squash + message * (1.0 - squash)).astype(BF16)
        message_ref[rows, :] = message.astype(BF16)
        activation = coming
        if first + size == edges:
            hot = hot_ref[(d + 1) * count - mesh_count : (d + 1) * count, :]
            sums.append(dot(hot, message_ref[d * edges : (d + 1) * edges, :]))
    return sums


def forward_kernel(
    steps,
    listed,
    mesh_count,
    mesh_cap,
    *refs,
):
    regions = len(steps)
    packed_refs = refs[:regions]
    (
        weights_ref,
        mesh_out_ref,
        grid_ref,
        mesh_ref,
        first_ref,
        sent_ref,
        hot_one_ref,
        hot_two_ref,
        turned_one_ref,
        turned_two_ref,
        hot_sent_ref,
        slope_one_ref,
        slope_two_ref,
        normed_one_ref,
        scaled_one_ref,
        normed_two_ref,
        scaled_two_ref,
        index_ref,
        message_ref,
        sum_ref,
    ) = refs[regions:]
    latent = weights_ref.shape[0]
    edges = slope_one_ref.shape[0] // regions
    capacity = listed // 3
    slots = regions * mesh_cap
    me = lax.axis_index("space")
    for step, packed_ref in zip(steps, packed_refs):
        region = lax.bitwise_xor(me, step)
        at = lambda rows: pl.ds(pl.multiple_of(region * rows, rows), rows)
        grid_ref[at(listed), :] = packed_ref[:listed, :]
        mesh_ref[at(mesh_count), :] = packed_ref[listed : listed + mesh_count, :]
        index_ref[at(INDEX_ROWS), :] = packed_ref[listed + mesh_count :, :].astype(F32)

    grid_proj = dot(grid_ref[...], weights_ref[:, :latent])
    mesh_proj = dot(mesh_ref[...], weights_ref[:, latent : 2 * latent])
    for d in range(regions):
        index = index_ref[d * INDEX_ROWS : (d + 1) * INDEX_ROWS, :].astype(jnp.int32)
        for row, senders, hot_ref, turned_ref in (
            (0, listed, hot_one_ref, turned_one_ref),
            (1, slots, hot_two_ref, turned_two_ref),
        ):
            count = senders + mesh_count
            hot = jnp.concatenate(
                [
                    one_hot(index[row : row + 1, :edges], senders),
                    one_hot(index[row : row + 1, edges:], mesh_count),
                ],
                axis=0,
            )
            hot_ref[d * count : (d + 1) * count, :] = hot
            turned_ref[d * edges : (d + 1) * edges, :] = hot.T
        hot_sent_ref[d * mesh_count : (d + 1) * mesh_count, :] = one_hot(
            index[2:3, :slots], mesh_count
        )

    blank = jnp.zeros((capacity, latent), F32)
    tables = []
    for d in range(regions):
        before = (d - 1) * listed + 2 * capacity
        within = d * listed + capacity
        after = (d + 1) * listed
        tables.append(
            jnp.concatenate(
                [
                    grid_proj[before : before + capacity] if d > 0 else blank,
                    grid_proj[within : within + capacity],
                    grid_proj[after : after + capacity] if d < regions - 1 else blank,
                    mesh_proj[d * mesh_count : (d + 1) * mesh_count],
                ],
                axis=0,
            ).astype(BF16)
        )
    sums = edge_forward(
        tables, hot_one_ref, turned_one_ref, slope_one_ref, message_ref, mesh_count
    )
    for d in range(regions):
        sum_ref[d * mesh_count : (d + 1) * mesh_count, :] = sums[d]
    centred, scaled = row_moments(sum_ref[...])
    normed = centred * scaled
    normed_one_ref[...] = normed
    scaled_one_ref[...] = jnp.broadcast_to(scaled, scaled_one_ref.shape)
    first_ref[...] = (mesh_ref[...].astype(F32) + normed).astype(BF16)

    for s in range(regions):
        rows = slice(s * mesh_count, (s + 1) * mesh_count)
        sent_ref[s * slots : (s + 1) * slots, :] = dot_first(
            hot_sent_ref[rows, :], first_ref[rows, :]
        ).astype(BF16)
    sent_proj = dot(sent_ref[...], weights_ref[:, 2 * latent : 3 * latent])
    first_proj = dot(first_ref[...], weights_ref[:, 3 * latent :])
    tables = []
    for d in range(regions):
        pieces = [
            sent_proj[s * slots + d * mesh_cap : s * slots + (d + 1) * mesh_cap]
            for s in range(regions)
        ]
        tables.append(
            jnp.concatenate(
                pieces + [first_proj[d * mesh_count : (d + 1) * mesh_count]], axis=0
            ).astype(BF16)
        )
    sums = edge_forward(
        tables, hot_two_ref, turned_two_ref, slope_two_ref, message_ref, mesh_count
    )
    for d in range(regions):
        sum_ref[d * mesh_count : (d + 1) * mesh_count, :] = sums[d]
    centred, scaled = row_moments(sum_ref[...])
    normed_two_ref[...] = centred * scaled
    scaled_two_ref[...] = jnp.broadcast_to(scaled, scaled_two_ref.shape)
    own = pl.ds(pl.multiple_of(me * mesh_count, mesh_count), mesh_count)
    mesh_out_ref[0] = (first_ref[own, :].astype(F32) + normed_two_ref[own, :]).astype(BF16)


def edge_backward(regions, agg_grad, hot_ref, turned_hot_ref, slope_ref, edge_grad_ref):
    edges = slope_ref.shape[0] // regions
    count = hot_ref.shape[0] // regions
    mesh_count = agg_grad.shape[0] // regions
    blank = jnp.zeros((count - mesh_count, agg_grad.shape[1]), BF16)
    work = [(d, first, size) for d in range(regions) for first, size in edge_blocks(edges)]

    def gathered(d, first, size):
        rows = slice(d * edges + first, d * edges + first + size)
        table = jnp.concatenate([blank, agg_grad[d * mesh_count : (d + 1) * mesh_count]], axis=0)
        return dot(turned_hot_ref[rows, :], table)

    sums = []
    upstream = gathered(*work[0])
    for n, (d, first, size) in enumerate(work):
        coming = gathered(*work[n + 1]) if n + 1 < len(work) else None
        rows = slice(d * edges + first, d * edges + first + size)
        edge_grad_ref[rows, :] = (upstream * slope_ref[rows, :].astype(F32)).astype(BF16)
        upstream = coming
        if first + size == edges:
            hot = hot_ref[d * count : (d + 1) * count, :]
            sums.append(dot(hot, edge_grad_ref[d * edges : (d + 1) * edges, :]))
    return sums


def halve(share_ref, keep_ref, give_ref):
    half = keep_ref.shape[0]
    core = lax.bitwise_and(lax.axis_index("rep"), 1)
    keep_ref[...] = share_ref[pl.ds(pl.multiple_of(core * half, half), half), :]
    give_ref[...] = share_ref[pl.ds(pl.multiple_of((1 - core) * half, half), half), :]


def process_back_kernel(steps, mesh_cap, *refs):
    regions = len(steps)
    cotangent_refs = refs[:regions]
    (
        turned_ref,
        first_ref,
        sent_ref,
        hot_ref,
        turned_hot_ref,
        hot_sent_ref,
        slope_ref,
        normed_ref,
        scaled_ref,
        mesh_grad_ref,
        keep_ref,
        give_ref,
        upstream_ref,
        slot_ref,
        recv_ref,
        share_ref,
        edge_grad_ref,
    ) = refs[regions:]
    latent = first_ref.shape[1]
    mesh_count = first_ref.shape[0] // regions
    slots = regions * mesh_cap
    me = lax.axis_index("space")
    for step, cotangent_ref in zip(steps, cotangent_refs):
        region = lax.bitwise_xor(me, step)
        at = pl.ds(pl.multiple_of(region * mesh_count, mesh_count), mesh_count)
        upstream_ref[at, :] = cotangent_ref[0].astype(F32)
    agg_grad = moments_back(normed_ref[...], scaled_ref[:, 0:1], upstream_ref[...]).astype(BF16)
    all_sums = edge_backward(
        regions, agg_grad, hot_ref, turned_hot_ref, slope_ref, edge_grad_ref
    )
    for d, sums in enumerate(all_sums):
        for s in range(regions):
            first = s * slots + d * mesh_cap
            slot_ref[first : first + mesh_cap, :] = sums[s * mesh_cap : (s + 1) * mesh_cap]
        recv_ref[d * mesh_count : (d + 1) * mesh_count, :] = sums[slots:].astype(BF16)
    slot_sum = slot_ref[...].astype(BF16)
    columns = share_ref.shape[0]
    mine = pl.ds(pl.multiple_of(me * columns, columns), columns)
    share_ref[:, :latent] = dot_first(sent_ref[:, mine], slot_sum).astype(BF16)
    share_ref[:, latent:] = dot_first(first_ref[:, mine], recv_ref[...]).astype(BF16)
    halve(share_ref, keep_ref, give_ref)
    returned = dot(slot_sum, turned_ref[:, latent : 2 * latent]).astype(BF16)
    grad = upstream_ref[...] + dot(recv_ref[...], turned_ref[:, 2 * latent :])
    for s in range(regions):
        rows = slice(s * mesh_count, (s + 1) * mesh_count)
        mesh_grad_ref[rows, :] = grad[rows] + dot(
            hot_sent_ref[rows, :], returned[s * slots : (s + 1) * slots]
        )


def encode_back_kernel(
    regions,
    grid_ref,
    mesh_ref,
    hot_ref,
    turned_hot_ref,
    slope_ref,
    normed_ref,
    scaled_ref,
    mesh_grad_ref,
    own_slot_ref,
    keep_ref,
    give_ref,
    slot_ref,
    recv_ref,
    share_ref,
    edge_grad_ref,
):
    latent = mesh_ref.shape[1]
    mesh_count = mesh_ref.shape[0] // regions
    listed = grid_ref.shape[0] // regions
    capacity = listed // 3
    me = lax.axis_index("space")
    agg_grad = moments_back(normed_ref[...], scaled_ref[:, 0:1], mesh_grad_ref[...]).astype(BF16)
    blank = jnp.zeros((capacity, latent), BF16)
    slot_ref[0:capacity, :] = blank
    slot_ref[regions * listed - capacity :, :] = blank
    all_sums = edge_backward(
        regions, agg_grad, hot_ref, turned_hot_ref, slope_ref, edge_grad_ref
    )
    for d, sums in enumerate(all_sums):
        sums = sums.astype(BF16)
        for j in range(3):
            source = d + j - 1
            if 0 <= source < regions:
                first = source * listed + (2 - j) * capacity
                slot_ref[first : first + capacity, :] = sums[j * capacity : (j + 1) * capacity]
        recv_ref[d * mesh_count : (d + 1) * mesh_count, :] = sums[listed:]
    columns = share_ref.shape[0]
    mine = pl.ds(pl.multiple_of(me * columns, columns), columns)
    share_ref[:, :latent] = dot_first(grid_ref[:, mine], slot_ref[...]).astype(BF16)
    share_ref[:, latent:] = dot_first(mesh_ref[:, mine], recv_ref[...]).astype(BF16)
    halve(share_ref, keep_ref, give_ref)
    own = pl.ds(pl.multiple_of(me * listed, listed), listed)
    own_slot_ref[...] = slot_ref[own, :]


def grid_back_kernel(turned_ref, pick_ref, own_slot_ref, grid_grad_ref):
    lists, _, capacity = pick_ref.shape
    latent = own_slot_ref.shape[1]
    returned = dot(own_slot_ref[...], turned_ref[:, :latent]).astype(BF16)
    total = None
    for i in range(lists):
        owner = one_hot(pick_ref[i], grid_grad_ref.shape[1])
        part = dot(owner, returned[i * capacity : (i + 1) * capacity])
        total = part if total is None else total + part
    grid_grad_ref[0] = total.astype(BF16)


def finish_kernel(one_ref, other_one_ref, two_ref, other_two_ref, weight_grad_ref):
    half, width = one_ref.shape
    core = lax.bitwise_and(lax.axis_index("rep"), 1)
    mine = pl.ds(pl.multiple_of(core * half, half), half)
    other = pl.ds(pl.multiple_of((1 - core) * half, half), half)
    weight_grad_ref[mine, :width] = one_ref[...].astype(F32)
    weight_grad_ref[other, :width] = other_one_ref[...].astype(F32)
    weight_grad_ref[mine, width:] = two_ref[...].astype(F32)
    weight_grad_ref[other, width:] = other_two_ref[...].astype(F32)


VMEM = pl.BlockSpec(memory_space=pltpu.VMEM)


def call(kernel, operands, outputs, scratch, flops, fetched=0, megabytes=40):
    hbm = pl.BlockSpec(memory_space=pltpu.HBM)
    return pl.pallas_call(
        kernel,
        out_shape=[jax.ShapeDtypeStruct(shape, kind) for shape, kind in outputs],
        in_specs=[hbm] * fetched + [VMEM] * (len(operands) - fetched),
        out_specs=[VMEM] * len(outputs),
        scratch_shapes=[pltpu.VMEM(shape, kind) for shape, kind in scratch]
        + ([pltpu.SemaphoreType.DMA((fetched,))] if fetched else []),
        compiler_params=pltpu.CompilerParams(vmem_limit_bytes=megabytes << 20),
        cost_estimate=pl.CostEstimate(flops=flops, bytes_accessed=4 << 20, transcendentals=0),
    )(*operands)


def swap(block, axis, bits):
    return lax.ppermute(block, axis, [(i, i ^ bits) for i in range(lax.axis_size(axis))])


def added(left, right):
    return (left.astype(F32) + right.astype(F32)).astype(BF16)


def summed_half(keep, give):
    half = added(keep, swap(give, "rep", 1))
    bit = 2
    while bit < lax.axis_size("rep"):
        half = added(half, swap(half, "rep", bit))
        bit *= 2
    return half, swap(half, "rep", 1)


def whole_sample_body(
    grid_latent,
    mesh_latent,
    mesh_cotangent,
    weights,
    g2m_pick,
    g2m_sender,
    g2m_receiver,
    m2m_pick,
    m2m_sender,
    m2m_receiver,
):
    regions = lax.axis_size("space")
    latent = weights.shape[0]
    listed = g2m_pick.shape[1] * g2m_pick.shape[2]
    mesh_count = mesh_latent.shape[1]
    mesh_cap = m2m_pick.shape[2]
    edges = g2m_sender.shape[0]
    columns = latent // regions
    half = columns // 2
    g2m_pick = g2m_pick.transpose(1, 0, 2)
    sources = (
        grid_latent,
        mesh_latent,
        g2m_pick,
        g2m_sender.reshape(1, -1),
        g2m_receiver.reshape(1, -1),
        m2m_pick,
        m2m_sender.reshape(1, -1),
        m2m_receiver.reshape(1, -1),
    )
    packed = call(
        pack_kernel,
        sources,
        [((listed + mesh_count + INDEX_ROWS, latent), BF16)],
        [((INDEX_ROWS, latent), F32)] + [(source.shape, source.dtype) for source in sources],
        10**7,
        fetched=len(sources),
        megabytes=56,
    )[0]
    packed, cotangent, weights = lax.optimization_barrier((packed, mesh_cotangent, weights))
    steps = tuple(range(regions))
    packs = [packed] + [swap(packed, "space", step) for step in steps[1:]]
    near = swap(cotangent, "space", 1)
    weights, turned = call(
        weights_kernel,
        (weights,),
        [(weights.shape, BF16), ((latent, 3 * latent), BF16)],
        [],
        10**8,
        fetched=1,
    )
    *packs[1:3], cotangent = lax.optimization_barrier((*packs[1:3], cotangent))
    cotangents = [cotangent, near] + [swap(cotangent, "space", step) for step in steps[2:]]
    rows = regions * mesh_count
    slots = regions * mesh_cap
    (
        mesh_out,
        grid_all,
        mesh_all,
        mesh_first,
        mesh_sent,
        hot_one,
        hot_two,
        turned_one,
        turned_two,
        hot_sent,
        slope_one,
        slope_two,
        normed_one,
        scaled_one,
        normed_two,
        scaled_two,
    ) = call(
        functools.partial(forward_kernel, steps, listed, mesh_count, mesh_cap),
        (*packs, weights),
        [
            (mesh_latent.shape, BF16),
            ((regions * listed, latent), BF16),
            ((rows, latent), BF16),
            ((rows, latent), BF16),
            ((regions * slots, latent), BF16),
            ((regions * (listed + mesh_count), edges), BF16),
            ((regions * (slots + mesh_count), edges), BF16),
            ((regions * edges, listed + mesh_count), BF16),
            ((regions * edges, slots + mesh_count), BF16),
            ((rows, slots), BF16),
            ((regions * edges, latent), BF16),
            ((regions * edges, latent), BF16),
            ((rows, latent), F32),
            ((rows, 128), F32),
            ((rows, latent), F32),
            ((rows, 128), F32),
        ],
        [
            ((regions * INDEX_ROWS, latent), F32),
            ((regions * edges, latent), BF16),
            ((rows, latent), F32),
        ],
        2 * 10**9,
    )
    mesh_grad, keep_two, give_two = call(
        functools.partial(process_back_kernel, steps, mesh_cap),
        (
            *cotangents,
            turned,
            mesh_first,
            mesh_sent,
            hot_two,
            turned_two,
            hot_sent,
            slope_two,
            normed_two,
            scaled_two,
        ),
        [((rows, latent), F32)] + [((half, 2 * latent), BF16)] * 2,
        [
            ((rows, latent), F32),
            ((regions * slots, latent), F32),
            ((rows, latent), BF16),
            ((columns, 2 * latent), BF16),
            ((regions * edges, latent), BF16),
        ],
        10**9,
    )
    own_slots, keep_one, give_one = call(
        functools.partial(encode_back_kernel, regions),
        (
            grid_all,
            mesh_all,
            hot_one,
            turned_one,
            slope_one,
            normed_one,
            scaled_one,
            mesh_grad,
        ),
        [((listed, latent), BF16)] + [((half, 2 * latent), BF16)] * 2,
        [
            ((regions * listed, latent), BF16),
            ((rows, latent), BF16),
            ((columns, 2 * latent), BF16),
            ((regions * edges, latent), BF16),
        ],
        10**9,
    )
    grid_grad = call(
        grid_back_kernel,
        (turned, g2m_pick, own_slots),
        [(grid_latent.shape, BF16)],
        [],
        10**8,
    )[0]
    weight_grad = call(
        finish_kernel,
        (*summed_half(keep_one, give_one), *summed_half(keep_two, give_two)),
        [((columns, 4 * latent), F32)],
        [],
        10**6,
    )[0]
    return (mesh_out, grid_grad, weight_grad)


def solution(mesh):
    regions = mesh.shape["space"]
    samples = mesh.shape["rep"]

    def whole(*arguments):
        edges = arguments[5].shape[0] + arguments[8].shape[0]
        latent = arguments[3].shape[0]
        fits = edges * latent * 4 <= SAMPLE_EDGE_BYTES and latent % (128 * regions) == 0
        paired = all(n > 1 and n & (n - 1) == 0 for n in (regions, samples))
        return sharded(whole_sample_body if fits and paired else partitioned_body)(*arguments)

    def sharded(body):
        return jax.shard_map(
            body,
            mesh=mesh,
            in_specs=(
                P(("groups", "rep"), "space", None),
                P(("groups", "rep"), "space", None),
                P(("groups", "rep"), "space", None),
                P(),
                P("space", None, None),
                P("space"),
                P("space"),
                P("space", None, None),
                P("space"),
                P("space"),
            ),
            out_specs=(
                P(("groups", "rep"), "space", None),
                P(("groups", "rep"), "space", None),
                P(("groups", "space"), None),
            ),
            check_vma=False,
        )

    return whole
```

```python
import functools

import jax
import jax.numpy as jnp
from jax import lax
from jax.experimental import pallas as pl
from jax.experimental.pallas import tpu as pltpu
from jax.sharding import PartitionSpec as P

EPSILON = 1e-05


def with_halo(cells, sides, width):
    for axis, dim in sides:
        count = lax.axis_size(axis)
        ends = count - 1
        head = lax.slice_in_dim(cells, 0, width, axis=dim)
        tail = lax.slice_in_dim(cells, cells.shape[dim] - width, cells.shape[dim], axis=dim)
        cells = jnp.concatenate(
            [
                lax.ppermute(tail, axis, [(i, (i + 1) % count) for i in range(ends)]),
                cells,
                lax.ppermute(head, axis, [((i + 1) % count, i) for i in range(ends)]),
            ],
            axis=dim,
        )
    return cells


def swish(values):
    return values * jax.nn.sigmoid(values)


def swish_slope(values):
    squash = jax.nn.sigmoid(values)
    return squash * (1.0 + values * (1.0 - squash))


def norm_rows(values):
    centred = values - jnp.mean(values, -1, keepdims=True)
    return centred * lax.rsqrt(jnp.mean(centred * centred, -1, keepdims=True) + EPSILON)


def norm_rows_back(values, upstream):
    centred = values - jnp.mean(values, -1, keepdims=True)
    scaled = lax.rsqrt(jnp.mean(centred * centred, -1, keepdims=True) + EPSILON)
    normed = centred * scaled
    return scaled * (
        upstream
        - jnp.mean(upstream, -1, keepdims=True)
        - normed * jnp.mean(upstream * normed, -1, keepdims=True)
    )


def slot_rows(pick_row):
    listed = pick_row.reshape(-1)
    return listed


def mesh_route(outgoing, capacity, peer_count):
    columns = outgoing.shape[1]
    pieces = lax.all_to_all(
        outgoing.reshape(peer_count, capacity, columns),
        "space",
        split_axis=0,
        concat_axis=0,
        tiled=True,
    )
    arrived = pieces.reshape(peer_count * capacity, columns)
    return arrived


def grid_route(outgoing, capacity):
    columns = outgoing.shape[1]
    lists = outgoing.reshape(3, capacity, columns)
    rims = with_halo(jnp.stack([lists[0], lists[2]]), (("space", 0),), 1)
    return jnp.concatenate([rims[0], lists[1], rims[3]], axis=0)


def edge_pass(arrived, recv_table, located, receiver, w_send, w_recv):
    recv_proj = jnp.dot(recv_table, w_recv, preferred_element_type=jnp.float32)
    slot_proj = jnp.dot(arrived, w_send, preferred_element_type=jnp.float32)
    activation = slot_proj[located] + recv_proj[receiver]
    message = swish(activation).astype(jnp.bfloat16)
    member = (
        receiver[None, :] == jnp.arange(recv_table.shape[0], dtype=jnp.int32)[:, None]
    ).astype(jnp.bfloat16)
    summed = jnp.dot(member, message, preferred_element_type=jnp.float32)
    return (activation, member, summed)


def backward_pass(slot_count, located, activation, member, receiver, agg_grad, w_send):
    edge_grad = (agg_grad[receiver] * swish_slope(activation)).astype(jnp.bfloat16)
    recv_sum = jnp.dot(member, edge_grad, preferred_element_type=jnp.float32).astype(jnp.bfloat16)
    slot_member = (located[None, :] == jnp.arange(slot_count, dtype=jnp.int32)[:, None]).astype(
        jnp.bfloat16
    )
    slot_sum = jnp.dot(slot_member, edge_grad, preferred_element_type=jnp.float32).astype(
        jnp.bfloat16
    )
    returned = jnp.dot(slot_sum, w_send.T, preferred_element_type=jnp.float32).astype(jnp.bfloat16)
    return (recv_sum, slot_sum, returned)


def gather_back(listed, back_rows, row_count):
    owner = (listed[None, :] == jnp.arange(row_count, dtype=jnp.int32)[:, None]).astype(
        jnp.bfloat16
    )
    return jnp.dot(owner, back_rows, preferred_element_type=jnp.float32)


def partitioned_body(
    grid_latent,
    mesh_latent,
    mesh_cotangent,
    weights,
    g2m_pick,
    g2m_sender,
    g2m_receiver,
    m2m_pick,
    m2m_sender,
    m2m_receiver,
):
    grid_rows = grid_latent[0]
    mesh_rows = mesh_latent[0]
    upstream = mesh_cotangent[0].astype(jnp.float32)
    latent = weights.shape[0]
    encode_sender = weights[:, :latent]
    encode_receiver = weights[:, latent : 2 * latent]
    process_sender = weights[:, 2 * latent : 3 * latent]
    process_receiver = weights[:, 3 * latent :]
    peer_count = lax.axis_size("space")
    grid_cap = g2m_pick.shape[2]
    mesh_cap = m2m_pick.shape[2]
    grid_listed = g2m_pick[0].reshape(-1)
    grid_arrived = grid_route(grid_rows[grid_listed], grid_cap)
    act_first, member_first, summed_first = edge_pass(
        grid_arrived, mesh_rows, g2m_sender, g2m_receiver, encode_sender, encode_receiver
    )
    mesh_first = (mesh_rows.astype(jnp.float32) + norm_rows(summed_first)).astype(jnp.bfloat16)
    mesh_listed = slot_rows(m2m_pick[0])
    mesh_arrived = mesh_route(mesh_first[mesh_listed], mesh_cap, peer_count)
    act_second, member_second, summed_second = edge_pass(
        mesh_arrived, mesh_first, m2m_sender, m2m_receiver, process_sender, process_receiver
    )
    mesh_final = (mesh_first.astype(jnp.float32) + norm_rows(summed_second)).astype(jnp.bfloat16)
    agg_second = norm_rows_back(summed_second, upstream)
    recv_second, slot_second, returned_second = backward_pass(
        mesh_arrived.shape[0],
        m2m_sender,
        act_second,
        member_second,
        m2m_receiver,
        agg_second,
        process_sender,
    )
    back_second = mesh_route(returned_second, mesh_cap, peer_count)
    mesh_grad = upstream + jnp.dot(
        recv_second, process_receiver.T, preferred_element_type=jnp.float32
    )
    mesh_grad = mesh_grad + gather_back(mesh_listed, back_second, mesh_rows.shape[0])
    agg_first = norm_rows_back(summed_first, mesh_grad)
    recv_first, slot_first, returned_first = backward_pass(
        grid_arrived.shape[0],
        g2m_sender,
        act_first,
        member_first,
        g2m_receiver,
        agg_first,
        encode_sender,
    )
    back_first = grid_route(returned_first, grid_cap)
    grid_grad = gather_back(grid_listed, back_first, grid_rows.shape[0]).astype(jnp.bfloat16)
    factor_pairs = (
        (grid_arrived, slot_first),
        (mesh_rows, recv_first),
        (mesh_arrived, slot_second),
        (mesh_first, recv_second),
    )
    blocks = []
    for first_factor, second_factor in factor_pairs:
        blocks.append(
            lax.dot_general(
                first_factor,
                second_factor,
                (((0,), (0,)), ((), ())),
                preferred_element_type=jnp.float32,
            )
        )
    shares = lax.psum_scatter(
        jnp.concatenate(blocks, axis=1).astype(jnp.bfloat16),
        "space",
        scatter_dimension=0,
        tiled=True,
    )
    weight_grad = lax.psum(shares, "rep").astype(jnp.float32)
    return (mesh_final[None], grid_grad[None], weight_grad)


F32 = jnp.float32
BF16 = jnp.bfloat16
INDEX_ROWS = 8
SAMPLE_EDGE_BYTES = 8 << 20


def dot(left, right):
    return jnp.dot(left, right, preferred_element_type=F32)


def dot_first(left, right):
    return lax.dot_general(left, right, (((0,), (0,)), ((), ())), preferred_element_type=F32)


def one_hot(labels, count):
    rows = lax.broadcasted_iota(jnp.int32, (count, labels.shape[-1]), 0)
    return (rows == labels).astype(F32).astype(BF16)


def row_moments(values):
    centred = values - jnp.mean(values, -1, keepdims=True)
    return centred, lax.rsqrt(jnp.mean(centred * centred, -1, keepdims=True) + EPSILON)


def moments_back(normed, scaled, upstream):
    return scaled * (
        upstream
        - jnp.mean(upstream, -1, keepdims=True)
        - normed * jnp.mean(upstream * normed, -1, keepdims=True)
    )


def fetch(pairs, semaphores):
    copies = [
        pltpu.make_async_copy(source, target, semaphores.at[n])
        for n, (source, target) in enumerate(pairs)
    ]
    for copy in copies:
        copy.start()
    for copy in copies:
        copy.wait()


def pack_kernel(*refs):
    sources, packed_ref, index_ref = refs[:7], refs[7], refs[8]
    local, semaphores = refs[9:16], refs[16]
    fetch(list(zip(sources, local)), semaphores)
    (
        grid_ref,
        g2m_pick_ref,
        g2m_sender_ref,
        g2m_receiver_ref,
        m2m_pick_ref,
        m2m_sender_ref,
        m2m_receiver_ref,
    ) = local
    lists, _, capacity = g2m_pick_ref.shape
    regions, mesh_cap = m2m_pick_ref.shape[1:]
    edges = g2m_sender_ref.shape[1]
    grid_rows = grid_ref[0]
    for i in range(lists):
        picked = one_hot(g2m_pick_ref[i], grid_rows.shape[0])
        packed_ref[i * capacity : (i + 1) * capacity, :] = dot_first(picked, grid_rows).astype(BF16)
    first = lists * capacity
    index_ref[...] = jnp.zeros_like(index_ref)
    index_ref[0:1, 0:edges] = g2m_sender_ref[...].astype(F32)
    index_ref[0:1, edges : 2 * edges] = g2m_receiver_ref[...].astype(F32)
    index_ref[1:2, 0:edges] = m2m_sender_ref[...].astype(F32)
    index_ref[1:2, edges : 2 * edges] = m2m_receiver_ref[...].astype(F32)
    slots = regions * mesh_cap
    lane = lax.broadcasted_iota(jnp.int32, (mesh_cap, slots), 1)
    spread = (lane % mesh_cap == lax.broadcasted_iota(jnp.int32, (mesh_cap, slots), 0)).astype(F32)
    spread = dot(m2m_pick_ref[0].astype(F32).astype(BF16), spread.astype(BF16))
    lane = lax.broadcasted_iota(jnp.int32, (regions, slots), 1)
    owned = lane // mesh_cap == lax.broadcasted_iota(jnp.int32, (regions, slots), 0)
    index_ref[2:3, 0:slots] = jnp.sum(jnp.where(owned, spread, 0.0), 0, keepdims=True)
    packed_ref[first:, :] = index_ref[...].astype(BF16)


def weights_kernel(source_ref, weights_ref, turned_ref, semaphores):
    fetch([(source_ref, weights_ref)], semaphores)
    latent = weights_ref.shape[0]
    for n, block in enumerate((0, 2, 3)):
        turned_ref[:, n * latent : (n + 1) * latent] = weights_ref[
            :, block * latent : (block + 1) * latent
        ].T


def edge_blocks(edges):
    size = min(edges, 128)
    return [(first, min(size, edges - first)) for first in range(0, edges, size)]


def edge_forward(tables, hot_ref, turned_hot_ref, slope_ref, message_ref, mesh_count):
    regions = len(tables)
    edges = slope_ref.shape[0] // regions
    count = hot_ref.shape[0] // regions
    work = [(d, first, size) for d in range(regions) for first, size in edge_blocks(edges)]

    def gathered(d, first, size):
        rows = slice(d * edges + first, d * edges + first + size)
        return dot(turned_hot_ref[rows, :], tables[d])

    sums = []
    activation = gathered(*work[0])
    for n, (d, first, size) in enumerate(work):
        coming = gathered(*work[n + 1]) if n + 1 < len(work) else None
        squash = 0.5 + 0.5 * jnp.tanh(0.5 * activation)
        message = activation * squash
        rows = slice(d * edges + first, d * edges + first + size)
        slope_ref[rows, :] = (squash + message * (1.0 - squash)).astype(BF16)
        message_ref[rows, :] = message.astype(BF16)
        activation = coming
        if first + size == edges:
            hot = hot_ref[(d + 1) * count - mesh_count : (d + 1) * count, :]
            sums.append(dot(hot, message_ref[d * edges : (d + 1) * edges, :]))
    return sums


def forward_kernel(
    steps,
    listed,
    mesh_count,
    mesh_cap,
    *refs,
):
    regions = len(steps)
    blocks = []
    for step in steps:
        taken = 2
        blocks.append((step, refs[:taken]))
        refs = refs[taken:]
    (
        weights_ref,
        mesh_out_ref,
        grid_ref,
        mesh_ref,
        first_ref,
        sent_ref,
        hot_one_ref,
        hot_two_ref,
        turned_one_ref,
        turned_two_ref,
        hot_sent_ref,
        slope_one_ref,
        slope_two_ref,
        normed_one_ref,
        scaled_one_ref,
        normed_two_ref,
        scaled_two_ref,
        index_ref,
        message_ref,
        sum_ref,
    ) = refs
    latent = weights_ref.shape[0]
    edges = slope_one_ref.shape[0] // regions
    capacity = listed // 3
    slots = regions * mesh_cap
    me = lax.axis_index("space")
    for step, block_refs in blocks:
        region = lax.bitwise_xor(me, step)
        at = lambda rows: pl.ds(pl.multiple_of(region * rows, rows), rows)
        listed_ref, latent_ref = block_refs
        mesh_ref[at(mesh_count), :] = latent_ref[0]
        grid_ref[at(listed), :] = listed_ref[:listed, :]
        index_ref[at(INDEX_ROWS), :] = listed_ref[listed:, :].astype(F32)

    grid_proj = dot(grid_ref[...], weights_ref[:, :latent])
    mesh_proj = dot(mesh_ref[...], weights_ref[:, latent : 2 * latent])
    for d in range(regions):
        index = index_ref[d * INDEX_ROWS : (d + 1) * INDEX_ROWS, :].astype(jnp.int32)
        for row, senders, hot_ref, turned_ref in (
            (0, listed, hot_one_ref, turned_one_ref),
            (1, slots, hot_two_ref, turned_two_ref),
        ):
            count = senders + mesh_count
            hot = jnp.concatenate(
                [
                    one_hot(index[row : row + 1, :edges], senders),
                    one_hot(index[row : row + 1, edges:], mesh_count),
                ],
                axis=0,
            )
            hot_ref[d * count : (d + 1) * count, :] = hot
            turned_ref[d * edges : (d + 1) * edges, :] = hot.T
        hot_sent_ref[d * mesh_count : (d + 1) * mesh_count, :] = one_hot(
            index[2:3, :slots], mesh_count
        )

    blank = jnp.zeros((capacity, latent), F32)
    tables = []
    for d in range(regions):
        before = (d - 1) * listed + 2 * capacity
        within = d * listed + capacity
        after = (d + 1) * listed
        tables.append(
            jnp.concatenate(
                [
                    grid_proj[before : before + capacity] if d > 0 else blank,
                    grid_proj[within : within + capacity],
                    grid_proj[after : after + capacity] if d < regions - 1 else blank,
                    mesh_proj[d * mesh_count : (d + 1) * mesh_count],
                ],
                axis=0,
            ).astype(BF16)
        )
    sums = edge_forward(
        tables, hot_one_ref, turned_one_ref, slope_one_ref, message_ref, mesh_count
    )
    for d in range(regions):
        sum_ref[d * mesh_count : (d + 1) * mesh_count, :] = sums[d]
    centred, scaled = row_moments(sum_ref[...])
    normed = centred * scaled
    normed_one_ref[...] = normed
    scaled_one_ref[...] = jnp.broadcast_to(scaled, scaled_one_ref.shape)
    first_ref[...] = (mesh_ref[...].astype(F32) + normed).astype(BF16)

    for s in range(regions):
        rows = slice(s * mesh_count, (s + 1) * mesh_count)
        sent_ref[s * slots : (s + 1) * slots, :] = dot_first(
            hot_sent_ref[rows, :], first_ref[rows, :]
        ).astype(BF16)
    sent_proj = dot(sent_ref[...], weights_ref[:, 2 * latent : 3 * latent])
    first_proj = dot(first_ref[...], weights_ref[:, 3 * latent :])
    tables = []
    for d in range(regions):
        pieces = [
            sent_proj[s * slots + d * mesh_cap : s * slots + (d + 1) * mesh_cap]
            for s in range(regions)
        ]
        tables.append(
            jnp.concatenate(
                pieces + [first_proj[d * mesh_count : (d + 1) * mesh_count]], axis=0
            ).astype(BF16)
        )
    sums = edge_forward(
        tables, hot_two_ref, turned_two_ref, slope_two_ref, message_ref, mesh_count
    )
    for d in range(regions):
        sum_ref[d * mesh_count : (d + 1) * mesh_count, :] = sums[d]
    centred, scaled = row_moments(sum_ref[...])
    normed_two_ref[...] = centred * scaled
    scaled_two_ref[...] = jnp.broadcast_to(scaled, scaled_two_ref.shape)
    own = pl.ds(pl.multiple_of(me * mesh_count, mesh_count), mesh_count)
    mesh_out_ref[0] = (first_ref[own, :].astype(F32) + normed_two_ref[own, :]).astype(BF16)


def edge_backward(regions, agg_grad, hot_ref, turned_hot_ref, slope_ref, edge_grad_ref):
    edges = slope_ref.shape[0] // regions
    count = hot_ref.shape[0] // regions
    mesh_count = agg_grad.shape[0] // regions
    blank = jnp.zeros((count - mesh_count, agg_grad.shape[1]), BF16)
    work = [(d, first, size) for d in range(regions) for first, size in edge_blocks(edges)]

    def gathered(d, first, size):
        rows = slice(d * edges + first, d * edges + first + size)
        table = jnp.concatenate([blank, agg_grad[d * mesh_count : (d + 1) * mesh_count]], axis=0)
        return dot(turned_hot_ref[rows, :], table)

    sums = []
    upstream = gathered(*work[0])
    for n, (d, first, size) in enumerate(work):
        coming = gathered(*work[n + 1]) if n + 1 < len(work) else None
        rows = slice(d * edges + first, d * edges + first + size)
        edge_grad_ref[rows, :] = (upstream * slope_ref[rows, :].astype(F32)).astype(BF16)
        upstream = coming
        if first + size == edges:
            hot = hot_ref[d * count : (d + 1) * count, :]
            sums.append(dot(hot, edge_grad_ref[d * edges : (d + 1) * edges, :]))
    return sums


def halve(share_ref, keep_ref, give_ref):
    half = keep_ref.shape[0]
    core = lax.bitwise_and(lax.axis_index("rep"), 1)
    keep_ref[...] = share_ref[pl.ds(pl.multiple_of(core * half, half), half), :]
    give_ref[...] = share_ref[pl.ds(pl.multiple_of((1 - core) * half, half), half), :]


def process_back_kernel(steps, mesh_cap, *refs):
    regions = len(steps)
    cotangent_refs = refs[:regions]
    (
        turned_ref,
        first_ref,
        sent_ref,
        hot_ref,
        turned_hot_ref,
        hot_sent_ref,
        slope_ref,
        normed_ref,
        scaled_ref,
        mesh_grad_ref,
        keep_ref,
        give_ref,
        upstream_ref,
        slot_ref,
        recv_ref,
        share_ref,
        edge_grad_ref,
    ) = refs[regions:]
    latent = first_ref.shape[1]
    mesh_count = first_ref.shape[0] // regions
    slots = regions * mesh_cap
    me = lax.axis_index("space")
    for step, cotangent_ref in zip(steps, cotangent_refs):
        region = lax.bitwise_xor(me, step)
        at = pl.ds(pl.multiple_of(region * mesh_count, mesh_count), mesh_count)
        upstream_ref[at, :] = cotangent_ref[0].astype(F32)
    agg_grad = moments_back(normed_ref[...], scaled_ref[:, 0:1], upstream_ref[...]).astype(BF16)
    all_sums = edge_backward(
        regions, agg_grad, hot_ref, turned_hot_ref, slope_ref, edge_grad_ref
    )
    for d, sums in enumerate(all_sums):
        for s in range(regions):
            first = s * slots + d * mesh_cap
            slot_ref[first : first + mesh_cap, :] = sums[s * mesh_cap : (s + 1) * mesh_cap]
        recv_ref[d * mesh_count : (d + 1) * mesh_count, :] = sums[slots:].astype(BF16)
    slot_sum = slot_ref[...].astype(BF16)
    columns = share_ref.shape[0]
    mine = pl.ds(pl.multiple_of(me * columns, columns), columns)
    share_ref[:, :latent] = dot_first(sent_ref[:, mine], slot_sum).astype(BF16)
    share_ref[:, latent:] = dot_first(first_ref[:, mine], recv_ref[...]).astype(BF16)
    halve(share_ref, keep_ref, give_ref)
    returned = dot(slot_sum, turned_ref[:, latent : 2 * latent]).astype(BF16)
    grad = upstream_ref[...] + dot(recv_ref[...], turned_ref[:, 2 * latent :])
    for s in range(regions):
        rows = slice(s * mesh_count, (s + 1) * mesh_count)
        mesh_grad_ref[rows, :] = grad[rows] + dot(
            hot_sent_ref[rows, :], returned[s * slots : (s + 1) * slots]
        )


def encode_back_kernel(
    regions,
    grid_ref,
    mesh_ref,
    hot_ref,
    turned_hot_ref,
    slope_ref,
    normed_ref,
    scaled_ref,
    mesh_grad_ref,
    own_slot_ref,
    keep_ref,
    give_ref,
    slot_ref,
    recv_ref,
    share_ref,
    edge_grad_ref,
):
    latent = mesh_ref.shape[1]
    mesh_count = mesh_ref.shape[0] // regions
    listed = grid_ref.shape[0] // regions
    capacity = listed // 3
    me = lax.axis_index("space")
    agg_grad = moments_back(normed_ref[...], scaled_ref[:, 0:1], mesh_grad_ref[...]).astype(BF16)
    blank = jnp.zeros((capacity, latent), BF16)
    slot_ref[0:capacity, :] = blank
    slot_ref[regions * listed - capacity :, :] = blank
    all_sums = edge_backward(
        regions, agg_grad, hot_ref, turned_hot_ref, slope_ref, edge_grad_ref
    )
    for d, sums in enumerate(all_sums):
        sums = sums.astype(BF16)
        for j in range(3):
            source = d + j - 1
            if 0 <= source < regions:
                first = source * listed + (2 - j) * capacity
                slot_ref[first : first + capacity, :] = sums[j * capacity : (j + 1) * capacity]
        recv_ref[d * mesh_count : (d + 1) * mesh_count, :] = sums[listed:]
    columns = share_ref.shape[0]
    mine = pl.ds(pl.multiple_of(me * columns, columns), columns)
    share_ref[:, :latent] = dot_first(grid_ref[:, mine], slot_ref[...]).astype(BF16)
    share_ref[:, latent:] = dot_first(mesh_ref[:, mine], recv_ref[...]).astype(BF16)
    halve(share_ref, keep_ref, give_ref)
    own = pl.ds(pl.multiple_of(me * listed, listed), listed)
    own_slot_ref[...] = slot_ref[own, :]


def grid_back_kernel(turned_ref, pick_ref, own_slot_ref, grid_grad_ref):
    lists, _, capacity = pick_ref.shape
    latent = own_slot_ref.shape[1]
    returned = dot(own_slot_ref[...], turned_ref[:, :latent]).astype(BF16)
    total = None
    for i in range(lists):
        owner = one_hot(pick_ref[i], grid_grad_ref.shape[1])
        part = dot(owner, returned[i * capacity : (i + 1) * capacity])
        total = part if total is None else total + part
    grid_grad_ref[0] = total.astype(BF16)


def finish_kernel(one_ref, other_one_ref, two_ref, other_two_ref, weight_grad_ref):
    half, width = one_ref.shape
    core = lax.bitwise_and(lax.axis_index("rep"), 1)
    mine = pl.ds(pl.multiple_of(core * half, half), half)
    other = pl.ds(pl.multiple_of((1 - core) * half, half), half)
    weight_grad_ref[mine, :width] = one_ref[...].astype(F32)
    weight_grad_ref[other, :width] = other_one_ref[...].astype(F32)
    weight_grad_ref[mine, width:] = two_ref[...].astype(F32)
    weight_grad_ref[other, width:] = other_two_ref[...].astype(F32)


VMEM = pl.BlockSpec(memory_space=pltpu.VMEM)


def call(kernel, operands, outputs, scratch, flops, fetched=0, megabytes=40):
    hbm = pl.BlockSpec(memory_space=pltpu.HBM)
    return pl.pallas_call(
        kernel,
        out_shape=[jax.ShapeDtypeStruct(shape, kind) for shape, kind in outputs],
        in_specs=[hbm] * fetched + [VMEM] * (len(operands) - fetched),
        out_specs=[VMEM] * len(outputs),
        scratch_shapes=[pltpu.VMEM(shape, kind) for shape, kind in scratch]
        + ([pltpu.SemaphoreType.DMA((fetched,))] if fetched else []),
        compiler_params=pltpu.CompilerParams(vmem_limit_bytes=megabytes << 20),
        cost_estimate=pl.CostEstimate(flops=flops, bytes_accessed=4 << 20, transcendentals=0),
    )(*operands)


def swap(block, axis, bits):
    return lax.ppermute(block, axis, [(i, i ^ bits) for i in range(lax.axis_size(axis))])


def added(left, right):
    return (left.astype(F32) + right.astype(F32)).astype(BF16)


def summed_half(keep, give):
    half = added(keep, swap(give, "rep", 1))
    bit = 2
    while bit < lax.axis_size("rep"):
        half = added(half, swap(half, "rep", bit))
        bit *= 2
    return half, swap(half, "rep", 1)


def whole_sample_body(
    grid_latent,
    mesh_latent,
    mesh_cotangent,
    weights,
    g2m_pick,
    g2m_sender,
    g2m_receiver,
    m2m_pick,
    m2m_sender,
    m2m_receiver,
):
    regions = lax.axis_size("space")
    latent = weights.shape[0]
    listed = g2m_pick.shape[1] * g2m_pick.shape[2]
    mesh_count = mesh_latent.shape[1]
    mesh_cap = m2m_pick.shape[2]
    edges = g2m_sender.shape[0]
    columns = latent // regions
    half = columns // 2
    g2m_pick = g2m_pick.transpose(1, 0, 2)
    sources = (
        grid_latent,
        g2m_pick,
        g2m_sender.reshape(1, -1),
        g2m_receiver.reshape(1, -1),
        m2m_pick,
        m2m_sender.reshape(1, -1),
        m2m_receiver.reshape(1, -1),
    )
    (listed_rows,) = call(
        pack_kernel,
        sources,
        [((listed + INDEX_ROWS, latent), BF16)],
        [((INDEX_ROWS, latent), F32)] + [(source.shape, source.dtype) for source in sources],
        10**7,
        fetched=len(sources),
        megabytes=56,
    )
    steps = (0, *range(2, regions), 1)
    latents = [mesh_latent] + [swap(mesh_latent, "space", step) for step in steps[1:]]
    *latents[1:], weights = lax.optimization_barrier((*latents[1:], weights))
    weights, turned = call(
        weights_kernel,
        (weights,),
        [(weights.shape, BF16), ((latent, 3 * latent), BF16)],
        [],
        10**8,
        fetched=1,
    )
    turned, cotangent = lax.optimization_barrier((turned, mesh_cotangent))
    packs = [listed_rows, mesh_latent]
    for step, latent_block in zip(steps[1:], latents[1:]):
        packs += [swap(listed_rows, "space", step), latent_block]
    cotangents = [cotangent] + [swap(cotangent, "space", step) for step in steps[1:]]
    rows = regions * mesh_count
    slots = regions * mesh_cap
    (
        mesh_out,
        grid_all,
        mesh_all,
        mesh_first,
        mesh_sent,
        hot_one,
        hot_two,
        turned_one,
        turned_two,
        hot_sent,
        slope_one,
        slope_two,
        normed_one,
        scaled_one,
        normed_two,
        scaled_two,
    ) = call(
        functools.partial(forward_kernel, steps, listed, mesh_count, mesh_cap),
        (*packs, weights),
        [
            (mesh_latent.shape, BF16),
            ((regions * listed, latent), BF16),
            ((rows, latent), BF16),
            ((rows, latent), BF16),
            ((regions * slots, latent), BF16),
            ((regions * (listed + mesh_count), edges), BF16),
            ((regions * (slots + mesh_count), edges), BF16),
            ((regions * edges, listed + mesh_count), BF16),
            ((regions * edges, slots + mesh_count), BF16),
            ((rows, slots), BF16),
            ((regions * edges, latent), BF16),
            ((regions * edges, latent), BF16),
            ((rows, latent), F32),
            ((rows, 128), F32),
            ((rows, latent), F32),
            ((rows, 128), F32),
        ],
        [
            ((regions * INDEX_ROWS, latent), F32),
            ((regions * edges, latent), BF16),
            ((rows, latent), F32),
        ],
        2 * 10**9,
    )
    mesh_grad, keep_two, give_two = call(
        functools.partial(process_back_kernel, steps, mesh_cap),
        (
            *cotangents,
            turned,
            mesh_first,
            mesh_sent,
            hot_two,
            turned_two,
            hot_sent,
            slope_two,
            normed_two,
            scaled_two,
        ),
        [((rows, latent), F32)] + [((half, 2 * latent), BF16)] * 2,
        [
            ((rows, latent), F32),
            ((regions * slots, latent), F32),
            ((rows, latent), BF16),
            ((columns, 2 * latent), BF16),
            ((regions * edges, latent), BF16),
        ],
        10**9,
    )
    own_slots, keep_one, give_one = call(
        functools.partial(encode_back_kernel, regions),
        (
            grid_all,
            mesh_all,
            hot_one,
            turned_one,
            slope_one,
            normed_one,
            scaled_one,
            mesh_grad,
        ),
        [((listed, latent), BF16)] + [((half, 2 * latent), BF16)] * 2,
        [
            ((regions * listed, latent), BF16),
            ((rows, latent), BF16),
            ((columns, 2 * latent), BF16),
            ((regions * edges, latent), BF16),
        ],
        10**9,
    )
    grid_grad = call(
        grid_back_kernel,
        (turned, g2m_pick, own_slots),
        [(grid_latent.shape, BF16)],
        [],
        10**8,
    )[0]
    weight_grad = call(
        finish_kernel,
        (*summed_half(keep_one, give_one), *summed_half(keep_two, give_two)),
        [((columns, 4 * latent), F32)],
        [],
        10**6,
    )[0]
    return (mesh_out, grid_grad, weight_grad)


def solution(mesh):
    regions = mesh.shape["space"]
    samples = mesh.shape["rep"]

    def whole(*arguments):
        edges = arguments[5].shape[0] + arguments[8].shape[0]
        latent = arguments[3].shape[0]
        fits = edges * latent * 4 <= SAMPLE_EDGE_BYTES and latent % (128 * regions) == 0
        paired = all(n > 1 and n & (n - 1) == 0 for n in (regions, samples))
        return sharded(whole_sample_body if fits and paired else partitioned_body)(*arguments)

    def sharded(body):
        return jax.shard_map(
            body,
            mesh=mesh,
            in_specs=(
                P(("groups", "rep"), "space", None),
                P(("groups", "rep"), "space", None),
                P(("groups", "rep"), "space", None),
                P(),
                P("space", None, None),
                P("space"),
                P("space"),
                P("space", None, None),
                P("space"),
                P("space"),
            ),
            out_specs=(
                P(("groups", "rep"), "space", None),
                P(("groups", "rep"), "space", None),
                P(("groups", "space"), None),
            ),
            check_vma=False,
        )

    return whole
```

```python
import functools

import jax
import jax.numpy as jnp
from jax import lax
from jax.experimental import pallas as pl
from jax.experimental.pallas import tpu as pltpu
from jax.sharding import PartitionSpec as P

EPSILON = 1e-05


def with_halo(cells, sides, width):
    for axis, dim in sides:
        count = lax.axis_size(axis)
        ends = count - 1
        head = lax.slice_in_dim(cells, 0, width, axis=dim)
        tail = lax.slice_in_dim(cells, cells.shape[dim] - width, cells.shape[dim], axis=dim)
        cells = jnp.concatenate(
            [
                lax.ppermute(tail, axis, [(i, (i + 1) % count) for i in range(ends)]),
                cells,
                lax.ppermute(head, axis, [((i + 1) % count, i) for i in range(ends)]),
            ],
            axis=dim,
        )
    return cells


def swish(values):
    return values * jax.nn.sigmoid(values)


def swish_slope(values):
    squash = jax.nn.sigmoid(values)
    return squash * (1.0 + values * (1.0 - squash))


def norm_rows(values):
    centred = values - jnp.mean(values, -1, keepdims=True)
    return centred * lax.rsqrt(jnp.mean(centred * centred, -1, keepdims=True) + EPSILON)


def norm_rows_back(values, upstream):
    centred = values - jnp.mean(values, -1, keepdims=True)
    scaled = lax.rsqrt(jnp.mean(centred * centred, -1, keepdims=True) + EPSILON)
    normed = centred * scaled
    return scaled * (
        upstream
        - jnp.mean(upstream, -1, keepdims=True)
        - normed * jnp.mean(upstream * normed, -1, keepdims=True)
    )


def slot_rows(pick_row):
    listed = pick_row.reshape(-1)
    return listed


def mesh_route(outgoing, capacity, peer_count):
    columns = outgoing.shape[1]
    pieces = lax.all_to_all(
        outgoing.reshape(peer_count, capacity, columns),
        "space",
        split_axis=0,
        concat_axis=0,
        tiled=True,
    )
    arrived = pieces.reshape(peer_count * capacity, columns)
    return arrived


def grid_route(outgoing, capacity):
    columns = outgoing.shape[1]
    lists = outgoing.reshape(3, capacity, columns)
    rims = with_halo(jnp.stack([lists[0], lists[2]]), (("space", 0),), 1)
    return jnp.concatenate([rims[0], lists[1], rims[3]], axis=0)


def edge_pass(arrived, recv_table, located, receiver, w_send, w_recv):
    recv_proj = jnp.dot(recv_table, w_recv, preferred_element_type=jnp.float32)
    slot_proj = jnp.dot(arrived, w_send, preferred_element_type=jnp.float32)
    activation = slot_proj[located] + recv_proj[receiver]
    message = swish(activation).astype(jnp.bfloat16)
    member = (
        receiver[None, :] == jnp.arange(recv_table.shape[0], dtype=jnp.int32)[:, None]
    ).astype(jnp.bfloat16)
    summed = jnp.dot(member, message, preferred_element_type=jnp.float32)
    return (activation, member, summed)


def backward_pass(slot_count, located, activation, member, receiver, agg_grad, w_send):
    edge_grad = (agg_grad[receiver] * swish_slope(activation)).astype(jnp.bfloat16)
    recv_sum = jnp.dot(member, edge_grad, preferred_element_type=jnp.float32).astype(jnp.bfloat16)
    slot_member = (located[None, :] == jnp.arange(slot_count, dtype=jnp.int32)[:, None]).astype(
        jnp.bfloat16
    )
    slot_sum = jnp.dot(slot_member, edge_grad, preferred_element_type=jnp.float32).astype(
        jnp.bfloat16
    )
    returned = jnp.dot(slot_sum, w_send.T, preferred_element_type=jnp.float32).astype(jnp.bfloat16)
    return (recv_sum, slot_sum, returned)


def gather_back(listed, back_rows, row_count):
    owner = (listed[None, :] == jnp.arange(row_count, dtype=jnp.int32)[:, None]).astype(
        jnp.bfloat16
    )
    return jnp.dot(owner, back_rows, preferred_element_type=jnp.float32)


def partitioned_body(
    grid_latent,
    mesh_latent,
    mesh_cotangent,
    weights,
    g2m_pick,
    g2m_sender,
    g2m_receiver,
    m2m_pick,
    m2m_sender,
    m2m_receiver,
):
    grid_rows = grid_latent[0]
    mesh_rows = mesh_latent[0]
    upstream = mesh_cotangent[0].astype(jnp.float32)
    latent = weights.shape[0]
    encode_sender = weights[:, :latent]
    encode_receiver = weights[:, latent : 2 * latent]
    process_sender = weights[:, 2 * latent : 3 * latent]
    process_receiver = weights[:, 3 * latent :]
    peer_count = lax.axis_size("space")
    grid_cap = g2m_pick.shape[2]
    mesh_cap = m2m_pick.shape[2]
    grid_listed = g2m_pick[0].reshape(-1)
    grid_arrived = grid_route(grid_rows[grid_listed], grid_cap)
    act_first, member_first, summed_first = edge_pass(
        grid_arrived, mesh_rows, g2m_sender, g2m_receiver, encode_sender, encode_receiver
    )
    mesh_first = (mesh_rows.astype(jnp.float32) + norm_rows(summed_first)).astype(jnp.bfloat16)
    mesh_listed = slot_rows(m2m_pick[0])
    mesh_arrived = mesh_route(mesh_first[mesh_listed], mesh_cap, peer_count)
    act_second, member_second, summed_second = edge_pass(
        mesh_arrived, mesh_first, m2m_sender, m2m_receiver, process_sender, process_receiver
    )
    mesh_final = (mesh_first.astype(jnp.float32) + norm_rows(summed_second)).astype(jnp.bfloat16)
    agg_second = norm_rows_back(summed_second, upstream)
    recv_second, slot_second, returned_second = backward_pass(
        mesh_arrived.shape[0],
        m2m_sender,
        act_second,
        member_second,
        m2m_receiver,
        agg_second,
        process_sender,
    )
    back_second = mesh_route(returned_second, mesh_cap, peer_count)
    mesh_grad = upstream + jnp.dot(
        recv_second, process_receiver.T, preferred_element_type=jnp.float32
    )
    mesh_grad = mesh_grad + gather_back(mesh_listed, back_second, mesh_rows.shape[0])
    agg_first = norm_rows_back(summed_first, mesh_grad)
    recv_first, slot_first, returned_first = backward_pass(
        grid_arrived.shape[0],
        g2m_sender,
        act_first,
        member_first,
        g2m_receiver,
        agg_first,
        encode_sender,
    )
    back_first = grid_route(returned_first, grid_cap)
    grid_grad = gather_back(grid_listed, back_first, grid_rows.shape[0]).astype(jnp.bfloat16)
    factor_pairs = (
        (grid_arrived, slot_first),
        (mesh_rows, recv_first),
        (mesh_arrived, slot_second),
        (mesh_first, recv_second),
    )
    blocks = []
    for first_factor, second_factor in factor_pairs:
        blocks.append(
            lax.dot_general(
                first_factor,
                second_factor,
                (((0,), (0,)), ((), ())),
                preferred_element_type=jnp.float32,
            )
        )
    shares = lax.psum_scatter(
        jnp.concatenate(blocks, axis=1).astype(jnp.bfloat16),
        "space",
        scatter_dimension=0,
        tiled=True,
    )
    weight_grad = lax.psum(shares, "rep").astype(jnp.float32)
    return (mesh_final[None], grid_grad[None], weight_grad)


F32 = jnp.float32
BF16 = jnp.bfloat16
INDEX_ROWS = 8
SAMPLE_EDGE_BYTES = 8 << 20


def dot(left, right):
    return jnp.dot(left, right, preferred_element_type=F32)


def dot_first(left, right):
    return lax.dot_general(left, right, (((0,), (0,)), ((), ())), preferred_element_type=F32)


def dot_last(left, right):
    return lax.dot_general(left, right, (((1,), (1,)), ((), ())), preferred_element_type=F32)


def one_hot(labels, count):
    rows = lax.broadcasted_iota(jnp.int32, (count, labels.shape[-1]), 0)
    return (rows == labels).astype(F32).astype(BF16)


def row_moments(values):
    centred = values - jnp.mean(values, -1, keepdims=True)
    return centred, lax.rsqrt(jnp.mean(centred * centred, -1, keepdims=True) + EPSILON)


def moments_back(normed, scaled, upstream):
    return scaled * (
        upstream
        - jnp.mean(upstream, -1, keepdims=True)
        - normed * jnp.mean(upstream * normed, -1, keepdims=True)
    )


def fetch(pairs, semaphores):
    copies = [
        pltpu.make_async_copy(source, target, semaphores.at[n])
        for n, (source, target) in enumerate(pairs)
    ]
    for copy in copies:
        copy.start()
    for copy in copies:
        copy.wait()


def pack_kernel(*refs):
    *sources, weights_source_ref, packed_ref, weights_ref, index_ref = refs[:11]
    local, semaphores = refs[11:18], refs[18]
    weights_copy = pltpu.make_async_copy(weights_source_ref, weights_ref, semaphores.at[7])
    weights_copy.start()
    fetch(list(zip(sources, local)), semaphores)
    (
        grid_ref,
        g2m_pick_ref,
        g2m_sender_ref,
        g2m_receiver_ref,
        m2m_pick_ref,
        m2m_sender_ref,
        m2m_receiver_ref,
    ) = local
    lists, _, capacity = g2m_pick_ref.shape
    regions, mesh_cap = m2m_pick_ref.shape[1:]
    edges = g2m_sender_ref.shape[1]
    grid_rows = grid_ref[0]
    for i in range(lists):
        picked = one_hot(g2m_pick_ref[i], grid_rows.shape[0])
        packed_ref[i * capacity : (i + 1) * capacity, :] = dot_first(picked, grid_rows).astype(BF16)
    first = lists * capacity
    index_ref[...] = jnp.zeros_like(index_ref)
    index_ref[0:1, 0:edges] = g2m_sender_ref[...].astype(F32)
    index_ref[0:1, edges : 2 * edges] = g2m_receiver_ref[...].astype(F32)
    index_ref[1:2, 0:edges] = m2m_sender_ref[...].astype(F32)
    index_ref[1:2, edges : 2 * edges] = m2m_receiver_ref[...].astype(F32)
    slots = regions * mesh_cap
    lane = lax.broadcasted_iota(jnp.int32, (mesh_cap, slots), 1)
    spread = (lane % mesh_cap == lax.broadcasted_iota(jnp.int32, (mesh_cap, slots), 0)).astype(F32)
    spread = dot(m2m_pick_ref[0].astype(F32).astype(BF16), spread.astype(BF16))
    lane = lax.broadcasted_iota(jnp.int32, (regions, slots), 1)
    owned = lane // mesh_cap == lax.broadcasted_iota(jnp.int32, (regions, slots), 0)
    index_ref[2:3, 0:slots] = jnp.sum(jnp.where(owned, spread, 0.0), 0, keepdims=True)
    packed_ref[first:, :] = index_ref[...].astype(BF16)
    weights_copy.wait()


def edge_blocks(edges):
    size = min(edges, 128)
    return [(first, min(size, edges - first)) for first in range(0, edges, size)]


def edge_forward(tables, hot_ref, turned_hot_ref, slope_ref, message_ref, mesh_count):
    regions = len(tables)
    edges = slope_ref.shape[0] // regions
    count = hot_ref.shape[0] // regions
    work = [(d, first, size) for d in range(regions) for first, size in edge_blocks(edges)]

    def gathered(d, first, size):
        rows = slice(d * edges + first, d * edges + first + size)
        return dot(turned_hot_ref[rows, :], tables[d])

    sums = []
    activation = gathered(*work[0])
    for n, (d, first, size) in enumerate(work):
        coming = gathered(*work[n + 1]) if n + 1 < len(work) else None
        squash = 0.5 + 0.5 * jnp.tanh(0.5 * activation)
        message = activation * squash
        rows = slice(d * edges + first, d * edges + first + size)
        slope_ref[rows, :] = (squash + message * (1.0 - squash)).astype(BF16)
        message_ref[rows, :] = message.astype(BF16)
        activation = coming
        if first + size == edges:
            hot = hot_ref[(d + 1) * count - mesh_count : (d + 1) * count, :]
            sums.append(dot(hot, message_ref[d * edges : (d + 1) * edges, :]))
    return sums


def forward_kernel(
    steps,
    listed,
    mesh_count,
    mesh_cap,
    *refs,
):
    regions = len(steps)
    blocks = []
    for step in steps:
        taken = 2
        blocks.append((step, refs[:taken]))
        refs = refs[taken:]
    (
        weights_ref,
        mesh_out_ref,
        grid_ref,
        mesh_ref,
        first_ref,
        sent_ref,
        hot_one_ref,
        hot_two_ref,
        turned_one_ref,
        turned_two_ref,
        hot_sent_ref,
        slope_one_ref,
        slope_two_ref,
        normed_one_ref,
        scaled_one_ref,
        normed_two_ref,
        scaled_two_ref,
        index_ref,
        message_ref,
        sum_ref,
    ) = refs
    latent = weights_ref.shape[0]
    edges = slope_one_ref.shape[0] // regions
    capacity = listed // 3
    slots = regions * mesh_cap
    me = lax.axis_index("space")
    for step, block_refs in blocks:
        region = lax.bitwise_xor(me, step)
        at = lambda rows: pl.ds(pl.multiple_of(region * rows, rows), rows)
        listed_ref, latent_ref = block_refs
        mesh_ref[at(mesh_count), :] = latent_ref[0]
        grid_ref[at(listed), :] = listed_ref[:listed, :]
        index_ref[at(INDEX_ROWS), :] = listed_ref[listed:, :].astype(F32)

    grid_proj = dot(grid_ref[...], weights_ref[:, :latent])
    mesh_proj = dot(mesh_ref[...], weights_ref[:, latent : 2 * latent])
    for d in range(regions):
        index = index_ref[d * INDEX_ROWS : (d + 1) * INDEX_ROWS, :].astype(jnp.int32)
        for row, senders, hot_ref, turned_ref in (
            (0, listed, hot_one_ref, turned_one_ref),
            (1, slots, hot_two_ref, turned_two_ref),
        ):
            count = senders + mesh_count
            hot = jnp.concatenate(
                [
                    one_hot(index[row : row + 1, :edges], senders),
                    one_hot(index[row : row + 1, edges:], mesh_count),
                ],
                axis=0,
            )
            hot_ref[d * count : (d + 1) * count, :] = hot
            turned_ref[d * edges : (d + 1) * edges, :] = hot.T
        hot_sent_ref[d * mesh_count : (d + 1) * mesh_count, :] = one_hot(
            index[2:3, :slots], mesh_count
        )

    blank = jnp.zeros((capacity, latent), F32)
    tables = []
    for d in range(regions):
        before = (d - 1) * listed + 2 * capacity
        within = d * listed + capacity
        after = (d + 1) * listed
        tables.append(
            jnp.concatenate(
                [
                    grid_proj[before : before + capacity] if d > 0 else blank,
                    grid_proj[within : within + capacity],
                    grid_proj[after : after + capacity] if d < regions - 1 else blank,
                    mesh_proj[d * mesh_count : (d + 1) * mesh_count],
                ],
                axis=0,
            ).astype(BF16)
        )
    sums = edge_forward(
        tables, hot_one_ref, turned_one_ref, slope_one_ref, message_ref, mesh_count
    )
    for d in range(regions):
        sum_ref[d * mesh_count : (d + 1) * mesh_count, :] = sums[d]
    centred, scaled = row_moments(sum_ref[...])
    normed = centred * scaled
    normed_one_ref[...] = normed
    scaled_one_ref[...] = jnp.broadcast_to(scaled, scaled_one_ref.shape)
    first_ref[...] = (mesh_ref[...].astype(F32) + normed).astype(BF16)

    for s in range(regions):
        rows = slice(s * mesh_count, (s + 1) * mesh_count)
        sent_ref[s * slots : (s + 1) * slots, :] = dot_first(
            hot_sent_ref[rows, :], first_ref[rows, :]
        ).astype(BF16)
    sent_proj = dot(sent_ref[...], weights_ref[:, 2 * latent : 3 * latent])
    first_proj = dot(first_ref[...], weights_ref[:, 3 * latent :])
    tables = []
    for d in range(regions):
        pieces = [
            sent_proj[s * slots + d * mesh_cap : s * slots + (d + 1) * mesh_cap]
            for s in range(regions)
        ]
        tables.append(
            jnp.concatenate(
                pieces + [first_proj[d * mesh_count : (d + 1) * mesh_count]], axis=0
            ).astype(BF16)
        )
    sums = edge_forward(
        tables, hot_two_ref, turned_two_ref, slope_two_ref, message_ref, mesh_count
    )
    for d in range(regions):
        sum_ref[d * mesh_count : (d + 1) * mesh_count, :] = sums[d]
    centred, scaled = row_moments(sum_ref[...])
    normed_two_ref[...] = centred * scaled
    scaled_two_ref[...] = jnp.broadcast_to(scaled, scaled_two_ref.shape)
    own = pl.ds(pl.multiple_of(me * mesh_count, mesh_count), mesh_count)
    mesh_out_ref[0] = (first_ref[own, :].astype(F32) + normed_two_ref[own, :]).astype(BF16)


def edge_backward(regions, agg_grad, hot_ref, turned_hot_ref, slope_ref, edge_grad_ref):
    edges = slope_ref.shape[0] // regions
    count = hot_ref.shape[0] // regions
    mesh_count = agg_grad.shape[0] // regions
    blank = jnp.zeros((count - mesh_count, agg_grad.shape[1]), BF16)
    work = [(d, first, size) for d in range(regions) for first, size in edge_blocks(edges)]

    def gathered(d, first, size):
        rows = slice(d * edges + first, d * edges + first + size)
        table = jnp.concatenate([blank, agg_grad[d * mesh_count : (d + 1) * mesh_count]], axis=0)
        return dot(turned_hot_ref[rows, :], table)

    sums = []
    upstream = gathered(*work[0])
    for n, (d, first, size) in enumerate(work):
        coming = gathered(*work[n + 1]) if n + 1 < len(work) else None
        rows = slice(d * edges + first, d * edges + first + size)
        edge_grad_ref[rows, :] = (upstream * slope_ref[rows, :].astype(F32)).astype(BF16)
        upstream = coming
        if first + size == edges:
            hot = hot_ref[d * count : (d + 1) * count, :]
            sums.append(dot(hot, edge_grad_ref[d * edges : (d + 1) * edges, :]))
    return sums


def halve(share_ref, keep_ref, give_ref):
    half = keep_ref.shape[0]
    core = lax.bitwise_and(lax.axis_index("rep"), 1)
    keep_ref[...] = share_ref[pl.ds(pl.multiple_of(core * half, half), half), :]
    give_ref[...] = share_ref[pl.ds(pl.multiple_of((1 - core) * half, half), half), :]


def process_back_kernel(steps, mesh_cap, *refs):
    regions = len(steps)
    cotangent_refs = refs[:regions]
    (
        weights_ref,
        first_ref,
        sent_ref,
        hot_ref,
        turned_hot_ref,
        hot_sent_ref,
        slope_ref,
        normed_ref,
        scaled_ref,
        mesh_grad_ref,
        keep_ref,
        give_ref,
        upstream_ref,
        slot_ref,
        recv_ref,
        share_ref,
        edge_grad_ref,
    ) = refs[regions:]
    latent = first_ref.shape[1]
    mesh_count = first_ref.shape[0] // regions
    slots = regions * mesh_cap
    me = lax.axis_index("space")
    for step, cotangent_ref in zip(steps, cotangent_refs):
        region = lax.bitwise_xor(me, step)
        at = pl.ds(pl.multiple_of(region * mesh_count, mesh_count), mesh_count)
        upstream_ref[at, :] = cotangent_ref[0].astype(F32)
    agg_grad = moments_back(normed_ref[...], scaled_ref[:, 0:1], upstream_ref[...]).astype(BF16)
    all_sums = edge_backward(
        regions, agg_grad, hot_ref, turned_hot_ref, slope_ref, edge_grad_ref
    )
    for d, sums in enumerate(all_sums):
        for s in range(regions):
            first = s * slots + d * mesh_cap
            slot_ref[first : first + mesh_cap, :] = sums[s * mesh_cap : (s + 1) * mesh_cap]
        recv_ref[d * mesh_count : (d + 1) * mesh_count, :] = sums[slots:].astype(BF16)
    slot_sum = slot_ref[...].astype(BF16)
    columns = share_ref.shape[0]
    mine = pl.ds(pl.multiple_of(me * columns, columns), columns)
    share_ref[:, :latent] = dot_first(sent_ref[:, mine], slot_sum).astype(BF16)
    share_ref[:, latent:] = dot_first(first_ref[:, mine], recv_ref[...]).astype(BF16)
    halve(share_ref, keep_ref, give_ref)
    returned = dot_last(slot_sum, weights_ref[:, 2 * latent : 3 * latent]).astype(BF16)
    grad = upstream_ref[...] + dot_last(recv_ref[...], weights_ref[:, 3 * latent :])
    for s in range(regions):
        rows = slice(s * mesh_count, (s + 1) * mesh_count)
        mesh_grad_ref[rows, :] = grad[rows] + dot(
            hot_sent_ref[rows, :], returned[s * slots : (s + 1) * slots]
        )


def encode_back_kernel(
    regions,
    grid_ref,
    mesh_ref,
    hot_ref,
    turned_hot_ref,
    slope_ref,
    normed_ref,
    scaled_ref,
    mesh_grad_ref,
    own_slot_ref,
    keep_ref,
    give_ref,
    slot_ref,
    recv_ref,
    share_ref,
    edge_grad_ref,
):
    latent = mesh_ref.shape[1]
    mesh_count = mesh_ref.shape[0] // regions
    listed = grid_ref.shape[0] // regions
    capacity = listed // 3
    me = lax.axis_index("space")
    agg_grad = moments_back(normed_ref[...], scaled_ref[:, 0:1], mesh_grad_ref[...]).astype(BF16)
    blank = jnp.zeros((capacity, latent), BF16)
    slot_ref[0:capacity, :] = blank
    slot_ref[regions * listed - capacity :, :] = blank
    all_sums = edge_backward(
        regions, agg_grad, hot_ref, turned_hot_ref, slope_ref, edge_grad_ref
    )
    for d, sums in enumerate(all_sums):
        sums = sums.astype(BF16)
        for j in range(3):
            source = d + j - 1
            if 0 <= source < regions:
                first = source * listed + (2 - j) * capacity
                slot_ref[first : first + capacity, :] = sums[j * capacity : (j + 1) * capacity]
        recv_ref[d * mesh_count : (d + 1) * mesh_count, :] = sums[listed:]
    columns = share_ref.shape[0]
    mine = pl.ds(pl.multiple_of(me * columns, columns), columns)
    share_ref[:, :latent] = dot_first(grid_ref[:, mine], slot_ref[...]).astype(BF16)
    share_ref[:, latent:] = dot_first(mesh_ref[:, mine], recv_ref[...]).astype(BF16)
    halve(share_ref, keep_ref, give_ref)
    own = pl.ds(pl.multiple_of(me * listed, listed), listed)
    own_slot_ref[...] = slot_ref[own, :]


def grid_back_kernel(weights_ref, pick_ref, own_slot_ref, grid_grad_ref):
    lists, _, capacity = pick_ref.shape
    latent = own_slot_ref.shape[1]
    returned = dot_last(own_slot_ref[...], weights_ref[:, :latent]).astype(BF16)
    total = None
    for i in range(lists):
        owner = one_hot(pick_ref[i], grid_grad_ref.shape[1])
        part = dot(owner, returned[i * capacity : (i + 1) * capacity])
        total = part if total is None else total + part
    grid_grad_ref[0] = total.astype(BF16)


def finish_kernel(one_ref, other_one_ref, two_ref, other_two_ref, weight_grad_ref):
    half, width = one_ref.shape
    core = lax.bitwise_and(lax.axis_index("rep"), 1)
    mine = pl.ds(pl.multiple_of(core * half, half), half)
    other = pl.ds(pl.multiple_of((1 - core) * half, half), half)
    weight_grad_ref[mine, :width] = one_ref[...].astype(F32)
    weight_grad_ref[other, :width] = other_one_ref[...].astype(F32)
    weight_grad_ref[mine, width:] = two_ref[...].astype(F32)
    weight_grad_ref[other, width:] = other_two_ref[...].astype(F32)


VMEM = pl.BlockSpec(memory_space=pltpu.VMEM)


def call(kernel, operands, outputs, scratch, flops, fetched=0):
    hbm = pl.BlockSpec(memory_space=pltpu.HBM)
    operands = [
        pltpu.with_memory_space_constraint(operand, pltpu.HBM) if n < fetched else operand
        for n, operand in enumerate(operands)
    ]
    return pl.pallas_call(
        kernel,
        out_shape=[jax.ShapeDtypeStruct(shape, kind) for shape, kind in outputs],
        in_specs=[hbm] * fetched + [VMEM] * (len(operands) - fetched),
        out_specs=[VMEM] * len(outputs),
        scratch_shapes=[pltpu.VMEM(shape, kind) for shape, kind in scratch]
        + ([pltpu.SemaphoreType.DMA((fetched,))] if fetched else []),
        compiler_params=pltpu.CompilerParams(vmem_limit_bytes=40 << 20),
        cost_estimate=pl.CostEstimate(flops=flops, bytes_accessed=4 << 20, transcendentals=0),
    )(*operands)


def swap(block, axis, bits):
    return lax.ppermute(block, axis, [(i, i ^ bits) for i in range(lax.axis_size(axis))])


def added(left, right):
    return (left.astype(F32) + right.astype(F32)).astype(BF16)


def summed_half(keep, give):
    half = added(keep, swap(give, "rep", 1))
    bit = 2
    while bit < lax.axis_size("rep"):
        half = added(half, swap(half, "rep", bit))
        bit *= 2
    return half, swap(half, "rep", 1)


def whole_sample_body(
    grid_latent,
    mesh_latent,
    mesh_cotangent,
    weights,
    g2m_pick,
    g2m_sender,
    g2m_receiver,
    m2m_pick,
    m2m_sender,
    m2m_receiver,
):
    regions = lax.axis_size("space")
    latent = weights.shape[0]
    listed = g2m_pick.shape[1] * g2m_pick.shape[2]
    mesh_count = mesh_latent.shape[1]
    mesh_cap = m2m_pick.shape[2]
    edges = g2m_sender.shape[0]
    columns = latent // regions
    half = columns // 2
    g2m_pick = g2m_pick.transpose(1, 0, 2)
    sources = (
        grid_latent,
        g2m_pick,
        g2m_sender.reshape(1, -1),
        g2m_receiver.reshape(1, -1),
        m2m_pick,
        m2m_sender.reshape(1, -1),
        m2m_receiver.reshape(1, -1),
    )
    listed_rows, weights = call(
        pack_kernel,
        (*sources, weights),
        [((listed + INDEX_ROWS, latent), BF16), (weights.shape, BF16)],
        [((INDEX_ROWS, latent), F32)] + [(source.shape, source.dtype) for source in sources],
        10**7,
        fetched=len(sources) + 1,
    )
    steps = (0, *range(2, regions), 1)
    latents = [mesh_latent] + [swap(mesh_latent, "space", step) for step in steps[1:]]
    *latents[1:], cotangent = lax.optimization_barrier((*latents[1:], mesh_cotangent))
    packs = [listed_rows, mesh_latent]
    for step, latent_block in zip(steps[1:], latents[1:]):
        packs += [swap(listed_rows, "space", step), latent_block]
    cotangents = [mesh_cotangent] + [swap(cotangent, "space", step) for step in steps[1:]]
    rows = regions * mesh_count
    slots = regions * mesh_cap
    (
        mesh_out,
        grid_all,
        mesh_all,
        mesh_first,
        mesh_sent,
        hot_one,
        hot_two,
        turned_one,
        turned_two,
        hot_sent,
        slope_one,
        slope_two,
        normed_one,
        scaled_one,
        normed_two,
        scaled_two,
    ) = call(
        functools.partial(forward_kernel, steps, listed, mesh_count, mesh_cap),
        (*packs, weights),
        [
            (mesh_latent.shape, BF16),
            ((regions * listed, latent), BF16),
            ((rows, latent), BF16),
            ((rows, latent), BF16),
            ((regions * slots, latent), BF16),
            ((regions * (listed + mesh_count), edges), BF16),
            ((regions * (slots + mesh_count), edges), BF16),
            ((regions * edges, listed + mesh_count), BF16),
            ((regions * edges, slots + mesh_count), BF16),
            ((rows, slots), BF16),
            ((regions * edges, latent), BF16),
            ((regions * edges, latent), BF16),
            ((rows, latent), F32),
            ((rows, 128), F32),
            ((rows, latent), F32),
            ((rows, 128), F32),
        ],
        [
            ((regions * INDEX_ROWS, latent), F32),
            ((regions * edges, latent), BF16),
            ((rows, latent), F32),
        ],
        2 * 10**9,
    )
    mesh_grad, keep_two, give_two = call(
        functools.partial(process_back_kernel, steps, mesh_cap),
        (
            *cotangents,
            weights,
            mesh_first,
            mesh_sent,
            hot_two,
            turned_two,
            hot_sent,
            slope_two,
            normed_two,
            scaled_two,
        ),
        [((rows, latent), F32)] + [((half, 2 * latent), BF16)] * 2,
        [
            ((rows, latent), F32),
            ((regions * slots, latent), F32),
            ((rows, latent), BF16),
            ((columns, 2 * latent), BF16),
            ((regions * edges, latent), BF16),
        ],
        10**9,
    )
    own_slots, keep_one, give_one = call(
        functools.partial(encode_back_kernel, regions),
        (
            grid_all,
            mesh_all,
            hot_one,
            turned_one,
            slope_one,
            normed_one,
            scaled_one,
            mesh_grad,
        ),
        [((listed, latent), BF16)] + [((half, 2 * latent), BF16)] * 2,
        [
            ((regions * listed, latent), BF16),
            ((rows, latent), BF16),
            ((columns, 2 * latent), BF16),
            ((regions * edges, latent), BF16),
        ],
        10**9,
    )
    grid_grad = call(
        grid_back_kernel,
        (weights, g2m_pick, own_slots),
        [(grid_latent.shape, BF16)],
        [],
        10**8,
    )[0]
    weight_grad = call(
        finish_kernel,
        (*summed_half(keep_one, give_one), *summed_half(keep_two, give_two)),
        [((columns, 4 * latent), F32)],
        [],
        10**6,
    )[0]
    return (mesh_out, grid_grad, weight_grad)


def solution(mesh):
    regions = mesh.shape["space"]
    samples = mesh.shape["rep"]

    def whole(*arguments):
        edges = arguments[5].shape[0] + arguments[8].shape[0]
        latent = arguments[3].shape[0]
        fits = edges * latent * 4 <= SAMPLE_EDGE_BYTES and latent % (128 * regions) == 0
        paired = all(n > 1 and n & (n - 1) == 0 for n in (regions, samples))
        return sharded(whole_sample_body if fits and paired else partitioned_body)(*arguments)

    def sharded(body):
        return jax.shard_map(
            body,
            mesh=mesh,
            in_specs=(
                P(("groups", "rep"), "space", None),
                P(("groups", "rep"), "space", None),
                P(("groups", "rep"), "space", None),
                P(),
                P("space", None, None),
                P("space"),
                P("space"),
                P("space", None, None),
                P("space"),
                P("space"),
            ),
            out_specs=(
                P(("groups", "rep"), "space", None),
                P(("groups", "rep"), "space", None),
                P(("groups", "space"), None),
            ),
            check_vma=False,
        )

    return whole
```

```python
import functools

import jax
import jax.numpy as jnp
from jax import lax
from jax.experimental import pallas as pl
from jax.experimental.pallas import tpu as pltpu
from jax.sharding import PartitionSpec as P

EPSILON = 1e-05


def with_halo(cells, sides, width):
    for axis, dim in sides:
        count = lax.axis_size(axis)
        ends = count - 1
        head = lax.slice_in_dim(cells, 0, width, axis=dim)
        tail = lax.slice_in_dim(cells, cells.shape[dim] - width, cells.shape[dim], axis=dim)
        cells = jnp.concatenate(
            [
                lax.ppermute(tail, axis, [(i, (i + 1) % count) for i in range(ends)]),
                cells,
                lax.ppermute(head, axis, [((i + 1) % count, i) for i in range(ends)]),
            ],
            axis=dim,
        )
    return cells


def swish(values):
    return values * jax.nn.sigmoid(values)


def swish_slope(values):
    squash = jax.nn.sigmoid(values)
    return squash * (1.0 + values * (1.0 - squash))


def norm_rows(values):
    centred = values - jnp.mean(values, -1, keepdims=True)
    return centred * lax.rsqrt(jnp.mean(centred * centred, -1, keepdims=True) + EPSILON)


def norm_rows_back(values, upstream):
    centred = values - jnp.mean(values, -1, keepdims=True)
    scaled = lax.rsqrt(jnp.mean(centred * centred, -1, keepdims=True) + EPSILON)
    normed = centred * scaled
    return scaled * (
        upstream
        - jnp.mean(upstream, -1, keepdims=True)
        - normed * jnp.mean(upstream * normed, -1, keepdims=True)
    )


def slot_rows(pick_row):
    listed = pick_row.reshape(-1)
    return listed


def mesh_route(outgoing, capacity, peer_count):
    columns = outgoing.shape[1]
    pieces = lax.all_to_all(
        outgoing.reshape(peer_count, capacity, columns),
        "space",
        split_axis=0,
        concat_axis=0,
        tiled=True,
    )
    arrived = pieces.reshape(peer_count * capacity, columns)
    return arrived


def grid_route(outgoing, capacity):
    columns = outgoing.shape[1]
    lists = outgoing.reshape(3, capacity, columns)
    rims = with_halo(jnp.stack([lists[0], lists[2]]), (("space", 0),), 1)
    return jnp.concatenate([rims[0], lists[1], rims[3]], axis=0)


def edge_pass(arrived, recv_table, located, receiver, w_send, w_recv):
    recv_proj = jnp.dot(recv_table, w_recv, preferred_element_type=jnp.float32)
    slot_proj = jnp.dot(arrived, w_send, preferred_element_type=jnp.float32)
    activation = slot_proj[located] + recv_proj[receiver]
    message = swish(activation).astype(jnp.bfloat16)
    member = (
        receiver[None, :] == jnp.arange(recv_table.shape[0], dtype=jnp.int32)[:, None]
    ).astype(jnp.bfloat16)
    summed = jnp.dot(member, message, preferred_element_type=jnp.float32)
    return (activation, member, summed)


def backward_pass(slot_count, located, activation, member, receiver, agg_grad, w_send):
    edge_grad = (agg_grad[receiver] * swish_slope(activation)).astype(jnp.bfloat16)
    recv_sum = jnp.dot(member, edge_grad, preferred_element_type=jnp.float32).astype(jnp.bfloat16)
    slot_member = (located[None, :] == jnp.arange(slot_count, dtype=jnp.int32)[:, None]).astype(
        jnp.bfloat16
    )
    slot_sum = jnp.dot(slot_member, edge_grad, preferred_element_type=jnp.float32).astype(
        jnp.bfloat16
    )
    returned = jnp.dot(slot_sum, w_send.T, preferred_element_type=jnp.float32).astype(jnp.bfloat16)
    return (recv_sum, slot_sum, returned)


def gather_back(listed, back_rows, row_count):
    owner = (listed[None, :] == jnp.arange(row_count, dtype=jnp.int32)[:, None]).astype(
        jnp.bfloat16
    )
    return jnp.dot(owner, back_rows, preferred_element_type=jnp.float32)


def partitioned_body(
    grid_latent,
    mesh_latent,
    mesh_cotangent,
    weights,
    g2m_pick,
    g2m_sender,
    g2m_receiver,
    m2m_pick,
    m2m_sender,
    m2m_receiver,
):
    grid_rows = grid_latent[0]
    mesh_rows = mesh_latent[0]
    upstream = mesh_cotangent[0].astype(jnp.float32)
    latent = weights.shape[0]
    encode_sender = weights[:, :latent]
    encode_receiver = weights[:, latent : 2 * latent]
    process_sender = weights[:, 2 * latent : 3 * latent]
    process_receiver = weights[:, 3 * latent :]
    peer_count = lax.axis_size("space")
    grid_cap = g2m_pick.shape[2]
    mesh_cap = m2m_pick.shape[2]
    grid_listed = g2m_pick[0].reshape(-1)
    grid_arrived = grid_route(grid_rows[grid_listed], grid_cap)
    act_first, member_first, summed_first = edge_pass(
        grid_arrived, mesh_rows, g2m_sender, g2m_receiver, encode_sender, encode_receiver
    )
    mesh_first = (mesh_rows.astype(jnp.float32) + norm_rows(summed_first)).astype(jnp.bfloat16)
    mesh_listed = slot_rows(m2m_pick[0])
    mesh_arrived = mesh_route(mesh_first[mesh_listed], mesh_cap, peer_count)
    act_second, member_second, summed_second = edge_pass(
        mesh_arrived, mesh_first, m2m_sender, m2m_receiver, process_sender, process_receiver
    )
    mesh_final = (mesh_first.astype(jnp.float32) + norm_rows(summed_second)).astype(jnp.bfloat16)
    agg_second = norm_rows_back(summed_second, upstream)
    recv_second, slot_second, returned_second = backward_pass(
        mesh_arrived.shape[0],
        m2m_sender,
        act_second,
        member_second,
        m2m_receiver,
        agg_second,
        process_sender,
    )
    back_second = mesh_route(returned_second, mesh_cap, peer_count)
    mesh_grad = upstream + jnp.dot(
        recv_second, process_receiver.T, preferred_element_type=jnp.float32
    )
    mesh_grad = mesh_grad + gather_back(mesh_listed, back_second, mesh_rows.shape[0])
    agg_first = norm_rows_back(summed_first, mesh_grad)
    recv_first, slot_first, returned_first = backward_pass(
        grid_arrived.shape[0],
        g2m_sender,
        act_first,
        member_first,
        g2m_receiver,
        agg_first,
        encode_sender,
    )
    back_first = grid_route(returned_first, grid_cap)
    grid_grad = gather_back(grid_listed, back_first, grid_rows.shape[0]).astype(jnp.bfloat16)
    factor_pairs = (
        (grid_arrived, slot_first),
        (mesh_rows, recv_first),
        (mesh_arrived, slot_second),
        (mesh_first, recv_second),
    )
    blocks = []
    for first_factor, second_factor in factor_pairs:
        blocks.append(
            lax.dot_general(
                first_factor,
                second_factor,
                (((0,), (0,)), ((), ())),
                preferred_element_type=jnp.float32,
            )
        )
    shares = lax.psum_scatter(
        jnp.concatenate(blocks, axis=1).astype(jnp.bfloat16),
        "space",
        scatter_dimension=0,
        tiled=True,
    )
    weight_grad = lax.psum(shares, "rep").astype(jnp.float32)
    return (mesh_final[None], grid_grad[None], weight_grad)


F32 = jnp.float32
BF16 = jnp.bfloat16
INDEX_ROWS = 8
SAMPLE_EDGE_BYTES = 8 << 20


def dot(left, right):
    return jnp.dot(left, right, preferred_element_type=F32)


def dot_first(left, right):
    return lax.dot_general(left, right, (((0,), (0,)), ((), ())), preferred_element_type=F32)


def one_hot(labels, count):
    rows = lax.broadcasted_iota(jnp.int32, (count, labels.shape[-1]), 0)
    return (rows == labels).astype(F32).astype(BF16)


def row_moments(values):
    centred = values - jnp.mean(values, -1, keepdims=True)
    return centred, lax.rsqrt(jnp.mean(centred * centred, -1, keepdims=True) + EPSILON)


def moments_back(normed, scaled, upstream):
    return scaled * (
        upstream
        - jnp.mean(upstream, -1, keepdims=True)
        - normed * jnp.mean(upstream * normed, -1, keepdims=True)
    )


def fetch(pairs, semaphores):
    copies = [
        pltpu.make_async_copy(source, target, semaphores.at[n])
        for n, (source, target) in enumerate(pairs)
    ]
    for copy in copies:
        copy.start()
    for copy in copies:
        copy.wait()


def pack_kernel(*refs):
    sources, packed_ref, index_ref = refs[:7], refs[7], refs[8]
    local, semaphores = refs[9:16], refs[16]
    fetch(list(zip(sources, local)), semaphores)
    (
        grid_ref,
        g2m_pick_ref,
        g2m_sender_ref,
        g2m_receiver_ref,
        m2m_pick_ref,
        m2m_sender_ref,
        m2m_receiver_ref,
    ) = local
    lists, _, capacity = g2m_pick_ref.shape
    regions, mesh_cap = m2m_pick_ref.shape[1:]
    edges = g2m_sender_ref.shape[1]
    grid_rows = grid_ref[0]
    for i in range(lists):
        picked = one_hot(g2m_pick_ref[i], grid_rows.shape[0])
        packed_ref[i * capacity : (i + 1) * capacity, :] = dot_first(picked, grid_rows).astype(BF16)
    first = lists * capacity
    index_ref[...] = jnp.zeros_like(index_ref)
    index_ref[0:1, 0:edges] = g2m_sender_ref[...].astype(F32)
    index_ref[0:1, edges : 2 * edges] = g2m_receiver_ref[...].astype(F32)
    index_ref[1:2, 0:edges] = m2m_sender_ref[...].astype(F32)
    index_ref[1:2, edges : 2 * edges] = m2m_receiver_ref[...].astype(F32)
    slots = regions * mesh_cap
    lane = lax.broadcasted_iota(jnp.int32, (mesh_cap, slots), 1)
    spread = (lane % mesh_cap == lax.broadcasted_iota(jnp.int32, (mesh_cap, slots), 0)).astype(F32)
    spread = dot(m2m_pick_ref[0].astype(F32).astype(BF16), spread.astype(BF16))
    lane = lax.broadcasted_iota(jnp.int32, (regions, slots), 1)
    owned = lane // mesh_cap == lax.broadcasted_iota(jnp.int32, (regions, slots), 0)
    index_ref[2:3, 0:slots] = jnp.sum(jnp.where(owned, spread, 0.0), 0, keepdims=True)
    packed_ref[first:, :] = index_ref[...].astype(BF16)


def weights_kernel(source_ref, weights_ref, turned_ref, semaphores):
    fetch([(source_ref, weights_ref)], semaphores)
    latent = weights_ref.shape[0]
    for n, block in enumerate((0, 2, 3)):
        turned_ref[:, n * latent : (n + 1) * latent] = weights_ref[
            :, block * latent : (block + 1) * latent
        ].T


def edge_blocks(edges):
    size = min(edges, 128)
    return [(first, min(size, edges - first)) for first in range(0, edges, size)]


def edge_forward(tables, hot_ref, turned_hot_ref, slope_ref, message_ref, mesh_count):
    regions = len(tables)
    edges = slope_ref.shape[0] // regions
    count = hot_ref.shape[0] // regions
    work = [(d, first, size) for d in range(regions) for first, size in edge_blocks(edges)]

    def gathered(d, first, size):
        rows = slice(d * edges + first, d * edges + first + size)
        return dot(turned_hot_ref[rows, :], tables[d])

    sums = []
    activation = gathered(*work[0])
    for n, (d, first, size) in enumerate(work):
        coming = gathered(*work[n + 1]) if n + 1 < len(work) else None
        squash = 0.5 + 0.5 * jnp.tanh(0.5 * activation)
        message = activation * squash
        rows = slice(d * edges + first, d * edges + first + size)
        slope_ref[rows, :] = (squash + message * (1.0 - squash)).astype(BF16)
        message_ref[rows, :] = message.astype(BF16)
        activation = coming
        if first + size == edges:
            hot = hot_ref[(d + 1) * count - mesh_count : (d + 1) * count, :]
            sums.append(dot(hot, message_ref[d * edges : (d + 1) * edges, :]))
    return sums


def forward_kernel(
    steps,
    listed,
    mesh_count,
    mesh_cap,
    *refs,
):
    regions = len(steps)
    blocks = []
    for step in steps:
        taken = 2
        blocks.append((step, refs[:taken]))
        refs = refs[taken:]
    (
        weights_ref,
        mesh_out_ref,
        grid_ref,
        mesh_ref,
        first_ref,
        sent_ref,
        hot_one_ref,
        hot_two_ref,
        turned_one_ref,
        turned_two_ref,
        hot_sent_ref,
        slope_one_ref,
        slope_two_ref,
        normed_one_ref,
        scaled_one_ref,
        normed_two_ref,
        scaled_two_ref,
        index_ref,
        message_ref,
        sum_ref,
    ) = refs
    latent = weights_ref.shape[0]
    edges = slope_one_ref.shape[0] // regions
    capacity = listed // 3
    slots = regions * mesh_cap
    me = lax.axis_index("space")
    for step, block_refs in blocks:
        region = lax.bitwise_xor(me, step)
        at = lambda rows: pl.ds(pl.multiple_of(region * rows, rows), rows)
        listed_ref, latent_ref = block_refs
        mesh_ref[at(mesh_count), :] = latent_ref[0]
        grid_ref[at(listed), :] = listed_ref[:listed, :]
        index_ref[at(INDEX_ROWS), :] = listed_ref[listed:, :].astype(F32)

    grid_proj = dot(grid_ref[...], weights_ref[:, :latent])
    mesh_proj = dot(mesh_ref[...], weights_ref[:, latent : 2 * latent])
    for d in range(regions):
        index = index_ref[d * INDEX_ROWS : (d + 1) * INDEX_ROWS, :].astype(jnp.int32)
        for row, senders, hot_ref, turned_ref in (
            (0, listed, hot_one_ref, turned_one_ref),
            (1, slots, hot_two_ref, turned_two_ref),
        ):
            count = senders + mesh_count
            hot = jnp.concatenate(
                [
                    one_hot(index[row : row + 1, :edges], senders),
                    one_hot(index[row : row + 1, edges:], mesh_count),
                ],
                axis=0,
            )
            hot_ref[d * count : (d + 1) * count, :] = hot
            turned_ref[d * edges : (d + 1) * edges, :] = hot.T
        hot_sent_ref[d * mesh_count : (d + 1) * mesh_count, :] = one_hot(
            index[2:3, :slots], mesh_count
        )

    blank = jnp.zeros((capacity, latent), F32)
    tables = []
    for d in range(regions):
        before = (d - 1) * listed + 2 * capacity
        within = d * listed + capacity
        after = (d + 1) * listed
        tables.append(
            jnp.concatenate(
                [
                    grid_proj[before : before + capacity] if d > 0 else blank,
                    grid_proj[within : within + capacity],
                    grid_proj[after : after + capacity] if d < regions - 1 else blank,
                    mesh_proj[d * mesh_count : (d + 1) * mesh_count],
                ],
                axis=0,
            ).astype(BF16)
        )
    sums = edge_forward(
        tables, hot_one_ref, turned_one_ref, slope_one_ref, message_ref, mesh_count
    )
    for d in range(regions):
        sum_ref[d * mesh_count : (d + 1) * mesh_count, :] = sums[d]
    centred, scaled = row_moments(sum_ref[...])
    normed = centred * scaled
    normed_one_ref[...] = normed
    scaled_one_ref[...] = jnp.broadcast_to(scaled, scaled_one_ref.shape)
    first_ref[...] = (mesh_ref[...].astype(F32) + normed).astype(BF16)

    for s in range(regions):
        rows = slice(s * mesh_count, (s + 1) * mesh_count)
        sent_ref[s * slots : (s + 1) * slots, :] = dot_first(
            hot_sent_ref[rows, :], first_ref[rows, :]
        ).astype(BF16)
    sent_proj = dot(sent_ref[...], weights_ref[:, 2 * latent : 3 * latent])
    first_proj = dot(first_ref[...], weights_ref[:, 3 * latent :])
    tables = []
    for d in range(regions):
        pieces = [
            sent_proj[s * slots + d * mesh_cap : s * slots + (d + 1) * mesh_cap]
            for s in range(regions)
        ]
        tables.append(
            jnp.concatenate(
                pieces + [first_proj[d * mesh_count : (d + 1) * mesh_count]], axis=0
            ).astype(BF16)
        )
    sums = edge_forward(
        tables, hot_two_ref, turned_two_ref, slope_two_ref, message_ref, mesh_count
    )
    for d in range(regions):
        sum_ref[d * mesh_count : (d + 1) * mesh_count, :] = sums[d]
    centred, scaled = row_moments(sum_ref[...])
    normed_two_ref[...] = centred * scaled
    scaled_two_ref[...] = jnp.broadcast_to(scaled, scaled_two_ref.shape)
    own = pl.ds(pl.multiple_of(me * mesh_count, mesh_count), mesh_count)
    mesh_out_ref[0] = (first_ref[own, :].astype(F32) + normed_two_ref[own, :]).astype(BF16)


def edge_backward(regions, agg_grad, hot_ref, turned_hot_ref, slope_ref, edge_grad_ref):
    edges = slope_ref.shape[0] // regions
    count = hot_ref.shape[0] // regions
    mesh_count = agg_grad.shape[0] // regions
    blank = jnp.zeros((count - mesh_count, agg_grad.shape[1]), BF16)
    work = [(d, first, size) for d in range(regions) for first, size in edge_blocks(edges)]

    def gathered(d, first, size):
        rows = slice(d * edges + first, d * edges + first + size)
        table = jnp.concatenate([blank, agg_grad[d * mesh_count : (d + 1) * mesh_count]], axis=0)
        return dot(turned_hot_ref[rows, :], table)

    sums = []
    upstream = gathered(*work[0])
    for n, (d, first, size) in enumerate(work):
        coming = gathered(*work[n + 1]) if n + 1 < len(work) else None
        rows = slice(d * edges + first, d * edges + first + size)
        edge_grad_ref[rows, :] = (upstream * slope_ref[rows, :].astype(F32)).astype(BF16)
        upstream = coming
        if first + size == edges:
            hot = hot_ref[d * count : (d + 1) * count, :]
            sums.append(dot(hot, edge_grad_ref[d * edges : (d + 1) * edges, :]))
    return sums


def halve(share_ref, keep_ref, give_ref):
    half = keep_ref.shape[0]
    core = lax.bitwise_and(lax.axis_index("rep"), 1)
    keep_ref[...] = share_ref[pl.ds(pl.multiple_of(core * half, half), half), :]
    give_ref[...] = share_ref[pl.ds(pl.multiple_of((1 - core) * half, half), half), :]


def process_back_kernel(steps, mesh_cap, *refs):
    regions = len(steps)
    cotangent_refs = refs[:regions]
    (
        turned_ref,
        first_ref,
        sent_ref,
        hot_ref,
        turned_hot_ref,
        hot_sent_ref,
        slope_ref,
        normed_ref,
        scaled_ref,
        mesh_grad_ref,
        keep_ref,
        give_ref,
        upstream_ref,
        slot_ref,
        recv_ref,
        share_ref,
        edge_grad_ref,
    ) = refs[regions:]
    latent = first_ref.shape[1]
    mesh_count = first_ref.shape[0] // regions
    slots = regions * mesh_cap
    me = lax.axis_index("space")
    for step, cotangent_ref in zip(steps, cotangent_refs):
        region = lax.bitwise_xor(me, step)
        at = pl.ds(pl.multiple_of(region * mesh_count, mesh_count), mesh_count)
        upstream_ref[at, :] = cotangent_ref[0].astype(F32)
    agg_grad = moments_back(normed_ref[...], scaled_ref[:, 0:1], upstream_ref[...]).astype(BF16)
    all_sums = edge_backward(
        regions, agg_grad, hot_ref, turned_hot_ref, slope_ref, edge_grad_ref
    )
    for d, sums in enumerate(all_sums):
        for s in range(regions):
            first = s * slots + d * mesh_cap
            slot_ref[first : first + mesh_cap, :] = sums[s * mesh_cap : (s + 1) * mesh_cap]
        recv_ref[d * mesh_count : (d + 1) * mesh_count, :] = sums[slots:].astype(BF16)
    slot_sum = slot_ref[...].astype(BF16)
    columns = share_ref.shape[0]
    mine = pl.ds(pl.multiple_of(me * columns, columns), columns)
    share_ref[:, :latent] = dot_first(sent_ref[:, mine], slot_sum).astype(BF16)
    share_ref[:, latent:] = dot_first(first_ref[:, mine], recv_ref[...]).astype(BF16)
    halve(share_ref, keep_ref, give_ref)
    returned = dot(slot_sum, turned_ref[:, latent : 2 * latent]).astype(BF16)
    grad = upstream_ref[...] + dot(recv_ref[...], turned_ref[:, 2 * latent :])
    for s in range(regions):
        rows = slice(s * mesh_count, (s + 1) * mesh_count)
        mesh_grad_ref[rows, :] = grad[rows] + dot(
            hot_sent_ref[rows, :], returned[s * slots : (s + 1) * slots]
        )


def encode_back_kernel(
    regions,
    grid_ref,
    mesh_ref,
    hot_ref,
    turned_hot_ref,
    slope_ref,
    normed_ref,
    scaled_ref,
    mesh_grad_ref,
    own_slot_ref,
    keep_ref,
    give_ref,
    slot_ref,
    recv_ref,
    share_ref,
    edge_grad_ref,
):
    latent = mesh_ref.shape[1]
    mesh_count = mesh_ref.shape[0] // regions
    listed = grid_ref.shape[0] // regions
    capacity = listed // 3
    me = lax.axis_index("space")
    agg_grad = moments_back(normed_ref[...], scaled_ref[:, 0:1], mesh_grad_ref[...]).astype(BF16)
    blank = jnp.zeros((capacity, latent), BF16)
    slot_ref[0:capacity, :] = blank
    slot_ref[regions * listed - capacity :, :] = blank
    all_sums = edge_backward(
        regions, agg_grad, hot_ref, turned_hot_ref, slope_ref, edge_grad_ref
    )
    for d, sums in enumerate(all_sums):
        sums = sums.astype(BF16)
        for j in range(3):
            source = d + j - 1
            if 0 <= source < regions:
                first = source * listed + (2 - j) * capacity
                slot_ref[first : first + capacity, :] = sums[j * capacity : (j + 1) * capacity]
        recv_ref[d * mesh_count : (d + 1) * mesh_count, :] = sums[listed:]
    columns = share_ref.shape[0]
    mine = pl.ds(pl.multiple_of(me * columns, columns), columns)
    share_ref[:, :latent] = dot_first(grid_ref[:, mine], slot_ref[...]).astype(BF16)
    share_ref[:, latent:] = dot_first(mesh_ref[:, mine], recv_ref[...]).astype(BF16)
    halve(share_ref, keep_ref, give_ref)
    own = pl.ds(pl.multiple_of(me * listed, listed), listed)
    own_slot_ref[...] = slot_ref[own, :]


def grid_back_kernel(turned_ref, pick_ref, own_slot_ref, grid_grad_ref):
    lists, _, capacity = pick_ref.shape
    latent = own_slot_ref.shape[1]
    returned = dot(own_slot_ref[...], turned_ref[:, :latent]).astype(BF16)
    total = None
    for i in range(lists):
        owner = one_hot(pick_ref[i], grid_grad_ref.shape[1])
        part = dot(owner, returned[i * capacity : (i + 1) * capacity])
        total = part if total is None else total + part
    grid_grad_ref[0] = total.astype(BF16)


def finish_kernel(one_ref, other_one_ref, two_ref, other_two_ref, weight_grad_ref):
    half, width = one_ref.shape
    core = lax.bitwise_and(lax.axis_index("rep"), 1)
    mine = pl.ds(pl.multiple_of(core * half, half), half)
    other = pl.ds(pl.multiple_of((1 - core) * half, half), half)
    weight_grad_ref[mine, :width] = one_ref[...].astype(F32)
    weight_grad_ref[other, :width] = other_one_ref[...].astype(F32)
    weight_grad_ref[mine, width:] = two_ref[...].astype(F32)
    weight_grad_ref[other, width:] = other_two_ref[...].astype(F32)


VMEM = pl.BlockSpec(memory_space=pltpu.VMEM)


def call(kernel, operands, outputs, scratch, flops, fetched=0):
    hbm = pl.BlockSpec(memory_space=pltpu.HBM)
    operands = [
        pltpu.with_memory_space_constraint(operand, pltpu.HBM) if n < fetched else operand
        for n, operand in enumerate(operands)
    ]
    return pl.pallas_call(
        kernel,
        out_shape=[jax.ShapeDtypeStruct(shape, kind) for shape, kind in outputs],
        in_specs=[hbm] * fetched + [VMEM] * (len(operands) - fetched),
        out_specs=[VMEM] * len(outputs),
        scratch_shapes=[pltpu.VMEM(shape, kind) for shape, kind in scratch]
        + ([pltpu.SemaphoreType.DMA((fetched,))] if fetched else []),
        compiler_params=pltpu.CompilerParams(vmem_limit_bytes=40 << 20),
        cost_estimate=pl.CostEstimate(flops=flops, bytes_accessed=4 << 20, transcendentals=0),
    )(*operands)


def swap(block, axis, bits):
    return lax.ppermute(block, axis, [(i, i ^ bits) for i in range(lax.axis_size(axis))])


def added(left, right):
    return (left.astype(F32) + right.astype(F32)).astype(BF16)


def summed_half(keep, give):
    half = added(keep, swap(give, "rep", 1))
    bit = 2
    while bit < lax.axis_size("rep"):
        half = added(half, swap(half, "rep", bit))
        bit *= 2
    return half, swap(half, "rep", 1)


def whole_sample_body(
    grid_latent,
    mesh_latent,
    mesh_cotangent,
    weights,
    g2m_pick,
    g2m_sender,
    g2m_receiver,
    m2m_pick,
    m2m_sender,
    m2m_receiver,
):
    regions = lax.axis_size("space")
    latent = weights.shape[0]
    listed = g2m_pick.shape[1] * g2m_pick.shape[2]
    mesh_count = mesh_latent.shape[1]
    mesh_cap = m2m_pick.shape[2]
    edges = g2m_sender.shape[0]
    columns = latent // regions
    half = columns // 2
    g2m_pick = g2m_pick.transpose(1, 0, 2)
    sources = (
        grid_latent,
        g2m_pick,
        g2m_sender.reshape(1, -1),
        g2m_receiver.reshape(1, -1),
        m2m_pick,
        m2m_sender.reshape(1, -1),
        m2m_receiver.reshape(1, -1),
    )
    (listed_rows,) = call(
        pack_kernel,
        sources,
        [((listed + INDEX_ROWS, latent), BF16)],
        [((INDEX_ROWS, latent), F32)] + [(source.shape, source.dtype) for source in sources],
        10**7,
        fetched=len(sources),
    )
    steps = (0, *range(2, regions), 1)
    latents = [mesh_latent] + [swap(mesh_latent, "space", step) for step in steps[1:]]
    *latents[1:], weights = lax.optimization_barrier((*latents[1:], weights))
    weights, turned = call(
        weights_kernel,
        (weights,),
        [(weights.shape, BF16), ((latent, 3 * latent), BF16)],
        [],
        10**8,
        fetched=1,
    )
    turned, cotangent = lax.optimization_barrier((turned, mesh_cotangent))
    packs = [listed_rows, mesh_latent]
    for step, latent_block in zip(steps[1:], latents[1:]):
        packs += [swap(listed_rows, "space", step), latent_block]
    near = swap(mesh_cotangent, "space", 1)
    cotangents = [mesh_cotangent] + [
        near if step == 1 else swap(cotangent, "space", step) for step in steps[1:]
    ]
    rows = regions * mesh_count
    slots = regions * mesh_cap
    (
        mesh_out,
        grid_all,
        mesh_all,
        mesh_first,
        mesh_sent,
        hot_one,
        hot_two,
        turned_one,
        turned_two,
        hot_sent,
        slope_one,
        slope_two,
        normed_one,
        scaled_one,
        normed_two,
        scaled_two,
    ) = call(
        functools.partial(forward_kernel, steps, listed, mesh_count, mesh_cap),
        (*packs, weights),
        [
            (mesh_latent.shape, BF16),
            ((regions * listed, latent), BF16),
            ((rows, latent), BF16),
            ((rows, latent), BF16),
            ((regions * slots, latent), BF16),
            ((regions * (listed + mesh_count), edges), BF16),
            ((regions * (slots + mesh_count), edges), BF16),
            ((regions * edges, listed + mesh_count), BF16),
            ((regions * edges, slots + mesh_count), BF16),
            ((rows, slots), BF16),
            ((regions * edges, latent), BF16),
            ((regions * edges, latent), BF16),
            ((rows, latent), F32),
            ((rows, 128), F32),
            ((rows, latent), F32),
            ((rows, 128), F32),
        ],
        [
            ((regions * INDEX_ROWS, latent), F32),
            ((regions * edges, latent), BF16),
            ((rows, latent), F32),
        ],
        2 * 10**9,
    )
    mesh_grad, keep_two, give_two = call(
        functools.partial(process_back_kernel, steps, mesh_cap),
        (
            *cotangents,
            turned,
            mesh_first,
            mesh_sent,
            hot_two,
            turned_two,
            hot_sent,
            slope_two,
            normed_two,
            scaled_two,
        ),
        [((rows, latent), F32)] + [((half, 2 * latent), BF16)] * 2,
        [
            ((rows, latent), F32),
            ((regions * slots, latent), F32),
            ((rows, latent), BF16),
            ((columns, 2 * latent), BF16),
            ((regions * edges, latent), BF16),
        ],
        10**9,
    )
    own_slots, keep_one, give_one = call(
        functools.partial(encode_back_kernel, regions),
        (
            grid_all,
            mesh_all,
            hot_one,
            turned_one,
            slope_one,
            normed_one,
            scaled_one,
            mesh_grad,
        ),
        [((listed, latent), BF16)] + [((half, 2 * latent), BF16)] * 2,
        [
            ((regions * listed, latent), BF16),
            ((rows, latent), BF16),
            ((columns, 2 * latent), BF16),
            ((regions * edges, latent), BF16),
        ],
        10**9,
    )
    grid_grad = call(
        grid_back_kernel,
        (turned, g2m_pick, own_slots),
        [(grid_latent.shape, BF16)],
        [],
        10**8,
    )[0]
    weight_grad = call(
        finish_kernel,
        (*summed_half(keep_one, give_one), *summed_half(keep_two, give_two)),
        [((columns, 4 * latent), F32)],
        [],
        10**6,
    )[0]
    return (mesh_out, grid_grad, weight_grad)


def solution(mesh):
    regions = mesh.shape["space"]
    samples = mesh.shape["rep"]

    def whole(*arguments):
        edges = arguments[5].shape[0] + arguments[8].shape[0]
        latent = arguments[3].shape[0]
        fits = edges * latent * 4 <= SAMPLE_EDGE_BYTES and latent % (128 * regions) == 0
        paired = all(n > 1 and n & (n - 1) == 0 for n in (regions, samples))
        return sharded(whole_sample_body if fits and paired else partitioned_body)(*arguments)

    def sharded(body):
        return jax.shard_map(
            body,
            mesh=mesh,
            in_specs=(
                P(("groups", "rep"), "space", None),
                P(("groups", "rep"), "space", None),
                P(("groups", "rep"), "space", None),
                P(),
                P("space", None, None),
                P("space"),
                P("space"),
                P("space", None, None),
                P("space"),
                P("space"),
            ),
            out_specs=(
                P(("groups", "rep"), "space", None),
                P(("groups", "rep"), "space", None),
                P(("groups", "space"), None),
            ),
            check_vma=False,
        )

    return whole
```

```python
import functools

import jax
import jax.numpy as jnp
from jax import lax
from jax.experimental import pallas as pl
from jax.experimental.pallas import tpu as pltpu
from jax.sharding import PartitionSpec as P

EPSILON = 1e-05


def with_halo(cells, sides, width):
    for axis, dim in sides:
        count = lax.axis_size(axis)
        ends = count - 1
        head = lax.slice_in_dim(cells, 0, width, axis=dim)
        tail = lax.slice_in_dim(cells, cells.shape[dim] - width, cells.shape[dim], axis=dim)
        cells = jnp.concatenate(
            [
                lax.ppermute(tail, axis, [(i, (i + 1) % count) for i in range(ends)]),
                cells,
                lax.ppermute(head, axis, [((i + 1) % count, i) for i in range(ends)]),
            ],
            axis=dim,
        )
    return cells


def swish(values):
    return values * jax.nn.sigmoid(values)


def swish_slope(values):
    squash = jax.nn.sigmoid(values)
    return squash * (1.0 + values * (1.0 - squash))


def norm_rows(values):
    centred = values - jnp.mean(values, -1, keepdims=True)
    return centred * lax.rsqrt(jnp.mean(centred * centred, -1, keepdims=True) + EPSILON)


def norm_rows_back(values, upstream):
    centred = values - jnp.mean(values, -1, keepdims=True)
    scaled = lax.rsqrt(jnp.mean(centred * centred, -1, keepdims=True) + EPSILON)
    normed = centred * scaled
    return scaled * (
        upstream
        - jnp.mean(upstream, -1, keepdims=True)
        - normed * jnp.mean(upstream * normed, -1, keepdims=True)
    )


def slot_rows(pick_row):
    listed = pick_row.reshape(-1)
    return listed


def mesh_route(outgoing, capacity, peer_count):
    columns = outgoing.shape[1]
    pieces = lax.all_to_all(
        outgoing.reshape(peer_count, capacity, columns),
        "space",
        split_axis=0,
        concat_axis=0,
        tiled=True,
    )
    arrived = pieces.reshape(peer_count * capacity, columns)
    return arrived


def grid_route(outgoing, capacity):
    columns = outgoing.shape[1]
    lists = outgoing.reshape(3, capacity, columns)
    rims = with_halo(jnp.stack([lists[0], lists[2]]), (("space", 0),), 1)
    return jnp.concatenate([rims[0], lists[1], rims[3]], axis=0)


def edge_pass(arrived, recv_table, located, receiver, w_send, w_recv):
    recv_proj = jnp.dot(recv_table, w_recv, preferred_element_type=jnp.float32)
    slot_proj = jnp.dot(arrived, w_send, preferred_element_type=jnp.float32)
    activation = slot_proj[located] + recv_proj[receiver]
    message = swish(activation).astype(jnp.bfloat16)
    member = (
        receiver[None, :] == jnp.arange(recv_table.shape[0], dtype=jnp.int32)[:, None]
    ).astype(jnp.bfloat16)
    summed = jnp.dot(member, message, preferred_element_type=jnp.float32)
    return (activation, member, summed)


def backward_pass(slot_count, located, activation, member, receiver, agg_grad, w_send):
    edge_grad = (agg_grad[receiver] * swish_slope(activation)).astype(jnp.bfloat16)
    recv_sum = jnp.dot(member, edge_grad, preferred_element_type=jnp.float32).astype(jnp.bfloat16)
    slot_member = (located[None, :] == jnp.arange(slot_count, dtype=jnp.int32)[:, None]).astype(
        jnp.bfloat16
    )
    slot_sum = jnp.dot(slot_member, edge_grad, preferred_element_type=jnp.float32).astype(
        jnp.bfloat16
    )
    returned = jnp.dot(slot_sum, w_send.T, preferred_element_type=jnp.float32).astype(jnp.bfloat16)
    return (recv_sum, slot_sum, returned)


def gather_back(listed, back_rows, row_count):
    owner = (listed[None, :] == jnp.arange(row_count, dtype=jnp.int32)[:, None]).astype(
        jnp.bfloat16
    )
    return jnp.dot(owner, back_rows, preferred_element_type=jnp.float32)


def partitioned_body(
    grid_latent,
    mesh_latent,
    mesh_cotangent,
    weights,
    g2m_pick,
    g2m_sender,
    g2m_receiver,
    m2m_pick,
    m2m_sender,
    m2m_receiver,
):
    grid_rows = grid_latent[0]
    mesh_rows = mesh_latent[0]
    upstream = mesh_cotangent[0].astype(jnp.float32)
    latent = weights.shape[0]
    encode_sender = weights[:, :latent]
    encode_receiver = weights[:, latent : 2 * latent]
    process_sender = weights[:, 2 * latent : 3 * latent]
    process_receiver = weights[:, 3 * latent :]
    peer_count = lax.axis_size("space")
    grid_cap = g2m_pick.shape[2]
    mesh_cap = m2m_pick.shape[2]
    grid_listed = g2m_pick[0].reshape(-1)
    grid_arrived = grid_route(grid_rows[grid_listed], grid_cap)
    act_first, member_first, summed_first = edge_pass(
        grid_arrived, mesh_rows, g2m_sender, g2m_receiver, encode_sender, encode_receiver
    )
    mesh_first = (mesh_rows.astype(jnp.float32) + norm_rows(summed_first)).astype(jnp.bfloat16)
    mesh_listed = slot_rows(m2m_pick[0])
    mesh_arrived = mesh_route(mesh_first[mesh_listed], mesh_cap, peer_count)
    act_second, member_second, summed_second = edge_pass(
        mesh_arrived, mesh_first, m2m_sender, m2m_receiver, process_sender, process_receiver
    )
    mesh_final = (mesh_first.astype(jnp.float32) + norm_rows(summed_second)).astype(jnp.bfloat16)
    agg_second = norm_rows_back(summed_second, upstream)
    recv_second, slot_second, returned_second = backward_pass(
        mesh_arrived.shape[0],
        m2m_sender,
        act_second,
        member_second,
        m2m_receiver,
        agg_second,
        process_sender,
    )
    back_second = mesh_route(returned_second, mesh_cap, peer_count)
    mesh_grad = upstream + jnp.dot(
        recv_second, process_receiver.T, preferred_element_type=jnp.float32
    )
    mesh_grad = mesh_grad + gather_back(mesh_listed, back_second, mesh_rows.shape[0])
    agg_first = norm_rows_back(summed_first, mesh_grad)
    recv_first, slot_first, returned_first = backward_pass(
        grid_arrived.shape[0],
        g2m_sender,
        act_first,
        member_first,
        g2m_receiver,
        agg_first,
        encode_sender,
    )
    back_first = grid_route(returned_first, grid_cap)
    grid_grad = gather_back(grid_listed, back_first, grid_rows.shape[0]).astype(jnp.bfloat16)
    factor_pairs = (
        (grid_arrived, slot_first),
        (mesh_rows, recv_first),
        (mesh_arrived, slot_second),
        (mesh_first, recv_second),
    )
    blocks = []
    for first_factor, second_factor in factor_pairs:
        blocks.append(
            lax.dot_general(
                first_factor,
                second_factor,
                (((0,), (0,)), ((), ())),
                preferred_element_type=jnp.float32,
            )
        )
    shares = lax.psum_scatter(
        jnp.concatenate(blocks, axis=1).astype(jnp.bfloat16),
        "space",
        scatter_dimension=0,
        tiled=True,
    )
    weight_grad = lax.psum(shares, "rep").astype(jnp.float32)
    return (mesh_final[None], grid_grad[None], weight_grad)


F32 = jnp.float32
BF16 = jnp.bfloat16
INDEX_ROWS = 8
SAMPLE_EDGE_BYTES = 8 << 20


def dot(left, right):
    return jnp.dot(left, right, preferred_element_type=F32)


def dot_first(left, right):
    return lax.dot_general(left, right, (((0,), (0,)), ((), ())), preferred_element_type=F32)


def one_hot(labels, count):
    rows = lax.broadcasted_iota(jnp.int32, (count, labels.shape[-1]), 0)
    return (rows == labels).astype(F32).astype(BF16)


def row_moments(values):
    centred = values - jnp.mean(values, -1, keepdims=True)
    return centred, lax.rsqrt(jnp.mean(centred * centred, -1, keepdims=True) + EPSILON)


def moments_back(normed, scaled, upstream):
    return scaled * (
        upstream
        - jnp.mean(upstream, -1, keepdims=True)
        - normed * jnp.mean(upstream * normed, -1, keepdims=True)
    )


def fetch(pairs, semaphores):
    copies = [
        pltpu.make_async_copy(source, target, semaphores.at[n])
        for n, (source, target) in enumerate(pairs)
    ]
    for copy in copies:
        copy.start()
    for copy in copies:
        copy.wait()


def pack_kernel(*refs):
    sources, packed_ref, index_ref = refs[:8], refs[8], refs[9]
    local, semaphores = refs[10:18], refs[18]
    fetch(list(zip(sources, local)), semaphores)
    (
        grid_ref,
        mesh_ref,
        g2m_pick_ref,
        g2m_sender_ref,
        g2m_receiver_ref,
        m2m_pick_ref,
        m2m_sender_ref,
        m2m_receiver_ref,
    ) = local
    lists, _, capacity = g2m_pick_ref.shape
    mesh_count = mesh_ref.shape[1]
    regions, mesh_cap = m2m_pick_ref.shape[1:]
    edges = g2m_sender_ref.shape[1]
    grid_rows = grid_ref[0]
    for i in range(lists):
        picked = one_hot(g2m_pick_ref[i], grid_rows.shape[0])
        packed_ref[i * capacity : (i + 1) * capacity, :] = dot_first(picked, grid_rows).astype(BF16)
    first = lists * capacity
    packed_ref[first : first + mesh_count, :] = mesh_ref[0]
    index_ref[...] = jnp.zeros_like(index_ref)
    index_ref[0:1, 0:edges] = g2m_sender_ref[...].astype(F32)
    index_ref[0:1, edges : 2 * edges] = g2m_receiver_ref[...].astype(F32)
    index_ref[1:2, 0:edges] = m2m_sender_ref[...].astype(F32)
    index_ref[1:2, edges : 2 * edges] = m2m_receiver_ref[...].astype(F32)
    slots = regions * mesh_cap
    lane = lax.broadcasted_iota(jnp.int32, (mesh_cap, slots), 1)
    spread = (lane % mesh_cap == lax.broadcasted_iota(jnp.int32, (mesh_cap, slots), 0)).astype(F32)
    spread = dot(m2m_pick_ref[0].astype(F32).astype(BF16), spread.astype(BF16))
    lane = lax.broadcasted_iota(jnp.int32, (regions, slots), 1)
    owned = lane // mesh_cap == lax.broadcasted_iota(jnp.int32, (regions, slots), 0)
    index_ref[2:3, 0:slots] = jnp.sum(jnp.where(owned, spread, 0.0), 0, keepdims=True)
    packed_ref[first + mesh_count :, :] = index_ref[...].astype(BF16)


def weights_kernel(source_ref, weights_ref, turned_ref, semaphores):
    fetch([(source_ref, weights_ref)], semaphores)
    latent = weights_ref.shape[0]
    for n, block in enumerate((0, 2, 3)):
        turned_ref[:, n * latent : (n + 1) * latent] = weights_ref[
            :, block * latent : (block + 1) * latent
        ].T


def edge_blocks(edges):
    size = min(edges, 128)
    return [(first, min(size, edges - first)) for first in range(0, edges, size)]


def edge_forward(tables, hot_ref, turned_hot_ref, slope_ref, message_ref, mesh_count):
    regions = len(tables)
    edges = slope_ref.shape[0] // regions
    count = hot_ref.shape[0] // regions
    work = [(d, first, size) for d in range(regions) for first, size in edge_blocks(edges)]

    def gathered(d, first, size):
        rows = slice(d * edges + first, d * edges + first + size)
        return dot(turned_hot_ref[rows, :], tables[d])

    sums = []
    activation = gathered(*work[0])
    for n, (d, first, size) in enumerate(work):
        coming = gathered(*work[n + 1]) if n + 1 < len(work) else None
        squash = 0.5 + 0.5 * jnp.tanh(0.5 * activation)
        message = activation * squash
        rows = slice(d * edges + first, d * edges + first + size)
        slope_ref[rows, :] = (squash + message * (1.0 - squash)).astype(BF16)
        message_ref[rows, :] = message.astype(BF16)
        activation = coming
        if first + size == edges:
            hot = hot_ref[(d + 1) * count - mesh_count : (d + 1) * count, :]
            sums.append(dot(hot, message_ref[d * edges : (d + 1) * edges, :]))
    return sums


def forward_kernel(
    steps,
    listed,
    mesh_count,
    mesh_cap,
    *refs,
):
    regions = len(steps)
    packed_refs = refs[:regions]
    (
        weights_ref,
        mesh_out_ref,
        grid_ref,
        mesh_ref,
        first_ref,
        sent_ref,
        hot_one_ref,
        hot_two_ref,
        turned_one_ref,
        turned_two_ref,
        hot_sent_ref,
        slope_one_ref,
        slope_two_ref,
        normed_one_ref,
        scaled_one_ref,
        normed_two_ref,
        scaled_two_ref,
        index_ref,
        message_ref,
        sum_ref,
    ) = refs[regions:]
    latent = weights_ref.shape[0]
    edges = slope_one_ref.shape[0] // regions
    capacity = listed // 3
    slots = regions * mesh_cap
    me = lax.axis_index("space")
    for step, packed_ref in zip(steps, packed_refs):
        region = lax.bitwise_xor(me, step)
        at = lambda rows: pl.ds(pl.multiple_of(region * rows, rows), rows)
        grid_ref[at(listed), :] = packed_ref[:listed, :]
        mesh_ref[at(mesh_count), :] = packed_ref[listed : listed + mesh_count, :]
        index_ref[at(INDEX_ROWS), :] = packed_ref[listed + mesh_count :, :].astype(F32)

    grid_proj = dot(grid_ref[...], weights_ref[:, :latent])
    mesh_proj = dot(mesh_ref[...], weights_ref[:, latent : 2 * latent])
    for d in range(regions):
        index = index_ref[d * INDEX_ROWS : (d + 1) * INDEX_ROWS, :].astype(jnp.int32)
        for row, senders, hot_ref, turned_ref in (
            (0, listed, hot_one_ref, turned_one_ref),
            (1, slots, hot_two_ref, turned_two_ref),
        ):
            count = senders + mesh_count
            hot = jnp.concatenate(
                [
                    one_hot(index[row : row + 1, :edges], senders),
                    one_hot(index[row : row + 1, edges:], mesh_count),
                ],
                axis=0,
            )
            hot_ref[d * count : (d + 1) * count, :] = hot
            turned_ref[d * edges : (d + 1) * edges, :] = hot.T
        hot_sent_ref[d * mesh_count : (d + 1) * mesh_count, :] = one_hot(
            index[2:3, :slots], mesh_count
        )

    blank = jnp.zeros((capacity, latent), F32)
    tables = []
    for d in range(regions):
        before = (d - 1) * listed + 2 * capacity
        within = d * listed + capacity
        after = (d + 1) * listed
        tables.append(
            jnp.concatenate(
                [
                    grid_proj[before : before + capacity] if d > 0 else blank,
                    grid_proj[within : within + capacity],
                    grid_proj[after : after + capacity] if d < regions - 1 else blank,
                    mesh_proj[d * mesh_count : (d + 1) * mesh_count],
                ],
                axis=0,
            ).astype(BF16)
        )
    sums = edge_forward(
        tables, hot_one_ref, turned_one_ref, slope_one_ref, message_ref, mesh_count
    )
    for d in range(regions):
        sum_ref[d * mesh_count : (d + 1) * mesh_count, :] = sums[d]
    centred, scaled = row_moments(sum_ref[...])
    normed = centred * scaled
    normed_one_ref[...] = normed
    scaled_one_ref[...] = jnp.broadcast_to(scaled, scaled_one_ref.shape)
    first_ref[...] = (mesh_ref[...].astype(F32) + normed).astype(BF16)

    for s in range(regions):
        rows = slice(s * mesh_count, (s + 1) * mesh_count)
        sent_ref[s * slots : (s + 1) * slots, :] = dot_first(
            hot_sent_ref[rows, :], first_ref[rows, :]
        ).astype(BF16)
    sent_proj = dot(sent_ref[...], weights_ref[:, 2 * latent : 3 * latent])
    first_proj = dot(first_ref[...], weights_ref[:, 3 * latent :])
    tables = []
    for d in range(regions):
        pieces = [
            sent_proj[s * slots + d * mesh_cap : s * slots + (d + 1) * mesh_cap]
            for s in range(regions)
        ]
        tables.append(
            jnp.concatenate(
                pieces + [first_proj[d * mesh_count : (d + 1) * mesh_count]], axis=0
            ).astype(BF16)
        )
    sums = edge_forward(
        tables, hot_two_ref, turned_two_ref, slope_two_ref, message_ref, mesh_count
    )
    for d in range(regions):
        sum_ref[d * mesh_count : (d + 1) * mesh_count, :] = sums[d]
    centred, scaled = row_moments(sum_ref[...])
    normed_two_ref[...] = centred * scaled
    scaled_two_ref[...] = jnp.broadcast_to(scaled, scaled_two_ref.shape)
    own = pl.ds(pl.multiple_of(me * mesh_count, mesh_count), mesh_count)
    mesh_out_ref[0] = (first_ref[own, :].astype(F32) + normed_two_ref[own, :]).astype(BF16)


def edge_backward(regions, agg_grad, hot_ref, turned_hot_ref, slope_ref, edge_grad_ref):
    edges = slope_ref.shape[0] // regions
    count = hot_ref.shape[0] // regions
    mesh_count = agg_grad.shape[0] // regions
    blank = jnp.zeros((count - mesh_count, agg_grad.shape[1]), BF16)
    work = [(d, first, size) for d in range(regions) for first, size in edge_blocks(edges)]

    def gathered(d, first, size):
        rows = slice(d * edges + first, d * edges + first + size)
        table = jnp.concatenate([blank, agg_grad[d * mesh_count : (d + 1) * mesh_count]], axis=0)
        return dot(turned_hot_ref[rows, :], table)

    sums = []
    upstream = gathered(*work[0])
    for n, (d, first, size) in enumerate(work):
        coming = gathered(*work[n + 1]) if n + 1 < len(work) else None
        rows = slice(d * edges + first, d * edges + first + size)
        edge_grad_ref[rows, :] = (upstream * slope_ref[rows, :].astype(F32)).astype(BF16)
        upstream = coming
        if first + size == edges:
            hot = hot_ref[d * count : (d + 1) * count, :]
            sums.append(dot(hot, edge_grad_ref[d * edges : (d + 1) * edges, :]))
    return sums


def halve(share_ref, keep_ref, give_ref):
    half = keep_ref.shape[0]
    core = lax.bitwise_and(lax.axis_index("rep"), 1)
    keep_ref[...] = share_ref[pl.ds(pl.multiple_of(core * half, half), half), :]
    give_ref[...] = share_ref[pl.ds(pl.multiple_of((1 - core) * half, half), half), :]


def process_back_kernel(steps, mesh_cap, *refs):
    regions = len(steps)
    cotangent_refs = refs[:regions]
    (
        turned_ref,
        first_ref,
        sent_ref,
        hot_ref,
        turned_hot_ref,
        hot_sent_ref,
        slope_ref,
        normed_ref,
        scaled_ref,
        mesh_grad_ref,
        keep_ref,
        give_ref,
        upstream_ref,
        slot_ref,
        recv_ref,
        share_ref,
        edge_grad_ref,
    ) = refs[regions:]
    latent = first_ref.shape[1]
    mesh_count = first_ref.shape[0] // regions
    slots = regions * mesh_cap
    me = lax.axis_index("space")
    for step, cotangent_ref in zip(steps, cotangent_refs):
        region = lax.bitwise_xor(me, step)
        at = pl.ds(pl.multiple_of(region * mesh_count, mesh_count), mesh_count)
        upstream_ref[at, :] = cotangent_ref[0].astype(F32)
    agg_grad = moments_back(normed_ref[...], scaled_ref[:, 0:1], upstream_ref[...]).astype(BF16)
    all_sums = edge_backward(
        regions, agg_grad, hot_ref, turned_hot_ref, slope_ref, edge_grad_ref
    )
    for d, sums in enumerate(all_sums):
        for s in range(regions):
            first = s * slots + d * mesh_cap
            slot_ref[first : first + mesh_cap, :] = sums[s * mesh_cap : (s + 1) * mesh_cap]
        recv_ref[d * mesh_count : (d + 1) * mesh_count, :] = sums[slots:].astype(BF16)
    slot_sum = slot_ref[...].astype(BF16)
    columns = share_ref.shape[0]
    mine = pl.ds(pl.multiple_of(me * columns, columns), columns)
    share_ref[:, :latent] = dot_first(sent_ref[:, mine], slot_sum).astype(BF16)
    share_ref[:, latent:] = dot_first(first_ref[:, mine], recv_ref[...]).astype(BF16)
    halve(share_ref, keep_ref, give_ref)
    returned = dot(slot_sum, turned_ref[:, latent : 2 * latent]).astype(BF16)
    grad = upstream_ref[...] + dot(recv_ref[...], turned_ref[:, 2 * latent :])
    for s in range(regions):
        rows = slice(s * mesh_count, (s + 1) * mesh_count)
        mesh_grad_ref[rows, :] = grad[rows] + dot(
            hot_sent_ref[rows, :], returned[s * slots : (s + 1) * slots]
        )


def encode_back_kernel(
    regions,
    grid_ref,
    mesh_ref,
    hot_ref,
    turned_hot_ref,
    slope_ref,
    normed_ref,
    scaled_ref,
    mesh_grad_ref,
    own_slot_ref,
    keep_ref,
    give_ref,
    slot_ref,
    recv_ref,
    share_ref,
    edge_grad_ref,
):
    latent = mesh_ref.shape[1]
    mesh_count = mesh_ref.shape[0] // regions
    listed = grid_ref.shape[0] // regions
    capacity = listed // 3
    me = lax.axis_index("space")
    agg_grad = moments_back(normed_ref[...], scaled_ref[:, 0:1], mesh_grad_ref[...]).astype(BF16)
    blank = jnp.zeros((capacity, latent), BF16)
    slot_ref[0:capacity, :] = blank
    slot_ref[regions * listed - capacity :, :] = blank
    all_sums = edge_backward(
        regions, agg_grad, hot_ref, turned_hot_ref, slope_ref, edge_grad_ref
    )
    for d, sums in enumerate(all_sums):
        sums = sums.astype(BF16)
        for j in range(3):
            source = d + j - 1
            if 0 <= source < regions:
                first = source * listed + (2 - j) * capacity
                slot_ref[first : first + capacity, :] = sums[j * capacity : (j + 1) * capacity]
        recv_ref[d * mesh_count : (d + 1) * mesh_count, :] = sums[listed:]
    columns = share_ref.shape[0]
    mine = pl.ds(pl.multiple_of(me * columns, columns), columns)
    share_ref[:, :latent] = dot_first(grid_ref[:, mine], slot_ref[...]).astype(BF16)
    share_ref[:, latent:] = dot_first(mesh_ref[:, mine], recv_ref[...]).astype(BF16)
    halve(share_ref, keep_ref, give_ref)
    own = pl.ds(pl.multiple_of(me * listed, listed), listed)
    own_slot_ref[...] = slot_ref[own, :]


def grid_back_kernel(turned_ref, pick_ref, own_slot_ref, grid_grad_ref):
    lists, _, capacity = pick_ref.shape
    latent = own_slot_ref.shape[1]
    returned = dot(own_slot_ref[...], turned_ref[:, :latent]).astype(BF16)
    total = None
    for i in range(lists):
        owner = one_hot(pick_ref[i], grid_grad_ref.shape[1])
        part = dot(owner, returned[i * capacity : (i + 1) * capacity])
        total = part if total is None else total + part
    grid_grad_ref[0] = total.astype(BF16)


def place(pairs, stages, semaphores):
    copies = []
    for n, (block_ref, target) in enumerate(pairs):
        stages[n][...] = block_ref[...].astype(F32)
        copies.append(pltpu.make_async_copy(stages[n], target, semaphores.at[n]))
        copies[n].start()
    for copy in copies:
        copy.wait()


def half_rows(half):
    core = lax.bitwise_and(lax.axis_index("rep"), 1)
    mine = pl.ds(pl.multiple_of(core * half, half), half)
    return mine, pl.ds(pl.multiple_of((1 - core) * half, half), half)


def settle_kernel(one_ref, two_ref, other_two_ref, weight_grad_ref, *scratch):
    half, width = one_ref.shape
    mine, other = half_rows(half)
    place(
        [
            (two_ref, weight_grad_ref.at[mine, width:]),
            (other_two_ref, weight_grad_ref.at[other, width:]),
            (one_ref, weight_grad_ref.at[mine, :width]),
        ],
        scratch[:3],
        scratch[3],
    )


def finish_kernel(other_one_ref, settled_ref, weight_grad_ref, stage, semaphores):
    half, width = other_one_ref.shape
    _, other = half_rows(half)
    place([(other_one_ref, weight_grad_ref.at[other, :width])], [stage], semaphores)


VMEM = pl.BlockSpec(memory_space=pltpu.VMEM)


def call(kernel, operands, outputs, scratch, flops, fetched=0):
    hbm = pl.BlockSpec(memory_space=pltpu.HBM)
    operands = [
        pltpu.with_memory_space_constraint(operand, pltpu.HBM) if n < fetched else operand
        for n, operand in enumerate(operands)
    ]
    return pl.pallas_call(
        kernel,
        out_shape=[jax.ShapeDtypeStruct(shape, kind) for shape, kind in outputs],
        in_specs=[hbm] * fetched + [VMEM] * (len(operands) - fetched),
        out_specs=[VMEM] * len(outputs),
        scratch_shapes=[pltpu.VMEM(shape, kind) for shape, kind in scratch]
        + ([pltpu.SemaphoreType.DMA((fetched,))] if fetched else []),
        compiler_params=pltpu.CompilerParams(vmem_limit_bytes=40 << 20),
        cost_estimate=pl.CostEstimate(flops=flops, bytes_accessed=4 << 20, transcendentals=0),
    )(*operands)


def swap(block, axis, bits):
    return lax.ppermute(block, axis, [(i, i ^ bits) for i in range(lax.axis_size(axis))])


def added(left, right):
    return (left.astype(F32) + right.astype(F32)).astype(BF16)


def summed_over_chips(half):
    bit = 2
    while bit < lax.axis_size("rep"):
        half = added(half, swap(half, "rep", bit))
        bit *= 2
    return half


def whole_sample_body(
    grid_latent,
    mesh_latent,
    mesh_cotangent,
    weights,
    g2m_pick,
    g2m_sender,
    g2m_receiver,
    m2m_pick,
    m2m_sender,
    m2m_receiver,
):
    regions = lax.axis_size("space")
    latent = weights.shape[0]
    listed = g2m_pick.shape[1] * g2m_pick.shape[2]
    mesh_count = mesh_latent.shape[1]
    mesh_cap = m2m_pick.shape[2]
    edges = g2m_sender.shape[0]
    columns = latent // regions
    half = columns // 2
    g2m_pick = g2m_pick.transpose(1, 0, 2)
    sources = (
        grid_latent,
        mesh_latent,
        g2m_pick,
        g2m_sender.reshape(1, -1),
        g2m_receiver.reshape(1, -1),
        m2m_pick,
        m2m_sender.reshape(1, -1),
        m2m_receiver.reshape(1, -1),
    )
    packed = call(
        pack_kernel,
        sources,
        [((listed + mesh_count + INDEX_ROWS, latent), BF16)],
        [((INDEX_ROWS, latent), F32)] + [(source.shape, source.dtype) for source in sources],
        10**7,
        fetched=len(sources),
    )[0]
    packed, cotangent, weights = lax.optimization_barrier((packed, mesh_cotangent, weights))
    steps = (0, *range(2, regions), 1)
    packs = [packed] + [swap(packed, "space", step) for step in steps[1:]]
    near = swap(cotangent, "space", 1)
    weights, turned = call(
        weights_kernel,
        (weights,),
        [(weights.shape, BF16), ((latent, 3 * latent), BF16)],
        [],
        10**8,
        fetched=1,
    )
    packs[1], cotangent = lax.optimization_barrier((packs[1], cotangent))
    cotangents = [cotangent] + [swap(cotangent, "space", step) for step in steps[1:-1]] + [near]
    rows = regions * mesh_count
    slots = regions * mesh_cap
    (
        mesh_out,
        grid_all,
        mesh_all,
        mesh_first,
        mesh_sent,
        hot_one,
        hot_two,
        turned_one,
        turned_two,
        hot_sent,
        slope_one,
        slope_two,
        normed_one,
        scaled_one,
        normed_two,
        scaled_two,
    ) = call(
        functools.partial(forward_kernel, steps, listed, mesh_count, mesh_cap),
        (*packs, weights),
        [
            (mesh_latent.shape, BF16),
            ((regions * listed, latent), BF16),
            ((rows, latent), BF16),
            ((rows, latent), BF16),
            ((regions * slots, latent), BF16),
            ((regions * (listed + mesh_count), edges), BF16),
            ((regions * (slots + mesh_count), edges), BF16),
            ((regions * edges, listed + mesh_count), BF16),
            ((regions * edges, slots + mesh_count), BF16),
            ((rows, slots), BF16),
            ((regions * edges, latent), BF16),
            ((regions * edges, latent), BF16),
            ((rows, latent), F32),
            ((rows, 128), F32),
            ((rows, latent), F32),
            ((rows, 128), F32),
        ],
        [
            ((regions * INDEX_ROWS, latent), F32),
            ((regions * edges, latent), BF16),
            ((rows, latent), F32),
        ],
        2 * 10**9,
    )
    mesh_grad, keep_two, give_two = call(
        functools.partial(process_back_kernel, steps, mesh_cap),
        (
            *cotangents,
            turned,
            mesh_first,
            mesh_sent,
            hot_two,
            turned_two,
            hot_sent,
            slope_two,
            normed_two,
            scaled_two,
        ),
        [((rows, latent), F32)] + [((half, 2 * latent), BF16)] * 2,
        [
            ((rows, latent), F32),
            ((regions * slots, latent), F32),
            ((rows, latent), BF16),
            ((columns, 2 * latent), BF16),
            ((regions * edges, latent), BF16),
        ],
        10**9,
    )
    own_slots, keep_one, give_one = call(
        functools.partial(encode_back_kernel, regions),
        (
            grid_all,
            mesh_all,
            hot_one,
            turned_one,
            slope_one,
            normed_one,
            scaled_one,
            mesh_grad,
        ),
        [((listed, latent), BF16)] + [((half, 2 * latent), BF16)] * 2,
        [
            ((regions * listed, latent), BF16),
            ((rows, latent), BF16),
            ((columns, 2 * latent), BF16),
            ((regions * edges, latent), BF16),
        ],
        10**9,
    )
    half_one = added(keep_one, swap(give_one, "rep", 1))
    half_two = added(keep_two, swap(give_two, "rep", 1))
    half_one, own_slots = lax.optimization_barrier((half_one, own_slots))
    grid_grad = call(
        grid_back_kernel,
        (turned, g2m_pick, own_slots),
        [(grid_latent.shape, BF16)],
        [],
        10**8,
    )[0]
    two = summed_over_chips(half_two)
    one, grid_grad = lax.optimization_barrier((summed_over_chips(half_one), grid_grad))
    hbm = pl.BlockSpec(memory_space=pltpu.HBM)
    stage = pltpu.VMEM((half, 2 * latent), F32)
    weight_shape = pltpu.HBM((columns, 4 * latent), F32)
    limit = pltpu.CompilerParams(vmem_limit_bytes=40 << 20)
    settled = pl.pallas_call(
        settle_kernel,
        out_shape=weight_shape,
        in_specs=[VMEM] * 3,
        out_specs=hbm,
        scratch_shapes=[stage] * 3 + [pltpu.SemaphoreType.DMA((3,))],
        compiler_params=limit,
    )(one, two, swap(two, "rep", 1))
    weight_grad = pl.pallas_call(
        finish_kernel,
        out_shape=weight_shape,
        in_specs=[VMEM, hbm],
        out_specs=hbm,
        scratch_shapes=[stage, pltpu.SemaphoreType.DMA((1,))],
        input_output_aliases={1: 0},
        compiler_params=limit,
    )(swap(one, "rep", 1), settled)
    return (mesh_out, grid_grad, weight_grad)


def solution(mesh):
    regions = mesh.shape["space"]
    samples = mesh.shape["rep"]

    def whole(*arguments):
        edges = arguments[5].shape[0] + arguments[8].shape[0]
        latent = arguments[3].shape[0]
        fits = edges * latent * 4 <= SAMPLE_EDGE_BYTES and latent % (128 * regions) == 0
        paired = all(n > 1 and n & (n - 1) == 0 for n in (regions, samples))
        return sharded(whole_sample_body if fits and paired else partitioned_body)(*arguments)

    def sharded(body):
        return jax.shard_map(
            body,
            mesh=mesh,
            in_specs=(
                P(("groups", "rep"), "space", None),
                P(("groups", "rep"), "space", None),
                P(("groups", "rep"), "space", None),
                P(),
                P("space", None, None),
                P("space"),
                P("space"),
                P("space", None, None),
                P("space"),
                P("space"),
            ),
            out_specs=(
                P(("groups", "rep"), "space", None),
                P(("groups", "rep"), "space", None),
                P(("groups", "space"), None),
            ),
            check_vma=False,
        )

    return whole
```

```python
import functools

import jax
import jax.numpy as jnp
from jax import lax
from jax.experimental import pallas as pl
from jax.experimental.pallas import tpu as pltpu
from jax.sharding import PartitionSpec as P

EPSILON = 1e-05


def with_halo(cells, sides, width):
    for axis, dim in sides:
        count = lax.axis_size(axis)
        ends = count - 1
        head = lax.slice_in_dim(cells, 0, width, axis=dim)
        tail = lax.slice_in_dim(cells, cells.shape[dim] - width, cells.shape[dim], axis=dim)
        cells = jnp.concatenate(
            [
                lax.ppermute(tail, axis, [(i, (i + 1) % count) for i in range(ends)]),
                cells,
                lax.ppermute(head, axis, [((i + 1) % count, i) for i in range(ends)]),
            ],
            axis=dim,
        )
    return cells


def swish(values):
    return values * jax.nn.sigmoid(values)


def swish_slope(values):
    squash = jax.nn.sigmoid(values)
    return squash * (1.0 + values * (1.0 - squash))


def norm_rows(values):
    centred = values - jnp.mean(values, -1, keepdims=True)
    return centred * lax.rsqrt(jnp.mean(centred * centred, -1, keepdims=True) + EPSILON)


def norm_rows_back(values, upstream):
    centred = values - jnp.mean(values, -1, keepdims=True)
    scaled = lax.rsqrt(jnp.mean(centred * centred, -1, keepdims=True) + EPSILON)
    normed = centred * scaled
    return scaled * (
        upstream
        - jnp.mean(upstream, -1, keepdims=True)
        - normed * jnp.mean(upstream * normed, -1, keepdims=True)
    )


def slot_rows(pick_row):
    listed = pick_row.reshape(-1)
    return listed


def mesh_route(outgoing, capacity, peer_count):
    columns = outgoing.shape[1]
    pieces = lax.all_to_all(
        outgoing.reshape(peer_count, capacity, columns),
        "space",
        split_axis=0,
        concat_axis=0,
        tiled=True,
    )
    arrived = pieces.reshape(peer_count * capacity, columns)
    return arrived


def grid_route(outgoing, capacity):
    columns = outgoing.shape[1]
    lists = outgoing.reshape(3, capacity, columns)
    rims = with_halo(jnp.stack([lists[0], lists[2]]), (("space", 0),), 1)
    return jnp.concatenate([rims[0], lists[1], rims[3]], axis=0)


def edge_pass(arrived, recv_table, located, receiver, w_send, w_recv):
    recv_proj = jnp.dot(recv_table, w_recv, preferred_element_type=jnp.float32)
    slot_proj = jnp.dot(arrived, w_send, preferred_element_type=jnp.float32)
    activation = slot_proj[located] + recv_proj[receiver]
    message = swish(activation).astype(jnp.bfloat16)
    member = (
        receiver[None, :] == jnp.arange(recv_table.shape[0], dtype=jnp.int32)[:, None]
    ).astype(jnp.bfloat16)
    summed = jnp.dot(member, message, preferred_element_type=jnp.float32)
    return (activation, member, summed)


def backward_pass(slot_count, located, activation, member, receiver, agg_grad, w_send):
    edge_grad = (agg_grad[receiver] * swish_slope(activation)).astype(jnp.bfloat16)
    recv_sum = jnp.dot(member, edge_grad, preferred_element_type=jnp.float32).astype(jnp.bfloat16)
    slot_member = (located[None, :] == jnp.arange(slot_count, dtype=jnp.int32)[:, None]).astype(
        jnp.bfloat16
    )
    slot_sum = jnp.dot(slot_member, edge_grad, preferred_element_type=jnp.float32).astype(
        jnp.bfloat16
    )
    returned = jnp.dot(slot_sum, w_send.T, preferred_element_type=jnp.float32).astype(jnp.bfloat16)
    return (recv_sum, slot_sum, returned)


def gather_back(listed, back_rows, row_count):
    owner = (listed[None, :] == jnp.arange(row_count, dtype=jnp.int32)[:, None]).astype(
        jnp.bfloat16
    )
    return jnp.dot(owner, back_rows, preferred_element_type=jnp.float32)


def partitioned_body(
    grid_latent,
    mesh_latent,
    mesh_cotangent,
    weights,
    g2m_pick,
    g2m_sender,
    g2m_receiver,
    m2m_pick,
    m2m_sender,
    m2m_receiver,
):
    grid_rows = grid_latent[0]
    mesh_rows = mesh_latent[0]
    upstream = mesh_cotangent[0].astype(jnp.float32)
    latent = weights.shape[0]
    encode_sender = weights[:, :latent]
    encode_receiver = weights[:, latent : 2 * latent]
    process_sender = weights[:, 2 * latent : 3 * latent]
    process_receiver = weights[:, 3 * latent :]
    peer_count = lax.axis_size("space")
    grid_cap = g2m_pick.shape[2]
    mesh_cap = m2m_pick.shape[2]
    grid_listed = g2m_pick[0].reshape(-1)
    grid_arrived = grid_route(grid_rows[grid_listed], grid_cap)
    act_first, member_first, summed_first = edge_pass(
        grid_arrived, mesh_rows, g2m_sender, g2m_receiver, encode_sender, encode_receiver
    )
    mesh_first = (mesh_rows.astype(jnp.float32) + norm_rows(summed_first)).astype(jnp.bfloat16)
    mesh_listed = slot_rows(m2m_pick[0])
    mesh_arrived = mesh_route(mesh_first[mesh_listed], mesh_cap, peer_count)
    act_second, member_second, summed_second = edge_pass(
        mesh_arrived, mesh_first, m2m_sender, m2m_receiver, process_sender, process_receiver
    )
    mesh_final = (mesh_first.astype(jnp.float32) + norm_rows(summed_second)).astype(jnp.bfloat16)
    agg_second = norm_rows_back(summed_second, upstream)
    recv_second, slot_second, returned_second = backward_pass(
        mesh_arrived.shape[0],
        m2m_sender,
        act_second,
        member_second,
        m2m_receiver,
        agg_second,
        process_sender,
    )
    back_second = mesh_route(returned_second, mesh_cap, peer_count)
    mesh_grad = upstream + jnp.dot(
        recv_second, process_receiver.T, preferred_element_type=jnp.float32
    )
    mesh_grad = mesh_grad + gather_back(mesh_listed, back_second, mesh_rows.shape[0])
    agg_first = norm_rows_back(summed_first, mesh_grad)
    recv_first, slot_first, returned_first = backward_pass(
        grid_arrived.shape[0],
        g2m_sender,
        act_first,
        member_first,
        g2m_receiver,
        agg_first,
        encode_sender,
    )
    back_first = grid_route(returned_first, grid_cap)
    grid_grad = gather_back(grid_listed, back_first, grid_rows.shape[0]).astype(jnp.bfloat16)
    factor_pairs = (
        (grid_arrived, slot_first),
        (mesh_rows, recv_first),
        (mesh_arrived, slot_second),
        (mesh_first, recv_second),
    )
    blocks = []
    for first_factor, second_factor in factor_pairs:
        blocks.append(
            lax.dot_general(
                first_factor,
                second_factor,
                (((0,), (0,)), ((), ())),
                preferred_element_type=jnp.float32,
            )
        )
    shares = lax.psum_scatter(
        jnp.concatenate(blocks, axis=1).astype(jnp.bfloat16),
        "space",
        scatter_dimension=0,
        tiled=True,
    )
    weight_grad = lax.psum(shares, "rep").astype(jnp.float32)
    return (mesh_final[None], grid_grad[None], weight_grad)


F32 = jnp.float32
BF16 = jnp.bfloat16
INDEX_ROWS = 8
SAMPLE_EDGE_BYTES = 8 << 20


def dot(left, right):
    return jnp.dot(left, right, preferred_element_type=F32)


def dot_first(left, right):
    return lax.dot_general(left, right, (((0,), (0,)), ((), ())), preferred_element_type=F32)


def one_hot(labels, count):
    rows = lax.broadcasted_iota(jnp.int32, (count, labels.shape[-1]), 0)
    return (rows == labels).astype(F32).astype(BF16)


def row_moments(values):
    centred = values - jnp.mean(values, -1, keepdims=True)
    return centred, lax.rsqrt(jnp.mean(centred * centred, -1, keepdims=True) + EPSILON)


def moments_back(normed, scaled, upstream):
    return scaled * (
        upstream
        - jnp.mean(upstream, -1, keepdims=True)
        - normed * jnp.mean(upstream * normed, -1, keepdims=True)
    )


def fetch(pairs, semaphores):
    copies = [
        pltpu.make_async_copy(source, target, semaphores.at[n])
        for n, (source, target) in enumerate(pairs)
    ]
    for copy in copies:
        copy.start()
    for copy in copies:
        copy.wait()


def pack_kernel(*refs):
    sources, packed_ref, index_ref = refs[:8], refs[8], refs[9]
    local, semaphores = refs[10:18], refs[18]
    fetch(list(zip(sources, local)), semaphores)
    (
        grid_ref,
        mesh_ref,
        g2m_pick_ref,
        g2m_sender_ref,
        g2m_receiver_ref,
        m2m_pick_ref,
        m2m_sender_ref,
        m2m_receiver_ref,
    ) = local
    lists, _, capacity = g2m_pick_ref.shape
    mesh_count = mesh_ref.shape[1]
    regions, mesh_cap = m2m_pick_ref.shape[1:]
    edges = g2m_sender_ref.shape[1]
    grid_rows = grid_ref[0]
    for i in range(lists):
        picked = one_hot(g2m_pick_ref[i], grid_rows.shape[0])
        packed_ref[i * capacity : (i + 1) * capacity, :] = dot_first(picked, grid_rows).astype(BF16)
    first = lists * capacity
    packed_ref[first : first + mesh_count, :] = mesh_ref[0]
    index_ref[...] = jnp.zeros_like(index_ref)
    index_ref[0:1, 0:edges] = g2m_sender_ref[...].astype(F32)
    index_ref[0:1, edges : 2 * edges] = g2m_receiver_ref[...].astype(F32)
    index_ref[1:2, 0:edges] = m2m_sender_ref[...].astype(F32)
    index_ref[1:2, edges : 2 * edges] = m2m_receiver_ref[...].astype(F32)
    slots = regions * mesh_cap
    lane = lax.broadcasted_iota(jnp.int32, (mesh_cap, slots), 1)
    spread = (lane % mesh_cap == lax.broadcasted_iota(jnp.int32, (mesh_cap, slots), 0)).astype(F32)
    spread = dot(m2m_pick_ref[0].astype(F32).astype(BF16), spread.astype(BF16))
    lane = lax.broadcasted_iota(jnp.int32, (regions, slots), 1)
    owned = lane // mesh_cap == lax.broadcasted_iota(jnp.int32, (regions, slots), 0)
    index_ref[2:3, 0:slots] = jnp.sum(jnp.where(owned, spread, 0.0), 0, keepdims=True)
    packed_ref[first + mesh_count :, :] = index_ref[...].astype(BF16)


def weights_kernel(source_ref, weights_ref, turned_ref, semaphores):
    fetch([(source_ref, weights_ref)], semaphores)
    latent = weights_ref.shape[0]
    for n, block in enumerate((0, 2, 3)):
        turned_ref[:, n * latent : (n + 1) * latent] = weights_ref[
            :, block * latent : (block + 1) * latent
        ].T


def edge_blocks(edges):
    size = min(edges, 128)
    return [(first, min(size, edges - first)) for first in range(0, edges, size)]


def edge_forward(tables, hot_ref, turned_hot_ref, slope_ref, message_ref, mesh_count):
    regions = len(tables)
    edges = slope_ref.shape[0] // regions
    count = hot_ref.shape[0] // regions
    work = [(d, first, size) for d in range(regions) for first, size in edge_blocks(edges)]

    def gathered(d, first, size):
        rows = slice(d * edges + first, d * edges + first + size)
        return dot(turned_hot_ref[rows, :], tables[d])

    sums = []
    activation = gathered(*work[0])
    for n, (d, first, size) in enumerate(work):
        coming = gathered(*work[n + 1]) if n + 1 < len(work) else None
        activation = activation.astype(BF16)
        squash = 0.5 + 0.5 * jnp.tanh(0.5 * activation)
        message = activation * squash
        rows = slice(d * edges + first, d * edges + first + size)
        slope_ref[rows, :] = squash + message * (1.0 - squash)
        message_ref[rows, :] = message
        activation = coming
        if first + size == edges:
            hot = hot_ref[(d + 1) * count - mesh_count : (d + 1) * count, :]
            sums.append(dot(hot, message_ref[d * edges : (d + 1) * edges, :]))
    return sums


def forward_kernel(
    steps,
    listed,
    mesh_count,
    mesh_cap,
    *refs,
):
    regions = len(steps)
    packed_refs = refs[:regions]
    (
        weights_ref,
        mesh_out_ref,
        grid_ref,
        mesh_ref,
        first_ref,
        sent_ref,
        hot_one_ref,
        hot_two_ref,
        turned_one_ref,
        turned_two_ref,
        hot_sent_ref,
        slope_one_ref,
        slope_two_ref,
        normed_one_ref,
        scaled_one_ref,
        normed_two_ref,
        scaled_two_ref,
        index_ref,
        message_ref,
        sum_ref,
    ) = refs[regions:]
    latent = weights_ref.shape[0]
    edges = slope_one_ref.shape[0] // regions
    capacity = listed // 3
    slots = regions * mesh_cap
    me = lax.axis_index("space")
    for step, packed_ref in zip(steps, packed_refs):
        region = lax.bitwise_xor(me, step)
        at = lambda rows: pl.ds(pl.multiple_of(region * rows, rows), rows)
        grid_ref[at(listed), :] = packed_ref[:listed, :]
        mesh_ref[at(mesh_count), :] = packed_ref[listed : listed + mesh_count, :]
        index_ref[at(INDEX_ROWS), :] = packed_ref[listed + mesh_count :, :].astype(F32)

    grid_proj = dot(grid_ref[...], weights_ref[:, :latent])
    mesh_proj = dot(mesh_ref[...], weights_ref[:, latent : 2 * latent])
    for d in range(regions):
        index = index_ref[d * INDEX_ROWS : (d + 1) * INDEX_ROWS, :].astype(jnp.int32)
        for row, senders, hot_ref, turned_ref in (
            (0, listed, hot_one_ref, turned_one_ref),
            (1, slots, hot_two_ref, turned_two_ref),
        ):
            count = senders + mesh_count
            hot = jnp.concatenate(
                [
                    one_hot(index[row : row + 1, :edges], senders),
                    one_hot(index[row : row + 1, edges:], mesh_count),
                ],
                axis=0,
            )
            hot_ref[d * count : (d + 1) * count, :] = hot
            turned_ref[d * edges : (d + 1) * edges, :] = hot.T
        hot_sent_ref[d * mesh_count : (d + 1) * mesh_count, :] = one_hot(
            index[2:3, :slots], mesh_count
        )

    blank = jnp.zeros((capacity, latent), F32)
    tables = []
    for d in range(regions):
        before = (d - 1) * listed + 2 * capacity
        within = d * listed + capacity
        after = (d + 1) * listed
        tables.append(
            jnp.concatenate(
                [
                    grid_proj[before : before + capacity] if d > 0 else blank,
                    grid_proj[within : within + capacity],
                    grid_proj[after : after + capacity] if d < regions - 1 else blank,
                    mesh_proj[d * mesh_count : (d + 1) * mesh_count],
                ],
                axis=0,
            ).astype(BF16)
        )
    sums = edge_forward(
        tables, hot_one_ref, turned_one_ref, slope_one_ref, message_ref, mesh_count
    )
    for d in range(regions):
        sum_ref[d * mesh_count : (d + 1) * mesh_count, :] = sums[d]
    centred, scaled = row_moments(sum_ref[...])
    normed = centred * scaled
    normed_one_ref[...] = normed
    scaled_one_ref[...] = jnp.broadcast_to(scaled, scaled_one_ref.shape)
    first_ref[...] = (mesh_ref[...].astype(F32) + normed).astype(BF16)

    for s in range(regions):
        rows = slice(s * mesh_count, (s + 1) * mesh_count)
        sent_ref[s * slots : (s + 1) * slots, :] = dot_first(
            hot_sent_ref[rows, :], first_ref[rows, :]
        ).astype(BF16)
    sent_proj = dot(sent_ref[...], weights_ref[:, 2 * latent : 3 * latent])
    first_proj = dot(first_ref[...], weights_ref[:, 3 * latent :])
    tables = []
    for d in range(regions):
        pieces = [
            sent_proj[s * slots + d * mesh_cap : s * slots + (d + 1) * mesh_cap]
            for s in range(regions)
        ]
        tables.append(
            jnp.concatenate(
                pieces + [first_proj[d * mesh_count : (d + 1) * mesh_count]], axis=0
            ).astype(BF16)
        )
    sums = edge_forward(
        tables, hot_two_ref, turned_two_ref, slope_two_ref, message_ref, mesh_count
    )
    for d in range(regions):
        sum_ref[d * mesh_count : (d + 1) * mesh_count, :] = sums[d]
    centred, scaled = row_moments(sum_ref[...])
    normed_two_ref[...] = centred * scaled
    scaled_two_ref[...] = jnp.broadcast_to(scaled, scaled_two_ref.shape)
    own = pl.ds(pl.multiple_of(me * mesh_count, mesh_count), mesh_count)
    mesh_out_ref[0] = (first_ref[own, :].astype(F32) + normed_two_ref[own, :]).astype(BF16)


def edge_backward(regions, agg_grad, hot_ref, turned_hot_ref, slope_ref, edge_grad_ref):
    edges = slope_ref.shape[0] // regions
    count = hot_ref.shape[0] // regions
    mesh_count = agg_grad.shape[0] // regions
    blank = jnp.zeros((count - mesh_count, agg_grad.shape[1]), BF16)
    work = [(d, first, size) for d in range(regions) for first, size in edge_blocks(edges)]

    def gathered(d, first, size):
        rows = slice(d * edges + first, d * edges + first + size)
        table = jnp.concatenate([blank, agg_grad[d * mesh_count : (d + 1) * mesh_count]], axis=0)
        return dot(turned_hot_ref[rows, :], table)

    sums = []
    upstream = gathered(*work[0])
    for n, (d, first, size) in enumerate(work):
        coming = gathered(*work[n + 1]) if n + 1 < len(work) else None
        rows = slice(d * edges + first, d * edges + first + size)
        edge_grad_ref[rows, :] = upstream.astype(BF16) * slope_ref[rows, :]
        upstream = coming
        if first + size == edges:
            hot = hot_ref[d * count : (d + 1) * count, :]
            sums.append(dot(hot, edge_grad_ref[d * edges : (d + 1) * edges, :]))
    return sums


def halve(share_ref, keep_ref, give_ref):
    half = keep_ref.shape[0]
    core = lax.bitwise_and(lax.axis_index("rep"), 1)
    keep_ref[...] = share_ref[pl.ds(pl.multiple_of(core * half, half), half), :]
    give_ref[...] = share_ref[pl.ds(pl.multiple_of((1 - core) * half, half), half), :]


def process_back_kernel(steps, mesh_cap, *refs):
    regions = len(steps)
    cotangent_refs = refs[:regions]
    (
        turned_ref,
        first_ref,
        sent_ref,
        hot_ref,
        turned_hot_ref,
        hot_sent_ref,
        slope_ref,
        normed_ref,
        scaled_ref,
        mesh_grad_ref,
        keep_ref,
        give_ref,
        upstream_ref,
        slot_ref,
        recv_ref,
        share_ref,
        edge_grad_ref,
    ) = refs[regions:]
    latent = first_ref.shape[1]
    mesh_count = first_ref.shape[0] // regions
    slots = regions * mesh_cap
    me = lax.axis_index("space")
    for step, cotangent_ref in zip(steps, cotangent_refs):
        region = lax.bitwise_xor(me, step)
        at = pl.ds(pl.multiple_of(region * mesh_count, mesh_count), mesh_count)
        upstream_ref[at, :] = cotangent_ref[0].astype(F32)
    agg_grad = moments_back(normed_ref[...], scaled_ref[:, 0:1], upstream_ref[...]).astype(BF16)
    all_sums = edge_backward(
        regions, agg_grad, hot_ref, turned_hot_ref, slope_ref, edge_grad_ref
    )
    for d, sums in enumerate(all_sums):
        for s in range(regions):
            first = s * slots + d * mesh_cap
            slot_ref[first : first + mesh_cap, :] = sums[s * mesh_cap : (s + 1) * mesh_cap]
        recv_ref[d * mesh_count : (d + 1) * mesh_count, :] = sums[slots:].astype(BF16)
    slot_sum = slot_ref[...].astype(BF16)
    columns = share_ref.shape[0]
    mine = pl.ds(pl.multiple_of(me * columns, columns), columns)
    share_ref[:, :latent] = dot_first(sent_ref[:, mine], slot_sum).astype(BF16)
    share_ref[:, latent:] = dot_first(first_ref[:, mine], recv_ref[...]).astype(BF16)
    halve(share_ref, keep_ref, give_ref)
    returned = dot(slot_sum, turned_ref[:, latent : 2 * latent]).astype(BF16)
    grad = upstream_ref[...] + dot(recv_ref[...], turned_ref[:, 2 * latent :])
    for s in range(regions):
        rows = slice(s * mesh_count, (s + 1) * mesh_count)
        mesh_grad_ref[rows, :] = grad[rows] + dot(
            hot_sent_ref[rows, :], returned[s * slots : (s + 1) * slots]
        )


def encode_back_kernel(
    regions,
    grid_ref,
    mesh_ref,
    hot_ref,
    turned_hot_ref,
    slope_ref,
    normed_ref,
    scaled_ref,
    mesh_grad_ref,
    own_slot_ref,
    keep_ref,
    give_ref,
    slot_ref,
    recv_ref,
    share_ref,
    edge_grad_ref,
):
    latent = mesh_ref.shape[1]
    mesh_count = mesh_ref.shape[0] // regions
    listed = grid_ref.shape[0] // regions
    capacity = listed // 3
    me = lax.axis_index("space")
    agg_grad = moments_back(normed_ref[...], scaled_ref[:, 0:1], mesh_grad_ref[...]).astype(BF16)
    blank = jnp.zeros((capacity, latent), BF16)
    slot_ref[0:capacity, :] = blank
    slot_ref[regions * listed - capacity :, :] = blank
    all_sums = edge_backward(
        regions, agg_grad, hot_ref, turned_hot_ref, slope_ref, edge_grad_ref
    )
    for d, sums in enumerate(all_sums):
        sums = sums.astype(BF16)
        for j in range(3):
            source = d + j - 1
            if 0 <= source < regions:
                first = source * listed + (2 - j) * capacity
                slot_ref[first : first + capacity, :] = sums[j * capacity : (j + 1) * capacity]
        recv_ref[d * mesh_count : (d + 1) * mesh_count, :] = sums[listed:]
    columns = share_ref.shape[0]
    mine = pl.ds(pl.multiple_of(me * columns, columns), columns)
    share_ref[:, :latent] = dot_first(grid_ref[:, mine], slot_ref[...]).astype(BF16)
    share_ref[:, latent:] = dot_first(mesh_ref[:, mine], recv_ref[...]).astype(BF16)
    halve(share_ref, keep_ref, give_ref)
    own = pl.ds(pl.multiple_of(me * listed, listed), listed)
    own_slot_ref[...] = slot_ref[own, :]


def grid_back_kernel(turned_ref, pick_ref, own_slot_ref, grid_grad_ref):
    lists, _, capacity = pick_ref.shape
    latent = own_slot_ref.shape[1]
    returned = dot(own_slot_ref[...], turned_ref[:, :latent]).astype(BF16)
    total = None
    for i in range(lists):
        owner = one_hot(pick_ref[i], grid_grad_ref.shape[1])
        part = dot(owner, returned[i * capacity : (i + 1) * capacity])
        total = part if total is None else total + part
    grid_grad_ref[0] = total.astype(BF16)


def place(pairs, stages, semaphores):
    copies = []
    for n, (block_ref, target) in enumerate(pairs):
        stages[n][...] = block_ref[...].astype(F32)
        copies.append(pltpu.make_async_copy(stages[n], target, semaphores.at[n]))
        copies[n].start()
    for copy in copies:
        copy.wait()


def half_rows(half):
    core = lax.bitwise_and(lax.axis_index("rep"), 1)
    mine = pl.ds(pl.multiple_of(core * half, half), half)
    return mine, pl.ds(pl.multiple_of((1 - core) * half, half), half)


def settle_kernel(one_ref, two_ref, other_two_ref, weight_grad_ref, *scratch):
    half, width = one_ref.shape
    mine, other = half_rows(half)
    place(
        [
            (two_ref, weight_grad_ref.at[mine, width:]),
            (other_two_ref, weight_grad_ref.at[other, width:]),
            (one_ref, weight_grad_ref.at[mine, :width]),
        ],
        scratch[:3],
        scratch[3],
    )


def finish_kernel(other_one_ref, settled_ref, weight_grad_ref, stage, semaphores):
    half, width = other_one_ref.shape
    _, other = half_rows(half)
    place([(other_one_ref, weight_grad_ref.at[other, :width])], [stage], semaphores)


VMEM = pl.BlockSpec(memory_space=pltpu.VMEM)


def call(kernel, operands, outputs, scratch, flops, fetched=0):
    hbm = pl.BlockSpec(memory_space=pltpu.HBM)
    operands = [
        pltpu.with_memory_space_constraint(operand, pltpu.HBM) if n < fetched else operand
        for n, operand in enumerate(operands)
    ]
    return pl.pallas_call(
        kernel,
        out_shape=[jax.ShapeDtypeStruct(shape, kind) for shape, kind in outputs],
        in_specs=[hbm] * fetched + [VMEM] * (len(operands) - fetched),
        out_specs=[VMEM] * len(outputs),
        scratch_shapes=[pltpu.VMEM(shape, kind) for shape, kind in scratch]
        + ([pltpu.SemaphoreType.DMA((fetched,))] if fetched else []),
        compiler_params=pltpu.CompilerParams(vmem_limit_bytes=40 << 20),
        cost_estimate=pl.CostEstimate(flops=flops, bytes_accessed=4 << 20, transcendentals=0),
    )(*operands)


def swap(block, axis, bits):
    return lax.ppermute(block, axis, [(i, i ^ bits) for i in range(lax.axis_size(axis))])


def added(left, right):
    return (left.astype(F32) + right.astype(F32)).astype(BF16)


def summed_over_chips(half):
    bit = 2
    while bit < lax.axis_size("rep"):
        half = added(half, swap(half, "rep", bit))
        bit *= 2
    return half


def whole_sample_body(
    grid_latent,
    mesh_latent,
    mesh_cotangent,
    weights,
    g2m_pick,
    g2m_sender,
    g2m_receiver,
    m2m_pick,
    m2m_sender,
    m2m_receiver,
):
    regions = lax.axis_size("space")
    latent = weights.shape[0]
    listed = g2m_pick.shape[1] * g2m_pick.shape[2]
    mesh_count = mesh_latent.shape[1]
    mesh_cap = m2m_pick.shape[2]
    edges = g2m_sender.shape[0]
    columns = latent // regions
    half = columns // 2
    g2m_pick = g2m_pick.transpose(1, 0, 2)
    sources = (
        grid_latent,
        mesh_latent,
        g2m_pick,
        g2m_sender.reshape(1, -1),
        g2m_receiver.reshape(1, -1),
        m2m_pick,
        m2m_sender.reshape(1, -1),
        m2m_receiver.reshape(1, -1),
    )
    packed = call(
        pack_kernel,
        sources,
        [((listed + mesh_count + INDEX_ROWS, latent), BF16)],
        [((INDEX_ROWS, latent), F32)] + [(source.shape, source.dtype) for source in sources],
        10**7,
        fetched=len(sources),
    )[0]
    packed, cotangent, weights = lax.optimization_barrier((packed, mesh_cotangent, weights))
    steps = (0, *range(2, regions), 1)
    packs = [packed] + [swap(packed, "space", step) for step in steps[1:]]
    near = swap(cotangent, "space", 1)
    weights, turned = call(
        weights_kernel,
        (weights,),
        [(weights.shape, BF16), ((latent, 3 * latent), BF16)],
        [],
        10**8,
        fetched=1,
    )
    packs[1], cotangent = lax.optimization_barrier((packs[1], cotangent))
    cotangents = [cotangent] + [swap(cotangent, "space", step) for step in steps[1:-1]] + [near]
    rows = regions * mesh_count
    slots = regions * mesh_cap
    (
        mesh_out,
        grid_all,
        mesh_all,
        mesh_first,
        mesh_sent,
        hot_one,
        hot_two,
        turned_one,
        turned_two,
        hot_sent,
        slope_one,
        slope_two,
        normed_one,
        scaled_one,
        normed_two,
        scaled_two,
    ) = call(
        functools.partial(forward_kernel, steps, listed, mesh_count, mesh_cap),
        (*packs, weights),
        [
            (mesh_latent.shape, BF16),
            ((regions * listed, latent), BF16),
            ((rows, latent), BF16),
            ((rows, latent), BF16),
            ((regions * slots, latent), BF16),
            ((regions * (listed + mesh_count), edges), BF16),
            ((regions * (slots + mesh_count), edges), BF16),
            ((regions * edges, listed + mesh_count), BF16),
            ((regions * edges, slots + mesh_count), BF16),
            ((rows, slots), BF16),
            ((regions * edges, latent), BF16),
            ((regions * edges, latent), BF16),
            ((rows, latent), F32),
            ((rows, 128), F32),
            ((rows, latent), F32),
            ((rows, 128), F32),
        ],
        [
            ((regions * INDEX_ROWS, latent), F32),
            ((regions * edges, latent), BF16),
            ((rows, latent), F32),
        ],
        2 * 10**9,
    )
    mesh_grad, keep_two, give_two = call(
        functools.partial(process_back_kernel, steps, mesh_cap),
        (
            *cotangents,
            turned,
            mesh_first,
            mesh_sent,
            hot_two,
            turned_two,
            hot_sent,
            slope_two,
            normed_two,
            scaled_two,
        ),
        [((rows, latent), F32)] + [((half, 2 * latent), BF16)] * 2,
        [
            ((rows, latent), F32),
            ((regions * slots, latent), F32),
            ((rows, latent), BF16),
            ((columns, 2 * latent), BF16),
            ((regions * edges, latent), BF16),
        ],
        10**9,
    )
    own_slots, keep_one, give_one = call(
        functools.partial(encode_back_kernel, regions),
        (
            grid_all,
            mesh_all,
            hot_one,
            turned_one,
            slope_one,
            normed_one,
            scaled_one,
            mesh_grad,
        ),
        [((listed, latent), BF16)] + [((half, 2 * latent), BF16)] * 2,
        [
            ((regions * listed, latent), BF16),
            ((rows, latent), BF16),
            ((columns, 2 * latent), BF16),
            ((regions * edges, latent), BF16),
        ],
        10**9,
    )
    half_one = added(keep_one, swap(give_one, "rep", 1))
    half_two = added(keep_two, swap(give_two, "rep", 1))
    half_one, own_slots = lax.optimization_barrier((half_one, own_slots))
    grid_grad = call(
        grid_back_kernel,
        (turned, g2m_pick, own_slots),
        [(grid_latent.shape, BF16)],
        [],
        10**8,
    )[0]
    two = summed_over_chips(half_two)
    one, grid_grad = lax.optimization_barrier((summed_over_chips(half_one), grid_grad))
    hbm = pl.BlockSpec(memory_space=pltpu.HBM)
    stage = pltpu.VMEM((half, 2 * latent), F32)
    weight_shape = pltpu.HBM((columns, 4 * latent), F32)
    limit = pltpu.CompilerParams(vmem_limit_bytes=40 << 20)
    settled = pl.pallas_call(
        settle_kernel,
        out_shape=weight_shape,
        in_specs=[VMEM] * 3,
        out_specs=hbm,
        scratch_shapes=[stage] * 3 + [pltpu.SemaphoreType.DMA((3,))],
        compiler_params=limit,
    )(one, two, swap(two, "rep", 1))
    weight_grad = pl.pallas_call(
        finish_kernel,
        out_shape=weight_shape,
        in_specs=[VMEM, hbm],
        out_specs=hbm,
        scratch_shapes=[stage, pltpu.SemaphoreType.DMA((1,))],
        input_output_aliases={1: 0},
        compiler_params=limit,
    )(swap(one, "rep", 1), settled)
    return (mesh_out, grid_grad, weight_grad)


def solution(mesh):
    regions = mesh.shape["space"]
    samples = mesh.shape["rep"]

    def whole(*arguments):
        edges = arguments[5].shape[0] + arguments[8].shape[0]
        latent = arguments[3].shape[0]
        fits = edges * latent * 4 <= SAMPLE_EDGE_BYTES and latent % (128 * regions) == 0
        paired = all(n > 1 and n & (n - 1) == 0 for n in (regions, samples))
        return sharded(whole_sample_body if fits and paired else partitioned_body)(*arguments)

    def sharded(body):
        return jax.shard_map(
            body,
            mesh=mesh,
            in_specs=(
                P(("groups", "rep"), "space", None),
                P(("groups", "rep"), "space", None),
                P(("groups", "rep"), "space", None),
                P(),
                P("space", None, None),
                P("space"),
                P("space"),
                P("space", None, None),
                P("space"),
                P("space"),
            ),
            out_specs=(
                P(("groups", "rep"), "space", None),
                P(("groups", "rep"), "space", None),
                P(("groups", "space"), None),
            ),
            check_vma=False,
        )

    return whole
```

```python
import functools

import jax
import jax.numpy as jnp
from jax import lax
from jax.experimental import pallas as pl
from jax.experimental.pallas import tpu as pltpu
from jax.sharding import PartitionSpec as P

EPSILON = 1e-05


def with_halo(cells, sides, width):
    for axis, dim in sides:
        count = lax.axis_size(axis)
        ends = count - 1
        head = lax.slice_in_dim(cells, 0, width, axis=dim)
        tail = lax.slice_in_dim(cells, cells.shape[dim] - width, cells.shape[dim], axis=dim)
        cells = jnp.concatenate(
            [
                lax.ppermute(tail, axis, [(i, (i + 1) % count) for i in range(ends)]),
                cells,
                lax.ppermute(head, axis, [((i + 1) % count, i) for i in range(ends)]),
            ],
            axis=dim,
        )
    return cells


def swish(values):
    return values * jax.nn.sigmoid(values)


def swish_slope(values):
    squash = jax.nn.sigmoid(values)
    return squash * (1.0 + values * (1.0 - squash))


def norm_rows(values):
    centred = values - jnp.mean(values, -1, keepdims=True)
    return centred * lax.rsqrt(jnp.mean(centred * centred, -1, keepdims=True) + EPSILON)


def norm_rows_back(values, upstream):
    centred = values - jnp.mean(values, -1, keepdims=True)
    scaled = lax.rsqrt(jnp.mean(centred * centred, -1, keepdims=True) + EPSILON)
    normed = centred * scaled
    return scaled * (
        upstream
        - jnp.mean(upstream, -1, keepdims=True)
        - normed * jnp.mean(upstream * normed, -1, keepdims=True)
    )


def slot_rows(pick_row):
    listed = pick_row.reshape(-1)
    return listed


def mesh_route(outgoing, capacity, peer_count):
    columns = outgoing.shape[1]
    pieces = lax.all_to_all(
        outgoing.reshape(peer_count, capacity, columns),
        "space",
        split_axis=0,
        concat_axis=0,
        tiled=True,
    )
    arrived = pieces.reshape(peer_count * capacity, columns)
    return arrived


def grid_route(outgoing, capacity):
    columns = outgoing.shape[1]
    lists = outgoing.reshape(3, capacity, columns)
    rims = with_halo(jnp.stack([lists[0], lists[2]]), (("space", 0),), 1)
    return jnp.concatenate([rims[0], lists[1], rims[3]], axis=0)


def edge_pass(arrived, recv_table, located, receiver, w_send, w_recv):
    recv_proj = jnp.dot(recv_table, w_recv, preferred_element_type=jnp.float32)
    slot_proj = jnp.dot(arrived, w_send, preferred_element_type=jnp.float32)
    activation = slot_proj[located] + recv_proj[receiver]
    message = swish(activation).astype(jnp.bfloat16)
    member = (
        receiver[None, :] == jnp.arange(recv_table.shape[0], dtype=jnp.int32)[:, None]
    ).astype(jnp.bfloat16)
    summed = jnp.dot(member, message, preferred_element_type=jnp.float32)
    return (activation, member, summed)


def backward_pass(slot_count, located, activation, member, receiver, agg_grad, w_send):
    edge_grad = (agg_grad[receiver] * swish_slope(activation)).astype(jnp.bfloat16)
    recv_sum = jnp.dot(member, edge_grad, preferred_element_type=jnp.float32).astype(jnp.bfloat16)
    slot_member = (located[None, :] == jnp.arange(slot_count, dtype=jnp.int32)[:, None]).astype(
        jnp.bfloat16
    )
    slot_sum = jnp.dot(slot_member, edge_grad, preferred_element_type=jnp.float32).astype(
        jnp.bfloat16
    )
    returned = jnp.dot(slot_sum, w_send.T, preferred_element_type=jnp.float32).astype(jnp.bfloat16)
    return (recv_sum, slot_sum, returned)


def gather_back(listed, back_rows, row_count):
    owner = (listed[None, :] == jnp.arange(row_count, dtype=jnp.int32)[:, None]).astype(
        jnp.bfloat16
    )
    return jnp.dot(owner, back_rows, preferred_element_type=jnp.float32)


def partitioned_body(
    grid_latent,
    mesh_latent,
    mesh_cotangent,
    weights,
    g2m_pick,
    g2m_sender,
    g2m_receiver,
    m2m_pick,
    m2m_sender,
    m2m_receiver,
):
    grid_rows = grid_latent[0]
    mesh_rows = mesh_latent[0]
    upstream = mesh_cotangent[0].astype(jnp.float32)
    latent = weights.shape[0]
    encode_sender = weights[:, :latent]
    encode_receiver = weights[:, latent : 2 * latent]
    process_sender = weights[:, 2 * latent : 3 * latent]
    process_receiver = weights[:, 3 * latent :]
    peer_count = lax.axis_size("space")
    grid_cap = g2m_pick.shape[2]
    mesh_cap = m2m_pick.shape[2]
    grid_listed = g2m_pick[0].reshape(-1)
    grid_arrived = grid_route(grid_rows[grid_listed], grid_cap)
    act_first, member_first, summed_first = edge_pass(
        grid_arrived, mesh_rows, g2m_sender, g2m_receiver, encode_sender, encode_receiver
    )
    mesh_first = (mesh_rows.astype(jnp.float32) + norm_rows(summed_first)).astype(jnp.bfloat16)
    mesh_listed = slot_rows(m2m_pick[0])
    mesh_arrived = mesh_route(mesh_first[mesh_listed], mesh_cap, peer_count)
    act_second, member_second, summed_second = edge_pass(
        mesh_arrived, mesh_first, m2m_sender, m2m_receiver, process_sender, process_receiver
    )
    mesh_final = (mesh_first.astype(jnp.float32) + norm_rows(summed_second)).astype(jnp.bfloat16)
    agg_second = norm_rows_back(summed_second, upstream)
    recv_second, slot_second, returned_second = backward_pass(
        mesh_arrived.shape[0],
        m2m_sender,
        act_second,
        member_second,
        m2m_receiver,
        agg_second,
        process_sender,
    )
    back_second = mesh_route(returned_second, mesh_cap, peer_count)
    mesh_grad = upstream + jnp.dot(
        recv_second, process_receiver.T, preferred_element_type=jnp.float32
    )
    mesh_grad = mesh_grad + gather_back(mesh_listed, back_second, mesh_rows.shape[0])
    agg_first = norm_rows_back(summed_first, mesh_grad)
    recv_first, slot_first, returned_first = backward_pass(
        grid_arrived.shape[0],
        g2m_sender,
        act_first,
        member_first,
        g2m_receiver,
        agg_first,
        encode_sender,
    )
    back_first = grid_route(returned_first, grid_cap)
    grid_grad = gather_back(grid_listed, back_first, grid_rows.shape[0]).astype(jnp.bfloat16)
    factor_pairs = (
        (grid_arrived, slot_first),
        (mesh_rows, recv_first),
        (mesh_arrived, slot_second),
        (mesh_first, recv_second),
    )
    blocks = []
    for first_factor, second_factor in factor_pairs:
        blocks.append(
            lax.dot_general(
                first_factor,
                second_factor,
                (((0,), (0,)), ((), ())),
                preferred_element_type=jnp.float32,
            )
        )
    shares = lax.psum_scatter(
        jnp.concatenate(blocks, axis=1).astype(jnp.bfloat16),
        "space",
        scatter_dimension=0,
        tiled=True,
    )
    weight_grad = lax.psum(shares, "rep").astype(jnp.float32)
    return (mesh_final[None], grid_grad[None], weight_grad)


F32 = jnp.float32
BF16 = jnp.bfloat16
INDEX_ROWS = 8
SAMPLE_EDGE_BYTES = 8 << 20


def dot(left, right):
    return jnp.dot(left, right, preferred_element_type=F32)


def dot_first(left, right):
    return lax.dot_general(left, right, (((0,), (0,)), ((), ())), preferred_element_type=F32)


def one_hot(labels, count):
    rows = lax.broadcasted_iota(jnp.int32, (count, labels.shape[-1]), 0)
    return (rows == labels).astype(F32).astype(BF16)


def row_moments(values):
    centred = values - jnp.mean(values, -1, keepdims=True)
    return centred, lax.rsqrt(jnp.mean(centred * centred, -1, keepdims=True) + EPSILON)


def moments_back(normed, scaled, upstream):
    return scaled * (
        upstream
        - jnp.mean(upstream, -1, keepdims=True)
        - normed * jnp.mean(upstream * normed, -1, keepdims=True)
    )


def fetch(pairs, semaphores):
    copies = [
        pltpu.make_async_copy(source, target, semaphores.at[n])
        for n, (source, target) in enumerate(pairs)
    ]
    for copy in copies:
        copy.start()
    for copy in copies:
        copy.wait()


def pack_kernel(*refs):
    sources, packed_ref, index_ref = refs[:8], refs[8], refs[9]
    local, semaphores = refs[10:18], refs[18]
    fetch(list(zip(sources, local)), semaphores)
    (
        grid_ref,
        mesh_ref,
        g2m_pick_ref,
        g2m_sender_ref,
        g2m_receiver_ref,
        m2m_pick_ref,
        m2m_sender_ref,
        m2m_receiver_ref,
    ) = local
    lists, _, capacity = g2m_pick_ref.shape
    mesh_count = mesh_ref.shape[1]
    regions, mesh_cap = m2m_pick_ref.shape[1:]
    edges = g2m_sender_ref.shape[1]
    grid_rows = grid_ref[0]
    for i in range(lists):
        picked = one_hot(g2m_pick_ref[i], grid_rows.shape[0])
        packed_ref[i * capacity : (i + 1) * capacity, :] = dot_first(picked, grid_rows).astype(BF16)
    first = lists * capacity
    packed_ref[first : first + mesh_count, :] = mesh_ref[0]
    index_ref[...] = jnp.zeros_like(index_ref)
    index_ref[0:1, 0:edges] = g2m_sender_ref[...].astype(F32)
    index_ref[0:1, edges : 2 * edges] = g2m_receiver_ref[...].astype(F32)
    index_ref[1:2, 0:edges] = m2m_sender_ref[...].astype(F32)
    index_ref[1:2, edges : 2 * edges] = m2m_receiver_ref[...].astype(F32)
    slots = regions * mesh_cap
    lane = lax.broadcasted_iota(jnp.int32, (mesh_cap, slots), 1)
    spread = (lane % mesh_cap == lax.broadcasted_iota(jnp.int32, (mesh_cap, slots), 0)).astype(F32)
    spread = dot(m2m_pick_ref[0].astype(F32).astype(BF16), spread.astype(BF16))
    lane = lax.broadcasted_iota(jnp.int32, (regions, slots), 1)
    owned = lane // mesh_cap == lax.broadcasted_iota(jnp.int32, (regions, slots), 0)
    index_ref[2:3, 0:slots] = jnp.sum(jnp.where(owned, spread, 0.0), 0, keepdims=True)
    packed_ref[first + mesh_count :, :] = index_ref[...].astype(BF16)


def weights_kernel(source_ref, weights_ref, turned_ref, semaphores):
    fetch([(source_ref, weights_ref)], semaphores)
    latent = weights_ref.shape[0]
    for n, block in enumerate((0, 2, 3)):
        turned_ref[:, n * latent : (n + 1) * latent] = weights_ref[
            :, block * latent : (block + 1) * latent
        ].T


def edge_blocks(edges):
    size = min(edges, 128)
    return [(first, min(size, edges - first)) for first in range(0, edges, size)]


def edge_forward(tables, hot_ref, turned_hot_ref, slope_ref, message_ref, mesh_count):
    regions = len(tables)
    edges = slope_ref.shape[0] // regions
    count = hot_ref.shape[0] // regions
    work = [(d, first, size) for d in range(regions) for first, size in edge_blocks(edges)]

    def gathered(d, first, size):
        rows = slice(d * edges + first, d * edges + first + size)
        return dot(turned_hot_ref[rows, :], tables[d])

    sums = []
    activation = gathered(*work[0])
    for n, (d, first, size) in enumerate(work):
        coming = gathered(*work[n + 1]) if n + 1 < len(work) else None
        activation = activation.astype(BF16)
        squash = 0.5 + 0.5 * jnp.tanh(0.5 * activation)
        message = activation * squash
        rows = slice(d * edges + first, d * edges + first + size)
        slope_ref[rows, :] = squash + message * (1.0 - squash)
        message_ref[rows, :] = message
        activation = coming
        if first + size == edges:
            hot = hot_ref[(d + 1) * count - mesh_count : (d + 1) * count, :]
            sums.append(dot(hot, message_ref[d * edges : (d + 1) * edges, :]))
    return sums


def forward_kernel(
    steps,
    listed,
    mesh_count,
    mesh_cap,
    *refs,
):
    regions = len(steps)
    packed_refs = refs[:regions]
    (
        weights_ref,
        mesh_out_ref,
        grid_ref,
        mesh_ref,
        first_ref,
        sent_ref,
        hot_one_ref,
        hot_two_ref,
        turned_one_ref,
        turned_two_ref,
        hot_sent_ref,
        slope_one_ref,
        slope_two_ref,
        normed_one_ref,
        scaled_one_ref,
        normed_two_ref,
        scaled_two_ref,
        index_ref,
        message_ref,
        sum_ref,
    ) = refs[regions:]
    latent = weights_ref.shape[0]
    edges = slope_one_ref.shape[0] // regions
    capacity = listed // 3
    slots = regions * mesh_cap
    me = lax.axis_index("space")
    for step, packed_ref in zip(steps, packed_refs):
        region = lax.bitwise_xor(me, step)
        at = lambda rows: pl.ds(pl.multiple_of(region * rows, rows), rows)
        grid_ref[at(listed), :] = packed_ref[:listed, :]
        mesh_ref[at(mesh_count), :] = packed_ref[listed : listed + mesh_count, :]
        index_ref[at(INDEX_ROWS), :] = packed_ref[listed + mesh_count :, :].astype(F32)

    grid_proj = dot(grid_ref[...], weights_ref[:, :latent])
    mesh_proj = dot(mesh_ref[...], weights_ref[:, latent : 2 * latent])
    for d in range(regions):
        index = index_ref[d * INDEX_ROWS : (d + 1) * INDEX_ROWS, :].astype(jnp.int32)
        for row, senders, hot_ref, turned_ref in (
            (0, listed, hot_one_ref, turned_one_ref),
            (1, slots, hot_two_ref, turned_two_ref),
        ):
            count = senders + mesh_count
            hot = jnp.concatenate(
                [
                    one_hot(index[row : row + 1, :edges], senders),
                    one_hot(index[row : row + 1, edges:], mesh_count),
                ],
                axis=0,
            )
            hot_ref[d * count : (d + 1) * count, :] = hot
            turned_ref[d * edges : (d + 1) * edges, :] = hot.T
        hot_sent_ref[d * mesh_count : (d + 1) * mesh_count, :] = one_hot(
            index[2:3, :slots], mesh_count
        )

    blank = jnp.zeros((capacity, latent), F32)
    tables = []
    for d in range(regions):
        before = (d - 1) * listed + 2 * capacity
        within = d * listed + capacity
        after = (d + 1) * listed
        tables.append(
            jnp.concatenate(
                [
                    grid_proj[before : before + capacity] if d > 0 else blank,
                    grid_proj[within : within + capacity],
                    grid_proj[after : after + capacity] if d < regions - 1 else blank,
                    mesh_proj[d * mesh_count : (d + 1) * mesh_count],
                ],
                axis=0,
            ).astype(BF16)
        )
    sums = edge_forward(
        tables, hot_one_ref, turned_one_ref, slope_one_ref, message_ref, mesh_count
    )
    for d in range(regions):
        sum_ref[d * mesh_count : (d + 1) * mesh_count, :] = sums[d]
    centred, scaled = row_moments(sum_ref[...])
    normed = centred * scaled
    normed_one_ref[...] = normed
    scaled_one_ref[...] = jnp.broadcast_to(scaled, scaled_one_ref.shape)
    first_ref[...] = (mesh_ref[...].astype(F32) + normed).astype(BF16)

    for s in range(regions):
        rows = slice(s * mesh_count, (s + 1) * mesh_count)
        sent_ref[s * slots : (s + 1) * slots, :] = dot_first(
            hot_sent_ref[rows, :], first_ref[rows, :]
        ).astype(BF16)
    sent_proj = dot(sent_ref[...], weights_ref[:, 2 * latent : 3 * latent])
    first_proj = dot(first_ref[...], weights_ref[:, 3 * latent :])
    tables = []
    for d in range(regions):
        pieces = [
            sent_proj[s * slots + d * mesh_cap : s * slots + (d + 1) * mesh_cap]
            for s in range(regions)
        ]
        tables.append(
            jnp.concatenate(
                pieces + [first_proj[d * mesh_count : (d + 1) * mesh_count]], axis=0
            ).astype(BF16)
        )
    sums = edge_forward(
        tables, hot_two_ref, turned_two_ref, slope_two_ref, message_ref, mesh_count
    )
    for d in range(regions):
        sum_ref[d * mesh_count : (d + 1) * mesh_count, :] = sums[d]
    centred, scaled = row_moments(sum_ref[...])
    normed_two_ref[...] = centred * scaled
    scaled_two_ref[...] = jnp.broadcast_to(scaled, scaled_two_ref.shape)
    own = pl.ds(pl.multiple_of(me * mesh_count, mesh_count), mesh_count)
    mesh_out_ref[0] = (first_ref[own, :].astype(F32) + normed_two_ref[own, :]).astype(BF16)


def edge_backward(regions, agg_grad_ref, hot_ref, turned_hot_ref, slope_ref, edge_grad_ref):
    mesh_count = agg_grad_ref.shape[0] // len(regions)
    edges = edge_grad_ref.shape[0] // len(regions)
    count = turned_hot_ref.shape[1]
    blank = jnp.zeros((count - mesh_count, agg_grad_ref.shape[1]), BF16)
    work = [(n, first, size) for n in range(len(regions)) for first, size in edge_blocks(edges)]

    def at(n, first, size):
        return pl.ds(pl.multiple_of(regions[n] * edges + first, size), size)

    def gathered(n, first, size):
        own = agg_grad_ref[n * mesh_count : (n + 1) * mesh_count, :]
        return dot(turned_hot_ref[at(n, first, size), :], jnp.concatenate([blank, own], axis=0))

    sums = []
    upstream = gathered(*work[0])
    for k, (n, first, size) in enumerate(work):
        coming = gathered(*work[k + 1]) if k + 1 < len(work) else None
        rows = slice(n * edges + first, n * edges + first + size)
        edge_grad_ref[rows, :] = upstream.astype(BF16) * slope_ref[at(n, first, size), :]
        upstream = coming
        if first + size == edges:
            hot = hot_ref[pl.ds(pl.multiple_of(regions[n] * count, count), count), :]
            sums.append(dot(hot, edge_grad_ref[n * edges : (n + 1) * edges, :]))
    return sums


def halve(share_ref, keep_ref, give_ref):
    half = keep_ref.shape[0]
    core = lax.bitwise_and(lax.axis_index("rep"), 1)
    keep_ref[...] = share_ref[pl.ds(pl.multiple_of(core * half, half), half), :]
    give_ref[...] = share_ref[pl.ds(pl.multiple_of((1 - core) * half, half), half), :]


def process_back_part(
    steps, mesh_count, cotangent_refs, hot_ref, turned_hot_ref, slope_ref, normed_ref, scaled_ref,
    agg_grad_ref, edge_grad_ref,
):
    me = lax.axis_index("space")
    regions = [lax.bitwise_xor(me, step) for step in steps]
    for n, (region, cotangent_ref) in enumerate(zip(regions, cotangent_refs)):
        rows = pl.ds(pl.multiple_of(region * mesh_count, mesh_count), mesh_count)
        agg_grad_ref[n * mesh_count : (n + 1) * mesh_count, :] = moments_back(
            normed_ref[rows, :], scaled_ref[rows, 0:1], cotangent_ref[0].astype(F32)
        ).astype(BF16)
    return regions, edge_backward(
        regions, agg_grad_ref, hot_ref, turned_hot_ref, slope_ref, edge_grad_ref
    )


def near_back_kernel(steps, *refs):
    cotangent_refs, refs = refs[: len(steps)], refs[len(steps) :]
    (
        hot_ref,
        turned_hot_ref,
        slope_ref,
        normed_ref,
        scaled_ref,
        *whole_refs,
    ) = refs[:9]
    sums_ref, *column_refs = refs[9:14]
    agg_grad_ref, edge_grad_ref = refs[14:]
    mesh_count = agg_grad_ref.shape[0] // len(steps)
    count = turned_hot_ref.shape[1]
    _, all_sums = process_back_part(
        steps, mesh_count, cotangent_refs, hot_ref, turned_hot_ref, slope_ref, normed_ref,
        scaled_ref, agg_grad_ref, edge_grad_ref,
    )
    for n, sums in enumerate(all_sums):
        sums_ref[n * count : (n + 1) * count, :] = sums
    columns = column_refs[0].shape[0]
    mine = pl.ds(pl.multiple_of(lax.axis_index("space") * columns, columns), columns)
    for whole_ref, column_ref in zip(whole_refs, column_refs):
        column_ref[...] = whole_ref[:, mine].T


def far_back_kernel(near, far, mesh_cap, *refs):
    regions = len(near) + len(far)
    cotangent_refs, refs = refs[:regions], refs[regions:]
    (
        turned_ref,
        first_columns_ref,
        sent_columns_ref,
        near_sums_ref,
        hot_ref,
        turned_hot_ref,
        hot_sent_ref,
        slope_ref,
        normed_ref,
        scaled_ref,
        mesh_grad_ref,
        keep_ref,
        give_ref,
        upstream_ref,
        slot_ref,
        recv_ref,
        share_ref,
        agg_grad_ref,
        edge_grad_ref,
    ) = refs
    latent = normed_ref.shape[1]
    mesh_count = normed_ref.shape[0] // regions
    count = turned_hot_ref.shape[1]
    slots = regions * mesh_cap
    me = lax.axis_index("space")
    far_regions, all_sums = process_back_part(
        far, mesh_count, cotangent_refs[len(near) :], hot_ref, turned_hot_ref, slope_ref,
        normed_ref, scaled_ref, agg_grad_ref, edge_grad_ref,
    )
    near_regions = [lax.bitwise_xor(me, step) for step in near]
    near_sums = [near_sums_ref[n * count : (n + 1) * count, :] for n in range(len(near))]
    for region, sums in zip(near_regions + far_regions, near_sums + all_sums):
        for s in range(regions):
            slot_ref[pl.ds(pl.multiple_of(s * slots + region * mesh_cap, mesh_cap), mesh_cap), :] = (
                sums[s * mesh_cap : (s + 1) * mesh_cap]
            )
        recv_ref[pl.ds(pl.multiple_of(region * mesh_count, mesh_count), mesh_count), :] = sums[
            slots:
        ].astype(BF16)
    for region, cotangent_ref in zip(near_regions + far_regions, cotangent_refs):
        rows = pl.ds(pl.multiple_of(region * mesh_count, mesh_count), mesh_count)
        upstream_ref[rows, :] = cotangent_ref[0].astype(F32)
    slot_sum = slot_ref[...].astype(BF16)
    share_ref[:, :latent] = dot(sent_columns_ref[...], slot_sum).astype(BF16)
    share_ref[:, latent:] = dot(first_columns_ref[...], recv_ref[...]).astype(BF16)
    halve(share_ref, keep_ref, give_ref)
    returned = dot(slot_sum, turned_ref[:, latent : 2 * latent]).astype(BF16)
    grad = upstream_ref[...] + dot(recv_ref[...], turned_ref[:, 2 * latent :])
    for s in range(regions):
        rows = slice(s * mesh_count, (s + 1) * mesh_count)
        mesh_grad_ref[rows, :] = grad[rows] + dot(
            hot_sent_ref[rows, :], returned[s * slots : (s + 1) * slots]
        )


def encode_back_kernel(
    regions,
    grid_columns_ref,
    mesh_columns_ref,
    hot_ref,
    turned_hot_ref,
    slope_ref,
    normed_ref,
    scaled_ref,
    mesh_grad_ref,
    own_slot_ref,
    keep_ref,
    give_ref,
    slot_ref,
    recv_ref,
    share_ref,
    agg_grad_ref,
    edge_grad_ref,
):
    latent = normed_ref.shape[1]
    mesh_count = normed_ref.shape[0] // regions
    listed = slot_ref.shape[0] // regions
    capacity = listed // 3
    me = lax.axis_index("space")
    agg_grad_ref[...] = moments_back(
        normed_ref[...], scaled_ref[:, 0:1], mesh_grad_ref[...]
    ).astype(BF16)
    blank = jnp.zeros((capacity, latent), BF16)
    slot_ref[0:capacity, :] = blank
    slot_ref[regions * listed - capacity :, :] = blank
    all_sums = edge_backward(
        range(regions), agg_grad_ref, hot_ref, turned_hot_ref, slope_ref, edge_grad_ref
    )
    for d, sums in enumerate(all_sums):
        sums = sums.astype(BF16)
        for j in range(3):
            source = d + j - 1
            if 0 <= source < regions:
                first = source * listed + (2 - j) * capacity
                slot_ref[first : first + capacity, :] = sums[j * capacity : (j + 1) * capacity]
        recv_ref[d * mesh_count : (d + 1) * mesh_count, :] = sums[listed:]
    share_ref[:, :latent] = dot(grid_columns_ref[...], slot_ref[...]).astype(BF16)
    share_ref[:, latent:] = dot(mesh_columns_ref[...], recv_ref[...]).astype(BF16)
    halve(share_ref, keep_ref, give_ref)
    own = pl.ds(pl.multiple_of(me * listed, listed), listed)
    own_slot_ref[...] = slot_ref[own, :]


def grid_back_kernel(turned_ref, pick_ref, own_slot_ref, grid_grad_ref):
    lists, _, capacity = pick_ref.shape
    latent = own_slot_ref.shape[1]
    returned = dot(own_slot_ref[...], turned_ref[:, :latent]).astype(BF16)
    total = None
    for i in range(lists):
        owner = one_hot(pick_ref[i], grid_grad_ref.shape[1])
        part = dot(owner, returned[i * capacity : (i + 1) * capacity])
        total = part if total is None else total + part
    grid_grad_ref[0] = total.astype(BF16)


def place(pairs, stages, semaphores):
    copies = []
    for n, (block_ref, target) in enumerate(pairs):
        stages[n][...] = block_ref[...].astype(F32)
        copies.append(pltpu.make_async_copy(stages[n], target, semaphores.at[n]))
        copies[n].start()
    for copy in copies:
        copy.wait()


def half_rows(half):
    core = lax.bitwise_and(lax.axis_index("rep"), 1)
    mine = pl.ds(pl.multiple_of(core * half, half), half)
    return mine, pl.ds(pl.multiple_of((1 - core) * half, half), half)


def settle_kernel(one_ref, two_ref, other_two_ref, weight_grad_ref, *scratch):
    half, width = one_ref.shape
    mine, other = half_rows(half)
    place(
        [
            (two_ref, weight_grad_ref.at[mine, width:]),
            (other_two_ref, weight_grad_ref.at[other, width:]),
            (one_ref, weight_grad_ref.at[mine, :width]),
        ],
        scratch[:3],
        scratch[3],
    )


def finish_kernel(other_one_ref, settled_ref, weight_grad_ref, stage, semaphores):
    half, width = other_one_ref.shape
    _, other = half_rows(half)
    place([(other_one_ref, weight_grad_ref.at[other, :width])], [stage], semaphores)


VMEM = pl.BlockSpec(memory_space=pltpu.VMEM)


def call(kernel, operands, outputs, scratch, flops, fetched=0):
    hbm = pl.BlockSpec(memory_space=pltpu.HBM)
    operands = [
        pltpu.with_memory_space_constraint(operand, pltpu.HBM) if n < fetched else operand
        for n, operand in enumerate(operands)
    ]
    return pl.pallas_call(
        kernel,
        out_shape=[jax.ShapeDtypeStruct(shape, kind) for shape, kind in outputs],
        in_specs=[hbm] * fetched + [VMEM] * (len(operands) - fetched),
        out_specs=[VMEM] * len(outputs),
        scratch_shapes=[pltpu.VMEM(shape, kind) for shape, kind in scratch]
        + ([pltpu.SemaphoreType.DMA((fetched,))] if fetched else []),
        compiler_params=pltpu.CompilerParams(vmem_limit_bytes=40 << 20),
        cost_estimate=pl.CostEstimate(flops=flops, bytes_accessed=4 << 20, transcendentals=0),
    )(*operands)


def swap(block, axis, bits):
    return lax.ppermute(block, axis, [(i, i ^ bits) for i in range(lax.axis_size(axis))])


def added(left, right):
    return (left.astype(F32) + right.astype(F32)).astype(BF16)


def summed_over_chips(half):
    bit = 2
    while bit < lax.axis_size("rep"):
        half = added(half, swap(half, "rep", bit))
        bit *= 2
    return half


def whole_sample_body(
    grid_latent,
    mesh_latent,
    mesh_cotangent,
    weights,
    g2m_pick,
    g2m_sender,
    g2m_receiver,
    m2m_pick,
    m2m_sender,
    m2m_receiver,
):
    regions = lax.axis_size("space")
    latent = weights.shape[0]
    listed = g2m_pick.shape[1] * g2m_pick.shape[2]
    mesh_count = mesh_latent.shape[1]
    mesh_cap = m2m_pick.shape[2]
    edges = g2m_sender.shape[0]
    columns = latent // regions
    half = columns // 2
    g2m_pick = g2m_pick.transpose(1, 0, 2)
    sources = (
        grid_latent,
        mesh_latent,
        g2m_pick,
        g2m_sender.reshape(1, -1),
        g2m_receiver.reshape(1, -1),
        m2m_pick,
        m2m_sender.reshape(1, -1),
        m2m_receiver.reshape(1, -1),
    )
    packed = call(
        pack_kernel,
        sources,
        [((listed + mesh_count + INDEX_ROWS, latent), BF16)],
        [((INDEX_ROWS, latent), F32)] + [(source.shape, source.dtype) for source in sources],
        10**7,
        fetched=len(sources),
    )[0]
    packed, cotangent, weights = lax.optimization_barrier((packed, mesh_cotangent, weights))
    steps = (0, *range(2, regions), 1)
    packs = [packed] + [swap(packed, "space", step) for step in steps[1:]]
    near = swap(cotangent, "space", 1)
    weights, turned = call(
        weights_kernel,
        (weights,),
        [(weights.shape, BF16), ((latent, 3 * latent), BF16)],
        [],
        10**8,
        fetched=1,
    )
    packs[1], cotangent = lax.optimization_barrier((packs[1], cotangent))
    cotangents = [cotangent] + [swap(cotangent, "space", step) for step in steps[1:-1]] + [near]
    rows = regions * mesh_count
    slots = regions * mesh_cap
    (
        mesh_out,
        grid_all,
        mesh_all,
        mesh_first,
        mesh_sent,
        hot_one,
        hot_two,
        turned_one,
        turned_two,
        hot_sent,
        slope_one,
        slope_two,
        normed_one,
        scaled_one,
        normed_two,
        scaled_two,
    ) = call(
        functools.partial(forward_kernel, steps, listed, mesh_count, mesh_cap),
        (*packs, weights),
        [
            (mesh_latent.shape, BF16),
            ((regions * listed, latent), BF16),
            ((rows, latent), BF16),
            ((rows, latent), BF16),
            ((regions * slots, latent), BF16),
            ((regions * (listed + mesh_count), edges), BF16),
            ((regions * (slots + mesh_count), edges), BF16),
            ((regions * edges, listed + mesh_count), BF16),
            ((regions * edges, slots + mesh_count), BF16),
            ((rows, slots), BF16),
            ((regions * edges, latent), BF16),
            ((regions * edges, latent), BF16),
            ((rows, latent), F32),
            ((rows, 128), F32),
            ((rows, latent), F32),
            ((rows, 128), F32),
        ],
        [
            ((regions * INDEX_ROWS, latent), F32),
            ((regions * edges, latent), BF16),
            ((rows, latent), F32),
        ],
        2 * 10**9,
    )
    by_step = dict(zip(steps, cotangents))
    near, far = (0, 1), tuple(step for step in steps if step > 1)
    count = slots + mesh_count
    near_sums, grid_columns, mesh_columns, sent_columns, first_columns = call(
        functools.partial(near_back_kernel, near),
        (
            *(by_step[step] for step in near),
            hot_two,
            turned_two,
            slope_two,
            normed_two,
            scaled_two,
            grid_all,
            mesh_all,
            mesh_sent,
            mesh_first,
        ),
        [
            ((len(near) * count, latent), F32),
            ((columns, regions * listed), BF16),
            ((columns, rows), BF16),
            ((columns, regions * slots), BF16),
            ((columns, rows), BF16),
        ],
        [((len(near) * mesh_count, latent), BF16), ((len(near) * edges, latent), BF16)],
        10**9,
    )
    mesh_grad, keep_two, give_two = call(
        functools.partial(far_back_kernel, near, far, mesh_cap),
        (
            *(by_step[step] for step in near + far),
            turned,
            first_columns,
            sent_columns,
            near_sums,
            hot_two,
            turned_two,
            hot_sent,
            slope_two,
            normed_two,
            scaled_two,
        ),
        [((rows, latent), F32)] + [((half, 2 * latent), BF16)] * 2,
        [
            ((rows, latent), F32),
            ((regions * slots, latent), F32),
            ((rows, latent), BF16),
            ((columns, 2 * latent), BF16),
            ((len(far) * mesh_count, latent), BF16),
            ((len(far) * edges, latent), BF16),
        ],
        10**9,
    )
    own_slots, keep_one, give_one = call(
        functools.partial(encode_back_kernel, regions),
        (
            grid_columns,
            mesh_columns,
            hot_one,
            turned_one,
            slope_one,
            normed_one,
            scaled_one,
            mesh_grad,
        ),
        [((listed, latent), BF16)] + [((half, 2 * latent), BF16)] * 2,
        [
            ((regions * listed, latent), BF16),
            ((rows, latent), BF16),
            ((columns, 2 * latent), BF16),
            ((rows, latent), BF16),
            ((regions * edges, latent), BF16),
        ],
        10**9,
    )
    half_one = added(keep_one, swap(give_one, "rep", 1))
    half_two = added(keep_two, swap(give_two, "rep", 1))
    half_one, own_slots = lax.optimization_barrier((half_one, own_slots))
    grid_grad = call(
        grid_back_kernel,
        (turned, g2m_pick, own_slots),
        [(grid_latent.shape, BF16)],
        [],
        10**8,
    )[0]
    two = summed_over_chips(half_two)
    one, grid_grad = lax.optimization_barrier((summed_over_chips(half_one), grid_grad))
    hbm = pl.BlockSpec(memory_space=pltpu.HBM)
    stage = pltpu.VMEM((half, 2 * latent), F32)
    weight_shape = pltpu.HBM((columns, 4 * latent), F32)
    limit = pltpu.CompilerParams(vmem_limit_bytes=40 << 20)
    settled = pl.pallas_call(
        settle_kernel,
        out_shape=weight_shape,
        in_specs=[VMEM] * 3,
        out_specs=hbm,
        scratch_shapes=[stage] * 3 + [pltpu.SemaphoreType.DMA((3,))],
        compiler_params=limit,
    )(one, two, swap(two, "rep", 1))
    weight_grad = pl.pallas_call(
        finish_kernel,
        out_shape=weight_shape,
        in_specs=[VMEM, hbm],
        out_specs=hbm,
        scratch_shapes=[stage, pltpu.SemaphoreType.DMA((1,))],
        input_output_aliases={1: 0},
        compiler_params=limit,
    )(swap(one, "rep", 1), settled)
    return (mesh_out, grid_grad, weight_grad)


def solution(mesh):
    regions = mesh.shape["space"]
    samples = mesh.shape["rep"]

    def whole(*arguments):
        edges = arguments[5].shape[0] + arguments[8].shape[0]
        latent = arguments[3].shape[0]
        fits = edges * latent * 4 <= SAMPLE_EDGE_BYTES and latent % (128 * regions) == 0
        paired = regions > 2 and samples > 1 and not (regions & (regions - 1) | samples & (samples - 1))
        return sharded(whole_sample_body if fits and paired else partitioned_body)(*arguments)

    def sharded(body):
        return jax.shard_map(
            body,
            mesh=mesh,
            in_specs=(
                P(("groups", "rep"), "space", None),
                P(("groups", "rep"), "space", None),
                P(("groups", "rep"), "space", None),
                P(),
                P("space", None, None),
                P("space"),
                P("space"),
                P("space", None, None),
                P("space"),
                P("space"),
            ),
            out_specs=(
                P(("groups", "rep"), "space", None),
                P(("groups", "rep"), "space", None),
                P(("groups", "space"), None),
            ),
            check_vma=False,
        )

    return whole
```

```python
import functools

import jax
import jax.numpy as jnp
from jax import lax
from jax.experimental import pallas as pl
from jax.experimental.pallas import tpu as pltpu
from jax.sharding import PartitionSpec as P

EPSILON = 1e-05


def with_halo(cells, sides, width):
    for axis, dim in sides:
        count = lax.axis_size(axis)
        ends = count - 1
        head = lax.slice_in_dim(cells, 0, width, axis=dim)
        tail = lax.slice_in_dim(cells, cells.shape[dim] - width, cells.shape[dim], axis=dim)
        cells = jnp.concatenate(
            [
                lax.ppermute(tail, axis, [(i, (i + 1) % count) for i in range(ends)]),
                cells,
                lax.ppermute(head, axis, [((i + 1) % count, i) for i in range(ends)]),
            ],
            axis=dim,
        )
    return cells


def swish(values):
    return values * jax.nn.sigmoid(values)


def swish_slope(values):
    squash = jax.nn.sigmoid(values)
    return squash * (1.0 + values * (1.0 - squash))


def norm_rows(values):
    centred = values - jnp.mean(values, -1, keepdims=True)
    return centred * lax.rsqrt(jnp.mean(centred * centred, -1, keepdims=True) + EPSILON)


def norm_rows_back(values, upstream):
    centred = values - jnp.mean(values, -1, keepdims=True)
    scaled = lax.rsqrt(jnp.mean(centred * centred, -1, keepdims=True) + EPSILON)
    normed = centred * scaled
    return scaled * (
        upstream
        - jnp.mean(upstream, -1, keepdims=True)
        - normed * jnp.mean(upstream * normed, -1, keepdims=True)
    )


def slot_rows(pick_row):
    listed = pick_row.reshape(-1)
    return listed


def mesh_route(outgoing, capacity, peer_count):
    columns = outgoing.shape[1]
    pieces = lax.all_to_all(
        outgoing.reshape(peer_count, capacity, columns),
        "space",
        split_axis=0,
        concat_axis=0,
        tiled=True,
    )
    arrived = pieces.reshape(peer_count * capacity, columns)
    return arrived


def grid_route(outgoing, capacity):
    columns = outgoing.shape[1]
    lists = outgoing.reshape(3, capacity, columns)
    rims = with_halo(jnp.stack([lists[0], lists[2]]), (("space", 0),), 1)
    return jnp.concatenate([rims[0], lists[1], rims[3]], axis=0)


def edge_pass(arrived, recv_table, located, receiver, w_send, w_recv):
    recv_proj = jnp.dot(recv_table, w_recv, preferred_element_type=jnp.float32)
    slot_proj = jnp.dot(arrived, w_send, preferred_element_type=jnp.float32)
    activation = slot_proj[located] + recv_proj[receiver]
    message = swish(activation).astype(jnp.bfloat16)
    member = (
        receiver[None, :] == jnp.arange(recv_table.shape[0], dtype=jnp.int32)[:, None]
    ).astype(jnp.bfloat16)
    summed = jnp.dot(member, message, preferred_element_type=jnp.float32)
    return (activation, member, summed)


def backward_pass(slot_count, located, activation, member, receiver, agg_grad, w_send):
    edge_grad = (agg_grad[receiver] * swish_slope(activation)).astype(jnp.bfloat16)
    recv_sum = jnp.dot(member, edge_grad, preferred_element_type=jnp.float32).astype(jnp.bfloat16)
    slot_member = (located[None, :] == jnp.arange(slot_count, dtype=jnp.int32)[:, None]).astype(
        jnp.bfloat16
    )
    slot_sum = jnp.dot(slot_member, edge_grad, preferred_element_type=jnp.float32).astype(
        jnp.bfloat16
    )
    returned = jnp.dot(slot_sum, w_send.T, preferred_element_type=jnp.float32).astype(jnp.bfloat16)
    return (recv_sum, slot_sum, returned)


def gather_back(listed, back_rows, row_count):
    owner = (listed[None, :] == jnp.arange(row_count, dtype=jnp.int32)[:, None]).astype(
        jnp.bfloat16
    )
    return jnp.dot(owner, back_rows, preferred_element_type=jnp.float32)


def partitioned_body(
    grid_latent,
    mesh_latent,
    mesh_cotangent,
    weights,
    g2m_pick,
    g2m_sender,
    g2m_receiver,
    m2m_pick,
    m2m_sender,
    m2m_receiver,
):
    grid_rows = grid_latent[0]
    mesh_rows = mesh_latent[0]
    upstream = mesh_cotangent[0].astype(jnp.float32)
    latent = weights.shape[0]
    encode_sender = weights[:, :latent]
    encode_receiver = weights[:, latent : 2 * latent]
    process_sender = weights[:, 2 * latent : 3 * latent]
    process_receiver = weights[:, 3 * latent :]
    peer_count = lax.axis_size("space")
    grid_cap = g2m_pick.shape[2]
    mesh_cap = m2m_pick.shape[2]
    grid_listed = g2m_pick[0].reshape(-1)
    grid_arrived = grid_route(grid_rows[grid_listed], grid_cap)
    act_first, member_first, summed_first = edge_pass(
        grid_arrived, mesh_rows, g2m_sender, g2m_receiver, encode_sender, encode_receiver
    )
    mesh_first = (mesh_rows.astype(jnp.float32) + norm_rows(summed_first)).astype(jnp.bfloat16)
    mesh_listed = slot_rows(m2m_pick[0])
    mesh_arrived = mesh_route(mesh_first[mesh_listed], mesh_cap, peer_count)
    act_second, member_second, summed_second = edge_pass(
        mesh_arrived, mesh_first, m2m_sender, m2m_receiver, process_sender, process_receiver
    )
    mesh_final = (mesh_first.astype(jnp.float32) + norm_rows(summed_second)).astype(jnp.bfloat16)
    agg_second = norm_rows_back(summed_second, upstream)
    recv_second, slot_second, returned_second = backward_pass(
        mesh_arrived.shape[0],
        m2m_sender,
        act_second,
        member_second,
        m2m_receiver,
        agg_second,
        process_sender,
    )
    back_second = mesh_route(returned_second, mesh_cap, peer_count)
    mesh_grad = upstream + jnp.dot(
        recv_second, process_receiver.T, preferred_element_type=jnp.float32
    )
    mesh_grad = mesh_grad + gather_back(mesh_listed, back_second, mesh_rows.shape[0])
    agg_first = norm_rows_back(summed_first, mesh_grad)
    recv_first, slot_first, returned_first = backward_pass(
        grid_arrived.shape[0],
        g2m_sender,
        act_first,
        member_first,
        g2m_receiver,
        agg_first,
        encode_sender,
    )
    back_first = grid_route(returned_first, grid_cap)
    grid_grad = gather_back(grid_listed, back_first, grid_rows.shape[0]).astype(jnp.bfloat16)
    factor_pairs = (
        (grid_arrived, slot_first),
        (mesh_rows, recv_first),
        (mesh_arrived, slot_second),
        (mesh_first, recv_second),
    )
    blocks = []
    for first_factor, second_factor in factor_pairs:
        blocks.append(
            lax.dot_general(
                first_factor,
                second_factor,
                (((0,), (0,)), ((), ())),
                preferred_element_type=jnp.float32,
            )
        )
    shares = lax.psum_scatter(
        jnp.concatenate(blocks, axis=1).astype(jnp.bfloat16),
        "space",
        scatter_dimension=0,
        tiled=True,
    )
    weight_grad = lax.psum(shares, "rep").astype(jnp.float32)
    return (mesh_final[None], grid_grad[None], weight_grad)


F32 = jnp.float32
BF16 = jnp.bfloat16
INDEX_ROWS = 8
SAMPLE_EDGE_BYTES = 8 << 20


def dot(left, right):
    return jnp.dot(left, right, preferred_element_type=F32)


def dot_first(left, right):
    return lax.dot_general(left, right, (((0,), (0,)), ((), ())), preferred_element_type=F32)


def one_hot(labels, count):
    rows = lax.broadcasted_iota(jnp.int32, (count, labels.shape[-1]), 0)
    return (rows == labels).astype(F32).astype(BF16)


def row_moments(values):
    centred = values - jnp.mean(values, -1, keepdims=True)
    return centred, lax.rsqrt(jnp.mean(centred * centred, -1, keepdims=True) + EPSILON)


def moments_back(normed, scaled, upstream):
    return scaled * (
        upstream
        - jnp.mean(upstream, -1, keepdims=True)
        - normed * jnp.mean(upstream * normed, -1, keepdims=True)
    )


def fetch(pairs, semaphores):
    copies = [
        pltpu.make_async_copy(source, target, semaphores.at[n])
        for n, (source, target) in enumerate(pairs)
    ]
    for copy in copies:
        copy.start()
    for copy in copies:
        copy.wait()


def pack_kernel(*refs):
    sources, packed_ref, index_ref = refs[:8], refs[8], refs[9]
    local, semaphores = refs[10:18], refs[18]
    fetch(list(zip(sources, local)), semaphores)
    (
        grid_ref,
        mesh_ref,
        g2m_pick_ref,
        g2m_sender_ref,
        g2m_receiver_ref,
        m2m_pick_ref,
        m2m_sender_ref,
        m2m_receiver_ref,
    ) = local
    lists, _, capacity = g2m_pick_ref.shape
    mesh_count = mesh_ref.shape[1]
    regions, mesh_cap = m2m_pick_ref.shape[1:]
    edges = g2m_sender_ref.shape[1]
    grid_rows = grid_ref[0]
    for i in range(lists):
        picked = one_hot(g2m_pick_ref[i], grid_rows.shape[0])
        packed_ref[i * capacity : (i + 1) * capacity, :] = dot_first(picked, grid_rows).astype(BF16)
    first = lists * capacity
    packed_ref[first : first + mesh_count, :] = mesh_ref[0]
    index_ref[...] = jnp.zeros_like(index_ref)
    index_ref[0:1, 0:edges] = g2m_sender_ref[...].astype(F32)
    index_ref[0:1, edges : 2 * edges] = g2m_receiver_ref[...].astype(F32)
    index_ref[1:2, 0:edges] = m2m_sender_ref[...].astype(F32)
    index_ref[1:2, edges : 2 * edges] = m2m_receiver_ref[...].astype(F32)
    slots = regions * mesh_cap
    lane = lax.broadcasted_iota(jnp.int32, (mesh_cap, slots), 1)
    spread = (lane % mesh_cap == lax.broadcasted_iota(jnp.int32, (mesh_cap, slots), 0)).astype(F32)
    spread = dot(m2m_pick_ref[0].astype(F32).astype(BF16), spread.astype(BF16))
    lane = lax.broadcasted_iota(jnp.int32, (regions, slots), 1)
    owned = lane // mesh_cap == lax.broadcasted_iota(jnp.int32, (regions, slots), 0)
    index_ref[2:3, 0:slots] = jnp.sum(jnp.where(owned, spread, 0.0), 0, keepdims=True)
    packed_ref[first + mesh_count :, :] = index_ref[...].astype(BF16)


def weights_kernel(source_ref, weights_ref, turned_ref, semaphores):
    fetch([(source_ref, weights_ref)], semaphores)
    latent = weights_ref.shape[0]
    for n, block in enumerate((0, 2, 3)):
        turned_ref[:, n * latent : (n + 1) * latent] = weights_ref[
            :, block * latent : (block + 1) * latent
        ].T


def edge_blocks(edges):
    size = min(edges, 128)
    return [(first, min(size, edges - first)) for first in range(0, edges, size)]


def edge_forward(tables, hot_ref, turned_hot_ref, slope_ref, message_ref, mesh_count):
    regions = len(tables)
    edges = slope_ref.shape[0] // regions
    count = hot_ref.shape[0] // regions
    work = [(d, first, size) for d in range(regions) for first, size in edge_blocks(edges)]

    def gathered(d, first, size):
        rows = slice(d * edges + first, d * edges + first + size)
        return dot(turned_hot_ref[rows, :], tables[d])

    sums = []
    activation = gathered(*work[0])
    for n, (d, first, size) in enumerate(work):
        coming = gathered(*work[n + 1]) if n + 1 < len(work) else None
        activation = activation.astype(BF16)
        squash = 0.5 + 0.5 * jnp.tanh(0.5 * activation)
        message = activation * squash
        rows = slice(d * edges + first, d * edges + first + size)
        slope_ref[rows, :] = squash + message * (1.0 - squash)
        message_ref[rows, :] = message
        activation = coming
        if first + size == edges:
            hot = hot_ref[(d + 1) * count - mesh_count : (d + 1) * count, :]
            sums.append(dot(hot, message_ref[d * edges : (d + 1) * edges, :]))
    return sums


def forward_kernel(
    steps,
    listed,
    mesh_count,
    mesh_cap,
    *refs,
):
    regions = len(steps)
    packed_refs = refs[:regions]
    (
        weights_ref,
        grid_ref,
        mesh_ref,
        first_ref,
        sent_ref,
        hot_one_ref,
        hot_two_ref,
        turned_one_ref,
        turned_two_ref,
        hot_sent_ref,
        slope_one_ref,
        slope_two_ref,
        normed_one_ref,
        scaled_one_ref,
        normed_two_ref,
        scaled_two_ref,
        index_ref,
        message_ref,
        sum_ref,
    ) = refs[regions:]
    latent = weights_ref.shape[0]
    edges = slope_one_ref.shape[0] // regions
    capacity = listed // 3
    slots = regions * mesh_cap
    me = lax.axis_index("space")
    for step, packed_ref in zip(steps, packed_refs):
        region = lax.rem(me + (regions - step), regions)
        at = lambda rows: pl.ds(pl.multiple_of(region * rows, rows), rows)
        grid_ref[at(listed), :] = packed_ref[:listed, :]
        mesh_ref[at(mesh_count), :] = packed_ref[listed : listed + mesh_count, :]
        index_ref[at(INDEX_ROWS), :] = packed_ref[listed + mesh_count :, :].astype(F32)

    grid_proj = dot(grid_ref[...], weights_ref[:, :latent])
    mesh_proj = dot(mesh_ref[...], weights_ref[:, latent : 2 * latent])
    for d in range(regions):
        index = index_ref[d * INDEX_ROWS : (d + 1) * INDEX_ROWS, :].astype(jnp.int32)
        for row, senders, hot_ref, turned_ref in (
            (0, listed, hot_one_ref, turned_one_ref),
            (1, slots, hot_two_ref, turned_two_ref),
        ):
            count = senders + mesh_count
            hot = jnp.concatenate(
                [
                    one_hot(index[row : row + 1, :edges], senders),
                    one_hot(index[row : row + 1, edges:], mesh_count),
                ],
                axis=0,
            )
            hot_ref[d * count : (d + 1) * count, :] = hot
            turned_ref[d * edges : (d + 1) * edges, :] = hot.T
        hot_sent_ref[d * mesh_count : (d + 1) * mesh_count, :] = one_hot(
            index[2:3, :slots], mesh_count
        )

    blank = jnp.zeros((capacity, latent), F32)
    tables = []
    for d in range(regions):
        before = (d - 1) * listed + 2 * capacity
        within = d * listed + capacity
        after = (d + 1) * listed
        tables.append(
            jnp.concatenate(
                [
                    grid_proj[before : before + capacity] if d > 0 else blank,
                    grid_proj[within : within + capacity],
                    grid_proj[after : after + capacity] if d < regions - 1 else blank,
                    mesh_proj[d * mesh_count : (d + 1) * mesh_count],
                ],
                axis=0,
            ).astype(BF16)
        )
    sums = edge_forward(
        tables, hot_one_ref, turned_one_ref, slope_one_ref, message_ref, mesh_count
    )
    for d in range(regions):
        sum_ref[d * mesh_count : (d + 1) * mesh_count, :] = sums[d]
    centred, scaled = row_moments(sum_ref[...])
    normed = centred * scaled
    normed_one_ref[...] = normed
    scaled_one_ref[...] = jnp.broadcast_to(scaled, scaled_one_ref.shape)
    first_ref[...] = (mesh_ref[...].astype(F32) + normed).astype(BF16)

    for s in range(regions):
        rows = slice(s * mesh_count, (s + 1) * mesh_count)
        sent_ref[s * slots : (s + 1) * slots, :] = dot_first(
            hot_sent_ref[rows, :], first_ref[rows, :]
        ).astype(BF16)
    sent_proj = dot(sent_ref[...], weights_ref[:, 2 * latent : 3 * latent])
    first_proj = dot(first_ref[...], weights_ref[:, 3 * latent :])
    tables = []
    for d in range(regions):
        pieces = [
            sent_proj[s * slots + d * mesh_cap : s * slots + (d + 1) * mesh_cap]
            for s in range(regions)
        ]
        tables.append(
            jnp.concatenate(
                pieces + [first_proj[d * mesh_count : (d + 1) * mesh_count]], axis=0
            ).astype(BF16)
        )
    sums = edge_forward(
        tables, hot_two_ref, turned_two_ref, slope_two_ref, message_ref, mesh_count
    )
    for d in range(regions):
        sum_ref[d * mesh_count : (d + 1) * mesh_count, :] = sums[d]
    centred, scaled = row_moments(sum_ref[...])
    normed_two_ref[...] = centred * scaled
    scaled_two_ref[...] = jnp.broadcast_to(scaled, scaled_two_ref.shape)


def edge_backward(regions, agg_grad_ref, hot_ref, turned_hot_ref, slope_ref, edge_grad_ref):
    mesh_count = agg_grad_ref.shape[0] // len(regions)
    edges = edge_grad_ref.shape[0] // len(regions)
    count = turned_hot_ref.shape[1]
    blank = jnp.zeros((count - mesh_count, agg_grad_ref.shape[1]), BF16)
    work = [(n, first, size) for n in range(len(regions)) for first, size in edge_blocks(edges)]

    def at(n, first, size):
        return pl.ds(pl.multiple_of(regions[n] * edges + first, size), size)

    def gathered(n, first, size):
        own = agg_grad_ref[n * mesh_count : (n + 1) * mesh_count, :]
        return dot(turned_hot_ref[at(n, first, size), :], jnp.concatenate([blank, own], axis=0))

    sums = []
    upstream = gathered(*work[0])
    for k, (n, first, size) in enumerate(work):
        coming = gathered(*work[k + 1]) if k + 1 < len(work) else None
        rows = slice(n * edges + first, n * edges + first + size)
        edge_grad_ref[rows, :] = upstream.astype(BF16) * slope_ref[at(n, first, size), :]
        upstream = coming
        if first + size == edges:
            hot = hot_ref[pl.ds(pl.multiple_of(regions[n] * count, count), count), :]
            sums.append(dot(hot, edge_grad_ref[n * edges : (n + 1) * edges, :]))
    return sums


def halve(share_ref, keep_ref, give_ref):
    half = keep_ref.shape[0]
    core = lax.bitwise_and(lax.axis_index("rep"), 1)
    keep_ref[...] = share_ref[pl.ds(pl.multiple_of(core * half, half), half), :]
    give_ref[...] = share_ref[pl.ds(pl.multiple_of((1 - core) * half, half), half), :]


def process_back_part(
    steps, mesh_count, cotangent_refs, hot_ref, turned_hot_ref, slope_ref, normed_ref, scaled_ref,
    agg_grad_ref, edge_grad_ref,
):
    me = lax.axis_index("space")
    regions = [lax.bitwise_xor(me, step) for step in steps]
    for n, (region, cotangent_ref) in enumerate(zip(regions, cotangent_refs)):
        rows = pl.ds(pl.multiple_of(region * mesh_count, mesh_count), mesh_count)
        agg_grad_ref[n * mesh_count : (n + 1) * mesh_count, :] = moments_back(
            normed_ref[rows, :], scaled_ref[rows, 0:1], cotangent_ref[0].astype(F32)
        ).astype(BF16)
    return regions, edge_backward(
        regions, agg_grad_ref, hot_ref, turned_hot_ref, slope_ref, edge_grad_ref
    )


def near_back_kernel(steps, *refs):
    cotangent_refs, refs = refs[: len(steps)], refs[len(steps) :]
    (
        hot_ref,
        turned_hot_ref,
        slope_ref,
        normed_ref,
        scaled_ref,
        *whole_refs,
    ) = refs[:9]
    sums_ref, *column_refs = refs[9:14]
    agg_grad_ref, edge_grad_ref = refs[14:]
    mesh_count = agg_grad_ref.shape[0] // len(steps)
    count = turned_hot_ref.shape[1]
    _, all_sums = process_back_part(
        steps, mesh_count, cotangent_refs, hot_ref, turned_hot_ref, slope_ref, normed_ref,
        scaled_ref, agg_grad_ref, edge_grad_ref,
    )
    for n, sums in enumerate(all_sums):
        sums_ref[n * count : (n + 1) * count, :] = sums
    columns = column_refs[0].shape[0]
    mine = pl.ds(pl.multiple_of(lax.axis_index("space") * columns, columns), columns)
    for whole_ref, column_ref in zip(whole_refs, column_refs):
        column_ref[...] = whole_ref[:, mine].T


def far_back_kernel(near, far, mesh_cap, *refs):
    regions = len(near) + len(far)
    cotangent_refs, refs = refs[:regions], refs[regions:]
    (
        turned_ref,
        first_columns_ref,
        sent_columns_ref,
        near_sums_ref,
        hot_ref,
        turned_hot_ref,
        hot_sent_ref,
        slope_ref,
        normed_ref,
        scaled_ref,
        mesh_grad_ref,
        keep_ref,
        give_ref,
        upstream_ref,
        slot_ref,
        recv_ref,
        share_ref,
        agg_grad_ref,
        edge_grad_ref,
    ) = refs
    latent = normed_ref.shape[1]
    mesh_count = normed_ref.shape[0] // regions
    count = turned_hot_ref.shape[1]
    slots = regions * mesh_cap
    me = lax.axis_index("space")
    far_regions, all_sums = process_back_part(
        far, mesh_count, cotangent_refs[len(near) :], hot_ref, turned_hot_ref, slope_ref,
        normed_ref, scaled_ref, agg_grad_ref, edge_grad_ref,
    )
    near_regions = [lax.bitwise_xor(me, step) for step in near]
    near_sums = [near_sums_ref[n * count : (n + 1) * count, :] for n in range(len(near))]
    for region, sums in zip(near_regions + far_regions, near_sums + all_sums):
        for s in range(regions):
            slot_ref[pl.ds(pl.multiple_of(s * slots + region * mesh_cap, mesh_cap), mesh_cap), :] = (
                sums[s * mesh_cap : (s + 1) * mesh_cap]
            )
        recv_ref[pl.ds(pl.multiple_of(region * mesh_count, mesh_count), mesh_count), :] = sums[
            slots:
        ].astype(BF16)
    for region, cotangent_ref in zip(near_regions + far_regions, cotangent_refs):
        rows = pl.ds(pl.multiple_of(region * mesh_count, mesh_count), mesh_count)
        upstream_ref[rows, :] = cotangent_ref[0].astype(F32)
    slot_sum = slot_ref[...].astype(BF16)
    share_ref[:, :latent] = dot(sent_columns_ref[...], slot_sum).astype(BF16)
    share_ref[:, latent:] = dot(first_columns_ref[...], recv_ref[...]).astype(BF16)
    halve(share_ref, keep_ref, give_ref)
    returned = dot(slot_sum, turned_ref[:, latent : 2 * latent]).astype(BF16)
    grad = upstream_ref[...] + dot(recv_ref[...], turned_ref[:, 2 * latent :])
    for s in range(regions):
        rows = slice(s * mesh_count, (s + 1) * mesh_count)
        mesh_grad_ref[rows, :] = grad[rows] + dot(
            hot_sent_ref[rows, :], returned[s * slots : (s + 1) * slots]
        )


def encode_back_kernel(
    regions,
    grid_columns_ref,
    mesh_columns_ref,
    hot_ref,
    turned_hot_ref,
    slope_ref,
    normed_ref,
    scaled_ref,
    mesh_grad_ref,
    own_slot_ref,
    keep_ref,
    give_ref,
    slot_ref,
    recv_ref,
    share_ref,
    agg_grad_ref,
    edge_grad_ref,
):
    latent = normed_ref.shape[1]
    mesh_count = normed_ref.shape[0] // regions
    listed = slot_ref.shape[0] // regions
    capacity = listed // 3
    me = lax.axis_index("space")
    agg_grad_ref[...] = moments_back(
        normed_ref[...], scaled_ref[:, 0:1], mesh_grad_ref[...]
    ).astype(BF16)
    blank = jnp.zeros((capacity, latent), BF16)
    slot_ref[0:capacity, :] = blank
    slot_ref[regions * listed - capacity :, :] = blank
    all_sums = edge_backward(
        range(regions), agg_grad_ref, hot_ref, turned_hot_ref, slope_ref, edge_grad_ref
    )
    for d, sums in enumerate(all_sums):
        sums = sums.astype(BF16)
        for j in range(3):
            source = d + j - 1
            if 0 <= source < regions:
                first = source * listed + (2 - j) * capacity
                slot_ref[first : first + capacity, :] = sums[j * capacity : (j + 1) * capacity]
        recv_ref[d * mesh_count : (d + 1) * mesh_count, :] = sums[listed:]
    share_ref[:, :latent] = dot(grid_columns_ref[...], slot_ref[...]).astype(BF16)
    share_ref[:, latent:] = dot(mesh_columns_ref[...], recv_ref[...]).astype(BF16)
    halve(share_ref, keep_ref, give_ref)
    own = pl.ds(pl.multiple_of(me * listed, listed), listed)
    own_slot_ref[...] = slot_ref[own, :]


def results_kernel(
    turned_ref, pick_ref, own_slot_ref, first_ref, normed_ref, grid_grad_ref, mesh_out_ref
):
    mesh_count = mesh_out_ref.shape[1]
    me = lax.axis_index("space")
    own = pl.ds(pl.multiple_of(me * mesh_count, mesh_count), mesh_count)
    mesh_out_ref[0] = (first_ref[own, :].astype(F32) + normed_ref[own, :]).astype(BF16)
    lists, _, capacity = pick_ref.shape
    latent = own_slot_ref.shape[1]
    returned = dot(own_slot_ref[...], turned_ref[:, :latent]).astype(BF16)
    total = None
    for i in range(lists):
        owner = one_hot(pick_ref[i], grid_grad_ref.shape[1])
        part = dot(owner, returned[i * capacity : (i + 1) * capacity])
        total = part if total is None else total + part
    grid_grad_ref[0] = total.astype(BF16)


def place(pairs, stages, semaphores):
    copies = []
    for n, (block_ref, target) in enumerate(pairs):
        stages[n][...] = block_ref[...].astype(F32)
        copies.append(pltpu.make_async_copy(stages[n], target, semaphores.at[n]))
        copies[n].start()
    for copy in copies:
        copy.wait()


def half_rows(half):
    core = lax.bitwise_and(lax.axis_index("rep"), 1)
    mine = pl.ds(pl.multiple_of(core * half, half), half)
    return mine, pl.ds(pl.multiple_of((1 - core) * half, half), half)


def settle_kernel(one_ref, two_ref, other_two_ref, weight_grad_ref, *scratch):
    half, width = one_ref.shape
    mine, other = half_rows(half)
    place(
        [
            (two_ref, weight_grad_ref.at[mine, width:]),
            (other_two_ref, weight_grad_ref.at[other, width:]),
            (one_ref, weight_grad_ref.at[mine, :width]),
        ],
        scratch[:3],
        scratch[3],
    )


def finish_kernel(other_one_ref, settled_ref, weight_grad_ref, stage, semaphores):
    half, width = other_one_ref.shape
    _, other = half_rows(half)
    place([(other_one_ref, weight_grad_ref.at[other, :width])], [stage], semaphores)


VMEM = pl.BlockSpec(memory_space=pltpu.VMEM)


def call(kernel, operands, outputs, scratch, flops, fetched=0):
    hbm = pl.BlockSpec(memory_space=pltpu.HBM)
    operands = [
        pltpu.with_memory_space_constraint(operand, pltpu.HBM) if n < fetched else operand
        for n, operand in enumerate(operands)
    ]
    return pl.pallas_call(
        kernel,
        out_shape=[jax.ShapeDtypeStruct(shape, kind) for shape, kind in outputs],
        in_specs=[hbm] * fetched + [VMEM] * (len(operands) - fetched),
        out_specs=[VMEM] * len(outputs),
        scratch_shapes=[pltpu.VMEM(shape, kind) for shape, kind in scratch]
        + ([pltpu.SemaphoreType.DMA((fetched,))] if fetched else []),
        compiler_params=pltpu.CompilerParams(vmem_limit_bytes=40 << 20),
        cost_estimate=pl.CostEstimate(flops=flops, bytes_accessed=4 << 20, transcendentals=0),
    )(*operands)


def swap(block, axis, bits):
    return lax.ppermute(block, axis, [(i, i ^ bits) for i in range(lax.axis_size(axis))])


def shifted(block, step):
    count = lax.axis_size("space")
    return lax.ppermute(block, "space", [(i, (i + step) % count) for i in range(count)])


def added(left, right):
    return (left.astype(F32) + right.astype(F32)).astype(BF16)


def summed_over_chips(half):
    bit = 2
    while bit < lax.axis_size("rep"):
        half = added(half, swap(half, "rep", bit))
        bit *= 2
    return half


def whole_sample_body(
    grid_latent,
    mesh_latent,
    mesh_cotangent,
    weights,
    g2m_pick,
    g2m_sender,
    g2m_receiver,
    m2m_pick,
    m2m_sender,
    m2m_receiver,
):
    regions = lax.axis_size("space")
    latent = weights.shape[0]
    listed = g2m_pick.shape[1] * g2m_pick.shape[2]
    mesh_count = mesh_latent.shape[1]
    mesh_cap = m2m_pick.shape[2]
    edges = g2m_sender.shape[0]
    columns = latent // regions
    half = columns // 2
    g2m_pick = g2m_pick.transpose(1, 0, 2)
    sources = (
        grid_latent,
        mesh_latent,
        g2m_pick,
        g2m_sender.reshape(1, -1),
        g2m_receiver.reshape(1, -1),
        m2m_pick,
        m2m_sender.reshape(1, -1),
        m2m_receiver.reshape(1, -1),
    )
    packed = call(
        pack_kernel,
        sources,
        [((listed + mesh_count + INDEX_ROWS, latent), BF16)],
        [((INDEX_ROWS, latent), F32)] + [(source.shape, source.dtype) for source in sources],
        10**7,
        fetched=len(sources),
    )[0]
    packed, cotangent, weights = lax.optimization_barrier((packed, mesh_cotangent, weights))
    ring = (0, *sorted(range(1, regions), key=lambda step: -min(step, regions - step)))
    packs = [packed] + [shifted(packed, step) for step in ring[1:]]
    steps = (0, *range(2, regions), 1)
    near = swap(cotangent, "space", 1)
    weights, turned = call(
        weights_kernel,
        (weights,),
        [(weights.shape, BF16), ((latent, 3 * latent), BF16)],
        [],
        10**8,
        fetched=1,
    )
    packs[1], cotangent = lax.optimization_barrier((packs[1], cotangent))
    cotangents = [cotangent] + [swap(cotangent, "space", step) for step in steps[1:-1]] + [near]
    rows = regions * mesh_count
    slots = regions * mesh_cap
    (
        grid_all,
        mesh_all,
        mesh_first,
        mesh_sent,
        hot_one,
        hot_two,
        turned_one,
        turned_two,
        hot_sent,
        slope_one,
        slope_two,
        normed_one,
        scaled_one,
        normed_two,
        scaled_two,
    ) = call(
        functools.partial(forward_kernel, ring, listed, mesh_count, mesh_cap),
        (*packs, weights),
        [
            ((regions * listed, latent), BF16),
            ((rows, latent), BF16),
            ((rows, latent), BF16),
            ((regions * slots, latent), BF16),
            ((regions * (listed + mesh_count), edges), BF16),
            ((regions * (slots + mesh_count), edges), BF16),
            ((regions * edges, listed + mesh_count), BF16),
            ((regions * edges, slots + mesh_count), BF16),
            ((rows, slots), BF16),
            ((regions * edges, latent), BF16),
            ((regions * edges, latent), BF16),
            ((rows, latent), F32),
            ((rows, 128), F32),
            ((rows, latent), F32),
            ((rows, 128), F32),
        ],
        [
            ((regions * INDEX_ROWS, latent), F32),
            ((regions * edges, latent), BF16),
            ((rows, latent), F32),
        ],
        2 * 10**9,
    )
    by_step = dict(zip(steps, cotangents))
    near, far = (0, 1), tuple(step for step in steps if step > 1)
    count = slots + mesh_count
    near_sums, grid_columns, mesh_columns, sent_columns, first_columns = call(
        functools.partial(near_back_kernel, near),
        (
            *(by_step[step] for step in near),
            hot_two,
            turned_two,
            slope_two,
            normed_two,
            scaled_two,
            grid_all,
            mesh_all,
            mesh_sent,
            mesh_first,
        ),
        [
            ((len(near) * count, latent), F32),
            ((columns, regions * listed), BF16),
            ((columns, rows), BF16),
            ((columns, regions * slots), BF16),
            ((columns, rows), BF16),
        ],
        [((len(near) * mesh_count, latent), BF16), ((len(near) * edges, latent), BF16)],
        10**9,
    )
    mesh_grad, keep_two, give_two = call(
        functools.partial(far_back_kernel, near, far, mesh_cap),
        (
            *(by_step[step] for step in near + far),
            turned,
            first_columns,
            sent_columns,
            near_sums,
            hot_two,
            turned_two,
            hot_sent,
            slope_two,
            normed_two,
            scaled_two,
        ),
        [((rows, latent), F32)] + [((half, 2 * latent), BF16)] * 2,
        [
            ((rows, latent), F32),
            ((regions * slots, latent), F32),
            ((rows, latent), BF16),
            ((columns, 2 * latent), BF16),
            ((len(far) * mesh_count, latent), BF16),
            ((len(far) * edges, latent), BF16),
        ],
        10**9,
    )
    own_slots, keep_one, give_one = call(
        functools.partial(encode_back_kernel, regions),
        (
            grid_columns,
            mesh_columns,
            hot_one,
            turned_one,
            slope_one,
            normed_one,
            scaled_one,
            mesh_grad,
        ),
        [((listed, latent), BF16)] + [((half, 2 * latent), BF16)] * 2,
        [
            ((regions * listed, latent), BF16),
            ((rows, latent), BF16),
            ((columns, 2 * latent), BF16),
            ((rows, latent), BF16),
            ((regions * edges, latent), BF16),
        ],
        10**9,
    )
    half_one = added(keep_one, swap(give_one, "rep", 1))
    half_two = added(keep_two, swap(give_two, "rep", 1))
    half_one, own_slots = lax.optimization_barrier((half_one, own_slots))
    grid_grad, mesh_out = call(
        results_kernel,
        (turned, g2m_pick, own_slots, mesh_first, normed_two),
        [(grid_latent.shape, BF16), (mesh_latent.shape, BF16)],
        [],
        10**8,
    )
    two = summed_over_chips(half_two)
    one, grid_grad = lax.optimization_barrier((summed_over_chips(half_one), grid_grad))
    hbm = pl.BlockSpec(memory_space=pltpu.HBM)
    stage = pltpu.VMEM((half, 2 * latent), F32)
    weight_shape = pltpu.HBM((columns, 4 * latent), F32)
    limit = pltpu.CompilerParams(vmem_limit_bytes=40 << 20)
    settled = pl.pallas_call(
        settle_kernel,
        out_shape=weight_shape,
        in_specs=[VMEM] * 3,
        out_specs=hbm,
        scratch_shapes=[stage] * 3 + [pltpu.SemaphoreType.DMA((3,))],
        compiler_params=limit,
    )(one, two, swap(two, "rep", 1))
    weight_grad = pl.pallas_call(
        finish_kernel,
        out_shape=weight_shape,
        in_specs=[VMEM, hbm],
        out_specs=hbm,
        scratch_shapes=[stage, pltpu.SemaphoreType.DMA((1,))],
        input_output_aliases={1: 0},
        compiler_params=limit,
    )(swap(one, "rep", 1), settled)
    return (mesh_out, grid_grad, weight_grad)


def solution(mesh):
    regions = mesh.shape["space"]
    samples = mesh.shape["rep"]

    def whole(*arguments):
        edges = arguments[5].shape[0] + arguments[8].shape[0]
        latent = arguments[3].shape[0]
        fits = edges * latent * 4 <= SAMPLE_EDGE_BYTES and latent % (128 * regions) == 0
        paired = regions > 2 and samples > 1 and not (regions & (regions - 1) | samples & (samples - 1))
        return sharded(whole_sample_body if fits and paired else partitioned_body)(*arguments)

    def sharded(body):
        return jax.shard_map(
            body,
            mesh=mesh,
            in_specs=(
                P(("groups", "rep"), "space", None),
                P(("groups", "rep"), "space", None),
                P(("groups", "rep"), "space", None),
                P(),
                P("space", None, None),
                P("space"),
                P("space"),
                P("space", None, None),
                P("space"),
                P("space"),
            ),
            out_specs=(
                P(("groups", "rep"), "space", None),
                P(("groups", "rep"), "space", None),
                P(("groups", "space"), None),
            ),
            check_vma=False,
        )

    return whole
```

```python
import functools

import jax
import jax.numpy as jnp
from jax import lax
from jax.experimental import pallas as pl
from jax.experimental.pallas import tpu as pltpu
from jax.sharding import PartitionSpec as P

EPSILON = 1e-05


def with_halo(cells, sides, width):
    for axis, dim in sides:
        count = lax.axis_size(axis)
        ends = count - 1
        head = lax.slice_in_dim(cells, 0, width, axis=dim)
        tail = lax.slice_in_dim(cells, cells.shape[dim] - width, cells.shape[dim], axis=dim)
        cells = jnp.concatenate(
            [
                lax.ppermute(tail, axis, [(i, (i + 1) % count) for i in range(ends)]),
                cells,
                lax.ppermute(head, axis, [((i + 1) % count, i) for i in range(ends)]),
            ],
            axis=dim,
        )
    return cells


def swish(values):
    return values * jax.nn.sigmoid(values)


def swish_slope(values):
    squash = jax.nn.sigmoid(values)
    return squash * (1.0 + values * (1.0 - squash))


def norm_rows(values):
    centred = values - jnp.mean(values, -1, keepdims=True)
    return centred * lax.rsqrt(jnp.mean(centred * centred, -1, keepdims=True) + EPSILON)


def norm_rows_back(values, upstream):
    centred = values - jnp.mean(values, -1, keepdims=True)
    scaled = lax.rsqrt(jnp.mean(centred * centred, -1, keepdims=True) + EPSILON)
    normed = centred * scaled
    return scaled * (
        upstream
        - jnp.mean(upstream, -1, keepdims=True)
        - normed * jnp.mean(upstream * normed, -1, keepdims=True)
    )


def slot_rows(pick_row):
    listed = pick_row.reshape(-1)
    return listed


def mesh_route(outgoing, capacity, peer_count):
    columns = outgoing.shape[1]
    pieces = lax.all_to_all(
        outgoing.reshape(peer_count, capacity, columns),
        "space",
        split_axis=0,
        concat_axis=0,
        tiled=True,
    )
    arrived = pieces.reshape(peer_count * capacity, columns)
    return arrived


def grid_route(outgoing, capacity):
    columns = outgoing.shape[1]
    lists = outgoing.reshape(3, capacity, columns)
    rims = with_halo(jnp.stack([lists[0], lists[2]]), (("space", 0),), 1)
    return jnp.concatenate([rims[0], lists[1], rims[3]], axis=0)


def edge_pass(arrived, recv_table, located, receiver, w_send, w_recv):
    recv_proj = jnp.dot(recv_table, w_recv, preferred_element_type=jnp.float32)
    slot_proj = jnp.dot(arrived, w_send, preferred_element_type=jnp.float32)
    activation = slot_proj[located] + recv_proj[receiver]
    message = swish(activation).astype(jnp.bfloat16)
    member = (
        receiver[None, :] == jnp.arange(recv_table.shape[0], dtype=jnp.int32)[:, None]
    ).astype(jnp.bfloat16)
    summed = jnp.dot(member, message, preferred_element_type=jnp.float32)
    return (activation, member, summed)


def backward_pass(slot_count, located, activation, member, receiver, agg_grad, w_send):
    edge_grad = (agg_grad[receiver] * swish_slope(activation)).astype(jnp.bfloat16)
    recv_sum = jnp.dot(member, edge_grad, preferred_element_type=jnp.float32).astype(jnp.bfloat16)
    slot_member = (located[None, :] == jnp.arange(slot_count, dtype=jnp.int32)[:, None]).astype(
        jnp.bfloat16
    )
    slot_sum = jnp.dot(slot_member, edge_grad, preferred_element_type=jnp.float32).astype(
        jnp.bfloat16
    )
    returned = jnp.dot(slot_sum, w_send.T, preferred_element_type=jnp.float32).astype(jnp.bfloat16)
    return (recv_sum, slot_sum, returned)


def gather_back(listed, back_rows, row_count):
    owner = (listed[None, :] == jnp.arange(row_count, dtype=jnp.int32)[:, None]).astype(
        jnp.bfloat16
    )
    return jnp.dot(owner, back_rows, preferred_element_type=jnp.float32)


def partitioned_body(
    grid_latent,
    mesh_latent,
    mesh_cotangent,
    weights,
    g2m_pick,
    g2m_sender,
    g2m_receiver,
    m2m_pick,
    m2m_sender,
    m2m_receiver,
):
    grid_rows = grid_latent[0]
    mesh_rows = mesh_latent[0]
    upstream = mesh_cotangent[0].astype(jnp.float32)
    latent = weights.shape[0]
    encode_sender = weights[:, :latent]
    encode_receiver = weights[:, latent : 2 * latent]
    process_sender = weights[:, 2 * latent : 3 * latent]
    process_receiver = weights[:, 3 * latent :]
    peer_count = lax.axis_size("space")
    grid_cap = g2m_pick.shape[2]
    mesh_cap = m2m_pick.shape[2]
    grid_listed = g2m_pick[0].reshape(-1)
    grid_arrived = grid_route(grid_rows[grid_listed], grid_cap)
    act_first, member_first, summed_first = edge_pass(
        grid_arrived, mesh_rows, g2m_sender, g2m_receiver, encode_sender, encode_receiver
    )
    mesh_first = (mesh_rows.astype(jnp.float32) + norm_rows(summed_first)).astype(jnp.bfloat16)
    mesh_listed = slot_rows(m2m_pick[0])
    mesh_arrived = mesh_route(mesh_first[mesh_listed], mesh_cap, peer_count)
    act_second, member_second, summed_second = edge_pass(
        mesh_arrived, mesh_first, m2m_sender, m2m_receiver, process_sender, process_receiver
    )
    mesh_final = (mesh_first.astype(jnp.float32) + norm_rows(summed_second)).astype(jnp.bfloat16)
    agg_second = norm_rows_back(summed_second, upstream)
    recv_second, slot_second, returned_second = backward_pass(
        mesh_arrived.shape[0],
        m2m_sender,
        act_second,
        member_second,
        m2m_receiver,
        agg_second,
        process_sender,
    )
    back_second = mesh_route(returned_second, mesh_cap, peer_count)
    mesh_grad = upstream + jnp.dot(
        recv_second, process_receiver.T, preferred_element_type=jnp.float32
    )
    mesh_grad = mesh_grad + gather_back(mesh_listed, back_second, mesh_rows.shape[0])
    agg_first = norm_rows_back(summed_first, mesh_grad)
    recv_first, slot_first, returned_first = backward_pass(
        grid_arrived.shape[0],
        g2m_sender,
        act_first,
        member_first,
        g2m_receiver,
        agg_first,
        encode_sender,
    )
    back_first = grid_route(returned_first, grid_cap)
    grid_grad = gather_back(grid_listed, back_first, grid_rows.shape[0]).astype(jnp.bfloat16)
    factor_pairs = (
        (grid_arrived, slot_first),
        (mesh_rows, recv_first),
        (mesh_arrived, slot_second),
        (mesh_first, recv_second),
    )
    blocks = []
    for first_factor, second_factor in factor_pairs:
        blocks.append(
            lax.dot_general(
                first_factor,
                second_factor,
                (((0,), (0,)), ((), ())),
                preferred_element_type=jnp.float32,
            )
        )
    shares = lax.psum_scatter(
        jnp.concatenate(blocks, axis=1).astype(jnp.bfloat16),
        "space",
        scatter_dimension=0,
        tiled=True,
    )
    weight_grad = lax.psum(shares, "rep").astype(jnp.float32)
    return (mesh_final[None], grid_grad[None], weight_grad)


F32 = jnp.float32
BF16 = jnp.bfloat16
INDEX_ROWS = 8
SAMPLE_EDGE_BYTES = 8 << 20


def dot(left, right):
    return jnp.dot(left, right, preferred_element_type=F32)


def dot_first(left, right):
    return lax.dot_general(left, right, (((0,), (0,)), ((), ())), preferred_element_type=F32)


def one_hot(labels, count):
    rows = lax.broadcasted_iota(jnp.int32, (count, labels.shape[-1]), 0)
    return (rows == labels).astype(F32).astype(BF16)


def row_moments(values):
    centred = values - jnp.mean(values, -1, keepdims=True)
    return centred, lax.rsqrt(jnp.mean(centred * centred, -1, keepdims=True) + EPSILON)


def moments_back(normed, scaled, upstream):
    return scaled * (
        upstream
        - jnp.mean(upstream, -1, keepdims=True)
        - normed * jnp.mean(upstream * normed, -1, keepdims=True)
    )


def fetch(pairs, semaphores):
    copies = [
        pltpu.make_async_copy(source, target, semaphores.at[n])
        for n, (source, target) in enumerate(pairs)
    ]
    for copy in copies:
        copy.start()
    for copy in copies:
        copy.wait()


def pack_kernel(*refs):
    sources, packed_ref, index_ref = refs[:8], refs[8], refs[9]
    local, semaphores = refs[10:18], refs[18]
    fetch(list(zip(sources, local)), semaphores)
    (
        grid_ref,
        mesh_ref,
        g2m_pick_ref,
        g2m_sender_ref,
        g2m_receiver_ref,
        m2m_pick_ref,
        m2m_sender_ref,
        m2m_receiver_ref,
    ) = local
    lists, _, capacity = g2m_pick_ref.shape
    mesh_count = mesh_ref.shape[1]
    regions, mesh_cap = m2m_pick_ref.shape[1:]
    edges = g2m_sender_ref.shape[1]
    grid_rows = grid_ref[0]
    for i in range(lists):
        picked = one_hot(g2m_pick_ref[i], grid_rows.shape[0])
        packed_ref[i * capacity : (i + 1) * capacity, :] = dot_first(picked, grid_rows).astype(BF16)
    first = lists * capacity
    packed_ref[first : first + mesh_count, :] = mesh_ref[0]
    index_ref[...] = jnp.zeros_like(index_ref)
    index_ref[0:1, 0:edges] = g2m_sender_ref[...].astype(F32)
    index_ref[0:1, edges : 2 * edges] = g2m_receiver_ref[...].astype(F32)
    index_ref[1:2, 0:edges] = m2m_sender_ref[...].astype(F32)
    index_ref[1:2, edges : 2 * edges] = m2m_receiver_ref[...].astype(F32)
    slots = regions * mesh_cap
    lane = lax.broadcasted_iota(jnp.int32, (mesh_cap, slots), 1)
    spread = (lane % mesh_cap == lax.broadcasted_iota(jnp.int32, (mesh_cap, slots), 0)).astype(F32)
    spread = dot(m2m_pick_ref[0].astype(F32).astype(BF16), spread.astype(BF16))
    lane = lax.broadcasted_iota(jnp.int32, (regions, slots), 1)
    owned = lane // mesh_cap == lax.broadcasted_iota(jnp.int32, (regions, slots), 0)
    index_ref[2:3, 0:slots] = jnp.sum(jnp.where(owned, spread, 0.0), 0, keepdims=True)
    packed_ref[first + mesh_count :, :] = index_ref[...].astype(BF16)


def weights_kernel(source_ref, weights_ref, turned_ref, semaphores):
    fetch([(source_ref, weights_ref)], semaphores)
    latent = weights_ref.shape[0]
    for n, block in enumerate((0, 2, 3)):
        turned_ref[:, n * latent : (n + 1) * latent] = weights_ref[
            :, block * latent : (block + 1) * latent
        ].T


def edge_blocks(edges):
    size = min(edges, 128)
    return [(first, min(size, edges - first)) for first in range(0, edges, size)]


def edge_forward(tables, hot_ref, turned_hot_ref, slope_ref, message_ref, mesh_count):
    regions = len(tables)
    edges = slope_ref.shape[0] // regions
    count = hot_ref.shape[0] // regions
    work = [(d, first, size) for d in range(regions) for first, size in edge_blocks(edges)]

    def gathered(d, first, size):
        rows = slice(d * edges + first, d * edges + first + size)
        return dot(turned_hot_ref[rows, :], tables[d])

    sums = []
    activation = gathered(*work[0])
    for n, (d, first, size) in enumerate(work):
        coming = gathered(*work[n + 1]) if n + 1 < len(work) else None
        activation = activation.astype(BF16)
        squash = 0.5 + 0.5 * jnp.tanh(0.5 * activation)
        message = activation * squash
        rows = slice(d * edges + first, d * edges + first + size)
        slope_ref[rows, :] = squash + message * (1.0 - squash)
        message_ref[rows, :] = message
        activation = coming
        if first + size == edges:
            hot = hot_ref[(d + 1) * count - mesh_count : (d + 1) * count, :]
            sums.append(dot(hot, message_ref[d * edges : (d + 1) * edges, :]))
    return sums


def forward_kernel(
    steps,
    listed,
    mesh_count,
    mesh_cap,
    *refs,
):
    regions = len(steps)
    packed_refs = refs[:regions]
    (
        weights_ref,
        grid_ref,
        mesh_ref,
        first_ref,
        sent_ref,
        hot_one_ref,
        hot_two_ref,
        turned_one_ref,
        turned_two_ref,
        hot_sent_ref,
        slope_one_ref,
        slope_two_ref,
        normed_one_ref,
        scaled_one_ref,
        normed_two_ref,
        scaled_two_ref,
        index_ref,
        message_ref,
        sum_ref,
    ) = refs[regions:]
    latent = weights_ref.shape[0]
    edges = slope_one_ref.shape[0] // regions
    capacity = listed // 3
    slots = regions * mesh_cap
    me = lax.axis_index("space")
    for step, packed_ref in zip(steps, packed_refs):
        region = lax.bitwise_xor(me, step)
        at = lambda rows: pl.ds(pl.multiple_of(region * rows, rows), rows)
        grid_ref[at(listed), :] = packed_ref[:listed, :]
        mesh_ref[at(mesh_count), :] = packed_ref[listed : listed + mesh_count, :]
        index_ref[at(INDEX_ROWS), :] = packed_ref[listed + mesh_count :, :].astype(F32)

    grid_proj = dot(grid_ref[...], weights_ref[:, :latent])
    mesh_proj = dot(mesh_ref[...], weights_ref[:, latent : 2 * latent])
    for d in range(regions):
        index = index_ref[d * INDEX_ROWS : (d + 1) * INDEX_ROWS, :].astype(jnp.int32)
        for row, senders, hot_ref, turned_ref in (
            (0, listed, hot_one_ref, turned_one_ref),
            (1, slots, hot_two_ref, turned_two_ref),
        ):
            count = senders + mesh_count
            hot = jnp.concatenate(
                [
                    one_hot(index[row : row + 1, :edges], senders),
                    one_hot(index[row : row + 1, edges:], mesh_count),
                ],
                axis=0,
            )
            hot_ref[d * count : (d + 1) * count, :] = hot
            turned_ref[d * edges : (d + 1) * edges, :] = hot.T
        hot_sent_ref[d * mesh_count : (d + 1) * mesh_count, :] = one_hot(
            index[2:3, :slots], mesh_count
        )

    blank = jnp.zeros((capacity, latent), F32)
    tables = []
    for d in range(regions):
        before = (d - 1) * listed + 2 * capacity
        within = d * listed + capacity
        after = (d + 1) * listed
        tables.append(
            jnp.concatenate(
                [
                    grid_proj[before : before + capacity] if d > 0 else blank,
                    grid_proj[within : within + capacity],
                    grid_proj[after : after + capacity] if d < regions - 1 else blank,
                    mesh_proj[d * mesh_count : (d + 1) * mesh_count],
                ],
                axis=0,
            ).astype(BF16)
        )
    sums = edge_forward(
        tables, hot_one_ref, turned_one_ref, slope_one_ref, message_ref, mesh_count
    )
    for d in range(regions):
        sum_ref[d * mesh_count : (d + 1) * mesh_count, :] = sums[d]
    centred, scaled = row_moments(sum_ref[...])
    normed = centred * scaled
    normed_one_ref[...] = normed
    scaled_one_ref[...] = jnp.broadcast_to(scaled, scaled_one_ref.shape)
    first_ref[...] = (mesh_ref[...].astype(F32) + normed).astype(BF16)

    for s in range(regions):
        rows = slice(s * mesh_count, (s + 1) * mesh_count)
        sent_ref[s * slots : (s + 1) * slots, :] = dot_first(
            hot_sent_ref[rows, :], first_ref[rows, :]
        ).astype(BF16)
    sent_proj = dot(sent_ref[...], weights_ref[:, 2 * latent : 3 * latent])
    first_proj = dot(first_ref[...], weights_ref[:, 3 * latent :])
    tables = []
    for d in range(regions):
        pieces = [
            sent_proj[s * slots + d * mesh_cap : s * slots + (d + 1) * mesh_cap]
            for s in range(regions)
        ]
        tables.append(
            jnp.concatenate(
                pieces + [first_proj[d * mesh_count : (d + 1) * mesh_count]], axis=0
            ).astype(BF16)
        )
    sums = edge_forward(
        tables, hot_two_ref, turned_two_ref, slope_two_ref, message_ref, mesh_count
    )
    for d in range(regions):
        sum_ref[d * mesh_count : (d + 1) * mesh_count, :] = sums[d]
    centred, scaled = row_moments(sum_ref[...])
    normed_two_ref[...] = centred * scaled
    scaled_two_ref[...] = jnp.broadcast_to(scaled, scaled_two_ref.shape)


def edge_backward(regions, agg_grad_ref, hot_ref, turned_hot_ref, slope_ref, edge_grad_ref):
    mesh_count = agg_grad_ref.shape[0] // len(regions)
    edges = edge_grad_ref.shape[0] // len(regions)
    count = turned_hot_ref.shape[1]
    blank = jnp.zeros((count - mesh_count, agg_grad_ref.shape[1]), BF16)
    work = [(n, first, size) for n in range(len(regions)) for first, size in edge_blocks(edges)]

    def at(n, first, size):
        return pl.ds(pl.multiple_of(regions[n] * edges + first, size), size)

    def gathered(n, first, size):
        own = agg_grad_ref[n * mesh_count : (n + 1) * mesh_count, :]
        return dot(turned_hot_ref[at(n, first, size), :], jnp.concatenate([blank, own], axis=0))

    sums = []
    upstream = gathered(*work[0])
    for k, (n, first, size) in enumerate(work):
        coming = gathered(*work[k + 1]) if k + 1 < len(work) else None
        rows = slice(n * edges + first, n * edges + first + size)
        edge_grad_ref[rows, :] = upstream.astype(BF16) * slope_ref[at(n, first, size), :]
        upstream = coming
        if first + size == edges:
            hot = hot_ref[pl.ds(pl.multiple_of(regions[n] * count, count), count), :]
            sums.append(dot(hot, edge_grad_ref[n * edges : (n + 1) * edges, :]))
    return sums


def halve(share_ref, keep_ref, give_ref):
    half = keep_ref.shape[0]
    core = lax.bitwise_and(lax.axis_index("rep"), 1)
    keep_ref[...] = share_ref[pl.ds(pl.multiple_of(core * half, half), half), :]
    give_ref[...] = share_ref[pl.ds(pl.multiple_of((1 - core) * half, half), half), :]


def process_back_part(
    steps, mesh_count, cotangent_refs, hot_ref, turned_hot_ref, slope_ref, normed_ref, scaled_ref,
    agg_grad_ref, edge_grad_ref,
):
    me = lax.axis_index("space")
    regions = [lax.bitwise_xor(me, step) for step in steps]
    for n, (region, cotangent_ref) in enumerate(zip(regions, cotangent_refs)):
        rows = pl.ds(pl.multiple_of(region * mesh_count, mesh_count), mesh_count)
        agg_grad_ref[n * mesh_count : (n + 1) * mesh_count, :] = moments_back(
            normed_ref[rows, :], scaled_ref[rows, 0:1], cotangent_ref[0].astype(F32)
        ).astype(BF16)
    return regions, edge_backward(
        regions, agg_grad_ref, hot_ref, turned_hot_ref, slope_ref, edge_grad_ref
    )


def near_back_kernel(steps, *refs):
    cotangent_refs, refs = refs[: len(steps)], refs[len(steps) :]
    (
        hot_ref,
        turned_hot_ref,
        slope_ref,
        normed_ref,
        scaled_ref,
        *whole_refs,
    ) = refs[:9]
    sums_ref, *column_refs = refs[9:14]
    agg_grad_ref, edge_grad_ref = refs[14:]
    mesh_count = agg_grad_ref.shape[0] // len(steps)
    count = turned_hot_ref.shape[1]
    _, all_sums = process_back_part(
        steps, mesh_count, cotangent_refs, hot_ref, turned_hot_ref, slope_ref, normed_ref,
        scaled_ref, agg_grad_ref, edge_grad_ref,
    )
    for n, sums in enumerate(all_sums):
        sums_ref[n * count : (n + 1) * count, :] = sums
    columns = column_refs[0].shape[0]
    mine = pl.ds(pl.multiple_of(lax.axis_index("space") * columns, columns), columns)
    for whole_ref, column_ref in zip(whole_refs, column_refs):
        column_ref[...] = whole_ref[:, mine].T


def far_back_kernel(near, far, mesh_cap, *refs):
    regions = len(near) + len(far)
    cotangent_refs, refs = refs[:regions], refs[regions:]
    (
        turned_ref,
        first_columns_ref,
        sent_columns_ref,
        near_sums_ref,
        hot_ref,
        turned_hot_ref,
        hot_sent_ref,
        slope_ref,
        normed_ref,
        scaled_ref,
        mesh_grad_ref,
        keep_ref,
        give_ref,
        upstream_ref,
        slot_ref,
        recv_ref,
        share_ref,
        agg_grad_ref,
        edge_grad_ref,
    ) = refs
    latent = normed_ref.shape[1]
    mesh_count = normed_ref.shape[0] // regions
    count = turned_hot_ref.shape[1]
    slots = regions * mesh_cap
    me = lax.axis_index("space")
    far_regions, all_sums = process_back_part(
        far, mesh_count, cotangent_refs[len(near) :], hot_ref, turned_hot_ref, slope_ref,
        normed_ref, scaled_ref, agg_grad_ref, edge_grad_ref,
    )
    near_regions = [lax.bitwise_xor(me, step) for step in near]
    near_sums = [near_sums_ref[n * count : (n + 1) * count, :] for n in range(len(near))]
    for region, sums in zip(near_regions + far_regions, near_sums + all_sums):
        for s in range(regions):
            slot_ref[pl.ds(pl.multiple_of(s * slots + region * mesh_cap, mesh_cap), mesh_cap), :] = (
                sums[s * mesh_cap : (s + 1) * mesh_cap]
            )
        recv_ref[pl.ds(pl.multiple_of(region * mesh_count, mesh_count), mesh_count), :] = sums[
            slots:
        ].astype(BF16)
    for region, cotangent_ref in zip(near_regions + far_regions, cotangent_refs):
        rows = pl.ds(pl.multiple_of(region * mesh_count, mesh_count), mesh_count)
        upstream_ref[rows, :] = cotangent_ref[0].astype(F32)
    slot_sum = slot_ref[...].astype(BF16)
    share_ref[:, :latent] = dot(sent_columns_ref[...], slot_sum).astype(BF16)
    share_ref[:, latent:] = dot(first_columns_ref[...], recv_ref[...]).astype(BF16)
    halve(share_ref, keep_ref, give_ref)
    returned = dot(slot_sum, turned_ref[:, latent : 2 * latent]).astype(BF16)
    grad = upstream_ref[...] + dot(recv_ref[...], turned_ref[:, 2 * latent :])
    for s in range(regions):
        rows = slice(s * mesh_count, (s + 1) * mesh_count)
        mesh_grad_ref[rows, :] = grad[rows] + dot(
            hot_sent_ref[rows, :], returned[s * slots : (s + 1) * slots]
        )


def encode_back_kernel(
    regions,
    grid_columns_ref,
    mesh_columns_ref,
    hot_ref,
    turned_hot_ref,
    slope_ref,
    normed_ref,
    scaled_ref,
    mesh_grad_ref,
    own_slot_ref,
    keep_ref,
    give_ref,
    slot_ref,
    recv_ref,
    share_ref,
    agg_grad_ref,
    edge_grad_ref,
):
    latent = normed_ref.shape[1]
    mesh_count = normed_ref.shape[0] // regions
    listed = slot_ref.shape[0] // regions
    capacity = listed // 3
    me = lax.axis_index("space")
    agg_grad_ref[...] = moments_back(
        normed_ref[...], scaled_ref[:, 0:1], mesh_grad_ref[...]
    ).astype(BF16)
    blank = jnp.zeros((capacity, latent), BF16)
    slot_ref[0:capacity, :] = blank
    slot_ref[regions * listed - capacity :, :] = blank
    all_sums = edge_backward(
        range(regions), agg_grad_ref, hot_ref, turned_hot_ref, slope_ref, edge_grad_ref
    )
    for d, sums in enumerate(all_sums):
        sums = sums.astype(BF16)
        for j in range(3):
            source = d + j - 1
            if 0 <= source < regions:
                first = source * listed + (2 - j) * capacity
                slot_ref[first : first + capacity, :] = sums[j * capacity : (j + 1) * capacity]
        recv_ref[d * mesh_count : (d + 1) * mesh_count, :] = sums[listed:]
    share_ref[:, :latent] = dot(grid_columns_ref[...], slot_ref[...]).astype(BF16)
    share_ref[:, latent:] = dot(mesh_columns_ref[...], recv_ref[...]).astype(BF16)
    halve(share_ref, keep_ref, give_ref)
    own = pl.ds(pl.multiple_of(me * listed, listed), listed)
    own_slot_ref[...] = slot_ref[own, :]


def results_kernel(
    turned_ref, pick_ref, own_slot_ref, first_ref, normed_ref, grid_grad_ref, mesh_out_ref
):
    mesh_count = mesh_out_ref.shape[1]
    me = lax.axis_index("space")
    own = pl.ds(pl.multiple_of(me * mesh_count, mesh_count), mesh_count)
    mesh_out_ref[0] = (first_ref[own, :].astype(F32) + normed_ref[own, :]).astype(BF16)
    lists, _, capacity = pick_ref.shape
    latent = own_slot_ref.shape[1]
    returned = dot(own_slot_ref[...], turned_ref[:, :latent]).astype(BF16)
    total = None
    for i in range(lists):
        owner = one_hot(pick_ref[i], grid_grad_ref.shape[1])
        part = dot(owner, returned[i * capacity : (i + 1) * capacity])
        total = part if total is None else total + part
    grid_grad_ref[0] = total.astype(BF16)


def place(pairs, stages, semaphores):
    copies = []
    for n, (block_ref, target) in enumerate(pairs):
        stages[n][...] = block_ref[...].astype(F32)
        copies.append(pltpu.make_async_copy(stages[n], target, semaphores.at[n]))
        copies[n].start()
    for copy in copies:
        copy.wait()


def half_rows(half):
    core = lax.bitwise_and(lax.axis_index("rep"), 1)
    mine = pl.ds(pl.multiple_of(core * half, half), half)
    return mine, pl.ds(pl.multiple_of((1 - core) * half, half), half)


def settle_kernel(one_ref, two_ref, other_two_ref, weight_grad_ref, *scratch):
    half, width = one_ref.shape
    mine, other = half_rows(half)
    place(
        [
            (two_ref, weight_grad_ref.at[mine, width:]),
            (other_two_ref, weight_grad_ref.at[other, width:]),
            (one_ref, weight_grad_ref.at[mine, :width]),
        ],
        scratch[:3],
        scratch[3],
    )


def finish_kernel(other_one_ref, settled_ref, weight_grad_ref, stage, semaphores):
    half, width = other_one_ref.shape
    _, other = half_rows(half)
    place([(other_one_ref, weight_grad_ref.at[other, :width])], [stage], semaphores)


VMEM = pl.BlockSpec(memory_space=pltpu.VMEM)


def call(kernel, operands, outputs, scratch, flops, fetched=0):
    hbm = pl.BlockSpec(memory_space=pltpu.HBM)
    operands = [
        pltpu.with_memory_space_constraint(operand, pltpu.HBM) if n < fetched else operand
        for n, operand in enumerate(operands)
    ]
    return pl.pallas_call(
        kernel,
        out_shape=[jax.ShapeDtypeStruct(shape, kind) for shape, kind in outputs],
        in_specs=[hbm] * fetched + [VMEM] * (len(operands) - fetched),
        out_specs=[VMEM] * len(outputs),
        scratch_shapes=[pltpu.VMEM(shape, kind) for shape, kind in scratch]
        + ([pltpu.SemaphoreType.DMA((fetched,))] if fetched else []),
        compiler_params=pltpu.CompilerParams(vmem_limit_bytes=40 << 20),
        cost_estimate=pl.CostEstimate(flops=flops, bytes_accessed=4 << 20, transcendentals=0),
    )(*operands)


def swap(block, axis, bits):
    return lax.ppermute(block, axis, [(i, i ^ bits) for i in range(lax.axis_size(axis))])


def added(left, right):
    return (left.astype(F32) + right.astype(F32)).astype(BF16)


def summed_over_chips(half):
    bit = 2
    while bit < lax.axis_size("rep"):
        half = added(half, swap(half, "rep", bit))
        bit *= 2
    return half


def whole_sample_body(
    grid_latent,
    mesh_latent,
    mesh_cotangent,
    weights,
    g2m_pick,
    g2m_sender,
    g2m_receiver,
    m2m_pick,
    m2m_sender,
    m2m_receiver,
):
    regions = lax.axis_size("space")
    latent = weights.shape[0]
    listed = g2m_pick.shape[1] * g2m_pick.shape[2]
    mesh_count = mesh_latent.shape[1]
    mesh_cap = m2m_pick.shape[2]
    edges = g2m_sender.shape[0]
    columns = latent // regions
    half = columns // 2
    g2m_pick = g2m_pick.transpose(1, 0, 2)
    sources = (
        grid_latent,
        mesh_latent,
        g2m_pick,
        g2m_sender.reshape(1, -1),
        g2m_receiver.reshape(1, -1),
        m2m_pick,
        m2m_sender.reshape(1, -1),
        m2m_receiver.reshape(1, -1),
    )
    packed = call(
        pack_kernel,
        sources,
        [((listed + mesh_count + INDEX_ROWS, latent), BF16)],
        [((INDEX_ROWS, latent), F32)] + [(source.shape, source.dtype) for source in sources],
        10**7,
        fetched=len(sources),
    )[0]
    packed, cotangent, weights = lax.optimization_barrier((packed, mesh_cotangent, weights))
    steps = (0, *range(2, regions), 1)
    packs = [packed] + [swap(packed, "space", step) for step in steps[1:]]
    near = swap(cotangent, "space", 1)
    weights, turned = call(
        weights_kernel,
        (weights,),
        [(weights.shape, BF16), ((latent, 3 * latent), BF16)],
        [],
        10**8,
        fetched=1,
    )
    packs[1], cotangent = lax.optimization_barrier((packs[1], cotangent))
    cotangents = [cotangent] + [swap(cotangent, "space", step) for step in steps[1:-1]] + [near]
    rows = regions * mesh_count
    slots = regions * mesh_cap
    (
        grid_all,
        mesh_all,
        mesh_first,
        mesh_sent,
        hot_one,
        hot_two,
        turned_one,
        turned_two,
        hot_sent,
        slope_one,
        slope_two,
        normed_one,
        scaled_one,
        normed_two,
        scaled_two,
    ) = call(
        functools.partial(forward_kernel, steps, listed, mesh_count, mesh_cap),
        (*packs, weights),
        [
            ((regions * listed, latent), BF16),
            ((rows, latent), BF16),
            ((rows, latent), BF16),
            ((regions * slots, latent), BF16),
            ((regions * (listed + mesh_count), edges), BF16),
            ((regions * (slots + mesh_count), edges), BF16),
            ((regions * edges, listed + mesh_count), BF16),
            ((regions * edges, slots + mesh_count), BF16),
            ((rows, slots), BF16),
            ((regions * edges, latent), BF16),
            ((regions * edges, latent), BF16),
            ((rows, latent), F32),
            ((rows, 128), F32),
            ((rows, latent), F32),
            ((rows, 128), F32),
        ],
        [
            ((regions * INDEX_ROWS, latent), F32),
            ((regions * edges, latent), BF16),
            ((rows, latent), F32),
        ],
        2 * 10**9,
    )
    by_step = dict(zip(steps, cotangents))
    near, far = (0, 1), tuple(step for step in steps if step > 1)
    count = slots + mesh_count
    near_sums, grid_columns, mesh_columns, sent_columns, first_columns = call(
        functools.partial(near_back_kernel, near),
        (
            *(by_step[step] for step in near),
            hot_two,
            turned_two,
            slope_two,
            normed_two,
            scaled_two,
            grid_all,
            mesh_all,
            mesh_sent,
            mesh_first,
        ),
        [
            ((len(near) * count, latent), F32),
            ((columns, regions * listed), BF16),
            ((columns, rows), BF16),
            ((columns, regions * slots), BF16),
            ((columns, rows), BF16),
        ],
        [((len(near) * mesh_count, latent), BF16), ((len(near) * edges, latent), BF16)],
        10**9,
    )
    mesh_grad, keep_two, give_two = call(
        functools.partial(far_back_kernel, near, far, mesh_cap),
        (
            *(by_step[step] for step in near + far),
            turned,
            first_columns,
            sent_columns,
            near_sums,
            hot_two,
            turned_two,
            hot_sent,
            slope_two,
            normed_two,
            scaled_two,
        ),
        [((rows, latent), F32)] + [((half, 2 * latent), BF16)] * 2,
        [
            ((rows, latent), F32),
            ((regions * slots, latent), F32),
            ((rows, latent), BF16),
            ((columns, 2 * latent), BF16),
            ((len(far) * mesh_count, latent), BF16),
            ((len(far) * edges, latent), BF16),
        ],
        10**9,
    )
    own_slots, keep_one, give_one = call(
        functools.partial(encode_back_kernel, regions),
        (
            grid_columns,
            mesh_columns,
            hot_one,
            turned_one,
            slope_one,
            normed_one,
            scaled_one,
            mesh_grad,
        ),
        [((listed, latent), BF16)] + [((half, 2 * latent), BF16)] * 2,
        [
            ((regions * listed, latent), BF16),
            ((rows, latent), BF16),
            ((columns, 2 * latent), BF16),
            ((rows, latent), BF16),
            ((regions * edges, latent), BF16),
        ],
        10**9,
    )
    half_one = added(keep_one, swap(give_one, "rep", 1))
    half_two = added(keep_two, swap(give_two, "rep", 1))
    half_one, own_slots = lax.optimization_barrier((half_one, own_slots))
    grid_grad, mesh_out = call(
        results_kernel,
        (turned, g2m_pick, own_slots, mesh_first, normed_two),
        [(grid_latent.shape, BF16), (mesh_latent.shape, BF16)],
        [],
        10**8,
    )
    two = summed_over_chips(half_two)
    one, grid_grad = lax.optimization_barrier((summed_over_chips(half_one), grid_grad))
    hbm = pl.BlockSpec(memory_space=pltpu.HBM)
    stage = pltpu.VMEM((half, 2 * latent), F32)
    weight_shape = pltpu.HBM((columns, 4 * latent), F32)
    limit = pltpu.CompilerParams(vmem_limit_bytes=40 << 20)
    settled = pl.pallas_call(
        settle_kernel,
        out_shape=weight_shape,
        in_specs=[VMEM] * 3,
        out_specs=hbm,
        scratch_shapes=[stage] * 3 + [pltpu.SemaphoreType.DMA((3,))],
        compiler_params=limit,
    )(one, two, swap(two, "rep", 1))
    weight_grad = pl.pallas_call(
        finish_kernel,
        out_shape=weight_shape,
        in_specs=[VMEM, hbm],
        out_specs=hbm,
        scratch_shapes=[stage, pltpu.SemaphoreType.DMA((1,))],
        input_output_aliases={1: 0},
        compiler_params=limit,
    )(swap(one, "rep", 1), settled)
    return (mesh_out, grid_grad, weight_grad)


def solution(mesh):
    regions = mesh.shape["space"]
    samples = mesh.shape["rep"]

    def whole(*arguments):
        edges = arguments[5].shape[0] + arguments[8].shape[0]
        latent = arguments[3].shape[0]
        fits = edges * latent * 4 <= SAMPLE_EDGE_BYTES and latent % (128 * regions) == 0
        paired = regions > 2 and samples > 1 and not (regions & (regions - 1) | samples & (samples - 1))
        return sharded(whole_sample_body if fits and paired else partitioned_body)(*arguments)

    def sharded(body):
        return jax.shard_map(
            body,
            mesh=mesh,
            in_specs=(
                P(("groups", "rep"), "space", None),
                P(("groups", "rep"), "space", None),
                P(("groups", "rep"), "space", None),
                P(),
                P("space", None, None),
                P("space"),
                P("space"),
                P("space", None, None),
                P("space"),
                P("space"),
            ),
            out_specs=(
                P(("groups", "rep"), "space", None),
                P(("groups", "rep"), "space", None),
                P(("groups", "space"), None),
            ),
            check_vma=False,
        )

    return whole
```

```python
import functools

import jax
import jax.numpy as jnp
from jax import lax
from jax.experimental import pallas as pl
from jax.experimental.pallas import tpu as pltpu
from jax.sharding import PartitionSpec as P

EPSILON = 1e-05


def with_halo(cells, sides, width):
    for axis, dim in sides:
        count = lax.axis_size(axis)
        ends = count - 1
        head = lax.slice_in_dim(cells, 0, width, axis=dim)
        tail = lax.slice_in_dim(cells, cells.shape[dim] - width, cells.shape[dim], axis=dim)
        cells = jnp.concatenate(
            [
                lax.ppermute(tail, axis, [(i, (i + 1) % count) for i in range(ends)]),
                cells,
                lax.ppermute(head, axis, [((i + 1) % count, i) for i in range(ends)]),
            ],
            axis=dim,
        )
    return cells


def swish(values):
    return values * jax.nn.sigmoid(values)


def swish_slope(values):
    squash = jax.nn.sigmoid(values)
    return squash * (1.0 + values * (1.0 - squash))


def norm_rows(values):
    centred = values - jnp.mean(values, -1, keepdims=True)
    return centred * lax.rsqrt(jnp.mean(centred * centred, -1, keepdims=True) + EPSILON)


def norm_rows_back(values, upstream):
    centred = values - jnp.mean(values, -1, keepdims=True)
    scaled = lax.rsqrt(jnp.mean(centred * centred, -1, keepdims=True) + EPSILON)
    normed = centred * scaled
    return scaled * (
        upstream
        - jnp.mean(upstream, -1, keepdims=True)
        - normed * jnp.mean(upstream * normed, -1, keepdims=True)
    )


def slot_rows(pick_row):
    listed = pick_row.reshape(-1)
    return listed


def mesh_route(outgoing, capacity, peer_count):
    columns = outgoing.shape[1]
    pieces = lax.all_to_all(
        outgoing.reshape(peer_count, capacity, columns),
        "space",
        split_axis=0,
        concat_axis=0,
        tiled=True,
    )
    arrived = pieces.reshape(peer_count * capacity, columns)
    return arrived


def grid_route(outgoing, capacity):
    columns = outgoing.shape[1]
    lists = outgoing.reshape(3, capacity, columns)
    rims = with_halo(jnp.stack([lists[0], lists[2]]), (("space", 0),), 1)
    return jnp.concatenate([rims[0], lists[1], rims[3]], axis=0)


def edge_pass(arrived, recv_table, located, receiver, w_send, w_recv):
    recv_proj = jnp.dot(recv_table, w_recv, preferred_element_type=jnp.float32)
    slot_proj = jnp.dot(arrived, w_send, preferred_element_type=jnp.float32)
    activation = slot_proj[located] + recv_proj[receiver]
    message = swish(activation).astype(jnp.bfloat16)
    member = (
        receiver[None, :] == jnp.arange(recv_table.shape[0], dtype=jnp.int32)[:, None]
    ).astype(jnp.bfloat16)
    summed = jnp.dot(member, message, preferred_element_type=jnp.float32)
    return (activation, member, summed)


def backward_pass(slot_count, located, activation, member, receiver, agg_grad, w_send):
    edge_grad = (agg_grad[receiver] * swish_slope(activation)).astype(jnp.bfloat16)
    recv_sum = jnp.dot(member, edge_grad, preferred_element_type=jnp.float32).astype(jnp.bfloat16)
    slot_member = (located[None, :] == jnp.arange(slot_count, dtype=jnp.int32)[:, None]).astype(
        jnp.bfloat16
    )
    slot_sum = jnp.dot(slot_member, edge_grad, preferred_element_type=jnp.float32).astype(
        jnp.bfloat16
    )
    returned = jnp.dot(slot_sum, w_send.T, preferred_element_type=jnp.float32).astype(jnp.bfloat16)
    return (recv_sum, slot_sum, returned)


def gather_back(listed, back_rows, row_count):
    owner = (listed[None, :] == jnp.arange(row_count, dtype=jnp.int32)[:, None]).astype(
        jnp.bfloat16
    )
    return jnp.dot(owner, back_rows, preferred_element_type=jnp.float32)


def partitioned_body(
    grid_latent,
    mesh_latent,
    mesh_cotangent,
    weights,
    g2m_pick,
    g2m_sender,
    g2m_receiver,
    m2m_pick,
    m2m_sender,
    m2m_receiver,
):
    grid_rows = grid_latent[0]
    mesh_rows = mesh_latent[0]
    upstream = mesh_cotangent[0].astype(jnp.float32)
    latent = weights.shape[0]
    encode_sender = weights[:, :latent]
    encode_receiver = weights[:, latent : 2 * latent]
    process_sender = weights[:, 2 * latent : 3 * latent]
    process_receiver = weights[:, 3 * latent :]
    peer_count = lax.axis_size("space")
    grid_cap = g2m_pick.shape[2]
    mesh_cap = m2m_pick.shape[2]
    grid_listed = g2m_pick[0].reshape(-1)
    grid_arrived = grid_route(grid_rows[grid_listed], grid_cap)
    act_first, member_first, summed_first = edge_pass(
        grid_arrived, mesh_rows, g2m_sender, g2m_receiver, encode_sender, encode_receiver
    )
    mesh_first = (mesh_rows.astype(jnp.float32) + norm_rows(summed_first)).astype(jnp.bfloat16)
    mesh_listed = slot_rows(m2m_pick[0])
    mesh_arrived = mesh_route(mesh_first[mesh_listed], mesh_cap, peer_count)
    act_second, member_second, summed_second = edge_pass(
        mesh_arrived, mesh_first, m2m_sender, m2m_receiver, process_sender, process_receiver
    )
    mesh_final = (mesh_first.astype(jnp.float32) + norm_rows(summed_second)).astype(jnp.bfloat16)
    agg_second = norm_rows_back(summed_second, upstream)
    recv_second, slot_second, returned_second = backward_pass(
        mesh_arrived.shape[0],
        m2m_sender,
        act_second,
        member_second,
        m2m_receiver,
        agg_second,
        process_sender,
    )
    back_second = mesh_route(returned_second, mesh_cap, peer_count)
    mesh_grad = upstream + jnp.dot(
        recv_second, process_receiver.T, preferred_element_type=jnp.float32
    )
    mesh_grad = mesh_grad + gather_back(mesh_listed, back_second, mesh_rows.shape[0])
    agg_first = norm_rows_back(summed_first, mesh_grad)
    recv_first, slot_first, returned_first = backward_pass(
        grid_arrived.shape[0],
        g2m_sender,
        act_first,
        member_first,
        g2m_receiver,
        agg_first,
        encode_sender,
    )
    back_first = grid_route(returned_first, grid_cap)
    grid_grad = gather_back(grid_listed, back_first, grid_rows.shape[0]).astype(jnp.bfloat16)
    factor_pairs = (
        (grid_arrived, slot_first),
        (mesh_rows, recv_first),
        (mesh_arrived, slot_second),
        (mesh_first, recv_second),
    )
    blocks = []
    for first_factor, second_factor in factor_pairs:
        blocks.append(
            lax.dot_general(
                first_factor,
                second_factor,
                (((0,), (0,)), ((), ())),
                preferred_element_type=jnp.float32,
            )
        )
    shares = lax.psum_scatter(
        jnp.concatenate(blocks, axis=1).astype(jnp.bfloat16),
        "space",
        scatter_dimension=0,
        tiled=True,
    )
    weight_grad = lax.psum(shares, "rep").astype(jnp.float32)
    return (mesh_final[None], grid_grad[None], weight_grad)


F32 = jnp.float32
BF16 = jnp.bfloat16
INDEX_ROWS = 8
SAMPLE_EDGE_BYTES = 8 << 20


def dot(left, right):
    return jnp.dot(left, right, preferred_element_type=F32)


def dot_first(left, right):
    return lax.dot_general(left, right, (((0,), (0,)), ((), ())), preferred_element_type=F32)


def one_hot(labels, count):
    rows = lax.broadcasted_iota(jnp.int32, (count, labels.shape[-1]), 0)
    return (rows == labels).astype(F32).astype(BF16)


def row_moments(values):
    centred = values - jnp.mean(values, -1, keepdims=True)
    return centred, lax.rsqrt(jnp.mean(centred * centred, -1, keepdims=True) + EPSILON)


def moments_back(normed, scaled, upstream):
    return scaled * (
        upstream
        - jnp.mean(upstream, -1, keepdims=True)
        - normed * jnp.mean(upstream * normed, -1, keepdims=True)
    )


def fetch(pairs, semaphores):
    copies = [
        pltpu.make_async_copy(source, target, semaphores.at[n])
        for n, (source, target) in enumerate(pairs)
    ]
    for copy in copies:
        copy.start()
    for copy in copies:
        copy.wait()


def pack_kernel(*refs):
    sources, packed_ref, index_ref = refs[:8], refs[8], refs[9]
    local, semaphores = refs[10:18], refs[18]
    fetch(list(zip(sources, local)), semaphores)
    (
        grid_ref,
        mesh_ref,
        g2m_pick_ref,
        g2m_sender_ref,
        g2m_receiver_ref,
        m2m_pick_ref,
        m2m_sender_ref,
        m2m_receiver_ref,
    ) = local
    lists, _, capacity = g2m_pick_ref.shape
    mesh_count = mesh_ref.shape[1]
    regions, mesh_cap = m2m_pick_ref.shape[1:]
    edges = g2m_sender_ref.shape[1]
    grid_rows = grid_ref[0]
    for i in range(lists):
        picked = one_hot(g2m_pick_ref[i], grid_rows.shape[0])
        packed_ref[i * capacity : (i + 1) * capacity, :] = dot_first(picked, grid_rows).astype(BF16)
    first = lists * capacity
    packed_ref[first : first + mesh_count, :] = mesh_ref[0]
    index_ref[...] = jnp.zeros_like(index_ref)
    index_ref[0:1, 0:edges] = g2m_sender_ref[...].astype(F32)
    index_ref[0:1, edges : 2 * edges] = g2m_receiver_ref[...].astype(F32)
    index_ref[1:2, 0:edges] = m2m_sender_ref[...].astype(F32)
    index_ref[1:2, edges : 2 * edges] = m2m_receiver_ref[...].astype(F32)
    slots = regions * mesh_cap
    lane = lax.broadcasted_iota(jnp.int32, (mesh_cap, slots), 1)
    spread = (lane % mesh_cap == lax.broadcasted_iota(jnp.int32, (mesh_cap, slots), 0)).astype(F32)
    spread = dot(m2m_pick_ref[0].astype(F32).astype(BF16), spread.astype(BF16))
    lane = lax.broadcasted_iota(jnp.int32, (regions, slots), 1)
    owned = lane // mesh_cap == lax.broadcasted_iota(jnp.int32, (regions, slots), 0)
    index_ref[2:3, 0:slots] = jnp.sum(jnp.where(owned, spread, 0.0), 0, keepdims=True)
    packed_ref[first + mesh_count :, :] = index_ref[...].astype(BF16)


def weights_kernel(source_ref, weights_ref, turned_ref, semaphores):
    fetch([(source_ref, weights_ref)], semaphores)
    latent = weights_ref.shape[0]
    for n, block in enumerate((0, 2, 3)):
        turned_ref[:, n * latent : (n + 1) * latent] = weights_ref[
            :, block * latent : (block + 1) * latent
        ].T


def edge_blocks(edges):
    size = min(edges, 128)
    return [(first, min(size, edges - first)) for first in range(0, edges, size)]


def edge_forward(tables, hot_ref, turned_hot_ref, slope_ref, message_ref, mesh_count):
    regions = len(tables)
    edges = slope_ref.shape[0] // regions
    count = hot_ref.shape[0] // regions
    work = [(d, first, size) for d in range(regions) for first, size in edge_blocks(edges)]

    def gathered(d, first, size):
        rows = slice(d * edges + first, d * edges + first + size)
        return dot(turned_hot_ref[rows, :], tables[d])

    sums = []
    activation = gathered(*work[0])
    for n, (d, first, size) in enumerate(work):
        coming = gathered(*work[n + 1]) if n + 1 < len(work) else None
        activation = activation.astype(BF16)
        squash = 0.5 + 0.5 * jnp.tanh(0.5 * activation)
        message = activation * squash
        rows = slice(d * edges + first, d * edges + first + size)
        slope_ref[rows, :] = squash + message * (1.0 - squash)
        message_ref[rows, :] = message
        activation = coming
        if first + size == edges:
            hot = hot_ref[(d + 1) * count - mesh_count : (d + 1) * count, :]
            sums.append(dot(hot, message_ref[d * edges : (d + 1) * edges, :]))
    return sums


def forward_kernel(
    steps,
    listed,
    mesh_count,
    mesh_cap,
    *refs,
):
    regions = len(steps)
    packed_refs = refs[:regions]
    (
        weights_ref,
        grid_ref,
        mesh_ref,
        first_ref,
        sent_ref,
        hot_one_ref,
        hot_two_ref,
        turned_one_ref,
        turned_two_ref,
        hot_sent_ref,
        slope_one_ref,
        slope_two_ref,
        normed_one_ref,
        scaled_one_ref,
        normed_two_ref,
        scaled_two_ref,
        index_ref,
        message_ref,
        sum_ref,
    ) = refs[regions:]
    latent = weights_ref.shape[0]
    edges = slope_one_ref.shape[0] // regions
    capacity = listed // 3
    slots = regions * mesh_cap
    me = lax.axis_index("space")
    for step, packed_ref in zip(steps, packed_refs):
        region = lax.bitwise_xor(me, step)
        at = lambda rows: pl.ds(pl.multiple_of(region * rows, rows), rows)
        grid_ref[at(listed), :] = packed_ref[:listed, :]
        mesh_ref[at(mesh_count), :] = packed_ref[listed : listed + mesh_count, :]
        index_ref[at(INDEX_ROWS), :] = packed_ref[listed + mesh_count :, :].astype(F32)

    grid_proj = dot(grid_ref[...], weights_ref[:, :latent])
    mesh_proj = dot(mesh_ref[...], weights_ref[:, latent : 2 * latent])
    for d in range(regions):
        index = index_ref[d * INDEX_ROWS : (d + 1) * INDEX_ROWS, :].astype(jnp.int32)
        for row, senders, hot_ref, turned_ref in (
            (0, listed, hot_one_ref, turned_one_ref),
            (1, slots, hot_two_ref, turned_two_ref),
        ):
            count = senders + mesh_count
            hot = jnp.concatenate(
                [
                    one_hot(index[row : row + 1, :edges], senders),
                    one_hot(index[row : row + 1, edges:], mesh_count),
                ],
                axis=0,
            )
            hot_ref[d * count : (d + 1) * count, :] = hot
            turned_ref[d * edges : (d + 1) * edges, :] = hot.T
        hot_sent_ref[d * mesh_count : (d + 1) * mesh_count, :] = one_hot(
            index[2:3, :slots], mesh_count
        )

    blank = jnp.zeros((capacity, latent), F32)
    tables = []
    for d in range(regions):
        before = (d - 1) * listed + 2 * capacity
        within = d * listed + capacity
        after = (d + 1) * listed
        tables.append(
            jnp.concatenate(
                [
                    grid_proj[before : before + capacity] if d > 0 else blank,
                    grid_proj[within : within + capacity],
                    grid_proj[after : after + capacity] if d < regions - 1 else blank,
                    mesh_proj[d * mesh_count : (d + 1) * mesh_count],
                ],
                axis=0,
            ).astype(BF16)
        )
    sums = edge_forward(
        tables, hot_one_ref, turned_one_ref, slope_one_ref, message_ref, mesh_count
    )
    for d in range(regions):
        sum_ref[d * mesh_count : (d + 1) * mesh_count, :] = sums[d]
    centred, scaled = row_moments(sum_ref[...])
    normed = centred * scaled
    normed_one_ref[...] = normed
    scaled_one_ref[...] = jnp.broadcast_to(scaled, scaled_one_ref.shape)
    first_ref[...] = (mesh_ref[...].astype(F32) + normed).astype(BF16)

    for s in range(regions):
        rows = slice(s * mesh_count, (s + 1) * mesh_count)
        sent_ref[s * slots : (s + 1) * slots, :] = dot_first(
            hot_sent_ref[rows, :], first_ref[rows, :]
        ).astype(BF16)
    sent_proj = dot(sent_ref[...], weights_ref[:, 2 * latent : 3 * latent])
    first_proj = dot(first_ref[...], weights_ref[:, 3 * latent :])
    tables = []
    for d in range(regions):
        pieces = [
            sent_proj[s * slots + d * mesh_cap : s * slots + (d + 1) * mesh_cap]
            for s in range(regions)
        ]
        tables.append(
            jnp.concatenate(
                pieces + [first_proj[d * mesh_count : (d + 1) * mesh_count]], axis=0
            ).astype(BF16)
        )
    sums = edge_forward(
        tables, hot_two_ref, turned_two_ref, slope_two_ref, message_ref, mesh_count
    )
    for d in range(regions):
        sum_ref[d * mesh_count : (d + 1) * mesh_count, :] = sums[d]
    centred, scaled = row_moments(sum_ref[...])
    normed_two_ref[...] = centred * scaled
    scaled_two_ref[...] = jnp.broadcast_to(scaled, scaled_two_ref.shape)


def edge_backward(regions, agg_grad_ref, hot_ref, turned_hot_ref, slope_ref, edge_grad_ref):
    mesh_count = agg_grad_ref.shape[0] // len(regions)
    edges = edge_grad_ref.shape[0] // len(regions)
    count = turned_hot_ref.shape[1]
    blank = jnp.zeros((count - mesh_count, agg_grad_ref.shape[1]), BF16)
    work = [(n, first, size) for n in range(len(regions)) for first, size in edge_blocks(edges)]

    def at(n, first, size):
        return pl.ds(pl.multiple_of(regions[n] * edges + first, size), size)

    def gathered(n, first, size):
        own = agg_grad_ref[n * mesh_count : (n + 1) * mesh_count, :]
        return dot(turned_hot_ref[at(n, first, size), :], jnp.concatenate([blank, own], axis=0))

    sums = []
    upstream = gathered(*work[0])
    for k, (n, first, size) in enumerate(work):
        coming = gathered(*work[k + 1]) if k + 1 < len(work) else None
        rows = slice(n * edges + first, n * edges + first + size)
        edge_grad_ref[rows, :] = upstream.astype(BF16) * slope_ref[at(n, first, size), :]
        upstream = coming
        if first + size == edges:
            hot = hot_ref[pl.ds(pl.multiple_of(regions[n] * count, count), count), :]
            sums.append(dot(hot, edge_grad_ref[n * edges : (n + 1) * edges, :]))
    return sums


def halve(share_ref, keep_ref, give_ref):
    half = keep_ref.shape[0]
    core = lax.bitwise_and(lax.axis_index("rep"), 1)
    keep_ref[...] = share_ref[pl.ds(pl.multiple_of(core * half, half), half), :]
    give_ref[...] = share_ref[pl.ds(pl.multiple_of((1 - core) * half, half), half), :]


def process_back_part(
    steps, mesh_count, cotangent_refs, hot_ref, turned_hot_ref, slope_ref, normed_ref, scaled_ref,
    agg_grad_ref, edge_grad_ref,
):
    me = lax.axis_index("space")
    regions = [lax.bitwise_xor(me, step) for step in steps]
    for n, (region, cotangent_ref) in enumerate(zip(regions, cotangent_refs)):
        rows = pl.ds(pl.multiple_of(region * mesh_count, mesh_count), mesh_count)
        agg_grad_ref[n * mesh_count : (n + 1) * mesh_count, :] = moments_back(
            normed_ref[rows, :], scaled_ref[rows, 0:1], cotangent_ref[0].astype(F32)
        ).astype(BF16)
    return regions, edge_backward(
        regions, agg_grad_ref, hot_ref, turned_hot_ref, slope_ref, edge_grad_ref
    )


def near_back_kernel(steps, *refs):
    cotangent_refs, refs = refs[: len(steps)], refs[len(steps) :]
    (
        hot_ref,
        turned_hot_ref,
        slope_ref,
        normed_ref,
        scaled_ref,
        *whole_refs,
    ) = refs[:9]
    sums_ref, *column_refs = refs[9:14]
    agg_grad_ref, edge_grad_ref = refs[14:]
    mesh_count = agg_grad_ref.shape[0] // len(steps)
    count = turned_hot_ref.shape[1]
    _, all_sums = process_back_part(
        steps, mesh_count, cotangent_refs, hot_ref, turned_hot_ref, slope_ref, normed_ref,
        scaled_ref, agg_grad_ref, edge_grad_ref,
    )
    for n, sums in enumerate(all_sums):
        sums_ref[n * count : (n + 1) * count, :] = sums
    columns = column_refs[0].shape[0]
    mine = pl.ds(pl.multiple_of(lax.axis_index("space") * columns, columns), columns)
    for whole_ref, column_ref in zip(whole_refs, column_refs):
        column_ref[...] = whole_ref[:, mine].T


def far_back_kernel(near, far, mesh_cap, *refs):
    regions = len(near) + len(far)
    cotangent_refs, refs = refs[:regions], refs[regions:]
    (
        turned_ref,
        first_columns_ref,
        sent_columns_ref,
        near_sums_ref,
        hot_ref,
        turned_hot_ref,
        hot_sent_ref,
        slope_ref,
        normed_ref,
        scaled_ref,
        mesh_grad_ref,
        keep_ref,
        give_ref,
        upstream_ref,
        slot_ref,
        recv_ref,
        share_ref,
        agg_grad_ref,
        edge_grad_ref,
    ) = refs
    latent = normed_ref.shape[1]
    mesh_count = normed_ref.shape[0] // regions
    count = turned_hot_ref.shape[1]
    slots = regions * mesh_cap
    me = lax.axis_index("space")
    far_regions, all_sums = process_back_part(
        far, mesh_count, cotangent_refs[len(near) :], hot_ref, turned_hot_ref, slope_ref,
        normed_ref, scaled_ref, agg_grad_ref, edge_grad_ref,
    )
    near_regions = [lax.bitwise_xor(me, step) for step in near]
    near_sums = [near_sums_ref[n * count : (n + 1) * count, :] for n in range(len(near))]
    for region, sums in zip(near_regions + far_regions, near_sums + all_sums):
        for s in range(regions):
            slot_ref[pl.ds(pl.multiple_of(s * slots + region * mesh_cap, mesh_cap), mesh_cap), :] = (
                sums[s * mesh_cap : (s + 1) * mesh_cap]
            )
        recv_ref[pl.ds(pl.multiple_of(region * mesh_count, mesh_count), mesh_count), :] = sums[
            slots:
        ].astype(BF16)
    for region, cotangent_ref in zip(near_regions + far_regions, cotangent_refs):
        rows = pl.ds(pl.multiple_of(region * mesh_count, mesh_count), mesh_count)
        upstream_ref[rows, :] = cotangent_ref[0].astype(F32)
    slot_sum = slot_ref[...].astype(BF16)
    share_ref[:, :latent] = dot(sent_columns_ref[...], slot_sum).astype(BF16)
    share_ref[:, latent:] = dot(first_columns_ref[...], recv_ref[...]).astype(BF16)
    halve(share_ref, keep_ref, give_ref)
    returned = dot(slot_sum, turned_ref[:, latent : 2 * latent]).astype(BF16)
    grad = upstream_ref[...] + dot(recv_ref[...], turned_ref[:, 2 * latent :])
    for s in range(regions):
        rows = slice(s * mesh_count, (s + 1) * mesh_count)
        mesh_grad_ref[rows, :] = grad[rows] + dot(
            hot_sent_ref[rows, :], returned[s * slots : (s + 1) * slots]
        )


def encode_back_kernel(
    regions,
    grid_columns_ref,
    mesh_columns_ref,
    hot_ref,
    turned_hot_ref,
    slope_ref,
    normed_ref,
    scaled_ref,
    mesh_grad_ref,
    own_slot_ref,
    keep_ref,
    give_ref,
    slot_ref,
    recv_ref,
    share_ref,
    agg_grad_ref,
    edge_grad_ref,
):
    latent = normed_ref.shape[1]
    mesh_count = normed_ref.shape[0] // regions
    listed = slot_ref.shape[0] // regions
    capacity = listed // 3
    me = lax.axis_index("space")
    agg_grad_ref[...] = moments_back(
        normed_ref[...], scaled_ref[:, 0:1], mesh_grad_ref[...]
    ).astype(BF16)
    blank = jnp.zeros((capacity, latent), BF16)
    slot_ref[0:capacity, :] = blank
    slot_ref[regions * listed - capacity :, :] = blank
    all_sums = edge_backward(
        range(regions), agg_grad_ref, hot_ref, turned_hot_ref, slope_ref, edge_grad_ref
    )
    for d, sums in enumerate(all_sums):
        sums = sums.astype(BF16)
        for j in range(3):
            source = d + j - 1
            if 0 <= source < regions:
                first = source * listed + (2 - j) * capacity
                slot_ref[first : first + capacity, :] = sums[j * capacity : (j + 1) * capacity]
        recv_ref[d * mesh_count : (d + 1) * mesh_count, :] = sums[listed:]
    share_ref[:, :latent] = dot(grid_columns_ref[...], slot_ref[...]).astype(BF16)
    share_ref[:, latent:] = dot(mesh_columns_ref[...], recv_ref[...]).astype(BF16)
    halve(share_ref, keep_ref, give_ref)
    own = pl.ds(pl.multiple_of(me * listed, listed), listed)
    own_slot_ref[...] = slot_ref[own, :]


def results_kernel(
    turned_ref, pick_ref, own_slot_ref, first_ref, normed_ref, grid_grad_ref, mesh_out_ref
):
    mesh_count = mesh_out_ref.shape[1]
    me = lax.axis_index("space")
    own = pl.ds(pl.multiple_of(me * mesh_count, mesh_count), mesh_count)
    mesh_out_ref[0] = (first_ref[own, :].astype(F32) + normed_ref[own, :]).astype(BF16)
    lists, _, capacity = pick_ref.shape
    latent = own_slot_ref.shape[1]
    returned = dot(own_slot_ref[...], turned_ref[:, :latent]).astype(BF16)
    total = None
    for i in range(lists):
        owner = one_hot(pick_ref[i], grid_grad_ref.shape[1])
        part = dot(owner, returned[i * capacity : (i + 1) * capacity])
        total = part if total is None else total + part
    grid_grad_ref[0] = total.astype(BF16)


def place(pairs, stages, semaphores):
    copies = []
    for n, (block_ref, target) in enumerate(pairs):
        stages[n][...] = block_ref[...].astype(F32)
        copies.append(pltpu.make_async_copy(stages[n], target, semaphores.at[n]))
        copies[n].start()
    for copy in copies:
        copy.wait()


def half_rows(half):
    core = lax.bitwise_and(lax.axis_index("rep"), 1)
    mine = pl.ds(pl.multiple_of(core * half, half), half)
    return mine, pl.ds(pl.multiple_of((1 - core) * half, half), half)


def settle_kernel(one_ref, two_ref, other_two_ref, weight_grad_ref, *scratch):
    half, width = one_ref.shape
    mine, other = half_rows(half)
    place(
        [
            (two_ref, weight_grad_ref.at[mine, width:]),
            (other_two_ref, weight_grad_ref.at[other, width:]),
            (one_ref, weight_grad_ref.at[mine, :width]),
        ],
        scratch[:3],
        scratch[3],
    )


def finish_kernel(other_one_ref, settled_ref, weight_grad_ref, stage, semaphores):
    half, width = other_one_ref.shape
    _, other = half_rows(half)
    place([(other_one_ref, weight_grad_ref.at[other, :width])], [stage], semaphores)


VMEM = pl.BlockSpec(memory_space=pltpu.VMEM)


def call(kernel, operands, outputs, scratch, flops, fetched=0):
    hbm = pl.BlockSpec(memory_space=pltpu.HBM)
    operands = [
        pltpu.with_memory_space_constraint(operand, pltpu.HBM) if n < fetched else operand
        for n, operand in enumerate(operands)
    ]
    return pl.pallas_call(
        kernel,
        out_shape=[jax.ShapeDtypeStruct(shape, kind) for shape, kind in outputs],
        in_specs=[hbm] * fetched + [VMEM] * (len(operands) - fetched),
        out_specs=[VMEM] * len(outputs),
        scratch_shapes=[pltpu.VMEM(shape, kind) for shape, kind in scratch]
        + ([pltpu.SemaphoreType.DMA((fetched,))] if fetched else []),
        compiler_params=pltpu.CompilerParams(vmem_limit_bytes=40 << 20),
        cost_estimate=pl.CostEstimate(flops=flops, bytes_accessed=4 << 20, transcendentals=0),
    )(*operands)


def swap(block, axis, bits):
    return lax.ppermute(block, axis, [(i, i ^ bits) for i in range(lax.axis_size(axis))])


def added(left, right):
    return (left.astype(F32) + right.astype(F32)).astype(BF16)


def summed_over_chips(half):
    bit = 2
    while bit < lax.axis_size("rep"):
        half = added(half, swap(half, "rep", bit))
        bit *= 2
    return half


def whole_sample_body(
    grid_latent,
    mesh_latent,
    mesh_cotangent,
    weights,
    g2m_pick,
    g2m_sender,
    g2m_receiver,
    m2m_pick,
    m2m_sender,
    m2m_receiver,
):
    regions = lax.axis_size("space")
    latent = weights.shape[0]
    listed = g2m_pick.shape[1] * g2m_pick.shape[2]
    mesh_count = mesh_latent.shape[1]
    mesh_cap = m2m_pick.shape[2]
    edges = g2m_sender.shape[0]
    columns = latent // regions
    half = columns // 2
    g2m_pick = g2m_pick.transpose(1, 0, 2)
    sources = (
        grid_latent,
        mesh_latent,
        g2m_pick,
        g2m_sender.reshape(1, -1),
        g2m_receiver.reshape(1, -1),
        m2m_pick,
        m2m_sender.reshape(1, -1),
        m2m_receiver.reshape(1, -1),
    )
    packed = call(
        pack_kernel,
        sources,
        [((listed + mesh_count + INDEX_ROWS, latent), BF16)],
        [((INDEX_ROWS, latent), F32)] + [(source.shape, source.dtype) for source in sources],
        10**7,
        fetched=len(sources),
    )[0]
    packed, cotangent, weights = lax.optimization_barrier((packed, mesh_cotangent, weights))
    steps = (0, *range(2, regions), 1)
    packs = [packed] + [swap(packed, "space", step) for step in steps[1:]]
    near = swap(cotangent, "space", 1)
    weights, turned = call(
        weights_kernel,
        (weights,),
        [(weights.shape, BF16), ((latent, 3 * latent), BF16)],
        [],
        10**8,
        fetched=1,
    )
    turned, early = lax.optimization_barrier((turned, cotangent))
    packs[1], late = lax.optimization_barrier((packs[1], cotangent))
    cotangents = (
        [cotangent, swap(late, "space", steps[1])]
        + [swap(early, "space", step) for step in steps[2:-1]]
        + [near]
    )
    rows = regions * mesh_count
    slots = regions * mesh_cap
    (
        grid_all,
        mesh_all,
        mesh_first,
        mesh_sent,
        hot_one,
        hot_two,
        turned_one,
        turned_two,
        hot_sent,
        slope_one,
        slope_two,
        normed_one,
        scaled_one,
        normed_two,
        scaled_two,
    ) = call(
        functools.partial(forward_kernel, steps, listed, mesh_count, mesh_cap),
        (*packs, weights),
        [
            ((regions * listed, latent), BF16),
            ((rows, latent), BF16),
            ((rows, latent), BF16),
            ((regions * slots, latent), BF16),
            ((regions * (listed + mesh_count), edges), BF16),
            ((regions * (slots + mesh_count), edges), BF16),
            ((regions * edges, listed + mesh_count), BF16),
            ((regions * edges, slots + mesh_count), BF16),
            ((rows, slots), BF16),
            ((regions * edges, latent), BF16),
            ((regions * edges, latent), BF16),
            ((rows, latent), F32),
            ((rows, 128), F32),
            ((rows, latent), F32),
            ((rows, 128), F32),
        ],
        [
            ((regions * INDEX_ROWS, latent), F32),
            ((regions * edges, latent), BF16),
            ((rows, latent), F32),
        ],
        2 * 10**9,
    )
    by_step = dict(zip(steps, cotangents))
    near, far = (0, 1), tuple(step for step in steps if step > 1)
    count = slots + mesh_count
    near_sums, grid_columns, mesh_columns, sent_columns, first_columns = call(
        functools.partial(near_back_kernel, near),
        (
            *(by_step[step] for step in near),
            hot_two,
            turned_two,
            slope_two,
            normed_two,
            scaled_two,
            grid_all,
            mesh_all,
            mesh_sent,
            mesh_first,
        ),
        [
            ((len(near) * count, latent), F32),
            ((columns, regions * listed), BF16),
            ((columns, rows), BF16),
            ((columns, regions * slots), BF16),
            ((columns, rows), BF16),
        ],
        [((len(near) * mesh_count, latent), BF16), ((len(near) * edges, latent), BF16)],
        10**9,
    )
    mesh_grad, keep_two, give_two = call(
        functools.partial(far_back_kernel, near, far, mesh_cap),
        (
            *(by_step[step] for step in near + far),
            turned,
            first_columns,
            sent_columns,
            near_sums,
            hot_two,
            turned_two,
            hot_sent,
            slope_two,
            normed_two,
            scaled_two,
        ),
        [((rows, latent), F32)] + [((half, 2 * latent), BF16)] * 2,
        [
            ((rows, latent), F32),
            ((regions * slots, latent), F32),
            ((rows, latent), BF16),
            ((columns, 2 * latent), BF16),
            ((len(far) * mesh_count, latent), BF16),
            ((len(far) * edges, latent), BF16),
        ],
        10**9,
    )
    own_slots, keep_one, give_one = call(
        functools.partial(encode_back_kernel, regions),
        (
            grid_columns,
            mesh_columns,
            hot_one,
            turned_one,
            slope_one,
            normed_one,
            scaled_one,
            mesh_grad,
        ),
        [((listed, latent), BF16)] + [((half, 2 * latent), BF16)] * 2,
        [
            ((regions * listed, latent), BF16),
            ((rows, latent), BF16),
            ((columns, 2 * latent), BF16),
            ((rows, latent), BF16),
            ((regions * edges, latent), BF16),
        ],
        10**9,
    )
    half_one = added(keep_one, swap(give_one, "rep", 1))
    half_two = added(keep_two, swap(give_two, "rep", 1))
    half_one, own_slots = lax.optimization_barrier((half_one, own_slots))
    grid_grad, mesh_out = call(
        results_kernel,
        (turned, g2m_pick, own_slots, mesh_first, normed_two),
        [(grid_latent.shape, BF16), (mesh_latent.shape, BF16)],
        [],
        10**8,
    )
    two = summed_over_chips(half_two)
    one, grid_grad = lax.optimization_barrier((summed_over_chips(half_one), grid_grad))
    hbm = pl.BlockSpec(memory_space=pltpu.HBM)
    stage = pltpu.VMEM((half, 2 * latent), F32)
    weight_shape = pltpu.HBM((columns, 4 * latent), F32)
    limit = pltpu.CompilerParams(vmem_limit_bytes=40 << 20)
    settled = pl.pallas_call(
        settle_kernel,
        out_shape=weight_shape,
        in_specs=[VMEM] * 3,
        out_specs=hbm,
        scratch_shapes=[stage] * 3 + [pltpu.SemaphoreType.DMA((3,))],
        compiler_params=limit,
    )(one, two, swap(two, "rep", 1))
    weight_grad = pl.pallas_call(
        finish_kernel,
        out_shape=weight_shape,
        in_specs=[VMEM, hbm],
        out_specs=hbm,
        scratch_shapes=[stage, pltpu.SemaphoreType.DMA((1,))],
        input_output_aliases={1: 0},
        compiler_params=limit,
    )(swap(one, "rep", 1), settled)
    return (mesh_out, grid_grad, weight_grad)


def solution(mesh):
    regions = mesh.shape["space"]
    samples = mesh.shape["rep"]

    def whole(*arguments):
        edges = arguments[5].shape[0] + arguments[8].shape[0]
        latent = arguments[3].shape[0]
        fits = edges * latent * 4 <= SAMPLE_EDGE_BYTES and latent % (128 * regions) == 0
        paired = regions > 2 and samples > 1 and not (regions & (regions - 1) | samples & (samples - 1))
        return sharded(whole_sample_body if fits and paired else partitioned_body)(*arguments)

    def sharded(body):
        return jax.shard_map(
            body,
            mesh=mesh,
            in_specs=(
                P(("groups", "rep"), "space", None),
                P(("groups", "rep"), "space", None),
                P(("groups", "rep"), "space", None),
                P(),
                P("space", None, None),
                P("space"),
                P("space"),
                P("space", None, None),
                P("space"),
                P("space"),
            ),
            out_specs=(
                P(("groups", "rep"), "space", None),
                P(("groups", "rep"), "space", None),
                P(("groups", "space"), None),
            ),
            check_vma=False,
        )

    return whole
```

```python
import functools

import jax
import jax.numpy as jnp
from jax import lax
from jax.experimental import pallas as pl
from jax.experimental.pallas import tpu as pltpu
from jax.sharding import PartitionSpec as P

EPSILON = 1e-05


def with_halo(cells, sides, width):
    for axis, dim in sides:
        count = lax.axis_size(axis)
        ends = count - 1
        head = lax.slice_in_dim(cells, 0, width, axis=dim)
        tail = lax.slice_in_dim(cells, cells.shape[dim] - width, cells.shape[dim], axis=dim)
        cells = jnp.concatenate(
            [
                lax.ppermute(tail, axis, [(i, (i + 1) % count) for i in range(ends)]),
                cells,
                lax.ppermute(head, axis, [((i + 1) % count, i) for i in range(ends)]),
            ],
            axis=dim,
        )
    return cells


def swish(values):
    return values * jax.nn.sigmoid(values)


def swish_slope(values):
    squash = jax.nn.sigmoid(values)
    return squash * (1.0 + values * (1.0 - squash))


def norm_rows(values):
    centred = values - jnp.mean(values, -1, keepdims=True)
    return centred * lax.rsqrt(jnp.mean(centred * centred, -1, keepdims=True) + EPSILON)


def norm_rows_back(values, upstream):
    centred = values - jnp.mean(values, -1, keepdims=True)
    scaled = lax.rsqrt(jnp.mean(centred * centred, -1, keepdims=True) + EPSILON)
    normed = centred * scaled
    return scaled * (
        upstream
        - jnp.mean(upstream, -1, keepdims=True)
        - normed * jnp.mean(upstream * normed, -1, keepdims=True)
    )


def slot_rows(pick_row):
    listed = pick_row.reshape(-1)
    return listed


def mesh_route(outgoing, capacity, peer_count):
    columns = outgoing.shape[1]
    pieces = lax.all_to_all(
        outgoing.reshape(peer_count, capacity, columns),
        "space",
        split_axis=0,
        concat_axis=0,
        tiled=True,
    )
    arrived = pieces.reshape(peer_count * capacity, columns)
    return arrived


def grid_route(outgoing, capacity):
    columns = outgoing.shape[1]
    lists = outgoing.reshape(3, capacity, columns)
    rims = with_halo(jnp.stack([lists[0], lists[2]]), (("space", 0),), 1)
    return jnp.concatenate([rims[0], lists[1], rims[3]], axis=0)


def edge_pass(arrived, recv_table, located, receiver, w_send, w_recv):
    recv_proj = jnp.dot(recv_table, w_recv, preferred_element_type=jnp.float32)
    slot_proj = jnp.dot(arrived, w_send, preferred_element_type=jnp.float32)
    activation = slot_proj[located] + recv_proj[receiver]
    message = swish(activation).astype(jnp.bfloat16)
    member = (
        receiver[None, :] == jnp.arange(recv_table.shape[0], dtype=jnp.int32)[:, None]
    ).astype(jnp.bfloat16)
    summed = jnp.dot(member, message, preferred_element_type=jnp.float32)
    return (activation, member, summed)


def backward_pass(slot_count, located, activation, member, receiver, agg_grad, w_send):
    edge_grad = (agg_grad[receiver] * swish_slope(activation)).astype(jnp.bfloat16)
    recv_sum = jnp.dot(member, edge_grad, preferred_element_type=jnp.float32).astype(jnp.bfloat16)
    slot_member = (located[None, :] == jnp.arange(slot_count, dtype=jnp.int32)[:, None]).astype(
        jnp.bfloat16
    )
    slot_sum = jnp.dot(slot_member, edge_grad, preferred_element_type=jnp.float32).astype(
        jnp.bfloat16
    )
    returned = jnp.dot(slot_sum, w_send.T, preferred_element_type=jnp.float32).astype(jnp.bfloat16)
    return (recv_sum, slot_sum, returned)


def gather_back(listed, back_rows, row_count):
    owner = (listed[None, :] == jnp.arange(row_count, dtype=jnp.int32)[:, None]).astype(
        jnp.bfloat16
    )
    return jnp.dot(owner, back_rows, preferred_element_type=jnp.float32)


def partitioned_body(
    grid_latent,
    mesh_latent,
    mesh_cotangent,
    weights,
    g2m_pick,
    g2m_sender,
    g2m_receiver,
    m2m_pick,
    m2m_sender,
    m2m_receiver,
):
    grid_rows = grid_latent[0]
    mesh_rows = mesh_latent[0]
    upstream = mesh_cotangent[0].astype(jnp.float32)
    latent = weights.shape[0]
    encode_sender = weights[:, :latent]
    encode_receiver = weights[:, latent : 2 * latent]
    process_sender = weights[:, 2 * latent : 3 * latent]
    process_receiver = weights[:, 3 * latent :]
    peer_count = lax.axis_size("space")
    grid_cap = g2m_pick.shape[2]
    mesh_cap = m2m_pick.shape[2]
    grid_listed = g2m_pick[0].reshape(-1)
    grid_arrived = grid_route(grid_rows[grid_listed], grid_cap)
    act_first, member_first, summed_first = edge_pass(
        grid_arrived, mesh_rows, g2m_sender, g2m_receiver, encode_sender, encode_receiver
    )
    mesh_first = (mesh_rows.astype(jnp.float32) + norm_rows(summed_first)).astype(jnp.bfloat16)
    mesh_listed = slot_rows(m2m_pick[0])
    mesh_arrived = mesh_route(mesh_first[mesh_listed], mesh_cap, peer_count)
    act_second, member_second, summed_second = edge_pass(
        mesh_arrived, mesh_first, m2m_sender, m2m_receiver, process_sender, process_receiver
    )
    mesh_final = (mesh_first.astype(jnp.float32) + norm_rows(summed_second)).astype(jnp.bfloat16)
    agg_second = norm_rows_back(summed_second, upstream)
    recv_second, slot_second, returned_second = backward_pass(
        mesh_arrived.shape[0],
        m2m_sender,
        act_second,
        member_second,
        m2m_receiver,
        agg_second,
        process_sender,
    )
    back_second = mesh_route(returned_second, mesh_cap, peer_count)
    mesh_grad = upstream + jnp.dot(
        recv_second, process_receiver.T, preferred_element_type=jnp.float32
    )
    mesh_grad = mesh_grad + gather_back(mesh_listed, back_second, mesh_rows.shape[0])
    agg_first = norm_rows_back(summed_first, mesh_grad)
    recv_first, slot_first, returned_first = backward_pass(
        grid_arrived.shape[0],
        g2m_sender,
        act_first,
        member_first,
        g2m_receiver,
        agg_first,
        encode_sender,
    )
    back_first = grid_route(returned_first, grid_cap)
    grid_grad = gather_back(grid_listed, back_first, grid_rows.shape[0]).astype(jnp.bfloat16)
    factor_pairs = (
        (grid_arrived, slot_first),
        (mesh_rows, recv_first),
        (mesh_arrived, slot_second),
        (mesh_first, recv_second),
    )
    blocks = []
    for first_factor, second_factor in factor_pairs:
        blocks.append(
            lax.dot_general(
                first_factor,
                second_factor,
                (((0,), (0,)), ((), ())),
                preferred_element_type=jnp.float32,
            )
        )
    shares = lax.psum_scatter(
        jnp.concatenate(blocks, axis=1).astype(jnp.bfloat16),
        "space",
        scatter_dimension=0,
        tiled=True,
    )
    weight_grad = lax.psum(shares, "rep").astype(jnp.float32)
    return (mesh_final[None], grid_grad[None], weight_grad)


F32 = jnp.float32
BF16 = jnp.bfloat16
INDEX_ROWS = 8
SAMPLE_EDGE_BYTES = 8 << 20


def dot(left, right):
    return jnp.dot(left, right, preferred_element_type=F32)


def dot_first(left, right):
    return lax.dot_general(left, right, (((0,), (0,)), ((), ())), preferred_element_type=F32)


def one_hot(labels, count):
    rows = lax.broadcasted_iota(jnp.int32, (count, labels.shape[-1]), 0)
    return (rows == labels).astype(F32).astype(BF16)


def row_moments(values):
    centred = values - jnp.mean(values, -1, keepdims=True)
    return centred, lax.rsqrt(jnp.mean(centred * centred, -1, keepdims=True) + EPSILON)


def moments_back(normed, scaled, upstream):
    return scaled * (
        upstream
        - jnp.mean(upstream, -1, keepdims=True)
        - normed * jnp.mean(upstream * normed, -1, keepdims=True)
    )


def fetch(pairs, semaphores):
    copies = [
        pltpu.make_async_copy(source, target, semaphores.at[n])
        for n, (source, target) in enumerate(pairs)
    ]
    for copy in copies:
        copy.start()
    for copy in copies:
        copy.wait()


def pack_kernel(*refs):
    sources, packed_ref, index_ref = refs[:8], refs[8], refs[9]
    local, semaphores = refs[10:18], refs[18]
    fetch(list(zip(sources, local)), semaphores)
    (
        grid_ref,
        mesh_ref,
        g2m_pick_ref,
        g2m_sender_ref,
        g2m_receiver_ref,
        m2m_pick_ref,
        m2m_sender_ref,
        m2m_receiver_ref,
    ) = local
    lists, _, capacity = g2m_pick_ref.shape
    mesh_count = mesh_ref.shape[1]
    regions, mesh_cap = m2m_pick_ref.shape[1:]
    edges = g2m_sender_ref.shape[1]
    grid_rows = grid_ref[0]
    for i in range(lists):
        picked = one_hot(g2m_pick_ref[i], grid_rows.shape[0])
        packed_ref[i * capacity : (i + 1) * capacity, :] = dot_first(picked, grid_rows).astype(BF16)
    first = lists * capacity
    packed_ref[first : first + mesh_count, :] = mesh_ref[0]
    index_ref[...] = jnp.zeros_like(index_ref)
    index_ref[0:1, 0:edges] = g2m_sender_ref[...].astype(F32)
    index_ref[0:1, edges : 2 * edges] = g2m_receiver_ref[...].astype(F32)
    index_ref[1:2, 0:edges] = m2m_sender_ref[...].astype(F32)
    index_ref[1:2, edges : 2 * edges] = m2m_receiver_ref[...].astype(F32)
    slots = regions * mesh_cap
    lane = lax.broadcasted_iota(jnp.int32, (mesh_cap, slots), 1)
    spread = (lane % mesh_cap == lax.broadcasted_iota(jnp.int32, (mesh_cap, slots), 0)).astype(F32)
    spread = dot(m2m_pick_ref[0].astype(F32).astype(BF16), spread.astype(BF16))
    lane = lax.broadcasted_iota(jnp.int32, (regions, slots), 1)
    owned = lane // mesh_cap == lax.broadcasted_iota(jnp.int32, (regions, slots), 0)
    index_ref[2:3, 0:slots] = jnp.sum(jnp.where(owned, spread, 0.0), 0, keepdims=True)
    packed_ref[first + mesh_count :, :] = index_ref[...].astype(BF16)


def weights_kernel(source_ref, weights_ref, turned_ref, semaphores):
    fetch([(source_ref, weights_ref)], semaphores)
    latent = weights_ref.shape[0]
    for n, block in enumerate((0, 2, 3)):
        turned_ref[:, n * latent : (n + 1) * latent] = weights_ref[
            :, block * latent : (block + 1) * latent
        ].T


def edge_blocks(edges):
    size = min(edges, 128)
    return [(first, min(size, edges - first)) for first in range(0, edges, size)]


def edge_forward(tables, hot_ref, turned_hot_ref, slope_ref, message_ref, mesh_count):
    regions = len(tables)
    edges = slope_ref.shape[0] // regions
    count = hot_ref.shape[0] // regions
    work = [(d, first, size) for d in range(regions) for first, size in edge_blocks(edges)]

    def gathered(d, first, size):
        rows = slice(d * edges + first, d * edges + first + size)
        return dot(turned_hot_ref[rows, :], tables[d])

    sums = []
    activation = gathered(*work[0])
    for n, (d, first, size) in enumerate(work):
        coming = gathered(*work[n + 1]) if n + 1 < len(work) else None
        activation = activation.astype(BF16)
        squash = 0.5 + 0.5 * jnp.tanh(0.5 * activation)
        message = activation * squash
        rows = slice(d * edges + first, d * edges + first + size)
        slope_ref[rows, :] = squash + message * (1.0 - squash)
        message_ref[rows, :] = message
        activation = coming
        if first + size == edges:
            hot = hot_ref[(d + 1) * count - mesh_count : (d + 1) * count, :]
            sums.append(dot(hot, message_ref[d * edges : (d + 1) * edges, :]))
    return sums


def forward_kernel(
    steps,
    listed,
    mesh_count,
    mesh_cap,
    *refs,
):
    regions = len(steps)
    packed_refs = refs[:regions]
    (
        weights_ref,
        grid_ref,
        mesh_ref,
        first_ref,
        sent_ref,
        hot_one_ref,
        hot_two_ref,
        turned_one_ref,
        turned_two_ref,
        hot_sent_ref,
        slope_one_ref,
        slope_two_ref,
        normed_one_ref,
        scaled_one_ref,
        normed_two_ref,
        scaled_two_ref,
        index_ref,
        message_ref,
        sum_ref,
    ) = refs[regions:]
    latent = weights_ref.shape[0]
    edges = slope_one_ref.shape[0] // regions
    capacity = listed // 3
    slots = regions * mesh_cap
    me = lax.axis_index("space")
    for step, packed_ref in zip(steps, packed_refs):
        region = lax.rem(me + (regions - step), regions)
        at = lambda rows: pl.ds(pl.multiple_of(region * rows, rows), rows)
        grid_ref[at(listed), :] = packed_ref[:listed, :]
        mesh_ref[at(mesh_count), :] = packed_ref[listed : listed + mesh_count, :]
        index_ref[at(INDEX_ROWS), :] = packed_ref[listed + mesh_count :, :].astype(F32)

    grid_proj = dot(grid_ref[...], weights_ref[:, :latent])
    mesh_proj = dot(mesh_ref[...], weights_ref[:, latent : 2 * latent])
    for d in range(regions):
        index = index_ref[d * INDEX_ROWS : (d + 1) * INDEX_ROWS, :].astype(jnp.int32)
        for row, senders, hot_ref, turned_ref in (
            (0, listed, hot_one_ref, turned_one_ref),
            (1, slots, hot_two_ref, turned_two_ref),
        ):
            count = senders + mesh_count
            hot = jnp.concatenate(
                [
                    one_hot(index[row : row + 1, :edges], senders),
                    one_hot(index[row : row + 1, edges:], mesh_count),
                ],
                axis=0,
            )
            hot_ref[d * count : (d + 1) * count, :] = hot
            turned_ref[d * edges : (d + 1) * edges, :] = hot.T
        hot_sent_ref[d * mesh_count : (d + 1) * mesh_count, :] = one_hot(
            index[2:3, :slots], mesh_count
        )

    blank = jnp.zeros((capacity, latent), F32)
    tables = []
    for d in range(regions):
        before = (d - 1) * listed + 2 * capacity
        within = d * listed + capacity
        after = (d + 1) * listed
        tables.append(
            jnp.concatenate(
                [
                    grid_proj[before : before + capacity] if d > 0 else blank,
                    grid_proj[within : within + capacity],
                    grid_proj[after : after + capacity] if d < regions - 1 else blank,
                    mesh_proj[d * mesh_count : (d + 1) * mesh_count],
                ],
                axis=0,
            ).astype(BF16)
        )
    sums = edge_forward(
        tables, hot_one_ref, turned_one_ref, slope_one_ref, message_ref, mesh_count
    )
    for d in range(regions):
        sum_ref[d * mesh_count : (d + 1) * mesh_count, :] = sums[d]
    centred, scaled = row_moments(sum_ref[...])
    normed = centred * scaled
    normed_one_ref[...] = normed
    scaled_one_ref[...] = jnp.broadcast_to(scaled, scaled_one_ref.shape)
    first_ref[...] = (mesh_ref[...].astype(F32) + normed).astype(BF16)

    for s in range(regions):
        rows = slice(s * mesh_count, (s + 1) * mesh_count)
        sent_ref[s * slots : (s + 1) * slots, :] = dot_first(
            hot_sent_ref[rows, :], first_ref[rows, :]
        ).astype(BF16)
    sent_proj = dot(sent_ref[...], weights_ref[:, 2 * latent : 3 * latent])
    first_proj = dot(first_ref[...], weights_ref[:, 3 * latent :])
    tables = []
    for d in range(regions):
        pieces = [
            sent_proj[s * slots + d * mesh_cap : s * slots + (d + 1) * mesh_cap]
            for s in range(regions)
        ]
        tables.append(
            jnp.concatenate(
                pieces + [first_proj[d * mesh_count : (d + 1) * mesh_count]], axis=0
            ).astype(BF16)
        )
    sums = edge_forward(
        tables, hot_two_ref, turned_two_ref, slope_two_ref, message_ref, mesh_count
    )
    for d in range(regions):
        sum_ref[d * mesh_count : (d + 1) * mesh_count, :] = sums[d]
    centred, scaled = row_moments(sum_ref[...])
    normed_two_ref[...] = centred * scaled
    scaled_two_ref[...] = jnp.broadcast_to(scaled, scaled_two_ref.shape)


def edge_backward(regions, agg_grad_ref, hot_ref, turned_hot_ref, slope_ref, edge_grad_ref):
    mesh_count = agg_grad_ref.shape[0] // len(regions)
    edges = edge_grad_ref.shape[0] // len(regions)
    count = turned_hot_ref.shape[1]
    blank = jnp.zeros((count - mesh_count, agg_grad_ref.shape[1]), BF16)
    work = [(n, first, size) for n in range(len(regions)) for first, size in edge_blocks(edges)]

    def at(n, first, size):
        return pl.ds(pl.multiple_of(regions[n] * edges + first, size), size)

    def gathered(n, first, size):
        own = agg_grad_ref[n * mesh_count : (n + 1) * mesh_count, :]
        return dot(turned_hot_ref[at(n, first, size), :], jnp.concatenate([blank, own], axis=0))

    sums = []
    upstream = gathered(*work[0])
    for k, (n, first, size) in enumerate(work):
        coming = gathered(*work[k + 1]) if k + 1 < len(work) else None
        rows = slice(n * edges + first, n * edges + first + size)
        edge_grad_ref[rows, :] = upstream.astype(BF16) * slope_ref[at(n, first, size), :]
        upstream = coming
        if first + size == edges:
            hot = hot_ref[pl.ds(pl.multiple_of(regions[n] * count, count), count), :]
            sums.append(dot(hot, edge_grad_ref[n * edges : (n + 1) * edges, :]))
    return sums


def halve(share_ref, keep_ref, give_ref):
    half = keep_ref.shape[0]
    core = lax.bitwise_and(lax.axis_index("rep"), 1)
    keep_ref[...] = share_ref[pl.ds(pl.multiple_of(core * half, half), half), :]
    give_ref[...] = share_ref[pl.ds(pl.multiple_of((1 - core) * half, half), half), :]


def process_back_part(
    steps, mesh_count, cotangent_refs, hot_ref, turned_hot_ref, slope_ref, normed_ref, scaled_ref,
    agg_grad_ref, edge_grad_ref,
):
    me = lax.axis_index("space")
    regions = [lax.bitwise_xor(me, step) for step in steps]
    for n, (region, cotangent_ref) in enumerate(zip(regions, cotangent_refs)):
        rows = pl.ds(pl.multiple_of(region * mesh_count, mesh_count), mesh_count)
        agg_grad_ref[n * mesh_count : (n + 1) * mesh_count, :] = moments_back(
            normed_ref[rows, :], scaled_ref[rows, 0:1], cotangent_ref[0].astype(F32)
        ).astype(BF16)
    return regions, edge_backward(
        regions, agg_grad_ref, hot_ref, turned_hot_ref, slope_ref, edge_grad_ref
    )


def near_back_kernel(steps, *refs):
    cotangent_refs, refs = refs[: len(steps)], refs[len(steps) :]
    (
        hot_ref,
        turned_hot_ref,
        slope_ref,
        normed_ref,
        scaled_ref,
        *whole_refs,
    ) = refs[:9]
    sums_ref, *column_refs = refs[9:14]
    agg_grad_ref, edge_grad_ref = refs[14:]
    mesh_count = agg_grad_ref.shape[0] // len(steps)
    count = turned_hot_ref.shape[1]
    _, all_sums = process_back_part(
        steps, mesh_count, cotangent_refs, hot_ref, turned_hot_ref, slope_ref, normed_ref,
        scaled_ref, agg_grad_ref, edge_grad_ref,
    )
    for n, sums in enumerate(all_sums):
        sums_ref[n * count : (n + 1) * count, :] = sums
    columns = column_refs[0].shape[0]
    mine = pl.ds(pl.multiple_of(lax.axis_index("space") * columns, columns), columns)
    for whole_ref, column_ref in zip(whole_refs, column_refs):
        column_ref[...] = whole_ref[:, mine].T


def far_back_kernel(near, far, mesh_cap, *refs):
    regions = len(near) + len(far)
    cotangent_refs, refs = refs[:regions], refs[regions:]
    (
        turned_ref,
        first_columns_ref,
        sent_columns_ref,
        near_sums_ref,
        hot_ref,
        turned_hot_ref,
        hot_sent_ref,
        slope_ref,
        normed_ref,
        scaled_ref,
        mesh_grad_ref,
        keep_ref,
        give_ref,
        upstream_ref,
        slot_ref,
        recv_ref,
        share_ref,
        agg_grad_ref,
        edge_grad_ref,
    ) = refs
    latent = normed_ref.shape[1]
    mesh_count = normed_ref.shape[0] // regions
    count = turned_hot_ref.shape[1]
    slots = regions * mesh_cap
    me = lax.axis_index("space")
    far_regions, all_sums = process_back_part(
        far, mesh_count, cotangent_refs[len(near) :], hot_ref, turned_hot_ref, slope_ref,
        normed_ref, scaled_ref, agg_grad_ref, edge_grad_ref,
    )
    near_regions = [lax.bitwise_xor(me, step) for step in near]
    near_sums = [near_sums_ref[n * count : (n + 1) * count, :] for n in range(len(near))]
    for region, sums in zip(near_regions + far_regions, near_sums + all_sums):
        for s in range(regions):
            slot_ref[pl.ds(pl.multiple_of(s * slots + region * mesh_cap, mesh_cap), mesh_cap), :] = (
                sums[s * mesh_cap : (s + 1) * mesh_cap]
            )
        recv_ref[pl.ds(pl.multiple_of(region * mesh_count, mesh_count), mesh_count), :] = sums[
            slots:
        ].astype(BF16)
    for region, cotangent_ref in zip(near_regions + far_regions, cotangent_refs):
        rows = pl.ds(pl.multiple_of(region * mesh_count, mesh_count), mesh_count)
        upstream_ref[rows, :] = cotangent_ref[0].astype(F32)
    slot_sum = slot_ref[...].astype(BF16)
    share_ref[:, :latent] = dot(sent_columns_ref[...], slot_sum).astype(BF16)
    share_ref[:, latent:] = dot(first_columns_ref[...], recv_ref[...]).astype(BF16)
    halve(share_ref, keep_ref, give_ref)
    returned = dot(slot_sum, turned_ref[:, latent : 2 * latent]).astype(BF16)
    grad = upstream_ref[...] + dot(recv_ref[...], turned_ref[:, 2 * latent :])
    for s in range(regions):
        rows = slice(s * mesh_count, (s + 1) * mesh_count)
        mesh_grad_ref[rows, :] = grad[rows] + dot(
            hot_sent_ref[rows, :], returned[s * slots : (s + 1) * slots]
        )


def encode_back_kernel(
    regions,
    grid_columns_ref,
    mesh_columns_ref,
    hot_ref,
    turned_hot_ref,
    slope_ref,
    normed_ref,
    scaled_ref,
    mesh_grad_ref,
    own_slot_ref,
    keep_ref,
    give_ref,
    slot_ref,
    recv_ref,
    share_ref,
    agg_grad_ref,
    edge_grad_ref,
):
    latent = normed_ref.shape[1]
    mesh_count = normed_ref.shape[0] // regions
    listed = slot_ref.shape[0] // regions
    capacity = listed // 3
    me = lax.axis_index("space")
    agg_grad_ref[...] = moments_back(
        normed_ref[...], scaled_ref[:, 0:1], mesh_grad_ref[...]
    ).astype(BF16)
    blank = jnp.zeros((capacity, latent), BF16)
    slot_ref[0:capacity, :] = blank
    slot_ref[regions * listed - capacity :, :] = blank
    all_sums = edge_backward(
        range(regions), agg_grad_ref, hot_ref, turned_hot_ref, slope_ref, edge_grad_ref
    )
    for d, sums in enumerate(all_sums):
        sums = sums.astype(BF16)
        for j in range(3):
            source = d + j - 1
            if 0 <= source < regions:
                first = source * listed + (2 - j) * capacity
                slot_ref[first : first + capacity, :] = sums[j * capacity : (j + 1) * capacity]
        recv_ref[d * mesh_count : (d + 1) * mesh_count, :] = sums[listed:]
    share_ref[:, :latent] = dot(grid_columns_ref[...], slot_ref[...]).astype(BF16)
    share_ref[:, latent:] = dot(mesh_columns_ref[...], recv_ref[...]).astype(BF16)
    halve(share_ref, keep_ref, give_ref)
    own = pl.ds(pl.multiple_of(me * listed, listed), listed)
    own_slot_ref[...] = slot_ref[own, :]


def results_kernel(
    turned_ref, pick_ref, own_slot_ref, first_ref, normed_ref, grid_grad_ref, mesh_out_ref
):
    mesh_count = mesh_out_ref.shape[1]
    me = lax.axis_index("space")
    own = pl.ds(pl.multiple_of(me * mesh_count, mesh_count), mesh_count)
    mesh_out_ref[0] = (first_ref[own, :].astype(F32) + normed_ref[own, :]).astype(BF16)
    lists, _, capacity = pick_ref.shape
    latent = own_slot_ref.shape[1]
    returned = dot(own_slot_ref[...], turned_ref[:, :latent]).astype(BF16)
    total = None
    for i in range(lists):
        owner = one_hot(pick_ref[i], grid_grad_ref.shape[1])
        part = dot(owner, returned[i * capacity : (i + 1) * capacity])
        total = part if total is None else total + part
    grid_grad_ref[0] = total.astype(BF16)


def place(pairs, stages, semaphores):
    copies = []
    for n, (block_ref, target) in enumerate(pairs):
        stages[n][...] = block_ref[...].astype(F32)
        copies.append(pltpu.make_async_copy(stages[n], target, semaphores.at[n]))
        copies[n].start()
    for copy in copies:
        copy.wait()


def half_rows(half):
    core = lax.bitwise_and(lax.axis_index("rep"), 1)
    mine = pl.ds(pl.multiple_of(core * half, half), half)
    return mine, pl.ds(pl.multiple_of((1 - core) * half, half), half)


def settle_kernel(one_ref, two_ref, other_two_ref, weight_grad_ref, *scratch):
    half, width = one_ref.shape
    mine, other = half_rows(half)
    place(
        [
            (two_ref, weight_grad_ref.at[mine, width:]),
            (other_two_ref, weight_grad_ref.at[other, width:]),
            (one_ref, weight_grad_ref.at[mine, :width]),
        ],
        scratch[:3],
        scratch[3],
    )


def finish_kernel(other_one_ref, settled_ref, weight_grad_ref, stage, semaphores):
    half, width = other_one_ref.shape
    _, other = half_rows(half)
    place([(other_one_ref, weight_grad_ref.at[other, :width])], [stage], semaphores)


VMEM = pl.BlockSpec(memory_space=pltpu.VMEM)


def call(kernel, operands, outputs, scratch, flops, fetched=0):
    hbm = pl.BlockSpec(memory_space=pltpu.HBM)
    operands = [
        pltpu.with_memory_space_constraint(operand, pltpu.HBM) if n < fetched else operand
        for n, operand in enumerate(operands)
    ]
    return pl.pallas_call(
        kernel,
        out_shape=[jax.ShapeDtypeStruct(shape, kind) for shape, kind in outputs],
        in_specs=[hbm] * fetched + [VMEM] * (len(operands) - fetched),
        out_specs=[VMEM] * len(outputs),
        scratch_shapes=[pltpu.VMEM(shape, kind) for shape, kind in scratch]
        + ([pltpu.SemaphoreType.DMA((fetched,))] if fetched else []),
        compiler_params=pltpu.CompilerParams(vmem_limit_bytes=40 << 20),
        cost_estimate=pl.CostEstimate(flops=flops, bytes_accessed=4 << 20, transcendentals=0),
    )(*operands)


def swap(block, axis, bits):
    return lax.ppermute(block, axis, [(i, i ^ bits) for i in range(lax.axis_size(axis))])


def shifted(block, step):
    count = lax.axis_size("space")
    return lax.ppermute(block, "space", [(i, (i + step) % count) for i in range(count)])


def added(left, right):
    return (left.astype(F32) + right.astype(F32)).astype(BF16)


def summed_over_chips(half):
    bit = 2
    while bit < lax.axis_size("rep"):
        half = added(half, swap(half, "rep", bit))
        bit *= 2
    return half


def whole_sample_body(
    grid_latent,
    mesh_latent,
    mesh_cotangent,
    weights,
    g2m_pick,
    g2m_sender,
    g2m_receiver,
    m2m_pick,
    m2m_sender,
    m2m_receiver,
):
    regions = lax.axis_size("space")
    latent = weights.shape[0]
    listed = g2m_pick.shape[1] * g2m_pick.shape[2]
    mesh_count = mesh_latent.shape[1]
    mesh_cap = m2m_pick.shape[2]
    edges = g2m_sender.shape[0]
    columns = latent // regions
    half = columns // 2
    g2m_pick = g2m_pick.transpose(1, 0, 2)
    sources = (
        grid_latent,
        mesh_latent,
        g2m_pick,
        g2m_sender.reshape(1, -1),
        g2m_receiver.reshape(1, -1),
        m2m_pick,
        m2m_sender.reshape(1, -1),
        m2m_receiver.reshape(1, -1),
    )
    packed = call(
        pack_kernel,
        sources,
        [((listed + mesh_count + INDEX_ROWS, latent), BF16)],
        [((INDEX_ROWS, latent), F32)] + [(source.shape, source.dtype) for source in sources],
        10**7,
        fetched=len(sources),
    )[0]
    packed, cotangent, weights = lax.optimization_barrier((packed, mesh_cotangent, weights))
    ring = (0, *sorted(range(1, regions), key=lambda step: -min(step, regions - step)))
    packs = [packed] + [shifted(packed, step) for step in ring[1:]]
    steps = (0, *range(2, regions), 1)
    near = swap(cotangent, "space", 1)
    weights, turned = call(
        weights_kernel,
        (weights,),
        [(weights.shape, BF16), ((latent, 3 * latent), BF16)],
        [],
        10**8,
        fetched=1,
    )
    *packs[1:3], cotangent = lax.optimization_barrier((*packs[1:3], cotangent))
    cotangents = [cotangent] + [swap(cotangent, "space", step) for step in steps[1:-1]] + [near]
    rows = regions * mesh_count
    slots = regions * mesh_cap
    (
        grid_all,
        mesh_all,
        mesh_first,
        mesh_sent,
        hot_one,
        hot_two,
        turned_one,
        turned_two,
        hot_sent,
        slope_one,
        slope_two,
        normed_one,
        scaled_one,
        normed_two,
        scaled_two,
    ) = call(
        functools.partial(forward_kernel, ring, listed, mesh_count, mesh_cap),
        (*packs, weights),
        [
            ((regions * listed, latent), BF16),
            ((rows, latent), BF16),
            ((rows, latent), BF16),
            ((regions * slots, latent), BF16),
            ((regions * (listed + mesh_count), edges), BF16),
            ((regions * (slots + mesh_count), edges), BF16),
            ((regions * edges, listed + mesh_count), BF16),
            ((regions * edges, slots + mesh_count), BF16),
            ((rows, slots), BF16),
            ((regions * edges, latent), BF16),
            ((regions * edges, latent), BF16),
            ((rows, latent), F32),
            ((rows, 128), F32),
            ((rows, latent), F32),
            ((rows, 128), F32),
        ],
        [
            ((regions * INDEX_ROWS, latent), F32),
            ((regions * edges, latent), BF16),
            ((rows, latent), F32),
        ],
        2 * 10**9,
    )
    by_step = dict(zip(steps, cotangents))
    near, far = (0, 1), tuple(step for step in steps if step > 1)
    count = slots + mesh_count
    near_sums, grid_columns, mesh_columns, sent_columns, first_columns = call(
        functools.partial(near_back_kernel, near),
        (
            *(by_step[step] for step in near),
            hot_two,
            turned_two,
            slope_two,
            normed_two,
            scaled_two,
            grid_all,
            mesh_all,
            mesh_sent,
            mesh_first,
        ),
        [
            ((len(near) * count, latent), F32),
            ((columns, regions * listed), BF16),
            ((columns, rows), BF16),
            ((columns, regions * slots), BF16),
            ((columns, rows), BF16),
        ],
        [((len(near) * mesh_count, latent), BF16), ((len(near) * edges, latent), BF16)],
        10**9,
    )
    mesh_grad, keep_two, give_two = call(
        functools.partial(far_back_kernel, near, far, mesh_cap),
        (
            *(by_step[step] for step in near + far),
            turned,
            first_columns,
            sent_columns,
            near_sums,
            hot_two,
            turned_two,
            hot_sent,
            slope_two,
            normed_two,
            scaled_two,
        ),
        [((rows, latent), F32)] + [((half, 2 * latent), BF16)] * 2,
        [
            ((rows, latent), F32),
            ((regions * slots, latent), F32),
            ((rows, latent), BF16),
            ((columns, 2 * latent), BF16),
            ((len(far) * mesh_count, latent), BF16),
            ((len(far) * edges, latent), BF16),
        ],
        10**9,
    )
    own_slots, keep_one, give_one = call(
        functools.partial(encode_back_kernel, regions),
        (
            grid_columns,
            mesh_columns,
            hot_one,
            turned_one,
            slope_one,
            normed_one,
            scaled_one,
            mesh_grad,
        ),
        [((listed, latent), BF16)] + [((half, 2 * latent), BF16)] * 2,
        [
            ((regions * listed, latent), BF16),
            ((rows, latent), BF16),
            ((columns, 2 * latent), BF16),
            ((rows, latent), BF16),
            ((regions * edges, latent), BF16),
        ],
        10**9,
    )
    half_one = added(keep_one, swap(give_one, "rep", 1))
    half_two = added(keep_two, swap(give_two, "rep", 1))
    half_one, own_slots = lax.optimization_barrier((half_one, own_slots))
    grid_grad, mesh_out = call(
        results_kernel,
        (turned, g2m_pick, own_slots, mesh_first, normed_two),
        [(grid_latent.shape, BF16), (mesh_latent.shape, BF16)],
        [],
        10**8,
    )
    two = summed_over_chips(half_two)
    one, grid_grad = lax.optimization_barrier((summed_over_chips(half_one), grid_grad))
    hbm = pl.BlockSpec(memory_space=pltpu.HBM)
    stage = pltpu.VMEM((half, 2 * latent), F32)
    weight_shape = pltpu.HBM((columns, 4 * latent), F32)
    limit = pltpu.CompilerParams(vmem_limit_bytes=40 << 20)
    settled = pl.pallas_call(
        settle_kernel,
        out_shape=weight_shape,
        in_specs=[VMEM] * 3,
        out_specs=hbm,
        scratch_shapes=[stage] * 3 + [pltpu.SemaphoreType.DMA((3,))],
        compiler_params=limit,
    )(one, two, swap(two, "rep", 1))
    weight_grad = pl.pallas_call(
        finish_kernel,
        out_shape=weight_shape,
        in_specs=[VMEM, hbm],
        out_specs=hbm,
        scratch_shapes=[stage, pltpu.SemaphoreType.DMA((1,))],
        input_output_aliases={1: 0},
        compiler_params=limit,
    )(swap(one, "rep", 1), settled)
    return (mesh_out, grid_grad, weight_grad)


def solution(mesh):
    regions = mesh.shape["space"]
    samples = mesh.shape["rep"]

    def whole(*arguments):
        edges = arguments[5].shape[0] + arguments[8].shape[0]
        latent = arguments[3].shape[0]
        fits = edges * latent * 4 <= SAMPLE_EDGE_BYTES and latent % (128 * regions) == 0
        paired = regions > 2 and samples > 1 and not (regions & (regions - 1) | samples & (samples - 1))
        return sharded(whole_sample_body if fits and paired else partitioned_body)(*arguments)

    def sharded(body):
        return jax.shard_map(
            body,
            mesh=mesh,
            in_specs=(
                P(("groups", "rep"), "space", None),
                P(("groups", "rep"), "space", None),
                P(("groups", "rep"), "space", None),
                P(),
                P("space", None, None),
                P("space"),
                P("space"),
                P("space", None, None),
                P("space"),
                P("space"),
            ),
            out_specs=(
                P(("groups", "rep"), "space", None),
                P(("groups", "rep"), "space", None),
                P(("groups", "space"), None),
            ),
            check_vma=False,
        )

    return whole
```

```python
import functools

import jax
import jax.numpy as jnp
from jax import lax
from jax.experimental import pallas as pl
from jax.experimental.pallas import tpu as pltpu
from jax.sharding import PartitionSpec as P

EPSILON = 1e-05


def with_halo(cells, sides, width):
    for axis, dim in sides:
        count = lax.axis_size(axis)
        ends = count - 1
        head = lax.slice_in_dim(cells, 0, width, axis=dim)
        tail = lax.slice_in_dim(cells, cells.shape[dim] - width, cells.shape[dim], axis=dim)
        cells = jnp.concatenate(
            [
                lax.ppermute(tail, axis, [(i, (i + 1) % count) for i in range(ends)]),
                cells,
                lax.ppermute(head, axis, [((i + 1) % count, i) for i in range(ends)]),
            ],
            axis=dim,
        )
    return cells


def swish(values):
    return values * jax.nn.sigmoid(values)


def swish_slope(values):
    squash = jax.nn.sigmoid(values)
    return squash * (1.0 + values * (1.0 - squash))


def norm_rows(values):
    centred = values - jnp.mean(values, -1, keepdims=True)
    return centred * lax.rsqrt(jnp.mean(centred * centred, -1, keepdims=True) + EPSILON)


def norm_rows_back(values, upstream):
    centred = values - jnp.mean(values, -1, keepdims=True)
    scaled = lax.rsqrt(jnp.mean(centred * centred, -1, keepdims=True) + EPSILON)
    normed = centred * scaled
    return scaled * (
        upstream
        - jnp.mean(upstream, -1, keepdims=True)
        - normed * jnp.mean(upstream * normed, -1, keepdims=True)
    )


def slot_rows(pick_row):
    listed = pick_row.reshape(-1)
    return listed


def mesh_route(outgoing, capacity, peer_count):
    columns = outgoing.shape[1]
    pieces = lax.all_to_all(
        outgoing.reshape(peer_count, capacity, columns),
        "space",
        split_axis=0,
        concat_axis=0,
        tiled=True,
    )
    arrived = pieces.reshape(peer_count * capacity, columns)
    return arrived


def grid_route(outgoing, capacity):
    columns = outgoing.shape[1]
    lists = outgoing.reshape(3, capacity, columns)
    rims = with_halo(jnp.stack([lists[0], lists[2]]), (("space", 0),), 1)
    return jnp.concatenate([rims[0], lists[1], rims[3]], axis=0)


def edge_pass(arrived, recv_table, located, receiver, w_send, w_recv):
    recv_proj = jnp.dot(recv_table, w_recv, preferred_element_type=jnp.float32)
    slot_proj = jnp.dot(arrived, w_send, preferred_element_type=jnp.float32)
    activation = slot_proj[located] + recv_proj[receiver]
    message = swish(activation).astype(jnp.bfloat16)
    member = (
        receiver[None, :] == jnp.arange(recv_table.shape[0], dtype=jnp.int32)[:, None]
    ).astype(jnp.bfloat16)
    summed = jnp.dot(member, message, preferred_element_type=jnp.float32)
    return (activation, member, summed)


def backward_pass(slot_count, located, activation, member, receiver, agg_grad, w_send):
    edge_grad = (agg_grad[receiver] * swish_slope(activation)).astype(jnp.bfloat16)
    recv_sum = jnp.dot(member, edge_grad, preferred_element_type=jnp.float32).astype(jnp.bfloat16)
    slot_member = (located[None, :] == jnp.arange(slot_count, dtype=jnp.int32)[:, None]).astype(
        jnp.bfloat16
    )
    slot_sum = jnp.dot(slot_member, edge_grad, preferred_element_type=jnp.float32).astype(
        jnp.bfloat16
    )
    returned = jnp.dot(slot_sum, w_send.T, preferred_element_type=jnp.float32).astype(jnp.bfloat16)
    return (recv_sum, slot_sum, returned)


def gather_back(listed, back_rows, row_count):
    owner = (listed[None, :] == jnp.arange(row_count, dtype=jnp.int32)[:, None]).astype(
        jnp.bfloat16
    )
    return jnp.dot(owner, back_rows, preferred_element_type=jnp.float32)


def partitioned_body(
    grid_latent,
    mesh_latent,
    mesh_cotangent,
    weights,
    g2m_pick,
    g2m_sender,
    g2m_receiver,
    m2m_pick,
    m2m_sender,
    m2m_receiver,
):
    grid_rows = grid_latent[0]
    mesh_rows = mesh_latent[0]
    upstream = mesh_cotangent[0].astype(jnp.float32)
    latent = weights.shape[0]
    encode_sender = weights[:, :latent]
    encode_receiver = weights[:, latent : 2 * latent]
    process_sender = weights[:, 2 * latent : 3 * latent]
    process_receiver = weights[:, 3 * latent :]
    peer_count = lax.axis_size("space")
    grid_cap = g2m_pick.shape[2]
    mesh_cap = m2m_pick.shape[2]
    grid_listed = g2m_pick[0].reshape(-1)
    grid_arrived = grid_route(grid_rows[grid_listed], grid_cap)
    act_first, member_first, summed_first = edge_pass(
        grid_arrived, mesh_rows, g2m_sender, g2m_receiver, encode_sender, encode_receiver
    )
    mesh_first = (mesh_rows.astype(jnp.float32) + norm_rows(summed_first)).astype(jnp.bfloat16)
    mesh_listed = slot_rows(m2m_pick[0])
    mesh_arrived = mesh_route(mesh_first[mesh_listed], mesh_cap, peer_count)
    act_second, member_second, summed_second = edge_pass(
        mesh_arrived, mesh_first, m2m_sender, m2m_receiver, process_sender, process_receiver
    )
    mesh_final = (mesh_first.astype(jnp.float32) + norm_rows(summed_second)).astype(jnp.bfloat16)
    agg_second = norm_rows_back(summed_second, upstream)
    recv_second, slot_second, returned_second = backward_pass(
        mesh_arrived.shape[0],
        m2m_sender,
        act_second,
        member_second,
        m2m_receiver,
        agg_second,
        process_sender,
    )
    back_second = mesh_route(returned_second, mesh_cap, peer_count)
    mesh_grad = upstream + jnp.dot(
        recv_second, process_receiver.T, preferred_element_type=jnp.float32
    )
    mesh_grad = mesh_grad + gather_back(mesh_listed, back_second, mesh_rows.shape[0])
    agg_first = norm_rows_back(summed_first, mesh_grad)
    recv_first, slot_first, returned_first = backward_pass(
        grid_arrived.shape[0],
        g2m_sender,
        act_first,
        member_first,
        g2m_receiver,
        agg_first,
        encode_sender,
    )
    back_first = grid_route(returned_first, grid_cap)
    grid_grad = gather_back(grid_listed, back_first, grid_rows.shape[0]).astype(jnp.bfloat16)
    factor_pairs = (
        (grid_arrived, slot_first),
        (mesh_rows, recv_first),
        (mesh_arrived, slot_second),
        (mesh_first, recv_second),
    )
    blocks = []
    for first_factor, second_factor in factor_pairs:
        blocks.append(
            lax.dot_general(
                first_factor,
                second_factor,
                (((0,), (0,)), ((), ())),
                preferred_element_type=jnp.float32,
            )
        )
    shares = lax.psum_scatter(
        jnp.concatenate(blocks, axis=1).astype(jnp.bfloat16),
        "space",
        scatter_dimension=0,
        tiled=True,
    )
    weight_grad = lax.psum(shares, "rep").astype(jnp.float32)
    return (mesh_final[None], grid_grad[None], weight_grad)


F32 = jnp.float32
BF16 = jnp.bfloat16
INDEX_ROWS = 8
SAMPLE_EDGE_BYTES = 8 << 20


def dot(left, right):
    return jnp.dot(left, right, preferred_element_type=F32)


def dot_first(left, right):
    return lax.dot_general(left, right, (((0,), (0,)), ((), ())), preferred_element_type=F32)


def one_hot(labels, count):
    rows = lax.broadcasted_iota(jnp.int32, (count, labels.shape[-1]), 0)
    return (rows == labels).astype(F32).astype(BF16)


def row_moments(values):
    centred = values - jnp.mean(values, -1, keepdims=True)
    return centred, lax.rsqrt(jnp.mean(centred * centred, -1, keepdims=True) + EPSILON)


def moments_back(normed, scaled, upstream):
    return scaled * (
        upstream
        - jnp.mean(upstream, -1, keepdims=True)
        - normed * jnp.mean(upstream * normed, -1, keepdims=True)
    )


def fetch(pairs, semaphores):
    copies = [
        pltpu.make_async_copy(source, target, semaphores.at[n])
        for n, (source, target) in enumerate(pairs)
    ]
    for copy in copies:
        copy.start()
    for copy in copies:
        copy.wait()


def pack_kernel(*refs):
    sources, packed_ref, index_ref = refs[:8], refs[8], refs[9]
    local, semaphores = refs[10:18], refs[18]
    fetch(list(zip(sources, local)), semaphores)
    (
        grid_ref,
        mesh_ref,
        g2m_pick_ref,
        g2m_sender_ref,
        g2m_receiver_ref,
        m2m_pick_ref,
        m2m_sender_ref,
        m2m_receiver_ref,
    ) = local
    lists, _, capacity = g2m_pick_ref.shape
    mesh_count = mesh_ref.shape[1]
    regions, mesh_cap = m2m_pick_ref.shape[1:]
    edges = g2m_sender_ref.shape[1]
    grid_rows = grid_ref[0]
    for i in range(lists):
        picked = one_hot(g2m_pick_ref[i], grid_rows.shape[0])
        packed_ref[i * capacity : (i + 1) * capacity, :] = dot_first(picked, grid_rows).astype(BF16)
    first = lists * capacity
    packed_ref[first : first + mesh_count, :] = mesh_ref[0]
    index_ref[...] = jnp.zeros_like(index_ref)
    index_ref[0:1, 0:edges] = g2m_sender_ref[...].astype(F32)
    index_ref[0:1, edges : 2 * edges] = g2m_receiver_ref[...].astype(F32)
    index_ref[1:2, 0:edges] = m2m_sender_ref[...].astype(F32)
    index_ref[1:2, edges : 2 * edges] = m2m_receiver_ref[...].astype(F32)
    slots = regions * mesh_cap
    lane = lax.broadcasted_iota(jnp.int32, (mesh_cap, slots), 1)
    spread = (lane % mesh_cap == lax.broadcasted_iota(jnp.int32, (mesh_cap, slots), 0)).astype(F32)
    spread = dot(m2m_pick_ref[0].astype(F32).astype(BF16), spread.astype(BF16))
    lane = lax.broadcasted_iota(jnp.int32, (regions, slots), 1)
    owned = lane // mesh_cap == lax.broadcasted_iota(jnp.int32, (regions, slots), 0)
    index_ref[2:3, 0:slots] = jnp.sum(jnp.where(owned, spread, 0.0), 0, keepdims=True)
    packed_ref[first + mesh_count :, :] = index_ref[...].astype(BF16)


def weights_kernel(source_ref, weights_ref, turned_ref, semaphores):
    fetch([(source_ref, weights_ref)], semaphores)
    latent = weights_ref.shape[0]
    for n, block in enumerate((0, 2, 3)):
        turned_ref[:, n * latent : (n + 1) * latent] = weights_ref[
            :, block * latent : (block + 1) * latent
        ].T


def edge_blocks(edges, size):
    size = min(edges, size)
    return [(first, min(size, edges - first)) for first in range(0, edges, size)]


def edge_forward(tables, hot_ref, turned_hot_ref, slope_ref, message_ref, mesh_count):
    regions = len(tables)
    edges = slope_ref.shape[0] // regions
    count = hot_ref.shape[0] // regions
    work = [(d, first, size) for d in range(regions) for first, size in edge_blocks(edges, 128)]

    def gathered(d, first, size):
        rows = slice(d * edges + first, d * edges + first + size)
        return dot(turned_hot_ref[rows, :], tables[d])

    sums = []
    activation = gathered(*work[0])
    for n, (d, first, size) in enumerate(work):
        coming = gathered(*work[n + 1]) if n + 1 < len(work) else None
        activation = activation.astype(BF16)
        squash = 0.5 + 0.5 * jnp.tanh(0.5 * activation)
        message = activation * squash
        rows = slice(d * edges + first, d * edges + first + size)
        slope_ref[rows, :] = squash + message * (1.0 - squash)
        message_ref[rows, :] = message
        activation = coming
        if first + size == edges:
            hot = hot_ref[(d + 1) * count - mesh_count : (d + 1) * count, :]
            sums.append(dot(hot, message_ref[d * edges : (d + 1) * edges, :]))
    return sums


def forward_kernel(
    steps,
    listed,
    mesh_count,
    mesh_cap,
    *refs,
):
    regions = len(steps)
    packed_refs = refs[:regions]
    (
        weights_ref,
        grid_ref,
        mesh_ref,
        first_ref,
        sent_ref,
        hot_one_ref,
        hot_two_ref,
        turned_one_ref,
        turned_two_ref,
        hot_sent_ref,
        slope_one_ref,
        slope_two_ref,
        normed_one_ref,
        scaled_one_ref,
        normed_two_ref,
        scaled_two_ref,
        index_ref,
        message_ref,
        sum_ref,
    ) = refs[regions:]
    latent = weights_ref.shape[0]
    edges = slope_one_ref.shape[0] // regions
    capacity = listed // 3
    slots = regions * mesh_cap
    me = lax.axis_index("space")
    for step, packed_ref in zip(steps, packed_refs):
        region = lax.bitwise_xor(me, step)
        at = lambda rows: pl.ds(pl.multiple_of(region * rows, rows), rows)
        grid_ref[at(listed), :] = packed_ref[:listed, :]
        mesh_ref[at(mesh_count), :] = packed_ref[listed : listed + mesh_count, :]
        index_ref[at(INDEX_ROWS), :] = packed_ref[listed + mesh_count :, :].astype(F32)

    grid_proj = dot(grid_ref[...], weights_ref[:, :latent])
    mesh_proj = dot(mesh_ref[...], weights_ref[:, latent : 2 * latent])
    for d in range(regions):
        index = index_ref[d * INDEX_ROWS : (d + 1) * INDEX_ROWS, :].astype(jnp.int32)
        for row, senders, hot_ref, turned_ref in (
            (0, listed, hot_one_ref, turned_one_ref),
            (1, slots, hot_two_ref, turned_two_ref),
        ):
            count = senders + mesh_count
            hot = jnp.concatenate(
                [
                    one_hot(index[row : row + 1, :edges], senders),
                    one_hot(index[row : row + 1, edges:], mesh_count),
                ],
                axis=0,
            )
            hot_ref[d * count : (d + 1) * count, :] = hot
            turned_ref[d * edges : (d + 1) * edges, :] = hot.T
        hot_sent_ref[d * mesh_count : (d + 1) * mesh_count, :] = one_hot(
            index[2:3, :slots], mesh_count
        )

    blank = jnp.zeros((capacity, latent), F32)
    tables = []
    for d in range(regions):
        before = (d - 1) * listed + 2 * capacity
        within = d * listed + capacity
        after = (d + 1) * listed
        tables.append(
            jnp.concatenate(
                [
                    grid_proj[before : before + capacity] if d > 0 else blank,
                    grid_proj[within : within + capacity],
                    grid_proj[after : after + capacity] if d < regions - 1 else blank,
                    mesh_proj[d * mesh_count : (d + 1) * mesh_count],
                ],
                axis=0,
            ).astype(BF16)
        )
    sums = edge_forward(
        tables, hot_one_ref, turned_one_ref, slope_one_ref, message_ref, mesh_count
    )
    for d in range(regions):
        sum_ref[d * mesh_count : (d + 1) * mesh_count, :] = sums[d]
    centred, scaled = row_moments(sum_ref[...])
    normed = centred * scaled
    normed_one_ref[...] = normed
    scaled_one_ref[...] = jnp.broadcast_to(scaled, scaled_one_ref.shape)
    first_ref[...] = (mesh_ref[...].astype(F32) + normed).astype(BF16)

    for s in range(regions):
        rows = slice(s * mesh_count, (s + 1) * mesh_count)
        sent_ref[s * slots : (s + 1) * slots, :] = dot_first(
            hot_sent_ref[rows, :], first_ref[rows, :]
        ).astype(BF16)
    sent_proj = dot(sent_ref[...], weights_ref[:, 2 * latent : 3 * latent])
    first_proj = dot(first_ref[...], weights_ref[:, 3 * latent :])
    tables = []
    for d in range(regions):
        pieces = [
            sent_proj[s * slots + d * mesh_cap : s * slots + (d + 1) * mesh_cap]
            for s in range(regions)
        ]
        tables.append(
            jnp.concatenate(
                pieces + [first_proj[d * mesh_count : (d + 1) * mesh_count]], axis=0
            ).astype(BF16)
        )
    sums = edge_forward(
        tables, hot_two_ref, turned_two_ref, slope_two_ref, message_ref, mesh_count
    )
    for d in range(regions):
        sum_ref[d * mesh_count : (d + 1) * mesh_count, :] = sums[d]
    centred, scaled = row_moments(sum_ref[...])
    normed_two_ref[...] = centred * scaled
    scaled_two_ref[...] = jnp.broadcast_to(scaled, scaled_two_ref.shape)


def edge_backward(regions, agg_grad_ref, hot_ref, turned_hot_ref, slope_ref, edge_grad_ref):
    mesh_count = agg_grad_ref.shape[0] // len(regions)
    edges = edge_grad_ref.shape[0] // len(regions)
    count = turned_hot_ref.shape[1]
    blank = jnp.zeros((count - mesh_count, agg_grad_ref.shape[1]), BF16)
    work = [(n, first, size) for n in range(len(regions)) for first, size in edge_blocks(edges, 256)]

    def at(n, first, size):
        return pl.ds(pl.multiple_of(regions[n] * edges + first, size), size)

    def gathered(n, first, size):
        own = agg_grad_ref[n * mesh_count : (n + 1) * mesh_count, :]
        return dot(turned_hot_ref[at(n, first, size), :], jnp.concatenate([blank, own], axis=0))

    sums = []
    upstream = gathered(*work[0])
    for k, (n, first, size) in enumerate(work):
        coming = gathered(*work[k + 1]) if k + 1 < len(work) else None
        rows = slice(n * edges + first, n * edges + first + size)
        edge_grad_ref[rows, :] = upstream.astype(BF16) * slope_ref[at(n, first, size), :]
        upstream = coming
        if first + size == edges:
            hot = hot_ref[pl.ds(pl.multiple_of(regions[n] * count, count), count), :]
            sums.append(dot(hot, edge_grad_ref[n * edges : (n + 1) * edges, :]))
    return sums


def halve(share_ref, keep_ref, give_ref):
    half = keep_ref.shape[0]
    core = lax.bitwise_and(lax.axis_index("rep"), 1)
    keep_ref[...] = share_ref[pl.ds(pl.multiple_of(core * half, half), half), :]
    give_ref[...] = share_ref[pl.ds(pl.multiple_of((1 - core) * half, half), half), :]


def process_back_part(
    steps, mesh_count, cotangent_refs, hot_ref, turned_hot_ref, slope_ref, normed_ref, scaled_ref,
    agg_grad_ref, edge_grad_ref,
):
    me = lax.axis_index("space")
    regions = [lax.bitwise_xor(me, step) for step in steps]
    for n, (region, cotangent_ref) in enumerate(zip(regions, cotangent_refs)):
        rows = pl.ds(pl.multiple_of(region * mesh_count, mesh_count), mesh_count)
        agg_grad_ref[n * mesh_count : (n + 1) * mesh_count, :] = moments_back(
            normed_ref[rows, :], scaled_ref[rows, 0:1], cotangent_ref[0].astype(F32)
        ).astype(BF16)
    return regions, edge_backward(
        regions, agg_grad_ref, hot_ref, turned_hot_ref, slope_ref, edge_grad_ref
    )


def near_back_kernel(steps, *refs):
    cotangent_refs, refs = refs[: len(steps)], refs[len(steps) :]
    (
        hot_ref,
        turned_hot_ref,
        slope_ref,
        normed_ref,
        scaled_ref,
        *whole_refs,
    ) = refs[:9]
    sums_ref, *column_refs = refs[9:14]
    agg_grad_ref, edge_grad_ref = refs[14:]
    mesh_count = agg_grad_ref.shape[0] // len(steps)
    count = turned_hot_ref.shape[1]
    _, all_sums = process_back_part(
        steps, mesh_count, cotangent_refs, hot_ref, turned_hot_ref, slope_ref, normed_ref,
        scaled_ref, agg_grad_ref, edge_grad_ref,
    )
    for n, sums in enumerate(all_sums):
        sums_ref[n * count : (n + 1) * count, :] = sums
    columns = column_refs[0].shape[0]
    mine = pl.ds(pl.multiple_of(lax.axis_index("space") * columns, columns), columns)
    for whole_ref, column_ref in zip(whole_refs, column_refs):
        column_ref[...] = whole_ref[:, mine].T


def far_back_kernel(near, far, mesh_cap, *refs):
    regions = len(near) + len(far)
    cotangent_refs, refs = refs[:regions], refs[regions:]
    (
        turned_ref,
        first_columns_ref,
        sent_columns_ref,
        near_sums_ref,
        hot_ref,
        turned_hot_ref,
        hot_sent_ref,
        slope_ref,
        normed_ref,
        scaled_ref,
        mesh_grad_ref,
        keep_ref,
        give_ref,
        upstream_ref,
        slot_ref,
        recv_ref,
        share_ref,
        agg_grad_ref,
        edge_grad_ref,
    ) = refs
    latent = normed_ref.shape[1]
    mesh_count = normed_ref.shape[0] // regions
    count = turned_hot_ref.shape[1]
    slots = regions * mesh_cap
    me = lax.axis_index("space")
    far_regions, all_sums = process_back_part(
        far, mesh_count, cotangent_refs[len(near) :], hot_ref, turned_hot_ref, slope_ref,
        normed_ref, scaled_ref, agg_grad_ref, edge_grad_ref,
    )
    near_regions = [lax.bitwise_xor(me, step) for step in near]
    near_sums = [near_sums_ref[n * count : (n + 1) * count, :] for n in range(len(near))]
    for region, sums in zip(near_regions + far_regions, near_sums + all_sums):
        for s in range(regions):
            slot_ref[pl.ds(pl.multiple_of(s * slots + region * mesh_cap, mesh_cap), mesh_cap), :] = (
                sums[s * mesh_cap : (s + 1) * mesh_cap]
            )
        recv_ref[pl.ds(pl.multiple_of(region * mesh_count, mesh_count), mesh_count), :] = sums[
            slots:
        ].astype(BF16)
    for region, cotangent_ref in zip(near_regions + far_regions, cotangent_refs):
        rows = pl.ds(pl.multiple_of(region * mesh_count, mesh_count), mesh_count)
        upstream_ref[rows, :] = cotangent_ref[0].astype(F32)
    slot_sum = slot_ref[...].astype(BF16)
    share_ref[:, :latent] = dot(sent_columns_ref[...], slot_sum).astype(BF16)
    share_ref[:, latent:] = dot(first_columns_ref[...], recv_ref[...]).astype(BF16)
    halve(share_ref, keep_ref, give_ref)
    returned = dot(slot_sum, turned_ref[:, latent : 2 * latent]).astype(BF16)
    grad = upstream_ref[...] + dot(recv_ref[...], turned_ref[:, 2 * latent :])
    for s in range(regions):
        rows = slice(s * mesh_count, (s + 1) * mesh_count)
        mesh_grad_ref[rows, :] = grad[rows] + dot(
            hot_sent_ref[rows, :], returned[s * slots : (s + 1) * slots]
        )


def encode_back_kernel(
    regions,
    grid_columns_ref,
    mesh_columns_ref,
    hot_ref,
    turned_hot_ref,
    slope_ref,
    normed_ref,
    scaled_ref,
    mesh_grad_ref,
    own_slot_ref,
    keep_ref,
    give_ref,
    slot_ref,
    recv_ref,
    share_ref,
    agg_grad_ref,
    edge_grad_ref,
):
    latent = normed_ref.shape[1]
    mesh_count = normed_ref.shape[0] // regions
    listed = slot_ref.shape[0] // regions
    capacity = listed // 3
    me = lax.axis_index("space")
    agg_grad_ref[...] = moments_back(
        normed_ref[...], scaled_ref[:, 0:1], mesh_grad_ref[...]
    ).astype(BF16)
    blank = jnp.zeros((capacity, latent), BF16)
    slot_ref[0:capacity, :] = blank
    slot_ref[regions * listed - capacity :, :] = blank
    all_sums = edge_backward(
        range(regions), agg_grad_ref, hot_ref, turned_hot_ref, slope_ref, edge_grad_ref
    )
    for d, sums in enumerate(all_sums):
        sums = sums.astype(BF16)
        for j in range(3):
            source = d + j - 1
            if 0 <= source < regions:
                first = source * listed + (2 - j) * capacity
                slot_ref[first : first + capacity, :] = sums[j * capacity : (j + 1) * capacity]
        recv_ref[d * mesh_count : (d + 1) * mesh_count, :] = sums[listed:]
    share_ref[:, :latent] = dot(grid_columns_ref[...], slot_ref[...]).astype(BF16)
    share_ref[:, latent:] = dot(mesh_columns_ref[...], recv_ref[...]).astype(BF16)
    halve(share_ref, keep_ref, give_ref)
    own = pl.ds(pl.multiple_of(me * listed, listed), listed)
    own_slot_ref[...] = slot_ref[own, :]


def results_kernel(
    turned_ref, pick_ref, own_slot_ref, first_ref, normed_ref, grid_grad_ref, mesh_out_ref
):
    mesh_count = mesh_out_ref.shape[1]
    me = lax.axis_index("space")
    own = pl.ds(pl.multiple_of(me * mesh_count, mesh_count), mesh_count)
    mesh_out_ref[0] = (first_ref[own, :].astype(F32) + normed_ref[own, :]).astype(BF16)
    lists, _, capacity = pick_ref.shape
    latent = own_slot_ref.shape[1]
    returned = dot(own_slot_ref[...], turned_ref[:, :latent]).astype(BF16)
    total = None
    for i in range(lists):
        owner = one_hot(pick_ref[i], grid_grad_ref.shape[1])
        part = dot(owner, returned[i * capacity : (i + 1) * capacity])
        total = part if total is None else total + part
    grid_grad_ref[0] = total.astype(BF16)


def place(pairs, stages, semaphores):
    copies = []
    for n, (block_ref, target) in enumerate(pairs):
        stages[n][...] = block_ref[...].astype(F32)
        copies.append(pltpu.make_async_copy(stages[n], target, semaphores.at[n]))
        copies[n].start()
    for copy in copies:
        copy.wait()


def half_rows(half):
    core = lax.bitwise_and(lax.axis_index("rep"), 1)
    mine = pl.ds(pl.multiple_of(core * half, half), half)
    return mine, pl.ds(pl.multiple_of((1 - core) * half, half), half)


def settle_kernel(one_ref, two_ref, other_two_ref, weight_grad_ref, *scratch):
    half, width = one_ref.shape
    mine, other = half_rows(half)
    place(
        [
            (two_ref, weight_grad_ref.at[mine, width:]),
            (other_two_ref, weight_grad_ref.at[other, width:]),
            (one_ref, weight_grad_ref.at[mine, :width]),
        ],
        scratch[:3],
        scratch[3],
    )


def finish_kernel(other_one_ref, settled_ref, weight_grad_ref, stage, semaphores):
    half, width = other_one_ref.shape
    _, other = half_rows(half)
    place([(other_one_ref, weight_grad_ref.at[other, :width])], [stage], semaphores)


VMEM = pl.BlockSpec(memory_space=pltpu.VMEM)


def call(kernel, operands, outputs, scratch, flops, fetched=0):
    hbm = pl.BlockSpec(memory_space=pltpu.HBM)
    operands = [
        pltpu.with_memory_space_constraint(operand, pltpu.HBM) if n < fetched else operand
        for n, operand in enumerate(operands)
    ]
    return pl.pallas_call(
        kernel,
        out_shape=[jax.ShapeDtypeStruct(shape, kind) for shape, kind in outputs],
        in_specs=[hbm] * fetched + [VMEM] * (len(operands) - fetched),
        out_specs=[VMEM] * len(outputs),
        scratch_shapes=[pltpu.VMEM(shape, kind) for shape, kind in scratch]
        + ([pltpu.SemaphoreType.DMA((fetched,))] if fetched else []),
        compiler_params=pltpu.CompilerParams(vmem_limit_bytes=40 << 20),
        cost_estimate=pl.CostEstimate(flops=flops, bytes_accessed=4 << 20, transcendentals=0),
    )(*operands)


def swap(block, axis, bits):
    return lax.ppermute(block, axis, [(i, i ^ bits) for i in range(lax.axis_size(axis))])


def added(left, right):
    return (left.astype(F32) + right.astype(F32)).astype(BF16)


def summed_over_chips(half):
    bit = 2
    while bit < lax.axis_size("rep"):
        half = added(half, swap(half, "rep", bit))
        bit *= 2
    return half


def whole_sample_body(
    grid_latent,
    mesh_latent,
    mesh_cotangent,
    weights,
    g2m_pick,
    g2m_sender,
    g2m_receiver,
    m2m_pick,
    m2m_sender,
    m2m_receiver,
):
    regions = lax.axis_size("space")
    latent = weights.shape[0]
    listed = g2m_pick.shape[1] * g2m_pick.shape[2]
    mesh_count = mesh_latent.shape[1]
    mesh_cap = m2m_pick.shape[2]
    edges = g2m_sender.shape[0]
    columns = latent // regions
    half = columns // 2
    g2m_pick = g2m_pick.transpose(1, 0, 2)
    sources = (
        grid_latent,
        mesh_latent,
        g2m_pick,
        g2m_sender.reshape(1, -1),
        g2m_receiver.reshape(1, -1),
        m2m_pick,
        m2m_sender.reshape(1, -1),
        m2m_receiver.reshape(1, -1),
    )
    packed = call(
        pack_kernel,
        sources,
        [((listed + mesh_count + INDEX_ROWS, latent), BF16)],
        [((INDEX_ROWS, latent), F32)] + [(source.shape, source.dtype) for source in sources],
        10**7,
        fetched=len(sources),
    )[0]
    packed, cotangent, weights = lax.optimization_barrier((packed, mesh_cotangent, weights))
    steps = (0, *range(2, regions), 1)
    packs = [packed] + [swap(packed, "space", step) for step in steps[1:]]
    near = swap(cotangent, "space", 1)
    weights, turned = call(
        weights_kernel,
        (weights,),
        [(weights.shape, BF16), ((latent, 3 * latent), BF16)],
        [],
        10**8,
        fetched=1,
    )
    turned, early = lax.optimization_barrier((turned, cotangent))
    packs[1], late = lax.optimization_barrier((packs[1], cotangent))
    cotangents = (
        [cotangent, swap(late, "space", steps[1])]
        + [swap(early, "space", step) for step in steps[2:-1]]
        + [near]
    )
    rows = regions * mesh_count
    slots = regions * mesh_cap
    (
        grid_all,
        mesh_all,
        mesh_first,
        mesh_sent,
        hot_one,
        hot_two,
        turned_one,
        turned_two,
        hot_sent,
        slope_one,
        slope_two,
        normed_one,
        scaled_one,
        normed_two,
        scaled_two,
    ) = call(
        functools.partial(forward_kernel, steps, listed, mesh_count, mesh_cap),
        (*packs, weights),
        [
            ((regions * listed, latent), BF16),
            ((rows, latent), BF16),
            ((rows, latent), BF16),
            ((regions * slots, latent), BF16),
            ((regions * (listed + mesh_count), edges), BF16),
            ((regions * (slots + mesh_count), edges), BF16),
            ((regions * edges, listed + mesh_count), BF16),
            ((regions * edges, slots + mesh_count), BF16),
            ((rows, slots), BF16),
            ((regions * edges, latent), BF16),
            ((regions * edges, latent), BF16),
            ((rows, latent), F32),
            ((rows, 128), F32),
            ((rows, latent), F32),
            ((rows, 128), F32),
        ],
        [
            ((regions * INDEX_ROWS, latent), F32),
            ((regions * edges, latent), BF16),
            ((rows, latent), F32),
        ],
        2 * 10**9,
    )
    by_step = dict(zip(steps, cotangents))
    near, far = (0, 1), tuple(step for step in steps if step > 1)
    count = slots + mesh_count
    near_sums, grid_columns, mesh_columns, sent_columns, first_columns = call(
        functools.partial(near_back_kernel, near),
        (
            *(by_step[step] for step in near),
            hot_two,
            turned_two,
            slope_two,
            normed_two,
            scaled_two,
            grid_all,
            mesh_all,
            mesh_sent,
            mesh_first,
        ),
        [
            ((len(near) * count, latent), F32),
            ((columns, regions * listed), BF16),
            ((columns, rows), BF16),
            ((columns, regions * slots), BF16),
            ((columns, rows), BF16),
        ],
        [((len(near) * mesh_count, latent), BF16), ((len(near) * edges, latent), BF16)],
        10**9,
    )
    mesh_grad, keep_two, give_two = call(
        functools.partial(far_back_kernel, near, far, mesh_cap),
        (
            *(by_step[step] for step in near + far),
            turned,
            first_columns,
            sent_columns,
            near_sums,
            hot_two,
            turned_two,
            hot_sent,
            slope_two,
            normed_two,
            scaled_two,
        ),
        [((rows, latent), F32)] + [((half, 2 * latent), BF16)] * 2,
        [
            ((rows, latent), F32),
            ((regions * slots, latent), F32),
            ((rows, latent), BF16),
            ((columns, 2 * latent), BF16),
            ((len(far) * mesh_count, latent), BF16),
            ((len(far) * edges, latent), BF16),
        ],
        10**9,
    )
    own_slots, keep_one, give_one = call(
        functools.partial(encode_back_kernel, regions),
        (
            grid_columns,
            mesh_columns,
            hot_one,
            turned_one,
            slope_one,
            normed_one,
            scaled_one,
            mesh_grad,
        ),
        [((listed, latent), BF16)] + [((half, 2 * latent), BF16)] * 2,
        [
            ((regions * listed, latent), BF16),
            ((rows, latent), BF16),
            ((columns, 2 * latent), BF16),
            ((rows, latent), BF16),
            ((regions * edges, latent), BF16),
        ],
        10**9,
    )
    half_one = added(keep_one, swap(give_one, "rep", 1))
    half_two = added(keep_two, swap(give_two, "rep", 1))
    half_one, own_slots = lax.optimization_barrier((half_one, own_slots))
    grid_grad, mesh_out = call(
        results_kernel,
        (turned, g2m_pick, own_slots, mesh_first, normed_two),
        [(grid_latent.shape, BF16), (mesh_latent.shape, BF16)],
        [],
        10**8,
    )
    two = summed_over_chips(half_two)
    one, grid_grad = lax.optimization_barrier((summed_over_chips(half_one), grid_grad))
    hbm = pl.BlockSpec(memory_space=pltpu.HBM)
    stage = pltpu.VMEM((half, 2 * latent), F32)
    weight_shape = pltpu.HBM((columns, 4 * latent), F32)
    limit = pltpu.CompilerParams(vmem_limit_bytes=40 << 20)
    settled = pl.pallas_call(
        settle_kernel,
        out_shape=weight_shape,
        in_specs=[VMEM] * 3,
        out_specs=hbm,
        scratch_shapes=[stage] * 3 + [pltpu.SemaphoreType.DMA((3,))],
        compiler_params=limit,
    )(one, two, swap(two, "rep", 1))
    weight_grad = pl.pallas_call(
        finish_kernel,
        out_shape=weight_shape,
        in_specs=[VMEM, hbm],
        out_specs=hbm,
        scratch_shapes=[stage, pltpu.SemaphoreType.DMA((1,))],
        input_output_aliases={1: 0},
        compiler_params=limit,
    )(swap(one, "rep", 1), settled)
    return (mesh_out, grid_grad, weight_grad)


def solution(mesh):
    regions = mesh.shape["space"]
    samples = mesh.shape["rep"]

    def whole(*arguments):
        edges = arguments[5].shape[0] + arguments[8].shape[0]
        latent = arguments[3].shape[0]
        fits = edges * latent * 4 <= SAMPLE_EDGE_BYTES and latent % (128 * regions) == 0
        paired = regions > 2 and samples > 1 and not (regions & (regions - 1) | samples & (samples - 1))
        return sharded(whole_sample_body if fits and paired else partitioned_body)(*arguments)

    def sharded(body):
        return jax.shard_map(
            body,
            mesh=mesh,
            in_specs=(
                P(("groups", "rep"), "space", None),
                P(("groups", "rep"), "space", None),
                P(("groups", "rep"), "space", None),
                P(),
                P("space", None, None),
                P("space"),
                P("space"),
                P("space", None, None),
                P("space"),
                P("space"),
            ),
            out_specs=(
                P(("groups", "rep"), "space", None),
                P(("groups", "rep"), "space", None),
                P(("groups", "space"), None),
            ),
            check_vma=False,
        )

    return whole
```

```python
import functools

import jax
import jax.numpy as jnp
from jax import lax
from jax.experimental import pallas as pl
from jax.experimental.pallas import tpu as pltpu
from jax.sharding import PartitionSpec as P

EPSILON = 1e-05


def with_halo(cells, sides, width):
    for axis, dim in sides:
        count = lax.axis_size(axis)
        ends = count - 1
        head = lax.slice_in_dim(cells, 0, width, axis=dim)
        tail = lax.slice_in_dim(cells, cells.shape[dim] - width, cells.shape[dim], axis=dim)
        cells = jnp.concatenate(
            [
                lax.ppermute(tail, axis, [(i, (i + 1) % count) for i in range(ends)]),
                cells,
                lax.ppermute(head, axis, [((i + 1) % count, i) for i in range(ends)]),
            ],
            axis=dim,
        )
    return cells


def swish(values):
    return values * jax.nn.sigmoid(values)


def swish_slope(values):
    squash = jax.nn.sigmoid(values)
    return squash * (1.0 + values * (1.0 - squash))


def norm_rows(values):
    centred = values - jnp.mean(values, -1, keepdims=True)
    return centred * lax.rsqrt(jnp.mean(centred * centred, -1, keepdims=True) + EPSILON)


def norm_rows_back(values, upstream):
    centred = values - jnp.mean(values, -1, keepdims=True)
    scaled = lax.rsqrt(jnp.mean(centred * centred, -1, keepdims=True) + EPSILON)
    normed = centred * scaled
    return scaled * (
        upstream
        - jnp.mean(upstream, -1, keepdims=True)
        - normed * jnp.mean(upstream * normed, -1, keepdims=True)
    )


def slot_rows(pick_row):
    listed = pick_row.reshape(-1)
    return listed


def mesh_route(outgoing, capacity, peer_count):
    columns = outgoing.shape[1]
    pieces = lax.all_to_all(
        outgoing.reshape(peer_count, capacity, columns),
        "space",
        split_axis=0,
        concat_axis=0,
        tiled=True,
    )
    arrived = pieces.reshape(peer_count * capacity, columns)
    return arrived


def grid_route(outgoing, capacity):
    columns = outgoing.shape[1]
    lists = outgoing.reshape(3, capacity, columns)
    rims = with_halo(jnp.stack([lists[0], lists[2]]), (("space", 0),), 1)
    return jnp.concatenate([rims[0], lists[1], rims[3]], axis=0)


def edge_pass(arrived, recv_table, located, receiver, w_send, w_recv):
    recv_proj = jnp.dot(recv_table, w_recv, preferred_element_type=jnp.float32)
    slot_proj = jnp.dot(arrived, w_send, preferred_element_type=jnp.float32)
    activation = slot_proj[located] + recv_proj[receiver]
    message = swish(activation).astype(jnp.bfloat16)
    member = (
        receiver[None, :] == jnp.arange(recv_table.shape[0], dtype=jnp.int32)[:, None]
    ).astype(jnp.bfloat16)
    summed = jnp.dot(member, message, preferred_element_type=jnp.float32)
    return (activation, member, summed)


def backward_pass(slot_count, located, activation, member, receiver, agg_grad, w_send):
    edge_grad = (agg_grad[receiver] * swish_slope(activation)).astype(jnp.bfloat16)
    recv_sum = jnp.dot(member, edge_grad, preferred_element_type=jnp.float32).astype(jnp.bfloat16)
    slot_member = (located[None, :] == jnp.arange(slot_count, dtype=jnp.int32)[:, None]).astype(
        jnp.bfloat16
    )
    slot_sum = jnp.dot(slot_member, edge_grad, preferred_element_type=jnp.float32).astype(
        jnp.bfloat16
    )
    returned = jnp.dot(slot_sum, w_send.T, preferred_element_type=jnp.float32).astype(jnp.bfloat16)
    return (recv_sum, slot_sum, returned)


def gather_back(listed, back_rows, row_count):
    owner = (listed[None, :] == jnp.arange(row_count, dtype=jnp.int32)[:, None]).astype(
        jnp.bfloat16
    )
    return jnp.dot(owner, back_rows, preferred_element_type=jnp.float32)


def partitioned_body(
    grid_latent,
    mesh_latent,
    mesh_cotangent,
    weights,
    g2m_pick,
    g2m_sender,
    g2m_receiver,
    m2m_pick,
    m2m_sender,
    m2m_receiver,
):
    grid_rows = grid_latent[0]
    mesh_rows = mesh_latent[0]
    upstream = mesh_cotangent[0].astype(jnp.float32)
    latent = weights.shape[0]
    encode_sender = weights[:, :latent]
    encode_receiver = weights[:, latent : 2 * latent]
    process_sender = weights[:, 2 * latent : 3 * latent]
    process_receiver = weights[:, 3 * latent :]
    peer_count = lax.axis_size("space")
    grid_cap = g2m_pick.shape[2]
    mesh_cap = m2m_pick.shape[2]
    grid_listed = g2m_pick[0].reshape(-1)
    grid_arrived = grid_route(grid_rows[grid_listed], grid_cap)
    act_first, member_first, summed_first = edge_pass(
        grid_arrived, mesh_rows, g2m_sender, g2m_receiver, encode_sender, encode_receiver
    )
    mesh_first = (mesh_rows.astype(jnp.float32) + norm_rows(summed_first)).astype(jnp.bfloat16)
    mesh_listed = slot_rows(m2m_pick[0])
    mesh_arrived = mesh_route(mesh_first[mesh_listed], mesh_cap, peer_count)
    act_second, member_second, summed_second = edge_pass(
        mesh_arrived, mesh_first, m2m_sender, m2m_receiver, process_sender, process_receiver
    )
    mesh_final = (mesh_first.astype(jnp.float32) + norm_rows(summed_second)).astype(jnp.bfloat16)
    agg_second = norm_rows_back(summed_second, upstream)
    recv_second, slot_second, returned_second = backward_pass(
        mesh_arrived.shape[0],
        m2m_sender,
        act_second,
        member_second,
        m2m_receiver,
        agg_second,
        process_sender,
    )
    back_second = mesh_route(returned_second, mesh_cap, peer_count)
    mesh_grad = upstream + jnp.dot(
        recv_second, process_receiver.T, preferred_element_type=jnp.float32
    )
    mesh_grad = mesh_grad + gather_back(mesh_listed, back_second, mesh_rows.shape[0])
    agg_first = norm_rows_back(summed_first, mesh_grad)
    recv_first, slot_first, returned_first = backward_pass(
        grid_arrived.shape[0],
        g2m_sender,
        act_first,
        member_first,
        g2m_receiver,
        agg_first,
        encode_sender,
    )
    back_first = grid_route(returned_first, grid_cap)
    grid_grad = gather_back(grid_listed, back_first, grid_rows.shape[0]).astype(jnp.bfloat16)
    factor_pairs = (
        (grid_arrived, slot_first),
        (mesh_rows, recv_first),
        (mesh_arrived, slot_second),
        (mesh_first, recv_second),
    )
    blocks = []
    for first_factor, second_factor in factor_pairs:
        blocks.append(
            lax.dot_general(
                first_factor,
                second_factor,
                (((0,), (0,)), ((), ())),
                preferred_element_type=jnp.float32,
            )
        )
    shares = lax.psum_scatter(
        jnp.concatenate(blocks, axis=1).astype(jnp.bfloat16),
        "space",
        scatter_dimension=0,
        tiled=True,
    )
    weight_grad = lax.psum(shares, "rep").astype(jnp.float32)
    return (mesh_final[None], grid_grad[None], weight_grad)


F32 = jnp.float32
BF16 = jnp.bfloat16
INDEX_ROWS = 8
SAMPLE_EDGE_BYTES = 8 << 20


def dot(left, right):
    return jnp.dot(left, right, preferred_element_type=F32)


def dot_first(left, right):
    return lax.dot_general(left, right, (((0,), (0,)), ((), ())), preferred_element_type=F32)


def one_hot(labels, count):
    rows = lax.broadcasted_iota(jnp.int32, (count, labels.shape[-1]), 0)
    return (rows == labels).astype(F32).astype(BF16)


def row_moments(values):
    centred = values - jnp.mean(values, -1, keepdims=True)
    return centred, lax.rsqrt(jnp.mean(centred * centred, -1, keepdims=True) + EPSILON)


def moments_back(normed, scaled, upstream):
    return scaled * (
        upstream
        - jnp.mean(upstream, -1, keepdims=True)
        - normed * jnp.mean(upstream * normed, -1, keepdims=True)
    )


def fetch(pairs, semaphores):
    copies = [
        pltpu.make_async_copy(source, target, semaphores.at[n])
        for n, (source, target) in enumerate(pairs)
    ]
    for copy in copies:
        copy.start()
    for copy in copies:
        copy.wait()


def pack_kernel(*refs):
    sources, packed_ref, index_ref = refs[:8], refs[8], refs[9]
    local, semaphores = refs[10:18], refs[18]
    fetch(list(zip(sources, local)), semaphores)
    (
        grid_ref,
        mesh_ref,
        g2m_pick_ref,
        g2m_sender_ref,
        g2m_receiver_ref,
        m2m_pick_ref,
        m2m_sender_ref,
        m2m_receiver_ref,
    ) = local
    lists, _, capacity = g2m_pick_ref.shape
    mesh_count = mesh_ref.shape[1]
    regions, mesh_cap = m2m_pick_ref.shape[1:]
    edges = g2m_sender_ref.shape[1]
    grid_rows = grid_ref[0]
    for i in range(lists):
        picked = one_hot(g2m_pick_ref[i], grid_rows.shape[0])
        packed_ref[i * capacity : (i + 1) * capacity, :] = dot_first(picked, grid_rows).astype(BF16)
    first = lists * capacity
    packed_ref[first : first + mesh_count, :] = mesh_ref[0]
    index_ref[...] = jnp.zeros_like(index_ref)
    index_ref[0:1, 0:edges] = g2m_sender_ref[...].astype(F32)
    index_ref[0:1, edges : 2 * edges] = g2m_receiver_ref[...].astype(F32)
    index_ref[1:2, 0:edges] = m2m_sender_ref[...].astype(F32)
    index_ref[1:2, edges : 2 * edges] = m2m_receiver_ref[...].astype(F32)
    slots = regions * mesh_cap
    lane = lax.broadcasted_iota(jnp.int32, (mesh_cap, slots), 1)
    spread = (lane % mesh_cap == lax.broadcasted_iota(jnp.int32, (mesh_cap, slots), 0)).astype(F32)
    spread = dot(m2m_pick_ref[0].astype(F32).astype(BF16), spread.astype(BF16))
    lane = lax.broadcasted_iota(jnp.int32, (regions, slots), 1)
    owned = lane // mesh_cap == lax.broadcasted_iota(jnp.int32, (regions, slots), 0)
    index_ref[2:3, 0:slots] = jnp.sum(jnp.where(owned, spread, 0.0), 0, keepdims=True)
    packed_ref[first + mesh_count :, :] = index_ref[...].astype(BF16)


def weights_kernel(source_ref, weights_ref, turned_ref, semaphores):
    fetch([(source_ref, weights_ref)], semaphores)
    latent = weights_ref.shape[0]
    for n, block in enumerate((0, 2, 3)):
        turned_ref[:, n * latent : (n + 1) * latent] = weights_ref[
            :, block * latent : (block + 1) * latent
        ].T


def edge_blocks(edges, size):
    size = min(edges, size)
    return [(first, min(size, edges - first)) for first in range(0, edges, size)]


def edge_forward(tables, hot_ref, turned_hot_ref, slope_ref, message_ref, mesh_count):
    regions = len(tables)
    edges = slope_ref.shape[0] // regions
    count = hot_ref.shape[0] // regions
    work = [(d, first, size) for d in range(regions) for first, size in edge_blocks(edges, 256)]

    def gathered(d, first, size):
        rows = slice(d * edges + first, d * edges + first + size)
        return dot(turned_hot_ref[rows, :], tables[d])

    sums = []
    activation = gathered(*work[0])
    for n, (d, first, size) in enumerate(work):
        coming = gathered(*work[n + 1]) if n + 1 < len(work) else None
        activation = activation.astype(BF16)
        squash = 0.5 + 0.5 * jnp.tanh(0.5 * activation)
        message = activation * squash
        rows = slice(d * edges + first, d * edges + first + size)
        slope_ref[rows, :] = squash + message * (1.0 - squash)
        message_ref[rows, :] = message
        activation = coming
        if first + size == edges:
            hot = hot_ref[(d + 1) * count - mesh_count : (d + 1) * count, :]
            sums.append(dot(hot, message_ref[d * edges : (d + 1) * edges, :]))
    return sums


def forward_kernel(
    steps,
    listed,
    mesh_count,
    mesh_cap,
    *refs,
):
    regions = len(steps)
    packed_refs = refs[:regions]
    (
        weights_ref,
        grid_ref,
        mesh_ref,
        first_ref,
        sent_ref,
        hot_one_ref,
        hot_two_ref,
        turned_one_ref,
        turned_two_ref,
        hot_sent_ref,
        slope_one_ref,
        slope_two_ref,
        normed_one_ref,
        scaled_one_ref,
        normed_two_ref,
        scaled_two_ref,
        index_ref,
        message_ref,
        sum_ref,
    ) = refs[regions:]
    latent = weights_ref.shape[0]
    edges = slope_one_ref.shape[0] // regions
    capacity = listed // 3
    slots = regions * mesh_cap
    me = lax.axis_index("space")
    for step, packed_ref in zip(steps, packed_refs):
        region = lax.bitwise_xor(me, step)
        at = lambda rows: pl.ds(pl.multiple_of(region * rows, rows), rows)
        grid_ref[at(listed), :] = packed_ref[:listed, :]
        mesh_ref[at(mesh_count), :] = packed_ref[listed : listed + mesh_count, :]
        index_ref[at(INDEX_ROWS), :] = packed_ref[listed + mesh_count :, :].astype(F32)

    grid_proj = dot(grid_ref[...], weights_ref[:, :latent])
    mesh_proj = dot(mesh_ref[...], weights_ref[:, latent : 2 * latent])
    for d in range(regions):
        index = index_ref[d * INDEX_ROWS : (d + 1) * INDEX_ROWS, :].astype(jnp.int32)
        for row, senders, hot_ref, turned_ref in (
            (0, listed, hot_one_ref, turned_one_ref),
            (1, slots, hot_two_ref, turned_two_ref),
        ):
            count = senders + mesh_count
            hot = jnp.concatenate(
                [
                    one_hot(index[row : row + 1, :edges], senders),
                    one_hot(index[row : row + 1, edges:], mesh_count),
                ],
                axis=0,
            )
            hot_ref[d * count : (d + 1) * count, :] = hot
            turned_ref[d * edges : (d + 1) * edges, :] = hot.T
        hot_sent_ref[d * mesh_count : (d + 1) * mesh_count, :] = one_hot(
            index[2:3, :slots], mesh_count
        )

    blank = jnp.zeros((capacity, latent), F32)
    tables = []
    for d in range(regions):
        before = (d - 1) * listed + 2 * capacity
        within = d * listed + capacity
        after = (d + 1) * listed
        tables.append(
            jnp.concatenate(
                [
                    grid_proj[before : before + capacity] if d > 0 else blank,
                    grid_proj[within : within + capacity],
                    grid_proj[after : after + capacity] if d < regions - 1 else blank,
                    mesh_proj[d * mesh_count : (d + 1) * mesh_count],
                ],
                axis=0,
            ).astype(BF16)
        )
    sums = edge_forward(
        tables, hot_one_ref, turned_one_ref, slope_one_ref, message_ref, mesh_count
    )
    for d in range(regions):
        sum_ref[d * mesh_count : (d + 1) * mesh_count, :] = sums[d]
    centred, scaled = row_moments(sum_ref[...])
    normed = centred * scaled
    normed_one_ref[...] = normed
    scaled_one_ref[...] = jnp.broadcast_to(scaled, scaled_one_ref.shape)
    first_ref[...] = (mesh_ref[...].astype(F32) + normed).astype(BF16)

    for s in range(regions):
        rows = slice(s * mesh_count, (s + 1) * mesh_count)
        sent_ref[s * slots : (s + 1) * slots, :] = dot_first(
            hot_sent_ref[rows, :], first_ref[rows, :]
        ).astype(BF16)
    sent_proj = dot(sent_ref[...], weights_ref[:, 2 * latent : 3 * latent])
    first_proj = dot(first_ref[...], weights_ref[:, 3 * latent :])
    tables = []
    for d in range(regions):
        pieces = [
            sent_proj[s * slots + d * mesh_cap : s * slots + (d + 1) * mesh_cap]
            for s in range(regions)
        ]
        tables.append(
            jnp.concatenate(
                pieces + [first_proj[d * mesh_count : (d + 1) * mesh_count]], axis=0
            ).astype(BF16)
        )
    sums = edge_forward(
        tables, hot_two_ref, turned_two_ref, slope_two_ref, message_ref, mesh_count
    )
    for d in range(regions):
        sum_ref[d * mesh_count : (d + 1) * mesh_count, :] = sums[d]
    centred, scaled = row_moments(sum_ref[...])
    normed_two_ref[...] = centred * scaled
    scaled_two_ref[...] = jnp.broadcast_to(scaled, scaled_two_ref.shape)


def edge_backward(regions, agg_grad_ref, hot_ref, turned_hot_ref, slope_ref, edge_grad_ref):
    mesh_count = agg_grad_ref.shape[0] // len(regions)
    edges = edge_grad_ref.shape[0] // len(regions)
    count = turned_hot_ref.shape[1]
    blank = jnp.zeros((count - mesh_count, agg_grad_ref.shape[1]), BF16)
    work = [(n, first, size) for n in range(len(regions)) for first, size in edge_blocks(edges, 256)]

    def at(n, first, size):
        return pl.ds(pl.multiple_of(regions[n] * edges + first, size), size)

    def gathered(n, first, size):
        own = agg_grad_ref[n * mesh_count : (n + 1) * mesh_count, :]
        return dot(turned_hot_ref[at(n, first, size), :], jnp.concatenate([blank, own], axis=0))

    sums = []
    upstream = gathered(*work[0])
    for k, (n, first, size) in enumerate(work):
        coming = gathered(*work[k + 1]) if k + 1 < len(work) else None
        rows = slice(n * edges + first, n * edges + first + size)
        edge_grad_ref[rows, :] = upstream.astype(BF16) * slope_ref[at(n, first, size), :]
        upstream = coming
        if first + size == edges:
            hot = hot_ref[pl.ds(pl.multiple_of(regions[n] * count, count), count), :]
            sums.append(dot(hot, edge_grad_ref[n * edges : (n + 1) * edges, :]))
    return sums


def halve(share_ref, keep_ref, give_ref):
    half = keep_ref.shape[0]
    core = lax.bitwise_and(lax.axis_index("rep"), 1)
    keep_ref[...] = share_ref[pl.ds(pl.multiple_of(core * half, half), half), :]
    give_ref[...] = share_ref[pl.ds(pl.multiple_of((1 - core) * half, half), half), :]


def process_back_part(
    steps, mesh_count, cotangent_refs, hot_ref, turned_hot_ref, slope_ref, normed_ref, scaled_ref,
    agg_grad_ref, edge_grad_ref,
):
    me = lax.axis_index("space")
    regions = [lax.bitwise_xor(me, step) for step in steps]
    for n, (region, cotangent_ref) in enumerate(zip(regions, cotangent_refs)):
        rows = pl.ds(pl.multiple_of(region * mesh_count, mesh_count), mesh_count)
        agg_grad_ref[n * mesh_count : (n + 1) * mesh_count, :] = moments_back(
            normed_ref[rows, :], scaled_ref[rows, 0:1], cotangent_ref[0].astype(F32)
        ).astype(BF16)
    return regions, edge_backward(
        regions, agg_grad_ref, hot_ref, turned_hot_ref, slope_ref, edge_grad_ref
    )


def near_back_kernel(steps, *refs):
    cotangent_refs, refs = refs[: len(steps)], refs[len(steps) :]
    (
        hot_ref,
        turned_hot_ref,
        slope_ref,
        normed_ref,
        scaled_ref,
        *whole_refs,
    ) = refs[:9]
    sums_ref, *column_refs = refs[9:14]
    agg_grad_ref, edge_grad_ref = refs[14:]
    mesh_count = agg_grad_ref.shape[0] // len(steps)
    count = turned_hot_ref.shape[1]
    _, all_sums = process_back_part(
        steps, mesh_count, cotangent_refs, hot_ref, turned_hot_ref, slope_ref, normed_ref,
        scaled_ref, agg_grad_ref, edge_grad_ref,
    )
    for n, sums in enumerate(all_sums):
        sums_ref[n * count : (n + 1) * count, :] = sums
    columns = column_refs[0].shape[0]
    mine = pl.ds(pl.multiple_of(lax.axis_index("space") * columns, columns), columns)
    for whole_ref, column_ref in zip(whole_refs, column_refs):
        column_ref[...] = whole_ref[:, mine].T


def far_back_kernel(near, far, mesh_cap, *refs):
    regions = len(near) + len(far)
    cotangent_refs, refs = refs[:regions], refs[regions:]
    (
        turned_ref,
        first_columns_ref,
        sent_columns_ref,
        near_sums_ref,
        hot_ref,
        turned_hot_ref,
        hot_sent_ref,
        slope_ref,
        normed_ref,
        scaled_ref,
        mesh_grad_ref,
        keep_ref,
        give_ref,
        upstream_ref,
        slot_ref,
        recv_ref,
        share_ref,
        agg_grad_ref,
        edge_grad_ref,
    ) = refs
    latent = normed_ref.shape[1]
    mesh_count = normed_ref.shape[0] // regions
    count = turned_hot_ref.shape[1]
    slots = regions * mesh_cap
    me = lax.axis_index("space")
    far_regions, all_sums = process_back_part(
        far, mesh_count, cotangent_refs[len(near) :], hot_ref, turned_hot_ref, slope_ref,
        normed_ref, scaled_ref, agg_grad_ref, edge_grad_ref,
    )
    near_regions = [lax.bitwise_xor(me, step) for step in near]
    near_sums = [near_sums_ref[n * count : (n + 1) * count, :] for n in range(len(near))]
    for region, sums in zip(near_regions + far_regions, near_sums + all_sums):
        for s in range(regions):
            slot_ref[pl.ds(pl.multiple_of(s * slots + region * mesh_cap, mesh_cap), mesh_cap), :] = (
                sums[s * mesh_cap : (s + 1) * mesh_cap]
            )
        recv_ref[pl.ds(pl.multiple_of(region * mesh_count, mesh_count), mesh_count), :] = sums[
            slots:
        ].astype(BF16)
    for region, cotangent_ref in zip(near_regions + far_regions, cotangent_refs):
        rows = pl.ds(pl.multiple_of(region * mesh_count, mesh_count), mesh_count)
        upstream_ref[rows, :] = cotangent_ref[0].astype(F32)
    slot_sum = slot_ref[...].astype(BF16)
    share_ref[:, :latent] = dot(sent_columns_ref[...], slot_sum).astype(BF16)
    share_ref[:, latent:] = dot(first_columns_ref[...], recv_ref[...]).astype(BF16)
    halve(share_ref, keep_ref, give_ref)
    returned = dot(slot_sum, turned_ref[:, latent : 2 * latent]).astype(BF16)
    grad = upstream_ref[...] + dot(recv_ref[...], turned_ref[:, 2 * latent :])
    for s in range(regions):
        rows = slice(s * mesh_count, (s + 1) * mesh_count)
        mesh_grad_ref[rows, :] = grad[rows] + dot(
            hot_sent_ref[rows, :], returned[s * slots : (s + 1) * slots]
        )


def encode_back_kernel(
    regions,
    grid_columns_ref,
    mesh_columns_ref,
    hot_ref,
    turned_hot_ref,
    slope_ref,
    normed_ref,
    scaled_ref,
    mesh_grad_ref,
    own_slot_ref,
    keep_ref,
    give_ref,
    slot_ref,
    recv_ref,
    share_ref,
    agg_grad_ref,
    edge_grad_ref,
):
    latent = normed_ref.shape[1]
    mesh_count = normed_ref.shape[0] // regions
    listed = slot_ref.shape[0] // regions
    capacity = listed // 3
    me = lax.axis_index("space")
    agg_grad_ref[...] = moments_back(
        normed_ref[...], scaled_ref[:, 0:1], mesh_grad_ref[...]
    ).astype(BF16)
    blank = jnp.zeros((capacity, latent), BF16)
    slot_ref[0:capacity, :] = blank
    slot_ref[regions * listed - capacity :, :] = blank
    all_sums = edge_backward(
        range(regions), agg_grad_ref, hot_ref, turned_hot_ref, slope_ref, edge_grad_ref
    )
    for d, sums in enumerate(all_sums):
        sums = sums.astype(BF16)
        for j in range(3):
            source = d + j - 1
            if 0 <= source < regions:
                first = source * listed + (2 - j) * capacity
                slot_ref[first : first + capacity, :] = sums[j * capacity : (j + 1) * capacity]
        recv_ref[d * mesh_count : (d + 1) * mesh_count, :] = sums[listed:]
    share_ref[:, :latent] = dot(grid_columns_ref[...], slot_ref[...]).astype(BF16)
    share_ref[:, latent:] = dot(mesh_columns_ref[...], recv_ref[...]).astype(BF16)
    halve(share_ref, keep_ref, give_ref)
    own = pl.ds(pl.multiple_of(me * listed, listed), listed)
    own_slot_ref[...] = slot_ref[own, :]


def results_kernel(
    turned_ref, pick_ref, own_slot_ref, first_ref, normed_ref, grid_grad_ref, mesh_out_ref
):
    mesh_count = mesh_out_ref.shape[1]
    me = lax.axis_index("space")
    own = pl.ds(pl.multiple_of(me * mesh_count, mesh_count), mesh_count)
    mesh_out_ref[0] = (first_ref[own, :].astype(F32) + normed_ref[own, :]).astype(BF16)
    lists, _, capacity = pick_ref.shape
    latent = own_slot_ref.shape[1]
    returned = dot(own_slot_ref[...], turned_ref[:, :latent]).astype(BF16)
    total = None
    for i in range(lists):
        owner = one_hot(pick_ref[i], grid_grad_ref.shape[1])
        part = dot(owner, returned[i * capacity : (i + 1) * capacity])
        total = part if total is None else total + part
    grid_grad_ref[0] = total.astype(BF16)


def place(pairs, stages, semaphores):
    copies = []
    for n, (block_ref, target) in enumerate(pairs):
        stages[n][...] = block_ref[...].astype(F32)
        copies.append(pltpu.make_async_copy(stages[n], target, semaphores.at[n]))
        copies[n].start()
    for copy in copies:
        copy.wait()


def half_rows(half):
    core = lax.bitwise_and(lax.axis_index("rep"), 1)
    mine = pl.ds(pl.multiple_of(core * half, half), half)
    return mine, pl.ds(pl.multiple_of((1 - core) * half, half), half)


def settle_kernel(one_ref, two_ref, other_two_ref, weight_grad_ref, *scratch):
    half, width = one_ref.shape
    mine, other = half_rows(half)
    place(
        [
            (two_ref, weight_grad_ref.at[mine, width:]),
            (other_two_ref, weight_grad_ref.at[other, width:]),
            (one_ref, weight_grad_ref.at[mine, :width]),
        ],
        scratch[:3],
        scratch[3],
    )


def finish_kernel(other_one_ref, settled_ref, weight_grad_ref, stage, semaphores):
    half, width = other_one_ref.shape
    _, other = half_rows(half)
    place([(other_one_ref, weight_grad_ref.at[other, :width])], [stage], semaphores)


VMEM = pl.BlockSpec(memory_space=pltpu.VMEM)


def call(kernel, operands, outputs, scratch, flops, fetched=0):
    hbm = pl.BlockSpec(memory_space=pltpu.HBM)
    operands = [
        pltpu.with_memory_space_constraint(operand, pltpu.HBM) if n < fetched else operand
        for n, operand in enumerate(operands)
    ]
    return pl.pallas_call(
        kernel,
        out_shape=[jax.ShapeDtypeStruct(shape, kind) for shape, kind in outputs],
        in_specs=[hbm] * fetched + [VMEM] * (len(operands) - fetched),
        out_specs=[VMEM] * len(outputs),
        scratch_shapes=[pltpu.VMEM(shape, kind) for shape, kind in scratch]
        + ([pltpu.SemaphoreType.DMA((fetched,))] if fetched else []),
        compiler_params=pltpu.CompilerParams(vmem_limit_bytes=40 << 20),
        cost_estimate=pl.CostEstimate(flops=flops, bytes_accessed=4 << 20, transcendentals=0),
    )(*operands)


def swap(block, axis, bits):
    return lax.ppermute(block, axis, [(i, i ^ bits) for i in range(lax.axis_size(axis))])


def added(left, right):
    return (left.astype(F32) + right.astype(F32)).astype(BF16)


def summed_over_chips(half):
    bit = 2
    while bit < lax.axis_size("rep"):
        half = added(half, swap(half, "rep", bit))
        bit *= 2
    return half


def whole_sample_body(
    grid_latent,
    mesh_latent,
    mesh_cotangent,
    weights,
    g2m_pick,
    g2m_sender,
    g2m_receiver,
    m2m_pick,
    m2m_sender,
    m2m_receiver,
):
    regions = lax.axis_size("space")
    latent = weights.shape[0]
    listed = g2m_pick.shape[1] * g2m_pick.shape[2]
    mesh_count = mesh_latent.shape[1]
    mesh_cap = m2m_pick.shape[2]
    edges = g2m_sender.shape[0]
    columns = latent // regions
    half = columns // 2
    g2m_pick = g2m_pick.transpose(1, 0, 2)
    sources = (
        grid_latent,
        mesh_latent,
        g2m_pick,
        g2m_sender.reshape(1, -1),
        g2m_receiver.reshape(1, -1),
        m2m_pick,
        m2m_sender.reshape(1, -1),
        m2m_receiver.reshape(1, -1),
    )
    packed = call(
        pack_kernel,
        sources,
        [((listed + mesh_count + INDEX_ROWS, latent), BF16)],
        [((INDEX_ROWS, latent), F32)] + [(source.shape, source.dtype) for source in sources],
        10**7,
        fetched=len(sources),
    )[0]
    packed, cotangent, weights = lax.optimization_barrier((packed, mesh_cotangent, weights))
    steps = (0, *range(2, regions), 1)
    packs = [packed] + [swap(packed, "space", step) for step in steps[1:]]
    near = swap(cotangent, "space", 1)
    weights, turned = call(
        weights_kernel,
        (weights,),
        [(weights.shape, BF16), ((latent, 3 * latent), BF16)],
        [],
        10**8,
        fetched=1,
    )
    turned, early = lax.optimization_barrier((turned, cotangent))
    packs[1], late = lax.optimization_barrier((packs[1], cotangent))
    cotangents = (
        [cotangent, swap(late, "space", steps[1])]
        + [swap(early, "space", step) for step in steps[2:-1]]
        + [near]
    )
    rows = regions * mesh_count
    slots = regions * mesh_cap
    (
        grid_all,
        mesh_all,
        mesh_first,
        mesh_sent,
        hot_one,
        hot_two,
        turned_one,
        turned_two,
        hot_sent,
        slope_one,
        slope_two,
        normed_one,
        scaled_one,
        normed_two,
        scaled_two,
    ) = call(
        functools.partial(forward_kernel, steps, listed, mesh_count, mesh_cap),
        (*packs, weights),
        [
            ((regions * listed, latent), BF16),
            ((rows, latent), BF16),
            ((rows, latent), BF16),
            ((regions * slots, latent), BF16),
            ((regions * (listed + mesh_count), edges), BF16),
            ((regions * (slots + mesh_count), edges), BF16),
            ((regions * edges, listed + mesh_count), BF16),
            ((regions * edges, slots + mesh_count), BF16),
            ((rows, slots), BF16),
            ((regions * edges, latent), BF16),
            ((regions * edges, latent), BF16),
            ((rows, latent), F32),
            ((rows, 128), F32),
            ((rows, latent), F32),
            ((rows, 128), F32),
        ],
        [
            ((regions * INDEX_ROWS, latent), F32),
            ((regions * edges, latent), BF16),
            ((rows, latent), F32),
        ],
        2 * 10**9,
    )
    by_step = dict(zip(steps, cotangents))
    near, far = (0, 1), tuple(step for step in steps if step > 1)
    count = slots + mesh_count
    near_sums, grid_columns, mesh_columns, sent_columns, first_columns = call(
        functools.partial(near_back_kernel, near),
        (
            *(by_step[step] for step in near),
            hot_two,
            turned_two,
            slope_two,
            normed_two,
            scaled_two,
            grid_all,
            mesh_all,
            mesh_sent,
            mesh_first,
        ),
        [
            ((len(near) * count, latent), F32),
            ((columns, regions * listed), BF16),
            ((columns, rows), BF16),
            ((columns, regions * slots), BF16),
            ((columns, rows), BF16),
        ],
        [((len(near) * mesh_count, latent), BF16), ((len(near) * edges, latent), BF16)],
        10**9,
    )
    mesh_grad, keep_two, give_two = call(
        functools.partial(far_back_kernel, near, far, mesh_cap),
        (
            *(by_step[step] for step in near + far),
            turned,
            first_columns,
            sent_columns,
            near_sums,
            hot_two,
            turned_two,
            hot_sent,
            slope_two,
            normed_two,
            scaled_two,
        ),
        [((rows, latent), F32)] + [((half, 2 * latent), BF16)] * 2,
        [
            ((rows, latent), F32),
            ((regions * slots, latent), F32),
            ((rows, latent), BF16),
            ((columns, 2 * latent), BF16),
            ((len(far) * mesh_count, latent), BF16),
            ((len(far) * edges, latent), BF16),
        ],
        10**9,
    )
    own_slots, keep_one, give_one = call(
        functools.partial(encode_back_kernel, regions),
        (
            grid_columns,
            mesh_columns,
            hot_one,
            turned_one,
            slope_one,
            normed_one,
            scaled_one,
            mesh_grad,
        ),
        [((listed, latent), BF16)] + [((half, 2 * latent), BF16)] * 2,
        [
            ((regions * listed, latent), BF16),
            ((rows, latent), BF16),
            ((columns, 2 * latent), BF16),
            ((rows, latent), BF16),
            ((regions * edges, latent), BF16),
        ],
        10**9,
    )
    half_one = added(keep_one, swap(give_one, "rep", 1))
    half_two = added(keep_two, swap(give_two, "rep", 1))
    half_one, own_slots = lax.optimization_barrier((half_one, own_slots))
    grid_grad, mesh_out = call(
        results_kernel,
        (turned, g2m_pick, own_slots, mesh_first, normed_two),
        [(grid_latent.shape, BF16), (mesh_latent.shape, BF16)],
        [],
        10**8,
    )
    two = summed_over_chips(half_two)
    one, grid_grad = lax.optimization_barrier((summed_over_chips(half_one), grid_grad))
    hbm = pl.BlockSpec(memory_space=pltpu.HBM)
    stage = pltpu.VMEM((half, 2 * latent), F32)
    weight_shape = pltpu.HBM((columns, 4 * latent), F32)
    limit = pltpu.CompilerParams(vmem_limit_bytes=40 << 20)
    settled = pl.pallas_call(
        settle_kernel,
        out_shape=weight_shape,
        in_specs=[VMEM] * 3,
        out_specs=hbm,
        scratch_shapes=[stage] * 3 + [pltpu.SemaphoreType.DMA((3,))],
        compiler_params=limit,
    )(one, two, swap(two, "rep", 1))
    weight_grad = pl.pallas_call(
        finish_kernel,
        out_shape=weight_shape,
        in_specs=[VMEM, hbm],
        out_specs=hbm,
        scratch_shapes=[stage, pltpu.SemaphoreType.DMA((1,))],
        input_output_aliases={1: 0},
        compiler_params=limit,
    )(swap(one, "rep", 1), settled)
    return (mesh_out, grid_grad, weight_grad)


def solution(mesh):
    regions = mesh.shape["space"]
    samples = mesh.shape["rep"]

    def whole(*arguments):
        edges = arguments[5].shape[0] + arguments[8].shape[0]
        latent = arguments[3].shape[0]
        fits = edges * latent * 4 <= SAMPLE_EDGE_BYTES and latent % (128 * regions) == 0
        paired = regions > 2 and samples > 1 and not (regions & (regions - 1) | samples & (samples - 1))
        return sharded(whole_sample_body if fits and paired else partitioned_body)(*arguments)

    def sharded(body):
        return jax.shard_map(
            body,
            mesh=mesh,
            in_specs=(
                P(("groups", "rep"), "space", None),
                P(("groups", "rep"), "space", None),
                P(("groups", "rep"), "space", None),
                P(),
                P("space", None, None),
                P("space"),
                P("space"),
                P("space", None, None),
                P("space"),
                P("space"),
            ),
            out_specs=(
                P(("groups", "rep"), "space", None),
                P(("groups", "rep"), "space", None),
                P(("groups", "space"), None),
            ),
            check_vma=False,
        )

    return whole
```

```python
import functools

import jax
import jax.numpy as jnp
from jax import lax
from jax.experimental import pallas as pl
from jax.experimental.pallas import tpu as pltpu
from jax.sharding import PartitionSpec as P

EPSILON = 1e-05


def with_halo(cells, sides, width):
    for axis, dim in sides:
        count = lax.axis_size(axis)
        ends = count - 1
        head = lax.slice_in_dim(cells, 0, width, axis=dim)
        tail = lax.slice_in_dim(cells, cells.shape[dim] - width, cells.shape[dim], axis=dim)
        cells = jnp.concatenate(
            [
                lax.ppermute(tail, axis, [(i, (i + 1) % count) for i in range(ends)]),
                cells,
                lax.ppermute(head, axis, [((i + 1) % count, i) for i in range(ends)]),
            ],
            axis=dim,
        )
    return cells


def swish(values):
    return values * jax.nn.sigmoid(values)


def swish_slope(values):
    squash = jax.nn.sigmoid(values)
    return squash * (1.0 + values * (1.0 - squash))


def norm_rows(values):
    centred = values - jnp.mean(values, -1, keepdims=True)
    return centred * lax.rsqrt(jnp.mean(centred * centred, -1, keepdims=True) + EPSILON)


def norm_rows_back(values, upstream):
    centred = values - jnp.mean(values, -1, keepdims=True)
    scaled = lax.rsqrt(jnp.mean(centred * centred, -1, keepdims=True) + EPSILON)
    normed = centred * scaled
    return scaled * (
        upstream
        - jnp.mean(upstream, -1, keepdims=True)
        - normed * jnp.mean(upstream * normed, -1, keepdims=True)
    )


def slot_rows(pick_row):
    listed = pick_row.reshape(-1)
    return listed


def mesh_route(outgoing, capacity, peer_count):
    columns = outgoing.shape[1]
    pieces = lax.all_to_all(
        outgoing.reshape(peer_count, capacity, columns),
        "space",
        split_axis=0,
        concat_axis=0,
        tiled=True,
    )
    arrived = pieces.reshape(peer_count * capacity, columns)
    return arrived


def grid_route(outgoing, capacity):
    columns = outgoing.shape[1]
    lists = outgoing.reshape(3, capacity, columns)
    rims = with_halo(jnp.stack([lists[0], lists[2]]), (("space", 0),), 1)
    return jnp.concatenate([rims[0], lists[1], rims[3]], axis=0)


def edge_pass(arrived, recv_table, located, receiver, w_send, w_recv):
    recv_proj = jnp.dot(recv_table, w_recv, preferred_element_type=jnp.float32)
    slot_proj = jnp.dot(arrived, w_send, preferred_element_type=jnp.float32)
    activation = slot_proj[located] + recv_proj[receiver]
    message = swish(activation).astype(jnp.bfloat16)
    member = (
        receiver[None, :] == jnp.arange(recv_table.shape[0], dtype=jnp.int32)[:, None]
    ).astype(jnp.bfloat16)
    summed = jnp.dot(member, message, preferred_element_type=jnp.float32)
    return (activation, member, summed)


def backward_pass(slot_count, located, activation, member, receiver, agg_grad, w_send):
    edge_grad = (agg_grad[receiver] * swish_slope(activation)).astype(jnp.bfloat16)
    recv_sum = jnp.dot(member, edge_grad, preferred_element_type=jnp.float32).astype(jnp.bfloat16)
    slot_member = (located[None, :] == jnp.arange(slot_count, dtype=jnp.int32)[:, None]).astype(
        jnp.bfloat16
    )
    slot_sum = jnp.dot(slot_member, edge_grad, preferred_element_type=jnp.float32).astype(
        jnp.bfloat16
    )
    returned = jnp.dot(slot_sum, w_send.T, preferred_element_type=jnp.float32).astype(jnp.bfloat16)
    return (recv_sum, slot_sum, returned)


def gather_back(listed, back_rows, row_count):
    owner = (listed[None, :] == jnp.arange(row_count, dtype=jnp.int32)[:, None]).astype(
        jnp.bfloat16
    )
    return jnp.dot(owner, back_rows, preferred_element_type=jnp.float32)


def partitioned_body(
    grid_latent,
    mesh_latent,
    mesh_cotangent,
    weights,
    g2m_pick,
    g2m_sender,
    g2m_receiver,
    m2m_pick,
    m2m_sender,
    m2m_receiver,
):
    grid_rows = grid_latent[0]
    mesh_rows = mesh_latent[0]
    upstream = mesh_cotangent[0].astype(jnp.float32)
    latent = weights.shape[0]
    encode_sender = weights[:, :latent]
    encode_receiver = weights[:, latent : 2 * latent]
    process_sender = weights[:, 2 * latent : 3 * latent]
    process_receiver = weights[:, 3 * latent :]
    peer_count = lax.axis_size("space")
    grid_cap = g2m_pick.shape[2]
    mesh_cap = m2m_pick.shape[2]
    grid_listed = g2m_pick[0].reshape(-1)
    grid_arrived = grid_route(grid_rows[grid_listed], grid_cap)
    act_first, member_first, summed_first = edge_pass(
        grid_arrived, mesh_rows, g2m_sender, g2m_receiver, encode_sender, encode_receiver
    )
    mesh_first = (mesh_rows.astype(jnp.float32) + norm_rows(summed_first)).astype(jnp.bfloat16)
    mesh_listed = slot_rows(m2m_pick[0])
    mesh_arrived = mesh_route(mesh_first[mesh_listed], mesh_cap, peer_count)
    act_second, member_second, summed_second = edge_pass(
        mesh_arrived, mesh_first, m2m_sender, m2m_receiver, process_sender, process_receiver
    )
    mesh_final = (mesh_first.astype(jnp.float32) + norm_rows(summed_second)).astype(jnp.bfloat16)
    agg_second = norm_rows_back(summed_second, upstream)
    recv_second, slot_second, returned_second = backward_pass(
        mesh_arrived.shape[0],
        m2m_sender,
        act_second,
        member_second,
        m2m_receiver,
        agg_second,
        process_sender,
    )
    back_second = mesh_route(returned_second, mesh_cap, peer_count)
    mesh_grad = upstream + jnp.dot(
        recv_second, process_receiver.T, preferred_element_type=jnp.float32
    )
    mesh_grad = mesh_grad + gather_back(mesh_listed, back_second, mesh_rows.shape[0])
    agg_first = norm_rows_back(summed_first, mesh_grad)
    recv_first, slot_first, returned_first = backward_pass(
        grid_arrived.shape[0],
        g2m_sender,
        act_first,
        member_first,
        g2m_receiver,
        agg_first,
        encode_sender,
    )
    back_first = grid_route(returned_first, grid_cap)
    grid_grad = gather_back(grid_listed, back_first, grid_rows.shape[0]).astype(jnp.bfloat16)
    factor_pairs = (
        (grid_arrived, slot_first),
        (mesh_rows, recv_first),
        (mesh_arrived, slot_second),
        (mesh_first, recv_second),
    )
    blocks = []
    for first_factor, second_factor in factor_pairs:
        blocks.append(
            lax.dot_general(
                first_factor,
                second_factor,
                (((0,), (0,)), ((), ())),
                preferred_element_type=jnp.float32,
            )
        )
    shares = lax.psum_scatter(
        jnp.concatenate(blocks, axis=1).astype(jnp.bfloat16),
        "space",
        scatter_dimension=0,
        tiled=True,
    )
    weight_grad = lax.psum(shares, "rep").astype(jnp.float32)
    return (mesh_final[None], grid_grad[None], weight_grad)


F32 = jnp.float32
BF16 = jnp.bfloat16
INDEX_ROWS = 8
SAMPLE_EDGE_BYTES = 8 << 20


def dot(left, right):
    return jnp.dot(left, right, preferred_element_type=F32)


def dot_first(left, right):
    return lax.dot_general(left, right, (((0,), (0,)), ((), ())), preferred_element_type=F32)


def one_hot(labels, count):
    rows = lax.broadcasted_iota(jnp.int32, (count, labels.shape[-1]), 0)
    return (rows == labels).astype(F32).astype(BF16)


def row_moments(values):
    centred = values - jnp.mean(values, -1, keepdims=True)
    return centred, lax.rsqrt(jnp.mean(centred * centred, -1, keepdims=True) + EPSILON)


def moments_back(normed, scaled, upstream):
    return scaled * (
        upstream
        - jnp.mean(upstream, -1, keepdims=True)
        - normed * jnp.mean(upstream * normed, -1, keepdims=True)
    )


def fetch(pairs, semaphores):
    copies = [
        pltpu.make_async_copy(source, target, semaphores.at[n])
        for n, (source, target) in enumerate(pairs)
    ]
    for copy in copies:
        copy.start()
    for copy in copies:
        copy.wait()


def pack_kernel(*refs):
    sources, packed_ref, index_ref = refs[:8], refs[8], refs[9]
    local, semaphores = refs[10:18], refs[18]
    fetch(list(zip(sources, local)), semaphores)
    (
        grid_ref,
        mesh_ref,
        g2m_pick_ref,
        g2m_sender_ref,
        g2m_receiver_ref,
        m2m_pick_ref,
        m2m_sender_ref,
        m2m_receiver_ref,
    ) = local
    lists, _, capacity = g2m_pick_ref.shape
    mesh_count = mesh_ref.shape[1]
    regions, mesh_cap = m2m_pick_ref.shape[1:]
    edges = g2m_sender_ref.shape[1]
    grid_rows = grid_ref[0]
    for i in range(lists):
        picked = one_hot(g2m_pick_ref[i], grid_rows.shape[0])
        packed_ref[i * capacity : (i + 1) * capacity, :] = dot_first(picked, grid_rows).astype(BF16)
    first = lists * capacity
    packed_ref[first : first + mesh_count, :] = mesh_ref[0]
    index_ref[...] = jnp.zeros_like(index_ref)
    index_ref[0:1, 0:edges] = g2m_sender_ref[...].astype(F32)
    index_ref[0:1, edges : 2 * edges] = g2m_receiver_ref[...].astype(F32)
    index_ref[1:2, 0:edges] = m2m_sender_ref[...].astype(F32)
    index_ref[1:2, edges : 2 * edges] = m2m_receiver_ref[...].astype(F32)
    slots = regions * mesh_cap
    lane = lax.broadcasted_iota(jnp.int32, (mesh_cap, slots), 1)
    spread = (lane % mesh_cap == lax.broadcasted_iota(jnp.int32, (mesh_cap, slots), 0)).astype(F32)
    spread = dot(m2m_pick_ref[0].astype(F32).astype(BF16), spread.astype(BF16))
    lane = lax.broadcasted_iota(jnp.int32, (regions, slots), 1)
    owned = lane // mesh_cap == lax.broadcasted_iota(jnp.int32, (regions, slots), 0)
    index_ref[2:3, 0:slots] = jnp.sum(jnp.where(owned, spread, 0.0), 0, keepdims=True)
    packed_ref[first + mesh_count :, :] = index_ref[...].astype(BF16)


def weights_kernel(source_ref, weights_ref, turned_ref, semaphores):
    fetch([(source_ref, weights_ref)], semaphores)
    latent = weights_ref.shape[0]
    for n, block in enumerate((0, 2, 3)):
        turned_ref[:, n * latent : (n + 1) * latent] = weights_ref[
            :, block * latent : (block + 1) * latent
        ].T


def edge_blocks(edges, size):
    size = min(edges, size)
    return [(first, min(size, edges - first)) for first in range(0, edges, size)]


def edge_forward(tables, hot_ref, turned_hot_ref, slope_ref, message_ref, mesh_count):
    regions = len(tables)
    edges = slope_ref.shape[0] // regions
    count = hot_ref.shape[0] // regions
    work = [(d, first, size) for d in range(regions) for first, size in edge_blocks(edges, 256)]

    def gathered(d, first, size):
        rows = slice(d * edges + first, d * edges + first + size)
        return dot(turned_hot_ref[rows, :], tables[d])

    sums = []
    activation = gathered(*work[0])
    for n, (d, first, size) in enumerate(work):
        coming = gathered(*work[n + 1]) if n + 1 < len(work) else None
        activation = activation.astype(BF16)
        squash = 0.5 + 0.5 * jnp.tanh(0.5 * activation)
        message = activation * squash
        rows = slice(d * edges + first, d * edges + first + size)
        slope_ref[rows, :] = squash + message * (1.0 - squash)
        message_ref[rows, :] = message
        activation = coming
        if first + size == edges:
            hot = hot_ref[(d + 1) * count - mesh_count : (d + 1) * count, :]
            sums.append(dot(hot, message_ref[d * edges : (d + 1) * edges, :]))
    return sums


def forward_kernel(
    steps,
    listed,
    mesh_count,
    mesh_cap,
    *refs,
):
    regions = len(steps)
    packed_refs = refs[:regions]
    (
        weights_ref,
        grid_ref,
        mesh_ref,
        first_ref,
        sent_ref,
        hot_one_ref,
        hot_two_ref,
        turned_one_ref,
        turned_two_ref,
        hot_sent_ref,
        slope_one_ref,
        slope_two_ref,
        normed_one_ref,
        scaled_one_ref,
        normed_two_ref,
        scaled_two_ref,
        index_ref,
        message_ref,
        sum_ref,
    ) = refs[regions:]
    latent = weights_ref.shape[0]
    edges = slope_one_ref.shape[0] // regions
    capacity = listed // 3
    slots = regions * mesh_cap
    me = lax.axis_index("space")
    for step, packed_ref in zip(steps, packed_refs):
        region = lax.bitwise_xor(me, step)
        at = lambda rows: pl.ds(pl.multiple_of(region * rows, rows), rows)
        grid_ref[at(listed), :] = packed_ref[:listed, :]
        mesh_ref[at(mesh_count), :] = packed_ref[listed : listed + mesh_count, :]
        index_ref[at(INDEX_ROWS), :] = packed_ref[listed + mesh_count :, :].astype(F32)

    grid_proj = dot(grid_ref[...], weights_ref[:, :latent])
    mesh_proj = dot(mesh_ref[...], weights_ref[:, latent : 2 * latent])
    for d in range(regions):
        index = index_ref[d * INDEX_ROWS : (d + 1) * INDEX_ROWS, :].astype(jnp.int32)
        for row, senders, hot_ref, turned_ref in (
            (0, listed, hot_one_ref, turned_one_ref),
            (1, slots, hot_two_ref, turned_two_ref),
        ):
            count = senders + mesh_count
            hot = jnp.concatenate(
                [
                    one_hot(index[row : row + 1, :edges], senders),
                    one_hot(index[row : row + 1, edges:], mesh_count),
                ],
                axis=0,
            )
            hot_ref[d * count : (d + 1) * count, :] = hot
            turned_ref[d * edges : (d + 1) * edges, :] = hot.T
        hot_sent_ref[d * mesh_count : (d + 1) * mesh_count, :] = one_hot(
            index[2:3, :slots], mesh_count
        )

    blank = jnp.zeros((capacity, latent), F32)
    tables = []
    for d in range(regions):
        before = (d - 1) * listed + 2 * capacity
        within = d * listed + capacity
        after = (d + 1) * listed
        tables.append(
            jnp.concatenate(
                [
                    grid_proj[before : before + capacity] if d > 0 else blank,
                    grid_proj[within : within + capacity],
                    grid_proj[after : after + capacity] if d < regions - 1 else blank,
                    mesh_proj[d * mesh_count : (d + 1) * mesh_count],
                ],
                axis=0,
            ).astype(BF16)
        )
    sums = edge_forward(
        tables, hot_one_ref, turned_one_ref, slope_one_ref, message_ref, mesh_count
    )
    for d in range(regions):
        sum_ref[d * mesh_count : (d + 1) * mesh_count, :] = sums[d]
    centred, scaled = row_moments(sum_ref[...])
    normed = centred * scaled
    normed_one_ref[...] = normed
    scaled_one_ref[...] = jnp.broadcast_to(scaled, scaled_one_ref.shape)
    first_ref[...] = (mesh_ref[...].astype(F32) + normed).astype(BF16)

    for s in range(regions):
        rows = slice(s * mesh_count, (s + 1) * mesh_count)
        sent_ref[s * slots : (s + 1) * slots, :] = dot_first(
            hot_sent_ref[rows, :], first_ref[rows, :]
        ).astype(BF16)
    sent_proj = dot(sent_ref[...], weights_ref[:, 2 * latent : 3 * latent])
    first_proj = dot(first_ref[...], weights_ref[:, 3 * latent :])
    tables = []
    for d in range(regions):
        pieces = [
            sent_proj[s * slots + d * mesh_cap : s * slots + (d + 1) * mesh_cap]
            for s in range(regions)
        ]
        tables.append(
            jnp.concatenate(
                pieces + [first_proj[d * mesh_count : (d + 1) * mesh_count]], axis=0
            ).astype(BF16)
        )
    sums = edge_forward(
        tables, hot_two_ref, turned_two_ref, slope_two_ref, message_ref, mesh_count
    )
    for d in range(regions):
        sum_ref[d * mesh_count : (d + 1) * mesh_count, :] = sums[d]
    centred, scaled = row_moments(sum_ref[...])
    normed_two_ref[...] = centred * scaled
    scaled_two_ref[...] = jnp.broadcast_to(scaled, scaled_two_ref.shape)


def edge_backward(regions, agg_grad_ref, hot_ref, turned_hot_ref, slope_ref, edge_grad_ref):
    mesh_count = agg_grad_ref.shape[0] // len(regions)
    edges = edge_grad_ref.shape[0] // len(regions)
    count = turned_hot_ref.shape[1]
    blank = jnp.zeros((count - mesh_count, agg_grad_ref.shape[1]), BF16)
    work = [(n, first, size) for n in range(len(regions)) for first, size in edge_blocks(edges, 256)]

    def at(n, first, size):
        return pl.ds(pl.multiple_of(regions[n] * edges + first, size), size)

    def gathered(n, first, size):
        own = agg_grad_ref[n * mesh_count : (n + 1) * mesh_count, :]
        return dot(turned_hot_ref[at(n, first, size), :], jnp.concatenate([blank, own], axis=0))

    sums = []
    upstream = gathered(*work[0])
    for k, (n, first, size) in enumerate(work):
        coming = gathered(*work[k + 1]) if k + 1 < len(work) else None
        rows = slice(n * edges + first, n * edges + first + size)
        edge_grad_ref[rows, :] = upstream.astype(BF16) * slope_ref[at(n, first, size), :]
        upstream = coming
        if first + size == edges:
            hot = hot_ref[pl.ds(pl.multiple_of(regions[n] * count, count), count), :]
            sums.append(dot(hot, edge_grad_ref[n * edges : (n + 1) * edges, :]))
    return sums


def halve(share_ref, keep_ref, give_ref):
    half = keep_ref.shape[0]
    core = lax.bitwise_and(lax.axis_index("rep"), 1)
    keep_ref[...] = share_ref[pl.ds(pl.multiple_of(core * half, half), half), :]
    give_ref[...] = share_ref[pl.ds(pl.multiple_of((1 - core) * half, half), half), :]


def process_back_part(
    steps, mesh_count, cotangent_refs, hot_ref, turned_hot_ref, slope_ref, normed_ref, scaled_ref,
    agg_grad_ref, edge_grad_ref,
):
    me = lax.axis_index("space")
    regions = [lax.bitwise_xor(me, step) for step in steps]
    for n, (region, cotangent_ref) in enumerate(zip(regions, cotangent_refs)):
        rows = pl.ds(pl.multiple_of(region * mesh_count, mesh_count), mesh_count)
        agg_grad_ref[n * mesh_count : (n + 1) * mesh_count, :] = moments_back(
            normed_ref[rows, :], scaled_ref[rows, 0:1], cotangent_ref[0].astype(F32)
        ).astype(BF16)
    return regions, edge_backward(
        regions, agg_grad_ref, hot_ref, turned_hot_ref, slope_ref, edge_grad_ref
    )


def near_back_kernel(steps, *refs):
    cotangent_refs, refs = refs[: len(steps)], refs[len(steps) :]
    (
        hot_ref,
        turned_hot_ref,
        slope_ref,
        normed_ref,
        scaled_ref,
        *whole_refs,
    ) = refs[:9]
    sums_ref, *column_refs = refs[9:14]
    agg_grad_ref, edge_grad_ref = refs[14:]
    mesh_count = agg_grad_ref.shape[0] // len(steps)
    count = turned_hot_ref.shape[1]
    _, all_sums = process_back_part(
        steps, mesh_count, cotangent_refs, hot_ref, turned_hot_ref, slope_ref, normed_ref,
        scaled_ref, agg_grad_ref, edge_grad_ref,
    )
    for n, sums in enumerate(all_sums):
        sums_ref[n * count : (n + 1) * count, :] = sums
    columns = column_refs[0].shape[0]
    mine = pl.ds(pl.multiple_of(lax.axis_index("space") * columns, columns), columns)
    for whole_ref, column_ref in zip(whole_refs, column_refs):
        column_ref[...] = whole_ref[:, mine].T


def far_back_kernel(near, far, mesh_cap, *refs):
    regions = len(near) + len(far)
    cotangent_refs, refs = refs[:regions], refs[regions:]
    (
        turned_ref,
        first_columns_ref,
        sent_columns_ref,
        near_sums_ref,
        hot_ref,
        turned_hot_ref,
        hot_sent_ref,
        slope_ref,
        normed_ref,
        scaled_ref,
        mesh_grad_ref,
        keep_ref,
        give_ref,
        upstream_ref,
        slot_ref,
        recv_ref,
        share_ref,
        agg_grad_ref,
        edge_grad_ref,
    ) = refs
    latent = normed_ref.shape[1]
    mesh_count = normed_ref.shape[0] // regions
    count = turned_hot_ref.shape[1]
    slots = regions * mesh_cap
    me = lax.axis_index("space")
    far_regions, all_sums = process_back_part(
        far, mesh_count, cotangent_refs[len(near) :], hot_ref, turned_hot_ref, slope_ref,
        normed_ref, scaled_ref, agg_grad_ref, edge_grad_ref,
    )
    near_regions = [lax.bitwise_xor(me, step) for step in near]
    near_sums = [near_sums_ref[n * count : (n + 1) * count, :] for n in range(len(near))]
    for region, sums in zip(near_regions + far_regions, near_sums + all_sums):
        for s in range(regions):
            slot_ref[pl.ds(pl.multiple_of(s * slots + region * mesh_cap, mesh_cap), mesh_cap), :] = (
                sums[s * mesh_cap : (s + 1) * mesh_cap]
            )
        recv_ref[pl.ds(pl.multiple_of(region * mesh_count, mesh_count), mesh_count), :] = sums[
            slots:
        ].astype(BF16)
    for region, cotangent_ref in zip(near_regions + far_regions, cotangent_refs):
        rows = pl.ds(pl.multiple_of(region * mesh_count, mesh_count), mesh_count)
        upstream_ref[rows, :] = cotangent_ref[0].astype(F32)
    slot_sum = slot_ref[...].astype(BF16)
    share_ref[:, :latent] = dot(sent_columns_ref[...], slot_sum).astype(BF16)
    share_ref[:, latent:] = dot(first_columns_ref[...], recv_ref[...]).astype(BF16)
    halve(share_ref, keep_ref, give_ref)
    returned = dot(slot_sum, turned_ref[:, latent : 2 * latent]).astype(BF16)
    grad = upstream_ref[...] + dot(recv_ref[...], turned_ref[:, 2 * latent :])
    for s in range(regions):
        rows = slice(s * mesh_count, (s + 1) * mesh_count)
        mesh_grad_ref[rows, :] = grad[rows] + dot(
            hot_sent_ref[rows, :], returned[s * slots : (s + 1) * slots]
        )


def encode_back_kernel(
    regions,
    grid_columns_ref,
    mesh_columns_ref,
    hot_ref,
    turned_hot_ref,
    slope_ref,
    normed_ref,
    scaled_ref,
    mesh_grad_ref,
    own_slot_ref,
    keep_ref,
    give_ref,
    slot_ref,
    recv_ref,
    share_ref,
    agg_grad_ref,
    edge_grad_ref,
):
    latent = normed_ref.shape[1]
    mesh_count = normed_ref.shape[0] // regions
    listed = slot_ref.shape[0] // regions
    capacity = listed // 3
    me = lax.axis_index("space")
    agg_grad_ref[...] = moments_back(
        normed_ref[...], scaled_ref[:, 0:1], mesh_grad_ref[...]
    ).astype(BF16)
    blank = jnp.zeros((capacity, latent), BF16)
    slot_ref[0:capacity, :] = blank
    slot_ref[regions * listed - capacity :, :] = blank
    all_sums = edge_backward(
        range(regions), agg_grad_ref, hot_ref, turned_hot_ref, slope_ref, edge_grad_ref
    )
    for d, sums in enumerate(all_sums):
        sums = sums.astype(BF16)
        for j in range(3):
            source = d + j - 1
            if 0 <= source < regions:
                first = source * listed + (2 - j) * capacity
                slot_ref[first : first + capacity, :] = sums[j * capacity : (j + 1) * capacity]
        recv_ref[d * mesh_count : (d + 1) * mesh_count, :] = sums[listed:]
    share_ref[:, :latent] = dot(grid_columns_ref[...], slot_ref[...]).astype(BF16)
    share_ref[:, latent:] = dot(mesh_columns_ref[...], recv_ref[...]).astype(BF16)
    halve(share_ref, keep_ref, give_ref)
    own = pl.ds(pl.multiple_of(me * listed, listed), listed)
    own_slot_ref[...] = slot_ref[own, :]


def results_kernel(
    turned_ref, pick_ref, own_slot_ref, first_ref, normed_ref, grid_grad_ref, mesh_out_ref
):
    mesh_count = mesh_out_ref.shape[1]
    me = lax.axis_index("space")
    own = pl.ds(pl.multiple_of(me * mesh_count, mesh_count), mesh_count)
    mesh_out_ref[0] = (first_ref[own, :].astype(F32) + normed_ref[own, :]).astype(BF16)
    lists, _, capacity = pick_ref.shape
    latent = own_slot_ref.shape[1]
    returned = dot(own_slot_ref[...], turned_ref[:, :latent]).astype(BF16)
    total = None
    for i in range(lists):
        owner = one_hot(pick_ref[i], grid_grad_ref.shape[1])
        part = dot(owner, returned[i * capacity : (i + 1) * capacity])
        total = part if total is None else total + part
    grid_grad_ref[0] = total.astype(BF16)


def place(pairs, stages, semaphores):
    copies = []
    for n, (block_ref, target) in enumerate(pairs):
        stages[n][...] = block_ref[...].astype(F32)
        copies.append(pltpu.make_async_copy(stages[n], target, semaphores.at[n]))
        copies[n].start()
    for copy in copies:
        copy.wait()


def half_rows(half):
    core = lax.bitwise_and(lax.axis_index("rep"), 1)
    mine = pl.ds(pl.multiple_of(core * half, half), half)
    return mine, pl.ds(pl.multiple_of((1 - core) * half, half), half)


def settle_kernel(one_ref, two_ref, other_two_ref, weight_grad_ref, *scratch):
    half, width = one_ref.shape
    mine, other = half_rows(half)
    place(
        [
            (two_ref, weight_grad_ref.at[mine, width:]),
            (other_two_ref, weight_grad_ref.at[other, width:]),
            (one_ref, weight_grad_ref.at[mine, :width]),
        ],
        scratch[:3],
        scratch[3],
    )


def finish_kernel(other_one_ref, settled_ref, weight_grad_ref, stage, semaphores):
    half, width = other_one_ref.shape
    _, other = half_rows(half)
    place([(other_one_ref, weight_grad_ref.at[other, :width])], [stage], semaphores)


VMEM = pl.BlockSpec(memory_space=pltpu.VMEM)


def call(kernel, operands, outputs, scratch, flops, fetched=0):
    hbm = pl.BlockSpec(memory_space=pltpu.HBM)
    operands = [
        pltpu.with_memory_space_constraint(operand, pltpu.HBM) if n < fetched else operand
        for n, operand in enumerate(operands)
    ]
    return pl.pallas_call(
        kernel,
        out_shape=[jax.ShapeDtypeStruct(shape, kind) for shape, kind in outputs],
        in_specs=[hbm] * fetched + [VMEM] * (len(operands) - fetched),
        out_specs=[VMEM] * len(outputs),
        scratch_shapes=[pltpu.VMEM(shape, kind) for shape, kind in scratch]
        + ([pltpu.SemaphoreType.DMA((fetched,))] if fetched else []),
        compiler_params=pltpu.CompilerParams(vmem_limit_bytes=40 << 20),
        cost_estimate=pl.CostEstimate(flops=flops, bytes_accessed=4 << 20, transcendentals=0),
    )(*operands)


def swap(block, axis, bits):
    return lax.ppermute(block, axis, [(i, i ^ bits) for i in range(lax.axis_size(axis))])


def added(left, right):
    return (left.astype(F32) + right.astype(F32)).astype(BF16)


def summed_over_chips(half):
    bit = 2
    while bit < lax.axis_size("rep"):
        half = added(half, swap(half, "rep", bit))
        bit *= 2
    return half


def whole_sample_body(
    grid_latent,
    mesh_latent,
    mesh_cotangent,
    weights,
    g2m_pick,
    g2m_sender,
    g2m_receiver,
    m2m_pick,
    m2m_sender,
    m2m_receiver,
):
    regions = lax.axis_size("space")
    latent = weights.shape[0]
    listed = g2m_pick.shape[1] * g2m_pick.shape[2]
    mesh_count = mesh_latent.shape[1]
    mesh_cap = m2m_pick.shape[2]
    edges = g2m_sender.shape[0]
    columns = latent // regions
    half = columns // 2
    g2m_pick = g2m_pick.transpose(1, 0, 2)
    sources = (
        grid_latent,
        mesh_latent,
        g2m_pick,
        g2m_sender.reshape(1, -1),
        g2m_receiver.reshape(1, -1),
        m2m_pick,
        m2m_sender.reshape(1, -1),
        m2m_receiver.reshape(1, -1),
    )
    packed = call(
        pack_kernel,
        sources,
        [((listed + mesh_count + INDEX_ROWS, latent), BF16)],
        [((INDEX_ROWS, latent), F32)] + [(source.shape, source.dtype) for source in sources],
        10**7,
        fetched=len(sources),
    )[0]
    packed, cotangent, weights = lax.optimization_barrier((packed, mesh_cotangent, weights))
    steps = (0, *range(2, regions), 1)
    packs = [packed] + [swap(packed, "space", step) for step in steps[1:]]
    near = swap(cotangent, "space", 1)
    weights, turned = call(
        weights_kernel,
        (weights,),
        [(weights.shape, BF16), ((latent, 3 * latent), BF16)],
        [],
        10**8,
        fetched=1,
    )
    turned, cotangent = lax.optimization_barrier((turned, cotangent))
    cotangents = [cotangent] + [swap(cotangent, "space", step) for step in steps[1:-1]] + [near]
    rows = regions * mesh_count
    slots = regions * mesh_cap
    (
        grid_all,
        mesh_all,
        mesh_first,
        mesh_sent,
        hot_one,
        hot_two,
        turned_one,
        turned_two,
        hot_sent,
        slope_one,
        slope_two,
        normed_one,
        scaled_one,
        normed_two,
        scaled_two,
    ) = call(
        functools.partial(forward_kernel, steps, listed, mesh_count, mesh_cap),
        (*packs, weights),
        [
            ((regions * listed, latent), BF16),
            ((rows, latent), BF16),
            ((rows, latent), BF16),
            ((regions * slots, latent), BF16),
            ((regions * (listed + mesh_count), edges), BF16),
            ((regions * (slots + mesh_count), edges), BF16),
            ((regions * edges, listed + mesh_count), BF16),
            ((regions * edges, slots + mesh_count), BF16),
            ((rows, slots), BF16),
            ((regions * edges, latent), BF16),
            ((regions * edges, latent), BF16),
            ((rows, latent), F32),
            ((rows, 128), F32),
            ((rows, latent), F32),
            ((rows, 128), F32),
        ],
        [
            ((regions * INDEX_ROWS, latent), F32),
            ((regions * edges, latent), BF16),
            ((rows, latent), F32),
        ],
        2 * 10**9,
    )
    by_step = dict(zip(steps, cotangents))
    near, far = (0, 1), tuple(step for step in steps if step > 1)
    count = slots + mesh_count
    near_sums, grid_columns, mesh_columns, sent_columns, first_columns = call(
        functools.partial(near_back_kernel, near),
        (
            *(by_step[step] for step in near),
            hot_two,
            turned_two,
            slope_two,
            normed_two,
            scaled_two,
            grid_all,
            mesh_all,
            mesh_sent,
            mesh_first,
        ),
        [
            ((len(near) * count, latent), F32),
            ((columns, regions * listed), BF16),
            ((columns, rows), BF16),
            ((columns, regions * slots), BF16),
            ((columns, rows), BF16),
        ],
        [((len(near) * mesh_count, latent), BF16), ((len(near) * edges, latent), BF16)],
        10**9,
    )
    mesh_grad, keep_two, give_two = call(
        functools.partial(far_back_kernel, near, far, mesh_cap),
        (
            *(by_step[step] for step in near + far),
            turned,
            first_columns,
            sent_columns,
            near_sums,
            hot_two,
            turned_two,
            hot_sent,
            slope_two,
            normed_two,
            scaled_two,
        ),
        [((rows, latent), F32)] + [((half, 2 * latent), BF16)] * 2,
        [
            ((rows, latent), F32),
            ((regions * slots, latent), F32),
            ((rows, latent), BF16),
            ((columns, 2 * latent), BF16),
            ((len(far) * mesh_count, latent), BF16),
            ((len(far) * edges, latent), BF16),
        ],
        10**9,
    )
    own_slots, keep_one, give_one = call(
        functools.partial(encode_back_kernel, regions),
        (
            grid_columns,
            mesh_columns,
            hot_one,
            turned_one,
            slope_one,
            normed_one,
            scaled_one,
            mesh_grad,
        ),
        [((listed, latent), BF16)] + [((half, 2 * latent), BF16)] * 2,
        [
            ((regions * listed, latent), BF16),
            ((rows, latent), BF16),
            ((columns, 2 * latent), BF16),
            ((rows, latent), BF16),
            ((regions * edges, latent), BF16),
        ],
        10**9,
    )
    half_one = added(keep_one, swap(give_one, "rep", 1))
    half_two = added(keep_two, swap(give_two, "rep", 1))
    half_one, own_slots = lax.optimization_barrier((half_one, own_slots))
    grid_grad, mesh_out = call(
        results_kernel,
        (turned, g2m_pick, own_slots, mesh_first, normed_two),
        [(grid_latent.shape, BF16), (mesh_latent.shape, BF16)],
        [],
        10**8,
    )
    two = summed_over_chips(half_two)
    one, grid_grad = lax.optimization_barrier((summed_over_chips(half_one), grid_grad))
    hbm = pl.BlockSpec(memory_space=pltpu.HBM)
    stage = pltpu.VMEM((half, 2 * latent), F32)
    weight_shape = pltpu.HBM((columns, 4 * latent), F32)
    limit = pltpu.CompilerParams(vmem_limit_bytes=40 << 20)
    settled = pl.pallas_call(
        settle_kernel,
        out_shape=weight_shape,
        in_specs=[VMEM] * 3,
        out_specs=hbm,
        scratch_shapes=[stage] * 3 + [pltpu.SemaphoreType.DMA((3,))],
        compiler_params=limit,
    )(one, two, swap(two, "rep", 1))
    weight_grad = pl.pallas_call(
        finish_kernel,
        out_shape=weight_shape,
        in_specs=[VMEM, hbm],
        out_specs=hbm,
        scratch_shapes=[stage, pltpu.SemaphoreType.DMA((1,))],
        input_output_aliases={1: 0},
        compiler_params=limit,
    )(swap(one, "rep", 1), settled)
    return (mesh_out, grid_grad, weight_grad)


def solution(mesh):
    regions = mesh.shape["space"]
    samples = mesh.shape["rep"]

    def whole(*arguments):
        edges = arguments[5].shape[0] + arguments[8].shape[0]
        latent = arguments[3].shape[0]
        fits = edges * latent * 4 <= SAMPLE_EDGE_BYTES and latent % (128 * regions) == 0
        paired = regions > 2 and samples > 1 and not (regions & (regions - 1) | samples & (samples - 1))
        return sharded(whole_sample_body if fits and paired else partitioned_body)(*arguments)

    def sharded(body):
        return jax.shard_map(
            body,
            mesh=mesh,
            in_specs=(
                P(("groups", "rep"), "space", None),
                P(("groups", "rep"), "space", None),
                P(("groups", "rep"), "space", None),
                P(),
                P("space", None, None),
                P("space"),
                P("space"),
                P("space", None, None),
                P("space"),
                P("space"),
            ),
            out_specs=(
                P(("groups", "rep"), "space", None),
                P(("groups", "rep"), "space", None),
                P(("groups", "space"), None),
            ),
            check_vma=False,
        )

    return whole
```

```python
import functools

import jax
import jax.numpy as jnp
from jax import lax
from jax.experimental import pallas as pl
from jax.experimental.pallas import tpu as pltpu
from jax.sharding import PartitionSpec as P

EPSILON = 1e-05


def with_halo(cells, sides, width):
    for axis, dim in sides:
        count = lax.axis_size(axis)
        ends = count - 1
        head = lax.slice_in_dim(cells, 0, width, axis=dim)
        tail = lax.slice_in_dim(cells, cells.shape[dim] - width, cells.shape[dim], axis=dim)
        cells = jnp.concatenate(
            [
                lax.ppermute(tail, axis, [(i, (i + 1) % count) for i in range(ends)]),
                cells,
                lax.ppermute(head, axis, [((i + 1) % count, i) for i in range(ends)]),
            ],
            axis=dim,
        )
    return cells


def swish(values):
    return values * jax.nn.sigmoid(values)


def swish_slope(values):
    squash = jax.nn.sigmoid(values)
    return squash * (1.0 + values * (1.0 - squash))


def norm_rows(values):
    centred = values - jnp.mean(values, -1, keepdims=True)
    return centred * lax.rsqrt(jnp.mean(centred * centred, -1, keepdims=True) + EPSILON)


def norm_rows_back(values, upstream):
    centred = values - jnp.mean(values, -1, keepdims=True)
    scaled = lax.rsqrt(jnp.mean(centred * centred, -1, keepdims=True) + EPSILON)
    normed = centred * scaled
    return scaled * (
        upstream
        - jnp.mean(upstream, -1, keepdims=True)
        - normed * jnp.mean(upstream * normed, -1, keepdims=True)
    )


def slot_rows(pick_row):
    listed = pick_row.reshape(-1)
    return listed


def mesh_route(outgoing, capacity, peer_count):
    columns = outgoing.shape[1]
    pieces = lax.all_to_all(
        outgoing.reshape(peer_count, capacity, columns),
        "space",
        split_axis=0,
        concat_axis=0,
        tiled=True,
    )
    arrived = pieces.reshape(peer_count * capacity, columns)
    return arrived


def grid_route(outgoing, capacity):
    columns = outgoing.shape[1]
    lists = outgoing.reshape(3, capacity, columns)
    rims = with_halo(jnp.stack([lists[0], lists[2]]), (("space", 0),), 1)
    return jnp.concatenate([rims[0], lists[1], rims[3]], axis=0)


def edge_pass(arrived, recv_table, located, receiver, w_send, w_recv):
    recv_proj = jnp.dot(recv_table, w_recv, preferred_element_type=jnp.float32)
    slot_proj = jnp.dot(arrived, w_send, preferred_element_type=jnp.float32)
    activation = slot_proj[located] + recv_proj[receiver]
    message = swish(activation).astype(jnp.bfloat16)
    member = (
        receiver[None, :] == jnp.arange(recv_table.shape[0], dtype=jnp.int32)[:, None]
    ).astype(jnp.bfloat16)
    summed = jnp.dot(member, message, preferred_element_type=jnp.float32)
    return (activation, member, summed)


def backward_pass(slot_count, located, activation, member, receiver, agg_grad, w_send):
    edge_grad = (agg_grad[receiver] * swish_slope(activation)).astype(jnp.bfloat16)
    recv_sum = jnp.dot(member, edge_grad, preferred_element_type=jnp.float32).astype(jnp.bfloat16)
    slot_member = (located[None, :] == jnp.arange(slot_count, dtype=jnp.int32)[:, None]).astype(
        jnp.bfloat16
    )
    slot_sum = jnp.dot(slot_member, edge_grad, preferred_element_type=jnp.float32).astype(
        jnp.bfloat16
    )
    returned = jnp.dot(slot_sum, w_send.T, preferred_element_type=jnp.float32).astype(jnp.bfloat16)
    return (recv_sum, slot_sum, returned)


def gather_back(listed, back_rows, row_count):
    owner = (listed[None, :] == jnp.arange(row_count, dtype=jnp.int32)[:, None]).astype(
        jnp.bfloat16
    )
    return jnp.dot(owner, back_rows, preferred_element_type=jnp.float32)


def partitioned_body(
    grid_latent,
    mesh_latent,
    mesh_cotangent,
    weights,
    g2m_pick,
    g2m_sender,
    g2m_receiver,
    m2m_pick,
    m2m_sender,
    m2m_receiver,
):
    grid_rows = grid_latent[0]
    mesh_rows = mesh_latent[0]
    upstream = mesh_cotangent[0].astype(jnp.float32)
    latent = weights.shape[0]
    encode_sender = weights[:, :latent]
    encode_receiver = weights[:, latent : 2 * latent]
    process_sender = weights[:, 2 * latent : 3 * latent]
    process_receiver = weights[:, 3 * latent :]
    peer_count = lax.axis_size("space")
    grid_cap = g2m_pick.shape[2]
    mesh_cap = m2m_pick.shape[2]
    grid_listed = g2m_pick[0].reshape(-1)
    grid_arrived = grid_route(grid_rows[grid_listed], grid_cap)
    act_first, member_first, summed_first = edge_pass(
        grid_arrived, mesh_rows, g2m_sender, g2m_receiver, encode_sender, encode_receiver
    )
    mesh_first = (mesh_rows.astype(jnp.float32) + norm_rows(summed_first)).astype(jnp.bfloat16)
    mesh_listed = slot_rows(m2m_pick[0])
    mesh_arrived = mesh_route(mesh_first[mesh_listed], mesh_cap, peer_count)
    act_second, member_second, summed_second = edge_pass(
        mesh_arrived, mesh_first, m2m_sender, m2m_receiver, process_sender, process_receiver
    )
    mesh_final = (mesh_first.astype(jnp.float32) + norm_rows(summed_second)).astype(jnp.bfloat16)
    agg_second = norm_rows_back(summed_second, upstream)
    recv_second, slot_second, returned_second = backward_pass(
        mesh_arrived.shape[0],
        m2m_sender,
        act_second,
        member_second,
        m2m_receiver,
        agg_second,
        process_sender,
    )
    back_second = mesh_route(returned_second, mesh_cap, peer_count)
    mesh_grad = upstream + jnp.dot(
        recv_second, process_receiver.T, preferred_element_type=jnp.float32
    )
    mesh_grad = mesh_grad + gather_back(mesh_listed, back_second, mesh_rows.shape[0])
    agg_first = norm_rows_back(summed_first, mesh_grad)
    recv_first, slot_first, returned_first = backward_pass(
        grid_arrived.shape[0],
        g2m_sender,
        act_first,
        member_first,
        g2m_receiver,
        agg_first,
        encode_sender,
    )
    back_first = grid_route(returned_first, grid_cap)
    grid_grad = gather_back(grid_listed, back_first, grid_rows.shape[0]).astype(jnp.bfloat16)
    factor_pairs = (
        (grid_arrived, slot_first),
        (mesh_rows, recv_first),
        (mesh_arrived, slot_second),
        (mesh_first, recv_second),
    )
    blocks = []
    for first_factor, second_factor in factor_pairs:
        blocks.append(
            lax.dot_general(
                first_factor,
                second_factor,
                (((0,), (0,)), ((), ())),
                preferred_element_type=jnp.float32,
            )
        )
    shares = lax.psum_scatter(
        jnp.concatenate(blocks, axis=1).astype(jnp.bfloat16),
        "space",
        scatter_dimension=0,
        tiled=True,
    )
    weight_grad = lax.psum(shares, "rep").astype(jnp.float32)
    return (mesh_final[None], grid_grad[None], weight_grad)


F32 = jnp.float32
BF16 = jnp.bfloat16
INDEX_ROWS = 8
SAMPLE_EDGE_BYTES = 8 << 20


def dot(left, right):
    return jnp.dot(left, right, preferred_element_type=F32)


def dot_first(left, right):
    return lax.dot_general(left, right, (((0,), (0,)), ((), ())), preferred_element_type=F32)


def one_hot(labels, count):
    rows = lax.broadcasted_iota(jnp.int32, (count, labels.shape[-1]), 0)
    return (rows == labels).astype(F32).astype(BF16)


def row_moments(values):
    centred = values - jnp.mean(values, -1, keepdims=True)
    return centred, lax.rsqrt(jnp.mean(centred * centred, -1, keepdims=True) + EPSILON)


def moments_back(normed, scaled, upstream):
    return scaled * (
        upstream
        - jnp.mean(upstream, -1, keepdims=True)
        - normed * jnp.mean(upstream * normed, -1, keepdims=True)
    )


def fetch(pairs, semaphores):
    copies = [
        pltpu.make_async_copy(source, target, semaphores.at[n])
        for n, (source, target) in enumerate(pairs)
    ]
    for copy in copies:
        copy.start()
    for copy in copies:
        copy.wait()


def pack_kernel(*refs):
    sources, packed_ref, index_ref = refs[:8], refs[8], refs[9]
    local, semaphores = refs[10:18], refs[18]
    fetch(list(zip(sources, local)), semaphores)
    (
        grid_ref,
        mesh_ref,
        g2m_pick_ref,
        g2m_sender_ref,
        g2m_receiver_ref,
        m2m_pick_ref,
        m2m_sender_ref,
        m2m_receiver_ref,
    ) = local
    lists, _, capacity = g2m_pick_ref.shape
    mesh_count = mesh_ref.shape[1]
    regions, mesh_cap = m2m_pick_ref.shape[1:]
    edges = g2m_sender_ref.shape[1]
    grid_rows = grid_ref[0]
    for i in range(lists):
        picked = one_hot(g2m_pick_ref[i], grid_rows.shape[0])
        packed_ref[i * capacity : (i + 1) * capacity, :] = dot_first(picked, grid_rows).astype(BF16)
    first = lists * capacity
    packed_ref[first : first + mesh_count, :] = mesh_ref[0]
    index_ref[...] = jnp.zeros_like(index_ref)
    index_ref[0:1, 0:edges] = g2m_sender_ref[...].astype(F32)
    index_ref[0:1, edges : 2 * edges] = g2m_receiver_ref[...].astype(F32)
    index_ref[1:2, 0:edges] = m2m_sender_ref[...].astype(F32)
    index_ref[1:2, edges : 2 * edges] = m2m_receiver_ref[...].astype(F32)
    slots = regions * mesh_cap
    lane = lax.broadcasted_iota(jnp.int32, (mesh_cap, slots), 1)
    spread = (lane % mesh_cap == lax.broadcasted_iota(jnp.int32, (mesh_cap, slots), 0)).astype(F32)
    spread = dot(m2m_pick_ref[0].astype(F32).astype(BF16), spread.astype(BF16))
    lane = lax.broadcasted_iota(jnp.int32, (regions, slots), 1)
    owned = lane // mesh_cap == lax.broadcasted_iota(jnp.int32, (regions, slots), 0)
    index_ref[2:3, 0:slots] = jnp.sum(jnp.where(owned, spread, 0.0), 0, keepdims=True)
    packed_ref[first + mesh_count :, :] = index_ref[...].astype(BF16)


def weights_kernel(source_ref, weights_ref, turned_ref, semaphores):
    fetch([(source_ref, weights_ref)], semaphores)
    latent = weights_ref.shape[0]
    for n, block in enumerate((0, 2, 3)):
        turned_ref[:, n * latent : (n + 1) * latent] = weights_ref[
            :, block * latent : (block + 1) * latent
        ].T


def edge_blocks(edges, size):
    size = min(edges, size)
    return [(first, min(size, edges - first)) for first in range(0, edges, size)]


def edge_forward(tables, hot_ref, turned_hot_ref, slope_ref, message_ref, mesh_count):
    regions = len(tables)
    edges = slope_ref.shape[0] // regions
    count = hot_ref.shape[0] // regions
    work = [(d, first, size) for d in range(regions) for first, size in edge_blocks(edges, 256)]

    def gathered(d, first, size):
        rows = slice(d * edges + first, d * edges + first + size)
        return dot(turned_hot_ref[rows, :], tables[d])

    sums = []
    activation = gathered(*work[0])
    for n, (d, first, size) in enumerate(work):
        coming = gathered(*work[n + 1]) if n + 1 < len(work) else None
        activation = activation.astype(BF16)
        squash = 0.5 + 0.5 * jnp.tanh(0.5 * activation)
        message = activation * squash
        rows = slice(d * edges + first, d * edges + first + size)
        slope_ref[rows, :] = squash + message * (1.0 - squash)
        message_ref[rows, :] = message
        activation = coming
        if first + size == edges:
            hot = hot_ref[(d + 1) * count - mesh_count : (d + 1) * count, :]
            sums.append(dot(hot, message_ref[d * edges : (d + 1) * edges, :]))
    return sums


def forward_kernel(
    steps,
    listed,
    mesh_count,
    mesh_cap,
    *refs,
):
    regions = len(steps)
    packed_refs = refs[:regions]
    (
        weights_ref,
        grid_ref,
        mesh_ref,
        first_ref,
        sent_ref,
        hot_one_ref,
        hot_two_ref,
        turned_one_ref,
        turned_two_ref,
        hot_sent_ref,
        slope_one_ref,
        slope_two_ref,
        normed_one_ref,
        scaled_one_ref,
        normed_two_ref,
        scaled_two_ref,
        index_ref,
        message_ref,
        sum_ref,
    ) = refs[regions:]
    latent = weights_ref.shape[0]
    edges = slope_one_ref.shape[0] // regions
    capacity = listed // 3
    slots = regions * mesh_cap
    me = lax.axis_index("space")
    for step, packed_ref in zip(steps, packed_refs):
        region = lax.bitwise_xor(me, step)
        at = lambda rows: pl.ds(pl.multiple_of(region * rows, rows), rows)
        grid_ref[at(listed), :] = packed_ref[:listed, :]
        mesh_ref[at(mesh_count), :] = packed_ref[listed : listed + mesh_count, :]
        index_ref[at(INDEX_ROWS), :] = packed_ref[listed + mesh_count :, :].astype(F32)

    grid_proj = dot(grid_ref[...], weights_ref[:, :latent])
    mesh_proj = dot(mesh_ref[...], weights_ref[:, latent : 2 * latent])
    for d in range(regions):
        index = index_ref[d * INDEX_ROWS : (d + 1) * INDEX_ROWS, :].astype(jnp.int32)
        for row, senders, hot_ref, turned_ref in (
            (0, listed, hot_one_ref, turned_one_ref),
            (1, slots, hot_two_ref, turned_two_ref),
        ):
            count = senders + mesh_count
            hot = jnp.concatenate(
                [
                    one_hot(index[row : row + 1, :edges], senders),
                    one_hot(index[row : row + 1, edges:], mesh_count),
                ],
                axis=0,
            )
            hot_ref[d * count : (d + 1) * count, :] = hot
            turned_ref[d * edges : (d + 1) * edges, :] = hot.T
        hot_sent_ref[d * mesh_count : (d + 1) * mesh_count, :] = one_hot(
            index[2:3, :slots], mesh_count
        )

    blank = jnp.zeros((capacity, latent), F32)
    tables = []
    for d in range(regions):
        before = (d - 1) * listed + 2 * capacity
        within = d * listed + capacity
        after = (d + 1) * listed
        tables.append(
            jnp.concatenate(
                [
                    grid_proj[before : before + capacity] if d > 0 else blank,
                    grid_proj[within : within + capacity],
                    grid_proj[after : after + capacity] if d < regions - 1 else blank,
                    mesh_proj[d * mesh_count : (d + 1) * mesh_count],
                ],
                axis=0,
            ).astype(BF16)
        )
    sums = edge_forward(
        tables, hot_one_ref, turned_one_ref, slope_one_ref, message_ref, mesh_count
    )
    for d in range(regions):
        sum_ref[d * mesh_count : (d + 1) * mesh_count, :] = sums[d]
    centred, scaled = row_moments(sum_ref[...])
    normed = centred * scaled
    normed_one_ref[...] = normed
    scaled_one_ref[...] = jnp.broadcast_to(scaled, scaled_one_ref.shape)
    first_ref[...] = (mesh_ref[...].astype(F32) + normed).astype(BF16)

    for s in range(regions):
        rows = slice(s * mesh_count, (s + 1) * mesh_count)
        sent_ref[s * slots : (s + 1) * slots, :] = dot_first(
            hot_sent_ref[rows, :], first_ref[rows, :]
        ).astype(BF16)
    sent_proj = dot(sent_ref[...], weights_ref[:, 2 * latent : 3 * latent])
    first_proj = dot(first_ref[...], weights_ref[:, 3 * latent :])
    tables = []
    for d in range(regions):
        pieces = [
            sent_proj[s * slots + d * mesh_cap : s * slots + (d + 1) * mesh_cap]
            for s in range(regions)
        ]
        tables.append(
            jnp.concatenate(
                pieces + [first_proj[d * mesh_count : (d + 1) * mesh_count]], axis=0
            ).astype(BF16)
        )
    sums = edge_forward(
        tables, hot_two_ref, turned_two_ref, slope_two_ref, message_ref, mesh_count
    )
    for d in range(regions):
        sum_ref[d * mesh_count : (d + 1) * mesh_count, :] = sums[d]
    centred, scaled = row_moments(sum_ref[...])
    normed_two_ref[...] = centred * scaled
    scaled_two_ref[...] = jnp.broadcast_to(scaled, scaled_two_ref.shape)


def edge_backward(regions, agg_grad_ref, hot_ref, turned_hot_ref, slope_ref, edge_grad_ref):
    mesh_count = agg_grad_ref.shape[0] // len(regions)
    edges = edge_grad_ref.shape[0] // len(regions)
    count = turned_hot_ref.shape[1]
    blank = jnp.zeros((count - mesh_count, agg_grad_ref.shape[1]), BF16)
    work = [(n, first, size) for n in range(len(regions)) for first, size in edge_blocks(edges, 256)]

    def at(n, first, size):
        return pl.ds(pl.multiple_of(regions[n] * edges + first, size), size)

    def gathered(n, first, size):
        own = agg_grad_ref[n * mesh_count : (n + 1) * mesh_count, :]
        return dot(turned_hot_ref[at(n, first, size), :], jnp.concatenate([blank, own], axis=0))

    sums = []
    upstream = gathered(*work[0])
    for k, (n, first, size) in enumerate(work):
        coming = gathered(*work[k + 1]) if k + 1 < len(work) else None
        rows = slice(n * edges + first, n * edges + first + size)
        edge_grad_ref[rows, :] = upstream.astype(BF16) * slope_ref[at(n, first, size), :]
        upstream = coming
        if first + size == edges:
            hot = hot_ref[pl.ds(pl.multiple_of(regions[n] * count, count), count), :]
            sums.append(dot(hot, edge_grad_ref[n * edges : (n + 1) * edges, :]))
    return sums


def halve(share_ref, keep_ref, give_ref):
    half = keep_ref.shape[0]
    core = lax.bitwise_and(lax.axis_index("rep"), 1)
    keep_ref[...] = share_ref[pl.ds(pl.multiple_of(core * half, half), half), :]
    give_ref[...] = share_ref[pl.ds(pl.multiple_of((1 - core) * half, half), half), :]


def process_back_part(
    steps, mesh_count, cotangent_refs, hot_ref, turned_hot_ref, slope_ref, normed_ref, scaled_ref,
    agg_grad_ref, edge_grad_ref,
):
    me = lax.axis_index("space")
    regions = [lax.bitwise_xor(me, step) for step in steps]
    for n, (region, cotangent_ref) in enumerate(zip(regions, cotangent_refs)):
        rows = pl.ds(pl.multiple_of(region * mesh_count, mesh_count), mesh_count)
        agg_grad_ref[n * mesh_count : (n + 1) * mesh_count, :] = moments_back(
            normed_ref[rows, :], scaled_ref[rows, 0:1], cotangent_ref[0].astype(F32)
        ).astype(BF16)
    return regions, edge_backward(
        regions, agg_grad_ref, hot_ref, turned_hot_ref, slope_ref, edge_grad_ref
    )


def near_back_kernel(steps, *refs):
    cotangent_refs, refs = refs[: len(steps)], refs[len(steps) :]
    (
        hot_ref,
        turned_hot_ref,
        slope_ref,
        normed_ref,
        scaled_ref,
        *whole_refs,
    ) = refs[:9]
    sums_ref, *column_refs = refs[9:14]
    agg_grad_ref, edge_grad_ref = refs[14:]
    mesh_count = agg_grad_ref.shape[0] // len(steps)
    count = turned_hot_ref.shape[1]
    _, all_sums = process_back_part(
        steps, mesh_count, cotangent_refs, hot_ref, turned_hot_ref, slope_ref, normed_ref,
        scaled_ref, agg_grad_ref, edge_grad_ref,
    )
    for n, sums in enumerate(all_sums):
        sums_ref[n * count : (n + 1) * count, :] = sums
    columns = column_refs[0].shape[0]
    mine = pl.ds(pl.multiple_of(lax.axis_index("space") * columns, columns), columns)
    for whole_ref, column_ref in zip(whole_refs, column_refs):
        column_ref[...] = whole_ref[:, mine].T


def far_back_kernel(near, far, mesh_cap, *refs):
    regions = len(near) + len(far)
    cotangent_refs, refs = refs[:regions], refs[regions:]
    (
        turned_ref,
        first_columns_ref,
        sent_columns_ref,
        near_sums_ref,
        hot_ref,
        turned_hot_ref,
        hot_sent_ref,
        slope_ref,
        normed_ref,
        scaled_ref,
        mesh_grad_ref,
        keep_ref,
        give_ref,
        upstream_ref,
        slot_ref,
        recv_ref,
        share_ref,
        agg_grad_ref,
        edge_grad_ref,
    ) = refs
    latent = normed_ref.shape[1]
    mesh_count = normed_ref.shape[0] // regions
    count = turned_hot_ref.shape[1]
    slots = regions * mesh_cap
    me = lax.axis_index("space")
    far_regions, all_sums = process_back_part(
        far, mesh_count, cotangent_refs[len(near) :], hot_ref, turned_hot_ref, slope_ref,
        normed_ref, scaled_ref, agg_grad_ref, edge_grad_ref,
    )
    near_regions = [lax.bitwise_xor(me, step) for step in near]
    near_sums = [near_sums_ref[n * count : (n + 1) * count, :] for n in range(len(near))]
    for region, sums in zip(near_regions + far_regions, near_sums + all_sums):
        for s in range(regions):
            slot_ref[pl.ds(pl.multiple_of(s * slots + region * mesh_cap, mesh_cap), mesh_cap), :] = (
                sums[s * mesh_cap : (s + 1) * mesh_cap]
            )
        recv_ref[pl.ds(pl.multiple_of(region * mesh_count, mesh_count), mesh_count), :] = sums[
            slots:
        ].astype(BF16)
    for region, cotangent_ref in zip(near_regions + far_regions, cotangent_refs):
        rows = pl.ds(pl.multiple_of(region * mesh_count, mesh_count), mesh_count)
        upstream_ref[rows, :] = cotangent_ref[0].astype(F32)
    slot_sum = slot_ref[...].astype(BF16)
    share_ref[:, :latent] = dot(sent_columns_ref[...], slot_sum).astype(BF16)
    share_ref[:, latent:] = dot(first_columns_ref[...], recv_ref[...]).astype(BF16)
    halve(share_ref, keep_ref, give_ref)
    returned = dot(slot_sum, turned_ref[:, latent : 2 * latent]).astype(BF16)
    grad = upstream_ref[...] + dot(recv_ref[...], turned_ref[:, 2 * latent :])
    for s in range(regions):
        rows = slice(s * mesh_count, (s + 1) * mesh_count)
        mesh_grad_ref[rows, :] = grad[rows] + dot(
            hot_sent_ref[rows, :], returned[s * slots : (s + 1) * slots]
        )


def encode_back_kernel(
    regions,
    grid_columns_ref,
    mesh_columns_ref,
    hot_ref,
    turned_hot_ref,
    slope_ref,
    normed_ref,
    scaled_ref,
    mesh_grad_ref,
    own_slot_ref,
    keep_ref,
    give_ref,
    slot_ref,
    recv_ref,
    share_ref,
    agg_grad_ref,
    edge_grad_ref,
):
    latent = normed_ref.shape[1]
    mesh_count = normed_ref.shape[0] // regions
    listed = slot_ref.shape[0] // regions
    capacity = listed // 3
    me = lax.axis_index("space")
    agg_grad_ref[...] = moments_back(
        normed_ref[...], scaled_ref[:, 0:1], mesh_grad_ref[...]
    ).astype(BF16)
    blank = jnp.zeros((capacity, latent), BF16)
    slot_ref[0:capacity, :] = blank
    slot_ref[regions * listed - capacity :, :] = blank
    all_sums = edge_backward(
        range(regions), agg_grad_ref, hot_ref, turned_hot_ref, slope_ref, edge_grad_ref
    )
    for d, sums in enumerate(all_sums):
        sums = sums.astype(BF16)
        for j in range(3):
            source = d + j - 1
            if 0 <= source < regions:
                first = source * listed + (2 - j) * capacity
                slot_ref[first : first + capacity, :] = sums[j * capacity : (j + 1) * capacity]
        recv_ref[d * mesh_count : (d + 1) * mesh_count, :] = sums[listed:]
    share_ref[:, :latent] = dot(grid_columns_ref[...], slot_ref[...]).astype(BF16)
    share_ref[:, latent:] = dot(mesh_columns_ref[...], recv_ref[...]).astype(BF16)
    halve(share_ref, keep_ref, give_ref)
    own = pl.ds(pl.multiple_of(me * listed, listed), listed)
    own_slot_ref[...] = slot_ref[own, :]


def results_kernel(
    turned_ref, pick_ref, own_slot_ref, first_ref, normed_ref, grid_grad_ref, mesh_out_ref
):
    mesh_count = mesh_out_ref.shape[1]
    me = lax.axis_index("space")
    own = pl.ds(pl.multiple_of(me * mesh_count, mesh_count), mesh_count)
    mesh_out_ref[0] = (first_ref[own, :].astype(F32) + normed_ref[own, :]).astype(BF16)
    lists, _, capacity = pick_ref.shape
    latent = own_slot_ref.shape[1]
    returned = dot(own_slot_ref[...], turned_ref[:, :latent]).astype(BF16)
    total = None
    for i in range(lists):
        owner = one_hot(pick_ref[i], grid_grad_ref.shape[1])
        part = dot(owner, returned[i * capacity : (i + 1) * capacity])
        total = part if total is None else total + part
    grid_grad_ref[0] = total.astype(BF16)


def place(pairs, stages, semaphores):
    copies = []
    for n, (block_ref, target) in enumerate(pairs):
        stages[n][...] = block_ref[...].astype(F32)
        copies.append(pltpu.make_async_copy(stages[n], target, semaphores.at[n]))
        copies[n].start()
    for copy in copies:
        copy.wait()


def half_rows(half):
    core = lax.bitwise_and(lax.axis_index("rep"), 1)
    mine = pl.ds(pl.multiple_of(core * half, half), half)
    return mine, pl.ds(pl.multiple_of((1 - core) * half, half), half)


def settle_kernel(one_ref, two_ref, other_two_ref, weight_grad_ref, *scratch):
    half, width = one_ref.shape
    mine, other = half_rows(half)
    place(
        [
            (two_ref, weight_grad_ref.at[mine, width:]),
            (other_two_ref, weight_grad_ref.at[other, width:]),
            (one_ref, weight_grad_ref.at[mine, :width]),
        ],
        scratch[:3],
        scratch[3],
    )


def finish_kernel(other_one_ref, settled_ref, weight_grad_ref, stage, semaphores):
    half, width = other_one_ref.shape
    _, other = half_rows(half)
    place([(other_one_ref, weight_grad_ref.at[other, :width])], [stage], semaphores)


VMEM = pl.BlockSpec(memory_space=pltpu.VMEM)


def call(kernel, operands, outputs, scratch, flops, fetched=0):
    hbm = pl.BlockSpec(memory_space=pltpu.HBM)
    operands = [
        pltpu.with_memory_space_constraint(operand, pltpu.HBM) if n < fetched else operand
        for n, operand in enumerate(operands)
    ]
    return pl.pallas_call(
        kernel,
        out_shape=[jax.ShapeDtypeStruct(shape, kind) for shape, kind in outputs],
        in_specs=[hbm] * fetched + [VMEM] * (len(operands) - fetched),
        out_specs=[VMEM] * len(outputs),
        scratch_shapes=[pltpu.VMEM(shape, kind) for shape, kind in scratch]
        + ([pltpu.SemaphoreType.DMA((fetched,))] if fetched else []),
        compiler_params=pltpu.CompilerParams(vmem_limit_bytes=40 << 20),
        cost_estimate=pl.CostEstimate(flops=flops, bytes_accessed=4 << 20, transcendentals=0),
    )(*operands)


def swap(block, axis, bits):
    return lax.ppermute(block, axis, [(i, i ^ bits) for i in range(lax.axis_size(axis))])


def added(left, right):
    return (left.astype(F32) + right.astype(F32)).astype(BF16)


def summed_over_chips(half):
    bit = 2
    while bit < lax.axis_size("rep"):
        half = added(half, swap(half, "rep", bit))
        bit *= 2
    return half


def whole_sample_body(
    grid_latent,
    mesh_latent,
    mesh_cotangent,
    weights,
    g2m_pick,
    g2m_sender,
    g2m_receiver,
    m2m_pick,
    m2m_sender,
    m2m_receiver,
):
    regions = lax.axis_size("space")
    latent = weights.shape[0]
    listed = g2m_pick.shape[1] * g2m_pick.shape[2]
    mesh_count = mesh_latent.shape[1]
    mesh_cap = m2m_pick.shape[2]
    edges = g2m_sender.shape[0]
    columns = latent // regions
    half = columns // 2
    g2m_pick = g2m_pick.transpose(1, 0, 2)
    sources = (
        grid_latent,
        mesh_latent,
        g2m_pick,
        g2m_sender.reshape(1, -1),
        g2m_receiver.reshape(1, -1),
        m2m_pick,
        m2m_sender.reshape(1, -1),
        m2m_receiver.reshape(1, -1),
    )
    packed = call(
        pack_kernel,
        sources,
        [((listed + mesh_count + INDEX_ROWS, latent), BF16)],
        [((INDEX_ROWS, latent), F32)] + [(source.shape, source.dtype) for source in sources],
        10**7,
        fetched=len(sources),
    )[0]
    packed, cotangent, weights = lax.optimization_barrier((packed, mesh_cotangent, weights))
    steps = (0, *range(2, regions), 1)
    packs = [packed] + [swap(packed, "space", step) for step in steps[1:]]
    near = swap(cotangent, "space", 1)
    weights, turned = call(
        weights_kernel,
        (weights,),
        [(weights.shape, BF16), ((latent, 3 * latent), BF16)],
        [],
        10**8,
        fetched=1,
    )
    cotangents = [cotangent] + [swap(cotangent, "space", step) for step in steps[1:-1]] + [near]
    rows = regions * mesh_count
    slots = regions * mesh_cap
    (
        grid_all,
        mesh_all,
        mesh_first,
        mesh_sent,
        hot_one,
        hot_two,
        turned_one,
        turned_two,
        hot_sent,
        slope_one,
        slope_two,
        normed_one,
        scaled_one,
        normed_two,
        scaled_two,
    ) = call(
        functools.partial(forward_kernel, steps, listed, mesh_count, mesh_cap),
        (*packs, weights),
        [
            ((regions * listed, latent), BF16),
            ((rows, latent), BF16),
            ((rows, latent), BF16),
            ((regions * slots, latent), BF16),
            ((regions * (listed + mesh_count), edges), BF16),
            ((regions * (slots + mesh_count), edges), BF16),
            ((regions * edges, listed + mesh_count), BF16),
            ((regions * edges, slots + mesh_count), BF16),
            ((rows, slots), BF16),
            ((regions * edges, latent), BF16),
            ((regions * edges, latent), BF16),
            ((rows, latent), F32),
            ((rows, 128), F32),
            ((rows, latent), F32),
            ((rows, 128), F32),
        ],
        [
            ((regions * INDEX_ROWS, latent), F32),
            ((regions * edges, latent), BF16),
            ((rows, latent), F32),
        ],
        2 * 10**9,
    )
    by_step = dict(zip(steps, cotangents))
    near, far = (0, 1), tuple(step for step in steps if step > 1)
    count = slots + mesh_count
    near_sums, grid_columns, mesh_columns, sent_columns, first_columns = call(
        functools.partial(near_back_kernel, near),
        (
            *(by_step[step] for step in near),
            hot_two,
            turned_two,
            slope_two,
            normed_two,
            scaled_two,
            grid_all,
            mesh_all,
            mesh_sent,
            mesh_first,
        ),
        [
            ((len(near) * count, latent), F32),
            ((columns, regions * listed), BF16),
            ((columns, rows), BF16),
            ((columns, regions * slots), BF16),
            ((columns, rows), BF16),
        ],
        [((len(near) * mesh_count, latent), BF16), ((len(near) * edges, latent), BF16)],
        10**9,
    )
    mesh_grad, keep_two, give_two = call(
        functools.partial(far_back_kernel, near, far, mesh_cap),
        (
            *(by_step[step] for step in near + far),
            turned,
            first_columns,
            sent_columns,
            near_sums,
            hot_two,
            turned_two,
            hot_sent,
            slope_two,
            normed_two,
            scaled_two,
        ),
        [((rows, latent), F32)] + [((half, 2 * latent), BF16)] * 2,
        [
            ((rows, latent), F32),
            ((regions * slots, latent), F32),
            ((rows, latent), BF16),
            ((columns, 2 * latent), BF16),
            ((len(far) * mesh_count, latent), BF16),
            ((len(far) * edges, latent), BF16),
        ],
        10**9,
    )
    own_slots, keep_one, give_one = call(
        functools.partial(encode_back_kernel, regions),
        (
            grid_columns,
            mesh_columns,
            hot_one,
            turned_one,
            slope_one,
            normed_one,
            scaled_one,
            mesh_grad,
        ),
        [((listed, latent), BF16)] + [((half, 2 * latent), BF16)] * 2,
        [
            ((regions * listed, latent), BF16),
            ((rows, latent), BF16),
            ((columns, 2 * latent), BF16),
            ((rows, latent), BF16),
            ((regions * edges, latent), BF16),
        ],
        10**9,
    )
    half_one = added(keep_one, swap(give_one, "rep", 1))
    half_two = added(keep_two, swap(give_two, "rep", 1))
    half_one, own_slots = lax.optimization_barrier((half_one, own_slots))
    grid_grad, mesh_out = call(
        results_kernel,
        (turned, g2m_pick, own_slots, mesh_first, normed_two),
        [(grid_latent.shape, BF16), (mesh_latent.shape, BF16)],
        [],
        10**8,
    )
    two = summed_over_chips(half_two)
    one, grid_grad = lax.optimization_barrier((summed_over_chips(half_one), grid_grad))
    hbm = pl.BlockSpec(memory_space=pltpu.HBM)
    stage = pltpu.VMEM((half, 2 * latent), F32)
    weight_shape = pltpu.HBM((columns, 4 * latent), F32)
    limit = pltpu.CompilerParams(vmem_limit_bytes=40 << 20)
    settled = pl.pallas_call(
        settle_kernel,
        out_shape=weight_shape,
        in_specs=[VMEM] * 3,
        out_specs=hbm,
        scratch_shapes=[stage] * 3 + [pltpu.SemaphoreType.DMA((3,))],
        compiler_params=limit,
    )(one, two, swap(two, "rep", 1))
    weight_grad = pl.pallas_call(
        finish_kernel,
        out_shape=weight_shape,
        in_specs=[VMEM, hbm],
        out_specs=hbm,
        scratch_shapes=[stage, pltpu.SemaphoreType.DMA((1,))],
        input_output_aliases={1: 0},
        compiler_params=limit,
    )(swap(one, "rep", 1), settled)
    return (mesh_out, grid_grad, weight_grad)


def solution(mesh):
    regions = mesh.shape["space"]
    samples = mesh.shape["rep"]

    def whole(*arguments):
        edges = arguments[5].shape[0] + arguments[8].shape[0]
        latent = arguments[3].shape[0]
        fits = edges * latent * 4 <= SAMPLE_EDGE_BYTES and latent % (128 * regions) == 0
        paired = regions > 2 and samples > 1 and not (regions & (regions - 1) | samples & (samples - 1))
        return sharded(whole_sample_body if fits and paired else partitioned_body)(*arguments)

    def sharded(body):
        return jax.shard_map(
            body,
            mesh=mesh,
            in_specs=(
                P(("groups", "rep"), "space", None),
                P(("groups", "rep"), "space", None),
                P(("groups", "rep"), "space", None),
                P(),
                P("space", None, None),
                P("space"),
                P("space"),
                P("space", None, None),
                P("space"),
                P("space"),
            ),
            out_specs=(
                P(("groups", "rep"), "space", None),
                P(("groups", "rep"), "space", None),
                P(("groups", "space"), None),
            ),
            check_vma=False,
        )

    return whole
```

```python
import functools

import jax
import jax.numpy as jnp
from jax import lax
from jax.experimental import pallas as pl
from jax.experimental.pallas import tpu as pltpu
from jax.sharding import PartitionSpec as P

EPSILON = 1e-05


def with_halo(cells, sides, width):
    for axis, dim in sides:
        count = lax.axis_size(axis)
        ends = count - 1
        head = lax.slice_in_dim(cells, 0, width, axis=dim)
        tail = lax.slice_in_dim(cells, cells.shape[dim] - width, cells.shape[dim], axis=dim)
        cells = jnp.concatenate(
            [
                lax.ppermute(tail, axis, [(i, (i + 1) % count) for i in range(ends)]),
                cells,
                lax.ppermute(head, axis, [((i + 1) % count, i) for i in range(ends)]),
            ],
            axis=dim,
        )
    return cells


def swish(values):
    return values * jax.nn.sigmoid(values)


def swish_slope(values):
    squash = jax.nn.sigmoid(values)
    return squash * (1.0 + values * (1.0 - squash))


def norm_rows(values):
    centred = values - jnp.mean(values, -1, keepdims=True)
    return centred * lax.rsqrt(jnp.mean(centred * centred, -1, keepdims=True) + EPSILON)


def norm_rows_back(values, upstream):
    centred = values - jnp.mean(values, -1, keepdims=True)
    scaled = lax.rsqrt(jnp.mean(centred * centred, -1, keepdims=True) + EPSILON)
    normed = centred * scaled
    return scaled * (
        upstream
        - jnp.mean(upstream, -1, keepdims=True)
        - normed * jnp.mean(upstream * normed, -1, keepdims=True)
    )


def slot_rows(pick_row):
    listed = pick_row.reshape(-1)
    return listed


def mesh_route(outgoing, capacity, peer_count):
    columns = outgoing.shape[1]
    pieces = lax.all_to_all(
        outgoing.reshape(peer_count, capacity, columns),
        "space",
        split_axis=0,
        concat_axis=0,
        tiled=True,
    )
    arrived = pieces.reshape(peer_count * capacity, columns)
    return arrived


def grid_route(outgoing, capacity):
    columns = outgoing.shape[1]
    lists = outgoing.reshape(3, capacity, columns)
    rims = with_halo(jnp.stack([lists[0], lists[2]]), (("space", 0),), 1)
    return jnp.concatenate([rims[0], lists[1], rims[3]], axis=0)


def edge_pass(arrived, recv_table, located, receiver, w_send, w_recv):
    recv_proj = jnp.dot(recv_table, w_recv, preferred_element_type=jnp.float32)
    slot_proj = jnp.dot(arrived, w_send, preferred_element_type=jnp.float32)
    activation = slot_proj[located] + recv_proj[receiver]
    message = swish(activation).astype(jnp.bfloat16)
    member = (
        receiver[None, :] == jnp.arange(recv_table.shape[0], dtype=jnp.int32)[:, None]
    ).astype(jnp.bfloat16)
    summed = jnp.dot(member, message, preferred_element_type=jnp.float32)
    return (activation, member, summed)


def backward_pass(slot_count, located, activation, member, receiver, agg_grad, w_send):
    edge_grad = (agg_grad[receiver] * swish_slope(activation)).astype(jnp.bfloat16)
    recv_sum = jnp.dot(member, edge_grad, preferred_element_type=jnp.float32).astype(jnp.bfloat16)
    slot_member = (located[None, :] == jnp.arange(slot_count, dtype=jnp.int32)[:, None]).astype(
        jnp.bfloat16
    )
    slot_sum = jnp.dot(slot_member, edge_grad, preferred_element_type=jnp.float32).astype(
        jnp.bfloat16
    )
    returned = jnp.dot(slot_sum, w_send.T, preferred_element_type=jnp.float32).astype(jnp.bfloat16)
    return (recv_sum, slot_sum, returned)


def gather_back(listed, back_rows, row_count):
    owner = (listed[None, :] == jnp.arange(row_count, dtype=jnp.int32)[:, None]).astype(
        jnp.bfloat16
    )
    return jnp.dot(owner, back_rows, preferred_element_type=jnp.float32)


def partitioned_body(
    grid_latent,
    mesh_latent,
    mesh_cotangent,
    weights,
    g2m_pick,
    g2m_sender,
    g2m_receiver,
    m2m_pick,
    m2m_sender,
    m2m_receiver,
):
    grid_rows = grid_latent[0]
    mesh_rows = mesh_latent[0]
    upstream = mesh_cotangent[0].astype(jnp.float32)
    latent = weights.shape[0]
    encode_sender = weights[:, :latent]
    encode_receiver = weights[:, latent : 2 * latent]
    process_sender = weights[:, 2 * latent : 3 * latent]
    process_receiver = weights[:, 3 * latent :]
    peer_count = lax.axis_size("space")
    grid_cap = g2m_pick.shape[2]
    mesh_cap = m2m_pick.shape[2]
    grid_listed = g2m_pick[0].reshape(-1)
    grid_arrived = grid_route(grid_rows[grid_listed], grid_cap)
    act_first, member_first, summed_first = edge_pass(
        grid_arrived, mesh_rows, g2m_sender, g2m_receiver, encode_sender, encode_receiver
    )
    mesh_first = (mesh_rows.astype(jnp.float32) + norm_rows(summed_first)).astype(jnp.bfloat16)
    mesh_listed = slot_rows(m2m_pick[0])
    mesh_arrived = mesh_route(mesh_first[mesh_listed], mesh_cap, peer_count)
    act_second, member_second, summed_second = edge_pass(
        mesh_arrived, mesh_first, m2m_sender, m2m_receiver, process_sender, process_receiver
    )
    mesh_final = (mesh_first.astype(jnp.float32) + norm_rows(summed_second)).astype(jnp.bfloat16)
    agg_second = norm_rows_back(summed_second, upstream)
    recv_second, slot_second, returned_second = backward_pass(
        mesh_arrived.shape[0],
        m2m_sender,
        act_second,
        member_second,
        m2m_receiver,
        agg_second,
        process_sender,
    )
    back_second = mesh_route(returned_second, mesh_cap, peer_count)
    mesh_grad = upstream + jnp.dot(
        recv_second, process_receiver.T, preferred_element_type=jnp.float32
    )
    mesh_grad = mesh_grad + gather_back(mesh_listed, back_second, mesh_rows.shape[0])
    agg_first = norm_rows_back(summed_first, mesh_grad)
    recv_first, slot_first, returned_first = backward_pass(
        grid_arrived.shape[0],
        g2m_sender,
        act_first,
        member_first,
        g2m_receiver,
        agg_first,
        encode_sender,
    )
    back_first = grid_route(returned_first, grid_cap)
    grid_grad = gather_back(grid_listed, back_first, grid_rows.shape[0]).astype(jnp.bfloat16)
    factor_pairs = (
        (grid_arrived, slot_first),
        (mesh_rows, recv_first),
        (mesh_arrived, slot_second),
        (mesh_first, recv_second),
    )
    blocks = []
    for first_factor, second_factor in factor_pairs:
        blocks.append(
            lax.dot_general(
                first_factor,
                second_factor,
                (((0,), (0,)), ((), ())),
                preferred_element_type=jnp.float32,
            )
        )
    shares = lax.psum_scatter(
        jnp.concatenate(blocks, axis=1).astype(jnp.bfloat16),
        "space",
        scatter_dimension=0,
        tiled=True,
    )
    weight_grad = lax.psum(shares, "rep").astype(jnp.float32)
    return (mesh_final[None], grid_grad[None], weight_grad)


F32 = jnp.float32
BF16 = jnp.bfloat16
INDEX_ROWS = 8
SAMPLE_EDGE_BYTES = 8 << 20


def dot(left, right):
    return jnp.dot(left, right, preferred_element_type=F32)


def dot_first(left, right):
    return lax.dot_general(left, right, (((0,), (0,)), ((), ())), preferred_element_type=F32)


def one_hot(labels, count):
    rows = lax.broadcasted_iota(jnp.int32, (count, labels.shape[-1]), 0)
    return (rows == labels).astype(F32).astype(BF16)


def row_moments(values):
    centred = values - jnp.mean(values, -1, keepdims=True)
    return centred, lax.rsqrt(jnp.mean(centred * centred, -1, keepdims=True) + EPSILON)


def moments_back(normed, scaled, upstream):
    return scaled * (
        upstream
        - jnp.mean(upstream, -1, keepdims=True)
        - normed * jnp.mean(upstream * normed, -1, keepdims=True)
    )


def fetch(pairs, semaphores):
    copies = [
        pltpu.make_async_copy(source, target, semaphores.at[n])
        for n, (source, target) in enumerate(pairs)
    ]
    for copy in copies:
        copy.start()
    for copy in copies:
        copy.wait()


def pack_kernel(*refs):
    sources, packed_ref, index_ref = refs[:8], refs[8], refs[9]
    local, semaphores = refs[10:18], refs[18]
    fetch(list(zip(sources, local)), semaphores)
    (
        grid_ref,
        mesh_ref,
        g2m_pick_ref,
        g2m_sender_ref,
        g2m_receiver_ref,
        m2m_pick_ref,
        m2m_sender_ref,
        m2m_receiver_ref,
    ) = local
    lists, _, capacity = g2m_pick_ref.shape
    mesh_count = mesh_ref.shape[1]
    regions, mesh_cap = m2m_pick_ref.shape[1:]
    edges = g2m_sender_ref.shape[1]
    grid_rows = grid_ref[0]
    for i in range(lists):
        picked = one_hot(g2m_pick_ref[i], grid_rows.shape[0])
        packed_ref[i * capacity : (i + 1) * capacity, :] = dot_first(picked, grid_rows).astype(BF16)
    first = lists * capacity
    packed_ref[first : first + mesh_count, :] = mesh_ref[0]
    index_ref[...] = jnp.zeros_like(index_ref)
    index_ref[0:1, 0:edges] = g2m_sender_ref[...].astype(F32)
    index_ref[0:1, edges : 2 * edges] = g2m_receiver_ref[...].astype(F32)
    index_ref[1:2, 0:edges] = m2m_sender_ref[...].astype(F32)
    index_ref[1:2, edges : 2 * edges] = m2m_receiver_ref[...].astype(F32)
    slots = regions * mesh_cap
    lane = lax.broadcasted_iota(jnp.int32, (mesh_cap, slots), 1)
    spread = (lane % mesh_cap == lax.broadcasted_iota(jnp.int32, (mesh_cap, slots), 0)).astype(F32)
    spread = dot(m2m_pick_ref[0].astype(F32).astype(BF16), spread.astype(BF16))
    lane = lax.broadcasted_iota(jnp.int32, (regions, slots), 1)
    owned = lane // mesh_cap == lax.broadcasted_iota(jnp.int32, (regions, slots), 0)
    index_ref[2:3, 0:slots] = jnp.sum(jnp.where(owned, spread, 0.0), 0, keepdims=True)
    packed_ref[first + mesh_count :, :] = index_ref[...].astype(BF16)


def weights_kernel(source_ref, weights_ref, turned_ref, semaphores):
    fetch([(source_ref, weights_ref)], semaphores)
    latent = weights_ref.shape[0]
    for n, block in enumerate((0, 2, 3)):
        turned_ref[:, n * latent : (n + 1) * latent] = weights_ref[
            :, block * latent : (block + 1) * latent
        ].T


def edge_blocks(edges, size):
    size = min(edges, size)
    return [(first, min(size, edges - first)) for first in range(0, edges, size)]


def edge_forward(tables, hot_ref, turned_hot_ref, slope_ref, message_ref, mesh_count):
    regions = len(tables)
    edges = slope_ref.shape[0] // regions
    count = hot_ref.shape[0] // regions
    work = [(d, first, size) for d in range(regions) for first, size in edge_blocks(edges, 256)]

    def gathered(d, first, size):
        rows = slice(d * edges + first, d * edges + first + size)
        return dot(turned_hot_ref[rows, :], tables[d])

    sums = []
    activation = gathered(*work[0])
    for n, (d, first, size) in enumerate(work):
        coming = gathered(*work[n + 1]) if n + 1 < len(work) else None
        activation = activation.astype(BF16)
        squash = 0.5 + 0.5 * jnp.tanh(0.5 * activation)
        message = activation * squash
        rows = slice(d * edges + first, d * edges + first + size)
        slope_ref[rows, :] = squash + message * (1.0 - squash)
        message_ref[rows, :] = message
        activation = coming
        if first + size == edges:
            hot = hot_ref[(d + 1) * count - mesh_count : (d + 1) * count, :]
            sums.append(dot(hot, message_ref[d * edges : (d + 1) * edges, :]))
    return sums


def forward_kernel(
    steps,
    listed,
    mesh_count,
    mesh_cap,
    *refs,
):
    regions = len(steps)
    packed_refs = refs[:regions]
    (
        weights_ref,
        grid_ref,
        mesh_ref,
        first_ref,
        sent_ref,
        hot_one_ref,
        hot_two_ref,
        turned_one_ref,
        turned_two_ref,
        hot_sent_ref,
        slope_one_ref,
        slope_two_ref,
        normed_one_ref,
        scaled_one_ref,
        normed_two_ref,
        scaled_two_ref,
        index_ref,
        message_ref,
        sum_ref,
    ) = refs[regions:]
    latent = weights_ref.shape[0]
    edges = slope_one_ref.shape[0] // regions
    capacity = listed // 3
    slots = regions * mesh_cap
    me = lax.axis_index("space")
    for step, packed_ref in zip(steps, packed_refs):
        region = lax.rem(me + (regions - step), regions)
        at = lambda rows: pl.ds(pl.multiple_of(region * rows, rows), rows)
        grid_ref[at(listed), :] = packed_ref[:listed, :]
        mesh_ref[at(mesh_count), :] = packed_ref[listed : listed + mesh_count, :]
        index_ref[at(INDEX_ROWS), :] = packed_ref[listed + mesh_count :, :].astype(F32)

    grid_proj = dot(grid_ref[...], weights_ref[:, :latent])
    mesh_proj = dot(mesh_ref[...], weights_ref[:, latent : 2 * latent])
    for d in range(regions):
        index = index_ref[d * INDEX_ROWS : (d + 1) * INDEX_ROWS, :].astype(jnp.int32)
        for row, senders, hot_ref, turned_ref in (
            (0, listed, hot_one_ref, turned_one_ref),
            (1, slots, hot_two_ref, turned_two_ref),
        ):
            count = senders + mesh_count
            hot = jnp.concatenate(
                [
                    one_hot(index[row : row + 1, :edges], senders),
                    one_hot(index[row : row + 1, edges:], mesh_count),
                ],
                axis=0,
            )
            hot_ref[d * count : (d + 1) * count, :] = hot
            turned_ref[d * edges : (d + 1) * edges, :] = hot.T
        hot_sent_ref[d * mesh_count : (d + 1) * mesh_count, :] = one_hot(
            index[2:3, :slots], mesh_count
        )

    blank = jnp.zeros((capacity, latent), F32)
    tables = []
    for d in range(regions):
        before = (d - 1) * listed + 2 * capacity
        within = d * listed + capacity
        after = (d + 1) * listed
        tables.append(
            jnp.concatenate(
                [
                    grid_proj[before : before + capacity] if d > 0 else blank,
                    grid_proj[within : within + capacity],
                    grid_proj[after : after + capacity] if d < regions - 1 else blank,
                    mesh_proj[d * mesh_count : (d + 1) * mesh_count],
                ],
                axis=0,
            ).astype(BF16)
        )
    sums = edge_forward(
        tables, hot_one_ref, turned_one_ref, slope_one_ref, message_ref, mesh_count
    )
    for d in range(regions):
        sum_ref[d * mesh_count : (d + 1) * mesh_count, :] = sums[d]
    centred, scaled = row_moments(sum_ref[...])
    normed = centred * scaled
    normed_one_ref[...] = normed
    scaled_one_ref[...] = jnp.broadcast_to(scaled, scaled_one_ref.shape)
    first_ref[...] = (mesh_ref[...].astype(F32) + normed).astype(BF16)

    for s in range(regions):
        rows = slice(s * mesh_count, (s + 1) * mesh_count)
        sent_ref[s * slots : (s + 1) * slots, :] = dot_first(
            hot_sent_ref[rows, :], first_ref[rows, :]
        ).astype(BF16)
    sent_proj = dot(sent_ref[...], weights_ref[:, 2 * latent : 3 * latent])
    first_proj = dot(first_ref[...], weights_ref[:, 3 * latent :])
    tables = []
    for d in range(regions):
        pieces = [
            sent_proj[s * slots + d * mesh_cap : s * slots + (d + 1) * mesh_cap]
            for s in range(regions)
        ]
        tables.append(
            jnp.concatenate(
                pieces + [first_proj[d * mesh_count : (d + 1) * mesh_count]], axis=0
            ).astype(BF16)
        )
    sums = edge_forward(
        tables, hot_two_ref, turned_two_ref, slope_two_ref, message_ref, mesh_count
    )
    for d in range(regions):
        sum_ref[d * mesh_count : (d + 1) * mesh_count, :] = sums[d]
    centred, scaled = row_moments(sum_ref[...])
    normed_two_ref[...] = centred * scaled
    scaled_two_ref[...] = jnp.broadcast_to(scaled, scaled_two_ref.shape)


def edge_backward(regions, agg_grad_ref, hot_ref, turned_hot_ref, slope_ref, edge_grad_ref):
    mesh_count = agg_grad_ref.shape[0] // len(regions)
    edges = edge_grad_ref.shape[0] // len(regions)
    count = turned_hot_ref.shape[1]
    blank = jnp.zeros((count - mesh_count, agg_grad_ref.shape[1]), BF16)
    work = [(n, first, size) for n in range(len(regions)) for first, size in edge_blocks(edges, 256)]

    def at(n, first, size):
        return pl.ds(pl.multiple_of(regions[n] * edges + first, size), size)

    def gathered(n, first, size):
        own = agg_grad_ref[n * mesh_count : (n + 1) * mesh_count, :]
        return dot(turned_hot_ref[at(n, first, size), :], jnp.concatenate([blank, own], axis=0))

    sums = []
    upstream = gathered(*work[0])
    for k, (n, first, size) in enumerate(work):
        coming = gathered(*work[k + 1]) if k + 1 < len(work) else None
        rows = slice(n * edges + first, n * edges + first + size)
        edge_grad_ref[rows, :] = upstream.astype(BF16) * slope_ref[at(n, first, size), :]
        upstream = coming
        if first + size == edges:
            hot = hot_ref[pl.ds(pl.multiple_of(regions[n] * count, count), count), :]
            sums.append(dot(hot, edge_grad_ref[n * edges : (n + 1) * edges, :]))
    return sums


def halve(share_ref, keep_ref, give_ref):
    half = keep_ref.shape[0]
    core = lax.bitwise_and(lax.axis_index("rep"), 1)
    keep_ref[...] = share_ref[pl.ds(pl.multiple_of(core * half, half), half), :]
    give_ref[...] = share_ref[pl.ds(pl.multiple_of((1 - core) * half, half), half), :]


def process_back_part(
    steps, mesh_count, cotangent_refs, hot_ref, turned_hot_ref, slope_ref, normed_ref, scaled_ref,
    agg_grad_ref, edge_grad_ref,
):
    me = lax.axis_index("space")
    regions = [lax.bitwise_xor(me, step) for step in steps]
    for n, (region, cotangent_ref) in enumerate(zip(regions, cotangent_refs)):
        rows = pl.ds(pl.multiple_of(region * mesh_count, mesh_count), mesh_count)
        agg_grad_ref[n * mesh_count : (n + 1) * mesh_count, :] = moments_back(
            normed_ref[rows, :], scaled_ref[rows, 0:1], cotangent_ref[0].astype(F32)
        ).astype(BF16)
    return regions, edge_backward(
        regions, agg_grad_ref, hot_ref, turned_hot_ref, slope_ref, edge_grad_ref
    )


def near_back_kernel(steps, *refs):
    cotangent_refs, refs = refs[: len(steps)], refs[len(steps) :]
    (
        hot_ref,
        turned_hot_ref,
        slope_ref,
        normed_ref,
        scaled_ref,
        *whole_refs,
    ) = refs[:9]
    sums_ref, *column_refs = refs[9:14]
    agg_grad_ref, edge_grad_ref = refs[14:]
    mesh_count = agg_grad_ref.shape[0] // len(steps)
    count = turned_hot_ref.shape[1]
    _, all_sums = process_back_part(
        steps, mesh_count, cotangent_refs, hot_ref, turned_hot_ref, slope_ref, normed_ref,
        scaled_ref, agg_grad_ref, edge_grad_ref,
    )
    for n, sums in enumerate(all_sums):
        sums_ref[n * count : (n + 1) * count, :] = sums
    columns = column_refs[0].shape[0]
    mine = pl.ds(pl.multiple_of(lax.axis_index("space") * columns, columns), columns)
    for whole_ref, column_ref in zip(whole_refs, column_refs):
        column_ref[...] = whole_ref[:, mine].T


def far_back_kernel(near, far, mesh_cap, *refs):
    regions = len(near) + len(far)
    cotangent_refs, refs = refs[:regions], refs[regions:]
    (
        turned_ref,
        first_columns_ref,
        sent_columns_ref,
        near_sums_ref,
        hot_ref,
        turned_hot_ref,
        hot_sent_ref,
        slope_ref,
        normed_ref,
        scaled_ref,
        mesh_grad_ref,
        keep_ref,
        give_ref,
        upstream_ref,
        slot_ref,
        recv_ref,
        share_ref,
        agg_grad_ref,
        edge_grad_ref,
    ) = refs
    latent = normed_ref.shape[1]
    mesh_count = normed_ref.shape[0] // regions
    count = turned_hot_ref.shape[1]
    slots = regions * mesh_cap
    me = lax.axis_index("space")
    far_regions, all_sums = process_back_part(
        far, mesh_count, cotangent_refs[len(near) :], hot_ref, turned_hot_ref, slope_ref,
        normed_ref, scaled_ref, agg_grad_ref, edge_grad_ref,
    )
    near_regions = [lax.bitwise_xor(me, step) for step in near]
    near_sums = [near_sums_ref[n * count : (n + 1) * count, :] for n in range(len(near))]
    for region, sums in zip(near_regions + far_regions, near_sums + all_sums):
        for s in range(regions):
            slot_ref[pl.ds(pl.multiple_of(s * slots + region * mesh_cap, mesh_cap), mesh_cap), :] = (
                sums[s * mesh_cap : (s + 1) * mesh_cap]
            )
        recv_ref[pl.ds(pl.multiple_of(region * mesh_count, mesh_count), mesh_count), :] = sums[
            slots:
        ].astype(BF16)
    for region, cotangent_ref in zip(near_regions + far_regions, cotangent_refs):
        rows = pl.ds(pl.multiple_of(region * mesh_count, mesh_count), mesh_count)
        upstream_ref[rows, :] = cotangent_ref[0].astype(F32)
    slot_sum = slot_ref[...].astype(BF16)
    share_ref[:, :latent] = dot(sent_columns_ref[...], slot_sum).astype(BF16)
    share_ref[:, latent:] = dot(first_columns_ref[...], recv_ref[...]).astype(BF16)
    halve(share_ref, keep_ref, give_ref)
    returned = dot(slot_sum, turned_ref[:, latent : 2 * latent]).astype(BF16)
    grad = upstream_ref[...] + dot(recv_ref[...], turned_ref[:, 2 * latent :])
    for s in range(regions):
        rows = slice(s * mesh_count, (s + 1) * mesh_count)
        mesh_grad_ref[rows, :] = grad[rows] + dot(
            hot_sent_ref[rows, :], returned[s * slots : (s + 1) * slots]
        )


def encode_back_kernel(
    regions,
    grid_columns_ref,
    mesh_columns_ref,
    hot_ref,
    turned_hot_ref,
    slope_ref,
    normed_ref,
    scaled_ref,
    mesh_grad_ref,
    own_slot_ref,
    keep_ref,
    give_ref,
    slot_ref,
    recv_ref,
    share_ref,
    agg_grad_ref,
    edge_grad_ref,
):
    latent = normed_ref.shape[1]
    mesh_count = normed_ref.shape[0] // regions
    listed = slot_ref.shape[0] // regions
    capacity = listed // 3
    me = lax.axis_index("space")
    agg_grad_ref[...] = moments_back(
        normed_ref[...], scaled_ref[:, 0:1], mesh_grad_ref[...]
    ).astype(BF16)
    blank = jnp.zeros((capacity, latent), BF16)
    slot_ref[0:capacity, :] = blank
    slot_ref[regions * listed - capacity :, :] = blank
    all_sums = edge_backward(
        range(regions), agg_grad_ref, hot_ref, turned_hot_ref, slope_ref, edge_grad_ref
    )
    for d, sums in enumerate(all_sums):
        sums = sums.astype(BF16)
        for j in range(3):
            source = d + j - 1
            if 0 <= source < regions:
                first = source * listed + (2 - j) * capacity
                slot_ref[first : first + capacity, :] = sums[j * capacity : (j + 1) * capacity]
        recv_ref[d * mesh_count : (d + 1) * mesh_count, :] = sums[listed:]
    share_ref[:, :latent] = dot(grid_columns_ref[...], slot_ref[...]).astype(BF16)
    share_ref[:, latent:] = dot(mesh_columns_ref[...], recv_ref[...]).astype(BF16)
    halve(share_ref, keep_ref, give_ref)
    own = pl.ds(pl.multiple_of(me * listed, listed), listed)
    own_slot_ref[...] = slot_ref[own, :]


def results_kernel(
    turned_ref, pick_ref, own_slot_ref, first_ref, normed_ref, grid_grad_ref, mesh_out_ref
):
    mesh_count = mesh_out_ref.shape[1]
    me = lax.axis_index("space")
    own = pl.ds(pl.multiple_of(me * mesh_count, mesh_count), mesh_count)
    mesh_out_ref[0] = (first_ref[own, :].astype(F32) + normed_ref[own, :]).astype(BF16)
    lists, _, capacity = pick_ref.shape
    latent = own_slot_ref.shape[1]
    returned = dot(own_slot_ref[...], turned_ref[:, :latent]).astype(BF16)
    total = None
    for i in range(lists):
        owner = one_hot(pick_ref[i], grid_grad_ref.shape[1])
        part = dot(owner, returned[i * capacity : (i + 1) * capacity])
        total = part if total is None else total + part
    grid_grad_ref[0] = total.astype(BF16)


def place(pairs, stages, semaphores):
    copies = []
    for n, (block_ref, target) in enumerate(pairs):
        stages[n][...] = block_ref[...].astype(F32)
        copies.append(pltpu.make_async_copy(stages[n], target, semaphores.at[n]))
        copies[n].start()
    for copy in copies:
        copy.wait()


def half_rows(half):
    core = lax.bitwise_and(lax.axis_index("rep"), 1)
    mine = pl.ds(pl.multiple_of(core * half, half), half)
    return mine, pl.ds(pl.multiple_of((1 - core) * half, half), half)


def settle_kernel(one_ref, two_ref, other_two_ref, weight_grad_ref, *scratch):
    half, width = one_ref.shape
    mine, other = half_rows(half)
    place(
        [
            (two_ref, weight_grad_ref.at[mine, width:]),
            (other_two_ref, weight_grad_ref.at[other, width:]),
            (one_ref, weight_grad_ref.at[mine, :width]),
        ],
        scratch[:3],
        scratch[3],
    )


def finish_kernel(other_one_ref, settled_ref, weight_grad_ref, stage, semaphores):
    half, width = other_one_ref.shape
    _, other = half_rows(half)
    place([(other_one_ref, weight_grad_ref.at[other, :width])], [stage], semaphores)


VMEM = pl.BlockSpec(memory_space=pltpu.VMEM)


def call(kernel, operands, outputs, scratch, flops, fetched=0):
    hbm = pl.BlockSpec(memory_space=pltpu.HBM)
    operands = [
        pltpu.with_memory_space_constraint(operand, pltpu.HBM) if n < fetched else operand
        for n, operand in enumerate(operands)
    ]
    return pl.pallas_call(
        kernel,
        out_shape=[jax.ShapeDtypeStruct(shape, kind) for shape, kind in outputs],
        in_specs=[hbm] * fetched + [VMEM] * (len(operands) - fetched),
        out_specs=[VMEM] * len(outputs),
        scratch_shapes=[pltpu.VMEM(shape, kind) for shape, kind in scratch]
        + ([pltpu.SemaphoreType.DMA((fetched,))] if fetched else []),
        compiler_params=pltpu.CompilerParams(vmem_limit_bytes=40 << 20),
        cost_estimate=pl.CostEstimate(flops=flops, bytes_accessed=4 << 20, transcendentals=0),
    )(*operands)


def swap(block, axis, bits):
    return lax.ppermute(block, axis, [(i, i ^ bits) for i in range(lax.axis_size(axis))])


def shifted(block, step):
    count = lax.axis_size("space")
    return lax.ppermute(block, "space", [(i, (i + step) % count) for i in range(count)])


def added(left, right):
    return (left.astype(F32) + right.astype(F32)).astype(BF16)


def summed_over_chips(half):
    bit = 2
    while bit < lax.axis_size("rep"):
        half = added(half, swap(half, "rep", bit))
        bit *= 2
    return half


def whole_sample_body(
    grid_latent,
    mesh_latent,
    mesh_cotangent,
    weights,
    g2m_pick,
    g2m_sender,
    g2m_receiver,
    m2m_pick,
    m2m_sender,
    m2m_receiver,
):
    regions = lax.axis_size("space")
    latent = weights.shape[0]
    listed = g2m_pick.shape[1] * g2m_pick.shape[2]
    mesh_count = mesh_latent.shape[1]
    mesh_cap = m2m_pick.shape[2]
    edges = g2m_sender.shape[0]
    columns = latent // regions
    half = columns // 2
    g2m_pick = g2m_pick.transpose(1, 0, 2)
    sources = (
        grid_latent,
        mesh_latent,
        g2m_pick,
        g2m_sender.reshape(1, -1),
        g2m_receiver.reshape(1, -1),
        m2m_pick,
        m2m_sender.reshape(1, -1),
        m2m_receiver.reshape(1, -1),
    )
    packed = call(
        pack_kernel,
        sources,
        [((listed + mesh_count + INDEX_ROWS, latent), BF16)],
        [((INDEX_ROWS, latent), F32)] + [(source.shape, source.dtype) for source in sources],
        10**7,
        fetched=len(sources),
    )[0]
    packed, cotangent, weights = lax.optimization_barrier((packed, mesh_cotangent, weights))
    ring = (0, *sorted(range(1, regions), key=lambda step: -min(step, regions - step)))
    packs = [packed] + [shifted(packed, step) for step in ring[1:]]
    steps = (0, *range(2, regions), 1)
    near = swap(cotangent, "space", 1)
    weights, turned = call(
        weights_kernel,
        (weights,),
        [(weights.shape, BF16), ((latent, 3 * latent), BF16)],
        [],
        10**8,
        fetched=1,
    )
    turned, cotangent = lax.optimization_barrier((turned, cotangent))
    cotangents = [cotangent] + [swap(cotangent, "space", step) for step in steps[1:-1]] + [near]
    rows = regions * mesh_count
    slots = regions * mesh_cap
    (
        grid_all,
        mesh_all,
        mesh_first,
        mesh_sent,
        hot_one,
        hot_two,
        turned_one,
        turned_two,
        hot_sent,
        slope_one,
        slope_two,
        normed_one,
        scaled_one,
        normed_two,
        scaled_two,
    ) = call(
        functools.partial(forward_kernel, ring, listed, mesh_count, mesh_cap),
        (*packs, weights),
        [
            ((regions * listed, latent), BF16),
            ((rows, latent), BF16),
            ((rows, latent), BF16),
            ((regions * slots, latent), BF16),
            ((regions * (listed + mesh_count), edges), BF16),
            ((regions * (slots + mesh_count), edges), BF16),
            ((regions * edges, listed + mesh_count), BF16),
            ((regions * edges, slots + mesh_count), BF16),
            ((rows, slots), BF16),
            ((regions * edges, latent), BF16),
            ((regions * edges, latent), BF16),
            ((rows, latent), F32),
            ((rows, 128), F32),
            ((rows, latent), F32),
            ((rows, 128), F32),
        ],
        [
            ((regions * INDEX_ROWS, latent), F32),
            ((regions * edges, latent), BF16),
            ((rows, latent), F32),
        ],
        2 * 10**9,
    )
    by_step = dict(zip(steps, cotangents))
    near, far = (0, 1), tuple(step for step in steps if step > 1)
    count = slots + mesh_count
    near_sums, grid_columns, mesh_columns, sent_columns, first_columns = call(
        functools.partial(near_back_kernel, near),
        (
            *(by_step[step] for step in near),
            hot_two,
            turned_two,
            slope_two,
            normed_two,
            scaled_two,
            grid_all,
            mesh_all,
            mesh_sent,
            mesh_first,
        ),
        [
            ((len(near) * count, latent), F32),
            ((columns, regions * listed), BF16),
            ((columns, rows), BF16),
            ((columns, regions * slots), BF16),
            ((columns, rows), BF16),
        ],
        [((len(near) * mesh_count, latent), BF16), ((len(near) * edges, latent), BF16)],
        10**9,
    )
    mesh_grad, keep_two, give_two = call(
        functools.partial(far_back_kernel, near, far, mesh_cap),
        (
            *(by_step[step] for step in near + far),
            turned,
            first_columns,
            sent_columns,
            near_sums,
            hot_two,
            turned_two,
            hot_sent,
            slope_two,
            normed_two,
            scaled_two,
        ),
        [((rows, latent), F32)] + [((half, 2 * latent), BF16)] * 2,
        [
            ((rows, latent), F32),
            ((regions * slots, latent), F32),
            ((rows, latent), BF16),
            ((columns, 2 * latent), BF16),
            ((len(far) * mesh_count, latent), BF16),
            ((len(far) * edges, latent), BF16),
        ],
        10**9,
    )
    own_slots, keep_one, give_one = call(
        functools.partial(encode_back_kernel, regions),
        (
            grid_columns,
            mesh_columns,
            hot_one,
            turned_one,
            slope_one,
            normed_one,
            scaled_one,
            mesh_grad,
        ),
        [((listed, latent), BF16)] + [((half, 2 * latent), BF16)] * 2,
        [
            ((regions * listed, latent), BF16),
            ((rows, latent), BF16),
            ((columns, 2 * latent), BF16),
            ((rows, latent), BF16),
            ((regions * edges, latent), BF16),
        ],
        10**9,
    )
    half_one = added(keep_one, swap(give_one, "rep", 1))
    half_two = added(keep_two, swap(give_two, "rep", 1))
    half_one, own_slots = lax.optimization_barrier((half_one, own_slots))
    grid_grad, mesh_out = call(
        results_kernel,
        (turned, g2m_pick, own_slots, mesh_first, normed_two),
        [(grid_latent.shape, BF16), (mesh_latent.shape, BF16)],
        [],
        10**8,
    )
    two = summed_over_chips(half_two)
    one, grid_grad = lax.optimization_barrier((summed_over_chips(half_one), grid_grad))
    hbm = pl.BlockSpec(memory_space=pltpu.HBM)
    stage = pltpu.VMEM((half, 2 * latent), F32)
    weight_shape = pltpu.HBM((columns, 4 * latent), F32)
    limit = pltpu.CompilerParams(vmem_limit_bytes=40 << 20)
    settled = pl.pallas_call(
        settle_kernel,
        out_shape=weight_shape,
        in_specs=[VMEM] * 3,
        out_specs=hbm,
        scratch_shapes=[stage] * 3 + [pltpu.SemaphoreType.DMA((3,))],
        compiler_params=limit,
    )(one, two, swap(two, "rep", 1))
    weight_grad = pl.pallas_call(
        finish_kernel,
        out_shape=weight_shape,
        in_specs=[VMEM, hbm],
        out_specs=hbm,
        scratch_shapes=[stage, pltpu.SemaphoreType.DMA((1,))],
        input_output_aliases={1: 0},
        compiler_params=limit,
    )(swap(one, "rep", 1), settled)
    return (mesh_out, grid_grad, weight_grad)


def solution(mesh):
    regions = mesh.shape["space"]
    samples = mesh.shape["rep"]

    def whole(*arguments):
        edges = arguments[5].shape[0] + arguments[8].shape[0]
        latent = arguments[3].shape[0]
        fits = edges * latent * 4 <= SAMPLE_EDGE_BYTES and latent % (128 * regions) == 0
        paired = regions > 2 and samples > 1 and not (regions & (regions - 1) | samples & (samples - 1))
        return sharded(whole_sample_body if fits and paired else partitioned_body)(*arguments)

    def sharded(body):
        return jax.shard_map(
            body,
            mesh=mesh,
            in_specs=(
                P(("groups", "rep"), "space", None),
                P(("groups", "rep"), "space", None),
                P(("groups", "rep"), "space", None),
                P(),
                P("space", None, None),
                P("space"),
                P("space"),
                P("space", None, None),
                P("space"),
                P("space"),
            ),
            out_specs=(
                P(("groups", "rep"), "space", None),
                P(("groups", "rep"), "space", None),
                P(("groups", "space"), None),
            ),
            check_vma=False,
        )

    return whole
```

```python
import functools

import jax
import jax.numpy as jnp
from jax import lax
from jax.experimental import pallas as pl
from jax.experimental.pallas import tpu as pltpu
from jax.sharding import PartitionSpec as P

EPSILON = 1e-05


def with_halo(cells, sides, width):
    for axis, dim in sides:
        count = lax.axis_size(axis)
        ends = count - 1
        head = lax.slice_in_dim(cells, 0, width, axis=dim)
        tail = lax.slice_in_dim(cells, cells.shape[dim] - width, cells.shape[dim], axis=dim)
        cells = jnp.concatenate(
            [
                lax.ppermute(tail, axis, [(i, (i + 1) % count) for i in range(ends)]),
                cells,
                lax.ppermute(head, axis, [((i + 1) % count, i) for i in range(ends)]),
            ],
            axis=dim,
        )
    return cells


def swish(values):
    return values * jax.nn.sigmoid(values)


def swish_slope(values):
    squash = jax.nn.sigmoid(values)
    return squash * (1.0 + values * (1.0 - squash))


def norm_rows(values):
    centred = values - jnp.mean(values, -1, keepdims=True)
    return centred * lax.rsqrt(jnp.mean(centred * centred, -1, keepdims=True) + EPSILON)


def norm_rows_back(values, upstream):
    centred = values - jnp.mean(values, -1, keepdims=True)
    scaled = lax.rsqrt(jnp.mean(centred * centred, -1, keepdims=True) + EPSILON)
    normed = centred * scaled
    return scaled * (
        upstream
        - jnp.mean(upstream, -1, keepdims=True)
        - normed * jnp.mean(upstream * normed, -1, keepdims=True)
    )


def slot_rows(pick_row):
    listed = pick_row.reshape(-1)
    return listed


def mesh_route(outgoing, capacity, peer_count):
    columns = outgoing.shape[1]
    pieces = lax.all_to_all(
        outgoing.reshape(peer_count, capacity, columns),
        "space",
        split_axis=0,
        concat_axis=0,
        tiled=True,
    )
    arrived = pieces.reshape(peer_count * capacity, columns)
    return arrived


def grid_route(outgoing, capacity):
    columns = outgoing.shape[1]
    lists = outgoing.reshape(3, capacity, columns)
    rims = with_halo(jnp.stack([lists[0], lists[2]]), (("space", 0),), 1)
    return jnp.concatenate([rims[0], lists[1], rims[3]], axis=0)


def edge_pass(arrived, recv_table, located, receiver, w_send, w_recv):
    recv_proj = jnp.dot(recv_table, w_recv, preferred_element_type=jnp.float32)
    slot_proj = jnp.dot(arrived, w_send, preferred_element_type=jnp.float32)
    activation = slot_proj[located] + recv_proj[receiver]
    message = swish(activation).astype(jnp.bfloat16)
    member = (
        receiver[None, :] == jnp.arange(recv_table.shape[0], dtype=jnp.int32)[:, None]
    ).astype(jnp.bfloat16)
    summed = jnp.dot(member, message, preferred_element_type=jnp.float32)
    return (activation, member, summed)


def backward_pass(slot_count, located, activation, member, receiver, agg_grad, w_send):
    edge_grad = (agg_grad[receiver] * swish_slope(activation)).astype(jnp.bfloat16)
    recv_sum = jnp.dot(member, edge_grad, preferred_element_type=jnp.float32).astype(jnp.bfloat16)
    slot_member = (located[None, :] == jnp.arange(slot_count, dtype=jnp.int32)[:, None]).astype(
        jnp.bfloat16
    )
    slot_sum = jnp.dot(slot_member, edge_grad, preferred_element_type=jnp.float32).astype(
        jnp.bfloat16
    )
    returned = jnp.dot(slot_sum, w_send.T, preferred_element_type=jnp.float32).astype(jnp.bfloat16)
    return (recv_sum, slot_sum, returned)


def gather_back(listed, back_rows, row_count):
    owner = (listed[None, :] == jnp.arange(row_count, dtype=jnp.int32)[:, None]).astype(
        jnp.bfloat16
    )
    return jnp.dot(owner, back_rows, preferred_element_type=jnp.float32)


def partitioned_body(
    grid_latent,
    mesh_latent,
    mesh_cotangent,
    weights,
    g2m_pick,
    g2m_sender,
    g2m_receiver,
    m2m_pick,
    m2m_sender,
    m2m_receiver,
):
    grid_rows = grid_latent[0]
    mesh_rows = mesh_latent[0]
    upstream = mesh_cotangent[0].astype(jnp.float32)
    latent = weights.shape[0]
    encode_sender = weights[:, :latent]
    encode_receiver = weights[:, latent : 2 * latent]
    process_sender = weights[:, 2 * latent : 3 * latent]
    process_receiver = weights[:, 3 * latent :]
    peer_count = lax.axis_size("space")
    grid_cap = g2m_pick.shape[2]
    mesh_cap = m2m_pick.shape[2]
    grid_listed = g2m_pick[0].reshape(-1)
    grid_arrived = grid_route(grid_rows[grid_listed], grid_cap)
    act_first, member_first, summed_first = edge_pass(
        grid_arrived, mesh_rows, g2m_sender, g2m_receiver, encode_sender, encode_receiver
    )
    mesh_first = (mesh_rows.astype(jnp.float32) + norm_rows(summed_first)).astype(jnp.bfloat16)
    mesh_listed = slot_rows(m2m_pick[0])
    mesh_arrived = mesh_route(mesh_first[mesh_listed], mesh_cap, peer_count)
    act_second, member_second, summed_second = edge_pass(
        mesh_arrived, mesh_first, m2m_sender, m2m_receiver, process_sender, process_receiver
    )
    mesh_final = (mesh_first.astype(jnp.float32) + norm_rows(summed_second)).astype(jnp.bfloat16)
    agg_second = norm_rows_back(summed_second, upstream)
    recv_second, slot_second, returned_second = backward_pass(
        mesh_arrived.shape[0],
        m2m_sender,
        act_second,
        member_second,
        m2m_receiver,
        agg_second,
        process_sender,
    )
    back_second = mesh_route(returned_second, mesh_cap, peer_count)
    mesh_grad = upstream + jnp.dot(
        recv_second, process_receiver.T, preferred_element_type=jnp.float32
    )
    mesh_grad = mesh_grad + gather_back(mesh_listed, back_second, mesh_rows.shape[0])
    agg_first = norm_rows_back(summed_first, mesh_grad)
    recv_first, slot_first, returned_first = backward_pass(
        grid_arrived.shape[0],
        g2m_sender,
        act_first,
        member_first,
        g2m_receiver,
        agg_first,
        encode_sender,
    )
    back_first = grid_route(returned_first, grid_cap)
    grid_grad = gather_back(grid_listed, back_first, grid_rows.shape[0]).astype(jnp.bfloat16)
    factor_pairs = (
        (grid_arrived, slot_first),
        (mesh_rows, recv_first),
        (mesh_arrived, slot_second),
        (mesh_first, recv_second),
    )
    blocks = []
    for first_factor, second_factor in factor_pairs:
        blocks.append(
            lax.dot_general(
                first_factor,
                second_factor,
                (((0,), (0,)), ((), ())),
                preferred_element_type=jnp.float32,
            )
        )
    shares = lax.psum_scatter(
        jnp.concatenate(blocks, axis=1).astype(jnp.bfloat16),
        "space",
        scatter_dimension=0,
        tiled=True,
    )
    weight_grad = lax.psum(shares, "rep").astype(jnp.float32)
    return (mesh_final[None], grid_grad[None], weight_grad)


F32 = jnp.float32
BF16 = jnp.bfloat16
INDEX_ROWS = 8
SAMPLE_EDGE_BYTES = 8 << 20


def dot(left, right):
    return jnp.dot(left, right, preferred_element_type=F32)


def dot_first(left, right):
    return lax.dot_general(left, right, (((0,), (0,)), ((), ())), preferred_element_type=F32)


def one_hot(labels, count):
    rows = lax.broadcasted_iota(jnp.int32, (count, labels.shape[-1]), 0)
    return (rows == labels).astype(F32).astype(BF16)


def row_moments(values):
    centred = values - jnp.mean(values, -1, keepdims=True)
    return centred, lax.rsqrt(jnp.mean(centred * centred, -1, keepdims=True) + EPSILON)


def moments_back(normed, scaled, upstream):
    return scaled * (
        upstream
        - jnp.mean(upstream, -1, keepdims=True)
        - normed * jnp.mean(upstream * normed, -1, keepdims=True)
    )


def fetch(pairs, semaphores):
    copies = [
        pltpu.make_async_copy(source, target, semaphores.at[n])
        for n, (source, target) in enumerate(pairs)
    ]
    for copy in copies:
        copy.start()
    for copy in copies:
        copy.wait()


def pack_kernel(*refs):
    sources, packed_ref, index_ref = refs[:8], refs[8], refs[9]
    local, semaphores = refs[10:18], refs[18]
    fetch(list(zip(sources, local)), semaphores)
    (
        grid_ref,
        mesh_ref,
        g2m_pick_ref,
        g2m_sender_ref,
        g2m_receiver_ref,
        m2m_pick_ref,
        m2m_sender_ref,
        m2m_receiver_ref,
    ) = local
    lists, _, capacity = g2m_pick_ref.shape
    mesh_count = mesh_ref.shape[1]
    regions, mesh_cap = m2m_pick_ref.shape[1:]
    edges = g2m_sender_ref.shape[1]
    grid_rows = grid_ref[0]
    for i in range(lists):
        picked = one_hot(g2m_pick_ref[i], grid_rows.shape[0])
        packed_ref[i * capacity : (i + 1) * capacity, :] = dot_first(picked, grid_rows).astype(BF16)
    first = lists * capacity
    packed_ref[first : first + mesh_count, :] = mesh_ref[0]
    index_ref[...] = jnp.zeros_like(index_ref)
    index_ref[0:1, 0:edges] = g2m_sender_ref[...].astype(F32)
    index_ref[0:1, edges : 2 * edges] = g2m_receiver_ref[...].astype(F32)
    index_ref[1:2, 0:edges] = m2m_sender_ref[...].astype(F32)
    index_ref[1:2, edges : 2 * edges] = m2m_receiver_ref[...].astype(F32)
    slots = regions * mesh_cap
    lane = lax.broadcasted_iota(jnp.int32, (mesh_cap, slots), 1)
    spread = (lane % mesh_cap == lax.broadcasted_iota(jnp.int32, (mesh_cap, slots), 0)).astype(F32)
    spread = dot(m2m_pick_ref[0].astype(F32).astype(BF16), spread.astype(BF16))
    lane = lax.broadcasted_iota(jnp.int32, (regions, slots), 1)
    owned = lane // mesh_cap == lax.broadcasted_iota(jnp.int32, (regions, slots), 0)
    index_ref[2:3, 0:slots] = jnp.sum(jnp.where(owned, spread, 0.0), 0, keepdims=True)
    packed_ref[first + mesh_count :, :] = index_ref[...].astype(BF16)


def weights_kernel(source_ref, weights_ref, turned_ref, semaphores):
    fetch([(source_ref, weights_ref)], semaphores)
    latent = weights_ref.shape[0]
    for n, block in enumerate((0, 2, 3)):
        turned_ref[:, n * latent : (n + 1) * latent] = weights_ref[
            :, block * latent : (block + 1) * latent
        ].T


def edge_blocks(edges, size):
    size = min(edges, size)
    return [(first, min(size, edges - first)) for first in range(0, edges, size)]


def edge_forward(tables, hot_ref, turned_hot_ref, slope_ref, message_ref, mesh_count):
    regions = len(tables)
    edges = slope_ref.shape[0] // regions
    count = hot_ref.shape[0] // regions
    work = [(d, first, size) for d in range(regions) for first, size in edge_blocks(edges, 256)]

    def gathered(d, first, size):
        rows = slice(d * edges + first, d * edges + first + size)
        return dot(turned_hot_ref[rows, :], tables[d])

    sums = []
    activation = gathered(*work[0])
    for n, (d, first, size) in enumerate(work):
        coming = gathered(*work[n + 1]) if n + 1 < len(work) else None
        activation = activation.astype(BF16)
        squash = 0.5 + 0.5 * jnp.tanh(0.5 * activation)
        message = activation * squash
        rows = slice(d * edges + first, d * edges + first + size)
        slope_ref[rows, :] = squash + message * (1.0 - squash)
        message_ref[rows, :] = message
        activation = coming
        if first + size == edges:
            hot = hot_ref[(d + 1) * count - mesh_count : (d + 1) * count, :]
            sums.append(dot(hot, message_ref[d * edges : (d + 1) * edges, :]))
    return sums


def forward_kernel(
    steps,
    listed,
    mesh_count,
    mesh_cap,
    *refs,
):
    regions = len(steps)
    packed_refs = refs[:regions]
    (
        weights_ref,
        grid_ref,
        mesh_ref,
        first_ref,
        sent_ref,
        hot_one_ref,
        hot_two_ref,
        turned_one_ref,
        turned_two_ref,
        hot_sent_ref,
        slope_one_ref,
        slope_two_ref,
        normed_one_ref,
        scaled_one_ref,
        normed_two_ref,
        scaled_two_ref,
        index_ref,
        message_ref,
        sum_ref,
    ) = refs[regions:]
    latent = weights_ref.shape[0]
    edges = slope_one_ref.shape[0] // regions
    capacity = listed // 3
    slots = regions * mesh_cap
    me = lax.axis_index("space")
    for step, packed_ref in zip(steps, packed_refs):
        region = lax.bitwise_xor(me, step)
        at = lambda rows: pl.ds(pl.multiple_of(region * rows, rows), rows)
        grid_ref[at(listed), :] = packed_ref[:listed, :]
        mesh_ref[at(mesh_count), :] = packed_ref[listed : listed + mesh_count, :]
        index_ref[at(INDEX_ROWS), :] = packed_ref[listed + mesh_count :, :].astype(F32)

    grid_proj = dot(grid_ref[...], weights_ref[:, :latent])
    mesh_proj = dot(mesh_ref[...], weights_ref[:, latent : 2 * latent])
    for d in range(regions):
        index = index_ref[d * INDEX_ROWS : (d + 1) * INDEX_ROWS, :].astype(jnp.int32)
        for row, senders, hot_ref, turned_ref in (
            (0, listed, hot_one_ref, turned_one_ref),
            (1, slots, hot_two_ref, turned_two_ref),
        ):
            count = senders + mesh_count
            hot = jnp.concatenate(
                [
                    one_hot(index[row : row + 1, :edges], senders),
                    one_hot(index[row : row + 1, edges:], mesh_count),
                ],
                axis=0,
            )
            hot_ref[d * count : (d + 1) * count, :] = hot
            turned_ref[d * edges : (d + 1) * edges, :] = hot.T
        hot_sent_ref[d * mesh_count : (d + 1) * mesh_count, :] = one_hot(
            index[2:3, :slots], mesh_count
        )

    blank = jnp.zeros((capacity, latent), F32)
    tables = []
    for d in range(regions):
        before = (d - 1) * listed + 2 * capacity
        within = d * listed + capacity
        after = (d + 1) * listed
        tables.append(
            jnp.concatenate(
                [
                    grid_proj[before : before + capacity] if d > 0 else blank,
                    grid_proj[within : within + capacity],
                    grid_proj[after : after + capacity] if d < regions - 1 else blank,
                    mesh_proj[d * mesh_count : (d + 1) * mesh_count],
                ],
                axis=0,
            ).astype(BF16)
        )
    sums = edge_forward(
        tables, hot_one_ref, turned_one_ref, slope_one_ref, message_ref, mesh_count
    )
    for d in range(regions):
        sum_ref[d * mesh_count : (d + 1) * mesh_count, :] = sums[d]
    centred, scaled = row_moments(sum_ref[...])
    normed = centred * scaled
    normed_one_ref[...] = normed
    scaled_one_ref[...] = jnp.broadcast_to(scaled, scaled_one_ref.shape)
    first_ref[...] = (mesh_ref[...].astype(F32) + normed).astype(BF16)

    for s in range(regions):
        rows = slice(s * mesh_count, (s + 1) * mesh_count)
        sent_ref[s * slots : (s + 1) * slots, :] = dot_first(
            hot_sent_ref[rows, :], first_ref[rows, :]
        ).astype(BF16)
    sent_proj = dot(sent_ref[...], weights_ref[:, 2 * latent : 3 * latent])
    first_proj = dot(first_ref[...], weights_ref[:, 3 * latent :])
    tables = []
    for d in range(regions):
        pieces = [
            sent_proj[s * slots + d * mesh_cap : s * slots + (d + 1) * mesh_cap]
            for s in range(regions)
        ]
        tables.append(
            jnp.concatenate(
                pieces + [first_proj[d * mesh_count : (d + 1) * mesh_count]], axis=0
            ).astype(BF16)
        )
    sums = edge_forward(
        tables, hot_two_ref, turned_two_ref, slope_two_ref, message_ref, mesh_count
    )
    for d in range(regions):
        sum_ref[d * mesh_count : (d + 1) * mesh_count, :] = sums[d]
    centred, scaled = row_moments(sum_ref[...])
    normed_two_ref[...] = centred * scaled
    scaled_two_ref[...] = jnp.broadcast_to(scaled, scaled_two_ref.shape)


def edge_backward(regions, agg_grad_ref, hot_ref, turned_hot_ref, slope_ref, edge_grad_ref):
    mesh_count = agg_grad_ref.shape[0] // len(regions)
    edges = edge_grad_ref.shape[0] // len(regions)
    count = turned_hot_ref.shape[1]
    blank = jnp.zeros((count - mesh_count, agg_grad_ref.shape[1]), BF16)
    work = [(n, first, size) for n in range(len(regions)) for first, size in edge_blocks(edges, 256)]

    def at(n, first, size):
        return pl.ds(pl.multiple_of(regions[n] * edges + first, size), size)

    def gathered(n, first, size):
        own = agg_grad_ref[n * mesh_count : (n + 1) * mesh_count, :]
        return dot(turned_hot_ref[at(n, first, size), :], jnp.concatenate([blank, own], axis=0))

    sums = []
    upstream = gathered(*work[0])
    for k, (n, first, size) in enumerate(work):
        coming = gathered(*work[k + 1]) if k + 1 < len(work) else None
        rows = slice(n * edges + first, n * edges + first + size)
        edge_grad_ref[rows, :] = upstream.astype(BF16) * slope_ref[at(n, first, size), :]
        upstream = coming
        if first + size == edges:
            hot = hot_ref[pl.ds(pl.multiple_of(regions[n] * count, count), count), :]
            sums.append(dot(hot, edge_grad_ref[n * edges : (n + 1) * edges, :]))
    return sums


def halve(share_ref, keep_ref, give_ref):
    half = keep_ref.shape[0]
    core = lax.bitwise_and(lax.axis_index("rep"), 1)
    keep_ref[...] = share_ref[pl.ds(pl.multiple_of(core * half, half), half), :]
    give_ref[...] = share_ref[pl.ds(pl.multiple_of((1 - core) * half, half), half), :]


def process_back_part(
    steps, mesh_count, cotangent_refs, hot_ref, turned_hot_ref, slope_ref, normed_ref, scaled_ref,
    agg_grad_ref, edge_grad_ref,
):
    me = lax.axis_index("space")
    regions = [lax.bitwise_xor(me, step) for step in steps]
    for n, (region, cotangent_ref) in enumerate(zip(regions, cotangent_refs)):
        rows = pl.ds(pl.multiple_of(region * mesh_count, mesh_count), mesh_count)
        agg_grad_ref[n * mesh_count : (n + 1) * mesh_count, :] = moments_back(
            normed_ref[rows, :], scaled_ref[rows, 0:1], cotangent_ref[0].astype(F32)
        ).astype(BF16)
    return regions, edge_backward(
        regions, agg_grad_ref, hot_ref, turned_hot_ref, slope_ref, edge_grad_ref
    )


def near_back_kernel(steps, *refs):
    cotangent_refs, refs = refs[: len(steps)], refs[len(steps) :]
    (
        hot_ref,
        turned_hot_ref,
        slope_ref,
        normed_ref,
        scaled_ref,
        *whole_refs,
    ) = refs[:9]
    sums_ref, *column_refs = refs[9:14]
    agg_grad_ref, edge_grad_ref = refs[14:]
    mesh_count = agg_grad_ref.shape[0] // len(steps)
    count = turned_hot_ref.shape[1]
    _, all_sums = process_back_part(
        steps, mesh_count, cotangent_refs, hot_ref, turned_hot_ref, slope_ref, normed_ref,
        scaled_ref, agg_grad_ref, edge_grad_ref,
    )
    for n, sums in enumerate(all_sums):
        sums_ref[n * count : (n + 1) * count, :] = sums
    columns = column_refs[0].shape[0]
    mine = pl.ds(pl.multiple_of(lax.axis_index("space") * columns, columns), columns)
    for whole_ref, column_ref in zip(whole_refs, column_refs):
        column_ref[...] = whole_ref[:, mine].T


def far_back_kernel(near, far, mesh_cap, *refs):
    regions = len(near) + len(far)
    cotangent_refs, refs = refs[:regions], refs[regions:]
    (
        turned_ref,
        first_columns_ref,
        sent_columns_ref,
        near_sums_ref,
        hot_ref,
        turned_hot_ref,
        hot_sent_ref,
        slope_ref,
        normed_ref,
        scaled_ref,
        mesh_grad_ref,
        keep_ref,
        give_ref,
        upstream_ref,
        slot_ref,
        recv_ref,
        share_ref,
        agg_grad_ref,
        edge_grad_ref,
    ) = refs
    latent = normed_ref.shape[1]
    mesh_count = normed_ref.shape[0] // regions
    count = turned_hot_ref.shape[1]
    slots = regions * mesh_cap
    me = lax.axis_index("space")
    far_regions, all_sums = process_back_part(
        far, mesh_count, cotangent_refs[len(near) :], hot_ref, turned_hot_ref, slope_ref,
        normed_ref, scaled_ref, agg_grad_ref, edge_grad_ref,
    )
    near_regions = [lax.bitwise_xor(me, step) for step in near]
    near_sums = [near_sums_ref[n * count : (n + 1) * count, :] for n in range(len(near))]
    for region, sums in zip(near_regions + far_regions, near_sums + all_sums):
        for s in range(regions):
            slot_ref[pl.ds(pl.multiple_of(s * slots + region * mesh_cap, mesh_cap), mesh_cap), :] = (
                sums[s * mesh_cap : (s + 1) * mesh_cap]
            )
        recv_ref[pl.ds(pl.multiple_of(region * mesh_count, mesh_count), mesh_count), :] = sums[
            slots:
        ].astype(BF16)
    for region, cotangent_ref in zip(near_regions + far_regions, cotangent_refs):
        rows = pl.ds(pl.multiple_of(region * mesh_count, mesh_count), mesh_count)
        upstream_ref[rows, :] = cotangent_ref[0].astype(F32)
    slot_sum = slot_ref[...].astype(BF16)
    share_ref[:, :latent] = dot(sent_columns_ref[...], slot_sum).astype(BF16)
    share_ref[:, latent:] = dot(first_columns_ref[...], recv_ref[...]).astype(BF16)
    halve(share_ref, keep_ref, give_ref)
    returned = dot(slot_sum, turned_ref[:, latent : 2 * latent]).astype(BF16)
    grad = upstream_ref[...] + dot(recv_ref[...], turned_ref[:, 2 * latent :])
    for s in range(regions):
        rows = slice(s * mesh_count, (s + 1) * mesh_count)
        mesh_grad_ref[rows, :] = grad[rows] + dot(
            hot_sent_ref[rows, :], returned[s * slots : (s + 1) * slots]
        )


def encode_back_kernel(
    regions,
    grid_columns_ref,
    mesh_columns_ref,
    hot_ref,
    turned_hot_ref,
    slope_ref,
    normed_ref,
    scaled_ref,
    mesh_grad_ref,
    own_slot_ref,
    keep_ref,
    give_ref,
    slot_ref,
    recv_ref,
    share_ref,
    agg_grad_ref,
    edge_grad_ref,
):
    latent = normed_ref.shape[1]
    mesh_count = normed_ref.shape[0] // regions
    listed = slot_ref.shape[0] // regions
    capacity = listed // 3
    me = lax.axis_index("space")
    agg_grad_ref[...] = moments_back(
        normed_ref[...], scaled_ref[:, 0:1], mesh_grad_ref[...]
    ).astype(BF16)
    blank = jnp.zeros((capacity, latent), BF16)
    slot_ref[0:capacity, :] = blank
    slot_ref[regions * listed - capacity :, :] = blank
    all_sums = edge_backward(
        range(regions), agg_grad_ref, hot_ref, turned_hot_ref, slope_ref, edge_grad_ref
    )
    for d, sums in enumerate(all_sums):
        sums = sums.astype(BF16)
        for j in range(3):
            source = d + j - 1
            if 0 <= source < regions:
                first = source * listed + (2 - j) * capacity
                slot_ref[first : first + capacity, :] = sums[j * capacity : (j + 1) * capacity]
        recv_ref[d * mesh_count : (d + 1) * mesh_count, :] = sums[listed:]
    share_ref[:, :latent] = dot(grid_columns_ref[...], slot_ref[...]).astype(BF16)
    share_ref[:, latent:] = dot(mesh_columns_ref[...], recv_ref[...]).astype(BF16)
    halve(share_ref, keep_ref, give_ref)
    own = pl.ds(pl.multiple_of(me * listed, listed), listed)
    own_slot_ref[...] = slot_ref[own, :]


def results_kernel(
    turned_ref, pick_ref, own_slot_ref, first_ref, normed_ref, grid_grad_ref, mesh_out_ref
):
    mesh_count = mesh_out_ref.shape[1]
    me = lax.axis_index("space")
    own = pl.ds(pl.multiple_of(me * mesh_count, mesh_count), mesh_count)
    mesh_out_ref[0] = (first_ref[own, :].astype(F32) + normed_ref[own, :]).astype(BF16)
    lists, _, capacity = pick_ref.shape
    latent = own_slot_ref.shape[1]
    returned = dot(own_slot_ref[...], turned_ref[:, :latent]).astype(BF16)
    total = None
    for i in range(lists):
        owner = one_hot(pick_ref[i], grid_grad_ref.shape[1])
        part = dot(owner, returned[i * capacity : (i + 1) * capacity])
        total = part if total is None else total + part
    grid_grad_ref[0] = total.astype(BF16)


def place(pairs, stages, semaphores):
    copies = []
    for n, (block_ref, target) in enumerate(pairs):
        stages[n][...] = block_ref[...].astype(F32)
        copies.append(pltpu.make_async_copy(stages[n], target, semaphores.at[n]))
        copies[n].start()
    for copy in copies:
        copy.wait()


def half_rows(half):
    core = lax.bitwise_and(lax.axis_index("rep"), 1)
    mine = pl.ds(pl.multiple_of(core * half, half), half)
    return mine, pl.ds(pl.multiple_of((1 - core) * half, half), half)


def settle_kernel(one_ref, two_ref, other_two_ref, weight_grad_ref, *scratch):
    half, width = one_ref.shape
    mine, other = half_rows(half)
    place(
        [
            (two_ref, weight_grad_ref.at[mine, width:]),
            (other_two_ref, weight_grad_ref.at[other, width:]),
            (one_ref, weight_grad_ref.at[mine, :width]),
        ],
        scratch[:3],
        scratch[3],
    )


def finish_kernel(other_one_ref, settled_ref, weight_grad_ref, stage, semaphores):
    half, width = other_one_ref.shape
    _, other = half_rows(half)
    place([(other_one_ref, weight_grad_ref.at[other, :width])], [stage], semaphores)


VMEM = pl.BlockSpec(memory_space=pltpu.VMEM)


def call(kernel, operands, outputs, scratch, flops, fetched=0):
    hbm = pl.BlockSpec(memory_space=pltpu.HBM)
    operands = [
        pltpu.with_memory_space_constraint(operand, pltpu.HBM) if n < fetched else operand
        for n, operand in enumerate(operands)
    ]
    return pl.pallas_call(
        kernel,
        out_shape=[jax.ShapeDtypeStruct(shape, kind) for shape, kind in outputs],
        in_specs=[hbm] * fetched + [VMEM] * (len(operands) - fetched),
        out_specs=[VMEM] * len(outputs),
        scratch_shapes=[pltpu.VMEM(shape, kind) for shape, kind in scratch]
        + ([pltpu.SemaphoreType.DMA((fetched,))] if fetched else []),
        compiler_params=pltpu.CompilerParams(vmem_limit_bytes=40 << 20),
        cost_estimate=pl.CostEstimate(flops=flops, bytes_accessed=4 << 20, transcendentals=0),
    )(*operands)


def swap(block, axis, bits):
    return lax.ppermute(block, axis, [(i, i ^ bits) for i in range(lax.axis_size(axis))])


def added(left, right):
    return (left.astype(F32) + right.astype(F32)).astype(BF16)


def summed_over_chips(half):
    bit = 2
    while bit < lax.axis_size("rep"):
        half = added(half, swap(half, "rep", bit))
        bit *= 2
    return half


def whole_sample_body(
    grid_latent,
    mesh_latent,
    mesh_cotangent,
    weights,
    g2m_pick,
    g2m_sender,
    g2m_receiver,
    m2m_pick,
    m2m_sender,
    m2m_receiver,
):
    regions = lax.axis_size("space")
    latent = weights.shape[0]
    listed = g2m_pick.shape[1] * g2m_pick.shape[2]
    mesh_count = mesh_latent.shape[1]
    mesh_cap = m2m_pick.shape[2]
    edges = g2m_sender.shape[0]
    columns = latent // regions
    half = columns // 2
    g2m_pick = g2m_pick.transpose(1, 0, 2)
    sources = (
        grid_latent,
        mesh_latent,
        g2m_pick,
        g2m_sender.reshape(1, -1),
        g2m_receiver.reshape(1, -1),
        m2m_pick,
        m2m_sender.reshape(1, -1),
        m2m_receiver.reshape(1, -1),
    )
    packed = call(
        pack_kernel,
        sources,
        [((listed + mesh_count + INDEX_ROWS, latent), BF16)],
        [((INDEX_ROWS, latent), F32)] + [(source.shape, source.dtype) for source in sources],
        10**7,
        fetched=len(sources),
    )[0]
    packed, cotangent, weights = lax.optimization_barrier((packed, mesh_cotangent, weights))
    steps = (0, *range(2, regions), 1)
    packs = [packed] + [swap(packed, "space", step) for step in steps[1:]]
    weights, turned = call(
        weights_kernel,
        (weights,),
        [(weights.shape, BF16), ((latent, 3 * latent), BF16)],
        [],
        10**8,
        fetched=1,
    )
    turned, cotangent = lax.optimization_barrier((turned, cotangent))
    cotangents = [cotangent] + [swap(cotangent, "space", step) for step in steps[1:]]
    rows = regions * mesh_count
    slots = regions * mesh_cap
    (
        grid_all,
        mesh_all,
        mesh_first,
        mesh_sent,
        hot_one,
        hot_two,
        turned_one,
        turned_two,
        hot_sent,
        slope_one,
        slope_two,
        normed_one,
        scaled_one,
        normed_two,
        scaled_two,
    ) = call(
        functools.partial(forward_kernel, steps, listed, mesh_count, mesh_cap),
        (*packs, weights),
        [
            ((regions * listed, latent), BF16),
            ((rows, latent), BF16),
            ((rows, latent), BF16),
            ((regions * slots, latent), BF16),
            ((regions * (listed + mesh_count), edges), BF16),
            ((regions * (slots + mesh_count), edges), BF16),
            ((regions * edges, listed + mesh_count), BF16),
            ((regions * edges, slots + mesh_count), BF16),
            ((rows, slots), BF16),
            ((regions * edges, latent), BF16),
            ((regions * edges, latent), BF16),
            ((rows, latent), F32),
            ((rows, 128), F32),
            ((rows, latent), F32),
            ((rows, 128), F32),
        ],
        [
            ((regions * INDEX_ROWS, latent), F32),
            ((regions * edges, latent), BF16),
            ((rows, latent), F32),
        ],
        2 * 10**9,
    )
    by_step = dict(zip(steps, cotangents))
    near, far = (0, 1), tuple(step for step in steps if step > 1)
    count = slots + mesh_count
    near_sums, grid_columns, mesh_columns, sent_columns, first_columns = call(
        functools.partial(near_back_kernel, near),
        (
            *(by_step[step] for step in near),
            hot_two,
            turned_two,
            slope_two,
            normed_two,
            scaled_two,
            grid_all,
            mesh_all,
            mesh_sent,
            mesh_first,
        ),
        [
            ((len(near) * count, latent), F32),
            ((columns, regions * listed), BF16),
            ((columns, rows), BF16),
            ((columns, regions * slots), BF16),
            ((columns, rows), BF16),
        ],
        [((len(near) * mesh_count, latent), BF16), ((len(near) * edges, latent), BF16)],
        10**9,
    )
    mesh_grad, keep_two, give_two = call(
        functools.partial(far_back_kernel, near, far, mesh_cap),
        (
            *(by_step[step] for step in near + far),
            turned,
            first_columns,
            sent_columns,
            near_sums,
            hot_two,
            turned_two,
            hot_sent,
            slope_two,
            normed_two,
            scaled_two,
        ),
        [((rows, latent), F32)] + [((half, 2 * latent), BF16)] * 2,
        [
            ((rows, latent), F32),
            ((regions * slots, latent), F32),
            ((rows, latent), BF16),
            ((columns, 2 * latent), BF16),
            ((len(far) * mesh_count, latent), BF16),
            ((len(far) * edges, latent), BF16),
        ],
        10**9,
    )
    own_slots, keep_one, give_one = call(
        functools.partial(encode_back_kernel, regions),
        (
            grid_columns,
            mesh_columns,
            hot_one,
            turned_one,
            slope_one,
            normed_one,
            scaled_one,
            mesh_grad,
        ),
        [((listed, latent), BF16)] + [((half, 2 * latent), BF16)] * 2,
        [
            ((regions * listed, latent), BF16),
            ((rows, latent), BF16),
            ((columns, 2 * latent), BF16),
            ((rows, latent), BF16),
            ((regions * edges, latent), BF16),
        ],
        10**9,
    )
    half_one = added(keep_one, swap(give_one, "rep", 1))
    half_two = added(keep_two, swap(give_two, "rep", 1))
    half_one, own_slots = lax.optimization_barrier((half_one, own_slots))
    grid_grad, mesh_out = call(
        results_kernel,
        (turned, g2m_pick, own_slots, mesh_first, normed_two),
        [(grid_latent.shape, BF16), (mesh_latent.shape, BF16)],
        [],
        10**8,
    )
    two = summed_over_chips(half_two)
    one, grid_grad = lax.optimization_barrier((summed_over_chips(half_one), grid_grad))
    hbm = pl.BlockSpec(memory_space=pltpu.HBM)
    stage = pltpu.VMEM((half, 2 * latent), F32)
    weight_shape = pltpu.HBM((columns, 4 * latent), F32)
    limit = pltpu.CompilerParams(vmem_limit_bytes=40 << 20)
    settled = pl.pallas_call(
        settle_kernel,
        out_shape=weight_shape,
        in_specs=[VMEM] * 3,
        out_specs=hbm,
        scratch_shapes=[stage] * 3 + [pltpu.SemaphoreType.DMA((3,))],
        compiler_params=limit,
    )(one, two, swap(two, "rep", 1))
    weight_grad = pl.pallas_call(
        finish_kernel,
        out_shape=weight_shape,
        in_specs=[VMEM, hbm],
        out_specs=hbm,
        scratch_shapes=[stage, pltpu.SemaphoreType.DMA((1,))],
        input_output_aliases={1: 0},
        compiler_params=limit,
    )(swap(one, "rep", 1), settled)
    return (mesh_out, grid_grad, weight_grad)


def solution(mesh):
    regions = mesh.shape["space"]
    samples = mesh.shape["rep"]

    def whole(*arguments):
        edges = arguments[5].shape[0] + arguments[8].shape[0]
        latent = arguments[3].shape[0]
        fits = edges * latent * 4 <= SAMPLE_EDGE_BYTES and latent % (128 * regions) == 0
        paired = regions > 2 and samples > 1 and not (regions & (regions - 1) | samples & (samples - 1))
        return sharded(whole_sample_body if fits and paired else partitioned_body)(*arguments)

    def sharded(body):
        return jax.shard_map(
            body,
            mesh=mesh,
            in_specs=(
                P(("groups", "rep"), "space", None),
                P(("groups", "rep"), "space", None),
                P(("groups", "rep"), "space", None),
                P(),
                P("space", None, None),
                P("space"),
                P("space"),
                P("space", None, None),
                P("space"),
                P("space"),
            ),
            out_specs=(
                P(("groups", "rep"), "space", None),
                P(("groups", "rep"), "space", None),
                P(("groups", "space"), None),
            ),
            check_vma=False,
        )

    return whole
```
